32 devices in a mesh: dp: 16 (over z, x, core), mp: 2 (over y).
Axes of the slice: x: 2, y: 2, z: 4, core: 2. Of those that a mesh axis runs over, the one named last changes fastest.
Arguments:
- tokens: bfloat16 [2, 8192, 768], P(None, 'dp'), may hold values from -6 to 6
- seg_ids: int32 [2, 16, 512], P(None, 'dp'), may hold values from 0 to 31, never falling along the last dimension, each value on 1 to 32 neighbouring positions
- buckets: int32 [1023], replicated, may hold values from 0 to 31
- labels: int32 [2, 512], P(None, 'dp'), may hold values from 0 to 511, as said below
- w_query: bfloat16 [768, 768], P('dp', 'mp'), may hold values from -0.21875 to 0.21875
- w_key: bfloat16 [768, 768], P('dp', 'mp'), may hold values from -0.21875 to 0.21875
- w_value: bfloat16 [768, 768], P('dp', 'mp'), may hold values from -0.21875 to 0.21875
- w_out: bfloat16 [768, 768], P('mp', 'dp'), may hold values from -0.875 to 0.875
- w_in: bfloat16 [768, 3072], P('dp', 'mp'), may hold values from -0.21875 to 0.21875
- w_back: bfloat16 [3072, 768], P('mp', 'dp'), may hold values from -0.15625 to 0.15625
- gain_attn: bfloat16 [768], P('dp'), may hold values from 0.5 to 1.5
- gain_ffn: bfloat16 [768], P('dp'), may hold values from 0.5 to 1.5
- gain_final: bfloat16 [768], P('dp'), may hold values from 0.5 to 1.5
- w_pool: bfloat16 [768, 768], P('dp'), may hold values from -0.21875 to 0.21875
- rel_table: bfloat16 [32, 12], P(None, 'mp'), may hold values from -3 to 3
Outputs:
- loss: float32 [], replicated
- grad_tokens: bfloat16 [2, 8192, 768], P(None, 'dp')
- grad_query: float32 [768, 768], P('dp', 'mp')
- grad_key: float32 [768, 768], P('dp', 'mp')
- grad_value: float32 [768, 768], P('dp', 'mp')
- grad_out: float32 [768, 768], P('mp', 'dp')
- grad_in: float32 [768, 3072], P('dp', 'mp')
- grad_back: float32 [3072, 768], P('mp', 'dp')
- grad_gain_attn: float32 [768], P('dp')
- grad_gain_ffn: float32 [768], P('dp')
- grad_gain_final: float32 [768], P('dp')
- grad_pool: float32 [768, 768], P('dp')
- grad_table: float32 [32, 12], P(None, 'mp')
The draws below stay inside these ranges and needn't reach their ends.
Inputs may be any that keep to these rules, and one draw needn't show every extreme that they name: In each micro-batch labels pair the 512 sentences off: labels[labels[i]] = i and labels[i] != i. `seg_ids`: within each row the ids never fall and every id from 0 to 31 occurs; one sentence of every row has 32 tokens at most.
All inputs are finite; a program needn't handle non-finite values.
Results may differ from the reference program's by a relative error of at most 0.02.
Values may be sent and summed in bfloat16 or wider, within the bound.
No kernel may reach another device: no remote copies, remote signals or barrier semaphores. Data moves between devices by JAX's collectives and lax.ppermute only.
A program may use at most 192 MiB of HBM per device.

```python
import math
import jax
import jax.numpy as jnp
import numpy as np
from jax import lax

D = 768
H = 12
DH = 64
FF = 3072
NB = 32
SEQ = 512
SENT = 32
MICRO = 2
INNER = 768
MOST = 32
ROWS_MB = 16
TOK_MB = 8192
NS = 512
N_MP = 2


def draw_labels(key, part):
    key = jax.random.fold_in(key, 7)
    keys = jax.random.split(key, MICRO)

    def pair_off(one_key):
        order = jax.random.permutation(one_key, NS).astype(jnp.int32)
        first = order[0::2]
        second = order[1::2]
        partner = jnp.zeros((NS,), jnp.int32)
        partner = partner.at[first].set(second)
        partner = partner.at[second].set(first)
        return partner
    return jax.vmap(pair_off)(keys)


def place_ends(array, own_key, smallest, high):
    longest = array.shape.index(max(array.shape))
    spots = []
    for shift in (0, 1):
        where = [jax.random.randint(jax.random.fold_in(own_key, axis), (), 0, length) for axis, length in enumerate(array.shape)]
        where[longest] = (where[longest] + shift) % array.shape[longest]
        spots.append(tuple(where))
    return array.at[spots[0]].set(smallest).at[spots[1]].set(high)


def steps_of(rng, dims, cuts, smallest, top_value):
    level = 1.0
    for position, blocks in cuts:
        draws = jax.random.uniform(jax.random.fold_in(jax.random.fold_in(rng, 6), position), (blocks,), jnp.float32, smallest / len(cuts), top_value / len(cuts))
        level = level * jnp.repeat(jnp.exp(draws), dims[position] // blocks).reshape((-1,) + (1,) * (len(dims) - 1 - position))
    return level


def profile(number_of, total, most, skew):
    portions = [(1 << 20) // math.isqrt(standing ** skew) + 1 for standing in range(2, number_of + 1)]
    rest, given = total - most - (number_of - 1), [1] * (number_of - 1)
    while rest > 0:
        free = [i for i in range(number_of - 1) if given[i] < most]
        pool, remaining = sum([portions[i] for i in free]), rest
        for i in free:
            more = min(most - given[i], max(1, remaining * portions[i] // pool), rest)
            given[i] = given[i] + more
            rest = rest - more
    return np.array([most] + given)


def uneven_parts(key, number_of, total, limit, lean):
    if number_of == 2:
        one = jax.random.randint(key, (), max(1, total - limit), min(limit, total - 1) + 1)
        return jnp.stack([one, total - one])
    lengths = jnp.asarray(profile(number_of, total, limit, lean), jnp.int32)
    pairs = (number_of - 1) // 2
    donor, receiver = lengths[1:1 + 2 * pairs:2], lengths[2:2 + 2 * pairs:2]
    margin = jnp.minimum(donor - 1, limit - receiver)
    passed = jax.random.randint(jax.random.fold_in(key, 1), (pairs,), 0, 1 << 20) % (margin + 1)
    lengths = lengths.at[1:1 + 2 * pairs:2].set(donor - passed).at[2:2 + 2 * pairs:2].set(receiver + passed)
    return lengths[jax.random.permutation(jax.random.fold_in(key, 2), number_of)]


def noise(rng, dims, scale, reach, cuts=(), kind=jnp.bfloat16):
    entries = scale * jax.random.normal(rng, dims, jnp.float32)
    if cuts:
        entries = entries * steps_of(rng, dims, cuts, -0.22, 0.18)
    return jnp.clip(entries, -reach, reach).astype(kind)


def setup_inputs(seed: int = 0) -> dict:
    seeds = jax.random.split(jax.random.key(seed), 16)
    return {
        "tokens": noise(seeds[0], (MICRO, TOK_MB, D), 1.0, 6.0, ((1, 16),)),
        "seg_ids": jax.vmap(lambda own: jnp.searchsorted(jnp.cumsum(uneven_parts(own, SENT, SEQ, MOST, 1)), jnp.arange(SEQ), side="right"))(jax.random.split(seeds[1], MICRO * ROWS_MB)).reshape((MICRO, ROWS_MB, SEQ)).astype(jnp.int32),
        "buckets": place_ends(jax.random.randint(seeds[2], (2 * SEQ - 1,), 0, NB), jax.random.fold_in(seeds[2], 1), 0, NB - 1).astype(jnp.int32),
        "labels": draw_labels(jax.random.fold_in(seeds[15], 71), 0),
        "w_query": noise(seeds[4], (D, INNER), D ** -0.5, 0.21875, ((0, 16), (1, 2))),
        "w_key": noise(seeds[5], (D, INNER), D ** -0.5, 0.21875, ((0, 16), (1, 2))),
        "w_value": noise(seeds[6], (D, INNER), D ** -0.5, 0.21875, ((0, 16), (1, 2))),
        "w_out": noise(seeds[7], (INNER, D), (INNER * SENT // SEQ) ** -0.5, 0.875, ((0, 2), (1, 16))),
        "w_in": noise(seeds[8], (D, FF), D ** -0.5, 0.21875, ((0, 16), (1, 2))),
        "w_back": noise(seeds[9], (FF, D), (FF // 2) ** -0.5, 0.15625, ((0, 2), (1, 16))),
        "gain_attn": jnp.clip(1.0 + 0.1 * jax.random.normal(seeds[10], (D,), jnp.float32), 0.5, 1.5).astype(jnp.bfloat16),
        "gain_ffn": jnp.clip(1.0 + 0.1 * jax.random.normal(seeds[11], (D,), jnp.float32), 0.5, 1.5).astype(jnp.bfloat16),
        "gain_final": jnp.clip(1.0 + 0.1 * jax.random.normal(seeds[12], (D,), jnp.float32), 0.5, 1.5).astype(jnp.bfloat16),
        "w_pool": noise(seeds[13], (D, D), D ** -0.5, 0.21875, ((0, 16),)),
        "rel_table": noise(seeds[14], (NB, H), 0.5, 3.0, ((1, 2),)),
    }


@jax.custom_vjp
def low(v):
    return lax.optimization_barrier(v.astype(jnp.bfloat16)).astype(jnp.float32)

@jax.custom_vjp
def low_back(v):
    return v

def low_keep(v):
    return (low(v), None)

def low_pass(kept, grad):
    return (grad,)

def back_keep(v):
    return (v, None)

def back_low(kept, grad):
    return (low(grad),)
low.defvjp(low_keep, low_pass)
low_back.defvjp(back_keep, back_low)
NEG_FILL = -1000000000.0
SCORE_SCALE = 0.125
SOFTMAX_TEMP = 50.0
LOSS_SCALE = 64.0
EPSILON = 1e-06

def matrix_multiply(left, right):
    return jnp.dot(left, right, precision=lax.Precision.HIGHEST, preferred_element_type=jnp.float32)

def rms_norm(value, gain):
    return value * lax.rsqrt(lax.optimization_barrier(jnp.mean(value * value, axis=-1, keepdims=True)) + EPSILON) * gain

def row_attention(query_row, key_row, value_row, segment, bias):
    query_heads = query_row.reshape(SEQ, H, DH)
    key_heads = key_row.reshape(SEQ, H, DH)
    value_heads = value_row.reshape(SEQ, H, DH)
    raw = jnp.einsum('qhd,khd->hqk', query_heads, key_heads, precision=lax.Precision.HIGHEST) * SCORE_SCALE
    scores = low_back(raw) + bias
    same_doc = segment[:, None] == segment[None, :]
    scores = jnp.where(same_doc[None], scores, NEG_FILL)
    weights = low(jax.nn.softmax(scores, axis=-1))
    context = jnp.einsum('hqk,khd->qhd', weights, value_heads, precision=lax.Precision.HIGHEST)
    return context.reshape(SEQ, INNER)

def split_sum(left, right, groups):
    group_width = left.shape[1] // groups
    result = jnp.zeros((left.shape[0], right.shape[1]), jnp.float32)
    for group_id in range(groups):
        lo_col = group_id * group_width
        result = result + low(matrix_multiply(left[:, lo_col:lo_col + group_width], right[lo_col:lo_col + group_width]))
    return result

def micro_loss(inputs, segments, partner, wq_full, wk_full, wv_full, wo_full, wi_full, wb_full, gain_one, gain_two, gain_three, wp_full, bias):
    row_total = segments.shape[0]
    normed1 = low(rms_norm(inputs, gain_one))
    query = low(low_back(matrix_multiply(normed1, wq_full)))
    key = low(low_back(matrix_multiply(normed1, wk_full)))
    value = low(low_back(matrix_multiply(normed1, wv_full)))
    checked = jax.checkpoint(row_attention)

    def scan_row(carry, pieces):
        return (carry, checked(pieces[0], pieces[1], pieces[2], pieces[3], bias))
    context = lax.scan(scan_row, jnp.zeros((), jnp.float32), (query.reshape(row_total, SEQ, INNER), key.reshape(row_total, SEQ, INNER), value.reshape(row_total, SEQ, INNER), segments))[1]
    context = low(low_back(context.reshape(row_total * SEQ, INNER)))
    attn = low_back(split_sum(context, wo_full, N_MP))
    hidden1 = inputs + attn
    normed2 = low(rms_norm(hidden1, gain_two))
    up_proj = low_back(matrix_multiply(normed2, wi_full))
    act = low(jax.nn.gelu(up_proj))
    ffn = low_back(split_sum(act, wb_full, N_MP))
    hidden2 = hidden1 + ffn
    final = rms_norm(hidden2, gain_three)
    sentence = (jnp.arange(row_total, dtype=jnp.int32)[:, None] * SENT + segments).reshape(-1)
    sent_total = row_total * SENT
    sums = jax.ops.segment_sum(final, sentence, num_segments=sent_total)
    counts = jax.ops.segment_sum(jnp.ones(sentence.shape, jnp.float32), sentence, num_segments=sent_total)
    pooled = low(sums / counts[:, None])
    embed = low_back(matrix_multiply(pooled, wp_full))
    unit_vectors = low(embed * lax.rsqrt(lax.optimization_barrier(jnp.sum(embed * embed, axis=-1, keepdims=True)) + EPSILON))
    cosine_scores = low_back(matrix_multiply(unit_vectors, unit_vectors.T) * SOFTMAX_TEMP)
    order = jnp.arange(sent_total, dtype=jnp.int32)
    cosine_scores = jnp.where(order[:, None] == order[None, :], NEG_FILL, cosine_scores)
    row_lse = jax.nn.logsumexp(cosine_scores, axis=-1)
    target = lax.optimization_barrier(jnp.sum(jnp.where(order[None, :] == partner[:, None], cosine_scores, 0.0), axis=-1))
    return jnp.sum(row_lse - target)

def reference(tokens, seg_ids, buckets, labels, w_query, w_key, w_value, w_out, w_in, w_back, gain_attn, gain_ffn, gain_final, w_pool, rel_table):
    params = tuple((item.astype(jnp.float32) for item in (tokens, w_query, w_key, w_value, w_out, w_in, w_back, gain_attn, gain_ffn, gain_final, w_pool, rel_table)))

    def forward(inputs, wq_full, wk_full, wv_full, wo_full, wi_full, wb_full, gain_one, gain_two, gain_three, wp_full, table):
        onehot = (buckets[:, None] == jnp.arange(NB, dtype=jnp.int32)[None, :]).astype(jnp.float32)
        relative = matrix_multiply(onehot, table)
        offsets = jnp.arange(SEQ, dtype=jnp.int32)[None, :] - jnp.arange(SEQ, dtype=jnp.int32)[:, None] + SEQ - 1
        bias = jnp.transpose(relative[offsets], (2, 0, 1))
        total = jnp.zeros((), jnp.float32)
        for micro_step in range(MICRO):
            total = total + micro_loss(inputs[micro_step], seg_ids[micro_step], labels[micro_step], wq_full, wk_full, wv_full, wo_full, wi_full, wb_full, gain_one, gain_two, gain_three, wp_full, bias)
        return total
    total, pullback = jax.vjp(forward, *params)
    grads = pullback(jnp.ones((), jnp.float32) * LOSS_SCALE)
    loss = total / (MICRO * NS)
    return (loss, grads[0].astype(jnp.bfloat16), grads[1], grads[2], grads[3], grads[4], grads[5], grads[6], grads[7], grads[8], grads[9], grads[10], grads[11])
```

```python
import functools

import jax
import jax.numpy as jnp
from jax import lax
from jax.experimental import pallas as pl
from jax.experimental.pallas import tpu as pltpu
from jax.sharding import PartitionSpec as P

NEG_FILL = -1000000000.0
SCORE_SCALE = 0.125
SOFTMAX_TEMP = 50.0
LOSS_SCALE = 64.0
EPSILON = 1e-06
REACH = 32
QB = 64
WIN = QB + 2 * REACH
LANES = 128

BF16 = jnp.bfloat16
F32 = jnp.float32
HIGHEST = lax.Precision.HIGHEST


def dot(left, right, dims=((1,), (0,)), precision=None):
    return lax.dot_general(
        left, right, (dims, ((), ())), precision=precision, preferred_element_type=F32
    )


def dot_nt(left, right):
    return dot(left, right, ((1,), (1,)))


def dot_tn(left, right):
    return dot(left, right, ((0,), (0,)))


def rms_forward(value, gain):
    inverse = lax.rsqrt(jnp.mean(value * value, axis=-1, keepdims=True) + EPSILON)
    return (value * inverse * gain, inverse)


def rms_backward(value, inverse, gain, grad):
    scaled = grad * gain
    inner_prod = jnp.mean(value * scaled, axis=-1, keepdims=True)
    d_value = inverse * scaled - value * (inverse * inverse * inverse) * inner_prod
    d_gain = jnp.sum(grad * value * inverse, axis=0)
    return (d_value, d_gain)


def _row_bits(shape):
    return lax.broadcasted_iota(jnp.int32, shape, 0) & (QB - 1)


def _stack_heads(part):
    lane = lax.broadcasted_iota(jnp.int32, part.shape, 1)
    zero = jnp.zeros_like(part)
    first = lane < LANES // 2
    return jnp.concatenate(
        [jnp.where(first, part, zero), jnp.where(first, zero, part)], axis=0
    )


def _unstack_heads(both):
    half = both.shape[0] // 2
    lane = lax.broadcasted_iota(jnp.int32, (half, LANES), 1)
    return jnp.where(lane < LANES // 2, both[:half], both[half:])


def attend_forward_kernel(q_ref, k_ref, v_ref, segq_ref, segw_ref, rel_ref, ctx_ref, probs_ref, kpad, vpad):
    seq = q_ref.shape[0]
    for pad, ref in ((kpad, k_ref), (vpad, v_ref)):
        pad[0:REACH] = jnp.zeros((REACH, LANES), BF16)
        pad[REACH + seq :] = jnp.zeros((REACH, LANES), BF16)
        pad[REACH : REACH + seq] = ref[...]
    rel = rel_ref[0]
    row = lax.broadcasted_iota(jnp.int32, (2 * QB, WIN), 0)
    bias = jnp.where(row < QB, rel[0:1, :], rel[1:2, :])
    bits = _row_bits((2 * QB, WIN))
    step = 1
    while step < QB:
        bias = jnp.where((bits & step) != 0, pltpu.roll(bias, step, 1), bias)
        step *= 2
    for b in range(seq // QB):
        here = slice(b * QB, (b + 1) * QB)
        window = slice(b * QB, b * QB + WIN)
        query = _stack_heads(q_ref[here] * jnp.asarray(SCORE_SCALE, BF16))
        scores = dot_nt(query, kpad[window]) + bias
        seg_part = segq_ref[here]
        same = jnp.concatenate([seg_part, seg_part], axis=0) == segw_ref[b : b + 1, :]
        scores = jnp.where(same, scores, NEG_FILL)
        top = jnp.max(scores, axis=1, keepdims=True)
        shifted = jnp.exp(scores - top)
        low = (shifted / jnp.sum(shifted, axis=1, keepdims=True)).astype(BF16)
        probs_ref[0, b] = low
        ctx_ref[here] = _unstack_heads(dot(low, vpad[window])).astype(BF16)


def attend_backward_kernel(
    q_ref, k_ref, v_ref, dctx_ref, probs_ref, dqkv_ref, dbias_ref, kpad, vpad, dk_acc, dv_acc
):
    pair = pl.program_id(0)
    pairs_half = pl.num_programs(0) // 2
    seq = q_ref.shape[0]
    for pad, ref in ((kpad, k_ref), (vpad, v_ref)):
        pad[0:REACH] = jnp.zeros((REACH, LANES), BF16)
        pad[REACH + seq :] = jnp.zeros((REACH, LANES), BF16)
        pad[REACH : REACH + seq] = ref[...]
    dk_acc[...] = jnp.zeros_like(dk_acc)
    dv_acc[...] = jnp.zeros_like(dv_acc)
    total = jnp.zeros((2 * QB, WIN), F32)
    base = (pair // pairs_half) * (3 * pairs_half * LANES) + (pair % pairs_half) * LANES
    q_lane = pl.multiple_of(base, LANES)
    k_lane = pl.multiple_of(base + pairs_half * LANES, LANES)
    v_lane = pl.multiple_of(base + 2 * pairs_half * LANES, LANES)
    for b in range(seq // QB):
        here = slice(b * QB, (b + 1) * QB)
        window = slice(b * QB, b * QB + WIN)
        query = _stack_heads(q_ref[here] * jnp.asarray(SCORE_SCALE, BF16))
        d_ctx = _stack_heads(dctx_ref[here])
        low = probs_ref[0, b]
        probs = low.astype(F32)
        d_probs = dot_nt(d_ctx, vpad[window])
        inner = jnp.sum(probs * d_probs, axis=1, keepdims=True)
        d_scores = probs * (d_probs - inner)
        total = total + d_scores
        d_low = d_scores.astype(BF16)
        dqkv_ref[here, pl.ds(q_lane, LANES)] = (
            _unstack_heads(dot(d_low, kpad[window])) * SCORE_SCALE
        ).astype(BF16)
        dk_acc[window] += dot_tn(d_low, query)
        dv_acc[window] += dot_tn(low, d_ctx)
    dqkv_ref[:, pl.ds(k_lane, LANES)] = dk_acc[REACH : REACH + seq].astype(BF16)
    dqkv_ref[:, pl.ds(v_lane, LANES)] = dv_acc[REACH : REACH + seq].astype(BF16)
    bits = _row_bits((2 * QB, WIN))
    step = 1
    while step < QB:
        total = jnp.where((bits & step) != 0, pltpu.roll(total, WIN - step, 1), total)
        step *= 2
    first = jnp.sum(total[:QB], axis=0, keepdims=True)
    second = jnp.sum(total[QB:], axis=0, keepdims=True)
    dbias_ref[0] = jnp.concatenate([first, second, jnp.zeros((6, WIN), F32)], axis=0)


def _qkv_specs(seq, pairs_half):
    def spec(kind):
        return pl.BlockSpec(
            (seq, LANES),
            lambda p: (0, (p // pairs_half) * 3 * pairs_half + kind * pairs_half + p % pairs_half),
        )

    return [spec(0), spec(1), spec(2)]


def attend_forward(qkv, seg_row, rel_window):
    seq = qkv.shape[0]
    pairs = rel_window.shape[0]
    blocks = seq // QB
    padded = jnp.pad(seg_row, (REACH, REACH), constant_values=-1)
    windows = jnp.stack([padded[b * QB : b * QB + WIN] for b in range(blocks)])
    return pl.pallas_call(
        attend_forward_kernel,
        grid=(pairs,),
        out_shape=(
            jax.ShapeDtypeStruct((seq, pairs * LANES), BF16),
            jax.ShapeDtypeStruct((pairs, blocks, 2 * QB, WIN), BF16),
        ),
        in_specs=_qkv_specs(seq, pairs // 2)
        + [
            pl.BlockSpec((seq, 1), lambda p: (0, 0)),
            pl.BlockSpec((blocks, WIN), lambda p: (0, 0)),
            pl.BlockSpec((1, 2, WIN), lambda p: (p, 0, 0)),
        ],
        out_specs=(
            pl.BlockSpec((seq, LANES), lambda p: (0, p)),
            pl.BlockSpec((1, blocks, 2 * QB, WIN), lambda p: (p, 0, 0, 0)),
        ),
        scratch_shapes=[pltpu.VMEM((seq + 2 * REACH, LANES), BF16)] * 2,
        compiler_params=pltpu.CompilerParams(vmem_limit_bytes=32 * 2**20),
        name="attend_forward",
    )(qkv, qkv, qkv, seg_row[:, None], windows, rel_window)


def attend_backward(qkv, d_context, probs):
    seq = qkv.shape[0]
    pairs = probs.shape[0]
    blocks = seq // QB
    return pl.pallas_call(
        attend_backward_kernel,
        grid=(pairs,),
        out_shape=(
            jax.ShapeDtypeStruct(qkv.shape, BF16),
            jax.ShapeDtypeStruct((pairs, 8, WIN), F32),
        ),
        in_specs=_qkv_specs(seq, pairs // 2)
        + [
            pl.BlockSpec((seq, LANES), lambda p: (0, p)),
            pl.BlockSpec((1, blocks, 2 * QB, WIN), lambda p: (p, 0, 0, 0)),
        ],
        out_specs=(
            pl.BlockSpec(qkv.shape, lambda p: (0, 0)),
            pl.BlockSpec((1, 8, WIN), lambda p: (p, 0, 0)),
        ),
        scratch_shapes=[pltpu.VMEM((seq + 2 * REACH, LANES), BF16)] * 2
        + [pltpu.VMEM((seq + 2 * REACH, LANES), F32)] * 2,
        compiler_params=pltpu.CompilerParams(vmem_limit_bytes=32 * 2**20),
        name="attend_backward",
    )(qkv, qkv, qkv, d_context, probs)


CORE = 1
CROSS = 2


def hop(value, mask):
    size = lax.axis_size("dp")
    return lax.ppermute(value, "dp", [(i, i ^ mask) for i in range(size)])


def over(value):
    return lax.ppermute(value, "mp", [(0, 1), (1, 0)])


def rest_digits(size):
    digits = []
    stride = 4
    while stride < size:
        radix = min(4, size // stride)
        digits.append((stride, radix))
        stride *= radix
    return digits


def slot_masks(size):
    rest = size // 4
    return [z * 4 + x * 2 + c for c in range(2) for x in range(2) for z in range(rest)]


def gather_rest(shard):
    pieces = shard
    for stride, radix in rest_digits(lax.axis_size("dp")):
        pieces = jnp.concatenate(
            [pieces] + [hop(pieces, j * stride) for j in range(1, radix)], axis=0
        )
    return pieces


def gather_both(shard, cross_first):
    near = gather_rest(shard)
    if cross_first:
        side = hop(near, CROSS)
        y_near = over(near)
        y_side = over(side)
    else:
        y_near = over(near)
        side = hop(near, CROSS)
        y_side = hop(y_near, CROSS)
    own = jnp.concatenate([near, side, hop(near, CORE), hop(side, CORE)], axis=0)
    other = jnp.concatenate([y_near, y_side, hop(y_near, CORE), hop(y_side, CORE)], axis=0)
    return own, other


def gather_dp(shard):
    near = gather_rest(shard)
    side = hop(near, CROSS)
    return jnp.concatenate([near, side, hop(near, CORE), hop(side, CORE)], axis=0)


def scatter_rest(value):
    for stride, radix in reversed(rest_digits(lax.axis_size("dp"))):
        rows = value.shape[0] // radix
        low = value.astype(BF16)
        total = value[:rows]
        for j in range(1, radix):
            total = total + hop(low[j * rows : (j + 1) * rows], j * stride).astype(F32)
        value = total
    return value


def scatter_both(left, right, cross_first):
    half = left.shape[1] // 2
    width = right.shape[1] // 2
    sent = dot_tn(left[:, half:], right).astype(BF16)
    kept = dot_tn(left[:, :half], right)
    value = kept + hop(sent, CORE).astype(F32)
    rows = half // 2
    if cross_first:
        value = value[:rows] + hop(value[rows:].astype(BF16), CROSS).astype(F32)
        value = value[:, :width] + over(value[:, width:].astype(BF16)).astype(F32)
    else:
        value = value[:, :width] + over(value[:, width:].astype(BF16)).astype(F32)
        value = value[:rows] + hop(value[rows:].astype(BF16), CROSS).astype(F32)
    return scatter_rest(value)


def shards(
    tokens,
    seg_ids,
    buckets,
    labels,
    w_query,
    w_key,
    w_value,
    w_out,
    w_in,
    w_back,
    gain_attn,
    gain_ffn,
    gain_final,
    w_pool,
    rel_table,
):
    micro_count, seq, width = tokens.shape
    size = lax.axis_size("dp")
    me = lax.axis_index("dp")
    mine = lax.axis_index("mp")
    block = width // size
    inner_half = w_query.shape[1]
    hidden_half = w_in.shape[1]
    sent_local = labels.shape[1]
    bucket_count = rel_table.shape[0]
    heads_half = rel_table.shape[1]
    masks = slot_masks(size)

    x_own = lax.dynamic_index_in_dim(tokens, mine, 0, keepdims=False)
    segments = lax.dynamic_index_in_dim(seg_ids, mine, 0, keepdims=False)[0]
    partner = lax.dynamic_index_in_dim(labels, mine, 0, keepdims=False)

    gains_col = jnp.pad(
        jnp.stack([gain_attn, gain_ffn, gain_final], axis=1), ((0, 0), (0, LANES - 3))
    )
    pool_half = w_pool.shape[1] // 2
    pool_own = lax.dynamic_slice_in_dim(w_pool, mine * pool_half, pool_half, axis=1)
    first_own, first_other = gather_both(
        jnp.concatenate([w_query, w_key, w_value, gains_col], axis=1), True
    )
    second_own, second_other = gather_both(jnp.concatenate([w_out.T, w_in], axis=1), False)
    third_own, third_other = gather_both(w_back.T, True)
    fourth_own, fourth_other = gather_both(pool_own, False)
    qkv_w = jnp.concatenate([first_own[:, : 3 * inner_half], first_other[:, : 3 * inner_half]], axis=1)
    out_t = jnp.concatenate([second_own[:, :inner_half], second_other[:, :inner_half]], axis=1)
    in_w = jnp.concatenate([second_own[:, inner_half:], second_other[:, inner_half:]], axis=1)
    back_t = jnp.concatenate([third_own, third_other], axis=1)
    pool_w = jnp.concatenate([fourth_own, fourth_other], axis=1)
    gains = first_own[:, 3 * inner_half : 3 * inner_half + 3].T.astype(F32)
    gain_one, gain_two, gain_three = gains[0:1], gains[1:2], gains[2:3]

    slot_block = jnp.stack([jnp.bitwise_xor(me, m) for m in masks]).astype(jnp.int32)
    source = (slot_block[:, None] * block + jnp.arange(block, dtype=jnp.int32)[None, :]).reshape(-1)
    order = (jnp.arange(width, dtype=jnp.int32)[:, None] == source[None, :]).astype(BF16)
    inputs = dot(x_own, order)

    rel_all = jnp.concatenate([rel_table, over(rel_table)], axis=1).astype(F32)
    near_buckets = lax.slice_in_dim(buckets, seq - 1 - REACH, seq - 1 - REACH + WIN)
    onehot = (near_buckets[None, :] == jnp.arange(bucket_count, dtype=jnp.int32)[:, None]).astype(F32)
    rel_window = dot(rel_all, onehot, ((0,), (0,)), HIGHEST).reshape(heads_half, 2, WIN)

    normed1, inverse1 = rms_forward(inputs, gain_one)
    normed1_low = normed1.astype(BF16)
    qkv = dot(normed1_low, qkv_w).astype(BF16)
    context, probs = attend_forward(qkv, segments, rel_window)
    hidden1 = inputs + dot_nt(context, out_t)
    normed2, inverse2 = rms_forward(hidden1, gain_two)
    normed2_low = normed2.astype(BF16)
    up_proj = dot(normed2_low, in_w)
    act, gelu_back = jax.vjp(jax.nn.gelu, up_proj)
    slope = gelu_back(jnp.ones_like(up_proj))[0].astype(BF16)
    act_low = act.astype(BF16)
    hidden2 = hidden1 + dot_nt(act_low, back_t)
    final, inverse3 = rms_forward(hidden2, gain_three)
    local_ids = jnp.arange(sent_local, dtype=jnp.int32)
    member = (segments[:, None] == local_ids[None, :]).astype(F32)
    counts = jnp.sum(member, axis=0)
    pooled = dot(member, final, ((0,), (0,)), HIGHEST) / counts[:, None]
    pooled_low = pooled.astype(BF16)
    embed = dot(pooled_low, pool_w)
    inverse_e = lax.rsqrt(jnp.sum(embed * embed, axis=-1, keepdims=True) + EPSILON)
    unit = embed * inverse_e
    unit_low = unit.astype(BF16)
    every = gather_dp(unit_low)

    sims = dot_nt(every, every) * SOFTMAX_TEMP
    total_sent = every.shape[0]
    position = jnp.arange(total_sent, dtype=jnp.int32)
    sims = jnp.where(position[:, None] == position[None, :], NEG_FILL, sims)
    lse_row = jax.nn.logsumexp(sims, axis=0, keepdims=True)
    own_sims = sims[:sent_local]
    own_lse = jax.nn.logsumexp(own_sims, axis=1, keepdims=True)
    column_id = (slot_block[:, None] * sent_local + local_ids[None, :]).reshape(-1)
    is_target = column_id[None, :] == partner[:, None]
    target = jnp.sum(jnp.where(is_target, own_sims, 0.0), axis=-1, keepdims=True)
    loss_local = jnp.sum(own_lse - target)
    hit = is_target.astype(F32)
    d_rows = (LOSS_SCALE * (jnp.exp(own_sims - own_lse) - hit)).astype(BF16)
    d_cols = (LOSS_SCALE * (jnp.exp(own_sims - lse_row) - hit)).astype(BF16)
    d_both = dot(jnp.concatenate([d_rows, d_cols], axis=0), every)
    d_unit = SOFTMAX_TEMP * (d_both[:sent_local] + d_both[sent_local:])
    d_embed = inverse_e * (d_unit - unit * jnp.sum(d_unit * unit, axis=-1, keepdims=True))
    embed_low = d_embed.astype(BF16)

    grad_pool = scatter_both(pooled_low, embed_low, False)
    d_pooled = dot_nt(embed_low, pool_w)
    d_final = dot(member, d_pooled / counts[:, None], precision=HIGHEST)
    d_hidden2, d_gain3 = rms_backward(hidden2, inverse3, gain_three, d_final)
    ffn_low = d_hidden2.astype(BF16)
    grad_back = scatter_both(ffn_low, act_low, True)
    up_low = (dot(ffn_low, back_t) * slope.astype(F32)).astype(BF16)
    grad_in = scatter_both(normed2_low, up_low, False)
    d_normed2 = dot_nt(up_low, in_w)
    d_part2, d_gain2 = rms_backward(hidden1, inverse2, gain_two, d_normed2)
    d_hidden1 = d_hidden2 + d_part2
    attn_low = d_hidden1.astype(BF16)
    grad_out = scatter_both(attn_low, context, True)
    d_context = dot(attn_low, out_t).astype(BF16)
    d_qkv, d_bias = attend_backward(qkv, d_context, probs)
    grad_qkv = scatter_both(normed1_low, d_qkv, True)
    d_normed1 = dot_nt(d_qkv, qkv_w)
    d_part1, d_gain1 = rms_backward(inputs, inverse1, gain_one, d_normed1)
    grad_slots = (d_hidden1 + d_part1).astype(BF16)
    grad_own = dot_nt(grad_slots, order).astype(BF16)
    grad_other = over(grad_own)
    grad_tokens = jnp.where(
        mine == 0, jnp.stack([grad_own, grad_other]), jnp.stack([grad_other, grad_own])
    )

    d_table = dot(onehot, d_bias[:, :2].reshape(2 * heads_half, WIN), ((1,), (1,)), HIGHEST)
    table_own, table_other = d_table[:, :heads_half], d_table[:, heads_half:]
    table_abs = jnp.where(
        mine == 0,
        jnp.concatenate([table_own, table_other], axis=1),
        jnp.concatenate([table_other, table_own], axis=1),
    )
    d_gains = dot(jnp.stack([d_gain1, d_gain2, d_gain3]), order.astype(F32), ((1,), (1,)), HIGHEST)
    flat = jnp.concatenate([d_gains.reshape(-1), table_abs.reshape(-1), loss_local.reshape(1)])
    flat = jnp.pad(flat, (0, -flat.shape[0] % (8 * LANES))).reshape(-1, LANES)
    flat = flat + over(flat)
    flat = flat + hop(flat, CORE)
    flat = flat + hop(flat, CROSS)
    for stride, radix in rest_digits(size):
        flat = flat + sum(hop(flat, j * stride) for j in range(1, radix))
    flat = flat.reshape(-1)
    gains_sum = flat[: 3 * width].reshape(3, width)
    gains_mine = lax.dynamic_slice_in_dim(gains_sum, me * block, block, axis=1)
    table_sum = flat[3 * width : 3 * width + table_abs.size].reshape(table_abs.shape)
    table_mine = lax.dynamic_slice_in_dim(table_sum, mine * heads_half, heads_half, axis=1)
    loss = flat[3 * width + table_abs.size] / (micro_count * sent_local * size)

    pool_other = over(grad_pool)
    grad_pool = jnp.where(
        mine == 0,
        jnp.concatenate([grad_pool, pool_other], axis=1),
        jnp.concatenate([pool_other, grad_pool], axis=1),
    )
    return (
        loss,
        grad_tokens,
        grad_qkv[:, :inner_half],
        grad_qkv[:, inner_half : 2 * inner_half],
        grad_qkv[:, 2 * inner_half :],
        grad_out.T,
        grad_in,
        grad_back.T,
        gains_mine[0],
        gains_mine[1],
        gains_mine[2],
        grad_pool,
        table_mine,
    )


def solution(mesh):
    placed = (
        P(None, "dp", None),
        P(None, "dp", None),
        P(),
        P(None, "dp"),
        P("dp", "mp"),
        P("dp", "mp"),
        P("dp", "mp"),
        P("mp", "dp"),
        P("dp", "mp"),
        P("mp", "dp"),
        P("dp"),
        P("dp"),
        P("dp"),
        P("dp", None),
        P(None, "mp"),
    )
    return jax.shard_map(
        shards,
        mesh=mesh,
        in_specs=placed,
        out_specs=(
            P(),
            P(None, "dp", None),
            P("dp", "mp"),
            P("dp", "mp"),
            P("dp", "mp"),
            P("mp", "dp"),
            P("dp", "mp"),
            P("mp", "dp"),
            P("dp"),
            P("dp"),
            P("dp"),
            P("dp", None),
            P(None, "mp"),
        ),
        check_vma=False,
    )
```

```python
import jax
import jax.numpy as jnp
from jax import lax
from jax.experimental import pallas as pl
from jax.experimental.pallas import tpu as pltpu
from jax.sharding import PartitionSpec as P

NEG_FILL = -1000000000.0
SCORE_SCALE = 0.125
SOFTMAX_TEMP = 50.0
LOSS_SCALE = 64.0
EPSILON = 1e-06
REACH = 32
QB = 64
WIN = QB + 2 * REACH
LANES = 128
GELU_A = 0.7978845608028654
GELU_B = 0.044715

BF16 = jnp.bfloat16
F32 = jnp.float32
HIGHEST = lax.Precision.HIGHEST


def dot(left, right, dims=((1,), (0,)), precision=None):
    return lax.dot_general(
        left, right, (dims, ((), ())), precision=precision, preferred_element_type=F32
    )


def dot_nt(left, right):
    return dot(left, right, ((1,), (1,)))


def dot_tn(left, right):
    return dot(left, right, ((0,), (0,)))


def rms_forward(value, gain):
    inverse = lax.rsqrt(jnp.mean(value * value, axis=-1, keepdims=True) + EPSILON)
    return (value * inverse * gain, inverse)


def rms_backward(value, inverse, gain, grad):
    scaled = grad * gain
    inner_prod = jnp.mean(value * scaled, axis=-1, keepdims=True)
    d_value = inverse * scaled - value * (inverse * inverse * inverse) * inner_prod
    d_gain = jnp.sum(grad * value * inverse, axis=0)
    return (d_value, d_gain)


def cost(flops, bytes_accessed):
    return pl.CostEstimate(flops=flops, bytes_accessed=bytes_accessed, transcendentals=0)


def params(mib=48):
    return pltpu.CompilerParams(vmem_limit_bytes=mib * 2**20)


def wide_kernel(x_ref, own_ref, other_ref, out_ref):
    half = own_ref.shape[1]
    x = x_ref[...]
    out_ref[:, :half] = dot(x, own_ref[...]).astype(out_ref.dtype)
    out_ref[:, half:] = dot(x, other_ref[...]).astype(out_ref.dtype)


def gelu_kernel(x_ref, own_ref, other_ref, act_ref, slope_ref):
    half = own_ref.shape[1]
    x = x_ref[...]
    for side, ref in enumerate((own_ref, other_ref)):
        here = slice(side * half, (side + 1) * half)
        up = dot(x, ref[...])
        square = up * up
        bend = jnp.tanh(GELU_A * up * (1.0 + GELU_B * square))
        half_one = 0.5 + 0.5 * bend
        act_ref[:, here] = (up * half_one).astype(BF16)
        inner = GELU_A + (3.0 * GELU_A * GELU_B) * square
        slope_ref[:, here] = (half_one + 0.5 * up * (1.0 - bend * bend) * inner).astype(BF16)


def slope_kernel(x_ref, own_ref, other_ref, slope_ref, out_ref):
    half = own_ref.shape[1]
    x = x_ref[...]
    for side, ref in enumerate((own_ref, other_ref)):
        here = slice(side * half, (side + 1) * half)
        out_ref[:, here] = (dot(x, ref[...]) * slope_ref[:, here].astype(F32)).astype(BF16)


def narrow_kernel(x_ref, own_ref, other_ref, out_ref):
    half = own_ref.shape[1]

    @pl.when(pl.program_id(0) == 0)
    def _():
        out_ref[...] = jnp.zeros_like(out_ref)

    out_ref[...] += dot_nt(x_ref[:, :half], own_ref[...]) + dot_nt(x_ref[:, half:], other_ref[...])


def _weight_spec(rows, n, first):
    return pl.BlockSpec((rows, n), lambda i: (0, first + i))


def wide(x, own, other, n, count, first=0, body=wide_kernel, outs=1, extra=()):
    rows, depth = x.shape
    block = pl.BlockSpec((rows, 2 * n), lambda i: (0, i))
    shape = jax.ShapeDtypeStruct((rows, 2 * n * count), BF16)
    result = pl.pallas_call(
        body,
        grid=(count,),
        out_shape=(shape,) * outs,
        in_specs=[pl.BlockSpec(x.shape, lambda i: (0, 0))]
        + [_weight_spec(depth, n, first)] * 2
        + [block] * len(extra),
        out_specs=(block,) * outs,
        compiler_params=params(),
        cost_estimate=cost(4 * rows * depth * n * count, 4 * depth * n * count),
    )(x, own, other, *extra)
    return result if outs > 1 else result[0]


def narrow(x, own, other, n, count, first=0):
    rows = x.shape[0]
    depth = own.shape[0]
    return pl.pallas_call(
        narrow_kernel,
        grid=(count,),
        out_shape=jax.ShapeDtypeStruct((rows, depth), F32),
        in_specs=[pl.BlockSpec((rows, 2 * n), lambda i: (0, i))] + [_weight_spec(depth, n, first)] * 2,
        out_specs=pl.BlockSpec((rows, depth), lambda i: (0, 0)),
        compiler_params=params(),
        cost_estimate=cost(4 * rows * depth * n * count, 4 * depth * n * count),
    )(x, own, other)


def _stack_heads(part):
    lane = lax.broadcasted_iota(jnp.int32, part.shape, 1)
    zero = jnp.zeros_like(part)
    first = lane < LANES // 2
    return jnp.concatenate(
        [jnp.where(first, part, zero), jnp.where(first, zero, part)], axis=0
    )


def _unstack_heads(both):
    half = both.shape[0] // 2
    lane = lax.broadcasted_iota(jnp.int32, (half, LANES), 1)
    return jnp.where(lane < LANES // 2, both[:half], both[half:])


def _pad_keys(pad, ref):
    seq = ref.shape[0]
    pad[0:REACH] = jnp.zeros((REACH, LANES), pad.dtype)
    pad[REACH + seq :] = jnp.zeros((REACH, LANES), pad.dtype)
    pad[REACH : REACH + seq] = ref[...]


def _query_bits(shape):
    return lax.broadcasted_iota(jnp.int32, shape, 0) & (QB - 1)


def attend_forward_kernel(
    q_ref, k_ref, v_ref, segq_ref, segk_ref, rel_ref, ctx_ref, probs_ref, kpad, vpad, mask, scores
):
    seq = q_ref.shape[0]
    blocks = seq // QB
    _pad_keys(kpad, k_ref)
    _pad_keys(vpad, v_ref)

    @pl.when(pl.program_id(0) == 0)
    def _():
        for b in range(blocks):
            same = segk_ref[b * QB : b * QB + WIN] == segq_ref[b : b + 1, :]
            mask[b] = jnp.where(same, 0.0, NEG_FILL)

    rel = rel_ref[0]
    row = lax.broadcasted_iota(jnp.int32, (2 * QB, WIN), 0)
    bias = jnp.where(row < QB, rel[0:1, :], rel[1:2, :])
    bits = _query_bits((2 * QB, WIN))
    step = 1
    while step < QB:
        bias = jnp.where((bits & step) != 0, pltpu.roll(bias, step, 1), bias)
        step *= 2
    bias = bias.T
    for b in range(blocks):
        query = _stack_heads(q_ref[b * QB : (b + 1) * QB] * jnp.asarray(SCORE_SCALE, BF16))
        scores[b] = dot_nt(kpad[b * QB : b * QB + WIN], query)
    values = scores[...] + bias[None] + mask[...]
    top = jnp.max(values, axis=1, keepdims=True)
    shifted = jnp.exp(values - top)
    total = jnp.sum(shifted, axis=1, keepdims=True)
    probs_ref[0] = (shifted * (1.0 / total)).astype(BF16)
    for b in range(blocks):
        part = dot_tn(probs_ref[0, b], vpad[b * QB : b * QB + WIN])
        ctx_ref[b * QB : (b + 1) * QB] = _unstack_heads(part).astype(BF16)


def attend_backward_kernel(
    q_ref, k_ref, v_ref, dctx_ref, probs_ref, dq_ref, dk_ref, dv_ref, dbias_ref,
    kpad, vpad, dk_acc, dv_acc, d_probs, d_low,
):
    seq = q_ref.shape[0]
    blocks = seq // QB
    _pad_keys(kpad, k_ref)
    _pad_keys(vpad, v_ref)
    dk_acc[...] = jnp.zeros_like(dk_acc)
    dv_acc[...] = jnp.zeros_like(dv_acc)
    for b in range(blocks):
        window = slice(b * QB, b * QB + WIN)
        d_ctx = _stack_heads(dctx_ref[b * QB : (b + 1) * QB])
        d_probs[b] = dot_nt(vpad[window], d_ctx)
        dv_acc[window] += dot(probs_ref[0, b], d_ctx)
    probs = probs_ref[0].astype(F32)
    product = probs * d_probs[...]
    inner = jnp.sum(product, axis=1, keepdims=True)
    d_scores = product - probs * inner
    d_low[...] = d_scores.astype(BF16)
    total = jnp.sum(d_scores, axis=0).T
    for b in range(blocks):
        here = slice(b * QB, (b + 1) * QB)
        window = slice(b * QB, b * QB + WIN)
        query = _stack_heads(q_ref[here] * jnp.asarray(SCORE_SCALE, BF16))
        dk_acc[window] += dot(d_low[b], query)
        d_query = _unstack_heads(dot_tn(d_low[b], kpad[window])) * SCORE_SCALE
        dq_ref[here] = d_query.astype(BF16)
    dk_ref[...] = dk_acc[REACH : REACH + seq].astype(BF16)
    dv_ref[...] = dv_acc[REACH : REACH + seq].astype(BF16)
    bits = _query_bits((2 * QB, WIN))
    step = 1
    while step < QB:
        total = jnp.where((bits & step) != 0, pltpu.roll(total, WIN - step, 1), total)
        step *= 2
    first = jnp.sum(total[:QB], axis=0, keepdims=True)
    second = jnp.sum(total[QB:], axis=0, keepdims=True)
    dbias_ref[0] = jnp.concatenate([first, second, jnp.zeros((6, WIN), F32)], axis=0)


def _qkv_specs(seq, pairs):
    def spec(kind):
        return pl.BlockSpec((seq, LANES), lambda p: (0, kind * pairs + p))

    return [spec(0), spec(1), spec(2)]


def attend_forward(qkv, seg_row, rel_window):
    seq = qkv.shape[0]
    pairs = rel_window.shape[0]
    blocks = seq // QB
    padded = jnp.pad(seg_row, (REACH, REACH), constant_values=-1)[:, None]
    twice = jnp.tile(seg_row.reshape(blocks, QB), (1, 2))
    return pl.pallas_call(
        attend_forward_kernel,
        grid=(pairs,),
        out_shape=(
            jax.ShapeDtypeStruct((seq, pairs * LANES), BF16),
            jax.ShapeDtypeStruct((pairs, blocks, WIN, 2 * QB), BF16),
        ),
        in_specs=_qkv_specs(seq, pairs)
        + [
            pl.BlockSpec((seq + 2 * REACH, 1), lambda p: (0, 0)),
            pl.BlockSpec((blocks, 2 * QB), lambda p: (0, 0)),
            pl.BlockSpec((1, 2, WIN), lambda p: (p, 0, 0)),
        ][1:2]
        + [
            pl.BlockSpec((seq + 2 * REACH, 1), lambda p: (0, 0)),
            pl.BlockSpec((1, 2, WIN), lambda p: (p, 0, 0)),
        ],
        out_specs=(
            pl.BlockSpec((seq, LANES), lambda p: (0, p)),
            pl.BlockSpec((1, blocks, WIN, 2 * QB), lambda p: (p, 0, 0, 0)),
        ),
        scratch_shapes=[pltpu.VMEM((seq + 2 * REACH, LANES), BF16)] * 2
        + [pltpu.VMEM((blocks, WIN, 2 * QB), F32)] * 2,
        compiler_params=params(),
        cost_estimate=cost(8 * seq * WIN * LANES * pairs * 4, 8 * seq * LANES * pairs),
        name="attend_forward",
    )(qkv, qkv, qkv, twice, padded, rel_window)


def attend_backward(qkv, d_context, probs):
    seq = qkv.shape[0]
    pairs = probs.shape[0]
    blocks = seq // QB
    lane_block = pl.BlockSpec((seq, LANES), lambda p: (0, p))
    grad_shape = jax.ShapeDtypeStruct((seq, pairs * LANES), BF16)
    return pl.pallas_call(
        attend_backward_kernel,
        grid=(pairs,),
        out_shape=(grad_shape,) * 3 + (jax.ShapeDtypeStruct((pairs, 8, WIN), F32),),
        in_specs=_qkv_specs(seq, pairs)
        + [
            lane_block,
            pl.BlockSpec((1, blocks, WIN, 2 * QB), lambda p: (p, 0, 0, 0)),
        ],
        out_specs=(lane_block,) * 3 + (pl.BlockSpec((1, 8, WIN), lambda p: (p, 0, 0)),),
        scratch_shapes=[pltpu.VMEM((seq + 2 * REACH, LANES), BF16)] * 2
        + [pltpu.VMEM((seq + 2 * REACH, LANES), F32)] * 2
        + [pltpu.VMEM((blocks, WIN, 2 * QB), F32), pltpu.VMEM((blocks, WIN, 2 * QB), BF16)],
        compiler_params=params(),
        cost_estimate=cost(16 * seq * WIN * LANES * pairs * 4, 16 * seq * LANES * pairs),
        name="attend_backward",
    )(qkv, qkv, qkv, d_context, probs)


CORE = 1
CROSS = 2


def after(value, *others):
    return lax.optimization_barrier((value, *others))[0]


def hop(value, mask):
    size = lax.axis_size("dp")
    return lax.ppermute(value, "dp", [(i, i ^ mask) for i in range(size)])


def over(value):
    return lax.ppermute(value, "mp", [(0, 1), (1, 0)])


class Lane:
    def __init__(self, send, depth=2):
        self.send = send
        self.depth = depth
        self.got = []

    def __call__(self, value):
        if len(self.got) >= self.depth:
            value = after(value, self.got[-self.depth])
        self.got.append(self.send(value))
        return self.got[-1]


def slot_masks(size):
    rest = size // 4
    return [z * 4 + x * 2 + c for c in range(2) for x in range(2) for z in range(rest)]


def strides(size):
    found = []
    stride = 4
    while stride < size:
        found.append(stride)
        stride *= 2
    return found


def gather_chunks(shards_in, cross_first):
    near = []
    last = None
    for shard in shards_in:
        if last is not None:
            shard = after(shard, last)
        last = None
        pieces = shard
        for stride in strides(lax.axis_size("dp")):
            got = hop(pieces, stride)
            last = got if last is None else last
            pieces = jnp.concatenate([pieces, got], axis=0)
        near.append(pieces)
    send_x = Lane(lambda v: hop(v, CROSS))
    send_y = Lane(over)
    out = []
    for here, first in zip(near, cross_first):
        if first:
            side = send_x(here)
            y_here = send_y(here)
            y_side = send_y(side)
        else:
            y_here = send_y(here)
            side = send_x(here)
            y_side = send_x(y_here)
        out.append(
            tuple(
                jnp.concatenate([a, b, hop(a, CORE), hop(b, CORE)], axis=0)
                for a, b in ((here, side), (y_here, y_side))
            )
        )
    return out


def gather_dp(shard):
    size = lax.axis_size("dp")
    pieces = shard
    stride = 4
    while stride < size:
        radix = min(4, size // stride)
        pieces = jnp.concatenate(
            [pieces] + [hop(pieces, j * stride) for j in range(1, radix)], axis=0
        )
        stride *= radix
    side = hop(pieces, CROSS)
    return jnp.concatenate([pieces, side, hop(pieces, CORE), hop(side, CORE)], axis=0)


def sent_part(left, right):
    return dot_tn(left[:, left.shape[1] // 2 :], right).astype(BF16)


def kept_part(left, right):
    return dot_tn(left[:, : left.shape[1] // 2], right)


def scatter_plane(kept, got, send_x, send_y, cross_first):
    value = kept + got.astype(F32)
    rows, width = value.shape[0] // 2, value.shape[1] // 2
    if cross_first:
        value = value[:rows] + send_x(value[rows:].astype(BF16)).astype(F32)
        return value[:, :width] + send_y(value[:, width:].astype(BF16)).astype(F32)
    value = value[:, :width] + send_y(value[:, width:].astype(BF16)).astype(F32)
    return value[:rows] + send_x(value[rows:].astype(BF16)).astype(F32)


def scatter_rest(value):
    for stride in reversed(strides(lax.axis_size("dp"))):
        rows = value.shape[0] // 2
        value = value[:rows] + hop(value[rows:].astype(BF16), stride).astype(F32)
    return value


def shards(
    tokens,
    seg_ids,
    buckets,
    labels,
    w_query,
    w_key,
    w_value,
    w_out,
    w_in,
    w_back,
    gain_attn,
    gain_ffn,
    gain_final,
    w_pool,
    rel_table,
):
    micro_count, seq, width = tokens.shape
    size = lax.axis_size("dp")
    me = lax.axis_index("dp")
    mine = lax.axis_index("mp")
    block = width // size
    inner_half = w_query.shape[1]
    hidden_half = w_in.shape[1]
    sent_local = labels.shape[1]
    bucket_count = rel_table.shape[0]
    heads_half = rel_table.shape[1]
    masks = slot_masks(size)

    x_own = lax.dynamic_index_in_dim(tokens, mine, 0, keepdims=False)
    segments = lax.dynamic_index_in_dim(seg_ids, mine, 0, keepdims=False)[0]
    partner = lax.dynamic_index_in_dim(labels, mine, 0, keepdims=False)

    gains_col = jnp.pad(
        jnp.stack([gain_attn, gain_ffn, gain_final], axis=1), ((0, 0), (0, LANES - 3))
    )
    pool_half = w_pool.shape[1] // 2
    pool_own = lax.dynamic_slice_in_dim(w_pool, mine * pool_half, pool_half, axis=1)
    piece = hidden_half // 2
    back_shard = w_back.T
    first, second, third, fourth = gather_chunks(
        [
            jnp.concatenate([w_query, w_key, w_value, gains_col], axis=1),
            jnp.concatenate([w_in, w_out.T], axis=1),
            jnp.concatenate([back_shard[:, :piece], pool_own], axis=1),
            back_shard[:, piece:],
        ],
        (True, False, True, False),
    )
    out_at = hidden_half // inner_half
    pool_own_w, pool_other_w = third[0][:, piece:], third[1][:, piece:]
    gains = first[0][:, 3 * inner_half : 3 * inner_half + 3].T.astype(F32)
    gain_one, gain_two, gain_three = gains[0:1], gains[1:2], gains[2:3]

    slot_block = jnp.stack([jnp.bitwise_xor(me, m) for m in masks]).astype(jnp.int32)
    source = (slot_block[:, None] * block + jnp.arange(block, dtype=jnp.int32)[None, :]).reshape(-1)
    order = (jnp.arange(width, dtype=jnp.int32)[:, None] == source[None, :]).astype(BF16)
    inputs = dot(x_own, order)

    rel_all = jnp.concatenate([rel_table, over(rel_table)], axis=1).astype(F32)
    near_buckets = lax.slice_in_dim(buckets, seq - 1 - REACH, seq - 1 - REACH + WIN)
    onehot = (near_buckets[None, :] == jnp.arange(bucket_count, dtype=jnp.int32)[:, None]).astype(F32)
    rel_window = dot(rel_all, onehot, ((0,), (0,)), HIGHEST).reshape(heads_half, 2, WIN)

    normed1, inverse1 = rms_forward(inputs, gain_one)
    normed1_low = normed1.astype(BF16)
    qkv = wide(normed1_low, *first, inner_half, 3)
    context, probs = attend_forward(qkv, segments, rel_window)
    hidden1 = inputs + narrow(context, *second, inner_half, 1, out_at)
    normed2, inverse2 = rms_forward(hidden1, gain_two)
    normed2_low = normed2.astype(BF16)
    act_low, slope = wide(normed2_low, *second, piece, 2, 0, gelu_kernel, 2)
    acts = (act_low[:, : 2 * piece], act_low[:, 2 * piece :])
    hidden2 = hidden1 + narrow(acts[0], *third, piece, 1)
    hidden2 = hidden2 + narrow(acts[1], *fourth, piece, 1)
    final, inverse3 = rms_forward(hidden2, gain_three)
    local_ids = jnp.arange(sent_local, dtype=jnp.int32)
    member = (segments[:, None] == local_ids[None, :]).astype(F32)
    counts = jnp.sum(member, axis=0)
    pooled = dot(member, final, ((0,), (0,)), HIGHEST) / counts[:, None]
    pooled_low = pooled.astype(BF16)
    embed = jnp.concatenate([dot(pooled_low, pool_own_w), dot(pooled_low, pool_other_w)], axis=1)
    inverse_e = lax.rsqrt(jnp.sum(embed * embed, axis=-1, keepdims=True) + EPSILON)
    unit = embed * inverse_e
    unit_low = unit.astype(BF16)
    every = gather_dp(unit_low)

    sims = dot_nt(every, every) * SOFTMAX_TEMP
    total_sent = every.shape[0]
    position = jnp.arange(total_sent, dtype=jnp.int32)
    sims = jnp.where(position[:, None] == position[None, :], NEG_FILL, sims)
    lse_row = jax.nn.logsumexp(sims, axis=0, keepdims=True)
    own_sims = sims[:sent_local]
    own_lse = jax.nn.logsumexp(own_sims, axis=1, keepdims=True)
    column_id = (slot_block[:, None] * sent_local + local_ids[None, :]).reshape(-1)
    is_target = column_id[None, :] == partner[:, None]
    target = jnp.sum(jnp.where(is_target, own_sims, 0.0), axis=-1, keepdims=True)
    loss_local = jnp.sum(own_lse - target)
    hit = is_target.astype(F32)
    d_rows = (LOSS_SCALE * (jnp.exp(own_sims - own_lse) - hit)).astype(BF16)
    d_cols = (LOSS_SCALE * (jnp.exp(own_sims - lse_row) - hit)).astype(BF16)
    d_both = dot(jnp.concatenate([d_rows, d_cols], axis=0), every)
    d_unit = SOFTMAX_TEMP * (d_both[:sent_local] + d_both[sent_local:])
    d_embed = inverse_e * (d_unit - unit * jnp.sum(d_unit * unit, axis=-1, keepdims=True))
    embed_low = d_embed.astype(BF16)

    send_x = Lane(lambda v: hop(v, CROSS))
    send_y = Lane(over)

    def plane(kept, got, cross_first):
        return scatter_plane(kept, got, send_x, send_y, cross_first)

    pool_kept = kept_part(pooled_low, embed_low)
    pool_got = hop(sent_part(pooled_low, embed_low), CORE)
    d_pooled = dot_nt(embed_low[:, :pool_half], pool_own_w) + dot_nt(embed_low[:, pool_half:], pool_other_w)
    d_final = dot(member, d_pooled / counts[:, None], precision=HIGHEST)
    d_hidden2, d_gain3 = rms_backward(hidden2, inverse3, gain_three, d_final)
    ffn_low = d_hidden2.astype(BF16)

    back_got = [hop(sent_part(ffn_low, part), CORE) for part in acts]
    back_kept = [kept_part(ffn_low, part) for part in acts]
    pool_value = plane(pool_kept, pool_got, True)
    ffn_later = after(ffn_low, *back_kept)
    slopes = (slope[:, : 2 * piece], slope[:, 2 * piece :])
    ups = [
        wide(ffn_later, *weights, piece, 1, 0, slope_kernel, 1, (part,))
        for weights, part in zip((third, fourth), slopes)
    ]
    ups = [after(part, *back_got) for part in ups]
    back_value = [plane(k, g, first_x) for k, g, first_x in zip(back_kept, back_got, (True, False))]

    in_got = [hop(sent_part(normed2_low, part), CORE) for part in ups]
    in_kept = [kept_part(normed2_low, part) for part in ups]
    up_later = after(jnp.concatenate(ups, axis=1), *in_kept)
    d_normed2 = narrow(up_later, *second, piece, 2)
    d_part2, d_gain2 = rms_backward(hidden1, inverse2, gain_two, d_normed2)
    d_hidden1 = d_hidden2 + d_part2
    attn_low = after(d_hidden1.astype(BF16), *in_got)
    out_got = hop(sent_part(attn_low, context), CORE)
    out_kept = kept_part(attn_low, context)
    in_value = [plane(k, g, first_x) for k, g, first_x in zip(in_kept, in_got, (True, False))]
    d_context = wide(after(attn_low, out_kept), *second, inner_half, 1, out_at)
    d_context = after(d_context, out_got, send_x.got[1], send_y.got[1])
    d_query, d_key, d_value, d_bias = attend_backward(qkv, d_context, probs)
    d_heads = (d_query, d_key, d_value)
    qkv_got = [hop(sent_part(normed1_low, part), CORE) for part in d_heads]
    qkv_kept = [kept_part(normed1_low, part) for part in d_heads]
    out_value = plane(out_kept, out_got, True)
    back_sum = scatter_rest(jnp.concatenate(back_value + [pool_value], axis=1))
    grad_back = back_sum[:, :hidden_half]
    grad_pool = back_sum[:, hidden_half:]
    d_heads_all = after(jnp.concatenate(d_heads, axis=1), *qkv_kept)
    d_normed1 = narrow(d_heads_all, *first, inner_half, 3)
    qkv_value = [plane(k, g, first_x) for k, g, first_x in zip(qkv_kept, qkv_got, (True, False, True))]
    in_sum = scatter_rest(jnp.concatenate(in_value + [out_value], axis=1))
    grad_in = in_sum[:, :hidden_half]
    grad_out = in_sum[:, hidden_half:]
    grad_qkv = scatter_rest(jnp.concatenate(qkv_value, axis=1))
    d_part1, d_gain1 = rms_backward(inputs, inverse1, gain_one, d_normed1)
    grad_slots = (d_hidden1 + d_part1).astype(BF16)
    grad_own = dot_nt(grad_slots, order).astype(BF16)
    grad_other = over(grad_own)
    grad_tokens = jnp.where(
        mine == 0, jnp.stack([grad_own, grad_other]), jnp.stack([grad_other, grad_own])
    )

    d_table = dot(onehot, d_bias[:, :2].reshape(2 * heads_half, WIN), ((1,), (1,)), HIGHEST)
    table_own, table_other = d_table[:, :heads_half], d_table[:, heads_half:]
    table_abs = jnp.where(
        mine == 0,
        jnp.concatenate([table_own, table_other], axis=1),
        jnp.concatenate([table_other, table_own], axis=1),
    )
    d_gains = dot(jnp.stack([d_gain1, d_gain2, d_gain3]), order.astype(F32), ((1,), (1,)), HIGHEST)
    flat = jnp.concatenate([d_gains.reshape(-1), table_abs.reshape(-1), loss_local.reshape(1)])
    flat = jnp.pad(flat, (0, -flat.shape[0] % (8 * LANES))).reshape(-1, LANES)
    flat = flat + over(flat)
    flat = flat + hop(flat, CORE)
    flat = flat + hop(flat, CROSS)
    for stride in strides(size):
        flat = flat + hop(flat, stride)
    flat = flat.reshape(-1)
    gains_sum = flat[: 3 * width].reshape(3, width)
    gains_mine = lax.dynamic_slice_in_dim(gains_sum, me * block, block, axis=1)
    table_sum = flat[3 * width : 3 * width + table_abs.size].reshape(table_abs.shape)
    table_mine = lax.dynamic_slice_in_dim(table_sum, mine * heads_half, heads_half, axis=1)
    loss = flat[3 * width + table_abs.size] / (micro_count * sent_local * size)

    pool_other = over(grad_pool)
    grad_pool = jnp.where(
        mine == 0,
        jnp.concatenate([grad_pool, pool_other], axis=1),
        jnp.concatenate([pool_other, grad_pool], axis=1),
    )
    return (
        loss,
        grad_tokens,
        grad_qkv[:, :inner_half],
        grad_qkv[:, inner_half : 2 * inner_half],
        grad_qkv[:, 2 * inner_half :],
        grad_out.T,
        grad_in,
        grad_back.T,
        gains_mine[0],
        gains_mine[1],
        gains_mine[2],
        grad_pool,
        table_mine,
    )


def solution(mesh):
    placed = (
        P(None, "dp", None),
        P(None, "dp", None),
        P(),
        P(None, "dp"),
        P("dp", "mp"),
        P("dp", "mp"),
        P("dp", "mp"),
        P("mp", "dp"),
        P("dp", "mp"),
        P("mp", "dp"),
        P("dp"),
        P("dp"),
        P("dp"),
        P("dp", None),
        P(None, "mp"),
    )
    return jax.shard_map(
        shards,
        mesh=mesh,
        in_specs=placed,
        out_specs=(
            P(),
            P(None, "dp", None),
            P("dp", "mp"),
            P("dp", "mp"),
            P("dp", "mp"),
            P("mp", "dp"),
            P("dp", "mp"),
            P("mp", "dp"),
            P("dp"),
            P("dp"),
            P("dp"),
            P("dp", None),
            P(None, "mp"),
        ),
        check_vma=False,
    )
```

```python
import functools

import jax
import jax.numpy as jnp
from jax import lax
from jax.experimental import pallas as pl
from jax.experimental.pallas import tpu as pltpu
from jax.sharding import PartitionSpec as P

NEG_FILL = -1000000000.0
SCORE_SCALE = 0.125
SOFTMAX_TEMP = 50.0
LOSS_SCALE = 64.0
EPSILON = 1e-06
REACH = 32
QB = 64
WIN = QB + 2 * REACH
LANES = 128
GELU_A = 0.7978845608028654
GELU_B = 0.044715

BF16 = jnp.bfloat16
F32 = jnp.float32
HIGHEST = lax.Precision.HIGHEST


def dot(left, right, dims=((1,), (0,)), precision=None):
    return lax.dot_general(
        left, right, (dims, ((), ())), precision=precision, preferred_element_type=F32
    )


def dot_nt(left, right):
    return dot(left, right, ((1,), (1,)))


def dot_tn(left, right):
    return dot(left, right, ((0,), (0,)))


def rms_forward(value, gain):
    inverse = lax.rsqrt(jnp.mean(value * value, axis=-1, keepdims=True) + EPSILON)
    return (value * inverse * gain, inverse)


def rms_backward(value, inverse, gain, grad):
    scaled = grad * gain
    inner_prod = jnp.mean(value * scaled, axis=-1, keepdims=True)
    d_value = inverse * scaled - value * (inverse * inverse * inverse) * inner_prod
    d_gain = jnp.sum(grad * value * inverse, axis=0)
    return (d_value, d_gain)


def cost(flops, bytes_accessed):
    return pl.CostEstimate(flops=0, bytes_accessed=0, transcendentals=0)


def params(mib=48):
    return pltpu.CompilerParams(vmem_limit_bytes=mib * 2**20)


def wide_kernel(x_ref, own_ref, other_ref, out_ref):
    half = own_ref.shape[1]
    x = x_ref[...]
    out_ref[:, :half] = dot(x, own_ref[...]).astype(out_ref.dtype)
    out_ref[:, half:] = dot(x, other_ref[...]).astype(out_ref.dtype)


def gelu_kernel(x_ref, own_ref, other_ref, act_ref, slope_ref):
    half = own_ref.shape[1]
    x = x_ref[...]
    for side, ref in enumerate((own_ref, other_ref)):
        here = slice(side * half, (side + 1) * half)
        up = dot(x, ref[...])
        square = up * up
        bend = jnp.tanh(GELU_A * up * (1.0 + GELU_B * square))
        half_one = 0.5 + 0.5 * bend
        act_ref[:, here] = (up * half_one).astype(BF16)
        inner = GELU_A + (3.0 * GELU_A * GELU_B) * square
        slope_ref[:, here] = (half_one + 0.5 * up * (1.0 - bend * bend) * inner).astype(BF16)


def slope_kernel(x_ref, own_ref, other_ref, slope_ref, out_ref):
    half = own_ref.shape[1]
    x = x_ref[...]
    for side, ref in enumerate((own_ref, other_ref)):
        here = slice(side * half, (side + 1) * half)
        out_ref[:, here] = (dot(x, ref[...]) * slope_ref[:, here].astype(F32)).astype(BF16)


def _weight_spec(rows, n, first):
    return pl.BlockSpec((rows, n), lambda i: (0, first + i))


def wide(x, own, other, n, count, first=0, body=wide_kernel, outs=1, extra=()):
    rows, depth = x.shape
    block = pl.BlockSpec((rows, 2 * n), lambda i: (0, i))
    shape = jax.ShapeDtypeStruct((rows, 2 * n * count), BF16)
    result = pl.pallas_call(
        body,
        grid=(count,),
        out_shape=(shape,) * outs,
        in_specs=[pl.BlockSpec(x.shape, lambda i: (0, 0))]
        + [_weight_spec(depth, n, first)] * 2
        + [block] * len(extra),
        out_specs=(block,) * outs,
        compiler_params=params(),
        cost_estimate=cost(4 * rows * depth * n * count, 4 * depth * n * count),
    )(x, own, other, *extra)
    return result if outs > 1 else result[0]


def _stack_heads(part):
    lane = lax.broadcasted_iota(jnp.int32, part.shape, 1)
    zero = jnp.zeros_like(part)
    first = lane < LANES // 2
    return jnp.concatenate(
        [jnp.where(first, part, zero), jnp.where(first, zero, part)], axis=0
    )


def _unstack_heads(both):
    half = both.shape[0] // 2
    lane = lax.broadcasted_iota(jnp.int32, (half, LANES), 1)
    return jnp.where(lane < LANES // 2, both[:half], both[half:])


def _pad_keys(pad, ref):
    seq = ref.shape[0]
    pad[0:REACH] = jnp.zeros((REACH, LANES), pad.dtype)
    pad[REACH + seq :] = jnp.zeros((REACH, LANES), pad.dtype)
    pad[REACH : REACH + seq] = ref[...]


def _query_bits(shape):
    return lax.broadcasted_iota(jnp.int32, shape, 0) & (QB - 1)


def attend_forward_kernel(
    q_ref, k_ref, v_ref, segq_ref, segk_ref, rel_ref, ctx_ref, probs_ref, kpad, vpad, mask, scores
):
    seq = q_ref.shape[0]
    blocks = seq // QB
    _pad_keys(kpad, k_ref)
    _pad_keys(vpad, v_ref)

    @pl.when(pl.program_id(0) == 0)
    def _():
        for b in range(blocks):
            same = segk_ref[b * QB : b * QB + WIN] == segq_ref[b : b + 1, :]
            mask[b] = jnp.where(same, 0.0, NEG_FILL)

    rel = rel_ref[0]
    row = lax.broadcasted_iota(jnp.int32, (2 * QB, WIN), 0)
    bias = jnp.where(row < QB, rel[0:1, :], rel[1:2, :])
    bits = _query_bits((2 * QB, WIN))
    step = 1
    while step < QB:
        bias = jnp.where((bits & step) != 0, pltpu.roll(bias, step, 1), bias)
        step *= 2
    bias = bias.T
    for b in range(blocks):
        query = _stack_heads(q_ref[b * QB : (b + 1) * QB] * jnp.asarray(SCORE_SCALE, BF16))
        scores[b] = dot_nt(kpad[b * QB : b * QB + WIN], query)
    values = scores[...] + bias[None] + mask[...]
    top = jnp.max(values, axis=1, keepdims=True)
    shifted = jnp.exp(values - top)
    total = jnp.sum(shifted, axis=1, keepdims=True)
    probs_ref[0] = (shifted * (1.0 / total)).astype(BF16)
    for b in range(blocks):
        part = dot_tn(probs_ref[0, b], vpad[b * QB : b * QB + WIN])
        ctx_ref[b * QB : (b + 1) * QB] = _unstack_heads(part).astype(BF16)


def attend_backward_kernel(
    q_ref, k_ref, v_ref, dctx_ref, probs_ref, dqkv_ref, dbias_ref,
    kpad, vpad, dk_acc, dv_acc, d_probs, d_low,
):
    seq = q_ref.shape[0]
    pair = pl.program_id(0)
    side = pl.num_programs(0) // 2
    later = pair // side
    q_at = pl.ds(pl.multiple_of(pair * LANES, LANES), LANES)
    k_at = pl.ds(pl.multiple_of((pair + 2 * side + later * side) * LANES, LANES), LANES)
    v_at = pl.ds(pl.multiple_of((pair + 3 * side + later * side) * LANES, LANES), LANES)
    blocks = seq // QB
    _pad_keys(kpad, k_ref)
    _pad_keys(vpad, v_ref)
    dk_acc[...] = jnp.zeros_like(dk_acc)
    dv_acc[...] = jnp.zeros_like(dv_acc)
    for b in range(blocks):
        window = slice(b * QB, b * QB + WIN)
        d_ctx = _stack_heads(dctx_ref[b * QB : (b + 1) * QB])
        d_probs[b] = dot_nt(vpad[window], d_ctx)
        dv_acc[window] += dot(probs_ref[0, b], d_ctx)
    probs = probs_ref[0].astype(F32)
    product = probs * d_probs[...]
    inner = jnp.sum(product, axis=1, keepdims=True)
    d_scores = product - probs * inner
    d_low[...] = d_scores.astype(BF16)
    total = jnp.sum(d_scores, axis=0).T
    for b in range(blocks):
        here = slice(b * QB, (b + 1) * QB)
        window = slice(b * QB, b * QB + WIN)
        query = _stack_heads(q_ref[here] * jnp.asarray(SCORE_SCALE, BF16))
        dk_acc[window] += dot(d_low[b], query)
        d_query = _unstack_heads(dot_tn(d_low[b], kpad[window])) * SCORE_SCALE
        dqkv_ref[here, q_at] = d_query.astype(BF16)
    dqkv_ref[:, k_at] = dk_acc[REACH : REACH + seq].astype(BF16)
    dqkv_ref[:, v_at] = dv_acc[REACH : REACH + seq].astype(BF16)
    bits = _query_bits((2 * QB, WIN))
    step = 1
    while step < QB:
        total = jnp.where((bits & step) != 0, pltpu.roll(total, WIN - step, 1), total)
        step *= 2
    first = jnp.sum(total[:QB], axis=0, keepdims=True)
    second = jnp.sum(total[QB:], axis=0, keepdims=True)
    dbias_ref[0] = jnp.concatenate([first, second, jnp.zeros((6, WIN), F32)], axis=0)


def _qkv_specs(seq, pairs):
    def spec(kind):
        return pl.BlockSpec((seq, LANES), lambda p: (0, kind * pairs + p))

    return [spec(0), spec(1), spec(2)]


def attend_forward(qkv, seg_row, rel_window):
    seq = qkv.shape[0]
    pairs = rel_window.shape[0]
    blocks = seq // QB
    padded = jnp.pad(seg_row, (REACH, REACH), constant_values=-1)[:, None]
    twice = jnp.tile(seg_row.reshape(blocks, QB), (1, 2))
    return pl.pallas_call(
        attend_forward_kernel,
        grid=(pairs,),
        out_shape=(
            jax.ShapeDtypeStruct((seq, pairs * LANES), BF16),
            jax.ShapeDtypeStruct((pairs, blocks, WIN, 2 * QB), BF16),
        ),
        in_specs=_qkv_specs(seq, pairs)
        + [
            pl.BlockSpec((blocks, 2 * QB), lambda p: (0, 0)),
            pl.BlockSpec((seq + 2 * REACH, 1), lambda p: (0, 0)),
            pl.BlockSpec((1, 2, WIN), lambda p: (p, 0, 0)),
        ],
        out_specs=(
            pl.BlockSpec((seq, LANES), lambda p: (0, p)),
            pl.BlockSpec((1, blocks, WIN, 2 * QB), lambda p: (p, 0, 0, 0)),
        ),
        scratch_shapes=[pltpu.VMEM((seq + 2 * REACH, LANES), BF16)] * 2
        + [pltpu.VMEM((blocks, WIN, 2 * QB), F32)] * 2,
        compiler_params=params(),
        cost_estimate=cost(8 * seq * WIN * LANES * pairs * 4, 8 * seq * LANES * pairs),
        name="attend_forward",
    )(qkv, qkv, qkv, twice, padded, rel_window)


def attend_backward(qkv, d_context, probs):
    seq = qkv.shape[0]
    pairs = probs.shape[0]
    blocks = seq // QB
    lane_block = pl.BlockSpec((seq, LANES), lambda p: (0, p))
    return pl.pallas_call(
        attend_backward_kernel,
        grid=(pairs,),
        out_shape=(
            jax.ShapeDtypeStruct((seq, 3 * pairs * LANES), BF16),
            jax.ShapeDtypeStruct((pairs, 8, WIN), F32),
        ),
        in_specs=_qkv_specs(seq, pairs)
        + [
            lane_block,
            pl.BlockSpec((1, blocks, WIN, 2 * QB), lambda p: (p, 0, 0, 0)),
        ],
        out_specs=(
            pl.BlockSpec((seq, 3 * pairs * LANES), lambda p: (0, 0)),
            pl.BlockSpec((1, 8, WIN), lambda p: (p, 0, 0)),
        ),
        scratch_shapes=[pltpu.VMEM((seq + 2 * REACH, LANES), BF16)] * 2
        + [pltpu.VMEM((seq + 2 * REACH, LANES), F32)] * 2
        + [pltpu.VMEM((blocks, WIN, 2 * QB), F32), pltpu.VMEM((blocks, WIN, 2 * QB), BF16)],
        compiler_params=params(),
        cost_estimate=cost(16 * seq * WIN * LANES * pairs * 4, 16 * seq * LANES * pairs),
        name="attend_backward",
    )(qkv, qkv, qkv, d_context, probs)


CORE = 1
CROSS = 2


def hop(value, mask):
    size = lax.axis_size("dp")
    return lax.ppermute(value, "dp", [(i, i ^ mask) for i in range(size)])


def over(value):
    return lax.ppermute(value, "mp", [(0, 1), (1, 0)])


def cross(value):
    return hop(value, CROSS)


def core(value):
    return hop(value, CORE)


def go(waits, *sends):
    values = [value for _, value in sends]
    held = lax.optimization_barrier((*values, *waits))
    return [how(value) for (how, _), value in zip(sends, held)]


def slot_masks(size):
    rest = size // 4
    return [z * 4 + x * 2 + c for c in range(2) for x in range(2) for z in range(rest)]


def strides(size):
    found = []
    stride = 4
    while stride < size:
        found.append(stride)
        stride *= 2
    return found


def step_one(value):
    return hop(value, 4) if lax.axis_size("dp") > 4 else value[:0]


def step_more(pieces):
    start = pieces.shape[0]
    for stride in strides(lax.axis_size("dp"))[1:]:
        pieces = jnp.concatenate([pieces, hop(pieces, stride)], axis=0)
    return pieces[start:]


def rows(*pieces):
    return jnp.concatenate(pieces, axis=0)


def columns(*pieces):
    return jnp.concatenate(pieces, axis=1)


def gather_weights(one, two, three):
    n_two = two.shape[1]
    (z1,) = go((), (step_one, one))
    one = rows(one, z1)
    z2, z1 = go((z1,), (step_more, one), (step_one, columns(two, three)))
    one = rows(one, z2)
    two = rows(two, z1[:, :n_two])
    three = rows(three, z1[:, n_two:])
    one_x, one_y, z_two = go((z2, z1), (cross, one), (over, one), (step_more, two))
    one_own = rows(one, one_x)
    two = rows(two, z_two)
    one_xy, z_three, one_core = go((one_x, one_y), (over, one_x), (step_more, three), (core, one_own))
    one_other = rows(one_y, one_xy)
    two_x, two_y, one_other_core = go(
        (one_xy, z_two, one_core), (cross, two), (over, two), (core, one_other)
    )
    three = rows(three, z_three)
    two_own = rows(two, two_x)
    two_xy, three_x, two_core = go(
        (two_x, two_y, z_three, one_other_core), (over, two_x), (cross, three), (core, two_own)
    )
    two_other = rows(two_y, two_xy)
    three_own = rows(three, three_x)
    three_y, three_xy, two_other_core, three_core = go(
        (two_xy, three_x, two_core),
        (over, three),
        (over, three_x),
        (core, two_other),
        (core, three_own),
    )
    three_other = rows(three_y, three_xy)
    (three_other_core,) = go((three_y, three_xy), (core, three_other))
    return (
        (rows(one_own, one_core), rows(one_other, one_other_core)),
        (rows(two_own, two_core), rows(two_other, two_other_core)),
        (rows(three_own, three_core), rows(three_other, three_other_core)),
    )


def gather_dp(shard):
    size = lax.axis_size("dp")
    pieces = shard
    stride = 4
    while stride < size:
        radix = min(4, size // stride)
        pieces = jnp.concatenate(
            [pieces] + [hop(pieces, j * stride) for j in range(1, radix)], axis=0
        )
        stride *= radix
    side = hop(pieces, CROSS)
    return jnp.concatenate([pieces, side, hop(pieces, CORE), hop(side, CORE)], axis=0)


def low(value):
    return value.astype(BF16)


def add(left, right):
    return (left.astype(F32) + right.astype(F32)).astype(BF16)


def product(left, begin, end, right, got=None):
    value = dot_tn(left[:, begin:end], right)
    if got is not None:
        value = value + got.astype(F32)
    return low(value)


def rest_start(value):
    half = value.shape[0] // 2
    return value[half:], value[:half]


def sum_half(value, send):
    gone, stays = rest_start(value)
    return stays + send(low(gone)).astype(F32)


def rest_hops(size):
    return [functools.partial(hop, mask=stride) for stride in reversed(strides(size))]


def shards(
    tokens,
    seg_ids,
    buckets,
    labels,
    w_query,
    w_key,
    w_value,
    w_out,
    w_in,
    w_back,
    gain_attn,
    gain_ffn,
    gain_final,
    w_pool,
    rel_table,
):
    micro_count, seq, width = tokens.shape
    size = lax.axis_size("dp")
    me = lax.axis_index("dp")
    mine = lax.axis_index("mp")
    block = width // size
    inner_half = w_query.shape[1]
    hidden_half = w_in.shape[1]
    sent_local = labels.shape[1]
    bucket_count = rel_table.shape[0]
    heads_half = rel_table.shape[1]
    masks = slot_masks(size)

    x_own = lax.dynamic_index_in_dim(tokens, mine, 0, keepdims=False)
    segments = lax.dynamic_index_in_dim(seg_ids, mine, 0, keepdims=False)[0]
    partner = lax.dynamic_index_in_dim(labels, mine, 0, keepdims=False)

    gains_col = jnp.pad(
        jnp.stack([gain_attn, gain_ffn, gain_final], axis=1), ((0, 0), (0, LANES - 3))
    )
    pool_half = w_pool.shape[1] // 2
    pool_own = lax.dynamic_slice_in_dim(w_pool, mine * pool_half, pool_half, axis=1)
    piece = hidden_half // 2
    first, second, third = gather_weights(
        columns(w_query, w_key, w_value, gains_col),
        columns(w_in, w_out.T),
        columns(w_back.T, pool_own),
    )
    heads = 3 * inner_half
    pool_w = [part[:, hidden_half:] for part in third]
    out_w = [part[:, hidden_half:] for part in second]
    gains = first[0][:, 3 * inner_half : 3 * inner_half + 3].T.astype(F32)
    gain_one, gain_two, gain_three = gains[0:1], gains[1:2], gains[2:3]

    slot_block = jnp.stack([jnp.bitwise_xor(me, m) for m in masks]).astype(jnp.int32)
    source = (slot_block[:, None] * block + jnp.arange(block, dtype=jnp.int32)[None, :]).reshape(-1)
    order = (jnp.arange(width, dtype=jnp.int32)[:, None] == source[None, :]).astype(BF16)
    inputs = dot(x_own, order)

    rel_all = jnp.concatenate([rel_table, over(rel_table)], axis=1).astype(F32)
    near_buckets = lax.slice_in_dim(buckets, seq - 1 - REACH, seq - 1 - REACH + WIN)
    onehot = (near_buckets[None, :] == jnp.arange(bucket_count, dtype=jnp.int32)[:, None]).astype(F32)
    rel_window = dot(rel_all, onehot, ((0,), (0,)), HIGHEST).reshape(heads_half, 2, WIN)

    normed1, inverse1 = rms_forward(inputs, gain_one)
    normed1_low = normed1.astype(BF16)
    qkv = wide(normed1_low, *first, inner_half, 3)
    context, probs = attend_forward(qkv, segments, rel_window)
    attn = sum(dot_nt(context[:, i * inner_half : (i + 1) * inner_half], out_w[i]) for i in range(2))
    hidden1 = inputs + attn
    normed2, inverse2 = rms_forward(hidden1, gain_two)
    normed2_low = normed2.astype(BF16)
    act_low, slope = wide(normed2_low, *second, piece, 2, 0, gelu_kernel, 2)

    def by_piece(value, weights):
        return sum(
            dot_nt(
                value[:, (2 * i + side) * piece : (2 * i + side + 1) * piece],
                weights[side][:, i * piece : (i + 1) * piece],
            )
            for i in range(2)
            for side in range(2)
        )

    hidden2 = hidden1 + by_piece(act_low, third)
    final, inverse3 = rms_forward(hidden2, gain_three)
    local_ids = jnp.arange(sent_local, dtype=jnp.int32)
    member = (segments[:, None] == local_ids[None, :]).astype(F32)
    counts = jnp.sum(member, axis=0)
    pooled = dot(member, final, ((0,), (0,)), HIGHEST) / counts[:, None]
    pooled_low = pooled.astype(BF16)
    embed = columns(dot(pooled_low, pool_w[0]), dot(pooled_low, pool_w[1]))
    inverse_e = lax.rsqrt(jnp.sum(embed * embed, axis=-1, keepdims=True) + EPSILON)
    unit = embed * inverse_e
    unit_low = unit.astype(BF16)
    every = gather_dp(unit_low)

    sims = dot_nt(every, every) * SOFTMAX_TEMP
    total_sent = every.shape[0]
    position = jnp.arange(total_sent, dtype=jnp.int32)
    sims = jnp.where(position[:, None] == position[None, :], NEG_FILL, sims)
    lse_row = jax.nn.logsumexp(sims, axis=0, keepdims=True)
    own_sims = sims[:sent_local]
    own_lse = jax.nn.logsumexp(own_sims, axis=1, keepdims=True)
    column_id = (slot_block[:, None] * sent_local + local_ids[None, :]).reshape(-1)
    is_target = column_id[None, :] == partner[:, None]
    target = jnp.sum(jnp.where(is_target, own_sims, 0.0), axis=-1, keepdims=True)
    loss_local = jnp.sum(own_lse - target)
    hit = is_target.astype(F32)
    d_rows = (LOSS_SCALE * (jnp.exp(own_sims - own_lse) - hit)).astype(BF16)
    d_cols = (LOSS_SCALE * (jnp.exp(own_sims - lse_row) - hit)).astype(BF16)
    d_both = dot(jnp.concatenate([d_rows, d_cols], axis=0), every)
    d_unit = SOFTMAX_TEMP * (d_both[:sent_local] + d_both[sent_local:])
    d_embed = inverse_e * (d_unit - unit * jnp.sum(d_unit * unit, axis=-1, keepdims=True))
    embed_low = d_embed.astype(BF16)

    half = width // 2
    quarter = width // 4
    both = 2 * piece
    d_pooled = dot_nt(embed_low[:, :pool_half], pool_w[0]) + dot_nt(embed_low[:, pool_half:], pool_w[1])
    d_final = dot(member, d_pooled / counts[:, None], precision=HIGHEST)
    d_hidden2, d_gain3 = rms_backward(hidden2, inverse3, gain_three, d_final)
    ffn_low = low(d_hidden2)

    pool_sent = product(pooled_low, half, width, embed_low)
    back_sent = product(ffn_low, half, width, act_low)
    pool_got, back_got = go((), (core, pool_sent), (core, back_sent))
    up_low = wide(
        lax.optimization_barrier((ffn_low, back_sent))[0], *third, piece, 2, 0, slope_kernel, 1, (slope,)
    )
    in_sent = product(normed2_low, half, width, up_low)

    pool_hi = product(pooled_low, quarter, half, embed_low, pool_got[quarter:])
    pool_lo = product(pooled_low, 0, quarter, embed_low, pool_got[:quarter])
    back_hi = product(ffn_low, quarter, half, act_low[:, :both], back_got[quarter:, :both])
    back_lo = product(ffn_low, 0, quarter, act_low[:, :both], back_got[:quarter, :both])
    back_own = product(ffn_low, 0, half, act_low[:, both : both + piece], back_got[:, both : both + piece])
    back_oth = product(ffn_low, 0, half, act_low[:, both + piece :], back_got[:, both + piece :])
    got_pool, got_lo, got_own, in_got = go(
        (up_low, pool_got, back_got),
        (cross, pool_hi),
        (cross, back_hi),
        (over, back_oth),
        (core, in_sent),
    )
    d_normed2 = by_piece(lax.optimization_barrier((up_low, in_sent))[0], second)
    d_part2, d_gain2 = rms_backward(hidden1, inverse2, gain_two, d_normed2)
    d_hidden1 = d_hidden2 + d_part2
    attn_low = low(d_hidden1)

    pool_lo = add(pool_lo, got_pool)
    back_lo = add(back_lo, got_lo)
    back_own = add(back_own, got_own)
    in_hi = product(normed2_low, quarter, half, up_low[:, :both], in_got[quarter:, :both])
    in_lo = product(normed2_low, 0, quarter, up_low[:, :both], in_got[:quarter, :both])
    in_own = product(normed2_low, 0, half, up_low[:, both : both + piece], in_got[:, both : both + piece])
    in_oth = product(normed2_low, 0, half, up_low[:, both + piece :], in_got[:, both + piece :])
    got_first, got_second, got_in_lo, got_in_own = go(
        (attn_low, got_pool, got_lo, got_own, in_got),
        (over, columns(back_lo[:, piece:], pool_lo[:, pool_half:])),
        (cross, back_own[quarter:]),
        (cross, in_hi),
        (over, in_oth),
    )
    d_context = low(
        columns(*(dot(lax.optimization_barrier((attn_low, in_lo))[0], part) for part in out_w))
    )
    d_qkv, d_bias = attend_backward(qkv, d_context, probs)

    back_all = columns(
        add(back_lo[:, :piece], got_first[:, :piece]),
        add(back_own[:quarter], got_second),
        add(pool_lo[:, :pool_half], got_first[:, piece:]),
    )
    in_lo = add(in_lo, got_in_lo)
    in_own = add(in_own, got_in_own)
    back_rest, back_stay = rest_start(back_all)
    far = rest_hops(size)
    out_sent = product(attn_low, half, width, context)
    qkv_sent = product(normed1_low, half, width, d_qkv)
    back_more, got_first, got_second, out_got, qkv_got = go(
        (d_qkv, got_first, got_second, got_in_lo, got_in_own),
        (far[0], back_rest),
        (over, in_lo[:, piece:]),
        (cross, in_own[quarter:]),
        (core, out_sent),
        (core, qkv_sent),
    )
    d_late = lax.optimization_barrier((d_qkv, qkv_sent))[0]
    query_both = 2 * inner_half
    d_normed1 = (
        dot_nt(d_late[:, :inner_half], first[0][:, :inner_half])
        + dot_nt(d_late[:, inner_half:query_both], first[1][:, :inner_half])
        + dot_nt(d_late[:, query_both : 2 * query_both], first[0][:, inner_half:heads])
        + dot_nt(d_late[:, 2 * query_both :], first[1][:, inner_half:heads])
    )

    back_all = add(back_stay, back_more)
    in_all = columns(add(in_lo[:, :piece], got_first), add(in_own[:quarter], got_second))
    in_rest, in_stay = rest_start(in_all)
    out_hi = product(attn_low, quarter, half, context, out_got[quarter:])
    out_lo = product(attn_low, 0, quarter, context, out_got[:quarter])
    query_hi = product(normed1_low, quarter, half, d_qkv[:, :query_both], qkv_got[quarter:, :query_both])
    query_lo = product(normed1_low, 0, quarter, d_qkv[:, :query_both], qkv_got[:quarter, :query_both])
    kv_own = product(
        normed1_low, 0, half, d_qkv[:, query_both : 2 * query_both], qkv_got[:, query_both : 2 * query_both]
    )
    kv_oth = product(normed1_low, 0, half, d_qkv[:, 2 * query_both :], qkv_got[:, 2 * query_both :])
    back_rest, back_stay = rest_start(back_all)
    back_more, in_more, got_out, got_query, got_kv = go(
        (back_more, got_first, got_second, out_got, qkv_got),
        (far[1], back_rest),
        (far[0], in_rest),
        (cross, out_hi),
        (cross, query_hi),
        (over, kv_oth),
    )
    d_part1, d_gain1 = rms_backward(inputs, inverse1, gain_one, d_normed1)
    grad_slots = (d_hidden1 + d_part1).astype(BF16)
    grad_own = dot_nt(grad_slots, order).astype(BF16)
    back_all = add(back_stay, back_more)
    in_all = add(in_stay, in_more)
    in_rest, in_stay = rest_start(in_all)
    out_lo = add(out_lo, got_out)
    query_lo = add(query_lo, got_query)
    kv_own = add(kv_own, got_kv)
    in_more, got_first, got_second, grad_other = go(
        (back_more, in_more, got_out, got_query, got_kv),
        (far[1], in_rest),
        (over, columns(out_lo[:, inner_half:], query_lo[:, inner_half:])),
        (cross, kv_own[quarter:]),
        (over, grad_own),
    )
    in_all = add(in_stay, in_more)
    last = columns(
        add(out_lo[:, :inner_half], got_first[:, :inner_half]),
        add(query_lo[:, :inner_half], got_first[:, inner_half:]),
        add(kv_own[:quarter], got_second),
    )
    last_rest, last_stay = rest_start(last)
    (last_more,) = go((in_more, got_first, got_second), (far[0], last_rest))
    last = add(last_stay, last_more)
    last_rest, last_stay = rest_start(last)
    (last_more,) = go((grad_other,), (far[1], last_rest))

    def finish(value):
        value = value.astype(F32)
        for send in far[2:]:
            value = sum_half(value, send)
        return value

    grad_last = finish(last_stay.astype(F32) + last_more.astype(F32))
    grad_in = finish(in_all)
    back_all = finish(back_all)
    grad_back = back_all[:, :hidden_half]
    grad_pool = back_all[:, hidden_half:]
    grad_out = grad_last[:, :inner_half]
    grad_qkv = grad_last[:, inner_half:]
    grad_tokens = jnp.where(
        mine == 0, jnp.stack([grad_own, grad_other]), jnp.stack([grad_other, grad_own])
    )

    d_table = dot(onehot, d_bias[:, :2].reshape(2 * heads_half, WIN), ((1,), (1,)), HIGHEST)
    table_own, table_other = d_table[:, :heads_half], d_table[:, heads_half:]
    table_abs = jnp.where(
        mine == 0,
        jnp.concatenate([table_own, table_other], axis=1),
        jnp.concatenate([table_other, table_own], axis=1),
    )
    d_gains = dot(jnp.stack([d_gain1, d_gain2, d_gain3]), order.astype(F32), ((1,), (1,)), HIGHEST)
    flat = jnp.concatenate([d_gains.reshape(-1), table_abs.reshape(-1), loss_local.reshape(1)])
    flat = jnp.pad(flat, (0, -flat.shape[0] % (8 * LANES))).reshape(-1, LANES)
    flat = flat + over(flat)
    flat = flat + hop(flat, CORE)
    flat = flat + hop(flat, CROSS)
    for stride in strides(size):
        flat = flat + hop(flat, stride)
    flat = flat.reshape(-1)
    gains_sum = flat[: 3 * width].reshape(3, width)
    gains_mine = lax.dynamic_slice_in_dim(gains_sum, me * block, block, axis=1)
    table_sum = flat[3 * width : 3 * width + table_abs.size].reshape(table_abs.shape)
    table_mine = lax.dynamic_slice_in_dim(table_sum, mine * heads_half, heads_half, axis=1)
    loss = flat[3 * width + table_abs.size] / (micro_count * sent_local * size)

    pool_other = over(grad_pool)
    grad_pool = jnp.where(
        mine == 0,
        jnp.concatenate([grad_pool, pool_other], axis=1),
        jnp.concatenate([pool_other, grad_pool], axis=1),
    )
    return (
        loss,
        grad_tokens,
        grad_qkv[:, :inner_half],
        grad_qkv[:, inner_half : 2 * inner_half],
        grad_qkv[:, 2 * inner_half :],
        grad_out.T,
        grad_in,
        grad_back.T,
        gains_mine[0],
        gains_mine[1],
        gains_mine[2],
        grad_pool,
        table_mine,
    )


def solution(mesh):
    placed = (
        P(None, "dp", None),
        P(None, "dp", None),
        P(),
        P(None, "dp"),
        P("dp", "mp"),
        P("dp", "mp"),
        P("dp", "mp"),
        P("mp", "dp"),
        P("dp", "mp"),
        P("mp", "dp"),
        P("dp"),
        P("dp"),
        P("dp"),
        P("dp", None),
        P(None, "mp"),
    )
    return jax.shard_map(
        shards,
        mesh=mesh,
        in_specs=placed,
        out_specs=(
            P(),
            P(None, "dp", None),
            P("dp", "mp"),
            P("dp", "mp"),
            P("dp", "mp"),
            P("mp", "dp"),
            P("dp", "mp"),
            P("mp", "dp"),
            P("dp"),
            P("dp"),
            P("dp"),
            P("dp", None),
            P(None, "mp"),
        ),
        check_vma=False,
    )
```

```python
import functools

import jax
import jax.numpy as jnp
from jax import lax
from jax.experimental import pallas as pl
from jax.experimental.pallas import tpu as pltpu
from jax.sharding import PartitionSpec as P

NEG_FILL = -1000000000.0
SCORE_SCALE = 0.125
SOFTMAX_TEMP = 50.0
LOSS_SCALE = 64.0
EPSILON = 1e-06
REACH = 32
QB = 64
WIN = QB + 2 * REACH
LANES = 128
GELU_A = 0.7978845608028654
GELU_B = 0.044715

BF16 = jnp.bfloat16
F32 = jnp.float32
HIGHEST = lax.Precision.HIGHEST


def dot(left, right, dims=((1,), (0,)), precision=None):
    return lax.dot_general(
        left, right, (dims, ((), ())), precision=precision, preferred_element_type=F32
    )


def dot_nt(left, right):
    return dot(left, right, ((1,), (1,)))


def dot_tn(left, right):
    return dot(left, right, ((0,), (0,)))


def rms_forward(value, gain):
    inverse = lax.rsqrt(jnp.mean(value * value, axis=-1, keepdims=True) + EPSILON)
    return (value * inverse * gain, inverse)


def cost(flops, bytes_accessed):
    return pl.CostEstimate(flops=0, bytes_accessed=0, transcendentals=0)


def params(mib=48):
    return pltpu.CompilerParams(vmem_limit_bytes=mib * 2**20)


def wide_kernel(x_ref, own_ref, other_ref, out_ref):
    half = own_ref.shape[1]
    x = x_ref[...]
    out_ref[:, :half] = dot(x, own_ref[...]).astype(out_ref.dtype)
    out_ref[:, half:] = dot(x, other_ref[...]).astype(out_ref.dtype)


def gelu_kernel(x_ref, own_ref, other_ref, act_ref, slope_ref):
    half = own_ref.shape[1]
    x = x_ref[...]
    for side, ref in enumerate((own_ref, other_ref)):
        here = slice(side * half, (side + 1) * half)
        up = dot(x, ref[...])
        square = up * up
        bend = jnp.tanh(GELU_A * up * (1.0 + GELU_B * square))
        half_one = 0.5 + 0.5 * bend
        act_ref[:, here] = (up * half_one).astype(BF16)
        inner = GELU_A + (3.0 * GELU_A * GELU_B) * square
        slope_ref[:, here] = (half_one + 0.5 * up * (1.0 - bend * bend) * inner).astype(BF16)


def slope_kernel(x_ref, own_ref, other_ref, slope_ref, out_ref):
    half = own_ref.shape[1]
    x = x_ref[...]
    for side, ref in enumerate((own_ref, other_ref)):
        here = slice(side * half, (side + 1) * half)
        out_ref[:, here] = (dot(x, ref[...]) * slope_ref[:, here].astype(F32)).astype(BF16)


def _weight_spec(rows, n, first):
    return pl.BlockSpec((rows, n), lambda i: (0, first + i))


def wide(x, own, other, n, count, first=0, body=wide_kernel, outs=1, extra=()):
    rows, depth = x.shape
    block = pl.BlockSpec((rows, 2 * n), lambda i: (0, i))
    shape = jax.ShapeDtypeStruct((rows, 2 * n * count), BF16)
    result = pl.pallas_call(
        body,
        grid=(count,),
        out_shape=(shape,) * outs,
        in_specs=[pl.BlockSpec(x.shape, lambda i: (0, 0))]
        + [_weight_spec(depth, n, first)] * 2
        + [block] * len(extra),
        out_specs=(block,) * outs,
        compiler_params=params(),
        cost_estimate=cost(4 * rows * depth * n * count, 4 * depth * n * count),
    )(x, own, other, *extra)
    return result if outs > 1 else result[0]


def split_dot(left, right, dims=((1,), (0,))):
    high = right.astype(BF16)
    rest = (right - high.astype(F32)).astype(BF16)
    return dot(left, high, dims) + dot(left, rest, dims)


def job_kernel(cols, operands, body, extra, outs, *refs):
    sources = refs[:operands]
    extra_refs = refs[operands : operands + extra]
    out_refs = refs[operands + extra : operands + extra + outs]
    buffers = refs[operands + extra + outs : -2]
    acc, sem = refs[-2:]
    copies = []
    for j, (x_id, x_col, w_id, w_col, n) in enumerate(cols):
        pair = []
        for side, (where, col) in enumerate(((x_id, x_col), (w_id, w_col))):
            copy = pltpu.make_async_copy(
                sources[where].at[:, pl.ds(col, n)], buffers[2 * j + side], sem.at[j, side]
            )
            copy.start()
            pair.append(copy)
        copies.append(pair)
    for j, pair in enumerate(copies):
        for copy in pair:
            copy.wait()
        part = dot_nt(buffers[2 * j][...], buffers[2 * j + 1][...])
        acc[...] = part if j == 0 else acc[...] + part
    body(acc, *extra_refs, *out_refs)


def jobs(work, body, extras, out_shapes, name):
    arrays = []

    def place(array):
        for i, known in enumerate(arrays):
            if known is array:
                return i
        arrays.append(array)
        return len(arrays) - 1

    cols = [(place(x), xc, place(w), wc, n) for x, xc, w, wc, n in work]
    rows_x, rows_w = work[0][0].shape[0], work[0][2].shape[0]
    scratch = []
    for *_, n in work:
        scratch += [pltpu.VMEM((rows_x, n), BF16), pltpu.VMEM((rows_w, n), BF16)]
    return pl.pallas_call(
        functools.partial(job_kernel, cols, len(arrays), body, len(extras), len(out_shapes)),
        out_shape=out_shapes,
        in_specs=[pl.BlockSpec(memory_space=pl.ANY)] * len(arrays)
        + [pl.BlockSpec(memory_space=pltpu.VMEM)] * len(extras),
        out_specs=tuple(pl.BlockSpec(memory_space=pltpu.VMEM) for _ in out_shapes),
        scratch_shapes=scratch
        + [pltpu.VMEM((rows_x, rows_w), F32), pltpu.SemaphoreType.DMA((len(work), 2))],
        compiler_params=params(),
        cost_estimate=cost(0, 0),
        name=name,
    )(*arrays, *extras)


def norm_body(acc, value_ref, gain_ref, hidden_ref, normed_ref, inverse_ref):
    hidden = value_ref[...] + acc[...]
    inverse = lax.rsqrt(jnp.mean(hidden * hidden, axis=1, keepdims=True) + EPSILON)
    hidden_ref[...] = hidden
    inverse_ref[...] = inverse
    normed_ref[...] = (hidden * inverse * gain_ref[...]).astype(BF16)


def norm_back(value, inverse, gain, grad):
    scaled = grad * gain
    inner = jnp.mean(value * scaled, axis=1, keepdims=True)
    d_value = inverse * scaled - value * (inverse * inverse * inverse) * inner
    return d_value, jnp.sum(grad * value * inverse, axis=0, keepdims=True)


def back_body(acc, value_ref, inverse_ref, gain_ref, grad_ref, hidden_ref, low_ref, gain_out):
    d_value, d_gain = norm_back(value_ref[...], inverse_ref[...], gain_ref[...], acc[...])
    total = grad_ref[...] + d_value
    hidden_ref[...] = total
    low_ref[...] = total.astype(BF16)
    gain_out[...] = d_gain


def tail_body(acc, value_ref, gain_ref, seg_ref, own_ref, other_ref, hidden_ref, inverse_ref, pooled_ref, unit_ref, scale_ref):
    hidden = value_ref[...] + acc[...]
    inverse = lax.rsqrt(jnp.mean(hidden * hidden, axis=1, keepdims=True) + EPSILON)
    hidden_ref[...] = hidden
    inverse_ref[...] = inverse
    final = hidden * inverse * gain_ref[...]
    sents, count = member_of(seg_ref, pooled_ref.shape[0])
    pooled = (split_dot(sents, final) / count).astype(BF16)
    pooled_ref[...] = pooled
    half = own_ref.shape[1]
    left = dot(pooled, own_ref[...])
    right = dot(pooled, other_ref[...])
    square = jnp.sum(left * left, axis=1, keepdims=True) + jnp.sum(right * right, axis=1, keepdims=True)
    scale = lax.rsqrt(square + EPSILON)
    scale_ref[...] = scale
    unit_ref[:, :half] = left * scale
    unit_ref[:, half:] = right * scale


def member_of(seg_ref, sent_count):
    ids = lax.broadcasted_iota(jnp.int32, (sent_count, seg_ref.shape[1]), 0)
    hit = jnp.where(seg_ref[...] == ids, 1.0, 0.0)
    return hit.astype(BF16), jnp.sum(hit, axis=1, keepdims=True)


def head_kernel(
    near_ref, side_ref, c_near_ref, c_side_ref, unit_ref, scale_ref, partner_ref, column_ref, seg_ref,
    own_ref, other_ref, value_ref, inverse_ref, gain_ref,
    loss_ref, embed_ref, hidden_ref, low_ref, gain_out, every,
):
    quarter = near_ref.shape[0]
    for i, ref in enumerate((near_ref, side_ref, c_near_ref, c_side_ref)):
        every[i * quarter : (i + 1) * quarter] = ref[...]
    total = every.shape[0]
    own_count = unit_ref.shape[0]
    sims = dot_nt(every[...], every[...]) * SOFTMAX_TEMP
    row = lax.broadcasted_iota(jnp.int32, (total, total), 0)
    column = lax.broadcasted_iota(jnp.int32, (total, total), 1)
    sims = jnp.where(row == column, NEG_FILL, sims)
    top = jnp.max(sims, axis=0, keepdims=True)
    lse_row = top + jnp.log(jnp.sum(jnp.exp(sims - top), axis=0, keepdims=True))
    own = sims[:own_count]
    own_top = jnp.max(own, axis=1, keepdims=True)
    own_lse = own_top + jnp.log(jnp.sum(jnp.exp(own - own_top), axis=1, keepdims=True))
    is_target = column_ref[...] == partner_ref[...]
    hit = jnp.where(is_target, 1.0, 0.0)
    target = jnp.sum(jnp.where(is_target, own, 0.0), axis=1, keepdims=True)
    loss_ref[...] = jnp.sum(own_lse - target, axis=0, keepdims=True)
    d_rows = (LOSS_SCALE * (jnp.exp(own - own_lse) - hit)).astype(BF16)
    d_cols = (LOSS_SCALE * (jnp.exp(own - lse_row) - hit)).astype(BF16)
    d_unit = SOFTMAX_TEMP * (dot(d_rows, every[...]) + dot(d_cols, every[...]))
    unit = unit_ref[...]
    inner = jnp.sum(d_unit * unit, axis=1, keepdims=True)
    d_embed = (scale_ref[...] * (d_unit - unit * inner)).astype(BF16)
    embed_ref[...] = d_embed
    sentence_back(d_embed, seg_ref, own_ref, other_ref, value_ref, inverse_ref, gain_ref, hidden_ref, low_ref, gain_out)


def sentence_kernel(embed_ref, *refs):
    sentence_back(embed_ref[...], *refs)


def sentence_back(d_embed, seg_ref, own_ref, other_ref, value_ref, inverse_ref, gain_ref, hidden_ref, low_ref, gain_out):
    half = own_ref.shape[1]
    d_pooled = dot_nt(d_embed[:, :half], own_ref[...]) + dot_nt(d_embed[:, half:], other_ref[...])
    sents, count = member_of(seg_ref, d_embed.shape[0])
    d_final = split_dot(sents, d_pooled / count, ((0,), (0,)))
    d_value, d_gain = norm_back(value_ref[...], inverse_ref[...], gain_ref[...], d_final)
    hidden_ref[...] = d_value
    low_ref[...] = d_value.astype(BF16)
    gain_out[...] = d_gain


def whole_call(body, args, out_shapes, scratch=(), name=None):
    return pl.pallas_call(
        body,
        out_shape=out_shapes,
        in_specs=[pl.BlockSpec(memory_space=pltpu.VMEM)] * len(args),
        out_specs=tuple(pl.BlockSpec(memory_space=pltpu.VMEM) for _ in out_shapes),
        scratch_shapes=scratch,
        compiler_params=params(),
        cost_estimate=cost(0, 0),
        name=name,
    )(*args)


def shape_of(kind, *dims):
    return jax.ShapeDtypeStruct(dims, kind)


def _stack_heads(part):
    lane = lax.broadcasted_iota(jnp.int32, part.shape, 1)
    zero = jnp.zeros_like(part)
    first = lane < LANES // 2
    return jnp.concatenate(
        [jnp.where(first, part, zero), jnp.where(first, zero, part)], axis=0
    )


def _unstack_heads(both):
    half = both.shape[0] // 2
    lane = lax.broadcasted_iota(jnp.int32, (half, LANES), 1)
    return jnp.where(lane < LANES // 2, both[:half], both[half:])


def _pad_keys(pad, ref):
    seq = ref.shape[0]
    pad[0:REACH] = jnp.zeros((REACH, LANES), pad.dtype)
    pad[REACH + seq :] = jnp.zeros((REACH, LANES), pad.dtype)
    pad[REACH : REACH + seq] = ref[...]


def _query_bits(shape):
    return lax.broadcasted_iota(jnp.int32, shape, 0) & (QB - 1)


def attend_forward_kernel(
    q_ref, k_ref, v_ref, segq_ref, segk_ref, rel_ref, ctx_ref, probs_ref, kpad, vpad, mask, scores
):
    seq = q_ref.shape[0]
    blocks = seq // QB
    _pad_keys(kpad, k_ref)
    _pad_keys(vpad, v_ref)

    @pl.when(pl.program_id(0) == 0)
    def _():
        for b in range(blocks):
            same = segk_ref[b * QB : b * QB + WIN] == segq_ref[b : b + 1, :]
            mask[b] = jnp.where(same, 0.0, NEG_FILL)

    rel = rel_ref[0]
    row = lax.broadcasted_iota(jnp.int32, (2 * QB, WIN), 0)
    bias = jnp.where(row < QB, rel[0:1, :], rel[1:2, :])
    bits = _query_bits((2 * QB, WIN))
    step = 1
    while step < QB:
        bias = jnp.where((bits & step) != 0, pltpu.roll(bias, step, 1), bias)
        step *= 2
    bias = bias.T
    for b in range(blocks):
        query = _stack_heads(q_ref[b * QB : (b + 1) * QB] * jnp.asarray(SCORE_SCALE, BF16))
        scores[b] = dot_nt(kpad[b * QB : b * QB + WIN], query)
    values = scores[...] + bias[None] + mask[...]
    top = jnp.max(values, axis=1, keepdims=True)
    shifted = jnp.exp(values - top)
    total = jnp.sum(shifted, axis=1, keepdims=True)
    probs_ref[0] = (shifted * (1.0 / total)).astype(BF16)
    for b in range(blocks):
        part = dot_tn(probs_ref[0, b], vpad[b * QB : b * QB + WIN])
        ctx_ref[b * QB : (b + 1) * QB] = _unstack_heads(part).astype(BF16)


def attend_backward_kernel(
    q_ref, k_ref, v_ref, dctx_ref, probs_ref, dqkv_ref, dbias_ref,
    kpad, vpad, dk_acc, dv_acc, d_probs, d_low,
):
    seq = q_ref.shape[0]
    pair = pl.program_id(0)
    side = pl.num_programs(0) // 2
    later = pair // side
    q_at = pl.ds(pl.multiple_of(pair * LANES, LANES), LANES)
    k_at = pl.ds(pl.multiple_of((pair + 2 * side + later * side) * LANES, LANES), LANES)
    v_at = pl.ds(pl.multiple_of((pair + 3 * side + later * side) * LANES, LANES), LANES)
    blocks = seq // QB
    _pad_keys(kpad, k_ref)
    _pad_keys(vpad, v_ref)
    dk_acc[...] = jnp.zeros_like(dk_acc)
    dv_acc[...] = jnp.zeros_like(dv_acc)
    for b in range(blocks):
        window = slice(b * QB, b * QB + WIN)
        d_ctx = _stack_heads(dctx_ref[b * QB : (b + 1) * QB])
        d_probs[b] = dot_nt(vpad[window], d_ctx)
        dv_acc[window] += dot(probs_ref[0, b], d_ctx)
    probs = probs_ref[0].astype(F32)
    product = probs * d_probs[...]
    inner = jnp.sum(product, axis=1, keepdims=True)
    d_scores = product - probs * inner
    d_low[...] = d_scores.astype(BF16)
    total = jnp.sum(d_scores, axis=0).T
    for b in range(blocks):
        here = slice(b * QB, (b + 1) * QB)
        window = slice(b * QB, b * QB + WIN)
        query = _stack_heads(q_ref[here] * jnp.asarray(SCORE_SCALE, BF16))
        dk_acc[window] += dot(d_low[b], query)
        d_query = _unstack_heads(dot_tn(d_low[b], kpad[window])) * SCORE_SCALE
        dqkv_ref[here, q_at] = d_query.astype(BF16)
    dqkv_ref[:, k_at] = dk_acc[REACH : REACH + seq].astype(BF16)
    dqkv_ref[:, v_at] = dv_acc[REACH : REACH + seq].astype(BF16)
    bits = _query_bits((2 * QB, WIN))
    step = 1
    while step < QB:
        total = jnp.where((bits & step) != 0, pltpu.roll(total, WIN - step, 1), total)
        step *= 2
    first = jnp.sum(total[:QB], axis=0, keepdims=True)
    second = jnp.sum(total[QB:], axis=0, keepdims=True)
    dbias_ref[0] = jnp.concatenate([first, second, jnp.zeros((6, WIN), F32)], axis=0)


def _qkv_specs(seq, pairs):
    def spec(kind):
        return pl.BlockSpec((seq, LANES), lambda p: (0, kind * pairs + p))

    return [spec(0), spec(1), spec(2)]


def attend_forward(qkv, seg_row, rel_window):
    seq = qkv.shape[0]
    pairs = rel_window.shape[0]
    blocks = seq // QB
    padded = jnp.pad(seg_row, (REACH, REACH), constant_values=-1)[:, None]
    twice = jnp.tile(seg_row.reshape(blocks, QB), (1, 2))
    return pl.pallas_call(
        attend_forward_kernel,
        grid=(pairs,),
        out_shape=(
            jax.ShapeDtypeStruct((seq, pairs * LANES), BF16),
            jax.ShapeDtypeStruct((pairs, blocks, WIN, 2 * QB), BF16),
        ),
        in_specs=_qkv_specs(seq, pairs)
        + [
            pl.BlockSpec((blocks, 2 * QB), lambda p: (0, 0)),
            pl.BlockSpec((seq + 2 * REACH, 1), lambda p: (0, 0)),
            pl.BlockSpec((1, 2, WIN), lambda p: (p, 0, 0)),
        ],
        out_specs=(
            pl.BlockSpec((seq, LANES), lambda p: (0, p)),
            pl.BlockSpec((1, blocks, WIN, 2 * QB), lambda p: (p, 0, 0, 0)),
        ),
        scratch_shapes=[pltpu.VMEM((seq + 2 * REACH, LANES), BF16)] * 2
        + [pltpu.VMEM((blocks, WIN, 2 * QB), F32)] * 2,
        compiler_params=params(),
        cost_estimate=cost(8 * seq * WIN * LANES * pairs * 4, 8 * seq * LANES * pairs),
        name="attend_forward",
    )(qkv, qkv, qkv, twice, padded, rel_window)


def attend_backward(qkv, d_context, probs):
    seq = qkv.shape[0]
    pairs = probs.shape[0]
    blocks = seq // QB
    lane_block = pl.BlockSpec((seq, LANES), lambda p: (0, p))
    return pl.pallas_call(
        attend_backward_kernel,
        grid=(pairs,),
        out_shape=(
            jax.ShapeDtypeStruct((seq, 3 * pairs * LANES), BF16),
            jax.ShapeDtypeStruct((pairs, 8, WIN), F32),
        ),
        in_specs=_qkv_specs(seq, pairs)
        + [
            lane_block,
            pl.BlockSpec((1, blocks, WIN, 2 * QB), lambda p: (p, 0, 0, 0)),
        ],
        out_specs=(
            pl.BlockSpec((seq, 3 * pairs * LANES), lambda p: (0, 0)),
            pl.BlockSpec((1, 8, WIN), lambda p: (p, 0, 0)),
        ),
        scratch_shapes=[pltpu.VMEM((seq + 2 * REACH, LANES), BF16)] * 2
        + [pltpu.VMEM((seq + 2 * REACH, LANES), F32)] * 2
        + [pltpu.VMEM((blocks, WIN, 2 * QB), F32), pltpu.VMEM((blocks, WIN, 2 * QB), BF16)],
        compiler_params=params(),
        cost_estimate=cost(16 * seq * WIN * LANES * pairs * 4, 16 * seq * LANES * pairs),
        name="attend_backward",
    )(qkv, qkv, qkv, d_context, probs)


CORE = 1
CROSS = 2


def hop(value, mask):
    size = lax.axis_size("dp")
    return lax.ppermute(value, "dp", [(i, i ^ mask) for i in range(size)])


def over(value):
    return lax.ppermute(value, "mp", [(0, 1), (1, 0)])


def cross(value):
    return hop(value, CROSS)


def core(value):
    return hop(value, CORE)


def go(waits, *sends):
    values = [value for _, value in sends]
    held = lax.optimization_barrier((*values, *waits))
    return [how(value) for (how, _), value in zip(sends, held)]


def slot_masks(size):
    rest = size // 4
    return [z * 4 + x * 2 + c for c in range(2) for x in range(2) for z in range(rest)]


def strides(size):
    found = []
    stride = 4
    while stride < size:
        found.append(stride)
        stride *= 2
    return found


def gather_near(shard, waits):
    size = lax.axis_size("dp")
    pieces = shard
    stride = 4
    while stride < size:
        radix = min(4, size // stride)
        sends = [(functools.partial(hop, mask=j * stride), pieces) for j in range(1, radix)]
        pieces = [pieces] + go(waits, *sends)
        pieces = jnp.concatenate(pieces, axis=0)
        stride *= radix
    return pieces


def rows(*pieces):
    return jnp.concatenate(pieces, axis=0)


def columns(*pieces):
    return jnp.concatenate(pieces, axis=1)


def gather_weights(one, two, three, four):
    n_one, n_three = one.shape[1], three.shape[1]
    near = gather_near(columns(one, two), ())
    one, two = near[:, :n_one], near[:, n_one:]
    later = columns(three, four)
    near = gather_near(later, (near,))
    three, four = near[:, :n_three], near[:, n_three:]
    one_x, two_y = go((), (cross, one), (over, two))
    one_own = rows(one, one_x)
    two_other_near = two_y
    one_y, one_xy, two_x, two_yx, one_core = go(
        (one_x, two_y), (over, one), (over, one_x), (cross, two), (cross, two_y), (core, one_own)
    )
    one_other = rows(one_y, one_xy)
    two_own = rows(two, two_x)
    two_other = rows(two_other_near, two_yx)
    three_x, four_y, one_other_core, two_core, two_other_core = go(
        (one_y, one_xy, two_x, two_yx, one_core, near),
        (cross, three),
        (over, four),
        (core, one_other),
        (core, two_own),
        (core, two_other),
    )
    three_own = rows(three, three_x)
    four_x, four_yx, three_y, three_xy, three_core = go(
        (three_x, four_y, one_other_core, two_core, two_other_core),
        (cross, four),
        (cross, four_y),
        (over, three),
        (over, three_x),
        (core, three_own),
    )
    four_own = rows(four, four_x)
    four_other = rows(four_y, four_yx)
    three_other = rows(three_y, three_xy)
    four_core, four_other_core, three_other_core = go(
        (four_x, four_yx, three_y, three_xy, three_core),
        (core, four_own),
        (core, four_other),
        (core, three_other),
    )
    return (
        (rows(one_own, one_core), rows(one_other, one_other_core)),
        (rows(two_own, two_core), rows(two_other, two_other_core)),
        (rows(three_own, three_core), rows(three_other, three_other_core)),
        (rows(four_own, four_core), rows(four_other, four_other_core)),
    )


def gather_dp(shard):
    near = gather_near(shard, ())
    side, c_near = go((near,), (cross, near), (core, near))
    return near, side, c_near, core(side)


def low(value):
    return value.astype(BF16)


def add(left, right):
    return (left.astype(F32) + right.astype(F32)).astype(BF16)


def product(left, begin, end, right, got=None):
    value = dot_tn(left[:, begin:end], right)
    if got is not None:
        value = value + got.astype(F32)
    return low(value)


def rest_start(value):
    half = value.shape[0] // 2
    return value[half:], value[:half]


def sum_half(value, send):
    gone, stays = rest_start(value)
    return stays + send(low(gone)).astype(F32)


def rest_hops(size):
    return [functools.partial(hop, mask=stride) for stride in reversed(strides(size))]


def shards(
    tokens,
    seg_ids,
    buckets,
    labels,
    w_query,
    w_key,
    w_value,
    w_out,
    w_in,
    w_back,
    gain_attn,
    gain_ffn,
    gain_final,
    w_pool,
    rel_table,
):
    micro_count, seq, width = tokens.shape
    size = lax.axis_size("dp")
    me = lax.axis_index("dp")
    mine = lax.axis_index("mp")
    block = width // size
    inner_half = w_query.shape[1]
    hidden_half = w_in.shape[1]
    sent_local = labels.shape[1]
    bucket_count = rel_table.shape[0]
    heads_half = rel_table.shape[1]
    masks = slot_masks(size)

    x_own = lax.dynamic_index_in_dim(tokens, mine, 0, keepdims=False)
    segments = lax.dynamic_index_in_dim(seg_ids, mine, 0, keepdims=False)[0]
    partner = lax.dynamic_index_in_dim(labels, mine, 0, keepdims=False)

    gains_col = jnp.pad(
        jnp.stack([gain_attn, gain_ffn, gain_final], axis=1), ((0, 0), (0, LANES - 3))
    )
    pool_half = w_pool.shape[1] // 2
    pool_own = lax.dynamic_slice_in_dim(w_pool, mine * pool_half, pool_half, axis=1)
    piece = hidden_half // 2
    back_shard = w_back.T
    first, second, third, fourth = gather_weights(
        columns(w_query, w_key, w_value, gains_col),
        columns(w_in[:, :piece], w_out.T),
        columns(back_shard[:, :piece], pool_own),
        columns(w_in[:, piece:], back_shard[:, piece:]),
    )
    pool_w = [part[:, piece:] for part in third]
    out_at = piece // inner_half
    gains = first[0][:, 3 * inner_half : 3 * inner_half + 3].T.astype(F32)
    gain_one, gain_two, gain_three = gains[0:1], gains[1:2], gains[2:3]

    slot_block = jnp.stack([jnp.bitwise_xor(me, m) for m in masks]).astype(jnp.int32)
    source = (slot_block[:, None] * block + jnp.arange(block, dtype=jnp.int32)[None, :]).reshape(-1)
    order = (jnp.arange(width, dtype=jnp.int32)[:, None] == source[None, :]).astype(BF16)
    inputs = dot(x_own, order)

    rel_all = jnp.concatenate([rel_table, over(rel_table)], axis=1).astype(F32)
    near_buckets = lax.slice_in_dim(buckets, seq - 1 - REACH, seq - 1 - REACH + WIN)
    onehot = (near_buckets[None, :] == jnp.arange(bucket_count, dtype=jnp.int32)[:, None]).astype(F32)
    rel_window = dot(rel_all, onehot, ((0,), (0,)), HIGHEST).reshape(heads_half, 2, WIN)

    normed1, inverse1 = rms_forward(inputs, gain_one)
    normed1_low = normed1.astype(BF16)
    qkv = wide(normed1_low, *first, inner_half, 3)
    context, probs = attend_forward(qkv, segments, rel_window)
    row_f32 = shape_of(F32, seq, width)
    row_low = shape_of(BF16, seq, width)
    column_f32 = shape_of(F32, seq, 1)
    gain_f32 = shape_of(F32, 1, width)
    hidden1, normed2_low, inverse2 = jobs(
        [(context, i * inner_half, second[i], piece, inner_half) for i in range(2)],
        norm_body,
        (inputs, gain_two),
        (row_f32, row_low, column_f32),
        "attn_out",
    )
    act0, slope0 = wide(normed2_low, *second, piece, 1, 0, gelu_kernel, 2)
    act1, slope1 = wide(normed2_low, *fourth, piece, 1, 0, gelu_kernel, 2)
    seg_lane = segments[None, :]
    hidden2, inverse3, pooled_low, unit, scale = jobs(
        [(act0, i * piece, third[i], 0, piece) for i in range(2)]
        + [(act1, i * piece, fourth[i], piece, piece) for i in range(2)],
        tail_body,
        (hidden1, gain_three, seg_lane, *pool_w),
        (
            row_f32,
            column_f32,
            shape_of(BF16, sent_local, width),
            shape_of(F32, sent_local, width),
            shape_of(F32, sent_local, 1),
        ),
        "ffn_out",
    )
    quarters = gather_dp(low(unit))

    local_ids = jnp.arange(sent_local, dtype=jnp.int32)
    column_id = (slot_block[:, None] * sent_local + local_ids[None, :]).reshape(1, -1)
    total_sent = column_id.shape[1]
    back_args = (seg_lane, *pool_w, hidden2, inverse3, gain_three)
    back_shapes = (row_f32, row_low, gain_f32)
    if total_sent <= 1024:
        loss_local, embed_low, d_hidden2, ffn_low, d_gain3 = whole_call(
            head_kernel,
            (*quarters, unit, scale, partner[:, None], column_id, *back_args),
            (shape_of(F32, 1, 1), shape_of(BF16, sent_local, width), *back_shapes),
            [pltpu.VMEM((total_sent, width), BF16)],
            "head",
        )
    else:
        every = rows(*quarters)
        position = jnp.arange(total_sent, dtype=jnp.int32)
        sims = dot_nt(every, every) * SOFTMAX_TEMP
        sims = jnp.where(position[:, None] == position[None, :], NEG_FILL, sims)
        lse_row = jax.nn.logsumexp(sims, axis=0, keepdims=True)
        own_sims = sims[:sent_local]
        own_lse = jax.nn.logsumexp(own_sims, axis=1, keepdims=True)
        is_target = column_id == partner[:, None]
        target = jnp.sum(jnp.where(is_target, own_sims, 0.0), axis=-1, keepdims=True)
        loss_local = jnp.sum(own_lse - target)
        hit = is_target.astype(F32)
        d_rows = low(LOSS_SCALE * (jnp.exp(own_sims - own_lse) - hit))
        d_cols = low(LOSS_SCALE * (jnp.exp(own_sims - lse_row) - hit))
        d_unit = SOFTMAX_TEMP * (dot(d_rows, every) + dot(d_cols, every))
        embed_low = low(scale * (d_unit - unit * jnp.sum(d_unit * unit, axis=-1, keepdims=True)))
        d_hidden2, ffn_low, d_gain3 = whole_call(
            sentence_kernel, (embed_low, *back_args), back_shapes, (), "sentence"
        )

    half = width // 2
    quarter = width // 4

    pool_sent = product(pooled_low, half, width, embed_low)
    back0_sent = product(ffn_low, half, width, act0)
    back1_sent = product(ffn_low, half, width, act1)
    pool_got, back0_got, back1_got = go((), (core, pool_sent), (core, back0_sent), (core, back1_sent))
    (ffn_later, *_) = lax.optimization_barrier((ffn_low, back0_sent, back1_sent))
    up0 = wide(ffn_later, *third, piece, 1, 0, slope_kernel, 1, (slope0,))
    up1 = wide(ffn_later, *fourth, piece, 1, 1, slope_kernel, 1, (slope1,))
    in0_sent = product(normed2_low, half, width, up0)
    in1_sent = product(normed2_low, half, width, up1)

    pool_hi = product(pooled_low, quarter, half, embed_low, pool_got[quarter:])
    pool_lo = product(pooled_low, 0, quarter, embed_low, pool_got[:quarter])
    back_hi = product(ffn_low, quarter, half, act0, back0_got[quarter:])
    back_lo = product(ffn_low, 0, quarter, act0, back0_got[:quarter])
    back_own = product(ffn_low, 0, half, act1[:, :piece], back1_got[:, :piece])
    back_oth = product(ffn_low, 0, half, act1[:, piece:], back1_got[:, piece:])
    got_pool, got_lo, got_own, in0_got, in1_got = go(
        (up0, up1, pool_lo, back_lo, back_own),
        (cross, pool_hi),
        (cross, back_hi),
        (over, back_oth),
        (core, in0_sent),
        (core, in1_sent),
    )
    up0_later, up1_later, *_ = lax.optimization_barrier((up0, up1, back_lo, back_own, in0_sent, in1_sent))
    d_hidden1, attn_low, d_gain2 = jobs(
        [(up0_later, i * piece, second[i], 0, piece) for i in range(2)]
        + [(up1_later, i * piece, fourth[i], 0, piece) for i in range(2)],
        back_body,
        (hidden1, inverse2, gain_two, d_hidden2),
        (row_f32, row_low, gain_f32),
        "ffn_in_back",
    )
    d_context = wide(attn_low, *second, inner_half, 1, out_at)
    out_sent = product(attn_low, half, width, context)

    pool_lo = add(pool_lo, got_pool)
    back_lo = add(back_lo, got_lo)
    back_own = add(back_own, got_own)
    in_hi = product(normed2_low, quarter, half, up0, in0_got[quarter:])
    in_lo = product(normed2_low, 0, quarter, up0, in0_got[:quarter])
    in_own = product(normed2_low, 0, half, up1[:, :piece], in1_got[:, :piece])
    in_oth = product(normed2_low, 0, half, up1[:, piece:], in1_got[:, piece:])
    got_first, got_second, got_in_lo, got_in_own, out_got = go(
        (d_context, got_pool, got_lo, got_own, in_lo, in_own),
        (over, columns(back_lo[:, piece:], pool_lo[:, pool_half:])),
        (cross, back_own[quarter:]),
        (cross, in_hi),
        (over, in_oth),
        (core, out_sent),
    )
    d_context_later, *_ = lax.optimization_barrier((d_context, in_lo, in_own, back_lo, back_own))
    d_qkv, d_bias = attend_backward(qkv, d_context_later, probs)
    query_both = 2 * inner_half
    _, grad_slots, d_gain1 = jobs(
        [(d_qkv, i * inner_half, first[i], 0, inner_half) for i in range(2)]
        + [(d_qkv, (1 + i) * query_both, first[i], inner_half, query_both) for i in range(2)],
        back_body,
        (inputs, inverse1, gain_one, d_hidden1),
        (row_f32, row_low, gain_f32),
        "qkv_back",
    )
    qkv_sent = product(normed1_low, half, width, d_qkv)
    d_table = dot(onehot, d_bias[:, :2].reshape(2 * heads_half, WIN), ((1,), (1,)), HIGHEST)
    table_own, table_other = d_table[:, :heads_half], d_table[:, heads_half:]
    table_abs = jnp.where(mine == 0, columns(table_own, table_other), columns(table_other, table_own))
    d_gains = dot(rows(d_gain1, d_gain2, d_gain3), order.astype(F32), ((1,), (1,)), HIGHEST)
    flat = jnp.concatenate([d_gains.reshape(-1), table_abs.reshape(-1), loss_local.reshape(1)])
    flat = jnp.pad(flat, (0, -flat.shape[0] % (8 * LANES))).reshape(-1, LANES)

    far = rest_hops(size)
    back_all = columns(
        add(back_lo[:, :piece], got_first[:, :piece]),
        add(back_own[:quarter], got_second),
        add(pool_lo[:, :pool_half], got_first[:, piece:]),
    )
    back_rest, back_stay = rest_start(back_all)
    in_lo = add(in_lo, got_in_lo)
    in_own = add(in_own, got_in_own)
    back_more, got_first, got_second, qkv_got, flat_got = go(
        (qkv_sent, grad_slots, back_stay, in_lo, in_own, out_got),
        (far[0], back_rest),
        (over, in_lo[:, piece:]),
        (cross, in_own[quarter:]),
        (core, qkv_sent),
        (over, flat),
    )
    flat = flat + flat_got
    grad_own = low(dot_nt(lax.optimization_barrier((grad_slots, back_stay, in_lo, in_own))[0], order))

    back_all = add(back_stay, back_more)
    back_rest, back_stay = rest_start(back_all)
    in_all = columns(add(in_lo[:, :piece], got_first), add(in_own[:quarter], got_second))
    in_rest, in_stay = rest_start(in_all)
    out_hi = product(attn_low, quarter, half, context, out_got[quarter:])
    out_lo = product(attn_low, 0, quarter, context, out_got[:quarter])
    query_hi = product(normed1_low, quarter, half, d_qkv[:, :query_both], qkv_got[quarter:, :query_both])
    query_lo = product(normed1_low, 0, quarter, d_qkv[:, :query_both], qkv_got[:quarter, :query_both])
    kv_own = product(
        normed1_low, 0, half, d_qkv[:, query_both : 2 * query_both], qkv_got[:, query_both : 2 * query_both]
    )
    kv_oth = product(normed1_low, 0, half, d_qkv[:, 2 * query_both :], qkv_got[:, 2 * query_both :])
    back_more, in_more, got_query, got_kv, flat_got = go(
        (back_stay, in_stay, out_lo, query_lo, kv_own, grad_own),
        (far[1], back_rest),
        (far[0], in_rest),
        (cross, columns(out_hi, query_hi)),
        (over, kv_oth),
        (core, flat),
    )
    flat = flat + flat_got

    back_all = add(back_stay, back_more)
    in_all = add(in_stay, in_more)
    in_rest, in_stay = rest_start(in_all)
    out_lo = add(out_lo, got_query[:, :query_both])
    query_lo = add(query_lo, got_query[:, query_both:])
    kv_own = add(kv_own, got_kv)
    in_more, got_first, got_second, grad_other, flat_got = go(
        (back_all, in_stay, out_lo, query_lo, kv_own),
        (far[1], in_rest),
        (over, columns(out_lo[:, inner_half:], query_lo[:, inner_half:])),
        (cross, kv_own[quarter:]),
        (over, grad_own),
        (cross, flat),
    )
    flat = flat + flat_got

    def finish(value):
        value = value.astype(F32)
        for send in far[2:]:
            value = sum_half(value, send)
        return value

    back_all = finish(back_all)
    grad_back = back_all[:, :hidden_half]
    grad_pool = back_all[:, hidden_half:]
    last = columns(
        add(out_lo[:, :inner_half], got_first[:, :inner_half]),
        add(query_lo[:, :inner_half], got_first[:, inner_half:]),
        add(kv_own[:quarter], got_second),
    )
    last_rest, last_stay = rest_start(last)
    last_more, flat_got, pool_other = go(
        (in_more, last_stay, flat_got), (far[0], last_rest), (far[1], flat), (over, grad_pool)
    )
    flat = flat + flat_got

    last = add(last_stay, last_more)
    last_rest, last_stay = rest_start(last)
    last_more, flat_got = go((grad_other, last_stay, flat), (far[1], last_rest), (far[0], flat))
    flat = flat + flat_got
    for send in far[2:]:
        flat = flat + send(flat)
    grad_last = finish(last_stay.astype(F32) + last_more.astype(F32))
    grad_in = finish(in_stay.astype(F32) + in_more.astype(F32))
    grad_out = grad_last[:, :inner_half]
    grad_qkv = grad_last[:, inner_half:]
    grad_tokens = jnp.where(
        mine == 0, jnp.stack([grad_own, grad_other]), jnp.stack([grad_other, grad_own])
    )
    flat = flat.reshape(-1)
    gains_sum = flat[: 3 * width].reshape(3, width)
    gains_mine = lax.dynamic_slice_in_dim(gains_sum, me * block, block, axis=1)
    table_sum = flat[3 * width : 3 * width + table_abs.size].reshape(table_abs.shape)
    table_mine = lax.dynamic_slice_in_dim(table_sum, mine * heads_half, heads_half, axis=1)
    loss = flat[3 * width + table_abs.size] / (micro_count * sent_local * size)

    grad_pool = jnp.where(
        mine == 0,
        jnp.concatenate([grad_pool, pool_other], axis=1),
        jnp.concatenate([pool_other, grad_pool], axis=1),
    )
    return (
        loss,
        grad_tokens,
        grad_qkv[:, :inner_half],
        grad_qkv[:, inner_half : 2 * inner_half],
        grad_qkv[:, 2 * inner_half :],
        grad_out.T,
        grad_in,
        grad_back.T,
        gains_mine[0],
        gains_mine[1],
        gains_mine[2],
        grad_pool,
        table_mine,
    )


def solution(mesh):
    placed = (
        P(None, "dp", None),
        P(None, "dp", None),
        P(),
        P(None, "dp"),
        P("dp", "mp"),
        P("dp", "mp"),
        P("dp", "mp"),
        P("mp", "dp"),
        P("dp", "mp"),
        P("mp", "dp"),
        P("dp"),
        P("dp"),
        P("dp"),
        P("dp", None),
        P(None, "mp"),
    )
    return jax.shard_map(
        shards,
        mesh=mesh,
        in_specs=placed,
        out_specs=(
            P(),
            P(None, "dp", None),
            P("dp", "mp"),
            P("dp", "mp"),
            P("dp", "mp"),
            P("mp", "dp"),
            P("dp", "mp"),
            P("mp", "dp"),
            P("dp"),
            P("dp"),
            P("dp"),
            P("dp", None),
            P(None, "mp"),
        ),
        check_vma=False,
    )
```

```python
import functools

import jax
import jax.numpy as jnp
from jax import lax
from jax.experimental import pallas as pl
from jax.experimental.pallas import tpu as pltpu
from jax.sharding import PartitionSpec as P

NEG_FILL = -1000000000.0
SCORE_SCALE = 0.125
SOFTMAX_TEMP = 50.0
LOSS_SCALE = 64.0
EPSILON = 1e-06
REACH = 32
QB = 64
WIN = QB + 2 * REACH
LANES = 128
GELU_A = 0.7978845608028654
GELU_B = 0.044715

BF16 = jnp.bfloat16
F32 = jnp.float32
HIGHEST = lax.Precision.HIGHEST


def dot(left, right, dims=((1,), (0,)), precision=None):
    return lax.dot_general(
        left, right, (dims, ((), ())), precision=precision, preferred_element_type=F32
    )


def dot_nt(left, right):
    return dot(left, right, ((1,), (1,)))


def dot_tn(left, right):
    return dot(left, right, ((0,), (0,)))


def rms_forward(value, gain):
    inverse = lax.rsqrt(jnp.mean(value * value, axis=-1, keepdims=True) + EPSILON)
    return (value * inverse * gain, inverse)


def cost(flops, bytes_accessed):
    return pl.CostEstimate(flops=0, bytes_accessed=0, transcendentals=0)


def params(mib=48):
    return pltpu.CompilerParams(vmem_limit_bytes=mib * 2**20)


def split_dot(left, right, dims=((1,), (0,))):
    high = right.astype(BF16)
    rest = (right - high.astype(F32)).astype(BF16)
    return dot(left, high, dims) + dot(left, rest, dims)


def stream_kernel(plan, operands, outs, body, *refs):
    sources, out_refs = refs[:operands], refs[operands : operands + outs]
    buffers = refs[operands + outs : operands + outs + len(plan)]
    more, sem = refs[operands + outs + len(plan) : -1], refs[-1]
    copies = []
    for load, buffer in zip(plan, buffers):
        group = []
        for which, at, count, col, width, number in load:
            copy = pltpu.make_async_copy(
                sources[which].at[:, pl.ds(col, width)], buffer.at[pl.ds(at, count)], sem.at[number]
            )
            copy.start()
            group.append(copy)
        copies.append(group)
    ready = set()

    def get(i):
        if i not in ready:
            ready.add(i)
            for copy in copies[i]:
                copy.wait()
        return buffers[i]

    body(get, *out_refs, *more)


def stream(name, loads, out_shapes, body, scratch=()):
    arrays = []

    def place(array):
        for i, known in enumerate(arrays):
            if known is array:
                return i
        arrays.append(array)
        return len(arrays) - 1

    plan, buffers, number = [], [], 0
    for load in loads:
        steps, at = [], 0
        for array, col, width in load:
            steps.append((place(array), at, array.shape[0], col, width, number))
            at += array.shape[0]
            number += 1
        plan.append(steps)
        buffers.append(pltpu.VMEM((at, load[0][2]), load[0][0].dtype))
    return pl.pallas_call(
        functools.partial(stream_kernel, plan, len(arrays), len(out_shapes), body),
        out_shape=tuple(out_shapes),
        in_specs=[pl.BlockSpec(memory_space=pl.ANY)] * len(arrays),
        out_specs=tuple(pl.BlockSpec(memory_space=pltpu.VMEM) for _ in out_shapes),
        scratch_shapes=buffers + list(scratch) + [pltpu.SemaphoreType.DMA((number,))],
        compiler_params=params(),
        cost_estimate=cost(0, 0),
        name=name,
    )(*arrays)


def part(array, col=0, width=None):
    return [(array, col, array.shape[1] - col if width is None else width)]


def weight(pieces, col, width):
    return [(piece, col, width) for piece in pieces]


def wide(name, x, blocks, extras=(), body=None, outs=1):
    widths = [width for *_, width in blocks]
    loads = [part(x)]
    for i, block in enumerate(blocks):
        loads.append(weight(*block))
        for extra in extras:
            loads.append(part(extra, sum(widths[:i]), widths[i]))

    def run(get, *out_refs):
        at = 0
        per = 1 + len(extras)
        for i, width in enumerate(widths):
            first = 1 + i * per
            value = dot(get(0)[...], get(first)[...])
            got = [get(first + 1 + j)[...] for j in range(len(extras))]
            values = (value,) if body is None else body(value, *got)
            for ref, result in zip(out_refs, values):
                ref[:, at : at + width] = result.astype(BF16)
            at += width

    shape = shape_of(BF16, x.shape[0], sum(widths))
    result = stream(name, loads, (shape,) * outs, run)
    return result if outs > 1 else result[0]


def gelu_both(up):
    square = up * up
    bend = jnp.tanh(GELU_A * up * (1.0 + GELU_B * square))
    half_one = 0.5 + 0.5 * bend
    inner = GELU_A + (3.0 * GELU_A * GELU_B) * square
    return up * half_one, half_one + 0.5 * up * (1.0 - bend * bend) * inner


def times_slope(value, slope):
    return (value * slope.astype(F32),)


def narrow(name, work, extras, out_shapes, body):
    loads = []
    for x, x_col, pieces, col, width in work:
        loads += [part(x, x_col, width), weight(pieces, col, width)]
    first = len(loads)
    loads += [part(extra) for extra in extras]

    def run(get, *refs):
        *out_refs, acc = refs
        for j in range(len(work)):
            value = dot_nt(get(2 * j)[...], get(2 * j + 1)[...])
            acc[...] = value if j == 0 else acc[...] + value
        body(acc, *(get(first + i) for i in range(len(extras))), *out_refs)

    depth = sum(piece.shape[0] for piece in work[0][2])
    return stream(
        name, loads, out_shapes, run, [pltpu.VMEM((work[0][0].shape[0], depth), F32)]
    )


def gradients(name, left, first, count, rights, out_of=None):
    loads = [part(left, first, count)] + [part(right) for right in rights]

    def run(get, *refs):
        *out_refs, turned = refs
        turned[...] = get(0)[...].T
        for i, ref in enumerate(out_refs):
            ref[...] = dot(turned[...], get(1 + i)[...]).astype(BF16)

    shapes = [shape_of(BF16, count, right.shape[1]) for right in rights]
    return stream(name, loads, shapes, run, [pltpu.VMEM((count, left.shape[0]), BF16)])


def stack_rows(pieces, widths):
    block = pieces[0].shape[0]
    cuts = [sum(widths[:i]) for i in range(len(widths))]
    if block % 16:
        whole = jnp.concatenate(pieces, axis=0)
        return [whole[:, at : at + width] for at, width in zip(cuts, widths)]

    def run(*refs):
        ins, outs, sem = refs[: len(pieces)], refs[len(pieces) : -1], refs[-1]
        copies = []
        for i, ref in enumerate(ins):
            for j, out in enumerate(outs):
                copy = pltpu.make_async_copy(
                    ref.at[:, pl.ds(cuts[j], widths[j])],
                    out.at[pl.ds(i * block, block)],
                    sem.at[i, j],
                )
                copy.start()
                copies.append(copy)
        for copy in copies:
            copy.wait()

    return pl.pallas_call(
        run,
        out_shape=tuple(shape_of(pieces[0].dtype, block * len(pieces), width) for width in widths),
        in_specs=[pl.BlockSpec(memory_space=pl.ANY)] * len(pieces),
        out_specs=tuple(pl.BlockSpec(memory_space=pl.ANY) for _ in widths),
        scratch_shapes=[pltpu.SemaphoreType.DMA((len(pieces), len(widths)))],
        cost_estimate=cost(0, 0),
        name="stack_rows",
    )(*pieces)


def qkv_call(inputs, inverse, first, n):
    blocks = [(side, i * n, n) for i in range(3) for side in first]
    loads = [part(inputs), part(inverse), weight(first[0], 3 * n, LANES)]
    loads += [weight(*block) for block in blocks]

    def run(get, qkv_ref, normed_ref, gains_ref):
        gains = get(2)[...].astype(F32).T[:8]
        gains_ref[...] = gains
        normed = (get(0)[...] * get(1)[...] * gains[0:1]).astype(BF16)
        normed_ref[...] = normed
        for i in range(len(blocks)):
            qkv_ref[:, i * n : (i + 1) * n] = dot(normed_ref[...], get(3 + i)[...]).astype(BF16)

    seq, width = inputs.shape
    shapes = (shape_of(BF16, seq, 6 * n), shape_of(BF16, seq, width), shape_of(F32, 8, width))
    return stream("qkv", loads, shapes, run)


def norm_body(row, acc, value_ref, gains_ref, hidden_ref, inverse_ref, normed_ref=None):
    hidden = value_ref[...] + acc[...]
    inverse = lax.rsqrt(jnp.mean(hidden * hidden, axis=1, keepdims=True) + EPSILON)
    hidden_ref[...] = hidden
    inverse_ref[...] = inverse
    if normed_ref is not None:
        normed_ref[...] = (hidden * inverse * gains_ref[row : row + 1, :]).astype(BF16)


def norm_back(value, inverse, gain, grad):
    scaled = grad * gain
    inner = jnp.mean(value * scaled, axis=1, keepdims=True)
    d_value = inverse * scaled - value * (inverse * inverse * inverse) * inner
    return d_value, jnp.sum(grad * value * inverse, axis=0, keepdims=True)


def back_body(row, acc, value_ref, inverse_ref, gains_ref, grad_ref, low_ref, gain_out, hidden_ref=None):
    d_value, d_gain = norm_back(
        value_ref[...], inverse_ref[...], gains_ref[row : row + 1, :], acc[...]
    )
    total = grad_ref[...] + d_value
    low_ref[...] = total.astype(BF16)
    gain_out[...] = d_gain
    if hidden_ref is not None:
        hidden_ref[...] = total


def turn_kernel(grad_ref, order_ref, out_ref):
    out_ref[...] = dot_nt(grad_ref[...], order_ref[...]).astype(BF16)


def small_kernel(heads_half, one_ref, two_ref, three_ref, order_ref, bias_ref, onehot_ref, loss_ref, mine_ref, out_ref):
    width = one_ref.shape[1]
    gains = jnp.concatenate([one_ref[...], two_ref[...], three_ref[...], jnp.zeros((5, width), F32)], axis=0)
    high = gains.astype(BF16)
    rest = (gains - high.astype(F32)).astype(BF16)
    gains = dot_nt(high, order_ref[...]) + dot_nt(rest, order_ref[...])
    out_ref[...] = jnp.zeros_like(out_ref)
    across = width // LANES
    for i in range(3):
        for j in range(across):
            at = i * across + j
            out_ref[at : at + 1, :] = gains[i : i + 1, j * LANES : (j + 1) * LANES]
    at = 3 * across
    lane = lax.broadcasted_iota(jnp.int32, (1, LANES), 1)
    out_ref[at : at + 1, :] = jnp.where(lane == 0, loss_ref[...], 0.0)
    bias = bias_ref[...]
    row = lax.broadcasted_iota(jnp.int32, (LANES, bias.shape[0]), 0)
    column = lax.broadcasted_iota(jnp.int32, (LANES, bias.shape[0]), 1)
    pick = jnp.where((column == 8 * (row // 2) + row % 2) & (row < 2 * heads_half), 1.0, 0.0)
    bias = split_dot(pick.astype(BF16), bias)
    high = bias.astype(BF16)
    rest = (bias - high.astype(F32)).astype(BF16)
    buckets = onehot_ref[...]
    table = dot_nt(buckets, high) + dot_nt(buckets, rest)
    lane = lax.broadcasted_iota(jnp.int32, table.shape, 1)
    swapped = jnp.where(
        lane < heads_half, pltpu.roll(table, LANES - heads_half, 1), pltpu.roll(table, heads_half, 1)
    )
    top = -(-(at + 1) // 8) * 8
    out_ref[top : top + table.shape[0], :] = jnp.where(mine_ref[...] == 0, table, swapped)


def member_of(seg_ref, sent_count):
    ids = lax.broadcasted_iota(jnp.int32, (sent_count, seg_ref.shape[1]), 0)
    hit = jnp.where(seg_ref[...] == ids, 1.0, 0.0)
    return hit.astype(BF16), jnp.sum(hit, axis=1, keepdims=True)


def head_kernel(
    near_ref, side_ref, c_near_ref, c_side_ref, unit_ref, scale_ref, partner_ref, column_ref, seg_ref,
    own_ref, other_ref, value_ref, inverse_ref, gain_ref,
    loss_ref, embed_ref, hidden_ref, low_ref, gain_out, every,
):
    quarter = near_ref.shape[0]
    for i, ref in enumerate((near_ref, side_ref, c_near_ref, c_side_ref)):
        every[i * quarter : (i + 1) * quarter] = ref[...]
    total = every.shape[0]
    own_count = unit_ref.shape[0]
    sims = dot_nt(every[...], every[...]) * SOFTMAX_TEMP
    row = lax.broadcasted_iota(jnp.int32, (total, total), 0)
    column = lax.broadcasted_iota(jnp.int32, (total, total), 1)
    sims = jnp.where(row == column, NEG_FILL, sims)
    top = jnp.max(sims, axis=0, keepdims=True)
    lse_row = top + jnp.log(jnp.sum(jnp.exp(sims - top), axis=0, keepdims=True))
    own = sims[:own_count]
    own_top = jnp.max(own, axis=1, keepdims=True)
    own_lse = own_top + jnp.log(jnp.sum(jnp.exp(own - own_top), axis=1, keepdims=True))
    is_target = column_ref[...] == partner_ref[...]
    hit = jnp.where(is_target, 1.0, 0.0)
    target = jnp.sum(jnp.where(is_target, own, 0.0), axis=1, keepdims=True)
    loss_ref[...] = jnp.sum(own_lse - target, axis=0, keepdims=True)
    d_rows = (LOSS_SCALE * (jnp.exp(own - own_lse) - hit)).astype(BF16)
    d_cols = (LOSS_SCALE * (jnp.exp(own - lse_row) - hit)).astype(BF16)
    d_unit = SOFTMAX_TEMP * (dot(d_rows, every[...]) + dot(d_cols, every[...]))
    unit = unit_ref[...]
    inner = jnp.sum(d_unit * unit, axis=1, keepdims=True)
    d_embed = (scale_ref[...] * (d_unit - unit * inner)).astype(BF16)
    embed_ref[...] = d_embed
    sentence_back(d_embed, seg_ref, own_ref, other_ref, value_ref, inverse_ref, gain_ref, hidden_ref, low_ref, gain_out)


def sentence_kernel(embed_ref, *refs):
    sentence_back(embed_ref[...], *refs)


def sentence_back(d_embed, seg_ref, own_ref, other_ref, value_ref, inverse_ref, gain_ref, hidden_ref, low_ref, gain_out):
    half = own_ref.shape[1]
    d_pooled = dot_nt(d_embed[:, :half], own_ref[...]) + dot_nt(d_embed[:, half:], other_ref[...])
    sents, count = member_of(seg_ref, d_embed.shape[0])
    d_final = split_dot(sents, d_pooled / count, ((0,), (0,)))
    d_value, d_gain = norm_back(value_ref[...], inverse_ref[...], gain_ref[...], d_final)
    hidden_ref[...] = d_value
    low_ref[...] = d_value.astype(BF16)
    gain_out[...] = d_gain


def whole_call(body, args, out_shapes, scratch=(), name=None):
    return pl.pallas_call(
        body,
        out_shape=out_shapes,
        in_specs=[pl.BlockSpec(memory_space=pltpu.VMEM)] * len(args),
        out_specs=tuple(pl.BlockSpec(memory_space=pltpu.VMEM) for _ in out_shapes),
        scratch_shapes=scratch,
        compiler_params=params(),
        cost_estimate=cost(0, 0),
        name=name,
    )(*args)


def shape_of(kind, *dims):
    return jax.ShapeDtypeStruct(dims, kind)


def _stack_heads(part):
    lane = lax.broadcasted_iota(jnp.int32, part.shape, 1)
    zero = jnp.zeros_like(part)
    first = lane < LANES // 2
    return jnp.concatenate(
        [jnp.where(first, part, zero), jnp.where(first, zero, part)], axis=0
    )


def _unstack_heads(both):
    half = both.shape[0] // 2
    lane = lax.broadcasted_iota(jnp.int32, (half, LANES), 1)
    return jnp.where(lane < LANES // 2, both[:half], both[half:])


def _pad_keys(pad, ref):
    seq = ref.shape[0]
    pad[0:REACH] = jnp.zeros((REACH, LANES), pad.dtype)
    pad[REACH + seq :] = jnp.zeros((REACH, LANES), pad.dtype)
    pad[REACH : REACH + seq] = ref[...]


def _query_bits(shape):
    return lax.broadcasted_iota(jnp.int32, shape, 0) & (QB - 1)


def attend_forward_kernel(
    q_ref, k_ref, v_ref, segq_ref, segk_ref, rel_ref, ctx_ref, probs_ref, kpad, vpad, mask, scores
):
    seq = q_ref.shape[0]
    blocks = seq // QB
    _pad_keys(kpad, k_ref)
    _pad_keys(vpad, v_ref)

    @pl.when(pl.program_id(0) == 0)
    def _():
        for b in range(blocks):
            same = segk_ref[b * QB : b * QB + WIN] == segq_ref[b : b + 1, :]
            mask[b] = jnp.where(same, 0.0, NEG_FILL)

    rel = rel_ref[0]
    row = lax.broadcasted_iota(jnp.int32, (2 * QB, WIN), 0)
    bias = jnp.where(row < QB, rel[0:1, :], rel[1:2, :])
    bits = _query_bits((2 * QB, WIN))
    step = 1
    while step < QB:
        bias = jnp.where((bits & step) != 0, pltpu.roll(bias, step, 1), bias)
        step *= 2
    bias = bias.T
    for b in range(blocks):
        query = _stack_heads(q_ref[b * QB : (b + 1) * QB] * jnp.asarray(SCORE_SCALE, BF16))
        scores[b] = dot_nt(kpad[b * QB : b * QB + WIN], query)
    values = scores[...] + bias[None] + mask[...]
    top = jnp.max(values, axis=1, keepdims=True)
    shifted = jnp.exp(values - top)
    total = jnp.sum(shifted, axis=1, keepdims=True)
    probs_ref[0] = (shifted * (1.0 / total)).astype(BF16)
    for b in range(blocks):
        part = dot_tn(probs_ref[0, b], vpad[b * QB : b * QB + WIN])
        ctx_ref[b * QB : (b + 1) * QB] = _unstack_heads(part).astype(BF16)


def attend_backward_kernel(
    q_ref, k_ref, v_ref, dctx_ref, probs_ref, dqkv_ref, dbias_ref,
    kpad, vpad, dk_acc, dv_acc, d_probs, d_low,
):
    seq = q_ref.shape[0]
    pair = pl.program_id(0)
    side = pl.num_programs(0) // 2
    later = pair // side
    q_at = pl.ds(pl.multiple_of(pair * LANES, LANES), LANES)
    k_at = pl.ds(pl.multiple_of((pair + 2 * side + later * side) * LANES, LANES), LANES)
    v_at = pl.ds(pl.multiple_of((pair + 3 * side + later * side) * LANES, LANES), LANES)
    blocks = seq // QB
    _pad_keys(kpad, k_ref)
    _pad_keys(vpad, v_ref)
    dk_acc[...] = jnp.zeros_like(dk_acc)
    dv_acc[...] = jnp.zeros_like(dv_acc)
    for b in range(blocks):
        window = slice(b * QB, b * QB + WIN)
        d_ctx = _stack_heads(dctx_ref[b * QB : (b + 1) * QB])
        d_probs[b] = dot_nt(vpad[window], d_ctx)
        dv_acc[window] += dot(probs_ref[0, b], d_ctx)
    probs = probs_ref[0].astype(F32)
    product = probs * d_probs[...]
    inner = jnp.sum(product, axis=1, keepdims=True)
    d_scores = product - probs * inner
    d_low[...] = d_scores.astype(BF16)
    total = jnp.sum(d_scores, axis=0).T
    for b in range(blocks):
        here = slice(b * QB, (b + 1) * QB)
        window = slice(b * QB, b * QB + WIN)
        query = _stack_heads(q_ref[here] * jnp.asarray(SCORE_SCALE, BF16))
        dk_acc[window] += dot(d_low[b], query)
        d_query = _unstack_heads(dot_tn(d_low[b], kpad[window])) * SCORE_SCALE
        dqkv_ref[here, q_at] = d_query.astype(BF16)
    dqkv_ref[:, k_at] = dk_acc[REACH : REACH + seq].astype(BF16)
    dqkv_ref[:, v_at] = dv_acc[REACH : REACH + seq].astype(BF16)
    bits = _query_bits((2 * QB, WIN))
    step = 1
    while step < QB:
        total = jnp.where((bits & step) != 0, pltpu.roll(total, WIN - step, 1), total)
        step *= 2
    first = jnp.sum(total[:QB], axis=0, keepdims=True)
    second = jnp.sum(total[QB:], axis=0, keepdims=True)
    dbias_ref[0] = jnp.concatenate([first, second, jnp.zeros((6, WIN), F32)], axis=0)


def _qkv_specs(seq, pairs):
    def spec(kind):
        return pl.BlockSpec((seq, LANES), lambda p: (0, kind * pairs + p))

    return [spec(0), spec(1), spec(2)]


def attend_forward(qkv, seg_row, rel_window):
    seq = qkv.shape[0]
    pairs = rel_window.shape[0]
    blocks = seq // QB
    padded = jnp.pad(seg_row, (REACH, REACH), constant_values=-1)[:, None]
    twice = jnp.tile(seg_row.reshape(blocks, QB), (1, 2))
    return pl.pallas_call(
        attend_forward_kernel,
        grid=(pairs,),
        out_shape=(
            jax.ShapeDtypeStruct((seq, pairs * LANES), BF16),
            jax.ShapeDtypeStruct((pairs, blocks, WIN, 2 * QB), BF16),
        ),
        in_specs=_qkv_specs(seq, pairs)
        + [
            pl.BlockSpec((blocks, 2 * QB), lambda p: (0, 0)),
            pl.BlockSpec((seq + 2 * REACH, 1), lambda p: (0, 0)),
            pl.BlockSpec((1, 2, WIN), lambda p: (p, 0, 0)),
        ],
        out_specs=(
            pl.BlockSpec((seq, LANES), lambda p: (0, p)),
            pl.BlockSpec((1, blocks, WIN, 2 * QB), lambda p: (p, 0, 0, 0)),
        ),
        scratch_shapes=[pltpu.VMEM((seq + 2 * REACH, LANES), BF16)] * 2
        + [pltpu.VMEM((blocks, WIN, 2 * QB), F32)] * 2,
        compiler_params=params(),
        cost_estimate=cost(8 * seq * WIN * LANES * pairs * 4, 8 * seq * LANES * pairs),
        name="attend_forward",
    )(qkv, qkv, qkv, twice, padded, rel_window)


def attend_backward(qkv, d_context, probs):
    seq = qkv.shape[0]
    pairs = probs.shape[0]
    blocks = seq // QB
    lane_block = pl.BlockSpec((seq, LANES), lambda p: (0, p))
    return pl.pallas_call(
        attend_backward_kernel,
        grid=(pairs,),
        out_shape=(
            jax.ShapeDtypeStruct((seq, 3 * pairs * LANES), BF16),
            jax.ShapeDtypeStruct((pairs, 8, WIN), F32),
        ),
        in_specs=_qkv_specs(seq, pairs)
        + [
            lane_block,
            pl.BlockSpec((1, blocks, WIN, 2 * QB), lambda p: (p, 0, 0, 0)),
        ],
        out_specs=(
            pl.BlockSpec((seq, 3 * pairs * LANES), lambda p: (0, 0)),
            pl.BlockSpec((1, 8, WIN), lambda p: (p, 0, 0)),
        ),
        scratch_shapes=[pltpu.VMEM((seq + 2 * REACH, LANES), BF16)] * 2
        + [pltpu.VMEM((seq + 2 * REACH, LANES), F32)] * 2
        + [pltpu.VMEM((blocks, WIN, 2 * QB), F32), pltpu.VMEM((blocks, WIN, 2 * QB), BF16)],
        compiler_params=params(),
        cost_estimate=cost(16 * seq * WIN * LANES * pairs * 4, 16 * seq * LANES * pairs),
        name="attend_backward",
    )(qkv, qkv, qkv, d_context, probs)


CORE = 1
CROSS = 2


def hop(value, mask):
    size = lax.axis_size("dp")
    return lax.ppermute(value, "dp", [(i, i ^ mask) for i in range(size)])


def over(value):
    return lax.ppermute(value, "mp", [(0, 1), (1, 0)])


def cross(value):
    return hop(value, CROSS)


def core(value):
    return hop(value, CORE)


def go(waits, *sends, keep=(), join=True):
    values = [value for _, value in sends]
    held = lax.optimization_barrier((*values, *keep, *waits))
    results = [how(value) for (how, _), value in zip(sends, held)]
    if join:
        results = list(lax.optimization_barrier(tuple(results)))
    return results + list(held[len(values) : len(values) + len(keep)])


def slot_masks(size):
    rest = size // 4
    return [z * 4 + x * 2 + c for c in range(2) for x in range(2) for z in range(rest)]


def strides(size):
    found = []
    stride = 4
    while stride < size:
        found.append(stride)
        stride *= 2
    return found


def gather_near(shard, waits, widths=None):
    size = lax.axis_size("dp")
    pieces = [shard]
    stride = 4
    while stride < size:
        radix = min(4, size // stride)
        shard = jnp.concatenate(pieces, axis=0) if len(pieces) > 1 else shard
        sends = [(functools.partial(hop, mask=j * stride), shard) for j in range(1, radix)]
        pieces = [shard] + go(waits, *sends)
        stride *= radix
    return jnp.concatenate(pieces, axis=0) if widths is None else stack_rows(pieces, widths)


def rows(*pieces):
    return jnp.concatenate(pieces, axis=0)


def columns(*pieces):
    return jnp.concatenate(pieces, axis=1)


def gather_weights(one, two, three, four, between):
    size = lax.axis_size("dp")
    steps = strides(size)
    later = columns(three, four)
    n_three = three.shape[1]
    one, two = gather_near(columns(one, two), (), (one.shape[1], two.shape[1]))
    one_x, two_y, *more = go(
        (), (cross, one), (over, two), *((functools.partial(hop, mask=stride), later) for stride in steps[:1])
    )
    later = rows(later, *more)
    for stride in steps[1:-1]:
        later = rows(later, hop(later, stride))
    one_y, one_xy, two_x, two_yx, *more = go(
        (one_x, two_y),
        (over, one),
        (over, one_x),
        (cross, two),
        (cross, two_y),
        *((functools.partial(hop, mask=stride), later) for stride in steps[1:][-1:]),
    )
    if more and later.shape[0] % 16 == 0:
        three, four = stack_rows((later, *more), (n_three, later.shape[1] - n_three))
    else:
        later = rows(later, *more)
        three, four = later[:, :n_three], later[:, n_three:]
    three_x, four_y, one_c, one_xc, two_c = go(
        (),
        (cross, three),
        (over, four),
        (core, one),
        (core, one_x),
        (core, two),
        keep=(one_y, one_xy, two_x, two_yx, two_y),
        join=False,
    )[:5]
    two_yc, one_yc, one_xyc = go(
        (one_c, one_xc, two_c), (core, two_y), (core, one_y), (core, one_xy)
    )
    two_xc, two_yxc = go((two_yc, one_yc, one_xyc), (core, two_x), (core, two_yx))
    first = ((one, one_x, one_c, one_xc), (one_y, one_xy, one_yc, one_xyc))
    second = ((two, two_x, two_c, two_xc), (two_y, two_yx, two_yc, two_yxc))
    four_x, four_yx, three_y, three_xy, four_c, *kept = go(
        (three_x, four_y),
        (cross, four),
        (cross, four_y),
        (over, three),
        (over, three_x),
        (core, four),
        keep=(*first[0], *first[1], *second[0], *second[1]),
        join=False,
    )
    first = (tuple(kept[:4]), tuple(kept[4:8]))
    second = (tuple(kept[8:12]), tuple(kept[12:]))
    done = between(first, second)
    four_yc, three_c = go((four_c,), (core, four_y), (core, three))
    (three_xc,) = go((four_yc, three_c), (core, three_x))
    four_xc, four_yxc, three_yc, three_xyc, *done = go(
        (three_xc,),
        (core, four_x),
        (core, four_yx),
        (core, three_y),
        (core, three_xy),
        keep=done,
        join=False,
    )
    third = ((three, three_x, three_c, three_xc), (three_y, three_xy, three_yc, three_xyc))
    fourth = ((four, four_x, four_c, four_xc), (four_y, four_yx, four_yc, four_yxc))
    return first, second, third, fourth, done


def gather_dp(shard):
    near = gather_near(shard, ())
    side, c_near = go((near,), (cross, near), (core, near))
    return near, side, c_near, core(side)


def low(value):
    return value.astype(BF16)


def add(left, right):
    return (left.astype(F32) + right.astype(F32)).astype(BF16)


def product(left, begin, end, right, got=None):
    value = dot_tn(left[:, begin:end], right)
    if got is not None:
        value = value + got.astype(F32)
    return low(value)


def rest_start(value):
    half = value.shape[0] // 2
    return value[half:], value[:half]


def sum_half(value, send):
    gone, stays = rest_start(value)
    return stays + send(low(gone)).astype(F32)


def rest_hops(size):
    return [functools.partial(hop, mask=stride) for stride in reversed(strides(size))]


def shards(
    tokens,
    seg_ids,
    buckets,
    labels,
    w_query,
    w_key,
    w_value,
    w_out,
    w_in,
    w_back,
    gain_attn,
    gain_ffn,
    gain_final,
    w_pool,
    rel_table,
):
    micro_count, seq, width = tokens.shape
    size = lax.axis_size("dp")
    me = lax.axis_index("dp")
    mine = lax.axis_index("mp")
    block = width // size
    inner_half = w_query.shape[1]
    hidden_half = w_in.shape[1]
    sent_local = labels.shape[1]
    bucket_count = rel_table.shape[0]
    heads_half = rel_table.shape[1]
    masks = slot_masks(size)

    x_own = lax.dynamic_index_in_dim(tokens, mine, 0, keepdims=False)
    segments = lax.dynamic_index_in_dim(seg_ids, mine, 0, keepdims=False)[0]
    partner = lax.dynamic_index_in_dim(labels, mine, 0, keepdims=False)

    slot_block = jnp.stack([jnp.bitwise_xor(me, m) for m in masks]).astype(jnp.int32)
    source = (slot_block[:, None] * block + jnp.arange(block, dtype=jnp.int32)[None, :]).reshape(-1)
    order = (jnp.arange(width, dtype=jnp.int32)[:, None] == source[None, :]).astype(BF16)
    order = lax.optimization_barrier(order)
    inputs = dot(x_own, order)
    inverse1 = lax.rsqrt(jnp.mean(inputs * inputs, axis=1, keepdims=True) + EPSILON)

    rel_all = jnp.concatenate([rel_table, over(rel_table)], axis=1).astype(F32)
    near_buckets = lax.slice_in_dim(buckets, seq - 1 - REACH, seq - 1 - REACH + WIN)
    onehot = (near_buckets[None, :] == jnp.arange(bucket_count, dtype=jnp.int32)[:, None]).astype(F32)
    onehot = lax.optimization_barrier(low(onehot))
    rel_window = dot(rel_all, onehot.astype(F32), ((0,), (0,)), HIGHEST).reshape(heads_half, 2, WIN)

    row_f32 = shape_of(F32, seq, width)
    row_low = shape_of(BF16, seq, width)
    column_f32 = shape_of(F32, seq, 1)
    gain_f32 = shape_of(F32, 1, width)
    heads = 3 * inner_half
    piece = hidden_half // 2
    halves = [(side, i * inner_half, inner_half) for side in range(2) for i in range(2)]

    def hidden_blocks(weights, first_col=0):
        return [(weights[side], first_col + col, n) for side, col, n in halves]

    def between(first, second):
        qkv, normed1_low, gains = qkv_call(inputs, inverse1, first, inner_half)
        context, probs = attend_forward(qkv, segments, rel_window)
        hidden1, inverse2, normed2_low = narrow(
            "attn_out",
            [(context, i * inner_half, second[i], piece, inner_half) for i in range(2)],
            (inputs, gains),
            (row_f32, column_f32, row_low),
            functools.partial(norm_body, 1),
        )
        act0, slope0 = wide("act0", normed2_low, hidden_blocks(second), (), gelu_both, 2)
        return normed1_low, gains, qkv, context, probs, hidden1, inverse2, normed2_low, act0, slope0

    gains_col = jnp.pad(
        jnp.stack([gain_attn, gain_ffn, gain_final], axis=1), ((0, 0), (0, LANES - 3))
    )
    pool_half = w_pool.shape[1] // 2
    pool_own = lax.dynamic_slice_in_dim(w_pool, mine * pool_half, pool_half, axis=1)
    back_shard = w_back.T
    first, second, third, fourth, done = gather_weights(
        columns(w_query, w_key, w_value, gains_col),
        columns(w_in[:, :piece], w_out.T),
        columns(back_shard[:, :piece], pool_own),
        columns(w_in[:, piece:], back_shard[:, piece:]),
        between,
    )
    pool_w = [rows(*(p[:, piece:] for p in side)) for side in third]
    normed1_low, gains, qkv, context, probs, hidden1, inverse2, normed2_low, act0, slope0 = done

    act1, slope1 = wide("act1", normed2_low, hidden_blocks(fourth), (), gelu_both, 2)
    seg_lane = segments[None, :]
    hidden2, inverse3 = narrow(
        "ffn_out",
        [(act0, i * piece, third[i], 0, piece) for i in range(2)]
        + [(act1, i * piece, fourth[i], piece, piece) for i in range(2)],
        (hidden1, gains),
        (row_f32, column_f32),
        functools.partial(norm_body, 2),
    )
    final = hidden2 * inverse3 * gains[2:3]
    local_ids = jnp.arange(sent_local, dtype=jnp.int32)
    member = (segments[:, None] == local_ids[None, :]).astype(F32)
    counts = jnp.sum(member, axis=0)
    pooled_low = low(dot(member, final, ((0,), (0,)), HIGHEST) / counts[:, None])
    embed = columns(dot(pooled_low, pool_w[0]), dot(pooled_low, pool_w[1]))
    scale = lax.rsqrt(jnp.sum(embed * embed, axis=-1, keepdims=True) + EPSILON)
    unit = embed * scale
    quarters = gather_dp(low(unit))

    column_id = (slot_block[:, None] * sent_local + local_ids[None, :]).reshape(1, -1)
    total_sent = column_id.shape[1]
    back_args = (seg_lane, *pool_w, hidden2, inverse3, gains[2:3])
    back_shapes = (row_f32, row_low, gain_f32)
    if total_sent <= 1024:
        loss_local, embed_low, d_hidden2, ffn_low, d_gain3 = whole_call(
            head_kernel,
            (*quarters, unit, scale, partner[:, None], column_id, *back_args),
            (shape_of(F32, 1, 1), shape_of(BF16, sent_local, width), *back_shapes),
            [pltpu.VMEM((total_sent, width), BF16)],
            "head",
        )
    else:
        every = rows(*quarters)
        position = jnp.arange(total_sent, dtype=jnp.int32)
        sims = dot_nt(every, every) * SOFTMAX_TEMP
        sims = jnp.where(position[:, None] == position[None, :], NEG_FILL, sims)
        lse_row = jax.nn.logsumexp(sims, axis=0, keepdims=True)
        own_sims = sims[:sent_local]
        own_lse = jax.nn.logsumexp(own_sims, axis=1, keepdims=True)
        is_target = column_id == partner[:, None]
        target = jnp.sum(jnp.where(is_target, own_sims, 0.0), axis=-1, keepdims=True)
        loss_local = jnp.sum(own_lse - target)
        hit = is_target.astype(F32)
        d_rows = low(LOSS_SCALE * (jnp.exp(own_sims - own_lse) - hit))
        d_cols = low(LOSS_SCALE * (jnp.exp(own_sims - lse_row) - hit))
        d_unit = SOFTMAX_TEMP * (dot(d_rows, every) + dot(d_cols, every))
        embed_low = low(scale * (d_unit - unit * jnp.sum(d_unit * unit, axis=-1, keepdims=True)))
        d_hidden2, ffn_low, d_gain3 = whole_call(
            sentence_kernel, (embed_low, *back_args), back_shapes, (), "sentence"
        )

    half = width // 2
    quarter = width // 4

    back0_sent, back1_sent = gradients("back_sent", ffn_low, half, half, (act0, act1))
    (pool_sent,) = gradients("pool_sent", pooled_low, half, half, (embed_low,))
    back0_got, back1_got, pool_got, ffn_later = go(
        (), (core, back0_sent), (core, back1_sent), (core, pool_sent), keep=(ffn_low,)
    )
    up0 = wide("up0", ffn_later, hidden_blocks(third), (slope0,), times_slope)

    pool_hi = product(pooled_low, quarter, half, embed_low, pool_got[quarter:])
    pool_lo = product(pooled_low, 0, quarter, embed_low, pool_got[:quarter])
    back_hi = product(ffn_low, quarter, half, act0, back0_got[quarter:])
    back_lo = product(ffn_low, 0, quarter, act0, back0_got[:quarter])
    back_own = product(ffn_low, 0, half, act1[:, :piece], back1_got[:, :piece])
    back_oth = product(ffn_low, 0, half, act1[:, piece:], back1_got[:, piece:])
    got_pool, got_lo, got_own, ffn_later, up0, pool_lo, back_lo, back_own = go(
        (),
        (cross, pool_hi),
        (cross, back_hi),
        (over, back_oth),
        keep=(ffn_later, up0, pool_lo, back_lo, back_own),
    )
    up1 = wide("up1", ffn_later, hidden_blocks(fourth, piece), (slope1,), times_slope)
    in0_sent, in1_sent = gradients("in_sent", normed2_low, half, half, (up0, up1))
    in0_got, in1_got, up0, up1 = go((), (core, in0_sent), (core, in1_sent), keep=(up0, up1))
    attn_low, d_gain2, d_hidden1 = narrow(
        "ffn_in_back",
        [(up0, i * piece, second[i], 0, piece) for i in range(2)]
        + [(up1, i * piece, fourth[i], 0, piece) for i in range(2)],
        (hidden1, inverse2, gains, d_hidden2),
        (row_low, gain_f32, row_f32),
        functools.partial(back_body, 1),
    )
    d_context = wide("d_context", attn_low, [(second[side], piece, inner_half) for side in range(2)])

    pool_lo = add(pool_lo, got_pool)
    back_lo = add(back_lo, got_lo)
    back_own = add(back_own, got_own)
    in_hi = product(normed2_low, quarter, half, up0, in0_got[quarter:])
    in_lo = product(normed2_low, 0, quarter, up0, in0_got[:quarter])
    in_own = product(normed2_low, 0, half, up1[:, :piece], in1_got[:, :piece])
    in_oth = product(normed2_low, 0, half, up1[:, piece:], in1_got[:, piece:])
    got_first, got_second, got_in_lo, got_in_own, d_context, pool_lo, back_lo, back_own, in_lo, in_own = go(
        (got_pool, got_lo, got_own),
        (over, columns(back_lo[:, piece:], pool_lo[:, pool_half:])),
        (cross, back_own[quarter:]),
        (cross, in_hi),
        (over, in_oth),
        keep=(d_context, pool_lo, back_lo, back_own, in_lo, in_own),
    )
    d_qkv, d_bias = attend_backward(qkv, d_context, probs)
    query_both = 2 * inner_half
    grad_slots, d_gain1 = narrow(
        "qkv_back",
        [(d_qkv, i * inner_half, first[i], 0, inner_half) for i in range(2)]
        + [(d_qkv, (1 + i) * query_both, first[i], inner_half, query_both) for i in range(2)],
        (inputs, inverse1, gains, d_hidden1),
        (row_low, gain_f32),
        functools.partial(back_body, 0),
    )
    (qkv_sent,) = gradients("qkv_sent", normed1_low, half, half, (d_qkv,))
    (out_sent,) = gradients("out_sent", attn_low, half, half, (context,))

    far = rest_hops(size)
    back_all = columns(
        add(back_lo[:, :piece], got_first[:, :piece]),
        add(back_own[:quarter], got_second),
        add(pool_lo[:, :pool_half], got_first[:, piece:]),
    )
    back_rest, back_stay = rest_start(back_all)
    in_lo = add(in_lo, got_in_lo)
    in_own = add(in_own, got_in_own)
    back_more, got_first, got_second, qkv_got, out_got, grad_slots, back_stay, in_lo, in_own = go(
        (got_first, got_second, got_in_lo, got_in_own),
        (far[0], back_rest),
        (over, in_lo[:, piece:]),
        (cross, in_own[quarter:]),
        (core, qkv_sent),
        (core, out_sent),
        keep=(grad_slots, back_stay, in_lo, in_own),
    )
    (grad_own,) = whole_call(turn_kernel, (grad_slots, order), (row_low,), (), "turn")
    small_rows = -(-(3 * (width // LANES) + 1) // 8) * 8 + bucket_count
    (flat,) = whole_call(
        functools.partial(small_kernel, heads_half),
        (d_gain1, d_gain2, d_gain3, order, d_bias.reshape(-1, WIN), onehot, loss_local.reshape(1, 1), mine.reshape(1, 1)),
        (shape_of(F32, small_rows, LANES),),
        (),
        "small",
    )

    back_all = add(back_stay, back_more)
    back_rest, back_stay = rest_start(back_all)
    in_all = columns(add(in_lo[:, :piece], got_first), add(in_own[:quarter], got_second))
    in_rest, in_stay = rest_start(in_all)
    out_hi = product(attn_low, quarter, half, context, out_got[quarter:])
    out_lo = product(attn_low, 0, quarter, context, out_got[:quarter])
    query_hi = product(normed1_low, quarter, half, d_qkv[:, :query_both], qkv_got[quarter:, :query_both])
    query_lo = product(normed1_low, 0, quarter, d_qkv[:, :query_both], qkv_got[:quarter, :query_both])
    kv_own = product(
        normed1_low, 0, half, d_qkv[:, query_both : 2 * query_both], qkv_got[:, query_both : 2 * query_both]
    )
    kv_oth = product(normed1_low, 0, half, d_qkv[:, 2 * query_both :], qkv_got[:, 2 * query_both :])
    back_more, in_more, got_query, got_kv, flat_got, back_stay, in_stay, out_lo, query_lo, kv_own = go(
        (back_more, got_first, got_second, grad_own),
        (far[1], back_rest),
        (far[0], in_rest),
        (cross, columns(out_hi, query_hi)),
        (over, kv_oth),
        (over, flat),
        keep=(back_stay, in_stay, out_lo, query_lo, kv_own),
    )
    flat = flat + flat_got

    back_all = add(back_stay, back_more)
    in_all = add(in_stay, in_more)
    in_rest, in_stay = rest_start(in_all)
    out_lo = add(out_lo, got_query[:, :query_both])
    query_lo = add(query_lo, got_query[:, query_both:])
    kv_own = add(kv_own, got_kv)
    in_more, got_first, got_second, grad_other, flat_got, back_all, in_stay, out_lo, query_lo, kv_own = go(
        (in_more, got_query, got_kv),
        (far[1], in_rest),
        (over, columns(out_lo[:, inner_half:], query_lo[:, inner_half:])),
        (cross, kv_own[quarter:]),
        (over, grad_own),
        (cross, flat),
        keep=(back_all, in_stay, out_lo, query_lo, kv_own),
        join=False,
    )
    in_more, got_first, got_second, flat_got = lax.optimization_barrier(
        (in_more, got_first, got_second, flat_got)
    )
    flat = flat + flat_got

    def finish(value):
        value = value.astype(F32)
        for send in far[2:]:
            value = sum_half(value, send)
        return value

    back_all = finish(back_all)
    grad_back = back_all[:, :hidden_half]
    grad_pool = back_all[:, hidden_half:]
    last = columns(
        add(out_lo[:, :inner_half], got_first[:, :inner_half]),
        add(query_lo[:, :inner_half], got_first[:, inner_half:]),
        add(kv_own[:quarter], got_second),
    )
    last_rest, last_stay = rest_start(last)
    last_more, flat_got, pool_other, last_stay = go(
        (in_more, got_first, got_second),
        (far[0], last_rest),
        (core, flat),
        (over, grad_pool),
        keep=(last_stay,),
    )
    flat = flat + flat_got

    last = add(last_stay, last_more)
    last_rest, last_stay = rest_start(last)
    last_more, *flat_got = go(
        (grad_other,),
        (far[1], last_rest),
        *((functools.partial(hop, mask=j * 4), flat) for j in range(1, min(4, size // 4))),
    )
    flat = flat + sum(flat_got)
    for send in far[:-2]:
        flat = flat + send(flat)
    grad_last = finish(last_stay.astype(F32) + last_more.astype(F32))
    grad_in = finish(in_stay.astype(F32) + in_more.astype(F32))
    grad_out = grad_last[:, :inner_half]
    grad_qkv = grad_last[:, inner_half:]
    grad_tokens = jnp.where(
        mine == 0, jnp.stack([grad_own, grad_other]), jnp.stack([grad_other, grad_own])
    )
    across = width // LANES
    gains_mine = lax.dynamic_slice_in_dim(flat[: 3 * across].reshape(3, width), me * block, block, axis=1)
    loss = flat[3 * across, 0] / (micro_count * sent_local * size)
    table_sum = flat[small_rows - bucket_count :, : 2 * heads_half]
    table_mine = lax.dynamic_slice_in_dim(table_sum, mine * heads_half, heads_half, axis=1)
    grad_pool = jnp.where(mine == 0, columns(grad_pool, pool_other), columns(pool_other, grad_pool))
    return (
        loss,
        grad_tokens,
        grad_qkv[:, :inner_half],
        grad_qkv[:, inner_half : 2 * inner_half],
        grad_qkv[:, 2 * inner_half :],
        grad_out.T,
        grad_in,
        grad_back.T,
        gains_mine[0],
        gains_mine[1],
        gains_mine[2],
        grad_pool,
        table_mine,
    )


def solution(mesh):
    placed = (
        P(None, "dp", None),
        P(None, "dp", None),
        P(),
        P(None, "dp"),
        P("dp", "mp"),
        P("dp", "mp"),
        P("dp", "mp"),
        P("mp", "dp"),
        P("dp", "mp"),
        P("mp", "dp"),
        P("dp"),
        P("dp"),
        P("dp"),
        P("dp", None),
        P(None, "mp"),
    )
    return jax.shard_map(
        shards,
        mesh=mesh,
        in_specs=placed,
        out_specs=(
            P(),
            P(None, "dp", None),
            P("dp", "mp"),
            P("dp", "mp"),
            P("dp", "mp"),
            P("mp", "dp"),
            P("dp", "mp"),
            P("mp", "dp"),
            P("dp"),
            P("dp"),
            P("dp"),
            P("dp", None),
            P(None, "mp"),
        ),
        check_vma=False,
    )
```

```python
import functools

import jax
import jax.numpy as jnp
from jax import lax
from jax.experimental import pallas as pl
from jax.experimental.pallas import tpu as pltpu
from jax.sharding import PartitionSpec as P

NEG_FILL = -1000000000.0
SCORE_SCALE = 0.125
SOFTMAX_TEMP = 50.0
LOSS_SCALE = 64.0
EPSILON = 1e-06
REACH = 32
QB = 64
WIN = QB + 2 * REACH
LANES = 128
GELU_A = 0.7978845608028654
GELU_B = 0.044715

BF16 = jnp.bfloat16
F32 = jnp.float32
HIGHEST = lax.Precision.HIGHEST


def dot(left, right, dims=((1,), (0,)), precision=None):
    return lax.dot_general(
        left, right, (dims, ((), ())), precision=precision, preferred_element_type=F32
    )


def dot_nt(left, right):
    return dot(left, right, ((1,), (1,)))


def dot_tn(left, right):
    return dot(left, right, ((0,), (0,)))


def rms_forward(value, gain):
    inverse = lax.rsqrt(jnp.mean(value * value, axis=-1, keepdims=True) + EPSILON)
    return (value * inverse * gain, inverse)


def cost(flops, bytes_accessed):
    return pl.CostEstimate(flops=0, bytes_accessed=0, transcendentals=0)


def params(mib=16):
    return pltpu.CompilerParams(vmem_limit_bytes=mib * 2**20)


def split_dot(left, right, dims=((1,), (0,))):
    high = right.astype(BF16)
    rest = (right - high.astype(F32)).astype(BF16)
    return dot(left, high, dims) + dot(left, rest, dims)


def stream_kernel(plan, operands, outs, body, *refs):
    sources, out_refs = refs[:operands], refs[operands : operands + outs]
    more = refs[operands + outs :]
    buffers, sem = more[: sum(len(load) > 1 for load in plan)], more[-1]
    more = more[len(buffers) : -1]
    copies, places, used = [], [], 0
    for load in plan:
        if len(load) == 1:
            which, _, _, col, width, _ = load[0]
            places.append(sources[which].at[:, pl.ds(col, width)])
            copies.append([])
            continue
        buffer = buffers[used]
        used += 1
        group = []
        for which, at, count, col, width, number in load:
            copy = pltpu.make_async_copy(
                sources[which].at[:, pl.ds(col, width)], buffer.at[pl.ds(at, count)], sem.at[number]
            )
            copy.start()
            group.append(copy)
        places.append(buffer)
        copies.append(group)
    ready = set()

    def get(i):
        if i not in ready:
            ready.add(i)
            for copy in copies[i]:
                copy.wait()
        return places[i]

    body(get, *out_refs, *more)


def stream(name, loads, out_shapes, body, scratch=(), mib=16):
    arrays, spaces = [], []

    def place(array, space):
        for i, known in enumerate(arrays):
            if known is array and spaces[i] is space:
                return i
        arrays.append(array)
        spaces.append(space)
        return len(arrays) - 1

    plan, buffers, number = [], [], 0
    for load in loads:
        steps, at = [], 0
        space = pltpu.VMEM if len(load) == 1 else pl.ANY
        for array, col, width in load:
            steps.append((place(array, space), at, array.shape[0], col, width, number))
            at += array.shape[0]
            number += 1
        plan.append(steps)
        if len(load) > 1:
            buffers.append(pltpu.VMEM((at, load[0][2]), load[0][0].dtype))
    return pl.pallas_call(
        functools.partial(stream_kernel, plan, len(arrays), len(out_shapes), body),
        out_shape=tuple(out_shapes),
        in_specs=[pl.BlockSpec(memory_space=space) for space in spaces],
        out_specs=tuple(pl.BlockSpec(memory_space=pltpu.VMEM) for _ in out_shapes),
        scratch_shapes=buffers + list(scratch) + [pltpu.SemaphoreType.DMA((number,))],
        compiler_params=params(mib),
        cost_estimate=cost(0, 0),
        name=name,
    )(*arrays)


def part(array, col=0, width=None):
    return [(array, col, array.shape[1] - col if width is None else width)]


def weight(pieces, col, width):
    return [(piece, col, width) for piece in pieces]


def wide(name, x, blocks, extras=(), body=None, outs=1):
    widths = [width for *_, width in blocks]
    loads = [part(x)]
    for i, block in enumerate(blocks):
        loads.append(weight(*block))
        for extra in extras:
            loads.append(part(extra, sum(widths[:i]), widths[i]))

    def run(get, *out_refs):
        at = 0
        per = 1 + len(extras)
        for i, width in enumerate(widths):
            first = 1 + i * per
            value = dot(get(0)[...], get(first)[...])
            got = [get(first + 1 + j)[...] for j in range(len(extras))]
            values = (value,) if body is None else body(value, *got)
            for ref, result in zip(out_refs, values):
                ref[:, at : at + width] = result.astype(BF16)
            at += width

    shape = shape_of(BF16, x.shape[0], sum(widths))
    result = stream(name, loads, (shape,) * outs, run)
    return result if outs > 1 else result[0]


def gelu_both(up):
    square = up * up
    bend = jnp.tanh(GELU_A * up * (1.0 + GELU_B * square))
    half_one = 0.5 + 0.5 * bend
    inner = GELU_A + (3.0 * GELU_A * GELU_B) * square
    return up * half_one, half_one + 0.5 * up * (1.0 - bend * bend) * inner


def times_slope(value, slope):
    return (value * slope.astype(F32),)


def narrow(name, work, extras, out_shapes, body, scratch=(), mib=16):
    loads = []
    for x, x_col, pieces, col, width in work:
        loads += [part(x, x_col, width), weight(pieces, col, width)]
    first = len(loads)
    loads += [extra if isinstance(extra, list) else part(extra) for extra in extras]

    def run(get, *refs):
        out_refs, more = refs[: len(out_shapes)], refs[len(out_shapes) :]
        acc = more[0]
        for j in range(len(work)):
            value = dot_nt(get(2 * j)[...], get(2 * j + 1)[...])
            acc[...] = value if j == 0 else acc[...] + value
        body(acc, *(get(first + i) for i in range(len(extras))), *out_refs, *more[1:])

    depth = sum(piece.shape[0] for piece in work[0][2])
    return stream(
        name, loads, out_shapes, run, [pltpu.VMEM((work[0][0].shape[0], depth), F32), *scratch], mib
    )


def gradients(name, left, first, count, rights, out_of=None):
    loads = [part(left, first, count)] + [part(right) for right in rights]

    def run(get, *refs):
        *out_refs, turned = refs
        turned[...] = get(0)[...].T
        for i, ref in enumerate(out_refs):
            ref[...] = dot(turned[...], get(1 + i)[...]).astype(BF16)

    shapes = [shape_of(BF16, count, right.shape[1]) for right in rights]
    return stream(name, loads, shapes, run, [pltpu.VMEM((count, left.shape[0]), BF16)])


def sent_columns(name, first, pairs):
    loads = [load for left, right in pairs for load in (part(left, first, first), part(right))]

    def run(get, out_ref, turned):
        at = 0
        for i, (_, right) in enumerate(pairs):
            turned[...] = get(2 * i)[...].T
            n = right.shape[1]
            out_ref[:, at : at + n] = dot(turned[...], get(2 * i + 1)[...]).astype(BF16)
            at += n

    shape = shape_of(BF16, first, sum(right.shape[1] for _, right in pairs))
    return stream(name, loads, (shape,), run, [pltpu.VMEM((first, pairs[0][0].shape[0]), BF16)])[0]


def stack_rows(pieces, widths):
    block = pieces[0].shape[0]
    cuts = [sum(widths[:i]) for i in range(len(widths))]
    if block % 16:
        whole = jnp.concatenate(pieces, axis=0)
        return [whole[:, at : at + width] for at, width in zip(cuts, widths)]

    def run(*refs):
        for i, ref in enumerate(refs[: len(pieces)]):
            for j, out in enumerate(refs[len(pieces) :]):
                out[i * block : (i + 1) * block] = ref[:, cuts[j] : cuts[j] + widths[j]]

    shapes = [shape_of(pieces[0].dtype, block * len(pieces), width) for width in widths]
    return whole_call(run, pieces, shapes, (), "stack_rows")


def qkv_call(inputs, inverse, first, n):
    blocks = [(side, i * n, n) for i in range(3) for side in first]
    loads = [part(inputs), part(inverse), weight(first[0], 3 * n, LANES)]
    loads += [weight(*block) for block in blocks]

    def run(get, qkv_ref, normed_ref, gains_ref):
        gains = get(2)[...].astype(F32).T[:8]
        gains_ref[...] = gains
        normed = (get(0)[...] * get(1)[...] * gains[0:1]).astype(BF16)
        normed_ref[...] = normed
        for i in range(len(blocks)):
            qkv_ref[:, i * n : (i + 1) * n] = dot(normed_ref[...], get(3 + i)[...]).astype(BF16)

    seq, width = inputs.shape
    shapes = (shape_of(BF16, seq, 6 * n), shape_of(BF16, seq, width), shape_of(F32, 8, width))
    return stream("qkv", loads, shapes, run)


def norm_body(row, acc, value_ref, gains_ref, hidden_ref, inverse_ref, normed_ref=None):
    hidden = value_ref[...] + acc[...]
    inverse = lax.rsqrt(jnp.mean(hidden * hidden, axis=1, keepdims=True) + EPSILON)
    hidden_ref[...] = hidden
    inverse_ref[...] = inverse
    if normed_ref is not None:
        normed_ref[...] = (hidden * inverse * gains_ref[row : row + 1, :]).astype(BF16)


def norm_back(value, inverse, gain, grad):
    scaled = grad * gain
    inner = jnp.mean(value * scaled, axis=1, keepdims=True)
    d_value = inverse * scaled - value * (inverse * inverse * inverse) * inner
    return d_value, jnp.sum(grad * value * inverse, axis=0, keepdims=True)


def back_body(row, acc, value_ref, inverse_ref, gains_ref, grad_ref, low_ref, gain_out, hidden_ref=None):
    d_value, d_gain = norm_back(
        value_ref[...], inverse_ref[...], gains_ref[row : row + 1, :], acc[...]
    )
    total = grad_ref[...] + d_value
    low_ref[...] = total.astype(BF16)
    gain_out[...] = d_gain
    if hidden_ref is not None:
        hidden_ref[...] = total


def turn_kernel(grad_ref, order_ref, out_ref):
    out_ref[...] = dot_nt(grad_ref[...], order_ref[...]).astype(BF16)


def small_kernel(heads_half, one_ref, two_ref, three_ref, order_ref, bias_ref, onehot_ref, loss_ref, mine_ref, out_ref):
    width = one_ref.shape[1]
    gains = jnp.concatenate([one_ref[...], two_ref[...], three_ref[...], jnp.zeros((5, width), F32)], axis=0)
    high = gains.astype(BF16)
    rest = (gains - high.astype(F32)).astype(BF16)
    gains = dot_nt(high, order_ref[...]) + dot_nt(rest, order_ref[...])
    out_ref[...] = jnp.zeros_like(out_ref)
    across = width // LANES
    for i in range(3):
        for j in range(across):
            at = i * across + j
            out_ref[at : at + 1, :] = gains[i : i + 1, j * LANES : (j + 1) * LANES]
    at = 3 * across
    lane = lax.broadcasted_iota(jnp.int32, (1, LANES), 1)
    out_ref[at : at + 1, :] = jnp.where(lane == 0, loss_ref[...], 0.0)
    bias = bias_ref[...]
    row = lax.broadcasted_iota(jnp.int32, (LANES, bias.shape[0]), 0)
    column = lax.broadcasted_iota(jnp.int32, (LANES, bias.shape[0]), 1)
    pick = jnp.where((column == 8 * (row // 2) + row % 2) & (row < 2 * heads_half), 1.0, 0.0)
    bias = split_dot(pick.astype(BF16), bias)
    high = bias.astype(BF16)
    rest = (bias - high.astype(F32)).astype(BF16)
    buckets = onehot_ref[...]
    table = dot_nt(buckets, high) + dot_nt(buckets, rest)
    lane = lax.broadcasted_iota(jnp.int32, table.shape, 1)
    swapped = jnp.where(
        lane < heads_half, pltpu.roll(table, LANES - heads_half, 1), pltpu.roll(table, heads_half, 1)
    )
    top = -(-(at + 1) // 8) * 8
    out_ref[top : top + table.shape[0], :] = jnp.where(mine_ref[...] == 0, table, swapped)


def member_of(seg_ref, sent_count):
    ids = lax.broadcasted_iota(jnp.int32, (sent_count, seg_ref.shape[1]), 0)
    hit = jnp.where(seg_ref[...] == ids, 1.0, 0.0)
    return hit.astype(BF16), jnp.sum(hit, axis=1, keepdims=True)


def tail_body(acc, value_ref, gains_ref, seg_ref, own_ref, other_ref, hidden_ref, inverse_ref, pooled_ref, unit_ref, low_ref, scale_ref, high, rest):
    hidden = value_ref[...] + acc[...]
    inverse = lax.rsqrt(jnp.mean(hidden * hidden, axis=1, keepdims=True) + EPSILON)
    hidden_ref[...] = hidden
    inverse_ref[...] = inverse
    final = hidden_ref[...] * inverse * gains_ref[2:3, :]
    high[...] = final.astype(BF16)
    rest[...] = (final - high[...].astype(F32)).astype(BF16)
    sents, count = member_of(seg_ref, pooled_ref.shape[0])
    pooled = ((dot(sents, high[...]) + dot(sents, rest[...])) / count).astype(BF16)
    pooled_ref[...] = pooled
    half = own_ref.shape[1]
    left = dot(pooled, own_ref[...])
    right = dot(pooled, other_ref[...])
    square = jnp.sum(left * left, axis=1, keepdims=True) + jnp.sum(right * right, axis=1, keepdims=True)
    scale = lax.rsqrt(square + EPSILON)
    scale_ref[...] = scale
    for at, value in ((0, left * scale), (half, right * scale)):
        unit_ref[:, at : at + half] = value
        low_ref[:, at : at + half] = value.astype(BF16)


def head_call(quarters, unit, scale, partner, column, sentence_loads, out_shapes):
    loads = [part(q) for q in (*quarters, unit, scale, partner, column)] + sentence_loads
    quarter = quarters[0].shape[0]
    total = 4 * quarter

    def run(get, loss_ref, embed_ref, *refs):
        *back_refs, every = refs
        for i in range(4):
            every[i * quarter : (i + 1) * quarter] = get(i)[...]
        unit, scale, partner, columns_id = (get(i)[...] for i in range(4, 8))
        own_count = unit.shape[0]
        sims = dot_nt(every[...], every[...]) * SOFTMAX_TEMP
        row = lax.broadcasted_iota(jnp.int32, (total, total), 0)
        column = lax.broadcasted_iota(jnp.int32, (total, total), 1)
        sims = jnp.where(row == column, NEG_FILL, sims)
        top = jnp.max(sims, axis=0, keepdims=True)
        lse_row = top + jnp.log(jnp.sum(jnp.exp(sims - top), axis=0, keepdims=True))
        own = sims[:own_count]
        own_top = jnp.max(own, axis=1, keepdims=True)
        own_lse = own_top + jnp.log(jnp.sum(jnp.exp(own - own_top), axis=1, keepdims=True))
        is_target = columns_id == partner
        hit = jnp.where(is_target, 1.0, 0.0)
        target = jnp.sum(jnp.where(is_target, own, 0.0), axis=1, keepdims=True)
        loss_ref[...] = jnp.sum(own_lse - target, axis=0, keepdims=True)
        d_rows = (LOSS_SCALE * (jnp.exp(own - own_lse) - hit)).astype(BF16)
        d_cols = (LOSS_SCALE * (jnp.exp(own - lse_row) - hit)).astype(BF16)
        d_unit = SOFTMAX_TEMP * (dot(d_rows, every[...]) + dot(d_cols, every[...]))
        inner = jnp.sum(d_unit * unit, axis=1, keepdims=True)
        d_embed = (scale * (d_unit - unit * inner)).astype(BF16)
        embed_ref[...] = d_embed
        sentence_back(d_embed, [get(8 + i) for i in range(len(sentence_loads))], *back_refs)

    return stream("head", loads, out_shapes, run, [pltpu.VMEM((total, unit.shape[1]), BF16)])


def sentence_call(embed, sentence_loads, out_shapes):
    def run(get, *back_refs):
        sentence_back(get(0)[...], [get(1 + i) for i in range(len(sentence_loads))], *back_refs)

    return stream("sentence", [part(embed)] + sentence_loads, out_shapes, run)


def sentence_back(d_embed, sources, hidden_ref, low_ref, gain_out):
    seg_ref, own_ref, other_ref, value_ref, inverse_ref, gains_ref = sources
    half = own_ref.shape[1]
    d_pooled = dot_nt(d_embed[:, :half], own_ref[...]) + dot_nt(d_embed[:, half:], other_ref[...])
    sents, count = member_of(seg_ref, d_embed.shape[0])
    d_final = split_dot(sents, d_pooled / count, ((0,), (0,)))
    d_value, d_gain = norm_back(value_ref[...], inverse_ref[...], gains_ref[2:3, :], d_final)
    hidden_ref[...] = d_value
    low_ref[...] = d_value.astype(BF16)
    gain_out[...] = d_gain


def whole_call(body, args, out_shapes, scratch=(), name=None):
    return pl.pallas_call(
        body,
        out_shape=tuple(out_shapes),
        in_specs=[pl.BlockSpec(memory_space=pltpu.VMEM)] * len(args),
        out_specs=tuple(pl.BlockSpec(memory_space=pltpu.VMEM) for _ in out_shapes),
        scratch_shapes=scratch,
        compiler_params=params(),
        cost_estimate=cost(0, 0),
        name=name,
    )(*args)


def shape_of(kind, *dims):
    return jax.ShapeDtypeStruct(dims, kind)


def _stack_heads(part):
    lane = lax.broadcasted_iota(jnp.int32, part.shape, 1)
    zero = jnp.zeros_like(part)
    first = lane < LANES // 2
    return jnp.concatenate(
        [jnp.where(first, part, zero), jnp.where(first, zero, part)], axis=0
    )


def _unstack_heads(both):
    half = both.shape[0] // 2
    lane = lax.broadcasted_iota(jnp.int32, (half, LANES), 1)
    return jnp.where(lane < LANES // 2, both[:half], both[half:])


def _pad_keys(pad, ref):
    seq = ref.shape[0]
    pad[0:REACH] = jnp.zeros((REACH, LANES), pad.dtype)
    pad[REACH + seq :] = jnp.zeros((REACH, LANES), pad.dtype)
    pad[REACH : REACH + seq] = ref[...]


def _query_bits(shape):
    return lax.broadcasted_iota(jnp.int32, shape, 0) & (QB - 1)


def attend_forward_kernel(
    q_ref, k_ref, v_ref, segq_ref, segk_ref, rel_ref, ctx_ref, probs_ref, kpad, vpad, mask, scores
):
    seq = q_ref.shape[0]
    blocks = seq // QB
    _pad_keys(kpad, k_ref)
    _pad_keys(vpad, v_ref)

    @pl.when(pl.program_id(0) == 0)
    def _():
        for b in range(blocks):
            same = segk_ref[b * QB : b * QB + WIN] == segq_ref[b : b + 1, :]
            mask[b] = jnp.where(same, 0.0, NEG_FILL)

    rel = rel_ref[0]
    row = lax.broadcasted_iota(jnp.int32, (2 * QB, WIN), 0)
    bias = jnp.where(row < QB, rel[0:1, :], rel[1:2, :])
    bits = _query_bits((2 * QB, WIN))
    step = 1
    while step < QB:
        bias = jnp.where((bits & step) != 0, pltpu.roll(bias, step, 1), bias)
        step *= 2
    bias = bias.T
    for b in range(blocks):
        query = _stack_heads(q_ref[b * QB : (b + 1) * QB] * jnp.asarray(SCORE_SCALE, BF16))
        scores[b] = dot_nt(kpad[b * QB : b * QB + WIN], query)
    values = scores[...] + bias[None] + mask[...]
    top = jnp.max(values, axis=1, keepdims=True)
    shifted = jnp.exp(values - top)
    total = jnp.sum(shifted, axis=1, keepdims=True)
    probs_ref[0] = (shifted * (1.0 / total)).astype(BF16)
    for b in range(blocks):
        part = dot_tn(probs_ref[0, b], vpad[b * QB : b * QB + WIN])
        ctx_ref[b * QB : (b + 1) * QB] = _unstack_heads(part).astype(BF16)


def attend_backward_kernel(
    q_ref, k_ref, v_ref, dctx_ref, probs_ref, dqkv_ref, dbias_ref,
    kpad, vpad, dk_acc, dv_acc, d_probs, d_low,
):
    seq = q_ref.shape[0]
    pair = pl.program_id(0)
    side = pl.num_programs(0) // 2
    later = pair // side
    q_at = pl.ds(pl.multiple_of(pair * LANES, LANES), LANES)
    k_at = pl.ds(pl.multiple_of((pair + 2 * side + later * side) * LANES, LANES), LANES)
    v_at = pl.ds(pl.multiple_of((pair + 3 * side + later * side) * LANES, LANES), LANES)
    blocks = seq // QB
    _pad_keys(kpad, k_ref)
    _pad_keys(vpad, v_ref)
    dk_acc[...] = jnp.zeros_like(dk_acc)
    dv_acc[...] = jnp.zeros_like(dv_acc)
    for b in range(blocks):
        window = slice(b * QB, b * QB + WIN)
        d_ctx = _stack_heads(dctx_ref[b * QB : (b + 1) * QB])
        d_probs[b] = dot_nt(vpad[window], d_ctx)
        dv_acc[window] += dot(probs_ref[0, b], d_ctx)
    probs = probs_ref[0].astype(F32)
    product = probs * d_probs[...]
    inner = jnp.sum(product, axis=1, keepdims=True)
    d_scores = product - probs * inner
    d_low[...] = d_scores.astype(BF16)
    total = jnp.sum(d_scores, axis=0).T
    for b in range(blocks):
        here = slice(b * QB, (b + 1) * QB)
        window = slice(b * QB, b * QB + WIN)
        query = _stack_heads(q_ref[here] * jnp.asarray(SCORE_SCALE, BF16))
        dk_acc[window] += dot(d_low[b], query)
        d_query = _unstack_heads(dot_tn(d_low[b], kpad[window])) * SCORE_SCALE
        dqkv_ref[here, q_at] = d_query.astype(BF16)
    dqkv_ref[:, k_at] = dk_acc[REACH : REACH + seq].astype(BF16)
    dqkv_ref[:, v_at] = dv_acc[REACH : REACH + seq].astype(BF16)
    bits = _query_bits((2 * QB, WIN))
    step = 1
    while step < QB:
        total = jnp.where((bits & step) != 0, pltpu.roll(total, WIN - step, 1), total)
        step *= 2
    first = jnp.sum(total[:QB], axis=0, keepdims=True)
    second = jnp.sum(total[QB:], axis=0, keepdims=True)
    dbias_ref[0] = jnp.concatenate([first, second, jnp.zeros((6, WIN), F32)], axis=0)


def _qkv_specs(seq, pairs):
    def spec(kind):
        return pl.BlockSpec((seq, LANES), lambda p: (0, kind * pairs + p))

    return [spec(0), spec(1), spec(2)]


def attend_forward(qkv, seg_row, rel_window):
    seq = qkv.shape[0]
    pairs = rel_window.shape[0]
    blocks = seq // QB
    padded = jnp.pad(seg_row, (REACH, REACH), constant_values=-1)[:, None]
    twice = jnp.tile(seg_row.reshape(blocks, QB), (1, 2))
    return pl.pallas_call(
        attend_forward_kernel,
        grid=(pairs,),
        out_shape=(
            jax.ShapeDtypeStruct((seq, pairs * LANES), BF16),
            jax.ShapeDtypeStruct((pairs, blocks, WIN, 2 * QB), BF16),
        ),
        in_specs=_qkv_specs(seq, pairs)
        + [
            pl.BlockSpec((blocks, 2 * QB), lambda p: (0, 0)),
            pl.BlockSpec((seq + 2 * REACH, 1), lambda p: (0, 0)),
            pl.BlockSpec((1, 2, WIN), lambda p: (p, 0, 0)),
        ],
        out_specs=(
            pl.BlockSpec((seq, LANES), lambda p: (0, p)),
            pl.BlockSpec((1, blocks, WIN, 2 * QB), lambda p: (p, 0, 0, 0)),
        ),
        scratch_shapes=[pltpu.VMEM((seq + 2 * REACH, LANES), BF16)] * 2
        + [pltpu.VMEM((blocks, WIN, 2 * QB), F32)] * 2,
        compiler_params=params(),
        cost_estimate=cost(8 * seq * WIN * LANES * pairs * 4, 8 * seq * LANES * pairs),
        name="attend_forward",
    )(qkv, qkv, qkv, twice, padded, rel_window)


def attend_backward(qkv, d_context, probs):
    seq = qkv.shape[0]
    pairs = probs.shape[0]
    blocks = seq // QB
    lane_block = pl.BlockSpec((seq, LANES), lambda p: (0, p))
    return pl.pallas_call(
        attend_backward_kernel,
        grid=(pairs,),
        out_shape=(
            jax.ShapeDtypeStruct((seq, 3 * pairs * LANES), BF16),
            jax.ShapeDtypeStruct((pairs, 8, WIN), F32),
        ),
        in_specs=_qkv_specs(seq, pairs)
        + [
            lane_block,
            pl.BlockSpec((1, blocks, WIN, 2 * QB), lambda p: (p, 0, 0, 0)),
        ],
        out_specs=(
            pl.BlockSpec((seq, 3 * pairs * LANES), lambda p: (0, 0)),
            pl.BlockSpec((1, 8, WIN), lambda p: (p, 0, 0)),
        ),
        scratch_shapes=[pltpu.VMEM((seq + 2 * REACH, LANES), BF16)] * 2
        + [pltpu.VMEM((seq + 2 * REACH, LANES), F32)] * 2
        + [pltpu.VMEM((blocks, WIN, 2 * QB), F32), pltpu.VMEM((blocks, WIN, 2 * QB), BF16)],
        compiler_params=params(),
        cost_estimate=cost(16 * seq * WIN * LANES * pairs * 4, 16 * seq * LANES * pairs),
        name="attend_backward",
    )(qkv, qkv, qkv, d_context, probs)


CORE = 1
CROSS = 2


def hop(value, mask):
    size = lax.axis_size("dp")
    return lax.ppermute(value, "dp", [(i, i ^ mask) for i in range(size)])


def over(value):
    return lax.ppermute(value, "mp", [(0, 1), (1, 0)])


def cross(value):
    return hop(value, CROSS)


def core(value):
    return hop(value, CORE)


def go(waits, *sends, keep=(), join=True):
    values = [value for _, value in sends]
    held = lax.optimization_barrier((*values, *keep, *waits))
    results = [how(value) for (how, _), value in zip(sends, held)]
    if join:
        results = list(lax.optimization_barrier(tuple(results)))
    return results + list(held[len(values) : len(values) + len(keep)])


def slot_masks(size):
    rest = size // 4
    return [z * 4 + x * 2 + c for c in range(2) for x in range(2) for z in range(rest)]


def strides(size):
    found = []
    stride = 4
    while stride < size:
        found.append(stride)
        stride *= 2
    return found


def gather_near(shard, waits, widths=None):
    size = lax.axis_size("dp")
    pieces = [shard]
    stride = 4
    while stride < size:
        radix = min(4, size // stride)
        shard = jnp.concatenate(pieces, axis=0) if len(pieces) > 1 else shard
        sends = [(functools.partial(hop, mask=j * stride), shard) for j in range(1, radix)]
        pieces = [shard] + go(waits, *sends)
        stride *= radix
    return jnp.concatenate(pieces, axis=0) if widths is None else stack_rows(pieces, widths)


def rows(*pieces):
    return jnp.concatenate(pieces, axis=0)


def columns(*pieces):
    return jnp.concatenate(pieces, axis=1)


def gather_weights(one, two, three, four, between):
    size = lax.axis_size("dp")
    steps = strides(size)
    later = columns(three, four)
    n_three = three.shape[1]
    one, two = gather_near(columns(one, two), (), (one.shape[1], two.shape[1]))
    one_x, two_y, *more = go(
        (), (cross, one), (over, two), *((functools.partial(hop, mask=stride), later) for stride in steps[:1])
    )
    later = rows(later, *more)
    for stride in steps[1:-1]:
        later = rows(later, hop(later, stride))
    one_y, one_xy, two_x, two_yx, *more = go(
        (one_x, two_y),
        (over, one),
        (over, one_x),
        (cross, two),
        (cross, two_y),
        *((functools.partial(hop, mask=stride), later) for stride in steps[1:][-1:]),
    )
    if more and later.shape[0] % 16 == 0:
        three, four = stack_rows((later, *more), (n_three, later.shape[1] - n_three))
    else:
        later = rows(later, *more)
        three, four = later[:, :n_three], later[:, n_three:]
    three_x, four_y, one_c, one_xc, two_c = go(
        (),
        (cross, three),
        (over, four),
        (core, one),
        (core, one_x),
        (core, two),
        keep=(one_y, one_xy, two_x, two_yx, two_y),
        join=False,
    )[:5]
    two_yc, one_yc, one_xyc = go(
        (one_c, one_xc, two_c), (core, two_y), (core, one_y), (core, one_xy)
    )
    two_xc, two_yxc = go((two_yc, one_yc, one_xyc), (core, two_x), (core, two_yx))
    first = ((one, one_x, one_c, one_xc), (one_y, one_xy, one_yc, one_xyc))
    second = ((two, two_x, two_c, two_xc), (two_y, two_yx, two_yc, two_yxc))
    four_x, four_yx, three_y, three_xy, four_c, *kept = go(
        (three_x, four_y),
        (cross, four),
        (cross, four_y),
        (over, three),
        (over, three_x),
        (core, four),
        keep=(*first[0], *first[1], *second[0], *second[1]),
        join=False,
    )
    first = (tuple(kept[:4]), tuple(kept[4:8]))
    second = (tuple(kept[8:12]), tuple(kept[12:]))
    done = between(first, second)
    four_yc, three_c = go((four_c,), (core, four_y), (core, three))
    (three_xc,) = go((four_yc, three_c), (core, three_x))
    four_xc, four_yxc, three_yc, three_xyc, *done = go(
        (three_xc,),
        (core, four_x),
        (core, four_yx),
        (core, three_y),
        (core, three_xy),
        keep=done,
        join=False,
    )
    third = ((three, three_x, three_c, three_xc), (three_y, three_xy, three_yc, three_xyc))
    fourth = ((four, four_x, four_c, four_xc), (four_y, four_yx, four_yc, four_yxc))
    return first, second, third, fourth, done


def gather_dp(shard):
    near = gather_near(shard, ())
    side, c_near = go((near,), (cross, near), (core, near))
    return near, side, c_near, core(side)


def low(value):
    return value.astype(BF16)


def add(left, right):
    return (left.astype(F32) + right.astype(F32)).astype(BF16)


def product(left, begin, end, right, got=None):
    value = dot_tn(left[:, begin:end], right)
    if got is not None:
        value = value + got.astype(F32)
    return low(value)


def rest_start(value):
    half = value.shape[0] // 2
    return value[half:], value[:half]


def sum_half(value, send):
    gone, stays = rest_start(value)
    return stays + send(low(gone)).astype(F32)


def rest_hops(size):
    return [functools.partial(hop, mask=stride) for stride in reversed(strides(size))]


def shards(
    tokens,
    seg_ids,
    buckets,
    labels,
    w_query,
    w_key,
    w_value,
    w_out,
    w_in,
    w_back,
    gain_attn,
    gain_ffn,
    gain_final,
    w_pool,
    rel_table,
):
    micro_count, seq, width = tokens.shape
    size = lax.axis_size("dp")
    me = lax.axis_index("dp")
    mine = lax.axis_index("mp")
    block = width // size
    inner_half = w_query.shape[1]
    hidden_half = w_in.shape[1]
    sent_local = labels.shape[1]
    bucket_count = rel_table.shape[0]
    heads_half = rel_table.shape[1]
    masks = slot_masks(size)

    x_own = lax.dynamic_index_in_dim(tokens, mine, 0, keepdims=False)
    segments = lax.dynamic_index_in_dim(seg_ids, mine, 0, keepdims=False)[0]
    partner = lax.dynamic_index_in_dim(labels, mine, 0, keepdims=False)

    slot_block = jnp.stack([jnp.bitwise_xor(me, m) for m in masks]).astype(jnp.int32)
    source = (slot_block[:, None] * block + jnp.arange(block, dtype=jnp.int32)[None, :]).reshape(-1)
    order = (jnp.arange(width, dtype=jnp.int32)[:, None] == source[None, :]).astype(BF16)
    order = lax.optimization_barrier(order)
    inputs = dot(x_own, order)
    inverse1 = lax.rsqrt(jnp.mean(inputs * inputs, axis=1, keepdims=True) + EPSILON)

    rel_all = jnp.concatenate([rel_table, over(rel_table)], axis=1).astype(F32)
    near_buckets = lax.slice_in_dim(buckets, seq - 1 - REACH, seq - 1 - REACH + WIN)
    onehot = (near_buckets[None, :] == jnp.arange(bucket_count, dtype=jnp.int32)[:, None]).astype(F32)
    onehot = lax.optimization_barrier(low(onehot))
    rel_window = dot(rel_all, onehot.astype(F32), ((0,), (0,)), HIGHEST).reshape(heads_half, 2, WIN)

    row_f32 = shape_of(F32, seq, width)
    row_low = shape_of(BF16, seq, width)
    column_f32 = shape_of(F32, seq, 1)
    gain_f32 = shape_of(F32, 1, width)
    heads = 3 * inner_half
    piece = hidden_half // 2
    halves = [(side, i * inner_half, inner_half) for side in range(2) for i in range(2)]

    def hidden_blocks(weights, first_col=0):
        return [(weights[side], first_col + col, n) for side, col, n in halves]

    def between(first, second):
        qkv, normed1_low, gains = qkv_call(inputs, inverse1, first, inner_half)
        context, probs = attend_forward(qkv, segments, rel_window)
        hidden1, inverse2, normed2_low = narrow(
            "attn_out",
            [(context, i * inner_half, second[i], piece, inner_half) for i in range(2)],
            (inputs, gains),
            (row_f32, column_f32, row_low),
            functools.partial(norm_body, 1),
        )
        act0, slope0 = wide("act0", normed2_low, hidden_blocks(second), (), gelu_both, 2)
        return normed1_low, gains, qkv, context, probs, hidden1, inverse2, normed2_low, act0, slope0

    gains_col = jnp.pad(
        jnp.stack([gain_attn, gain_ffn, gain_final], axis=1), ((0, 0), (0, LANES - 3))
    )
    pool_half = w_pool.shape[1] // 2
    pool_own = lax.dynamic_slice_in_dim(w_pool, mine * pool_half, pool_half, axis=1)
    back_shard = w_back.T
    first, second, third, fourth, done = gather_weights(
        columns(w_query, w_key, w_value, gains_col),
        columns(w_in[:, :piece], w_out.T),
        columns(back_shard[:, :piece], pool_own),
        columns(w_in[:, piece:], back_shard[:, piece:]),
        between,
    )
    normed1_low, gains, qkv, context, probs, hidden1, inverse2, normed2_low, act0, slope0 = done

    act1, slope1 = wide("act1", normed2_low, hidden_blocks(fourth), (), gelu_both, 2)
    seg_lane = segments[None, :]
    local_ids = jnp.arange(sent_local, dtype=jnp.int32)
    pool_loads = [weight(side, piece, pool_half) for side in third]
    hidden2, inverse3, pooled_low, unit, unit_low, scale = narrow(
        "ffn_out",
        [(act0, i * piece, third[i], 0, piece) for i in range(2)]
        + [(act1, i * piece, fourth[i], piece, piece) for i in range(2)],
        (hidden1, gains, seg_lane, *pool_loads),
        (
            row_f32,
            column_f32,
            shape_of(BF16, sent_local, width),
            shape_of(F32, sent_local, width),
            shape_of(BF16, sent_local, width),
            shape_of(F32, sent_local, 1),
        ),
        tail_body,
        [pltpu.VMEM((seq, width), BF16)] * 2,
    )
    quarters = gather_dp(unit_low)

    column_id = (slot_block[:, None] * sent_local + local_ids[None, :]).reshape(1, -1)
    total_sent = column_id.shape[1]
    sentence_loads = [part(seg_lane), *pool_loads, part(hidden2), part(inverse3), part(gains)]
    back_shapes = (row_f32, row_low, gain_f32)
    if total_sent <= 1024:
        loss_local, embed_low, d_hidden2, ffn_low, d_gain3 = head_call(
            quarters,
            unit,
            scale,
            partner[:, None],
            column_id,
            sentence_loads,
            (shape_of(F32, 1, 1), shape_of(BF16, sent_local, width), *back_shapes),
        )
    else:
        every = rows(*quarters)
        position = jnp.arange(total_sent, dtype=jnp.int32)
        sims = dot_nt(every, every) * SOFTMAX_TEMP
        sims = jnp.where(position[:, None] == position[None, :], NEG_FILL, sims)
        lse_row = jax.nn.logsumexp(sims, axis=0, keepdims=True)
        own_sims = sims[:sent_local]
        own_lse = jax.nn.logsumexp(own_sims, axis=1, keepdims=True)
        is_target = column_id == partner[:, None]
        target = jnp.sum(jnp.where(is_target, own_sims, 0.0), axis=-1, keepdims=True)
        loss_local = jnp.sum(own_lse - target)
        hit = is_target.astype(F32)
        d_rows = low(LOSS_SCALE * (jnp.exp(own_sims - own_lse) - hit))
        d_cols = low(LOSS_SCALE * (jnp.exp(own_sims - lse_row) - hit))
        d_unit = SOFTMAX_TEMP * (dot(d_rows, every) + dot(d_cols, every))
        embed_low = low(scale * (d_unit - unit * jnp.sum(d_unit * unit, axis=-1, keepdims=True)))
        d_hidden2, ffn_low, d_gain3 = sentence_call(embed_low, sentence_loads, back_shapes)

    half = width // 2
    quarter = width // 4

    back0_sent, back1_sent = gradients("back_sent", ffn_low, half, half, (act0, act1))
    (pool_sent,) = gradients("pool_sent", pooled_low, half, half, (embed_low,))
    back0_got, back1_got, pool_got, ffn_later = go(
        (), (core, back0_sent), (core, back1_sent), (core, pool_sent), keep=(ffn_low,)
    )
    up0 = wide("up0", ffn_later, hidden_blocks(third), (slope0,), times_slope)

    pool_hi = product(pooled_low, quarter, half, embed_low, pool_got[quarter:])
    pool_lo = product(pooled_low, 0, quarter, embed_low, pool_got[:quarter])
    back_hi = product(ffn_low, quarter, half, act0, back0_got[quarter:])
    back_lo = product(ffn_low, 0, quarter, act0, back0_got[:quarter])
    back_own = product(ffn_low, 0, half, act1[:, :piece], back1_got[:, :piece])
    back_oth = product(ffn_low, 0, half, act1[:, piece:], back1_got[:, piece:])
    got_pool, got_lo, got_own, ffn_later, up0, pool_lo, back_lo, back_own = go(
        (),
        (cross, pool_hi),
        (cross, back_hi),
        (over, back_oth),
        keep=(ffn_later, up0, pool_lo, back_lo, back_own),
    )
    up1 = wide("up1", ffn_later, hidden_blocks(fourth, piece), (slope1,), times_slope)
    in0_sent, in1_sent = gradients("in_sent", normed2_low, half, half, (up0, up1))
    in0_got, in1_got, up0, up1 = go((), (core, in0_sent), (core, in1_sent), keep=(up0, up1))
    attn_low, d_gain2, d_hidden1 = narrow(
        "ffn_in_back",
        [(up0, i * piece, second[i], 0, piece) for i in range(2)]
        + [(up1, i * piece, fourth[i], 0, piece) for i in range(2)],
        (hidden1, inverse2, gains, d_hidden2),
        (row_low, gain_f32, row_f32),
        functools.partial(back_body, 1),
    )
    d_context = wide("d_context", attn_low, [(second[side], piece, inner_half) for side in range(2)])

    pool_lo = add(pool_lo, got_pool)
    back_lo = add(back_lo, got_lo)
    back_own = add(back_own, got_own)
    in_hi = product(normed2_low, quarter, half, up0, in0_got[quarter:])
    in_lo = product(normed2_low, 0, quarter, up0, in0_got[:quarter])
    in_own = product(normed2_low, 0, half, up1[:, :piece], in1_got[:, :piece])
    in_oth = product(normed2_low, 0, half, up1[:, piece:], in1_got[:, piece:])
    got_first, got_second, got_in_lo, got_in_own, d_context, pool_lo, back_lo, back_own, in_lo, in_own = go(
        (got_pool, got_lo, got_own),
        (over, columns(back_lo[:, piece:], pool_lo[:, pool_half:])),
        (cross, back_own[quarter:]),
        (cross, in_hi),
        (over, in_oth),
        keep=(d_context, pool_lo, back_lo, back_own, in_lo, in_own),
    )
    d_qkv, d_bias = attend_backward(qkv, d_context, probs)
    query_both = 2 * inner_half
    late_sent = sent_columns("late_sent", half, ((attn_low, context), (normed1_low, d_qkv)))
    late_got, d_qkv_later = go((), (core, late_sent), keep=(d_qkv,))
    grad_slots, d_gain1 = narrow(
        "qkv_back",
        [(d_qkv_later, i * inner_half, first[i], 0, inner_half) for i in range(2)]
        + [(d_qkv_later, (1 + i) * query_both, first[i], inner_half, query_both) for i in range(2)],
        (inputs, inverse1, gains, d_hidden1),
        (row_low, gain_f32),
        functools.partial(back_body, 0),
    )

    small_rows = -(-(3 * (width // LANES) + 1) // 8) * 8 + bucket_count
    (flat,) = whole_call(
        functools.partial(small_kernel, heads_half),
        (d_gain1, d_gain2, d_gain3, order, d_bias.reshape(-1, WIN), onehot, loss_local.reshape(1, 1), mine.reshape(1, 1)),
        (shape_of(F32, small_rows, LANES),),
        (),
        "small",
    )
    (grad_own,) = whole_call(turn_kernel, (grad_slots, order), (row_low,), (), "turn")

    far = rest_hops(size)
    back_all = columns(
        add(back_lo[:, :piece], got_first[:, :piece]),
        add(back_own[:quarter], got_second),
        add(pool_lo[:, :pool_half], got_first[:, piece:]),
    )
    back_rest, back_stay = rest_start(back_all)
    in_lo = add(in_lo, got_in_lo)
    in_own = add(in_own, got_in_own)
    out_got, qkv_got = late_got[:, :query_both], late_got[:, query_both:]
    out_hi = product(attn_low, quarter, half, context, out_got[quarter:])
    out_lo = product(attn_low, 0, quarter, context, out_got[:quarter])
    query_hi = product(normed1_low, quarter, half, d_qkv[:, :query_both], qkv_got[quarter:, :query_both])
    query_lo = product(normed1_low, 0, quarter, d_qkv[:, :query_both], qkv_got[:quarter, :query_both])
    kv_own = product(
        normed1_low, 0, half, d_qkv[:, query_both : 2 * query_both], qkv_got[:, query_both : 2 * query_both]
    )
    kv_oth = product(normed1_low, 0, half, d_qkv[:, 2 * query_both :], qkv_got[:, 2 * query_both :])
    back_more, got_first, got_second, got_query, got_kv, back_stay, in_lo, in_own, out_lo, query_lo, kv_own = go(
        (got_first, got_second, got_in_lo, got_in_own, late_got, grad_own, flat),
        (far[0], back_rest),
        (over, in_lo[:, piece:]),
        (cross, in_own[quarter:]),
        (cross, columns(out_hi, query_hi)),
        (over, kv_oth),
        keep=(back_stay, in_lo, in_own, out_lo, query_lo, kv_own),
    )

    back_all = add(back_stay, back_more)
    back_rest, back_stay = rest_start(back_all)
    in_all = columns(add(in_lo[:, :piece], got_first), add(in_own[:quarter], got_second))
    in_rest, in_stay = rest_start(in_all)
    out_lo = add(out_lo, got_query[:, :query_both])
    query_lo = add(query_lo, got_query[:, query_both:])
    kv_own = add(kv_own, got_kv)
    back_more, in_more, got_first, got_second, flat_got, back_stay, in_stay, out_lo, query_lo, kv_own = go(
        (back_more, got_first, got_second, got_query, got_kv),
        (far[1], back_rest),
        (far[0], in_rest),
        (over, columns(out_lo[:, inner_half:], query_lo[:, inner_half:])),
        (cross, kv_own[quarter:]),
        (over, flat),
        keep=(back_stay, in_stay, out_lo, query_lo, kv_own),
    )
    flat = flat + flat_got

    def finish(value):
        value = value.astype(F32)
        for send in far[2:]:
            value = sum_half(value, send)
        return value

    back_all = finish(back_stay.astype(F32) + back_more.astype(F32))
    grad_back = back_all[:, :hidden_half]
    grad_pool = back_all[:, hidden_half:]
    in_all = add(in_stay, in_more)
    in_rest, in_stay = rest_start(in_all)
    last = columns(
        add(out_lo[:, :inner_half], got_first[:, :inner_half]),
        add(query_lo[:, :inner_half], got_first[:, inner_half:]),
        add(kv_own[:quarter], got_second),
    )
    last_rest, last_stay = rest_start(last)
    in_more, last_more, grad_other, flat_got, pool_other, in_stay, last_stay = go(
        (in_more, got_first, got_second),
        (far[1], in_rest),
        (far[0], last_rest),
        (over, grad_own),
        (cross, flat),
        (over, grad_pool),
        keep=(in_stay, last_stay),
        join=False,
    )
    flat = flat + flat_got
    flat_got, flat = go((), (core, flat), keep=(flat,))
    flat = flat + flat_got

    last = add(last_stay, last_more)
    last_rest, last_stay = rest_start(last)
    last_more, *flat_got = go(
        (in_more, grad_other, pool_other),
        (far[1], last_rest),
        *((functools.partial(hop, mask=j * 4), flat) for j in range(1, min(4, size // 4))),
        join=False,
    )
    flat = flat + sum(flat_got)
    for send in far[:-2]:
        flat = flat + send(flat)
    grad_last = finish(last_stay.astype(F32) + last_more.astype(F32))
    grad_in = finish(in_stay.astype(F32) + in_more.astype(F32))
    grad_out = grad_last[:, :inner_half]
    grad_qkv = grad_last[:, inner_half:]
    grad_tokens = jnp.where(
        mine == 0, jnp.stack([grad_own, grad_other]), jnp.stack([grad_other, grad_own])
    )
    across = width // LANES
    gains_mine = lax.dynamic_slice_in_dim(flat[: 3 * across].reshape(3, width), me * block, block, axis=1)
    loss = flat[3 * across, 0] / (micro_count * sent_local * size)
    table_sum = flat[small_rows - bucket_count :, : 2 * heads_half]
    table_mine = lax.dynamic_slice_in_dim(table_sum, mine * heads_half, heads_half, axis=1)
    grad_pool = jnp.where(mine == 0, columns(grad_pool, pool_other), columns(pool_other, grad_pool))
    return (
        loss,
        grad_tokens,
        grad_qkv[:, :inner_half],
        grad_qkv[:, inner_half : 2 * inner_half],
        grad_qkv[:, 2 * inner_half :],
        grad_out.T,
        grad_in,
        grad_back.T,
        gains_mine[0],
        gains_mine[1],
        gains_mine[2],
        grad_pool,
        table_mine,
    )


def solution(mesh):
    placed = (
        P(None, "dp", None),
        P(None, "dp", None),
        P(),
        P(None, "dp"),
        P("dp", "mp"),
        P("dp", "mp"),
        P("dp", "mp"),
        P("mp", "dp"),
        P("dp", "mp"),
        P("mp", "dp"),
        P("dp"),
        P("dp"),
        P("dp"),
        P("dp", None),
        P(None, "mp"),
    )
    return jax.shard_map(
        shards,
        mesh=mesh,
        in_specs=placed,
        out_specs=(
            P(),
            P(None, "dp", None),
            P("dp", "mp"),
            P("dp", "mp"),
            P("dp", "mp"),
            P("mp", "dp"),
            P("dp", "mp"),
            P("mp", "dp"),
            P("dp"),
            P("dp"),
            P("dp"),
            P("dp", None),
            P(None, "mp"),
        ),
        check_vma=False,
    )
```

```python
import functools

import jax
import jax.numpy as jnp
from jax import lax
from jax.experimental import pallas as pl
from jax.experimental.pallas import tpu as pltpu
from jax.sharding import PartitionSpec as P

NEG_FILL = -1000000000.0
SCORE_SCALE = 0.125
SOFTMAX_TEMP = 50.0
LOSS_SCALE = 64.0
EPSILON = 1e-06
REACH = 32
QB = 64
WIN = QB + 2 * REACH
LANES = 128
GELU_A = 0.7978845608028654
GELU_B = 0.044715

BF16 = jnp.bfloat16
F32 = jnp.float32
HIGHEST = lax.Precision.HIGHEST


def dot(left, right, dims=((1,), (0,)), precision=None):
    return lax.dot_general(
        left, right, (dims, ((), ())), precision=precision, preferred_element_type=F32
    )


def dot_nt(left, right):
    return dot(left, right, ((1,), (1,)))


def dot_tn(left, right):
    return dot(left, right, ((0,), (0,)))


def rms_forward(value, gain):
    inverse = lax.rsqrt(jnp.mean(value * value, axis=-1, keepdims=True) + EPSILON)
    return (value * inverse * gain, inverse)


def cost(flops, bytes_accessed):
    return pl.CostEstimate(flops=0, bytes_accessed=0, transcendentals=0)


def params(mib=16):
    return pltpu.CompilerParams(vmem_limit_bytes=mib * 2**20)


def split_dot(left, right, dims=((1,), (0,))):
    high = right.astype(BF16)
    rest = (right - high.astype(F32)).astype(BF16)
    return dot(left, high, dims) + dot(left, rest, dims)


def stream_kernel(plan, operands, outs, body, *refs):
    sources, out_refs = refs[:operands], refs[operands : operands + outs]
    more = refs[operands + outs :]
    buffers, sem = more[: sum(len(load) > 1 for load in plan)], more[-1]
    more = more[len(buffers) : -1]
    copies, places, used = [], [], 0
    for load in plan:
        if len(load) == 1:
            which, _, _, col, width, _ = load[0]
            places.append(sources[which].at[:, pl.ds(col, width)])
            copies.append([])
            continue
        buffer = buffers[used]
        used += 1
        group = []
        for which, at, count, col, width, number in load:
            copy = pltpu.make_async_copy(
                sources[which].at[:, pl.ds(col, width)], buffer.at[pl.ds(at, count)], sem.at[number]
            )
            copy.start()
            group.append(copy)
        places.append(buffer)
        copies.append(group)
    ready = set()

    def get(i):
        if i not in ready:
            ready.add(i)
            for copy in copies[i]:
                copy.wait()
        return places[i]

    body(get, *out_refs, *more)


def stream(name, loads, out_shapes, body, scratch=(), mib=16):
    arrays, spaces = [], []

    def place(array, space):
        for i, known in enumerate(arrays):
            if known is array and spaces[i] is space:
                return i
        arrays.append(array)
        spaces.append(space)
        return len(arrays) - 1

    plan, buffers, number = [], [], 0
    for load in loads:
        steps, at = [], 0
        space = pltpu.VMEM if len(load) == 1 else pltpu.HBM
        for array, col, width in load:
            steps.append((place(array, space), at, array.shape[0], col, width, number))
            at += array.shape[0]
            number += 1
        plan.append(steps)
        if len(load) > 1:
            buffers.append(pltpu.VMEM((at, load[0][2]), load[0][0].dtype))
    return pl.pallas_call(
        functools.partial(stream_kernel, plan, len(arrays), len(out_shapes), body),
        out_shape=tuple(out_shapes),
        in_specs=[pl.BlockSpec(memory_space=space) for space in spaces],
        out_specs=tuple(pl.BlockSpec(memory_space=pltpu.VMEM) for _ in out_shapes),
        scratch_shapes=buffers + list(scratch) + [pltpu.SemaphoreType.DMA((number,))],
        compiler_params=params(mib),
        cost_estimate=cost(0, 0),
        name=name,
    )(*arrays)


def part(array, col=0, width=None):
    return [(array, col, array.shape[1] - col if width is None else width)]


def weight(pieces, col, width):
    return [(piece, col, width) for piece in pieces]


def wide(name, x, blocks, extras=(), body=None, outs=1):
    widths = [width for *_, width in blocks]
    loads = [part(x)]
    for i, block in enumerate(blocks):
        loads.append(weight(*block))
        for extra in extras:
            loads.append(part(extra, sum(widths[:i]), widths[i]))

    def run(get, *out_refs):
        at = 0
        per = 1 + len(extras)
        for i, width in enumerate(widths):
            first = 1 + i * per
            value = dot(get(0)[...], get(first)[...])
            got = [get(first + 1 + j)[...] for j in range(len(extras))]
            values = (value,) if body is None else body(value, *got)
            for ref, result in zip(out_refs, values):
                ref[:, at : at + width] = result.astype(BF16)
            at += width

    shape = shape_of(BF16, x.shape[0], sum(widths))
    result = stream(name, loads, (shape,) * outs, run)
    return result if outs > 1 else result[0]


def gelu_both(up):
    square = up * up
    bend = jnp.tanh(GELU_A * up * (1.0 + GELU_B * square))
    half_one = 0.5 + 0.5 * bend
    inner = GELU_A + (3.0 * GELU_A * GELU_B) * square
    return up * half_one, half_one + 0.5 * up * (1.0 - bend * bend) * inner


def times_slope(value, slope):
    return (value * slope.astype(F32),)


def narrow(name, work, extras, out_shapes, body, scratch=(), mib=16):
    loads = []
    for x, x_col, pieces, col, width in work:
        loads += [part(x, x_col, width), weight(pieces, col, width)]
    first = len(loads)
    loads += [extra if isinstance(extra, list) else part(extra) for extra in extras]

    def run(get, *refs):
        out_refs, more = refs[: len(out_shapes)], refs[len(out_shapes) :]
        acc = more[0]
        for j in range(len(work)):
            value = dot_nt(get(2 * j)[...], get(2 * j + 1)[...])
            acc[...] = value if j == 0 else acc[...] + value
        body(acc, *(get(first + i) for i in range(len(extras))), *out_refs, *more[1:])

    depth = sum(piece.shape[0] for piece in work[0][2])
    return stream(
        name, loads, out_shapes, run, [pltpu.VMEM((work[0][0].shape[0], depth), F32), *scratch], mib
    )


def gradients(name, left, first, count, rights, out_of=None):
    loads = [part(left, first, count)] + [part(right) for right in rights]

    def run(get, *refs):
        *out_refs, turned = refs
        turned[...] = get(0)[...].T
        for i, ref in enumerate(out_refs):
            ref[...] = dot(turned[...], get(1 + i)[...]).astype(BF16)

    shapes = [shape_of(BF16, count, right.shape[1]) for right in rights]
    return stream(name, loads, shapes, run, [pltpu.VMEM((count, left.shape[0]), BF16)])


def sent_columns(name, first, pairs):
    loads = [load for left, right in pairs for load in (part(left, first, first), part(right))]

    def run(get, out_ref, turned):
        at = 0
        for i, (_, right) in enumerate(pairs):
            turned[...] = get(2 * i)[...].T
            n = right.shape[1]
            out_ref[:, at : at + n] = dot(turned[...], get(2 * i + 1)[...]).astype(BF16)
            at += n

    shape = shape_of(BF16, first, sum(right.shape[1] for _, right in pairs))
    return stream(name, loads, (shape,), run, [pltpu.VMEM((first, pairs[0][0].shape[0]), BF16)])[0]


def stack_rows(pieces, widths):
    block = pieces[0].shape[0]
    cuts = [sum(widths[:i]) for i in range(len(widths))]
    if block % 16:
        whole = jnp.concatenate(pieces, axis=0)
        return [whole[:, at : at + width] for at, width in zip(cuts, widths)]

    def run(*refs):
        for i, ref in enumerate(refs[: len(pieces)]):
            for j, out in enumerate(refs[len(pieces) :]):
                out[i * block : (i + 1) * block] = ref[:, cuts[j] : cuts[j] + widths[j]]

    shapes = [shape_of(pieces[0].dtype, block * len(pieces), width) for width in widths]
    return whole_call(run, pieces, shapes, (), "stack_rows")


def qkv_call(inputs, inverse, first, n):
    blocks = [(side, i * n, n) for i in range(3) for side in first]
    loads = [part(inputs), part(inverse), weight(first[0], 3 * n, LANES)]
    loads += [weight(*block) for block in blocks]

    def run(get, qkv_ref, normed_ref, gains_ref):
        gains = get(2)[...].astype(F32).T[:8]
        gains_ref[...] = gains
        normed = (get(0)[...] * get(1)[...] * gains[0:1]).astype(BF16)
        normed_ref[...] = normed
        for i in range(len(blocks)):
            qkv_ref[:, i * n : (i + 1) * n] = dot(normed_ref[...], get(3 + i)[...]).astype(BF16)

    seq, width = inputs.shape
    shapes = (shape_of(BF16, seq, 6 * n), shape_of(BF16, seq, width), shape_of(F32, 8, width))
    return stream("qkv", loads, shapes, run)


def norm_body(row, acc, value_ref, gains_ref, hidden_ref, inverse_ref, normed_ref=None):
    hidden = value_ref[...] + acc[...]
    inverse = lax.rsqrt(jnp.mean(hidden * hidden, axis=1, keepdims=True) + EPSILON)
    hidden_ref[...] = hidden
    inverse_ref[...] = inverse
    if normed_ref is not None:
        normed_ref[...] = (hidden * inverse * gains_ref[row : row + 1, :]).astype(BF16)


def norm_back(value, inverse, gain, grad):
    scaled = grad * gain
    inner = jnp.mean(value * scaled, axis=1, keepdims=True)
    d_value = inverse * scaled - value * (inverse * inverse * inverse) * inner
    return d_value, jnp.sum(grad * value * inverse, axis=0, keepdims=True)


def back_body(row, acc, value_ref, inverse_ref, gains_ref, grad_ref, low_ref, gain_out, hidden_ref=None):
    d_value, d_gain = norm_back(
        value_ref[...], inverse_ref[...], gains_ref[row : row + 1, :], acc[...]
    )
    total = grad_ref[...] + d_value
    low_ref[...] = total.astype(BF16)
    gain_out[...] = d_gain
    if hidden_ref is not None:
        hidden_ref[...] = total


def turn_kernel(grad_ref, order_ref, out_ref):
    out_ref[...] = dot_nt(grad_ref[...], order_ref[...]).astype(BF16)


def small_kernel(heads_half, one_ref, two_ref, three_ref, order_ref, bias_ref, onehot_ref, loss_ref, mine_ref, out_ref):
    width = one_ref.shape[1]
    gains = jnp.concatenate([one_ref[...], two_ref[...], three_ref[...], jnp.zeros((5, width), F32)], axis=0)
    high = gains.astype(BF16)
    rest = (gains - high.astype(F32)).astype(BF16)
    gains = dot_nt(high, order_ref[...]) + dot_nt(rest, order_ref[...])
    out_ref[...] = jnp.zeros_like(out_ref)
    across = width // LANES
    for i in range(3):
        for j in range(across):
            at = i * across + j
            out_ref[at : at + 1, :] = gains[i : i + 1, j * LANES : (j + 1) * LANES]
    at = 3 * across
    lane = lax.broadcasted_iota(jnp.int32, (1, LANES), 1)
    out_ref[at : at + 1, :] = jnp.where(lane == 0, loss_ref[...], 0.0)
    bias = bias_ref[...]
    row = lax.broadcasted_iota(jnp.int32, (LANES, bias.shape[0]), 0)
    column = lax.broadcasted_iota(jnp.int32, (LANES, bias.shape[0]), 1)
    pick = jnp.where((column == 8 * (row // 2) + row % 2) & (row < 2 * heads_half), 1.0, 0.0)
    bias = split_dot(pick.astype(BF16), bias)
    high = bias.astype(BF16)
    rest = (bias - high.astype(F32)).astype(BF16)
    buckets = onehot_ref[...]
    table = dot_nt(buckets, high) + dot_nt(buckets, rest)
    lane = lax.broadcasted_iota(jnp.int32, table.shape, 1)
    swapped = jnp.where(
        lane < heads_half, pltpu.roll(table, LANES - heads_half, 1), pltpu.roll(table, heads_half, 1)
    )
    top = -(-(at + 1) // 8) * 8
    out_ref[top : top + table.shape[0], :] = jnp.where(mine_ref[...] == 0, table, swapped)


def member_of(seg_ref, sent_count):
    ids = lax.broadcasted_iota(jnp.int32, (sent_count, seg_ref.shape[1]), 0)
    hit = jnp.where(seg_ref[...] == ids, 1.0, 0.0)
    return hit.astype(BF16), jnp.sum(hit, axis=1, keepdims=True)


def tail_body(acc, value_ref, gains_ref, seg_ref, own_ref, other_ref, hidden_ref, inverse_ref, pooled_ref, unit_ref, low_ref, scale_ref, high, rest):
    hidden = value_ref[...] + acc[...]
    inverse = lax.rsqrt(jnp.mean(hidden * hidden, axis=1, keepdims=True) + EPSILON)
    hidden_ref[...] = hidden
    inverse_ref[...] = inverse
    final = hidden_ref[...] * inverse * gains_ref[2:3, :]
    high[...] = final.astype(BF16)
    rest[...] = (final - high[...].astype(F32)).astype(BF16)
    sents, count = member_of(seg_ref, pooled_ref.shape[0])
    pooled = ((dot(sents, high[...]) + dot(sents, rest[...])) / count).astype(BF16)
    pooled_ref[...] = pooled
    half = own_ref.shape[1]
    left = dot(pooled, own_ref[...])
    right = dot(pooled, other_ref[...])
    square = jnp.sum(left * left, axis=1, keepdims=True) + jnp.sum(right * right, axis=1, keepdims=True)
    scale = lax.rsqrt(square + EPSILON)
    scale_ref[...] = scale
    for at, value in ((0, left * scale), (half, right * scale)):
        unit_ref[:, at : at + half] = value
        low_ref[:, at : at + half] = value.astype(BF16)


def head_call(quarters, unit, scale, partner, column, sentence_loads, out_shapes):
    loads = [part(q) for q in (*quarters, unit, scale, partner, column)] + sentence_loads
    quarter = quarters[0].shape[0]
    total = 4 * quarter

    def run(get, loss_ref, embed_ref, *refs):
        *back_refs, every = refs
        for i in range(4):
            every[i * quarter : (i + 1) * quarter] = get(i)[...]
        unit, scale, partner, columns_id = (get(i)[...] for i in range(4, 8))
        own_count = unit.shape[0]
        sims = dot_nt(every[...], every[...]) * SOFTMAX_TEMP
        row = lax.broadcasted_iota(jnp.int32, (total, total), 0)
        column = lax.broadcasted_iota(jnp.int32, (total, total), 1)
        sims = jnp.where(row == column, NEG_FILL, sims)
        top = jnp.max(sims, axis=0, keepdims=True)
        lse_row = top + jnp.log(jnp.sum(jnp.exp(sims - top), axis=0, keepdims=True))
        own = sims[:own_count]
        own_top = jnp.max(own, axis=1, keepdims=True)
        own_lse = own_top + jnp.log(jnp.sum(jnp.exp(own - own_top), axis=1, keepdims=True))
        is_target = columns_id == partner
        hit = jnp.where(is_target, 1.0, 0.0)
        target = jnp.sum(jnp.where(is_target, own, 0.0), axis=1, keepdims=True)
        loss_ref[...] = jnp.sum(own_lse - target, axis=0, keepdims=True)
        d_rows = (LOSS_SCALE * (jnp.exp(own - own_lse) - hit)).astype(BF16)
        d_cols = (LOSS_SCALE * (jnp.exp(own - lse_row) - hit)).astype(BF16)
        d_unit = SOFTMAX_TEMP * (dot(d_rows, every[...]) + dot(d_cols, every[...]))
        inner = jnp.sum(d_unit * unit, axis=1, keepdims=True)
        d_embed = (scale * (d_unit - unit * inner)).astype(BF16)
        embed_ref[...] = d_embed
        sentence_back(d_embed, [get(8 + i) for i in range(len(sentence_loads))], *back_refs)

    return stream("head", loads, out_shapes, run, [pltpu.VMEM((total, unit.shape[1]), BF16)])


def sentence_call(embed, sentence_loads, out_shapes):
    def run(get, *back_refs):
        sentence_back(get(0)[...], [get(1 + i) for i in range(len(sentence_loads))], *back_refs)

    return stream("sentence", [part(embed)] + sentence_loads, out_shapes, run)


def sentence_back(d_embed, sources, hidden_ref, low_ref, gain_out):
    seg_ref, own_ref, other_ref, value_ref, inverse_ref, gains_ref = sources
    half = own_ref.shape[1]
    d_pooled = dot_nt(d_embed[:, :half], own_ref[...]) + dot_nt(d_embed[:, half:], other_ref[...])
    sents, count = member_of(seg_ref, d_embed.shape[0])
    d_final = split_dot(sents, d_pooled / count, ((0,), (0,)))
    d_value, d_gain = norm_back(value_ref[...], inverse_ref[...], gains_ref[2:3, :], d_final)
    hidden_ref[...] = d_value
    low_ref[...] = d_value.astype(BF16)
    gain_out[...] = d_gain


def whole_call(body, args, out_shapes, scratch=(), name=None):
    return pl.pallas_call(
        body,
        out_shape=tuple(out_shapes),
        in_specs=[pl.BlockSpec(memory_space=pltpu.VMEM)] * len(args),
        out_specs=tuple(pl.BlockSpec(memory_space=pltpu.VMEM) for _ in out_shapes),
        scratch_shapes=scratch,
        compiler_params=params(),
        cost_estimate=cost(0, 0),
        name=name,
    )(*args)


def shape_of(kind, *dims):
    return jax.ShapeDtypeStruct(dims, kind)


def _stack_heads(part):
    lane = lax.broadcasted_iota(jnp.int32, part.shape, 1)
    zero = jnp.zeros_like(part)
    first = lane < LANES // 2
    return jnp.concatenate(
        [jnp.where(first, part, zero), jnp.where(first, zero, part)], axis=0
    )


def _unstack_heads(both):
    half = both.shape[0] // 2
    lane = lax.broadcasted_iota(jnp.int32, (half, LANES), 1)
    return jnp.where(lane < LANES // 2, both[:half], both[half:])


def _pad_keys(pad, ref):
    seq = ref.shape[0]
    pad[0:REACH] = jnp.zeros((REACH, LANES), pad.dtype)
    pad[REACH + seq :] = jnp.zeros((REACH, LANES), pad.dtype)
    pad[REACH : REACH + seq] = ref[...]


def _query_bits(shape):
    return lax.broadcasted_iota(jnp.int32, shape, 0) & (QB - 1)


def attend_forward_kernel(
    q_ref, k_ref, v_ref, segq_ref, segk_ref, rel_ref, ctx_ref, probs_ref, kpad, vpad, mask, scores
):
    seq = q_ref.shape[0]
    blocks = seq // QB
    _pad_keys(kpad, k_ref)
    _pad_keys(vpad, v_ref)

    @pl.when(pl.program_id(0) == 0)
    def _():
        for b in range(blocks):
            same = segk_ref[b * QB : b * QB + WIN] == segq_ref[b : b + 1, :]
            mask[b] = jnp.where(same, 0.0, NEG_FILL)

    rel = rel_ref[0]
    row = lax.broadcasted_iota(jnp.int32, (2 * QB, WIN), 0)
    bias = jnp.where(row < QB, rel[0:1, :], rel[1:2, :])
    bits = _query_bits((2 * QB, WIN))
    step = 1
    while step < QB:
        bias = jnp.where((bits & step) != 0, pltpu.roll(bias, step, 1), bias)
        step *= 2
    bias = bias.T
    for b in range(blocks):
        query = _stack_heads(q_ref[b * QB : (b + 1) * QB] * jnp.asarray(SCORE_SCALE, BF16))
        scores[b] = dot_nt(kpad[b * QB : b * QB + WIN], query)
    values = scores[...] + bias[None] + mask[...]
    top = jnp.max(values, axis=1, keepdims=True)
    shifted = jnp.exp(values - top)
    total = jnp.sum(shifted, axis=1, keepdims=True)
    probs_ref[0] = (shifted * (1.0 / total)).astype(BF16)
    for b in range(blocks):
        part = dot_tn(probs_ref[0, b], vpad[b * QB : b * QB + WIN])
        ctx_ref[b * QB : (b + 1) * QB] = _unstack_heads(part).astype(BF16)


def attend_backward_kernel(
    q_ref, k_ref, v_ref, dctx_ref, probs_ref, dqkv_ref, dbias_ref,
    kpad, vpad, dk_acc, dv_acc, d_probs, d_low,
):
    seq = q_ref.shape[0]
    pair = pl.program_id(0)
    side = pl.num_programs(0) // 2
    later = pair // side
    q_at = pl.ds(pl.multiple_of(pair * LANES, LANES), LANES)
    k_at = pl.ds(pl.multiple_of((pair + 2 * side + later * side) * LANES, LANES), LANES)
    v_at = pl.ds(pl.multiple_of((pair + 3 * side + later * side) * LANES, LANES), LANES)
    blocks = seq // QB
    _pad_keys(kpad, k_ref)
    _pad_keys(vpad, v_ref)
    dk_acc[...] = jnp.zeros_like(dk_acc)
    dv_acc[...] = jnp.zeros_like(dv_acc)
    for b in range(blocks):
        window = slice(b * QB, b * QB + WIN)
        d_ctx = _stack_heads(dctx_ref[b * QB : (b + 1) * QB])
        d_probs[b] = dot_nt(vpad[window], d_ctx)
        dv_acc[window] += dot(probs_ref[0, b], d_ctx)
    probs = probs_ref[0].astype(F32)
    product = probs * d_probs[...]
    inner = jnp.sum(product, axis=1, keepdims=True)
    d_scores = product - probs * inner
    d_low[...] = d_scores.astype(BF16)
    total = jnp.sum(d_scores, axis=0).T
    for b in range(blocks):
        here = slice(b * QB, (b + 1) * QB)
        window = slice(b * QB, b * QB + WIN)
        query = _stack_heads(q_ref[here] * jnp.asarray(SCORE_SCALE, BF16))
        dk_acc[window] += dot(d_low[b], query)
        d_query = _unstack_heads(dot_tn(d_low[b], kpad[window])) * SCORE_SCALE
        dqkv_ref[here, q_at] = d_query.astype(BF16)
    dqkv_ref[:, k_at] = dk_acc[REACH : REACH + seq].astype(BF16)
    dqkv_ref[:, v_at] = dv_acc[REACH : REACH + seq].astype(BF16)
    bits = _query_bits((2 * QB, WIN))
    step = 1
    while step < QB:
        total = jnp.where((bits & step) != 0, pltpu.roll(total, WIN - step, 1), total)
        step *= 2
    first = jnp.sum(total[:QB], axis=0, keepdims=True)
    second = jnp.sum(total[QB:], axis=0, keepdims=True)
    dbias_ref[0] = jnp.concatenate([first, second, jnp.zeros((6, WIN), F32)], axis=0)


def _qkv_specs(seq, pairs):
    def spec(kind):
        return pl.BlockSpec((seq, LANES), lambda p: (0, kind * pairs + p))

    return [spec(0), spec(1), spec(2)]


def attend_forward(qkv, twice, padded, rel_window):
    seq = qkv.shape[0]
    pairs = rel_window.shape[0]
    blocks = seq // QB
    return pl.pallas_call(
        attend_forward_kernel,
        grid=(pairs,),
        out_shape=(
            jax.ShapeDtypeStruct((seq, pairs * LANES), BF16),
            jax.ShapeDtypeStruct((pairs, blocks, WIN, 2 * QB), BF16),
        ),
        in_specs=_qkv_specs(seq, pairs)
        + [
            pl.BlockSpec((blocks, 2 * QB), lambda p: (0, 0)),
            pl.BlockSpec((seq + 2 * REACH, 1), lambda p: (0, 0)),
            pl.BlockSpec((1, 2, WIN), lambda p: (p, 0, 0)),
        ],
        out_specs=(
            pl.BlockSpec((seq, LANES), lambda p: (0, p)),
            pl.BlockSpec((1, blocks, WIN, 2 * QB), lambda p: (p, 0, 0, 0)),
        ),
        scratch_shapes=[pltpu.VMEM((seq + 2 * REACH, LANES), BF16)] * 2
        + [pltpu.VMEM((blocks, WIN, 2 * QB), F32)] * 2,
        compiler_params=params(),
        cost_estimate=cost(8 * seq * WIN * LANES * pairs * 4, 8 * seq * LANES * pairs),
        name="attend_forward",
    )(qkv, qkv, qkv, twice, padded, rel_window)


def attend_backward(qkv, d_context, probs):
    seq = qkv.shape[0]
    pairs = probs.shape[0]
    blocks = seq // QB
    lane_block = pl.BlockSpec((seq, LANES), lambda p: (0, p))
    return pl.pallas_call(
        attend_backward_kernel,
        grid=(pairs,),
        out_shape=(
            jax.ShapeDtypeStruct((seq, 3 * pairs * LANES), BF16),
            jax.ShapeDtypeStruct((pairs, 8, WIN), F32),
        ),
        in_specs=_qkv_specs(seq, pairs)
        + [
            lane_block,
            pl.BlockSpec((1, blocks, WIN, 2 * QB), lambda p: (p, 0, 0, 0)),
        ],
        out_specs=(
            pl.BlockSpec((seq, 3 * pairs * LANES), lambda p: (0, 0)),
            pl.BlockSpec((1, 8, WIN), lambda p: (p, 0, 0)),
        ),
        scratch_shapes=[pltpu.VMEM((seq + 2 * REACH, LANES), BF16)] * 2
        + [pltpu.VMEM((seq + 2 * REACH, LANES), F32)] * 2
        + [pltpu.VMEM((blocks, WIN, 2 * QB), F32), pltpu.VMEM((blocks, WIN, 2 * QB), BF16)],
        compiler_params=params(),
        cost_estimate=cost(16 * seq * WIN * LANES * pairs * 4, 16 * seq * LANES * pairs),
        name="attend_backward",
    )(qkv, qkv, qkv, d_context, probs)


CORE = 1
CROSS = 2


def hop(value, mask):
    size = lax.axis_size("dp")
    return lax.ppermute(value, "dp", [(i, i ^ mask) for i in range(size)])


def over(value):
    return lax.ppermute(value, "mp", [(0, 1), (1, 0)])


def cross(value):
    return hop(value, CROSS)


def core(value):
    return hop(value, CORE)


def go(waits, *sends, keep=(), join=True):
    values = [value for _, value in sends]
    held = lax.optimization_barrier((*values, *keep, *waits))
    results = [how(value) for (how, _), value in zip(sends, held)]
    if join:
        results = list(lax.optimization_barrier(tuple(results)))
    return results + list(held[len(values) : len(values) + len(keep)])


def slot_masks(size):
    rest = size // 4
    return [z * 4 + x * 2 + c for c in range(2) for x in range(2) for z in range(rest)]


def strides(size):
    found = []
    stride = 4
    while stride < size:
        found.append(stride)
        stride *= 2
    return found


def gather_near(shard, waits, widths=None):
    size = lax.axis_size("dp")
    pieces = [shard]
    stride = 4
    while stride < size:
        radix = min(4, size // stride)
        shard = jnp.concatenate(pieces, axis=0) if len(pieces) > 1 else shard
        sends = [(functools.partial(hop, mask=j * stride), shard) for j in range(1, radix)]
        pieces = [shard] + go(waits, *sends)
        stride *= radix
    return jnp.concatenate(pieces, axis=0) if widths is None else stack_rows(pieces, widths)


def rows(*pieces):
    return jnp.concatenate(pieces, axis=0)


def columns(*pieces):
    return jnp.concatenate(pieces, axis=1)


def gather_weights(start, later, n_one, n_three, early, begin, between):
    steps = strides(lax.axis_size("dp"))
    one, two = gather_near(start, (), (n_one, start.shape[1] - n_one))
    one_x, two_y, *more, one_c, two_c = go(
        early,
        (cross, one),
        (over, two),
        *((functools.partial(hop, mask=stride), later) for stride in steps[:1]),
        (core, one),
        (core, two),
    )
    later = rows(later, *more)
    for stride in steps[1:-1]:
        later = rows(later, hop(later, stride))
    one_y, one_xy, two_x, two_yx, *more = go(
        (one_x, two_y, one_c, two_c),
        (over, one),
        (over, one_x),
        (cross, two),
        (cross, two_y),
        *((functools.partial(hop, mask=stride), later) for stride in steps[1:][-1:]),
    )
    if more and later.shape[0] % 16 == 0:
        three, four = stack_rows((later, *more), (n_three, later.shape[1] - n_three))
    else:
        later = rows(later, *more)
        three, four = later[:, :n_three], later[:, n_three:]
    three_x, four_y, one_xc, one_yc, one_xyc, two_y, two_x, two_yx = go(
        (),
        (cross, three),
        (over, four),
        (core, one_x),
        (core, one_y),
        (core, one_xy),
        keep=(two_y, two_x, two_yx),
    )
    first = ((one, one_x, one_c, one_xc), (one_y, one_xy, one_yc, one_xyc))
    four_x, three_y, two_yc, two_xc, two_yxc, *kept = go(
        (three_x, four_y),
        (cross, four),
        (over, three),
        (core, two_y),
        (core, two_x),
        (core, two_yx),
        keep=(*first[0], *first[1], *early),
    )
    first = (tuple(kept[:4]), tuple(kept[4:8]))
    early = kept[8:]
    started = begin(first, early)
    second = ((two, two_x, two_c, two_xc), (two_y, two_yx, two_yc, two_yxc))
    four_yx, three_xy, four_c, four_yc, three_c, *kept = go(
        (four_x, three_y, two_yc, two_xc, two_yxc),
        (cross, four_y),
        (over, three_x),
        (core, four),
        (core, four_y),
        (core, three),
        keep=(*second[0], *second[1], *started),
    )
    second = (tuple(kept[:4]), tuple(kept[4:8]))
    done = between(kept[8:], second, early)
    four_xc, four_yxc, three_xc, three_yc, three_xyc, *done = go(
        (four_yx, three_xy, four_c, four_yc, three_c),
        (core, four_x),
        (core, four_yx),
        (core, three_x),
        (core, three_y),
        (core, three_xy),
        keep=done,
        join=False,
    )
    third = ((three, three_x, three_c, three_xc), (three_y, three_xy, three_yc, three_xyc))
    fourth = ((four, four_x, four_c, four_xc), (four_y, four_yx, four_yc, four_yxc))
    return first, second, third, fourth, early, done


def pack_start(w_query, w_key, w_value, gains, w_in, w_out):
    block, n = w_query.shape
    wide_in = w_in.shape[1]

    def run(q_ref, k_ref, v_ref, g_ref, in_ref, out_ref_t, ref):
        ref[:, :n] = q_ref[...]
        ref[:, n : 2 * n] = k_ref[...]
        ref[:, 2 * n : 3 * n] = v_ref[...]
        ref[:, 3 * n : 3 * n + LANES] = g_ref[...]
        at = 3 * n + LANES
        ref[:, at : at + wide_in] = in_ref[...]
        ref[:, at + wide_in :] = out_ref_t[...]

    shape = shape_of(BF16, block, 3 * n + LANES + wide_in + w_out.shape[1])
    return whole_call(run, (w_query, w_key, w_value, gains, w_in, w_out), (shape,), (), "pack_start")[0]


def gather_dp(shard):
    near = gather_near(shard, ())
    side, c_near = go((near,), (cross, near), (core, near))
    return near, side, c_near, core(side)


def low(value):
    return value.astype(BF16)


def add(left, right):
    return (left.astype(F32) + right.astype(F32)).astype(BF16)


def product(left, begin, end, right, got=None):
    value = dot_tn(left[:, begin:end], right)
    if got is not None:
        value = value + got.astype(F32)
    return low(value)


def rest_start(value):
    half = value.shape[0] // 2
    return value[half:], value[:half]


def sum_half(value, send):
    gone, stays = rest_start(value)
    return stays + send(low(gone)).astype(F32)


def rest_hops(size):
    return [functools.partial(hop, mask=stride) for stride in reversed(strides(size))]


def shards(
    tokens,
    seg_ids,
    buckets,
    labels,
    w_query,
    w_key,
    w_value,
    w_out,
    w_in,
    w_back,
    gain_attn,
    gain_ffn,
    gain_final,
    w_pool,
    rel_table,
):
    micro_count, seq, width = tokens.shape
    size = lax.axis_size("dp")
    me = lax.axis_index("dp")
    mine = lax.axis_index("mp")
    block = width // size
    inner_half = w_query.shape[1]
    hidden_half = w_in.shape[1]
    sent_local = labels.shape[1]
    bucket_count = rel_table.shape[0]
    heads_half = rel_table.shape[1]
    masks = slot_masks(size)

    x_own = lax.dynamic_index_in_dim(tokens, mine, 0, keepdims=False)
    segments = lax.dynamic_index_in_dim(seg_ids, mine, 0, keepdims=False)[0]
    partner = lax.dynamic_index_in_dim(labels, mine, 0, keepdims=False)

    slot_block = jnp.stack([jnp.bitwise_xor(me, m) for m in masks]).astype(jnp.int32)
    source = (slot_block[:, None] * block + jnp.arange(block, dtype=jnp.int32)[None, :]).reshape(-1)
    order = (jnp.arange(width, dtype=jnp.int32)[:, None] == source[None, :]).astype(BF16)
    order = lax.optimization_barrier(order)
    inputs = dot(x_own, order)
    inverse1 = lax.rsqrt(jnp.mean(inputs * inputs, axis=1, keepdims=True) + EPSILON)

    rel_all = jnp.concatenate([rel_table, over(rel_table)], axis=1).astype(F32)
    near_buckets = lax.slice_in_dim(buckets, seq - 1 - REACH, seq - 1 - REACH + WIN)
    onehot = (near_buckets[None, :] == jnp.arange(bucket_count, dtype=jnp.int32)[:, None]).astype(F32)
    onehot = lax.optimization_barrier(low(onehot))
    rel_window = dot(rel_all, onehot.astype(F32), ((0,), (0,)), HIGHEST).reshape(heads_half, 2, WIN)

    row_f32 = shape_of(F32, seq, width)
    row_low = shape_of(BF16, seq, width)
    column_f32 = shape_of(F32, seq, 1)
    gain_f32 = shape_of(F32, 1, width)
    heads = 3 * inner_half
    piece = hidden_half // 2
    halves = [(side, i * inner_half, inner_half) for side in range(2) for i in range(2)]

    def hidden_blocks(weights, first_col=0):
        return [(weights[side], first_col + col, n) for side, col, n in halves]

    def begin(first, early):
        inputs, inverse1, rel_window, twice, padded, *_ = early
        qkv, normed1_low, gains = qkv_call(inputs, inverse1, first, inner_half)
        context, probs = attend_forward(qkv, twice, padded, rel_window)
        return qkv, normed1_low, gains, context, probs

    def between(started, second, early):
        qkv, normed1_low, gains, context, probs = started
        inputs = early[0]
        hidden1, inverse2, normed2_low = narrow(
            "attn_out",
            [(context, i * inner_half, second[i], piece, inner_half) for i in range(2)],
            (inputs, gains),
            (row_f32, column_f32, row_low),
            functools.partial(norm_body, 1),
        )
        act0, slope0 = wide("act0", normed2_low, hidden_blocks(second), (), gelu_both, 2)
        return normed1_low, gains, qkv, context, probs, hidden1, inverse2, normed2_low, act0, slope0

    gains_col = jnp.pad(
        jnp.stack([gain_attn, gain_ffn, gain_final], axis=1), ((0, 0), (0, LANES - 3))
    )
    pool_half = w_pool.shape[1] // 2
    pool_own = lax.dynamic_slice_in_dim(w_pool, mine * pool_half, pool_half, axis=1)
    back_shard = w_back.T
    padded = jnp.pad(segments, (REACH, REACH), constant_values=-1)[:, None]
    twice = jnp.tile(segments.reshape(seq // QB, QB), (1, 2))
    local_ids = jnp.arange(sent_local, dtype=jnp.int32)
    column_id = (slot_block[:, None] * sent_local + local_ids[None, :]).reshape(1, -1)
    early = (
        inputs, inverse1, rel_window, twice, padded, order, onehot, column_id, partner[:, None], segments[None, :]
    )
    first, second, third, fourth, early, done = gather_weights(
        pack_start(w_query, w_key, w_value, gains_col, w_in[:, :piece], w_out.T),
        columns(back_shard[:, :piece], pool_own, w_in[:, piece:], back_shard[:, piece:]),
        heads + LANES,
        piece + pool_half,
        early,
        begin,
        between,
    )
    inputs, inverse1, rel_window, twice, padded, order, onehot, column_id, partner, seg_lane = early
    normed1_low, gains, qkv, context, probs, hidden1, inverse2, normed2_low, act0, slope0 = done

    act1, slope1 = wide("act1", normed2_low, hidden_blocks(fourth), (), gelu_both, 2)
    pool_loads = [weight(side, piece, pool_half) for side in third]
    hidden2, inverse3, pooled_low, unit, unit_low, scale = narrow(
        "ffn_out",
        [(act0, i * piece, third[i], 0, piece) for i in range(2)]
        + [(act1, i * piece, fourth[i], piece, piece) for i in range(2)],
        (hidden1, gains, seg_lane, *pool_loads),
        (
            row_f32,
            column_f32,
            shape_of(BF16, sent_local, width),
            shape_of(F32, sent_local, width),
            shape_of(BF16, sent_local, width),
            shape_of(F32, sent_local, 1),
        ),
        tail_body,
        [pltpu.VMEM((seq, width), BF16)] * 2,
    )
    quarters = gather_dp(unit_low)

    total_sent = column_id.shape[1]
    sentence_loads = [part(seg_lane), *pool_loads, part(hidden2), part(inverse3), part(gains)]
    back_shapes = (row_f32, row_low, gain_f32)
    if total_sent <= 1024:
        loss_local, embed_low, d_hidden2, ffn_low, d_gain3 = head_call(
            quarters,
            unit,
            scale,
            partner,
            column_id,
            sentence_loads,
            (shape_of(F32, 1, 1), shape_of(BF16, sent_local, width), *back_shapes),
        )
    else:
        every = rows(*quarters)
        position = jnp.arange(total_sent, dtype=jnp.int32)
        sims = dot_nt(every, every) * SOFTMAX_TEMP
        sims = jnp.where(position[:, None] == position[None, :], NEG_FILL, sims)
        lse_row = jax.nn.logsumexp(sims, axis=0, keepdims=True)
        own_sims = sims[:sent_local]
        own_lse = jax.nn.logsumexp(own_sims, axis=1, keepdims=True)
        is_target = column_id == partner
        target = jnp.sum(jnp.where(is_target, own_sims, 0.0), axis=-1, keepdims=True)
        loss_local = jnp.sum(own_lse - target)
        hit = is_target.astype(F32)
        d_rows = low(LOSS_SCALE * (jnp.exp(own_sims - own_lse) - hit))
        d_cols = low(LOSS_SCALE * (jnp.exp(own_sims - lse_row) - hit))
        d_unit = SOFTMAX_TEMP * (dot(d_rows, every) + dot(d_cols, every))
        embed_low = low(scale * (d_unit - unit * jnp.sum(d_unit * unit, axis=-1, keepdims=True)))
        d_hidden2, ffn_low, d_gain3 = sentence_call(embed_low, sentence_loads, back_shapes)

    half = width // 2
    quarter = width // 4

    back0_sent, back1_sent = gradients("back_sent", ffn_low, half, half, (act0, act1))
    (pool_sent,) = gradients("pool_sent", pooled_low, half, half, (embed_low,))
    back0_got, back1_got, pool_got, ffn_later = go(
        (), (core, back0_sent), (core, back1_sent), (core, pool_sent), keep=(ffn_low,)
    )
    up0 = wide("up0", ffn_later, hidden_blocks(third), (slope0,), times_slope)

    pool_hi = product(pooled_low, quarter, half, embed_low, pool_got[quarter:])
    pool_lo = product(pooled_low, 0, quarter, embed_low, pool_got[:quarter])
    back_hi = product(ffn_low, quarter, half, act0, back0_got[quarter:])
    back_lo = product(ffn_low, 0, quarter, act0, back0_got[:quarter])
    back_own = product(ffn_low, 0, half, act1[:, :piece], back1_got[:, :piece])
    back_oth = product(ffn_low, 0, half, act1[:, piece:], back1_got[:, piece:])
    got_pool, got_lo, got_own, ffn_later, up0, pool_lo, back_lo, back_own = go(
        (),
        (cross, pool_hi),
        (cross, back_hi),
        (over, back_oth),
        keep=(ffn_later, up0, pool_lo, back_lo, back_own),
    )
    up1 = wide("up1", ffn_later, hidden_blocks(fourth, piece), (slope1,), times_slope)
    in0_sent, in1_sent = gradients("in_sent", normed2_low, half, half, (up0, up1))
    in0_got, in1_got, up0, up1 = go((), (core, in0_sent), (core, in1_sent), keep=(up0, up1))
    attn_low, d_gain2, d_hidden1 = narrow(
        "ffn_in_back",
        [(up0, i * piece, second[i], 0, piece) for i in range(2)]
        + [(up1, i * piece, fourth[i], 0, piece) for i in range(2)],
        (hidden1, inverse2, gains, d_hidden2),
        (row_low, gain_f32, row_f32),
        functools.partial(back_body, 1),
    )
    d_context = wide("d_context", attn_low, [(second[side], piece, inner_half) for side in range(2)])

    pool_lo = add(pool_lo, got_pool)
    back_lo = add(back_lo, got_lo)
    back_own = add(back_own, got_own)
    in_hi = product(normed2_low, quarter, half, up0, in0_got[quarter:])
    in_lo = product(normed2_low, 0, quarter, up0, in0_got[:quarter])
    in_own = product(normed2_low, 0, half, up1[:, :piece], in1_got[:, :piece])
    in_oth = product(normed2_low, 0, half, up1[:, piece:], in1_got[:, piece:])
    got_first, got_second, got_in_lo, got_in_own, d_context, pool_lo, back_lo, back_own, in_lo, in_own = go(
        (got_pool, got_lo, got_own),
        (over, columns(back_lo[:, piece:], pool_lo[:, pool_half:])),
        (cross, back_own[quarter:]),
        (cross, in_hi),
        (over, in_oth),
        keep=(d_context, pool_lo, back_lo, back_own, in_lo, in_own),
    )
    d_qkv, d_bias = attend_backward(qkv, d_context, probs)
    query_both = 2 * inner_half
    late_sent = sent_columns("late_sent", half, ((attn_low, context), (normed1_low, d_qkv)))
    late_got, d_qkv_later = go((), (core, late_sent), keep=(d_qkv,))
    grad_slots, d_gain1 = narrow(
        "qkv_back",
        [(d_qkv_later, i * inner_half, first[i], 0, inner_half) for i in range(2)]
        + [(d_qkv_later, (1 + i) * query_both, first[i], inner_half, query_both) for i in range(2)],
        (inputs, inverse1, gains, d_hidden1),
        (row_low, gain_f32),
        functools.partial(back_body, 0),
    )

    small_rows = -(-(3 * (width // LANES) + 1) // 8) * 8 + bucket_count
    (flat,) = whole_call(
        functools.partial(small_kernel, heads_half),
        (d_gain1, d_gain2, d_gain3, order, d_bias.reshape(-1, WIN), onehot, loss_local.reshape(1, 1), mine.reshape(1, 1)),
        (shape_of(F32, small_rows, LANES),),
        (),
        "small",
    )
    (grad_own,) = whole_call(turn_kernel, (grad_slots, order), (row_low,), (), "turn")

    far = rest_hops(size)
    back_all = columns(
        add(back_lo[:, :piece], got_first[:, :piece]),
        add(back_own[:quarter], got_second),
        add(pool_lo[:, :pool_half], got_first[:, piece:]),
    )
    back_rest, back_stay = rest_start(back_all)
    in_lo = add(in_lo, got_in_lo)
    in_own = add(in_own, got_in_own)
    out_got, qkv_got = late_got[:, :query_both], late_got[:, query_both:]
    out_hi = product(attn_low, quarter, half, context, out_got[quarter:])
    out_lo = product(attn_low, 0, quarter, context, out_got[:quarter])
    query_hi = product(normed1_low, quarter, half, d_qkv[:, :query_both], qkv_got[quarter:, :query_both])
    query_lo = product(normed1_low, 0, quarter, d_qkv[:, :query_both], qkv_got[:quarter, :query_both])
    kv_own = product(
        normed1_low, 0, half, d_qkv[:, query_both : 2 * query_both], qkv_got[:, query_both : 2 * query_both]
    )
    kv_oth = product(normed1_low, 0, half, d_qkv[:, 2 * query_both :], qkv_got[:, 2 * query_both :])
    rest_hop = [functools.partial(hop, mask=j * 4) for j in range(1, min(4, size // 4))]
    back_more, got_first, got_x, got_kv, flat_got, back_stay, in_lo, in_own, out_lo, query_lo, kv_own, flat = go(
        (got_first, got_second, got_in_lo, got_in_own, late_got, grad_own, flat),
        (far[0], back_rest),
        (over, in_lo[:, piece:]),
        (cross, columns(in_own[quarter:], out_hi, query_hi)),
        (over, kv_oth),
        (over, flat),
        keep=(back_stay, in_lo, in_own, out_lo, query_lo, kv_own, flat),
    )
    flat = flat + flat_got
    got_second, got_out, got_query = got_x[:, :piece], got_x[:, piece:][:, :query_both], got_x[:, piece + query_both :]

    back_all = add(back_stay, back_more)
    back_rest, back_stay = rest_start(back_all)
    in_all = columns(add(in_lo[:, :piece], got_first), add(in_own[:quarter], got_second))
    in_rest, in_stay = rest_start(in_all)
    out_lo = add(out_lo, got_out)
    query_lo = add(query_lo, got_query)
    kv_own = add(kv_own, got_kv)
    back_more, in_more, got_first, got_second, grad_other, flat_got, back_stay, in_stay, out_lo, query_lo, kv_own, flat = go(
        (),
        (far[1], back_rest),
        (far[0], in_rest),
        (over, columns(out_lo[:, inner_half:], query_lo[:, inner_half:])),
        (cross, kv_own[quarter:]),
        (over, grad_own),
        (core, flat),
        keep=(back_stay, in_stay, out_lo, query_lo, kv_own, flat),
        join=False,
    )
    back_more, in_more, got_first, got_second, flat_got = lax.optimization_barrier(
        (back_more, in_more, got_first, got_second, flat_got)
    )
    flat = flat + flat_got

    def finish(value):
        value = value.astype(F32)
        for send in far[2:]:
            value = sum_half(value, send)
        return value

    back_all = finish(back_stay.astype(F32) + back_more.astype(F32))
    grad_back = back_all[:, :hidden_half]
    grad_pool = back_all[:, hidden_half:]
    in_all = add(in_stay, in_more)
    in_rest, in_stay = rest_start(in_all)
    last = columns(
        add(out_lo[:, :inner_half], got_first[:, :inner_half]),
        add(query_lo[:, :inner_half], got_first[:, inner_half:]),
        add(kv_own[:quarter], got_second),
    )
    n_in, n_last = in_rest.shape[1], last.shape[1]
    if len(far) == 2:
        rest = last.shape[0] // 4
        got_one, got_two, got_three, flat_got, in_stay, last_stay, flat = go(
            (),
            (rest_hop[0], columns(in_rest, last[rest : 2 * rest])),
            (rest_hop[1], last[2 * rest : 3 * rest]),
            (rest_hop[2], last[3 * rest :]),
            (cross, flat),
            keep=(in_stay, last[:rest], flat),
        )
        in_more = got_one[:, :n_in]
        last_more = got_one[:, n_in:].astype(F32) + got_two.astype(F32) + got_three.astype(F32)
    else:
        in_more, last_more, flat_got = go(
            (), (far[1], in_rest), (far[0], last[last.shape[0] // 2 :]), (cross, flat)
        )
        last = add(last[: last.shape[0] // 2], last_more)
        last_rest, last_stay = rest_start(last)
        last_more = far[1](last_rest)

    flat = flat + flat_got
    pool_other, *flat_got = go(
        (in_more, last_more), (over, grad_pool), *((how, flat) for how in rest_hop), join=False
    )
    flat = flat + sum(flat_got)
    for send in far[:-2]:
        flat = flat + send(flat)
    grad_last = finish(last_stay.astype(F32) + last_more.astype(F32))
    grad_in = finish(in_stay.astype(F32) + in_more.astype(F32))
    grad_out = grad_last[:, :inner_half]
    grad_qkv = grad_last[:, inner_half:]
    grad_tokens = jnp.where(
        mine == 0, jnp.stack([grad_own, grad_other]), jnp.stack([grad_other, grad_own])
    )
    across = width // LANES
    gains_mine = lax.dynamic_slice_in_dim(flat[: 3 * across].reshape(3, width), me * block, block, axis=1)
    loss = flat[3 * across, 0] / (micro_count * sent_local * size)
    table_sum = flat[small_rows - bucket_count :, : 2 * heads_half]
    table_mine = lax.dynamic_slice_in_dim(table_sum, mine * heads_half, heads_half, axis=1)
    grad_pool = jnp.where(mine == 0, columns(grad_pool, pool_other), columns(pool_other, grad_pool))
    return (
        loss,
        grad_tokens,
        grad_qkv[:, :inner_half],
        grad_qkv[:, inner_half : 2 * inner_half],
        grad_qkv[:, 2 * inner_half :],
        grad_out.T,
        grad_in,
        grad_back.T,
        gains_mine[0],
        gains_mine[1],
        gains_mine[2],
        grad_pool,
        table_mine,
    )


def solution(mesh):
    placed = (
        P(None, "dp", None),
        P(None, "dp", None),
        P(),
        P(None, "dp"),
        P("dp", "mp"),
        P("dp", "mp"),
        P("dp", "mp"),
        P("mp", "dp"),
        P("dp", "mp"),
        P("mp", "dp"),
        P("dp"),
        P("dp"),
        P("dp"),
        P("dp", None),
        P(None, "mp"),
    )
    return jax.shard_map(
        shards,
        mesh=mesh,
        in_specs=placed,
        out_specs=(
            P(),
            P(None, "dp", None),
            P("dp", "mp"),
            P("dp", "mp"),
            P("dp", "mp"),
            P("mp", "dp"),
            P("dp", "mp"),
            P("mp", "dp"),
            P("dp"),
            P("dp"),
            P("dp"),
            P("dp", None),
            P(None, "mp"),
        ),
        check_vma=False,
    )
```

```python
import functools

import jax
import jax.numpy as jnp
from jax import lax
from jax.experimental import pallas as pl
from jax.experimental.pallas import tpu as pltpu
from jax.sharding import PartitionSpec as P

NEG_FILL = -1000000000.0
SCORE_SCALE = 0.125
SOFTMAX_TEMP = 50.0
LOSS_SCALE = 64.0
EPSILON = 1e-06
REACH = 32
QB = 64
WIN = QB + 2 * REACH
LANES = 128
GELU_A = 0.7978845608028654
GELU_B = 0.044715

BF16 = jnp.bfloat16
F32 = jnp.float32
HIGHEST = lax.Precision.HIGHEST


def dot(left, right, dims=((1,), (0,)), precision=None):
    return lax.dot_general(
        left, right, (dims, ((), ())), precision=precision, preferred_element_type=F32
    )


def dot_nt(left, right):
    return dot(left, right, ((1,), (1,)))


def dot_tn(left, right):
    return dot(left, right, ((0,), (0,)))


def rms_forward(value, gain):
    inverse = lax.rsqrt(jnp.mean(value * value, axis=-1, keepdims=True) + EPSILON)
    return (value * inverse * gain, inverse)


def cost(flops, bytes_accessed):
    return pl.CostEstimate(flops=0, bytes_accessed=0, transcendentals=0)


def params(mib=16):
    return pltpu.CompilerParams(vmem_limit_bytes=mib * 2**20)


def split_dot(left, right, dims=((1,), (0,))):
    high = right.astype(BF16)
    rest = (right - high.astype(F32)).astype(BF16)
    return dot(left, high, dims) + dot(left, rest, dims)


def stream_kernel(plan, operands, outs, body, *refs):
    sources, out_refs = refs[:operands], refs[operands : operands + outs]
    more = refs[operands + outs :]
    buffers, sem = more[: sum(len(load) > 1 for load in plan)], more[-1]
    more = more[len(buffers) : -1]
    copies, places, used = [], [], 0
    for load in plan:
        if len(load) == 1:
            which, _, _, col, width, _ = load[0]
            places.append(sources[which].at[:, pl.ds(col, width)])
            copies.append([])
            continue
        buffer = buffers[used]
        used += 1
        group = []
        for which, at, count, col, width, number in load:
            copy = pltpu.make_async_copy(
                sources[which].at[:, pl.ds(col, width)], buffer.at[pl.ds(at, count)], sem.at[number]
            )
            copy.start()
            group.append(copy)
        places.append(buffer)
        copies.append(group)
    ready = set()

    def get(i):
        if i not in ready:
            ready.add(i)
            for copy in copies[i]:
                copy.wait()
        return places[i]

    body(get, *out_refs, *more)


def stream(name, loads, out_shapes, body, scratch=(), mib=16):
    arrays, spaces = [], []

    def place(array, space):
        for i, known in enumerate(arrays):
            if known is array and spaces[i] is space:
                return i
        arrays.append(array)
        spaces.append(space)
        return len(arrays) - 1

    plan, buffers, number = [], [], 0
    for load in loads:
        steps, at = [], 0
        space = pltpu.VMEM if len(load) == 1 else pltpu.HBM
        for array, col, width in load:
            steps.append((place(array, space), at, array.shape[0], col, width, number))
            at += array.shape[0]
            number += 1
        plan.append(steps)
        if len(load) > 1:
            buffers.append(pltpu.VMEM((at, load[0][2]), load[0][0].dtype))
    return pl.pallas_call(
        functools.partial(stream_kernel, plan, len(arrays), len(out_shapes), body),
        out_shape=tuple(out_shapes),
        in_specs=[pl.BlockSpec(memory_space=space) for space in spaces],
        out_specs=tuple(pl.BlockSpec(memory_space=pltpu.VMEM) for _ in out_shapes),
        scratch_shapes=buffers + list(scratch) + [pltpu.SemaphoreType.DMA((number,))],
        compiler_params=params(mib),
        cost_estimate=cost(0, 0),
        name=name,
    )(*arrays)


def part(array, col=0, width=None):
    return [(array, col, array.shape[1] - col if width is None else width)]


def weight(pieces, col, width):
    return [(piece, col, width) for piece in pieces]


def wide(name, x, blocks, extras=(), body=None, outs=1):
    widths = [width for *_, width in blocks]
    loads = [part(x)]
    for i, block in enumerate(blocks):
        loads.append(weight(*block))
        for extra in extras:
            loads.append(part(extra, sum(widths[:i]), widths[i]))

    def run(get, *out_refs):
        at = 0
        per = 1 + len(extras)
        for i, width in enumerate(widths):
            first = 1 + i * per
            value = dot(get(0)[...], get(first)[...])
            got = [get(first + 1 + j)[...] for j in range(len(extras))]
            values = (value,) if body is None else body(value, *got)
            for ref, result in zip(out_refs, values):
                ref[:, at : at + width] = result.astype(BF16)
            at += width

    shape = shape_of(BF16, x.shape[0], sum(widths))
    result = stream(name, loads, (shape,) * outs, run)
    return result if outs > 1 else result[0]


def gelu_both(up):
    square = up * up
    bend = jnp.tanh(GELU_A * up * (1.0 + GELU_B * square))
    half_one = 0.5 + 0.5 * bend
    inner = GELU_A + (3.0 * GELU_A * GELU_B) * square
    return up * half_one, half_one + 0.5 * up * (1.0 - bend * bend) * inner


def times_slope(value, slope):
    return (value * slope.astype(F32),)


def narrow(name, work, extras, out_shapes, body, scratch=(), mib=16):
    loads = []
    for x, x_col, pieces, col, width in work:
        loads += [part(x, x_col, width), weight(pieces, col, width)]
    first = len(loads)
    loads += [extra if isinstance(extra, list) else part(extra) for extra in extras]

    def run(get, *refs):
        out_refs, more = refs[: len(out_shapes)], refs[len(out_shapes) :]
        acc = more[0]
        for j in range(len(work)):
            value = dot_nt(get(2 * j)[...], get(2 * j + 1)[...])
            acc[...] = value if j == 0 else acc[...] + value
        body(acc, *(get(first + i) for i in range(len(extras))), *out_refs, *more[1:])

    depth = sum(piece.shape[0] for piece in work[0][2])
    return stream(
        name, loads, out_shapes, run, [pltpu.VMEM((work[0][0].shape[0], depth), F32), *scratch], mib
    )


def gradients(name, left, first, count, rights, out_of=None):
    loads = [part(left, first, count)] + [part(right) for right in rights]

    def run(get, *refs):
        *out_refs, turned = refs
        turned[...] = get(0)[...].T
        for i, ref in enumerate(out_refs):
            ref[...] = dot(turned[...], get(1 + i)[...]).astype(BF16)

    shapes = [shape_of(BF16, count, right.shape[1]) for right in rights]
    return stream(name, loads, shapes, run, [pltpu.VMEM((count, left.shape[0]), BF16)])


def sent_columns(name, first, pairs):
    loads = [load for left, right in pairs for load in (part(left, first, first), part(right))]

    def run(get, out_ref, turned):
        at = 0
        for i, (_, right) in enumerate(pairs):
            turned[...] = get(2 * i)[...].T
            n = right.shape[1]
            out_ref[:, at : at + n] = dot(turned[...], get(2 * i + 1)[...]).astype(BF16)
            at += n

    shape = shape_of(BF16, first, sum(right.shape[1] for _, right in pairs))
    return stream(name, loads, (shape,), run, [pltpu.VMEM((first, pairs[0][0].shape[0]), BF16)])[0]


def stack_rows(pieces, widths):
    block = pieces[0].shape[0]
    cuts = [sum(widths[:i]) for i in range(len(widths))]
    if block % 16:
        whole = jnp.concatenate(pieces, axis=0)
        return [whole[:, at : at + width] for at, width in zip(cuts, widths)]

    def run(*refs):
        for i, ref in enumerate(refs[: len(pieces)]):
            for j, out in enumerate(refs[len(pieces) :]):
                out[i * block : (i + 1) * block] = ref[:, cuts[j] : cuts[j] + widths[j]]

    shapes = [shape_of(pieces[0].dtype, block * len(pieces), width) for width in widths]
    return whole_call(run, pieces, shapes, (), "stack_rows")


def qkv_call(inputs, first, n):
    blocks = [(side, i * n, n) for i in range(3) for side in first]
    loads = [part(inputs), weight(first[0], 3 * n, LANES)] + [weight(*block) for block in blocks]

    def run(get, qkv_ref, normed_ref, inverse_ref, gains_ref):
        value = get(0)[...]
        inverse = lax.rsqrt(jnp.mean(value * value, axis=1, keepdims=True) + EPSILON)
        inverse_ref[...] = inverse
        gains = get(1)[...].astype(F32).T[:8]
        gains_ref[...] = gains
        normed_ref[...] = (value * inverse * gains[0:1]).astype(BF16)
        for i in range(len(blocks)):
            qkv_ref[:, i * n : (i + 1) * n] = dot(normed_ref[...], get(2 + i)[...]).astype(BF16)

    seq, width = inputs.shape
    shapes = (
        shape_of(BF16, seq, 6 * n),
        shape_of(BF16, seq, width),
        shape_of(F32, seq, 1),
        shape_of(F32, 8, width),
    )
    return stream("qkv", loads, shapes, run)


def norm_body(row, acc, value_ref, gains_ref, hidden_ref, inverse_ref, normed_ref=None):
    hidden = value_ref[...] + acc[...]
    inverse = lax.rsqrt(jnp.mean(hidden * hidden, axis=1, keepdims=True) + EPSILON)
    hidden_ref[...] = hidden
    inverse_ref[...] = inverse
    if normed_ref is not None:
        normed_ref[...] = (hidden * inverse * gains_ref[row : row + 1, :]).astype(BF16)


def norm_back(value, inverse, gain, grad):
    scaled = grad * gain
    inner = jnp.mean(value * scaled, axis=1, keepdims=True)
    d_value = inverse * scaled - value * (inverse * inverse * inverse) * inner
    return d_value, jnp.sum(grad * value * inverse, axis=0, keepdims=True)


def back_body(row, acc, value_ref, inverse_ref, gains_ref, grad_ref, low_ref, gain_out, hidden_ref=None):
    d_value, d_gain = norm_back(
        value_ref[...], inverse_ref[...], gains_ref[row : row + 1, :], acc[...]
    )
    total = grad_ref[...] + d_value
    low_ref[...] = total.astype(BF16)
    gain_out[...] = d_gain
    if hidden_ref is not None:
        hidden_ref[...] = total


def turn_kernel(grad_ref, order_ref, out_ref):
    out_ref[...] = dot_nt(grad_ref[...], order_ref[...]).astype(BF16)


def small_kernel(heads_half, one_ref, two_ref, three_ref, order_ref, bias_ref, onehot_ref, loss_ref, mine_ref, out_ref):
    width = one_ref.shape[1]
    gains = jnp.concatenate([one_ref[...], two_ref[...], three_ref[...], jnp.zeros((5, width), F32)], axis=0)
    high = gains.astype(BF16)
    rest = (gains - high.astype(F32)).astype(BF16)
    gains = dot_nt(high, order_ref[...]) + dot_nt(rest, order_ref[...])
    out_ref[...] = jnp.zeros_like(out_ref)
    across = width // LANES
    for i in range(3):
        for j in range(across):
            at = i * across + j
            out_ref[at : at + 1, :] = gains[i : i + 1, j * LANES : (j + 1) * LANES]
    at = 3 * across
    lane = lax.broadcasted_iota(jnp.int32, (1, LANES), 1)
    out_ref[at : at + 1, :] = jnp.where(lane == 0, loss_ref[...], 0.0)
    bias = bias_ref[...]
    row = lax.broadcasted_iota(jnp.int32, (LANES, bias.shape[0]), 0)
    column = lax.broadcasted_iota(jnp.int32, (LANES, bias.shape[0]), 1)
    pick = jnp.where((column == 8 * (row // 2) + row % 2) & (row < 2 * heads_half), 1.0, 0.0)
    bias = split_dot(pick.astype(BF16), bias)
    high = bias.astype(BF16)
    rest = (bias - high.astype(F32)).astype(BF16)
    buckets = onehot_ref[...]
    table = dot_nt(buckets, high) + dot_nt(buckets, rest)
    lane = lax.broadcasted_iota(jnp.int32, table.shape, 1)
    swapped = jnp.where(
        lane < heads_half, pltpu.roll(table, LANES - heads_half, 1), pltpu.roll(table, heads_half, 1)
    )
    top = -(-(at + 1) // 8) * 8
    out_ref[top : top + table.shape[0], :] = jnp.where(mine_ref[...] == 0, table, swapped)


def member_of(seg_ref, sent_count):
    ids = lax.broadcasted_iota(jnp.int32, (sent_count, seg_ref.shape[1]), 0)
    hit = jnp.where(seg_ref[...] == ids, 1.0, 0.0)
    return hit.astype(BF16), jnp.sum(hit, axis=1, keepdims=True)


def tail_body(acc, value_ref, gains_ref, seg_ref, own_ref, other_ref, hidden_ref, inverse_ref, pooled_ref, unit_ref, low_ref, scale_ref, high, rest):
    hidden = value_ref[...] + acc[...]
    inverse = lax.rsqrt(jnp.mean(hidden * hidden, axis=1, keepdims=True) + EPSILON)
    hidden_ref[...] = hidden
    inverse_ref[...] = inverse
    final = hidden_ref[...] * inverse * gains_ref[2:3, :]
    high[...] = final.astype(BF16)
    rest[...] = (final - high[...].astype(F32)).astype(BF16)
    sents, count = member_of(seg_ref, pooled_ref.shape[0])
    pooled = ((dot(sents, high[...]) + dot(sents, rest[...])) / count).astype(BF16)
    pooled_ref[...] = pooled
    half = own_ref.shape[1]
    left = dot(pooled, own_ref[...])
    right = dot(pooled, other_ref[...])
    square = jnp.sum(left * left, axis=1, keepdims=True) + jnp.sum(right * right, axis=1, keepdims=True)
    scale = lax.rsqrt(square + EPSILON)
    scale_ref[...] = scale
    for at, value in ((0, left * scale), (half, right * scale)):
        unit_ref[:, at : at + half] = value
        low_ref[:, at : at + half] = value.astype(BF16)


def head_call(quarters, unit, scale, partner, column, sentence_loads, out_shapes):
    loads = [part(q) for q in (*quarters, unit, scale, partner, column)] + sentence_loads
    quarter = quarters[0].shape[0]
    total = 4 * quarter

    def run(get, loss_ref, embed_ref, *refs):
        *back_refs, every = refs
        for i in range(4):
            every[i * quarter : (i + 1) * quarter] = get(i)[...]
        unit, scale, partner, columns_id = (get(i)[...] for i in range(4, 8))
        partner = as_columns(
            jnp.concatenate([partner, jnp.zeros((1, LANES - partner.shape[1]), jnp.int32)], axis=1)
        )[: partner.shape[1], 0:1]
        own_count = unit.shape[0]
        sims = dot_nt(every[...], every[...]) * SOFTMAX_TEMP
        row = lax.broadcasted_iota(jnp.int32, (total, total), 0)
        column = lax.broadcasted_iota(jnp.int32, (total, total), 1)
        sims = jnp.where(row == column, NEG_FILL, sims)
        top = jnp.max(sims, axis=0, keepdims=True)
        lse_row = top + jnp.log(jnp.sum(jnp.exp(sims - top), axis=0, keepdims=True))
        own = sims[:own_count]
        own_top = jnp.max(own, axis=1, keepdims=True)
        own_lse = own_top + jnp.log(jnp.sum(jnp.exp(own - own_top), axis=1, keepdims=True))
        is_target = columns_id.astype(F32) == partner
        hit = jnp.where(is_target, 1.0, 0.0)
        target = jnp.sum(jnp.where(is_target, own, 0.0), axis=1, keepdims=True)
        loss_ref[...] = jnp.sum(own_lse - target, axis=0, keepdims=True)
        d_rows = (LOSS_SCALE * (jnp.exp(own - own_lse) - hit)).astype(BF16)
        d_cols = (LOSS_SCALE * (jnp.exp(own - lse_row) - hit)).astype(BF16)
        d_unit = SOFTMAX_TEMP * (dot(d_rows, every[...]) + dot(d_cols, every[...]))
        inner = jnp.sum(d_unit * unit, axis=1, keepdims=True)
        d_embed = (scale * (d_unit - unit * inner)).astype(BF16)
        embed_ref[...] = d_embed
        sentence_back(d_embed, [get(8 + i) for i in range(len(sentence_loads))], *back_refs)

    return stream("head", loads, out_shapes, run, [pltpu.VMEM((total, unit.shape[1]), BF16)])


def sentence_call(embed, sentence_loads, out_shapes):
    def run(get, *back_refs):
        sentence_back(get(0)[...], [get(1 + i) for i in range(len(sentence_loads))], *back_refs)

    return stream("sentence", [part(embed)] + sentence_loads, out_shapes, run)


def sentence_back(d_embed, sources, hidden_ref, low_ref, gain_out):
    seg_ref, own_ref, other_ref, value_ref, inverse_ref, gains_ref = sources
    half = own_ref.shape[1]
    d_pooled = dot_nt(d_embed[:, :half], own_ref[...]) + dot_nt(d_embed[:, half:], other_ref[...])
    sents, count = member_of(seg_ref, d_embed.shape[0])
    d_final = split_dot(sents, d_pooled / count, ((0,), (0,)))
    d_value, d_gain = norm_back(value_ref[...], inverse_ref[...], gains_ref[2:3, :], d_final)
    hidden_ref[...] = d_value
    low_ref[...] = d_value.astype(BF16)
    gain_out[...] = d_gain


def whole_call(body, args, out_shapes, scratch=(), name=None):
    return pl.pallas_call(
        body,
        out_shape=tuple(out_shapes),
        in_specs=[pl.BlockSpec(memory_space=pltpu.VMEM)] * len(args),
        out_specs=tuple(pl.BlockSpec(memory_space=pltpu.VMEM) for _ in out_shapes),
        scratch_shapes=scratch,
        compiler_params=params(),
        cost_estimate=cost(0, 0),
        name=name,
    )(*args)


def shape_of(kind, *dims):
    return jax.ShapeDtypeStruct(dims, kind)


def _stack_heads(part):
    lane = lax.broadcasted_iota(jnp.int32, part.shape, 1)
    zero = jnp.zeros_like(part)
    first = lane < LANES // 2
    return jnp.concatenate(
        [jnp.where(first, part, zero), jnp.where(first, zero, part)], axis=0
    )


def _unstack_heads(both):
    half = both.shape[0] // 2
    lane = lax.broadcasted_iota(jnp.int32, (half, LANES), 1)
    return jnp.where(lane < LANES // 2, both[:half], both[half:])


def _pad_keys(pad, ref):
    seq = ref.shape[0]
    pad[0:REACH] = jnp.zeros((REACH, LANES), pad.dtype)
    pad[REACH + seq :] = jnp.zeros((REACH, LANES), pad.dtype)
    pad[REACH : REACH + seq] = ref[...]


def _query_bits(shape):
    return lax.broadcasted_iota(jnp.int32, shape, 0) & (QB - 1)


def as_columns(values):
    count, length = values.shape
    side = max(LANES, length)
    square = jnp.concatenate([values.astype(F32), jnp.zeros((side - count, length), F32)], axis=0)
    return square.T


def attend_forward_kernel(
    q_ref, k_ref, v_ref, segq_ref, segk_ref, rel_ref, ctx_ref, probs_ref, kpad, vpad, mask, scores
):
    seq = q_ref.shape[0]
    blocks = seq // QB
    _pad_keys(kpad, k_ref)
    _pad_keys(vpad, v_ref)

    @pl.when(pl.program_id(0) == 0)
    def _():
        keys = as_columns(segk_ref[...])
        for b in range(blocks):
            same = keys[:, b : b + 1] == segq_ref[b : b + 1, :].astype(F32)
            mask[b] = jnp.where(same, 0.0, NEG_FILL)

    rel = rel_ref[0]
    row = lax.broadcasted_iota(jnp.int32, (2 * QB, WIN), 0)
    bias = jnp.where(row < QB, rel[0:1, :], rel[1:2, :])
    bits = _query_bits((2 * QB, WIN))
    step = 1
    while step < QB:
        bias = jnp.where((bits & step) != 0, pltpu.roll(bias, step, 1), bias)
        step *= 2
    bias = bias.T
    for b in range(blocks):
        query = _stack_heads(q_ref[b * QB : (b + 1) * QB] * jnp.asarray(SCORE_SCALE, BF16))
        scores[b] = dot_nt(kpad[b * QB : b * QB + WIN], query)
    values = scores[...] + bias[None] + mask[...]
    top = jnp.max(values, axis=1, keepdims=True)
    shifted = jnp.exp(values - top)
    total = jnp.sum(shifted, axis=1, keepdims=True)
    probs_ref[0] = (shifted * (1.0 / total)).astype(BF16)
    for b in range(blocks):
        part = dot_tn(probs_ref[0, b], vpad[b * QB : b * QB + WIN])
        ctx_ref[b * QB : (b + 1) * QB] = _unstack_heads(part).astype(BF16)


def attend_backward_kernel(
    q_ref, k_ref, v_ref, dctx_ref, probs_ref, dqkv_ref, dbias_ref,
    kpad, vpad, dk_acc, dv_acc, d_probs, d_low,
):
    seq = q_ref.shape[0]
    pair = pl.program_id(0)
    side = pl.num_programs(0) // 2
    later = pair // side
    q_at = pl.ds(pl.multiple_of(pair * LANES, LANES), LANES)
    k_at = pl.ds(pl.multiple_of((pair + 2 * side + later * side) * LANES, LANES), LANES)
    v_at = pl.ds(pl.multiple_of((pair + 3 * side + later * side) * LANES, LANES), LANES)
    blocks = seq // QB
    _pad_keys(kpad, k_ref)
    _pad_keys(vpad, v_ref)
    dk_acc[...] = jnp.zeros_like(dk_acc)
    dv_acc[...] = jnp.zeros_like(dv_acc)
    for b in range(blocks):
        window = slice(b * QB, b * QB + WIN)
        d_ctx = _stack_heads(dctx_ref[b * QB : (b + 1) * QB])
        d_probs[b] = dot_nt(vpad[window], d_ctx)
        dv_acc[window] += dot(probs_ref[0, b], d_ctx)
    probs = probs_ref[0].astype(F32)
    product = probs * d_probs[...]
    inner = jnp.sum(product, axis=1, keepdims=True)
    d_scores = product - probs * inner
    d_low[...] = d_scores.astype(BF16)
    total = jnp.sum(d_scores, axis=0).T
    for b in range(blocks):
        here = slice(b * QB, (b + 1) * QB)
        window = slice(b * QB, b * QB + WIN)
        query = _stack_heads(q_ref[here] * jnp.asarray(SCORE_SCALE, BF16))
        dk_acc[window] += dot(d_low[b], query)
        d_query = _unstack_heads(dot_tn(d_low[b], kpad[window])) * SCORE_SCALE
        dqkv_ref[here, q_at] = d_query.astype(BF16)
    dqkv_ref[:, k_at] = dk_acc[REACH : REACH + seq].astype(BF16)
    dqkv_ref[:, v_at] = dv_acc[REACH : REACH + seq].astype(BF16)
    bits = _query_bits((2 * QB, WIN))
    step = 1
    while step < QB:
        total = jnp.where((bits & step) != 0, pltpu.roll(total, WIN - step, 1), total)
        step *= 2
    first = jnp.sum(total[:QB], axis=0, keepdims=True)
    second = jnp.sum(total[QB:], axis=0, keepdims=True)
    dbias_ref[0] = jnp.concatenate([first, second, jnp.zeros((6, WIN), F32)], axis=0)


def _qkv_specs(seq, pairs):
    def spec(kind):
        return pl.BlockSpec((seq, LANES), lambda p: (0, kind * pairs + p))

    return [spec(0), spec(1), spec(2)]


def attend_forward(qkv, twice, windows, rel_window):
    seq = qkv.shape[0]
    pairs = rel_window.shape[0]
    blocks = seq // QB
    return pl.pallas_call(
        attend_forward_kernel,
        grid=(pairs,),
        out_shape=(
            jax.ShapeDtypeStruct((seq, pairs * LANES), BF16),
            jax.ShapeDtypeStruct((pairs, blocks, WIN, 2 * QB), BF16),
        ),
        in_specs=_qkv_specs(seq, pairs)
        + [
            pl.BlockSpec((blocks, 2 * QB), lambda p: (0, 0)),
            pl.BlockSpec((blocks, WIN), lambda p: (0, 0)),
            pl.BlockSpec((1, 2, WIN), lambda p: (p, 0, 0)),
        ],
        out_specs=(
            pl.BlockSpec((seq, LANES), lambda p: (0, p)),
            pl.BlockSpec((1, blocks, WIN, 2 * QB), lambda p: (p, 0, 0, 0)),
        ),
        scratch_shapes=[pltpu.VMEM((seq + 2 * REACH, LANES), BF16)] * 2
        + [pltpu.VMEM((blocks, WIN, 2 * QB), F32)] * 2,
        compiler_params=params(),
        cost_estimate=cost(8 * seq * WIN * LANES * pairs * 4, 8 * seq * LANES * pairs),
        name="attend_forward",
    )(qkv, qkv, qkv, twice, windows, rel_window)


def attend_backward(qkv, d_context, probs):
    seq = qkv.shape[0]
    pairs = probs.shape[0]
    blocks = seq // QB
    lane_block = pl.BlockSpec((seq, LANES), lambda p: (0, p))
    return pl.pallas_call(
        attend_backward_kernel,
        grid=(pairs,),
        out_shape=(
            jax.ShapeDtypeStruct((seq, 3 * pairs * LANES), BF16),
            jax.ShapeDtypeStruct((pairs, 8, WIN), F32),
        ),
        in_specs=_qkv_specs(seq, pairs)
        + [
            lane_block,
            pl.BlockSpec((1, blocks, WIN, 2 * QB), lambda p: (p, 0, 0, 0)),
        ],
        out_specs=(
            pl.BlockSpec((seq, 3 * pairs * LANES), lambda p: (0, 0)),
            pl.BlockSpec((1, 8, WIN), lambda p: (p, 0, 0)),
        ),
        scratch_shapes=[pltpu.VMEM((seq + 2 * REACH, LANES), BF16)] * 2
        + [pltpu.VMEM((seq + 2 * REACH, LANES), F32)] * 2
        + [pltpu.VMEM((blocks, WIN, 2 * QB), F32), pltpu.VMEM((blocks, WIN, 2 * QB), BF16)],
        compiler_params=params(),
        cost_estimate=cost(16 * seq * WIN * LANES * pairs * 4, 16 * seq * LANES * pairs),
        name="attend_backward",
    )(qkv, qkv, qkv, d_context, probs)


CORE = 1
CROSS = 2


def hop(value, mask):
    size = lax.axis_size("dp")
    return lax.ppermute(value, "dp", [(i, i ^ mask) for i in range(size)])


def over(value):
    return lax.ppermute(value, "mp", [(0, 1), (1, 0)])


def cross(value):
    return hop(value, CROSS)


def core(value):
    return hop(value, CORE)


def go(waits, *sends, keep=(), join=True):
    values = [value for _, value in sends]
    held = lax.optimization_barrier((*values, *keep, *waits))
    results = [how(value) for (how, _), value in zip(sends, held)]
    if join:
        results = list(lax.optimization_barrier(tuple(results)))
    return results + list(held[len(values) : len(values) + len(keep)])


def slot_masks(size):
    rest = size // 4
    return [z * 4 + x * 2 + c for c in range(2) for x in range(2) for z in range(rest)]


def strides(size):
    found = []
    stride = 4
    while stride < size:
        found.append(stride)
        stride *= 2
    return found


def gather_near(shard, waits, widths=None):
    size = lax.axis_size("dp")
    pieces = [shard]
    stride = 4
    while stride < size:
        radix = min(4, size // stride)
        shard = jnp.concatenate(pieces, axis=0) if len(pieces) > 1 else shard
        sends = [(functools.partial(hop, mask=j * stride), shard) for j in range(1, radix)]
        pieces = [shard] + go(waits, *sends)
        stride *= radix
    return jnp.concatenate(pieces, axis=0) if widths is None else stack_rows(pieces, widths)


def rows(*pieces):
    return jnp.concatenate(pieces, axis=0)


def columns(*pieces):
    return jnp.concatenate(pieces, axis=1)


def gather_weights(start, later, n_one, n_three, early, begin, between):
    steps = strides(lax.axis_size("dp"))
    one, two = gather_near(start, (), (n_one, start.shape[1] - n_one))
    one_x, two_y, *more, one_c, two_c = go(
        early,
        (cross, one),
        (over, two),
        *((functools.partial(hop, mask=stride), later) for stride in steps[:1]),
        (core, one),
        (core, two),
    )
    later = rows(later, *more)
    for stride in steps[1:-1]:
        later = rows(later, hop(later, stride))
    one_y, one_xy, two_x, two_yx, *more = go(
        (one_x, two_y, one_c, two_c),
        (over, one),
        (over, one_x),
        (cross, two),
        (cross, two_y),
        *((functools.partial(hop, mask=stride), later) for stride in steps[1:][-1:]),
    )
    if more and later.shape[0] % 16 == 0:
        three, four = stack_rows((later, *more), (n_three, later.shape[1] - n_three))
    else:
        later = rows(later, *more)
        three, four = later[:, :n_three], later[:, n_three:]
    three_x, four_y, one_xc, one_yc, one_xyc, two_y, two_x, two_yx = go(
        (),
        (cross, three),
        (over, four),
        (core, one_x),
        (core, one_y),
        (core, one_xy),
        keep=(two_y, two_x, two_yx),
    )
    first = ((one, one_x, one_c, one_xc), (one_y, one_xy, one_yc, one_xyc))
    four_x, three_y, two_yc, two_xc, two_yxc, *kept = go(
        (three_x, four_y),
        (cross, four),
        (over, three),
        (core, two_y),
        (core, two_x),
        (core, two_yx),
        keep=(*first[0], *first[1], *early),
    )
    first = (tuple(kept[:4]), tuple(kept[4:8]))
    early = kept[8:]
    started = begin(first, early)
    second = ((two, two_x, two_c, two_xc), (two_y, two_yx, two_yc, two_yxc))
    four_yx, three_xy, four_c, four_yc, three_c, *kept = go(
        (four_x, three_y, two_yc, two_xc, two_yxc),
        (cross, four_y),
        (over, three_x),
        (core, four),
        (core, four_y),
        (core, three),
        keep=(*second[0], *second[1], *started),
    )
    second = (tuple(kept[:4]), tuple(kept[4:8]))
    done = between(kept[8:], second, early)
    four_xc, four_yxc, three_xc, three_yc, three_xyc, *done = go(
        (four_yx, three_xy, four_c, four_yc, three_c),
        (core, four_x),
        (core, four_yx),
        (core, three_x),
        (core, three_y),
        (core, three_xy),
        keep=done,
        join=False,
    )
    third = ((three, three_x, three_c, three_xc), (three_y, three_xy, three_yc, three_xyc))
    fourth = ((four, four_x, four_c, four_xc), (four_y, four_yx, four_yc, four_yxc))
    return first, second, third, fourth, early, done


def pack_start(w_query, w_key, w_value, gains, w_in, w_out):
    block, n = w_query.shape
    wide_in = w_in.shape[1]

    def run(q_ref, k_ref, v_ref, g_ref, in_ref, out_ref_t, ref):
        ref[:, :n] = q_ref[...]
        ref[:, n : 2 * n] = k_ref[...]
        ref[:, 2 * n : 3 * n] = v_ref[...]
        ref[:, 3 * n : 3 * n + LANES] = g_ref[...]
        at = 3 * n + LANES
        ref[:, at : at + wide_in] = in_ref[...]
        ref[:, at + wide_in :] = out_ref_t[...]

    shape = shape_of(BF16, block, 3 * n + LANES + wide_in + w_out.shape[1])
    return whole_call(run, (w_query, w_key, w_value, gains, w_in, w_out), (shape,), (), "pack_start")[0]


def gather_dp(shard):
    near = gather_near(shard, ())
    side, c_near = go((near,), (cross, near), (core, near))
    return near, side, c_near, core(side)


def low(value):
    return value.astype(BF16)


def add(left, right):
    return (left.astype(F32) + right.astype(F32)).astype(BF16)


def product(left, begin, end, right, got=None):
    value = dot_tn(left[:, begin:end], right)
    if got is not None:
        value = value + got.astype(F32)
    return low(value)


def rest_start(value):
    half = value.shape[0] // 2
    return value[half:], value[:half]


def sum_half(value, send):
    gone, stays = rest_start(value)
    return stays + send(low(gone)).astype(F32)


def rest_hops(size):
    return [functools.partial(hop, mask=stride) for stride in reversed(strides(size))]


def shards(
    tokens,
    seg_ids,
    buckets,
    labels,
    w_query,
    w_key,
    w_value,
    w_out,
    w_in,
    w_back,
    gain_attn,
    gain_ffn,
    gain_final,
    w_pool,
    rel_table,
):
    micro_count, seq, width = tokens.shape
    size = lax.axis_size("dp")
    me = lax.axis_index("dp")
    mine = lax.axis_index("mp")
    block = width // size
    inner_half = w_query.shape[1]
    hidden_half = w_in.shape[1]
    sent_local = labels.shape[1]
    bucket_count = rel_table.shape[0]
    heads_half = rel_table.shape[1]
    masks = slot_masks(size)

    x_own = lax.dynamic_index_in_dim(tokens, mine, 0, keepdims=False)
    segments = lax.dynamic_index_in_dim(seg_ids, mine, 0, keepdims=False)[0]
    partner = lax.dynamic_index_in_dim(labels, mine, 0, keepdims=False)

    slot_block = jnp.stack([jnp.bitwise_xor(me, m) for m in masks]).astype(jnp.int32)
    source = (slot_block[:, None] * block + jnp.arange(block, dtype=jnp.int32)[None, :]).reshape(-1)
    order = (jnp.arange(width, dtype=jnp.int32)[:, None] == source[None, :]).astype(BF16)
    order = lax.optimization_barrier(order)
    inputs = dot(x_own, order)

    rel_all = jnp.concatenate([rel_table, over(rel_table)], axis=1).astype(F32)
    near_buckets = lax.slice_in_dim(buckets, seq - 1 - REACH, seq - 1 - REACH + WIN)
    onehot = (near_buckets[None, :] == jnp.arange(bucket_count, dtype=jnp.int32)[:, None]).astype(F32)
    onehot = lax.optimization_barrier(low(onehot))
    rel_window = dot(rel_all, onehot.astype(F32), ((0,), (0,)), HIGHEST).reshape(heads_half, 2, WIN)

    row_f32 = shape_of(F32, seq, width)
    row_low = shape_of(BF16, seq, width)
    column_f32 = shape_of(F32, seq, 1)
    gain_f32 = shape_of(F32, 1, width)
    heads = 3 * inner_half
    piece = hidden_half // 2
    halves = [(side, i * inner_half, inner_half) for side in range(2) for i in range(2)]

    def hidden_blocks(weights, first_col=0):
        return [(weights[side], first_col + col, n) for side, col, n in halves]

    def begin(first, early):
        inputs, rel_window, twice, windows, *_ = early
        qkv, normed1_low, inverse1, gains = qkv_call(inputs, first, inner_half)
        context, probs = attend_forward(qkv, twice, windows, rel_window)
        return qkv, normed1_low, inverse1, gains, context, probs

    def between(started, second, early):
        qkv, normed1_low, inverse1, gains, context, probs = started
        inputs = early[0]
        hidden1, inverse2, normed2_low = narrow(
            "attn_out",
            [(context, i * inner_half, second[i], piece, inner_half) for i in range(2)],
            (inputs, gains),
            (row_f32, column_f32, row_low),
            functools.partial(norm_body, 1),
        )
        act0, slope0 = wide("act0", normed2_low, hidden_blocks(second), (), gelu_both, 2)
        return normed1_low, inverse1, gains, qkv, context, probs, hidden1, inverse2, normed2_low, act0, slope0

    gains_col = jnp.pad(
        jnp.stack([gain_attn, gain_ffn, gain_final], axis=1), ((0, 0), (0, LANES - 3))
    )
    pool_half = w_pool.shape[1] // 2
    pool_own = lax.dynamic_slice_in_dim(w_pool, mine * pool_half, pool_half, axis=1)
    back_shard = w_back.T
    padded = jnp.pad(segments, (REACH, REACH), constant_values=-1)
    windows = jnp.stack([padded[at : at + WIN] for at in range(0, seq, QB)])
    twice = jnp.tile(segments.reshape(seq // QB, QB), (1, 2))
    local_ids = jnp.arange(sent_local, dtype=jnp.int32)
    column_id = (slot_block[:, None] * sent_local + local_ids[None, :]).reshape(1, -1)
    early = (
        inputs, rel_window, twice, windows, order, onehot, column_id, partner[None, :], segments[None, :]
    )
    first, second, third, fourth, early, done = gather_weights(
        pack_start(w_query, w_key, w_value, gains_col, w_in[:, :piece], w_out.T),
        columns(back_shard[:, :piece], pool_own, w_in[:, piece:], back_shard[:, piece:]),
        heads + LANES,
        piece + pool_half,
        early,
        begin,
        between,
    )
    inputs, rel_window, twice, windows, order, onehot, column_id, partner, seg_lane = early
    normed1_low, inverse1, gains, qkv, context, probs, hidden1, inverse2, normed2_low, act0, slope0 = done

    act1, slope1 = wide("act1", normed2_low, hidden_blocks(fourth), (), gelu_both, 2)
    pool_loads = [weight(side, piece, pool_half) for side in third]
    hidden2, inverse3, pooled_low, unit, unit_low, scale = narrow(
        "ffn_out",
        [(act0, i * piece, third[i], 0, piece) for i in range(2)]
        + [(act1, i * piece, fourth[i], piece, piece) for i in range(2)],
        (hidden1, gains, seg_lane, *pool_loads),
        (
            row_f32,
            column_f32,
            shape_of(BF16, sent_local, width),
            shape_of(F32, sent_local, width),
            shape_of(BF16, sent_local, width),
            shape_of(F32, sent_local, 1),
        ),
        tail_body,
        [pltpu.VMEM((seq, width), BF16)] * 2,
    )
    quarters = gather_dp(unit_low)

    total_sent = column_id.shape[1]
    sentence_loads = [part(seg_lane), *pool_loads, part(hidden2), part(inverse3), part(gains)]
    back_shapes = (row_f32, row_low, gain_f32)
    if total_sent <= 1024:
        loss_local, embed_low, d_hidden2, ffn_low, d_gain3 = head_call(
            quarters,
            unit,
            scale,
            partner,
            column_id,
            sentence_loads,
            (shape_of(F32, 1, 1), shape_of(BF16, sent_local, width), *back_shapes),
        )
    else:
        every = rows(*quarters)
        position = jnp.arange(total_sent, dtype=jnp.int32)
        sims = dot_nt(every, every) * SOFTMAX_TEMP
        sims = jnp.where(position[:, None] == position[None, :], NEG_FILL, sims)
        lse_row = jax.nn.logsumexp(sims, axis=0, keepdims=True)
        own_sims = sims[:sent_local]
        own_lse = jax.nn.logsumexp(own_sims, axis=1, keepdims=True)
        is_target = column_id == partner.reshape(-1, 1)
        target = jnp.sum(jnp.where(is_target, own_sims, 0.0), axis=-1, keepdims=True)
        loss_local = jnp.sum(own_lse - target)
        hit = is_target.astype(F32)
        d_rows = low(LOSS_SCALE * (jnp.exp(own_sims - own_lse) - hit))
        d_cols = low(LOSS_SCALE * (jnp.exp(own_sims - lse_row) - hit))
        d_unit = SOFTMAX_TEMP * (dot(d_rows, every) + dot(d_cols, every))
        embed_low = low(scale * (d_unit - unit * jnp.sum(d_unit * unit, axis=-1, keepdims=True)))
        d_hidden2, ffn_low, d_gain3 = sentence_call(embed_low, sentence_loads, back_shapes)

    half = width // 2
    quarter = width // 4

    back0_sent, back1_sent = gradients("back_sent", ffn_low, half, half, (act0, act1))
    (pool_sent,) = gradients("pool_sent", pooled_low, half, half, (embed_low,))
    back0_got, back1_got, pool_got, ffn_later = go(
        (), (core, back0_sent), (core, back1_sent), (core, pool_sent), keep=(ffn_low,)
    )
    up0 = wide("up0", ffn_later, hidden_blocks(third), (slope0,), times_slope)

    pool_hi = product(pooled_low, quarter, half, embed_low, pool_got[quarter:])
    pool_lo = product(pooled_low, 0, quarter, embed_low, pool_got[:quarter])
    back_hi = product(ffn_low, quarter, half, act0, back0_got[quarter:])
    back_lo = product(ffn_low, 0, quarter, act0, back0_got[:quarter])
    back_own = product(ffn_low, 0, half, act1[:, :piece], back1_got[:, :piece])
    back_oth = product(ffn_low, 0, half, act1[:, piece:], back1_got[:, piece:])
    got_pool, got_lo, got_own, ffn_later, up0, pool_lo, back_lo, back_own = go(
        (),
        (cross, pool_hi),
        (cross, back_hi),
        (over, back_oth),
        keep=(ffn_later, up0, pool_lo, back_lo, back_own),
    )
    up1 = wide("up1", ffn_later, hidden_blocks(fourth, piece), (slope1,), times_slope)
    in0_sent, in1_sent = gradients("in_sent", normed2_low, half, half, (up0, up1))
    in0_got, in1_got, up0, up1 = go((), (core, in0_sent), (core, in1_sent), keep=(up0, up1))
    attn_low, d_gain2, d_hidden1 = narrow(
        "ffn_in_back",
        [(up0, i * piece, second[i], 0, piece) for i in range(2)]
        + [(up1, i * piece, fourth[i], 0, piece) for i in range(2)],
        (hidden1, inverse2, gains, d_hidden2),
        (row_low, gain_f32, row_f32),
        functools.partial(back_body, 1),
    )
    d_context = wide("d_context", attn_low, [(second[side], piece, inner_half) for side in range(2)])

    pool_lo = add(pool_lo, got_pool)
    back_lo = add(back_lo, got_lo)
    back_own = add(back_own, got_own)
    in_hi = product(normed2_low, quarter, half, up0, in0_got[quarter:])
    in_lo = product(normed2_low, 0, quarter, up0, in0_got[:quarter])
    in_own = product(normed2_low, 0, half, up1[:, :piece], in1_got[:, :piece])
    in_oth = product(normed2_low, 0, half, up1[:, piece:], in1_got[:, piece:])
    got_first, got_second, got_in_lo, got_in_own, d_context, pool_lo, back_lo, back_own, in_lo, in_own = go(
        (got_pool, got_lo, got_own),
        (over, columns(back_lo[:, piece:], pool_lo[:, pool_half:])),
        (cross, back_own[quarter:]),
        (cross, in_hi),
        (over, in_oth),
        keep=(d_context, pool_lo, back_lo, back_own, in_lo, in_own),
    )
    d_qkv, d_bias = attend_backward(qkv, d_context, probs)
    query_both = 2 * inner_half
    late_sent = sent_columns("late_sent", half, ((attn_low, context), (normed1_low, d_qkv)))
    late_got, d_qkv_later = go((), (core, late_sent), keep=(d_qkv,))
    grad_slots, d_gain1 = narrow(
        "qkv_back",
        [(d_qkv_later, i * inner_half, first[i], 0, inner_half) for i in range(2)]
        + [(d_qkv_later, (1 + i) * query_both, first[i], inner_half, query_both) for i in range(2)],
        (inputs, inverse1, gains, d_hidden1),
        (row_low, gain_f32),
        functools.partial(back_body, 0),
    )

    small_rows = -(-(3 * (width // LANES) + 1) // 8) * 8 + bucket_count
    (flat,) = whole_call(
        functools.partial(small_kernel, heads_half),
        (d_gain1, d_gain2, d_gain3, order, d_bias.reshape(-1, WIN), onehot, loss_local.reshape(1, 1), mine.reshape(1, 1)),
        (shape_of(F32, small_rows, LANES),),
        (),
        "small",
    )
    (grad_own,) = whole_call(turn_kernel, (grad_slots, order), (row_low,), (), "turn")

    far = rest_hops(size)
    back_all = columns(
        add(back_lo[:, :piece], got_first[:, :piece]),
        add(back_own[:quarter], got_second),
        add(pool_lo[:, :pool_half], got_first[:, piece:]),
    )
    back_rest, back_stay = rest_start(back_all)
    in_lo = add(in_lo, got_in_lo)
    in_own = add(in_own, got_in_own)
    out_got, qkv_got = late_got[:, :query_both], late_got[:, query_both:]
    out_hi = product(attn_low, quarter, half, context, out_got[quarter:])
    out_lo = product(attn_low, 0, quarter, context, out_got[:quarter])
    query_hi = product(normed1_low, quarter, half, d_qkv[:, :query_both], qkv_got[quarter:, :query_both])
    query_lo = product(normed1_low, 0, quarter, d_qkv[:, :query_both], qkv_got[:quarter, :query_both])
    kv_own = product(
        normed1_low, 0, half, d_qkv[:, query_both : 2 * query_both], qkv_got[:, query_both : 2 * query_both]
    )
    kv_oth = product(normed1_low, 0, half, d_qkv[:, 2 * query_both :], qkv_got[:, 2 * query_both :])
    rest_hop = [functools.partial(hop, mask=j * 4) for j in range(1, min(4, size // 4))]
    back_more, got_first, got_x, got_kv, flat_got, back_stay, in_lo, in_own, out_lo, query_lo, kv_own, flat = go(
        (got_first, got_second, got_in_lo, got_in_own, late_got, grad_own, flat),
        (far[0], back_rest),
        (over, in_lo[:, piece:]),
        (cross, columns(in_own[quarter:], out_hi, query_hi)),
        (over, kv_oth),
        (over, flat),
        keep=(back_stay, in_lo, in_own, out_lo, query_lo, kv_own, flat),
    )
    flat = flat + flat_got
    got_second, got_out, got_query = got_x[:, :piece], got_x[:, piece:][:, :query_both], got_x[:, piece + query_both :]

    back_all = add(back_stay, back_more)
    back_rest, back_stay = rest_start(back_all)
    in_all = columns(add(in_lo[:, :piece], got_first), add(in_own[:quarter], got_second))
    in_rest, in_stay = rest_start(in_all)
    out_lo = add(out_lo, got_out)
    query_lo = add(query_lo, got_query)
    kv_own = add(kv_own, got_kv)
    back_more, in_more, got_first, got_second, grad_other, flat_got, back_stay, in_stay, out_lo, query_lo, kv_own, flat = go(
        (),
        (far[1], back_rest),
        (far[0], in_rest),
        (over, columns(out_lo[:, inner_half:], query_lo[:, inner_half:])),
        (cross, kv_own[quarter:]),
        (over, grad_own),
        (core, flat),
        keep=(back_stay, in_stay, out_lo, query_lo, kv_own, flat),
        join=False,
    )
    back_more, in_more, got_first, got_second, flat_got = lax.optimization_barrier(
        (back_more, in_more, got_first, got_second, flat_got)
    )
    flat = flat + flat_got

    def finish(value):
        value = value.astype(F32)
        for send in far[2:]:
            value = sum_half(value, send)
        return value

    back_all = finish(back_stay.astype(F32) + back_more.astype(F32))
    grad_back = back_all[:, :hidden_half]
    grad_pool = back_all[:, hidden_half:]
    in_all = add(in_stay, in_more)
    in_rest, in_stay = rest_start(in_all)
    last = columns(
        add(out_lo[:, :inner_half], got_first[:, :inner_half]),
        add(query_lo[:, :inner_half], got_first[:, inner_half:]),
        add(kv_own[:quarter], got_second),
    )
    n_in, n_last = in_rest.shape[1], last.shape[1]
    if len(far) == 2:
        rest = last.shape[0] // 4
        got_one, got_two, got_three, flat_got, in_stay, last_stay, flat = go(
            (),
            (rest_hop[0], columns(in_rest, last[rest : 2 * rest])),
            (rest_hop[1], last[2 * rest : 3 * rest]),
            (rest_hop[2], last[3 * rest :]),
            (cross, flat),
            keep=(in_stay, last[:rest], flat),
        )
        in_more = got_one[:, :n_in]
        last_more = got_one[:, n_in:].astype(F32) + got_two.astype(F32) + got_three.astype(F32)
    else:
        in_more, last_more, flat_got = go(
            (), (far[1], in_rest), (far[0], last[last.shape[0] // 2 :]), (cross, flat)
        )
        last = add(last[: last.shape[0] // 2], last_more)
        last_rest, last_stay = rest_start(last)
        last_more = far[1](last_rest)

    flat = flat + flat_got
    pool_other, *flat_got = go(
        (in_more, last_more), (over, grad_pool), *((how, flat) for how in rest_hop), join=False
    )
    flat = flat + sum(flat_got)
    for send in far[:-2]:
        flat = flat + send(flat)
    grad_last = finish(last_stay.astype(F32) + last_more.astype(F32))
    grad_in = finish(in_stay.astype(F32) + in_more.astype(F32))
    grad_out = grad_last[:, :inner_half]
    grad_qkv = grad_last[:, inner_half:]
    grad_tokens = jnp.where(
        mine == 0, jnp.stack([grad_own, grad_other]), jnp.stack([grad_other, grad_own])
    )
    across = width // LANES
    gains_mine = lax.dynamic_slice_in_dim(flat[: 3 * across].reshape(3, width), me * block, block, axis=1)
    loss = flat[3 * across, 0] / (micro_count * sent_local * size)
    table_sum = flat[small_rows - bucket_count :, : 2 * heads_half]
    table_mine = lax.dynamic_slice_in_dim(table_sum, mine * heads_half, heads_half, axis=1)
    grad_pool = jnp.where(mine == 0, columns(grad_pool, pool_other), columns(pool_other, grad_pool))
    return (
        loss,
        grad_tokens,
        grad_qkv[:, :inner_half],
        grad_qkv[:, inner_half : 2 * inner_half],
        grad_qkv[:, 2 * inner_half :],
        grad_out.T,
        grad_in,
        grad_back.T,
        gains_mine[0],
        gains_mine[1],
        gains_mine[2],
        grad_pool,
        table_mine,
    )


def solution(mesh):
    placed = (
        P(None, "dp", None),
        P(None, "dp", None),
        P(),
        P(None, "dp"),
        P("dp", "mp"),
        P("dp", "mp"),
        P("dp", "mp"),
        P("mp", "dp"),
        P("dp", "mp"),
        P("mp", "dp"),
        P("dp"),
        P("dp"),
        P("dp"),
        P("dp", None),
        P(None, "mp"),
    )
    return jax.shard_map(
        shards,
        mesh=mesh,
        in_specs=placed,
        out_specs=(
            P(),
            P(None, "dp", None),
            P("dp", "mp"),
            P("dp", "mp"),
            P("dp", "mp"),
            P("mp", "dp"),
            P("dp", "mp"),
            P("mp", "dp"),
            P("dp"),
            P("dp"),
            P("dp"),
            P("dp", None),
            P(None, "mp"),
        ),
        check_vma=False,
    )
```

```python
import functools

import jax
import jax.numpy as jnp
from jax import lax
from jax.experimental import pallas as pl
from jax.experimental.pallas import tpu as pltpu
from jax.sharding import PartitionSpec as P

NEG_FILL = -1000000000.0
SCORE_SCALE = 0.125
SOFTMAX_TEMP = 50.0
LOSS_SCALE = 64.0
EPSILON = 1e-06
REACH = 32
QB = 64
WIN = QB + 2 * REACH
LANES = 128
GELU_A = 0.7978845608028654
GELU_B = 0.044715

BF16 = jnp.bfloat16
F32 = jnp.float32
HIGHEST = lax.Precision.HIGHEST


def dot(left, right, dims=((1,), (0,)), precision=None):
    return lax.dot_general(
        left, right, (dims, ((), ())), precision=precision, preferred_element_type=F32
    )


def dot_nt(left, right):
    return dot(left, right, ((1,), (1,)))


def dot_tn(left, right):
    return dot(left, right, ((0,), (0,)))


def rms_forward(value, gain):
    inverse = lax.rsqrt(jnp.mean(value * value, axis=-1, keepdims=True) + EPSILON)
    return (value * inverse * gain, inverse)


def cost(flops, bytes_accessed):
    return pl.CostEstimate(flops=0, bytes_accessed=0, transcendentals=0)


def params(mib=16):
    return pltpu.CompilerParams(vmem_limit_bytes=mib * 2**20)


def split_dot(left, right, dims=((1,), (0,))):
    high = right.astype(BF16)
    rest = (right - high.astype(F32)).astype(BF16)
    return dot(left, high, dims) + dot(left, rest, dims)


def stream_kernel(plan, operands, outs, body, *refs):
    sources, out_refs = refs[:operands], refs[operands : operands + outs]
    more = refs[operands + outs :]
    buffers, sem = more[: sum(len(load) > 1 for load in plan)], more[-1]
    more = more[len(buffers) : -1]
    copies, places, used = [], [], 0
    for load in plan:
        if len(load) == 1:
            which, _, _, col, width, _ = load[0]
            places.append(sources[which].at[:, pl.ds(col, width)])
            copies.append([])
            continue
        buffer = buffers[used]
        used += 1
        group = []
        for which, at, count, col, width, number in load:
            copy = pltpu.make_async_copy(
                sources[which].at[:, pl.ds(col, width)], buffer.at[pl.ds(at, count)], sem.at[number]
            )
            copy.start()
            group.append(copy)
        places.append(buffer)
        copies.append(group)
    ready = set()

    def get(i):
        if i not in ready:
            ready.add(i)
            for copy in copies[i]:
                copy.wait()
        return places[i]

    body(get, *out_refs, *more)


def stream(name, loads, out_shapes, body, scratch=(), mib=16):
    arrays, spaces = [], []

    def place(array, space):
        for i, known in enumerate(arrays):
            if known is array and spaces[i] is space:
                return i
        arrays.append(array)
        spaces.append(space)
        return len(arrays) - 1

    plan, buffers, number = [], [], 0
    for load in loads:
        steps, at = [], 0
        space = pltpu.VMEM if len(load) == 1 else pltpu.HBM
        for array, col, width in load:
            steps.append((place(array, space), at, array.shape[0], col, width, number))
            at += array.shape[0]
            number += 1
        plan.append(steps)
        if len(load) > 1:
            buffers.append(pltpu.VMEM((at, load[0][2]), load[0][0].dtype))
    return pl.pallas_call(
        functools.partial(stream_kernel, plan, len(arrays), len(out_shapes), body),
        out_shape=tuple(out_shapes),
        in_specs=[pl.BlockSpec(memory_space=space) for space in spaces],
        out_specs=tuple(pl.BlockSpec(memory_space=pltpu.VMEM) for _ in out_shapes),
        scratch_shapes=buffers + list(scratch) + [pltpu.SemaphoreType.DMA((number,))],
        compiler_params=params(mib),
        cost_estimate=cost(0, 0),
        name=name,
    )(*arrays)


def part(array, col=0, width=None):
    return [(array, col, array.shape[1] - col if width is None else width)]


def weight(pieces, col, width):
    return [(piece, col, width) for piece in pieces]


def wide(name, x, blocks, extras=(), body=None, outs=1):
    widths = [width for *_, width in blocks]
    loads = [part(x)]
    for i, block in enumerate(blocks):
        loads.append(weight(*block))
        for extra in extras:
            loads.append(part(extra, sum(widths[:i]), widths[i]))

    def run(get, *out_refs):
        at = 0
        per = 1 + len(extras)
        for i, width in enumerate(widths):
            first = 1 + i * per
            value = dot(get(0)[...], get(first)[...])
            got = [get(first + 1 + j)[...] for j in range(len(extras))]
            values = (value,) if body is None else body(value, *got)
            for ref, result in zip(out_refs, values):
                ref[:, at : at + width] = result.astype(BF16)
            at += width

    shape = shape_of(BF16, x.shape[0], sum(widths))
    result = stream(name, loads, (shape,) * outs, run)
    return result if outs > 1 else result[0]


def gelu_both(up):
    square = up * up
    bend = jnp.tanh(GELU_A * up * (1.0 + GELU_B * square))
    half_one = 0.5 + 0.5 * bend
    inner = GELU_A + (3.0 * GELU_A * GELU_B) * square
    return up * half_one, half_one + 0.5 * up * (1.0 - bend * bend) * inner


def times_slope(value, slope):
    return (value * slope.astype(F32),)


def narrow(name, work, extras, out_shapes, body, scratch=(), mib=16):
    loads = []
    for x, x_col, pieces, col, width in work:
        loads += [part(x, x_col, width), weight(pieces, col, width)]
    first = len(loads)
    loads += [extra if isinstance(extra, list) else part(extra) for extra in extras]

    def run(get, *refs):
        out_refs, more = refs[: len(out_shapes)], refs[len(out_shapes) :]
        acc = more[0]
        for j in range(len(work)):
            value = dot_nt(get(2 * j)[...], get(2 * j + 1)[...])
            acc[...] = value if j == 0 else acc[...] + value
        body(acc, *(get(first + i) for i in range(len(extras))), *out_refs, *more[1:])

    depth = sum(piece.shape[0] for piece in work[0][2])
    return stream(
        name, loads, out_shapes, run, [pltpu.VMEM((work[0][0].shape[0], depth), F32), *scratch], mib
    )


def gradients(name, left, first, count, rights, out_of=None):
    loads = [part(left, first, count)] + [part(right) for right in rights]

    def run(get, *refs):
        *out_refs, turned = refs
        turned[...] = get(0)[...].T
        for i, ref in enumerate(out_refs):
            ref[...] = dot(turned[...], get(1 + i)[...]).astype(BF16)

    shapes = [shape_of(BF16, count, right.shape[1]) for right in rights]
    return stream(name, loads, shapes, run, [pltpu.VMEM((count, left.shape[0]), BF16)])


def sent_columns(name, first, pairs):
    loads = [load for left, right in pairs for load in (part(left, first, first), part(right))]

    def run(get, out_ref, turned):
        at = 0
        for i, (_, right) in enumerate(pairs):
            turned[...] = get(2 * i)[...].T
            n = right.shape[1]
            out_ref[:, at : at + n] = dot(turned[...], get(2 * i + 1)[...]).astype(BF16)
            at += n

    shape = shape_of(BF16, first, sum(right.shape[1] for _, right in pairs))
    return stream(name, loads, (shape,), run, [pltpu.VMEM((first, pairs[0][0].shape[0]), BF16)])[0]


def stack_rows(pieces, widths):
    block = pieces[0].shape[0]
    cuts = [sum(widths[:i]) for i in range(len(widths))]
    if block % 16:
        whole = jnp.concatenate(pieces, axis=0)
        return [whole[:, at : at + width] for at, width in zip(cuts, widths)]

    def run(*refs):
        for i, ref in enumerate(refs[: len(pieces)]):
            for j, out in enumerate(refs[len(pieces) :]):
                out[i * block : (i + 1) * block] = ref[:, cuts[j] : cuts[j] + widths[j]]

    shapes = [shape_of(pieces[0].dtype, block * len(pieces), width) for width in widths]
    return whole_call(run, pieces, shapes, (), "stack_rows")


def qkv_call(inputs, first, n):
    blocks = [(side, i * n, n) for i in range(3) for side in first]
    loads = [part(inputs), weight(first[0], 3 * n, LANES)] + [weight(*block) for block in blocks]

    def run(get, qkv_ref, normed_ref, inverse_ref, gains_ref):
        value = get(0)[...]
        inverse = lax.rsqrt(jnp.mean(value * value, axis=1, keepdims=True) + EPSILON)
        inverse_ref[...] = inverse
        gains = get(1)[...].astype(F32).T[:8]
        gains_ref[...] = gains
        normed_ref[...] = (value * inverse * gains[0:1]).astype(BF16)
        for i in range(len(blocks)):
            qkv_ref[:, i * n : (i + 1) * n] = dot(normed_ref[...], get(2 + i)[...]).astype(BF16)

    seq, width = inputs.shape
    shapes = (
        shape_of(BF16, seq, 6 * n),
        shape_of(BF16, seq, width),
        shape_of(F32, seq, 1),
        shape_of(F32, 8, width),
    )
    return stream("qkv", loads, shapes, run)


def norm_body(row, acc, value_ref, gains_ref, hidden_ref, inverse_ref, normed_ref=None):
    hidden = value_ref[...] + acc[...]
    inverse = lax.rsqrt(jnp.mean(hidden * hidden, axis=1, keepdims=True) + EPSILON)
    hidden_ref[...] = hidden
    inverse_ref[...] = inverse
    if normed_ref is not None:
        normed_ref[...] = (hidden * inverse * gains_ref[row : row + 1, :]).astype(BF16)


def norm_back(value, inverse, gain, grad):
    scaled = grad * gain
    inner = jnp.mean(value * scaled, axis=1, keepdims=True)
    d_value = inverse * scaled - value * (inverse * inverse * inverse) * inner
    return d_value, jnp.sum(grad * value * inverse, axis=0, keepdims=True)


def back_body(row, acc, value_ref, inverse_ref, gains_ref, grad_ref, low_ref, gain_out, hidden_ref=None):
    d_value, d_gain = norm_back(
        value_ref[...], inverse_ref[...], gains_ref[row : row + 1, :], acc[...]
    )
    total = grad_ref[...] + d_value
    low_ref[...] = total.astype(BF16)
    gain_out[...] = d_gain
    if hidden_ref is not None:
        hidden_ref[...] = total


def turn_kernel(grad_ref, order_ref, out_ref):
    out_ref[...] = dot_nt(grad_ref[...], order_ref[...]).astype(BF16)


def small_kernel(heads_half, one_ref, two_ref, three_ref, order_ref, bias_ref, onehot_ref, loss_ref, mine_ref, out_ref):
    width = one_ref.shape[1]
    gains = jnp.concatenate([one_ref[...], two_ref[...], three_ref[...], jnp.zeros((5, width), F32)], axis=0)
    high = gains.astype(BF16)
    rest = (gains - high.astype(F32)).astype(BF16)
    gains = dot_nt(high, order_ref[...]) + dot_nt(rest, order_ref[...])
    out_ref[...] = jnp.zeros_like(out_ref)
    across = width // LANES
    for i in range(3):
        for j in range(across):
            at = i * across + j
            out_ref[at : at + 1, :] = gains[i : i + 1, j * LANES : (j + 1) * LANES]
    at = 3 * across
    lane = lax.broadcasted_iota(jnp.int32, (1, LANES), 1)
    out_ref[at : at + 1, :] = jnp.where(lane == 0, loss_ref[...], 0.0)
    bias = bias_ref[...]
    heads = 2 * heads_half
    row = lax.broadcasted_iota(jnp.int32, (LANES, bias.shape[0]), 0)
    column = lax.broadcasted_iota(jnp.int32, (LANES, bias.shape[0]), 1)
    source = row + jnp.where(mine_ref[...] == 0, 0, heads_half)
    source = jnp.where(source >= heads, source - heads, source)
    pick = jnp.where((column == 8 * (source // 2) + source % 2) & (row < heads), 1.0, 0.0)
    bias = split_dot(pick.astype(BF16), bias)
    high = bias.astype(BF16)
    rest = (bias - high.astype(F32)).astype(BF16)
    table = dot_nt(high, onehot_ref[...]) + dot_nt(rest, onehot_ref[...])
    count = table.shape[1]
    a_row = LANES // count
    for head in range(heads):
        place = head % a_row * count
        line = at + 1 + head // a_row
        out_ref[line : line + 1, place : place + count] = table[head : head + 1, :]


def member_of(seg_ref, sent_count):
    ids = lax.broadcasted_iota(jnp.int32, (sent_count, seg_ref.shape[1]), 0)
    hit = jnp.where(seg_ref[...] == ids, 1.0, 0.0)
    return hit.astype(BF16), jnp.sum(hit, axis=1, keepdims=True)


def tail_body(acc, value_ref, gains_ref, seg_ref, own_ref, other_ref, hidden_ref, inverse_ref, pooled_ref, unit_ref, low_ref, scale_ref, high, rest):
    hidden = value_ref[...] + acc[...]
    inverse = lax.rsqrt(jnp.mean(hidden * hidden, axis=1, keepdims=True) + EPSILON)
    hidden_ref[...] = hidden
    inverse_ref[...] = inverse
    final = hidden_ref[...] * inverse * gains_ref[2:3, :]
    high[...] = final.astype(BF16)
    rest[...] = (final - high[...].astype(F32)).astype(BF16)
    sents, count = member_of(seg_ref, pooled_ref.shape[0])
    pooled = ((dot(sents, high[...]) + dot(sents, rest[...])) / count).astype(BF16)
    pooled_ref[...] = pooled
    half = own_ref.shape[1]
    left = dot(pooled, own_ref[...])
    right = dot(pooled, other_ref[...])
    square = jnp.sum(left * left, axis=1, keepdims=True) + jnp.sum(right * right, axis=1, keepdims=True)
    scale = lax.rsqrt(square + EPSILON)
    scale_ref[...] = scale
    for at, value in ((0, left * scale), (half, right * scale)):
        unit_ref[:, at : at + half] = value
        low_ref[:, at : at + half] = value.astype(BF16)


def head_call(quarters, unit, scale, partner, column, sentence_loads, out_shapes):
    loads = [part(q) for q in (*quarters, unit, scale, partner, column)] + sentence_loads
    quarter = quarters[0].shape[0]
    total = 4 * quarter

    def run(get, loss_ref, embed_ref, *refs):
        *back_refs, every = refs
        for i in range(4):
            every[i * quarter : (i + 1) * quarter] = get(i)[...]
        unit, scale, partner, columns_id = (get(i)[...] for i in range(4, 8))
        partner = as_columns(
            jnp.concatenate([partner, jnp.zeros((1, LANES - partner.shape[1]), jnp.int32)], axis=1)
        )[: partner.shape[1], 0:1]
        own_count = unit.shape[0]
        sims = dot_nt(every[...], every[...]) * SOFTMAX_TEMP
        row = lax.broadcasted_iota(jnp.int32, (total, total), 0)
        column = lax.broadcasted_iota(jnp.int32, (total, total), 1)
        sims = jnp.where(row == column, NEG_FILL, sims)
        top = jnp.max(sims, axis=0, keepdims=True)
        lse_row = top + jnp.log(jnp.sum(jnp.exp(sims - top), axis=0, keepdims=True))
        own = sims[:own_count]
        own_top = jnp.max(own, axis=1, keepdims=True)
        own_lse = own_top + jnp.log(jnp.sum(jnp.exp(own - own_top), axis=1, keepdims=True))
        is_target = columns_id.astype(F32) == partner
        hit = jnp.where(is_target, 1.0, 0.0)
        target = jnp.sum(jnp.where(is_target, own, 0.0), axis=1, keepdims=True)
        loss_ref[...] = jnp.sum(own_lse - target, axis=0, keepdims=True)
        d_rows = (LOSS_SCALE * (jnp.exp(own - own_lse) - hit)).astype(BF16)
        d_cols = (LOSS_SCALE * (jnp.exp(own - lse_row) - hit)).astype(BF16)
        d_unit = SOFTMAX_TEMP * (dot(d_rows, every[...]) + dot(d_cols, every[...]))
        inner = jnp.sum(d_unit * unit, axis=1, keepdims=True)
        d_embed = (scale * (d_unit - unit * inner)).astype(BF16)
        embed_ref[...] = d_embed
        sentence_back(d_embed, [get(8 + i) for i in range(len(sentence_loads))], *back_refs)

    return stream("head", loads, out_shapes, run, [pltpu.VMEM((total, unit.shape[1]), BF16)])


def sentence_call(embed, sentence_loads, out_shapes):
    def run(get, *back_refs):
        sentence_back(get(0)[...], [get(1 + i) for i in range(len(sentence_loads))], *back_refs)

    return stream("sentence", [part(embed)] + sentence_loads, out_shapes, run)


def sentence_back(d_embed, sources, hidden_ref, low_ref, gain_out):
    seg_ref, own_ref, other_ref, value_ref, inverse_ref, gains_ref = sources
    half = own_ref.shape[1]
    d_pooled = dot_nt(d_embed[:, :half], own_ref[...]) + dot_nt(d_embed[:, half:], other_ref[...])
    sents, count = member_of(seg_ref, d_embed.shape[0])
    d_final = split_dot(sents, d_pooled / count, ((0,), (0,)))
    d_value, d_gain = norm_back(value_ref[...], inverse_ref[...], gains_ref[2:3, :], d_final)
    hidden_ref[...] = d_value
    low_ref[...] = d_value.astype(BF16)
    gain_out[...] = d_gain


def whole_call(body, args, out_shapes, scratch=(), name=None):
    return pl.pallas_call(
        body,
        out_shape=tuple(out_shapes),
        in_specs=[pl.BlockSpec(memory_space=pltpu.VMEM)] * len(args),
        out_specs=tuple(pl.BlockSpec(memory_space=pltpu.VMEM) for _ in out_shapes),
        scratch_shapes=scratch,
        compiler_params=params(),
        cost_estimate=cost(0, 0),
        name=name,
    )(*args)


def shape_of(kind, *dims):
    return jax.ShapeDtypeStruct(dims, kind)


def _stack_heads(part):
    lane = lax.broadcasted_iota(jnp.int32, part.shape, 1)
    zero = jnp.zeros_like(part)
    first = lane < LANES // 2
    return jnp.concatenate(
        [jnp.where(first, part, zero), jnp.where(first, zero, part)], axis=0
    )


def _unstack_heads(both):
    half = both.shape[0] // 2
    lane = lax.broadcasted_iota(jnp.int32, (half, LANES), 1)
    return jnp.where(lane < LANES // 2, both[:half], both[half:])


def _pad_keys(pad, ref):
    seq = ref.shape[0]
    pad[0:REACH] = jnp.zeros((REACH, LANES), pad.dtype)
    pad[REACH + seq :] = jnp.zeros((REACH, LANES), pad.dtype)
    pad[REACH : REACH + seq] = ref[...]


def _query_bits(shape):
    return lax.broadcasted_iota(jnp.int32, shape, 0) & (QB - 1)


def as_columns(values):
    count, length = values.shape
    side = max(LANES, length)
    square = jnp.concatenate([values.astype(F32), jnp.zeros((side - count, length), F32)], axis=0)
    return square.T


def attend_forward_kernel(
    q_ref, k_ref, v_ref, segq_ref, segk_ref, rel_ref, ctx_ref, probs_ref, kpad, vpad, mask, scores
):
    seq = q_ref.shape[0]
    blocks = seq // QB
    _pad_keys(kpad, k_ref)
    _pad_keys(vpad, v_ref)

    @pl.when(pl.program_id(0) == 0)
    def _():
        keys = as_columns(segk_ref[...])
        for b in range(blocks):
            same = keys[:, b : b + 1] == segq_ref[b : b + 1, :].astype(F32)
            mask[b] = jnp.where(same, 0.0, NEG_FILL)

    rel = rel_ref[0]
    row = lax.broadcasted_iota(jnp.int32, (2 * QB, WIN), 0)
    bias = jnp.where(row < QB, rel[0:1, :], rel[1:2, :])
    bits = _query_bits((2 * QB, WIN))
    step = 1
    while step < QB:
        bias = jnp.where((bits & step) != 0, pltpu.roll(bias, step, 1), bias)
        step *= 2
    bias = bias.T
    for b in range(blocks):
        query = _stack_heads(q_ref[b * QB : (b + 1) * QB] * jnp.asarray(SCORE_SCALE, BF16))
        scores[b] = dot_nt(kpad[b * QB : b * QB + WIN], query)
    values = scores[...] + bias[None] + mask[...]
    top = jnp.max(values, axis=1, keepdims=True)
    shifted = jnp.exp(values - top)
    total = jnp.sum(shifted, axis=1, keepdims=True)
    probs_ref[0] = (shifted * (1.0 / total)).astype(BF16)
    for b in range(blocks):
        part = dot_tn(probs_ref[0, b], vpad[b * QB : b * QB + WIN])
        ctx_ref[b * QB : (b + 1) * QB] = _unstack_heads(part).astype(BF16)


def attend_backward_kernel(
    q_ref, k_ref, v_ref, dctx_ref, probs_ref, dqkv_ref, dbias_ref,
    kpad, vpad, dk_acc, dv_acc, d_probs, d_low,
):
    seq = q_ref.shape[0]
    pair = pl.program_id(0)
    side = pl.num_programs(0) // 2
    later = pair // side
    q_at = pl.ds(pl.multiple_of(pair * LANES, LANES), LANES)
    k_at = pl.ds(pl.multiple_of((pair + 2 * side + later * side) * LANES, LANES), LANES)
    v_at = pl.ds(pl.multiple_of((pair + 3 * side + later * side) * LANES, LANES), LANES)
    blocks = seq // QB
    _pad_keys(kpad, k_ref)
    _pad_keys(vpad, v_ref)
    dk_acc[...] = jnp.zeros_like(dk_acc)
    dv_acc[...] = jnp.zeros_like(dv_acc)
    for b in range(blocks):
        window = slice(b * QB, b * QB + WIN)
        d_ctx = _stack_heads(dctx_ref[b * QB : (b + 1) * QB])
        d_probs[b] = dot_nt(vpad[window], d_ctx)
        dv_acc[window] += dot(probs_ref[0, b], d_ctx)
    probs = probs_ref[0].astype(F32)
    product = probs * d_probs[...]
    inner = jnp.sum(product, axis=1, keepdims=True)
    d_scores = product - probs * inner
    d_low[...] = d_scores.astype(BF16)
    total = jnp.sum(d_scores, axis=0).T
    for b in range(blocks):
        here = slice(b * QB, (b + 1) * QB)
        window = slice(b * QB, b * QB + WIN)
        query = _stack_heads(q_ref[here] * jnp.asarray(SCORE_SCALE, BF16))
        dk_acc[window] += dot(d_low[b], query)
        d_query = _unstack_heads(dot_tn(d_low[b], kpad[window])) * SCORE_SCALE
        dqkv_ref[here, q_at] = d_query.astype(BF16)
    dqkv_ref[:, k_at] = dk_acc[REACH : REACH + seq].astype(BF16)
    dqkv_ref[:, v_at] = dv_acc[REACH : REACH + seq].astype(BF16)
    bits = _query_bits((2 * QB, WIN))
    step = 1
    while step < QB:
        total = jnp.where((bits & step) != 0, pltpu.roll(total, WIN - step, 1), total)
        step *= 2
    first = jnp.sum(total[:QB], axis=0, keepdims=True)
    second = jnp.sum(total[QB:], axis=0, keepdims=True)
    dbias_ref[0] = jnp.concatenate([first, second, jnp.zeros((6, WIN), F32)], axis=0)


def _qkv_specs(seq, pairs):
    def spec(kind):
        return pl.BlockSpec((seq, LANES), lambda p: (0, kind * pairs + p))

    return [spec(0), spec(1), spec(2)]


def attend_forward(qkv, twice, windows, rel_window):
    seq = qkv.shape[0]
    pairs = rel_window.shape[0]
    blocks = seq // QB
    return pl.pallas_call(
        attend_forward_kernel,
        grid=(pairs,),
        out_shape=(
            jax.ShapeDtypeStruct((seq, pairs * LANES), BF16),
            jax.ShapeDtypeStruct((pairs, blocks, WIN, 2 * QB), BF16),
        ),
        in_specs=_qkv_specs(seq, pairs)
        + [
            pl.BlockSpec((blocks, 2 * QB), lambda p: (0, 0)),
            pl.BlockSpec((blocks, WIN), lambda p: (0, 0)),
            pl.BlockSpec((1, 2, WIN), lambda p: (p, 0, 0)),
        ],
        out_specs=(
            pl.BlockSpec((seq, LANES), lambda p: (0, p)),
            pl.BlockSpec((1, blocks, WIN, 2 * QB), lambda p: (p, 0, 0, 0)),
        ),
        scratch_shapes=[pltpu.VMEM((seq + 2 * REACH, LANES), BF16)] * 2
        + [pltpu.VMEM((blocks, WIN, 2 * QB), F32)] * 2,
        compiler_params=params(),
        cost_estimate=cost(8 * seq * WIN * LANES * pairs * 4, 8 * seq * LANES * pairs),
        name="attend_forward",
    )(qkv, qkv, qkv, twice, windows, rel_window)


def attend_backward(qkv, d_context, probs):
    seq = qkv.shape[0]
    pairs = probs.shape[0]
    blocks = seq // QB
    lane_block = pl.BlockSpec((seq, LANES), lambda p: (0, p))
    return pl.pallas_call(
        attend_backward_kernel,
        grid=(pairs,),
        out_shape=(
            jax.ShapeDtypeStruct((seq, 3 * pairs * LANES), BF16),
            jax.ShapeDtypeStruct((pairs, 8, WIN), F32),
        ),
        in_specs=_qkv_specs(seq, pairs)
        + [
            lane_block,
            pl.BlockSpec((1, blocks, WIN, 2 * QB), lambda p: (p, 0, 0, 0)),
        ],
        out_specs=(
            pl.BlockSpec((seq, 3 * pairs * LANES), lambda p: (0, 0)),
            pl.BlockSpec((1, 8, WIN), lambda p: (p, 0, 0)),
        ),
        scratch_shapes=[pltpu.VMEM((seq + 2 * REACH, LANES), BF16)] * 2
        + [pltpu.VMEM((seq + 2 * REACH, LANES), F32)] * 2
        + [pltpu.VMEM((blocks, WIN, 2 * QB), F32), pltpu.VMEM((blocks, WIN, 2 * QB), BF16)],
        compiler_params=params(),
        cost_estimate=cost(16 * seq * WIN * LANES * pairs * 4, 16 * seq * LANES * pairs),
        name="attend_backward",
    )(qkv, qkv, qkv, d_context, probs)


CORE = 1
CROSS = 2


def hop(value, mask):
    size = lax.axis_size("dp")
    return lax.ppermute(value, "dp", [(i, i ^ mask) for i in range(size)])


def over(value):
    return lax.ppermute(value, "mp", [(0, 1), (1, 0)])


def cross(value):
    return hop(value, CROSS)


def core(value):
    return hop(value, CORE)


def go(waits, *sends, keep=(), join=True):
    values = [value for _, value in sends]
    held = lax.optimization_barrier((*values, *keep, *waits))
    results = [how(value) for (how, _), value in zip(sends, held)]
    if join:
        results = list(lax.optimization_barrier(tuple(results)))
    return results + list(held[len(values) : len(values) + len(keep)])


def slot_masks(size):
    rest = size // 4
    return [z * 4 + x * 2 + c for c in range(2) for x in range(2) for z in range(rest)]


def strides(size):
    found = []
    stride = 4
    while stride < size:
        found.append(stride)
        stride *= 2
    return found


def gather_near(shard, waits, widths=None):
    size = lax.axis_size("dp")
    pieces = [shard]
    stride = 4
    while stride < size:
        radix = min(4, size // stride)
        shard = jnp.concatenate(pieces, axis=0) if len(pieces) > 1 else shard
        sends = [(functools.partial(hop, mask=j * stride), shard) for j in range(1, radix)]
        pieces = [shard] + go(waits, *sends)
        stride *= radix
    return jnp.concatenate(pieces, axis=0) if widths is None else stack_rows(pieces, widths)


def rows(*pieces):
    return jnp.concatenate(pieces, axis=0)


def columns(*pieces):
    return jnp.concatenate(pieces, axis=1)


def gather_weights(start, later, n_one, n_three, early, begin, between):
    size = lax.axis_size("dp")
    steps = strides(size)
    n_two = start.shape[1] - n_one
    if len(steps) == 2:
        got = go((), *((functools.partial(hop, mask=4 * j), start) for j in range(1, 4)))
        more = hop(later, 4)
        one, two = stack_rows([start, *got], (n_one, n_two))
        later = rows(later, more)
        wide_step = functools.partial(hop, mask=steps[1])
    else:
        one, two = gather_near(start, (), (n_one, n_two))

        def wide_step(value):
            whole = gather_near(value, ())
            return whole[value.shape[0] :]

    one_x, two_y, more, one_c, two_c = go(
        early, (cross, one), (over, two), (wide_step, later), (core, one), (core, two), join=False
    )
    one_x, two_y, one_c, two_c = lax.optimization_barrier((one_x, two_y, one_c, two_c))
    one_y, one_xy, two_x, two_yx = go(
        (),
        (over, one),
        (over, one_x),
        (cross, two),
        (cross, two_y),
        join=False,
    )
    one_y, one_xy, two_x, two_yx, more = lax.optimization_barrier((one_y, one_xy, two_x, two_yx, more))
    if later.shape[0] % 16 == 0:
        three, four = stack_rows((later, more), (n_three, later.shape[1] - n_three))
    else:
        later = rows(later, more)
        three, four = later[:, :n_three], later[:, n_three:]
    three_x, four_y, one_xc, one_yc, one_xyc, two_y, two_x, two_yx = go(
        (),
        (cross, three),
        (over, four),
        (core, one_x),
        (core, one_y),
        (core, one_xy),
        keep=(two_y, two_x, two_yx),
    )
    first = ((one, one_x, one_c, one_xc), (one_y, one_xy, one_yc, one_xyc))
    four_x, three_y, two_yc, two_xc, two_yxc, *kept = go(
        (three_x, four_y),
        (cross, four),
        (over, three),
        (core, two_y),
        (core, two_x),
        (core, two_yx),
        keep=(*first[0], *first[1], *early),
    )
    first = (tuple(kept[:4]), tuple(kept[4:8]))
    early = kept[8:]
    started = begin(first, early)
    second = ((two, two_x, two_c, two_xc), (two_y, two_yx, two_yc, two_yxc))
    four_yx, three_xy, four_c, four_yc, three_c, *kept = go(
        (four_x, three_y, two_yc, two_xc, two_yxc),
        (cross, four_y),
        (over, three_x),
        (core, four),
        (core, four_y),
        (core, three),
        keep=(*second[0], *second[1], *started),
    )
    second = (tuple(kept[:4]), tuple(kept[4:8]))
    done = between(kept[8:], second, early)
    four_xc, four_yxc, three_xc, three_yc, three_xyc, *done = go(
        (four_yx, three_xy, four_c, four_yc, three_c),
        (core, four_x),
        (core, four_yx),
        (core, three_x),
        (core, three_y),
        (core, three_xy),
        keep=done,
        join=False,
    )
    third = ((three, three_x, three_c, three_xc), (three_y, three_xy, three_yc, three_xyc))
    fourth = ((four, four_x, four_c, four_xc), (four_y, four_yx, four_yc, four_yxc))
    return first, second, third, fourth, early, done


def pack(name, sources):
    block = next(a.shape[0] for a, _, _, turned in sources if not turned)
    widths = [count for _, _, count, _ in sources]
    arrays = []
    for array, *_ in sources:
        if not any(array is known for known in arrays):
            arrays.append(array)

    def index(array):
        return next(i for i, known in enumerate(arrays) if known is array)

    def run(*refs):
        ins, out = refs[: len(arrays)], refs[len(arrays)]
        buffers, sem = refs[len(arrays) + 1 : -1], refs[-1]
        copies = []
        for i, (array, first, count, turned) in enumerate(sources):
            ref = ins[index(array)]
            ref = ref.at[pl.ds(first, count)] if turned else ref.at[:, pl.ds(first, count)]
            copies.append(pltpu.make_async_copy(ref, buffers[i], sem.at[i]))
            copies[-1].start()
        at = 0
        for copy, buffer, width, (_, _, _, turned) in zip(copies, buffers, widths, sources):
            copy.wait()
            value = buffer[...]
            out[:, at : at + width] = value.T if turned else value
            at += width

    scratch = [
        pltpu.VMEM((count, block) if turned else (block, count), BF16)
        for _, _, count, turned in sources
    ]
    return pl.pallas_call(
        run,
        out_shape=shape_of(BF16, block, sum(widths)),
        in_specs=[pl.BlockSpec(memory_space=pltpu.HBM)] * len(arrays),
        out_specs=pl.BlockSpec(memory_space=pltpu.VMEM),
        scratch_shapes=scratch + [pltpu.SemaphoreType.DMA((len(sources),))],
        compiler_params=params(),
        cost_estimate=cost(0, 0),
        name=name,
    )(*arrays)


def gather_dp(shard):
    near = gather_near(shard, ())
    side, c_near = go((near,), (cross, near), (core, near))
    return near, side, c_near, core(side)


def low(value):
    return value.astype(BF16)


def add(left, right):
    return (left.astype(F32) + right.astype(F32)).astype(BF16)


def product(left, begin, end, right, got=None):
    value = dot_tn(left[:, begin:end], right)
    if got is not None:
        value = value + got.astype(F32)
    return low(value)


def rest_start(value):
    half = value.shape[0] // 2
    return value[half:], value[:half]


def sum_half(value, send):
    gone, stays = rest_start(value)
    return stays + send(low(gone)).astype(F32)


def rest_hops(size):
    return [functools.partial(hop, mask=stride) for stride in reversed(strides(size))]


def shards(
    tokens,
    seg_ids,
    buckets,
    labels,
    w_query,
    w_key,
    w_value,
    w_out,
    w_in,
    w_back,
    gain_attn,
    gain_ffn,
    gain_final,
    w_pool,
    rel_table,
):
    micro_count, seq, width = tokens.shape
    size = lax.axis_size("dp")
    me = lax.axis_index("dp")
    mine = lax.axis_index("mp")
    block = width // size
    inner_half = w_query.shape[1]
    hidden_half = w_in.shape[1]
    sent_local = labels.shape[1]
    bucket_count = rel_table.shape[0]
    heads_half = rel_table.shape[1]
    masks = slot_masks(size)

    x_own = lax.dynamic_index_in_dim(tokens, mine, 0, keepdims=False)
    segments = lax.dynamic_index_in_dim(seg_ids, mine, 0, keepdims=False)[0]
    partner = lax.dynamic_index_in_dim(labels, mine, 0, keepdims=False)

    slot_block = jnp.stack([jnp.bitwise_xor(me, m) for m in masks]).astype(jnp.int32)
    source = (slot_block[:, None] * block + jnp.arange(block, dtype=jnp.int32)[None, :]).reshape(-1)
    order = (jnp.arange(width, dtype=jnp.int32)[:, None] == source[None, :]).astype(BF16)
    order = lax.optimization_barrier(order)
    inputs = dot(x_own, order)

    rel_all = jnp.concatenate([rel_table, over(rel_table)], axis=1).astype(F32)
    near_buckets = lax.slice_in_dim(buckets, seq - 1 - REACH, seq - 1 - REACH + WIN)
    onehot = (near_buckets[None, :] == jnp.arange(bucket_count, dtype=jnp.int32)[:, None]).astype(F32)
    onehot = lax.optimization_barrier(low(onehot))
    rel_window = dot(rel_all, onehot.astype(F32), ((0,), (0,)), HIGHEST).reshape(heads_half, 2, WIN)

    row_f32 = shape_of(F32, seq, width)
    row_low = shape_of(BF16, seq, width)
    column_f32 = shape_of(F32, seq, 1)
    gain_f32 = shape_of(F32, 1, width)
    heads = 3 * inner_half
    piece = hidden_half // 2
    halves = [(side, i * inner_half, inner_half) for side in range(2) for i in range(2)]

    def hidden_blocks(weights, first_col=0):
        return [(weights[side], first_col + col, n) for side, col, n in halves]

    def begin(first, early):
        inputs, rel_window, twice, windows, *_ = early
        qkv, normed1_low, inverse1, gains = qkv_call(inputs, first, inner_half)
        context, probs = attend_forward(qkv, twice, windows, rel_window)
        return qkv, normed1_low, inverse1, gains, context, probs

    def between(started, second, early):
        qkv, normed1_low, inverse1, gains, context, probs = started
        inputs = early[0]
        hidden1, inverse2, normed2_low = narrow(
            "attn_out",
            [(context, i * inner_half, second[i], piece, inner_half) for i in range(2)],
            (inputs, gains),
            (row_f32, column_f32, row_low),
            functools.partial(norm_body, 1),
        )
        act0, slope0 = wide("act0", normed2_low, hidden_blocks(second), (), gelu_both, 2)
        return normed1_low, inverse1, gains, qkv, context, probs, hidden1, inverse2, normed2_low, act0, slope0

    gains_col = jnp.pad(
        jnp.stack([gain_attn, gain_ffn, gain_final], axis=1), ((0, 0), (0, LANES - 3))
    )
    pool_half = w_pool.shape[1] // 2
    pool_own = lax.dynamic_slice_in_dim(w_pool, mine * pool_half, pool_half, axis=1)
    padded = jnp.pad(segments, (REACH, REACH), constant_values=-1)
    windows = jnp.stack([padded[at : at + WIN] for at in range(0, seq, QB)])
    twice = jnp.tile(segments.reshape(seq // QB, QB), (1, 2))
    local_ids = jnp.arange(sent_local, dtype=jnp.int32)
    column_id = (slot_block[:, None] * sent_local + local_ids[None, :]).reshape(1, -1)
    early = (
        inputs, rel_window, twice, windows, order, onehot, column_id, partner[None, :], segments[None, :]
    )
    if block % 16:
        back_shard = w_back.T
        start = columns(w_query, w_key, w_value, gains_col, w_in[:, :piece], w_out.T)
        later = columns(back_shard[:, :piece], pool_own, w_in[:, piece:], back_shard[:, piece:])
    else:
        start = pack(
            "pack_start",
            [(w, 0, inner_half, False) for w in (w_query, w_key, w_value)]
            + [(gains_col, 0, LANES, False), (w_in, 0, piece, False), (w_out, 0, inner_half, True)],
        )
        later = pack(
            "pack_later",
            [
                (w_back, 0, piece, True),
                (pool_own, 0, pool_half, False),
                (w_in, piece, piece, False),
                (w_back, piece, piece, True),
            ],
        )
    first, second, third, fourth, early, done = gather_weights(
        start,
        later,
        heads + LANES,
        piece + pool_half,
        early,
        begin,
        between,
    )
    inputs, rel_window, twice, windows, order, onehot, column_id, partner, seg_lane = early
    normed1_low, inverse1, gains, qkv, context, probs, hidden1, inverse2, normed2_low, act0, slope0 = done

    act1, slope1 = wide("act1", normed2_low, hidden_blocks(fourth), (), gelu_both, 2)
    pool_loads = [weight(side, piece, pool_half) for side in third]
    hidden2, inverse3, pooled_low, unit, unit_low, scale = narrow(
        "ffn_out",
        [(act0, i * piece, third[i], 0, piece) for i in range(2)]
        + [(act1, i * piece, fourth[i], piece, piece) for i in range(2)],
        (hidden1, gains, seg_lane, *pool_loads),
        (
            row_f32,
            column_f32,
            shape_of(BF16, sent_local, width),
            shape_of(F32, sent_local, width),
            shape_of(BF16, sent_local, width),
            shape_of(F32, sent_local, 1),
        ),
        tail_body,
        [pltpu.VMEM((seq, width), BF16)] * 2,
    )
    quarters = gather_dp(unit_low)

    total_sent = column_id.shape[1]
    sentence_loads = [part(seg_lane), *pool_loads, part(hidden2), part(inverse3), part(gains)]
    back_shapes = (row_f32, row_low, gain_f32)
    if total_sent <= 1024:
        loss_local, embed_low, d_hidden2, ffn_low, d_gain3 = head_call(
            quarters,
            unit,
            scale,
            partner,
            column_id,
            sentence_loads,
            (shape_of(F32, 1, 1), shape_of(BF16, sent_local, width), *back_shapes),
        )
    else:
        every = rows(*quarters)
        position = jnp.arange(total_sent, dtype=jnp.int32)
        sims = dot_nt(every, every) * SOFTMAX_TEMP
        sims = jnp.where(position[:, None] == position[None, :], NEG_FILL, sims)
        lse_row = jax.nn.logsumexp(sims, axis=0, keepdims=True)
        own_sims = sims[:sent_local]
        own_lse = jax.nn.logsumexp(own_sims, axis=1, keepdims=True)
        is_target = column_id == partner.reshape(-1, 1)
        target = jnp.sum(jnp.where(is_target, own_sims, 0.0), axis=-1, keepdims=True)
        loss_local = jnp.sum(own_lse - target)
        hit = is_target.astype(F32)
        d_rows = low(LOSS_SCALE * (jnp.exp(own_sims - own_lse) - hit))
        d_cols = low(LOSS_SCALE * (jnp.exp(own_sims - lse_row) - hit))
        d_unit = SOFTMAX_TEMP * (dot(d_rows, every) + dot(d_cols, every))
        embed_low = low(scale * (d_unit - unit * jnp.sum(d_unit * unit, axis=-1, keepdims=True)))
        d_hidden2, ffn_low, d_gain3 = sentence_call(embed_low, sentence_loads, back_shapes)

    half = width // 2
    quarter = width // 4

    (pool_sent,) = gradients("pool_sent", pooled_low, half, half, (embed_low,))
    pool_got, ffn_later = go((), (core, pool_sent), keep=(ffn_low,))
    back0_sent, back1_sent = gradients("back_sent", ffn_later, half, half, (act0, act1))
    back0_got, back1_got, ffn_later = go(
        (), (core, back0_sent), (core, back1_sent), keep=(ffn_later,)
    )
    pool_hi = product(pooled_low, quarter, half, embed_low, pool_got[quarter:])
    pool_lo = product(pooled_low, 0, quarter, embed_low, pool_got[:quarter])
    got_pool, ffn_later, pool_lo = go((), (cross, pool_hi), keep=(ffn_later, pool_lo))
    up0 = wide("up0", ffn_later, hidden_blocks(third), (slope0,), times_slope)

    back_hi = product(ffn_low, quarter, half, act0, back0_got[quarter:])
    back_lo = product(ffn_low, 0, quarter, act0, back0_got[:quarter])
    back_own = product(ffn_low, 0, half, act1[:, :piece], back1_got[:, :piece])
    back_oth = product(ffn_low, 0, half, act1[:, piece:], back1_got[:, piece:])
    pool_lo = add(pool_lo, got_pool)
    got_pool, got_lo, got_own, ffn_later, up0, pool_lo, back_lo, back_own = go(
        (),
        (over, pool_lo),
        (cross, back_hi),
        (over, back_oth),
        keep=(ffn_later, up0, pool_lo, back_lo, back_own),
    )
    up1 = wide("up1", ffn_later, hidden_blocks(fourth, piece), (slope1,), times_slope)
    in0_sent, in1_sent = gradients("in_sent", normed2_low, half, half, (up0, up1))
    in0_got, in1_got, up0, up1 = go((), (core, in0_sent), (core, in1_sent), keep=(up0, up1))
    attn_low, d_gain2, d_hidden1 = narrow(
        "ffn_in_back",
        [(up0, i * piece, second[i], 0, piece) for i in range(2)]
        + [(up1, i * piece, fourth[i], 0, piece) for i in range(2)],
        (hidden1, inverse2, gains, d_hidden2),
        (row_low, gain_f32, row_f32),
        functools.partial(back_body, 1),
    )
    d_context = wide("d_context", attn_low, [(second[side], piece, inner_half) for side in range(2)])

    back_lo = add(back_lo, got_lo)
    back_own = add(back_own, got_own)
    in_hi = product(normed2_low, quarter, half, up0, in0_got[quarter:])
    in_lo = product(normed2_low, 0, quarter, up0, in0_got[:quarter])
    in_own = product(normed2_low, 0, half, up1[:, :piece], in1_got[:, :piece])
    in_oth = product(normed2_low, 0, half, up1[:, piece:], in1_got[:, piece:])
    got_first, got_x, got_in_own, d_context, pool_lo, back_lo, back_own, in_lo, in_own = go(
        (got_pool, got_lo, got_own),
        (over, back_lo[:, piece:]),
        (cross, columns(back_own[quarter:], in_hi)),
        (over, in_oth),
        keep=(d_context, pool_lo, back_lo, back_own, in_lo, in_own),
        join=False,
    )
    d_qkv, d_bias = attend_backward(qkv, d_context, probs)
    query_both = 2 * inner_half
    late_sent = sent_columns("late_sent", half, ((attn_low, context), (normed1_low, d_qkv)))
    late_got, d_qkv_later = go((), (core, late_sent), keep=(d_qkv,), join=False)
    grad_slots, d_gain1 = narrow(
        "qkv_back",
        [(d_qkv_later, i * inner_half, first[i], 0, inner_half) for i in range(2)]
        + [(d_qkv_later, (1 + i) * query_both, first[i], inner_half, query_both) for i in range(2)],
        (inputs, inverse1, gains, d_hidden1),
        (row_low, gain_f32),
        functools.partial(back_body, 0),
    )

    table_row = 3 * (width // LANES) + 1
    table_rows = -(-2 * heads_half * bucket_count // LANES)
    small_rows = -(-(table_row + table_rows) // 8) * 8
    (flat,) = whole_call(
        functools.partial(small_kernel, heads_half),
        (d_gain1, d_gain2, d_gain3, order, d_bias.reshape(-1, WIN), onehot, loss_local.reshape(1, 1), mine.reshape(1, 1)),
        (shape_of(F32, small_rows, LANES),),
        (),
        "small",
    )
    (grad_own,) = whole_call(turn_kernel, (grad_slots, order), (row_low,), (), "turn")
    flat_got, flat = go((), (over, flat), keep=(flat,), join=False)
    got_first, got_x, got_in_own = lax.optimization_barrier((got_first, got_x, got_in_own))
    flat = flat + flat_got
    got_second, got_in_lo = got_x[:, :piece], got_x[:, piece:]

    far = rest_hops(size)
    back_all = columns(
        add(back_lo[:, :piece], got_first),
        add(back_own[:quarter], got_second),
        add(pool_lo[:, :pool_half], got_pool[:, pool_half:]),
        add(pool_lo[:, pool_half:], got_pool[:, :pool_half]),
    )
    back_rest, back_stay = rest_start(back_all)
    in_lo = add(in_lo, got_in_lo)
    in_own = add(in_own, got_in_own)
    out_got, qkv_got = late_got[:, :query_both], late_got[:, query_both:]
    out_hi = product(attn_low, quarter, half, context, out_got[quarter:])
    out_lo = product(attn_low, 0, quarter, context, out_got[:quarter])
    query_hi = product(normed1_low, quarter, half, d_qkv[:, :query_both], qkv_got[quarter:, :query_both])
    query_lo = product(normed1_low, 0, quarter, d_qkv[:, :query_both], qkv_got[:quarter, :query_both])
    kv_own = product(
        normed1_low, 0, half, d_qkv[:, query_both : 2 * query_both], qkv_got[:, query_both : 2 * query_both]
    )
    kv_oth = product(normed1_low, 0, half, d_qkv[:, 2 * query_both :], qkv_got[:, 2 * query_both :])
    rest_hop = [functools.partial(hop, mask=j * 4) for j in range(1, min(4, size // 4))]
    back_more, got_first, got_x, got_kv, flat_got, back_stay, in_lo, in_own, out_lo, query_lo, kv_own, flat = go(
        (grad_own,),
        (far[0], back_rest),
        (over, in_lo[:, piece:]),
        (cross, columns(in_own[quarter:], out_hi, query_hi)),
        (over, kv_oth),
        (core, flat),
        keep=(back_stay, in_lo, in_own, out_lo, query_lo, kv_own, flat),
    )
    flat = flat + flat_got
    got_second, got_out, got_query = got_x[:, :piece], got_x[:, piece:][:, :query_both], got_x[:, piece + query_both :]

    back_all = add(back_stay, back_more)
    back_rest, back_stay = rest_start(back_all)
    in_all = columns(add(in_lo[:, :piece], got_first), add(in_own[:quarter], got_second))
    in_rest, in_stay = rest_start(in_all)
    out_lo = add(out_lo, got_out)
    query_lo = add(query_lo, got_query)
    kv_own = add(kv_own, got_kv)
    back_more, in_more, got_first, got_second, grad_other, flat_got, back_stay, in_stay, out_lo, query_lo, kv_own, flat = go(
        (),
        (far[1], back_rest),
        (far[0], in_rest),
        (over, columns(out_lo[:, inner_half:], query_lo[:, inner_half:])),
        (cross, kv_own[quarter:]),
        (over, grad_own),
        (cross, flat),
        keep=(back_stay, in_stay, out_lo, query_lo, kv_own, flat),
        join=False,
    )
    back_more, in_more, got_first, got_second, flat_got = lax.optimization_barrier(
        (back_more, in_more, got_first, got_second, flat_got)
    )
    flat = flat + flat_got

    def finish(value):
        value = value.astype(F32)
        for send in far[2:]:
            value = sum_half(value, send)
        return value

    back_all = finish(back_stay.astype(F32) + back_more.astype(F32))
    grad_back = back_all[:, :hidden_half]
    grad_pool = back_all[:, hidden_half:]
    in_all = add(in_stay, in_more)
    in_rest, in_stay = rest_start(in_all)
    last = columns(
        add(out_lo[:, :inner_half], got_first[:, :inner_half]),
        add(query_lo[:, :inner_half], got_first[:, inner_half:]),
        add(kv_own[:quarter], got_second),
    )
    n_in, n_last = in_rest.shape[1], last.shape[1]
    if len(far) == 2:
        rest = last.shape[0] // 4
        flat_high = lax.optimization_barrier(low(flat))
        flat_pair = rows(flat_high, low(flat - flat_high.astype(F32)))
        got_one, got_two, got_three, in_stay, last_stay, flat = go(
            (),
            (rest_hop[0], columns(flat_pair, in_rest, last[rest : 2 * rest])),
            (rest_hop[1], columns(flat_pair, last[2 * rest : 3 * rest])),
            (rest_hop[2], columns(flat_pair, last[3 * rest :])),
            keep=(in_stay, last[:rest], flat),
            join=False,
        )
        got_one, got_two, got_three, grad_other = lax.optimization_barrier(
            (got_one, got_two, got_three, grad_other)
        )
        in_more = got_one[:, LANES : LANES + n_in]
        last_more = sum(
            got[:, begin:].astype(F32)
            for got, begin in ((got_one, LANES + n_in), (got_two, LANES), (got_three, LANES))
        )
        count = flat.shape[0]
        flat_got = [
            got[:count, :LANES].astype(F32) + got[count : 2 * count, :LANES].astype(F32)
            for got in (got_one, got_two, got_three)
        ]
    else:
        in_more, last_more, *flat_got = go(
            (),
            (far[1], in_rest),
            (far[0], last[last.shape[0] // 2 :]),
            *((how, flat) for how in rest_hop),
        )
        last = add(last[: last.shape[0] // 2], last_more)
        last_rest, last_stay = rest_start(last)
        last_more = far[1](last_rest)
    flat = flat + sum(flat_got)
    for send in far[:-2]:
        flat = flat + send(flat)
    grad_last = finish(last_stay.astype(F32) + last_more.astype(F32))
    grad_in = finish(in_stay.astype(F32) + in_more.astype(F32))
    grad_out = grad_last[:, :inner_half]
    grad_qkv = grad_last[:, inner_half:]
    grad_tokens = jnp.where(
        mine == 0, jnp.stack([grad_own, grad_other]), jnp.stack([grad_other, grad_own])
    )
    across = width // LANES
    gains_mine = lax.dynamic_slice_in_dim(flat[: 3 * across].reshape(3, width), me * block, block, axis=1)
    loss = flat[3 * across, 0] / (micro_count * sent_local * size)
    table_sum = flat[table_row : table_row + table_rows].reshape(-1, bucket_count)[: 2 * heads_half]
    table_mine = lax.dynamic_slice_in_dim(table_sum, mine * heads_half, heads_half, axis=0).T
    grad_pool = jnp.where(
        mine == 0, grad_pool, columns(grad_pool[:, pool_half:], grad_pool[:, :pool_half])
    )
    return (
        loss,
        grad_tokens,
        grad_qkv[:, :inner_half],
        grad_qkv[:, inner_half : 2 * inner_half],
        grad_qkv[:, 2 * inner_half :],
        grad_out.T,
        grad_in,
        grad_back.T,
        gains_mine[0],
        gains_mine[1],
        gains_mine[2],
        grad_pool,
        table_mine,
    )


def solution(mesh):
    placed = (
        P(None, "dp", None),
        P(None, "dp", None),
        P(),
        P(None, "dp"),
        P("dp", "mp"),
        P("dp", "mp"),
        P("dp", "mp"),
        P("mp", "dp"),
        P("dp", "mp"),
        P("mp", "dp"),
        P("dp"),
        P("dp"),
        P("dp"),
        P("dp", None),
        P(None, "mp"),
    )
    return jax.shard_map(
        shards,
        mesh=mesh,
        in_specs=placed,
        out_specs=(
            P(),
            P(None, "dp", None),
            P("dp", "mp"),
            P("dp", "mp"),
            P("dp", "mp"),
            P("mp", "dp"),
            P("dp", "mp"),
            P("mp", "dp"),
            P("dp"),
            P("dp"),
            P("dp"),
            P("dp", None),
            P(None, "mp"),
        ),
        check_vma=False,
    )
```

```python
import functools

import jax
import jax.numpy as jnp
from jax import lax
from jax.experimental import pallas as pl
from jax.experimental.pallas import tpu as pltpu
from jax.sharding import PartitionSpec as P

NEG_FILL = -1000000000.0
SCORE_SCALE = 0.125
SOFTMAX_TEMP = 50.0
LOSS_SCALE = 64.0
EPSILON = 1e-06
REACH = 32
QB = 64
WIN = QB + 2 * REACH
LANES = 128
GELU_A = 0.7978845608028654
GELU_B = 0.044715

BF16 = jnp.bfloat16
F32 = jnp.float32
HIGHEST = lax.Precision.HIGHEST


def dot(left, right, dims=((1,), (0,)), precision=None):
    return lax.dot_general(
        left, right, (dims, ((), ())), precision=precision, preferred_element_type=F32
    )


def dot_nt(left, right):
    return dot(left, right, ((1,), (1,)))


def dot_tn(left, right):
    return dot(left, right, ((0,), (0,)))


def rms_forward(value, gain):
    inverse = lax.rsqrt(jnp.mean(value * value, axis=-1, keepdims=True) + EPSILON)
    return (value * inverse * gain, inverse)


def cost(flops, bytes_accessed):
    return pl.CostEstimate(flops=0, bytes_accessed=0, transcendentals=0)


def params(mib=16):
    return pltpu.CompilerParams(vmem_limit_bytes=mib * 2**20)


def split_dot(left, right, dims=((1,), (0,))):
    high = right.astype(BF16)
    rest = (right - high.astype(F32)).astype(BF16)
    return dot(left, high, dims) + dot(left, rest, dims)


def stream_kernel(plan, operands, outs, body, *refs):
    sources, out_refs = refs[:operands], refs[operands : operands + outs]
    more = refs[operands + outs :]
    buffers, sem = more[: sum(len(load) > 1 for load in plan)], more[-1]
    more = more[len(buffers) : -1]
    copies, places, used = [], [], 0
    for load in plan:
        if len(load) == 1:
            which, _, _, col, width, _ = load[0]
            places.append(sources[which].at[:, pl.ds(col, width)])
            copies.append([])
            continue
        buffer = buffers[used]
        used += 1
        group = []
        for which, at, count, col, width, number in load:
            copy = pltpu.make_async_copy(
                sources[which].at[:, pl.ds(col, width)], buffer.at[pl.ds(at, count)], sem.at[number]
            )
            copy.start()
            group.append(copy)
        places.append(buffer)
        copies.append(group)
    ready = set()

    def get(i):
        if i not in ready:
            ready.add(i)
            for copy in copies[i]:
                copy.wait()
        return places[i]

    body(get, *out_refs, *more)


def stream(name, loads, out_shapes, body, scratch=(), mib=16):
    arrays, spaces = [], []

    def place(array, space):
        for i, known in enumerate(arrays):
            if known is array and spaces[i] is space:
                return i
        arrays.append(array)
        spaces.append(space)
        return len(arrays) - 1

    plan, buffers, number = [], [], 0
    for load in loads:
        steps, at = [], 0
        space = pltpu.VMEM if len(load) == 1 else pltpu.HBM
        for array, col, width in load:
            steps.append((place(array, space), at, array.shape[0], col, width, number))
            at += array.shape[0]
            number += 1
        plan.append(steps)
        if len(load) > 1:
            buffers.append(pltpu.VMEM((at, load[0][2]), load[0][0].dtype))
    return pl.pallas_call(
        functools.partial(stream_kernel, plan, len(arrays), len(out_shapes), body),
        out_shape=tuple(out_shapes),
        in_specs=[pl.BlockSpec(memory_space=space) for space in spaces],
        out_specs=tuple(pl.BlockSpec(memory_space=pltpu.VMEM) for _ in out_shapes),
        scratch_shapes=buffers + list(scratch) + [pltpu.SemaphoreType.DMA((number,))],
        compiler_params=params(mib),
        cost_estimate=cost(0, 0),
        name=name,
    )(*arrays)


def part(array, col=0, width=None):
    return [(array, col, array.shape[1] - col if width is None else width)]


def weight(pieces, col, width):
    return [(piece, col, width) for piece in pieces]


def wide(name, x, blocks, extras=(), body=None, outs=1):
    widths = [width for *_, width in blocks]
    loads = [part(x)]
    for i, block in enumerate(blocks):
        loads.append(weight(*block))
        for extra in extras:
            loads.append(part(extra, sum(widths[:i]), widths[i]))

    def run(get, *out_refs):
        at = 0
        per = 1 + len(extras)
        for i, width in enumerate(widths):
            first = 1 + i * per
            value = dot(get(0)[...], get(first)[...])
            got = [get(first + 1 + j)[...] for j in range(len(extras))]
            values = (value,) if body is None else body(value, *got)
            for ref, result in zip(out_refs, values):
                ref[:, at : at + width] = result.astype(BF16)
            at += width

    shape = shape_of(BF16, x.shape[0], sum(widths))
    result = stream(name, loads, (shape,) * outs, run)
    return result if outs > 1 else result[0]


def gelu_both(up):
    square = up * up
    bend = jnp.tanh(GELU_A * up * (1.0 + GELU_B * square))
    half_one = 0.5 + 0.5 * bend
    inner = GELU_A + (3.0 * GELU_A * GELU_B) * square
    return up * half_one, half_one + 0.5 * up * (1.0 - bend * bend) * inner


def times_slope(value, slope):
    return (value * slope.astype(F32),)


def narrow(name, work, extras, out_shapes, body, scratch=(), mib=16):
    loads = []
    for x, x_col, pieces, col, width in work:
        loads += [part(x, x_col, width), weight(pieces, col, width)]
    first = len(loads)
    loads += [extra if isinstance(extra, list) else part(extra) for extra in extras]

    def run(get, *refs):
        out_refs, more = refs[: len(out_shapes)], refs[len(out_shapes) :]
        acc = more[0]
        for j in range(len(work)):
            value = dot_nt(get(2 * j)[...], get(2 * j + 1)[...])
            acc[...] = value if j == 0 else acc[...] + value
        body(acc, *(get(first + i) for i in range(len(extras))), *out_refs, *more[1:])

    depth = sum(piece.shape[0] for piece in work[0][2])
    return stream(
        name, loads, out_shapes, run, [pltpu.VMEM((work[0][0].shape[0], depth), F32), *scratch], mib
    )


def gradients(name, left, first, count, rights, out_of=None):
    loads = [part(left, first, count)] + [part(right) for right in rights]

    def run(get, *refs):
        *out_refs, turned = refs
        turned[...] = get(0)[...].T
        for i, ref in enumerate(out_refs):
            ref[...] = dot(turned[...], get(1 + i)[...]).astype(BF16)

    shapes = [shape_of(BF16, count, right.shape[1]) for right in rights]
    return stream(name, loads, shapes, run, [pltpu.VMEM((count, left.shape[0]), BF16)])


def sent_columns(name, first, pairs):
    loads = [load for left, right in pairs for load in (part(left, first, first), part(right))]

    def run(get, out_ref, turned):
        at = 0
        for i, (_, right) in enumerate(pairs):
            turned[...] = get(2 * i)[...].T
            n = right.shape[1]
            out_ref[:, at : at + n] = dot(turned[...], get(2 * i + 1)[...]).astype(BF16)
            at += n

    shape = shape_of(BF16, first, sum(right.shape[1] for _, right in pairs))
    return stream(name, loads, (shape,), run, [pltpu.VMEM((first, pairs[0][0].shape[0]), BF16)])[0]


def stack_rows(pieces, widths):
    block = pieces[0].shape[0]
    cuts = [sum(widths[:i]) for i in range(len(widths))]
    if block % 16:
        whole = jnp.concatenate(pieces, axis=0)
        return [whole[:, at : at + width] for at, width in zip(cuts, widths)]

    def run(*refs):
        for i, ref in enumerate(refs[: len(pieces)]):
            for j, out in enumerate(refs[len(pieces) :]):
                out[i * block : (i + 1) * block] = ref[:, cuts[j] : cuts[j] + widths[j]]

    shapes = [shape_of(pieces[0].dtype, block * len(pieces), width) for width in widths]
    return whole_call(run, pieces, shapes, (), "stack_rows")


def qkv_call(inputs, first, n):
    blocks = [(side, i * n, n) for i in range(3) for side in first]
    loads = [part(inputs), weight(first[0], 3 * n, LANES)] + [weight(*block) for block in blocks]

    def run(get, qkv_ref, normed_ref, inverse_ref, gains_ref):
        value = get(0)[...]
        inverse = lax.rsqrt(jnp.mean(value * value, axis=1, keepdims=True) + EPSILON)
        inverse_ref[...] = inverse
        gains = get(1)[...].astype(F32).T[:8]
        gains_ref[...] = gains
        normed_ref[...] = (value * inverse * gains[0:1]).astype(BF16)
        for i in range(len(blocks)):
            qkv_ref[:, i * n : (i + 1) * n] = dot(normed_ref[...], get(2 + i)[...]).astype(BF16)

    seq, width = inputs.shape
    shapes = (
        shape_of(BF16, seq, 6 * n),
        shape_of(BF16, seq, width),
        shape_of(F32, seq, 1),
        shape_of(F32, 8, width),
    )
    return stream("qkv", loads, shapes, run)


def norm_body(row, acc, value_ref, gains_ref, hidden_ref, inverse_ref, normed_ref=None):
    hidden = value_ref[...] + acc[...]
    inverse = lax.rsqrt(jnp.mean(hidden * hidden, axis=1, keepdims=True) + EPSILON)
    hidden_ref[...] = hidden
    inverse_ref[...] = inverse
    if normed_ref is not None:
        normed_ref[...] = (hidden * inverse * gains_ref[row : row + 1, :]).astype(BF16)


def norm_back(value, inverse, gain, grad):
    scaled = grad * gain
    inner = jnp.mean(value * scaled, axis=1, keepdims=True)
    d_value = inverse * scaled - value * (inverse * inverse * inverse) * inner
    return d_value, jnp.sum(grad * value * inverse, axis=0, keepdims=True)


def back_body(row, acc, value_ref, inverse_ref, gains_ref, grad_ref, low_ref, gain_out, hidden_ref=None):
    d_value, d_gain = norm_back(
        value_ref[...], inverse_ref[...], gains_ref[row : row + 1, :], acc[...]
    )
    total = grad_ref[...] + d_value
    low_ref[...] = total.astype(BF16)
    gain_out[...] = d_gain
    if hidden_ref is not None:
        hidden_ref[...] = total


def turn_kernel(grad_ref, order_ref, out_ref):
    out_ref[...] = dot_nt(grad_ref[...], order_ref[...]).astype(BF16)


def small_kernel(heads_half, one_ref, two_ref, three_ref, order_ref, bias_ref, onehot_ref, loss_ref, mine_ref, out_ref):
    width = one_ref.shape[1]
    gains = jnp.concatenate([one_ref[...], two_ref[...], three_ref[...], jnp.zeros((5, width), F32)], axis=0)
    high = gains.astype(BF16)
    rest = (gains - high.astype(F32)).astype(BF16)
    gains = dot_nt(high, order_ref[...]) + dot_nt(rest, order_ref[...])
    out_ref[...] = jnp.zeros_like(out_ref)
    across = width // LANES
    for i in range(3):
        for j in range(across):
            at = i * across + j
            out_ref[at : at + 1, :] = gains[i : i + 1, j * LANES : (j + 1) * LANES]
    at = 3 * across
    lane = lax.broadcasted_iota(jnp.int32, (1, LANES), 1)
    out_ref[at : at + 1, :] = jnp.where(lane == 0, loss_ref[...], 0.0)
    bias = bias_ref[...]
    heads = 2 * heads_half
    row = lax.broadcasted_iota(jnp.int32, (LANES, bias.shape[0]), 0)
    column = lax.broadcasted_iota(jnp.int32, (LANES, bias.shape[0]), 1)
    source = row + jnp.where(mine_ref[...] == 0, 0, heads_half)
    source = jnp.where(source >= heads, source - heads, source)
    pick = jnp.where((column == 8 * (source // 2) + source % 2) & (row < heads), 1.0, 0.0)
    bias = split_dot(pick.astype(BF16), bias)
    high = bias.astype(BF16)
    rest = (bias - high.astype(F32)).astype(BF16)
    table = dot_nt(high, onehot_ref[...]) + dot_nt(rest, onehot_ref[...])
    count = table.shape[1]
    a_row = LANES // count
    for head in range(heads):
        place = head % a_row * count
        line = at + 1 + head // a_row
        out_ref[line : line + 1, place : place + count] = table[head : head + 1, :]


def member_of(seg_ref, sent_count):
    ids = lax.broadcasted_iota(jnp.int32, (sent_count, seg_ref.shape[1]), 0)
    hit = jnp.where(seg_ref[...] == ids, 1.0, 0.0)
    return hit.astype(BF16), jnp.sum(hit, axis=1, keepdims=True)


def tail_body(acc, value_ref, gains_ref, seg_ref, own_ref, other_ref, hidden_ref, inverse_ref, pooled_ref, unit_ref, low_ref, scale_ref, high, rest):
    hidden = value_ref[...] + acc[...]
    inverse = lax.rsqrt(jnp.mean(hidden * hidden, axis=1, keepdims=True) + EPSILON)
    hidden_ref[...] = hidden
    inverse_ref[...] = inverse
    final = hidden_ref[...] * inverse * gains_ref[2:3, :]
    high[...] = final.astype(BF16)
    rest[...] = (final - high[...].astype(F32)).astype(BF16)
    sents, count = member_of(seg_ref, pooled_ref.shape[0])
    pooled = ((dot(sents, high[...]) + dot(sents, rest[...])) / count).astype(BF16)
    pooled_ref[...] = pooled
    half = own_ref.shape[1]
    left = dot(pooled, own_ref[...])
    right = dot(pooled, other_ref[...])
    square = jnp.sum(left * left, axis=1, keepdims=True) + jnp.sum(right * right, axis=1, keepdims=True)
    scale = lax.rsqrt(square + EPSILON)
    scale_ref[...] = scale
    for at, value in ((0, left * scale), (half, right * scale)):
        unit_ref[:, at : at + half] = value
        low_ref[:, at : at + half] = value.astype(BF16)


def head_call(quarters, unit, scale, partner, column, sentence_loads, out_shapes):
    loads = [part(q) for q in (*quarters, unit, scale, partner, column)] + sentence_loads
    quarter = quarters[0].shape[0]
    total = 4 * quarter

    def run(get, loss_ref, embed_ref, *refs):
        *back_refs, every = refs
        for i in range(4):
            every[i * quarter : (i + 1) * quarter] = get(i)[...]
        unit, scale, partner, columns_id = (get(i)[...] for i in range(4, 8))
        partner = as_columns(
            jnp.concatenate([partner, jnp.zeros((1, LANES - partner.shape[1]), jnp.int32)], axis=1)
        )[: partner.shape[1], 0:1]
        own_count = unit.shape[0]
        sims = dot_nt(every[...], every[...]) * SOFTMAX_TEMP
        row = lax.broadcasted_iota(jnp.int32, (total, total), 0)
        column = lax.broadcasted_iota(jnp.int32, (total, total), 1)
        sims = jnp.where(row == column, NEG_FILL, sims)
        top = jnp.max(sims, axis=0, keepdims=True)
        lse_row = top + jnp.log(jnp.sum(jnp.exp(sims - top), axis=0, keepdims=True))
        own = sims[:own_count]
        own_top = jnp.max(own, axis=1, keepdims=True)
        own_lse = own_top + jnp.log(jnp.sum(jnp.exp(own - own_top), axis=1, keepdims=True))
        is_target = columns_id.astype(F32) == partner
        hit = jnp.where(is_target, 1.0, 0.0)
        target = jnp.sum(jnp.where(is_target, own, 0.0), axis=1, keepdims=True)
        loss_ref[...] = jnp.sum(own_lse - target, axis=0, keepdims=True)
        d_rows = (LOSS_SCALE * (jnp.exp(own - own_lse) - hit)).astype(BF16)
        d_cols = (LOSS_SCALE * (jnp.exp(own - lse_row) - hit)).astype(BF16)
        d_unit = SOFTMAX_TEMP * (dot(d_rows, every[...]) + dot(d_cols, every[...]))
        inner = jnp.sum(d_unit * unit, axis=1, keepdims=True)
        d_embed = (scale * (d_unit - unit * inner)).astype(BF16)
        embed_ref[...] = d_embed
        sentence_back(d_embed, [get(8 + i) for i in range(len(sentence_loads))], *back_refs)

    return stream("head", loads, out_shapes, run, [pltpu.VMEM((total, unit.shape[1]), BF16)])


def sentence_call(embed, sentence_loads, out_shapes):
    def run(get, *back_refs):
        sentence_back(get(0)[...], [get(1 + i) for i in range(len(sentence_loads))], *back_refs)

    return stream("sentence", [part(embed)] + sentence_loads, out_shapes, run)


def sentence_back(d_embed, sources, hidden_ref, low_ref, gain_out):
    seg_ref, own_ref, other_ref, value_ref, inverse_ref, gains_ref = sources
    half = own_ref.shape[1]
    d_pooled = dot_nt(d_embed[:, :half], own_ref[...]) + dot_nt(d_embed[:, half:], other_ref[...])
    sents, count = member_of(seg_ref, d_embed.shape[0])
    d_final = split_dot(sents, d_pooled / count, ((0,), (0,)))
    d_value, d_gain = norm_back(value_ref[...], inverse_ref[...], gains_ref[2:3, :], d_final)
    hidden_ref[...] = d_value
    low_ref[...] = d_value.astype(BF16)
    gain_out[...] = d_gain


def whole_call(body, args, out_shapes, scratch=(), name=None):
    return pl.pallas_call(
        body,
        out_shape=tuple(out_shapes),
        in_specs=[pl.BlockSpec(memory_space=pltpu.VMEM)] * len(args),
        out_specs=tuple(pl.BlockSpec(memory_space=pltpu.VMEM) for _ in out_shapes),
        scratch_shapes=scratch,
        compiler_params=params(),
        cost_estimate=cost(0, 0),
        name=name,
    )(*args)


def shape_of(kind, *dims):
    return jax.ShapeDtypeStruct(dims, kind)


def _stack_heads(part):
    lane = lax.broadcasted_iota(jnp.int32, part.shape, 1)
    zero = jnp.zeros_like(part)
    first = lane < LANES // 2
    return jnp.concatenate(
        [jnp.where(first, part, zero), jnp.where(first, zero, part)], axis=0
    )


def _unstack_heads(both):
    half = both.shape[0] // 2
    lane = lax.broadcasted_iota(jnp.int32, (half, LANES), 1)
    return jnp.where(lane < LANES // 2, both[:half], both[half:])


def _pad_keys(pad, ref):
    seq = ref.shape[0]
    pad[0:REACH] = jnp.zeros((REACH, LANES), pad.dtype)
    pad[REACH + seq :] = jnp.zeros((REACH, LANES), pad.dtype)
    pad[REACH : REACH + seq] = ref[...]


def _query_bits(shape):
    return lax.broadcasted_iota(jnp.int32, shape, 0) & (QB - 1)


def as_columns(values):
    count, length = values.shape
    side = max(LANES, length)
    square = jnp.concatenate([values.astype(F32), jnp.zeros((side - count, length), F32)], axis=0)
    return square.T


def attend_forward_kernel(
    q_ref, k_ref, v_ref, segq_ref, segk_ref, rel_ref, ctx_ref, probs_ref, kpad, vpad, mask, scores
):
    seq = q_ref.shape[0]
    blocks = seq // QB
    _pad_keys(kpad, k_ref)
    _pad_keys(vpad, v_ref)

    @pl.when(pl.program_id(0) == 0)
    def _():
        keys = as_columns(segk_ref[...])
        for b in range(blocks):
            same = keys[:, b : b + 1] == segq_ref[b : b + 1, :].astype(F32)
            mask[b] = jnp.where(same, 0.0, NEG_FILL)

    rel = rel_ref[0]
    row = lax.broadcasted_iota(jnp.int32, (2 * QB, WIN), 0)
    bias = jnp.where(row < QB, rel[0:1, :], rel[1:2, :])
    bits = _query_bits((2 * QB, WIN))
    step = 1
    while step < QB:
        bias = jnp.where((bits & step) != 0, pltpu.roll(bias, step, 1), bias)
        step *= 2
    bias = bias.T
    for b in range(blocks):
        query = _stack_heads(q_ref[b * QB : (b + 1) * QB] * jnp.asarray(SCORE_SCALE, BF16))
        scores[b] = dot_nt(kpad[b * QB : b * QB + WIN], query)
    values = scores[...] + bias[None] + mask[...]
    top = jnp.max(values, axis=1, keepdims=True)
    shifted = jnp.exp(values - top)
    total = jnp.sum(shifted, axis=1, keepdims=True)
    probs_ref[0] = (shifted * (1.0 / total)).astype(BF16)
    for b in range(blocks):
        part = dot_tn(probs_ref[0, b], vpad[b * QB : b * QB + WIN])
        ctx_ref[b * QB : (b + 1) * QB] = _unstack_heads(part).astype(BF16)


def attend_backward_kernel(
    q_ref, k_ref, v_ref, dctx_ref, probs_ref, dqkv_ref, dbias_ref,
    kpad, vpad, dk_acc, dv_acc, d_probs, d_low,
):
    seq = q_ref.shape[0]
    pair = pl.program_id(0)
    side = pl.num_programs(0) // 2
    later = pair // side
    q_at = pl.ds(pl.multiple_of(pair * LANES, LANES), LANES)
    k_at = pl.ds(pl.multiple_of((pair + 2 * side + later * side) * LANES, LANES), LANES)
    v_at = pl.ds(pl.multiple_of((pair + 3 * side + later * side) * LANES, LANES), LANES)
    blocks = seq // QB
    _pad_keys(kpad, k_ref)
    _pad_keys(vpad, v_ref)
    dk_acc[...] = jnp.zeros_like(dk_acc)
    dv_acc[...] = jnp.zeros_like(dv_acc)
    for b in range(blocks):
        window = slice(b * QB, b * QB + WIN)
        d_ctx = _stack_heads(dctx_ref[b * QB : (b + 1) * QB])
        d_probs[b] = dot_nt(vpad[window], d_ctx)
        dv_acc[window] += dot(probs_ref[0, b], d_ctx)
    probs = probs_ref[0].astype(F32)
    product = probs * d_probs[...]
    inner = jnp.sum(product, axis=1, keepdims=True)
    d_scores = product - probs * inner
    d_low[...] = d_scores.astype(BF16)
    total = jnp.sum(d_scores, axis=0).T
    for b in range(blocks):
        here = slice(b * QB, (b + 1) * QB)
        window = slice(b * QB, b * QB + WIN)
        query = _stack_heads(q_ref[here] * jnp.asarray(SCORE_SCALE, BF16))
        dk_acc[window] += dot(d_low[b], query)
        d_query = _unstack_heads(dot_tn(d_low[b], kpad[window])) * SCORE_SCALE
        dqkv_ref[here, q_at] = d_query.astype(BF16)
    dqkv_ref[:, k_at] = dk_acc[REACH : REACH + seq].astype(BF16)
    dqkv_ref[:, v_at] = dv_acc[REACH : REACH + seq].astype(BF16)
    bits = _query_bits((2 * QB, WIN))
    step = 1
    while step < QB:
        total = jnp.where((bits & step) != 0, pltpu.roll(total, WIN - step, 1), total)
        step *= 2
    first = jnp.sum(total[:QB], axis=0, keepdims=True)
    second = jnp.sum(total[QB:], axis=0, keepdims=True)
    dbias_ref[0] = jnp.concatenate([first, second, jnp.zeros((6, WIN), F32)], axis=0)


def _qkv_specs(seq, pairs):
    def spec(kind):
        return pl.BlockSpec((seq, LANES), lambda p: (0, kind * pairs + p))

    return [spec(0), spec(1), spec(2)]


def attend_forward(qkv, twice, windows, rel_window):
    seq = qkv.shape[0]
    pairs = rel_window.shape[0]
    blocks = seq // QB
    return pl.pallas_call(
        attend_forward_kernel,
        grid=(pairs,),
        out_shape=(
            jax.ShapeDtypeStruct((seq, pairs * LANES), BF16),
            jax.ShapeDtypeStruct((pairs, blocks, WIN, 2 * QB), BF16),
        ),
        in_specs=_qkv_specs(seq, pairs)
        + [
            pl.BlockSpec((blocks, 2 * QB), lambda p: (0, 0)),
            pl.BlockSpec((blocks, WIN), lambda p: (0, 0)),
            pl.BlockSpec((1, 2, WIN), lambda p: (p, 0, 0)),
        ],
        out_specs=(
            pl.BlockSpec((seq, LANES), lambda p: (0, p)),
            pl.BlockSpec((1, blocks, WIN, 2 * QB), lambda p: (p, 0, 0, 0)),
        ),
        scratch_shapes=[pltpu.VMEM((seq + 2 * REACH, LANES), BF16)] * 2
        + [pltpu.VMEM((blocks, WIN, 2 * QB), F32)] * 2,
        compiler_params=params(),
        cost_estimate=cost(8 * seq * WIN * LANES * pairs * 4, 8 * seq * LANES * pairs),
        name="attend_forward",
    )(qkv, qkv, qkv, twice, windows, rel_window)


def attend_backward(qkv, d_context, probs):
    seq = qkv.shape[0]
    pairs = probs.shape[0]
    blocks = seq // QB
    lane_block = pl.BlockSpec((seq, LANES), lambda p: (0, p))
    return pl.pallas_call(
        attend_backward_kernel,
        grid=(pairs,),
        out_shape=(
            jax.ShapeDtypeStruct((seq, 3 * pairs * LANES), BF16),
            jax.ShapeDtypeStruct((pairs, 8, WIN), F32),
        ),
        in_specs=_qkv_specs(seq, pairs)
        + [
            lane_block,
            pl.BlockSpec((1, blocks, WIN, 2 * QB), lambda p: (p, 0, 0, 0)),
        ],
        out_specs=(
            pl.BlockSpec((seq, 3 * pairs * LANES), lambda p: (0, 0)),
            pl.BlockSpec((1, 8, WIN), lambda p: (p, 0, 0)),
        ),
        scratch_shapes=[pltpu.VMEM((seq + 2 * REACH, LANES), BF16)] * 2
        + [pltpu.VMEM((seq + 2 * REACH, LANES), F32)] * 2
        + [pltpu.VMEM((blocks, WIN, 2 * QB), F32), pltpu.VMEM((blocks, WIN, 2 * QB), BF16)],
        compiler_params=params(),
        cost_estimate=cost(16 * seq * WIN * LANES * pairs * 4, 16 * seq * LANES * pairs),
        name="attend_backward",
    )(qkv, qkv, qkv, d_context, probs)


CORE = 1
CROSS = 2


def hop(value, mask):
    size = lax.axis_size("dp")
    return lax.ppermute(value, "dp", [(i, i ^ mask) for i in range(size)])


def over(value):
    return lax.ppermute(value, "mp", [(0, 1), (1, 0)])


def cross(value):
    return hop(value, CROSS)


def core(value):
    return hop(value, CORE)


def go(waits, *sends, keep=(), join=True):
    values = [value for _, value in sends]
    held = lax.optimization_barrier((*values, *keep, *waits))
    results = [how(value) for (how, _), value in zip(sends, held)]
    if join:
        results = list(lax.optimization_barrier(tuple(results)))
    return results + list(held[len(values) : len(values) + len(keep)])


def slot_masks(size):
    rest = size // 4
    return [z * 4 + x * 2 + c for c in range(2) for x in range(2) for z in range(rest)]


def strides(size):
    found = []
    stride = 4
    while stride < size:
        found.append(stride)
        stride *= 2
    return found


def gather_near(shard, waits, widths=None):
    size = lax.axis_size("dp")
    pieces = [shard]
    stride = 4
    while stride < size:
        radix = min(4, size // stride)
        shard = jnp.concatenate(pieces, axis=0) if len(pieces) > 1 else shard
        sends = [(functools.partial(hop, mask=j * stride), shard) for j in range(1, radix)]
        pieces = [shard] + go(waits, *sends)
        stride *= radix
    return jnp.concatenate(pieces, axis=0) if widths is None else stack_rows(pieces, widths)


def rows(*pieces):
    return jnp.concatenate(pieces, axis=0)


def columns(*pieces):
    return jnp.concatenate(pieces, axis=1)


def gather_weights(start, later, n_one, n_three, early, begin, between):
    size = lax.axis_size("dp")
    steps = strides(size)
    n_two = start.shape[1] - n_one
    if len(steps) == 2:
        got = go((), *((functools.partial(hop, mask=4 * j), start) for j in range(1, 4)))
        more = hop(later, 4)
        one, two = stack_rows([start, *got], (n_one, n_two))
        later = rows(later, more)
        wide_step = functools.partial(hop, mask=steps[1])
    else:
        one, two = gather_near(start, (), (n_one, n_two))

        def wide_step(value):
            whole = gather_near(value, ())
            return whole[value.shape[0] :]

    one_x, two_y, more, one_c, two_c = go(
        early, (cross, one), (over, two), (wide_step, later), (core, one), (core, two), join=False
    )
    one_x, two_y, one_c, two_c = lax.optimization_barrier((one_x, two_y, one_c, two_c))
    one_y, one_xy, two_x, two_yx = go(
        (),
        (over, one),
        (over, one_x),
        (cross, two),
        (cross, two_y),
        join=False,
    )
    one_y, one_xy, two_x, two_yx, more = lax.optimization_barrier((one_y, one_xy, two_x, two_yx, more))
    if later.shape[0] % 16 == 0:
        three, four = stack_rows((later, more), (n_three, later.shape[1] - n_three))
    else:
        later = rows(later, more)
        three, four = later[:, :n_three], later[:, n_three:]
    three_x, four_y, one_xc, one_yc, one_xyc, two_y, two_x, two_yx = go(
        (),
        (cross, three),
        (over, four),
        (core, one_x),
        (core, one_y),
        (core, one_xy),
        keep=(two_y, two_x, two_yx),
    )
    first = ((one, one_x, one_c, one_xc), (one_y, one_xy, one_yc, one_xyc))
    four_x, three_y, two_yc, two_xc, two_yxc, *kept = go(
        (three_x, four_y),
        (cross, four),
        (over, three),
        (core, two_y),
        (core, two_x),
        (core, two_yx),
        keep=(*first[0], *first[1], *early),
    )
    first = (tuple(kept[:4]), tuple(kept[4:8]))
    early = kept[8:]
    started = begin(first, early)
    second = ((two, two_x, two_c, two_xc), (two_y, two_yx, two_yc, two_yxc))
    four_yx, three_xy, four_c, four_yc, three_c, *kept = go(
        (four_x, three_y, two_yc, two_xc, two_yxc),
        (cross, four_y),
        (over, three_x),
        (core, four),
        (core, four_y),
        (core, three),
        keep=(*second[0], *second[1], *started),
    )
    second = (tuple(kept[:4]), tuple(kept[4:8]))
    done = between(kept[8:], second, early)
    four_xc, four_yxc, three_xc, three_yc, three_xyc, *done = go(
        (four_yx, three_xy, four_c, four_yc, three_c),
        (core, four_x),
        (core, four_yx),
        (core, three_x),
        (core, three_y),
        (core, three_xy),
        keep=done,
        join=False,
    )
    third = ((three, three_x, three_c, three_xc), (three_y, three_xy, three_yc, three_xyc))
    fourth = ((four, four_x, four_c, four_xc), (four_y, four_yx, four_yc, four_yxc))
    return first, second, third, fourth, early, done


def pack(name, sources):
    widths = [count for *_, count in sources]

    def run(get, out_ref):
        at = 0
        for i, width in enumerate(widths):
            out_ref[:, at : at + width] = get(i)[...]
            at += width

    shape = shape_of(BF16, sources[0][0].shape[0], sum(widths))
    return stream(name, [part(*source) for source in sources], (shape,), run)[0]


def gather_dp(shard):
    near = gather_near(shard, ())
    side, c_near = go((near,), (cross, near), (core, near))
    return near, side, c_near, core(side)


def low(value):
    return value.astype(BF16)


def add(left, right):
    return (left.astype(F32) + right.astype(F32)).astype(BF16)


def product(left, begin, end, right, got=None):
    value = dot_tn(left[:, begin:end], right)
    if got is not None:
        value = value + got.astype(F32)
    return low(value)


def rest_start(value):
    half = value.shape[0] // 2
    return value[half:], value[:half]


def sum_half(value, send):
    gone, stays = rest_start(value)
    return stays + send(low(gone)).astype(F32)


def rest_hops(size):
    return [functools.partial(hop, mask=stride) for stride in reversed(strides(size))]


def shards(
    tokens,
    seg_ids,
    buckets,
    labels,
    w_query,
    w_key,
    w_value,
    w_out,
    w_in,
    w_back,
    gain_attn,
    gain_ffn,
    gain_final,
    w_pool,
    rel_table,
):
    micro_count, seq, width = tokens.shape
    size = lax.axis_size("dp")
    me = lax.axis_index("dp")
    mine = lax.axis_index("mp")
    block = width // size
    inner_half = w_query.shape[1]
    hidden_half = w_in.shape[1]
    sent_local = labels.shape[1]
    bucket_count = rel_table.shape[0]
    heads_half = rel_table.shape[1]
    masks = slot_masks(size)

    x_own = lax.dynamic_index_in_dim(tokens, mine, 0, keepdims=False)
    segments = lax.dynamic_index_in_dim(seg_ids, mine, 0, keepdims=False)[0]
    partner = lax.dynamic_index_in_dim(labels, mine, 0, keepdims=False)

    slot_block = jnp.stack([jnp.bitwise_xor(me, m) for m in masks]).astype(jnp.int32)
    source = (slot_block[:, None] * block + jnp.arange(block, dtype=jnp.int32)[None, :]).reshape(-1)
    order = (jnp.arange(width, dtype=jnp.int32)[:, None] == source[None, :]).astype(BF16)
    order = lax.optimization_barrier(order)
    inputs = dot(x_own, order)


    row_f32 = shape_of(F32, seq, width)
    row_low = shape_of(BF16, seq, width)
    column_f32 = shape_of(F32, seq, 1)
    gain_f32 = shape_of(F32, 1, width)
    heads = 3 * inner_half
    piece = hidden_half // 2
    halves = [(side, i * inner_half, inner_half) for side in range(2) for i in range(2)]

    def hidden_blocks(weights, first_col=0):
        return [(weights[side], first_col + col, n) for side, col, n in halves]

    def begin(first, early):
        inputs, rel_window, twice, windows, *_ = early
        qkv, normed1_low, inverse1, gains = qkv_call(inputs, first, inner_half)
        context, probs = attend_forward(qkv, twice, windows, rel_window)
        return qkv, normed1_low, inverse1, gains, context, probs

    def between(started, second, early):
        qkv, normed1_low, inverse1, gains, context, probs = started
        inputs = early[0]
        hidden1, inverse2, normed2_low = narrow(
            "attn_out",
            [(context, i * inner_half, second[i], piece, inner_half) for i in range(2)],
            (inputs, gains),
            (row_f32, column_f32, row_low),
            functools.partial(norm_body, 1),
        )
        act0, slope0 = wide("act0", normed2_low, hidden_blocks(second), (), gelu_both, 2)
        return normed1_low, inverse1, gains, qkv, context, probs, hidden1, inverse2, normed2_low, act0, slope0

    gains_col = jnp.pad(
        jnp.stack([gain_attn, gain_ffn, gain_final], axis=1), ((0, 0), (0, LANES - 3))
    )
    pool_half = w_pool.shape[1] // 2
    pool_own = lax.dynamic_slice_in_dim(w_pool, mine * pool_half, pool_half, axis=1)
    back_shard = w_back.T
    if block % 16:
        start = columns(w_query, w_key, w_value, gains_col, w_in[:, :piece], w_out.T)
        later = columns(back_shard[:, :piece], pool_own, w_in[:, piece:], back_shard[:, piece:])
    else:
        start = pack(
            "pack_start",
            [(w, 0, inner_half) for w in (w_query, w_key, w_value)]
            + [(gains_col, 0, LANES), (w_in, 0, piece), (w_out.T, 0, inner_half)],
        )
        back_shard, w_in, _ = lax.optimization_barrier((back_shard, w_in, start))
        later = pack(
            "pack_later",
            [
                (back_shard, 0, piece),
                (pool_own, 0, pool_half),
                (w_in, piece, piece),
                (back_shard, piece, piece),
            ],
        )
    rel_other = over(lax.optimization_barrier((rel_table, start))[0])
    rel_all = jnp.concatenate([rel_table, rel_other], axis=1).astype(F32)
    near_buckets = lax.slice_in_dim(buckets, seq - 1 - REACH, seq - 1 - REACH + WIN)
    onehot = (near_buckets[None, :] == jnp.arange(bucket_count, dtype=jnp.int32)[:, None]).astype(F32)
    onehot = lax.optimization_barrier(low(onehot))
    rel_window = dot(rel_all, onehot.astype(F32), ((0,), (0,)), HIGHEST).reshape(heads_half, 2, WIN)
    padded = jnp.pad(segments, (REACH, REACH), constant_values=-1)
    windows = jnp.stack([padded[at : at + WIN] for at in range(0, seq, QB)])
    twice = jnp.tile(segments.reshape(seq // QB, QB), (1, 2))
    local_ids = jnp.arange(sent_local, dtype=jnp.int32)
    column_id = (slot_block[:, None] * sent_local + local_ids[None, :]).reshape(1, -1)
    early = (
        inputs, rel_window, twice, windows, order, onehot, column_id, partner[None, :], segments[None, :]
    )
    first, second, third, fourth, early, done = gather_weights(
        start,
        later,
        heads + LANES,
        piece + pool_half,
        early,
        begin,
        between,
    )
    inputs, rel_window, twice, windows, order, onehot, column_id, partner, seg_lane = early
    normed1_low, inverse1, gains, qkv, context, probs, hidden1, inverse2, normed2_low, act0, slope0 = done

    act1, slope1 = wide("act1", normed2_low, hidden_blocks(fourth), (), gelu_both, 2)
    pool_loads = [weight(side, piece, pool_half) for side in third]
    hidden2, inverse3, pooled_low, unit, unit_low, scale = narrow(
        "ffn_out",
        [(act0, i * piece, third[i], 0, piece) for i in range(2)]
        + [(act1, i * piece, fourth[i], piece, piece) for i in range(2)],
        (hidden1, gains, seg_lane, *pool_loads),
        (
            row_f32,
            column_f32,
            shape_of(BF16, sent_local, width),
            shape_of(F32, sent_local, width),
            shape_of(BF16, sent_local, width),
            shape_of(F32, sent_local, 1),
        ),
        tail_body,
        [pltpu.VMEM((seq, width), BF16)] * 2,
    )
    quarters = gather_dp(unit_low)

    total_sent = column_id.shape[1]
    sentence_loads = [part(seg_lane), *pool_loads, part(hidden2), part(inverse3), part(gains)]
    back_shapes = (row_f32, row_low, gain_f32)
    if total_sent <= 1024:
        loss_local, embed_low, d_hidden2, ffn_low, d_gain3 = head_call(
            quarters,
            unit,
            scale,
            partner,
            column_id,
            sentence_loads,
            (shape_of(F32, 1, 1), shape_of(BF16, sent_local, width), *back_shapes),
        )
    else:
        every = rows(*quarters)
        position = jnp.arange(total_sent, dtype=jnp.int32)
        sims = dot_nt(every, every) * SOFTMAX_TEMP
        sims = jnp.where(position[:, None] == position[None, :], NEG_FILL, sims)
        lse_row = jax.nn.logsumexp(sims, axis=0, keepdims=True)
        own_sims = sims[:sent_local]
        own_lse = jax.nn.logsumexp(own_sims, axis=1, keepdims=True)
        is_target = column_id == partner.reshape(-1, 1)
        target = jnp.sum(jnp.where(is_target, own_sims, 0.0), axis=-1, keepdims=True)
        loss_local = jnp.sum(own_lse - target)
        hit = is_target.astype(F32)
        d_rows = low(LOSS_SCALE * (jnp.exp(own_sims - own_lse) - hit))
        d_cols = low(LOSS_SCALE * (jnp.exp(own_sims - lse_row) - hit))
        d_unit = SOFTMAX_TEMP * (dot(d_rows, every) + dot(d_cols, every))
        embed_low = low(scale * (d_unit - unit * jnp.sum(d_unit * unit, axis=-1, keepdims=True)))
        d_hidden2, ffn_low, d_gain3 = sentence_call(embed_low, sentence_loads, back_shapes)

    half = width // 2
    quarter = width // 4

    (pool_sent,) = gradients("pool_sent", pooled_low, half, half, (embed_low,))
    pool_got, ffn_later = go((), (core, pool_sent), keep=(ffn_low,))
    back0_sent, back1_sent = gradients("back_sent", ffn_later, half, half, (act0, act1))
    back0_got, back1_got, ffn_later = go(
        (), (core, back0_sent), (core, back1_sent), keep=(ffn_later,)
    )
    pool_hi = product(pooled_low, quarter, half, embed_low, pool_got[quarter:])
    pool_lo = product(pooled_low, 0, quarter, embed_low, pool_got[:quarter])
    got_pool, ffn_later = go((), (cross, pool_hi), keep=(ffn_later,))
    up0 = wide("up0", ffn_later, hidden_blocks(third), (slope0,), times_slope)

    back_hi = product(ffn_low, quarter, half, act0, back0_got[quarter:])
    back_lo = product(ffn_low, 0, quarter, act0, back0_got[:quarter])
    back_own = product(ffn_low, 0, half, act1[:, :piece], back1_got[:, :piece])
    back_oth = product(ffn_low, 0, half, act1[:, piece:], back1_got[:, piece:])
    got_lo, got_own, ffn_later, up0, back_lo, back_own = go(
        (got_pool,), (cross, back_hi), (over, back_oth), keep=(ffn_later, up0, back_lo, back_own)
    )
    up1 = wide("up1", ffn_later, hidden_blocks(fourth, piece), (slope1,), times_slope)
    in0_sent, in1_sent = gradients("in_sent", normed2_low, half, half, (up0, up1))
    in0_got, in1_got, up0, up1 = go((), (core, in0_sent), (core, in1_sent), keep=(up0, up1))
    attn_low, d_gain2, d_hidden1 = narrow(
        "ffn_in_back",
        [(up0, i * piece, second[i], 0, piece) for i in range(2)]
        + [(up1, i * piece, fourth[i], 0, piece) for i in range(2)],
        (hidden1, inverse2, gains, d_hidden2),
        (row_low, gain_f32, row_f32),
        functools.partial(back_body, 1),
    )
    d_context = wide("d_context", attn_low, [(second[side], piece, inner_half) for side in range(2)])

    pool_lo = add(pool_lo, got_pool)
    back_lo = add(back_lo, got_lo)
    back_own = add(back_own, got_own)
    in_hi = product(normed2_low, quarter, half, up0, in0_got[quarter:])
    in_lo = product(normed2_low, 0, quarter, up0, in0_got[:quarter])
    in_own = product(normed2_low, 0, half, up1[:, :piece], in1_got[:, :piece])
    in_oth = product(normed2_low, 0, half, up1[:, piece:], in1_got[:, piece:])
    got_first, got_x, got_in_own, d_context, pool_lo, back_lo, back_own, in_lo, in_own = go(
        (got_lo, got_own),
        (over, columns(back_lo[:, piece:], pool_lo[:, pool_half:])),
        (cross, columns(back_own[quarter:], in_hi)),
        (over, in_oth),
        keep=(d_context, pool_lo, back_lo, back_own, in_lo, in_own),
        join=False,
    )
    d_qkv, d_bias = attend_backward(qkv, d_context, probs)
    query_both = 2 * inner_half
    late_sent = sent_columns("late_sent", half, ((attn_low, context), (normed1_low, d_qkv)))
    late_got, d_qkv_later = go((), (core, late_sent), keep=(d_qkv,), join=False)
    grad_slots, d_gain1 = narrow(
        "qkv_back",
        [(d_qkv_later, i * inner_half, first[i], 0, inner_half) for i in range(2)]
        + [(d_qkv_later, (1 + i) * query_both, first[i], inner_half, query_both) for i in range(2)],
        (inputs, inverse1, gains, d_hidden1),
        (row_low, gain_f32),
        functools.partial(back_body, 0),
    )

    table_row = 3 * (width // LANES) + 1
    table_rows = -(-2 * heads_half * bucket_count // LANES)
    small_rows = -(-(table_row + table_rows) // 8) * 8
    (flat,) = whole_call(
        functools.partial(small_kernel, heads_half),
        (d_gain1, d_gain2, d_gain3, order, d_bias.reshape(-1, WIN), onehot, loss_local.reshape(1, 1), mine.reshape(1, 1)),
        (shape_of(F32, small_rows, LANES),),
        (),
        "small",
    )
    (grad_own,) = whole_call(turn_kernel, (grad_slots, order), (row_low,), (), "turn")
    flat_got, flat = go((), (over, flat), keep=(flat,), join=False)
    got_first, got_x, got_in_own = lax.optimization_barrier((got_first, got_x, got_in_own))
    flat = flat + flat_got
    got_second, got_in_lo = got_x[:, :piece], got_x[:, piece:]

    far = rest_hops(size)
    back_all = columns(
        add(back_lo[:, :piece], got_first[:, :piece]),
        add(back_own[:quarter], got_second),
        add(pool_lo[:, :pool_half], got_first[:, piece:]),
    )
    back_rest, back_stay = rest_start(back_all)
    in_lo = add(in_lo, got_in_lo)
    in_own = add(in_own, got_in_own)
    out_got, qkv_got = late_got[:, :query_both], late_got[:, query_both:]
    out_hi = product(attn_low, quarter, half, context, out_got[quarter:])
    out_lo = product(attn_low, 0, quarter, context, out_got[:quarter])
    query_hi = product(normed1_low, quarter, half, d_qkv[:, :query_both], qkv_got[quarter:, :query_both])
    query_lo = product(normed1_low, 0, quarter, d_qkv[:, :query_both], qkv_got[:quarter, :query_both])
    kv_own = product(
        normed1_low, 0, half, d_qkv[:, query_both : 2 * query_both], qkv_got[:, query_both : 2 * query_both]
    )
    kv_oth = product(normed1_low, 0, half, d_qkv[:, 2 * query_both :], qkv_got[:, 2 * query_both :])
    rest_hop = [functools.partial(hop, mask=j * 4) for j in range(1, min(4, size // 4))]
    back_more, got_first, got_x, got_kv, flat_got, back_stay, in_lo, in_own, out_lo, query_lo, kv_own, flat = go(
        (grad_own,),
        (far[0], back_rest),
        (over, in_lo[:, piece:]),
        (cross, columns(in_own[quarter:], out_hi, query_hi)),
        (over, kv_oth),
        (core, flat),
        keep=(back_stay, in_lo, in_own, out_lo, query_lo, kv_own, flat),
    )

    count = flat.shape[0]

    def in_two(value):
        high = value.astype(BF16).astype(F32)
        return jnp.concatenate([high, value - high], axis=0).astype(BF16)

    def from_two(pair):
        return pair[:count].astype(F32) + pair[count : 2 * count].astype(F32)

    def late_adds(
        stay, more, in_lo, got_first, in_own, got_x, out_lo, query_lo, kv_own, got_kv, flat, got_flat, *outs
    ):
        back_gone, back_keep, in_gone, in_keep, heads_gone, heads_keep, kv_gone, kv_keep, small = outs
        rows_z = stay.shape[0] // 2
        total = add(stay[...], more[...])
        back_keep[...] = total[:rows_z]
        back_gone[...] = total[rows_z:]
        rows_z = in_lo.shape[0] // 2
        for at, total in (
            (0, add(in_lo[:, :piece], got_first[...])),
            (piece, add(in_own[:quarter], got_x[:, :piece])),
        ):
            in_keep[:, at : at + piece] = total[:rows_z]
            in_gone[:, at : at + piece] = total[rows_z:]
        for i, ref in enumerate((out_lo, query_lo)):
            first_col = piece + i * query_both
            total = add(ref[...], got_x[:, first_col : first_col + query_both])
            heads_keep[:, i * inner_half : (i + 1) * inner_half] = total[:, :inner_half]
            heads_gone[:, i * inner_half : (i + 1) * inner_half] = total[:, inner_half:]
        kv_keep[...] = add(kv_own[:quarter], got_kv[:quarter])
        kv_gone[:, :query_both] = add(kv_own[quarter:], got_kv[quarter:])
        small[...] = flat[...] + got_flat[...]
        kv_gone[:, query_both:] = jnp.zeros((quarter, LANES), BF16)
        pair = in_two(small[...])
        kv_gone[: 2 * count, query_both:] = pair
        small[...] = from_two(pair)

    cut = [shape_of(BF16, back_stay.shape[0] // 2, back_stay.shape[1])] * 2
    cut += [shape_of(BF16, quarter // 2, hidden_half)] * 2 + [shape_of(BF16, quarter, query_both)] * 2
    cut += [
        shape_of(BF16, quarter, query_both + LANES),
        shape_of(BF16, quarter, query_both),
        shape_of(F32, count, LANES),
    ]
    back_rest, back_stay, in_rest, in_stay, heads_gone, heads_keep, kv_gone, kv_keep, flat = whole_call(
        late_adds,
        (back_stay, back_more, in_lo, got_first, in_own, got_x, out_lo, query_lo, kv_own, got_kv, flat, flat_got),
        cut,
        (),
        "late_adds",
    )
    half_seq = seq // 2
    back_more, in_more, got_first, got_second, grad_other, back_stay, in_stay, heads_keep, kv_keep, flat = go(
        (),
        (far[1], back_rest),
        (far[0], in_rest),
        (over, heads_gone),
        (cross, kv_gone),
        (over, grad_own[:half_seq]),
        keep=(back_stay, in_stay, heads_keep, kv_keep, flat),
    )

    def finish(value):
        value = value.astype(F32)
        for send in far[2:]:
            value = sum_half(value, send)
        return value

    n_last = query_both + query_both
    if len(far) == 2:
        rest = block

        def last_adds(stay, more, heads_ref, got_heads, kv_ref, got_kv, flat_ref, back_ref, back_got, own_ref, *outs):
            one, two, three, in_keep, keep, flat_out, tail, pool_ref = outs
            pool = add(back_ref[:, hidden_half:], back_got[:, hidden_half:])
            pool_ref[...] = pool
            tail[:half_seq] = own_ref[half_seq:]
            tail[half_seq:, :pool_half] = pool
            tail[half_seq:, pool_half:] = jnp.zeros((rest, width - pool_half), BF16)
            total = add(stay[...], more[...])
            in_keep[...] = total[:rest]
            one[:, LANES : LANES + hidden_half] = total[rest:]
            pair = in_two(flat_ref[...] + from_two(got_kv[:, query_both:]))
            flat_out[...] = from_two(pair)
            for i, (ref, at) in enumerate(((keep, 0), (one, LANES + hidden_half), (two, LANES), (three, LANES))):
                here = slice(i * rest, (i + 1) * rest)
                if i:
                    ref[:, :LANES] = pair
                ref[:, at : at + query_both] = add(heads_ref[here], got_heads[here])
                ref[:, at + query_both : at + n_last] = add(kv_ref[here], got_kv[here, :query_both])

        one, two, three, in_stay, last_stay, flat, tail, grad_pool = whole_call(
            last_adds,
            (in_stay, in_more, heads_keep, got_first, kv_keep, got_second, flat, back_stay, back_more, grad_own),
            (
                shape_of(BF16, rest, LANES + hidden_half + n_last),
                shape_of(BF16, rest, LANES + n_last),
                shape_of(BF16, rest, LANES + n_last),
                shape_of(BF16, rest, hidden_half),
                shape_of(BF16, rest, n_last),
                shape_of(F32, count, LANES),
                shape_of(BF16, half_seq + rest, width),
                shape_of(BF16, rest, pool_half),
            ),
            (),
            "last_adds",
        )
        got_one, got_two, got_three, got_tail, back_stay, back_more = go(
            (),
            (rest_hop[0], one),
            (rest_hop[1], two),
            (rest_hop[2], three),
            (over, tail),
            keep=(back_stay, back_more),
            join=False,
        )

        def back_final(stay, more, back_ref):
            back_ref[...] = stay[:, :hidden_half].astype(F32) + more[:, :hidden_half].astype(F32)

        (grad_back,) = whole_call(
            back_final, (back_stay, back_more), (shape_of(F32, rest, hidden_half),), (), "back_final"
        )

        def tokens_final(mine_ref, own_ref, first_ref, tail_ref, pool_own, out_ref, pool_ref):
            first = mine_ref[...] == 0
            own, other = pool_own[...].astype(F32), tail_ref[half_seq:, :pool_half].astype(F32)
            pool_ref[:, :pool_half] = jnp.where(first, own, other)
            pool_ref[:, pool_half:] = jnp.where(first, other, own)
            for at, ref in ((0, first_ref), (half_seq, tail_ref)):
                here = slice(at, at + half_seq)
                own, other = own_ref[here].astype(F32), ref[:half_seq].astype(F32)
                out_ref[0, here] = jnp.where(first, own, other).astype(BF16)
                out_ref[1, here] = jnp.where(first, other, own).astype(BF16)

        grad_tokens, grad_pool = whole_call(
            tokens_final,
            (mine.reshape(1, 1), grad_own, grad_other, got_tail, grad_pool),
            (shape_of(BF16, 2, seq, width), shape_of(F32, rest, 2 * pool_half)),
            (),
            "tokens_final",
        )
        got_one, got_two, got_three, grad_tokens = lax.optimization_barrier(
            (got_one, got_two, got_three, grad_tokens)
        )

        def last_final(stay, in_keep, one_ref, two_ref, three_ref, flat_ref, *outs):
            in_ref, out_ref, q_ref, k_ref, v_ref, flat_out = outs
            in_ref[...] = in_keep[...].astype(F32) + one_ref[:, LANES : LANES + hidden_half].astype(F32)
            total = stay[...].astype(F32) + one_ref[:, LANES + hidden_half :].astype(F32)
            total = total + two_ref[:, LANES:].astype(F32) + three_ref[:, LANES:].astype(F32)
            for i, ref in enumerate((out_ref, q_ref, k_ref, v_ref)):
                ref[...] = total[:, i * inner_half : (i + 1) * inner_half]
            small = flat_ref[...]
            for ref in (one_ref, two_ref, three_ref):
                small = small + from_two(ref[:, :LANES])
            flat_out[...] = small

        head_shape = shape_of(F32, rest, inner_half)
        grad_in, grad_out, grad_query, grad_key, grad_value, flat = whole_call(
            last_final,
            (last_stay, in_stay, got_one, got_two, got_three, flat),
            (shape_of(F32, rest, hidden_half), *(head_shape,) * 4, shape_of(F32, count, LANES)),
            (),
            "last_final",
        )
    else:
        flat = flat + from_two(got_second[:, query_both:])
        grad_other = rows(grad_other, over(grad_own[half_seq:]))
        in_rest, in_stay = rest_start(add(in_stay, in_more))
        last = columns(add(heads_keep, got_first), add(kv_keep, got_second[:, :query_both]))
        last_rest, last_stay = rest_start(last)
        in_more, last_more, *flat_got = go(
            (), (far[1], in_rest), (far[0], last_rest), *((how, flat) for how in rest_hop)
        )
        last_rest, last_stay = rest_start(add(last_stay, last_more))
        last_more = far[1](last_rest)
        flat = flat + sum(flat_got)
        for send in far[:-2]:
            flat = flat + send(flat)
        grad_last = finish(last_stay.astype(F32) + last_more.astype(F32))
        grad_in = finish(in_stay.astype(F32) + in_more.astype(F32))
        back_all = finish(back_stay.astype(F32) + back_more.astype(F32))
        grad_back, grad_pool = back_all[:, :hidden_half], back_all[:, hidden_half:]
        pool_other = over(grad_pool)
        grad_pool = jnp.where(mine == 0, columns(grad_pool, pool_other), columns(pool_other, grad_pool))
        grad_out, grad_query, grad_key, grad_value = (
            grad_last[:, i * inner_half : (i + 1) * inner_half] for i in range(4)
        )
        grad_tokens = jnp.where(
            mine == 0, jnp.stack([grad_own, grad_other]), jnp.stack([grad_other, grad_own])
        )
    across = width // LANES
    gains_mine = lax.dynamic_slice_in_dim(flat[: 3 * across].reshape(3, width), me * block, block, axis=1)
    loss = flat[3 * across, 0] / (micro_count * sent_local * size)
    table_sum = flat[table_row : table_row + table_rows].reshape(-1, bucket_count)[: 2 * heads_half]
    table_mine = lax.dynamic_slice_in_dim(table_sum, mine * heads_half, heads_half, axis=0).T
    return (
        loss,
        grad_tokens,
        grad_query,
        grad_key,
        grad_value,
        grad_out.T,
        grad_in,
        grad_back.T,
        gains_mine[0],
        gains_mine[1],
        gains_mine[2],
        grad_pool,
        table_mine,
    )


def solution(mesh):
    placed = (
        P(None, "dp", None),
        P(None, "dp", None),
        P(),
        P(None, "dp"),
        P("dp", "mp"),
        P("dp", "mp"),
        P("dp", "mp"),
        P("mp", "dp"),
        P("dp", "mp"),
        P("mp", "dp"),
        P("dp"),
        P("dp"),
        P("dp"),
        P("dp", None),
        P(None, "mp"),
    )
    return jax.shard_map(
        shards,
        mesh=mesh,
        in_specs=placed,
        out_specs=(
            P(),
            P(None, "dp", None),
            P("dp", "mp"),
            P("dp", "mp"),
            P("dp", "mp"),
            P("mp", "dp"),
            P("dp", "mp"),
            P("mp", "dp"),
            P("dp"),
            P("dp"),
            P("dp"),
            P("dp", None),
            P(None, "mp"),
        ),
        check_vma=False,
    )
```

```python
import functools

import jax
import jax.numpy as jnp
from jax import lax
from jax.experimental import pallas as pl
from jax.experimental.pallas import tpu as pltpu
from jax.sharding import PartitionSpec as P

NEG_FILL = -1000000000.0
SCORE_SCALE = 0.125
SOFTMAX_TEMP = 50.0
LOSS_SCALE = 64.0
EPSILON = 1e-06
REACH = 32
QB = 64
WIN = QB + 2 * REACH
LANES = 128
GELU_A = 0.7978845608028654
GELU_B = 0.044715

BF16 = jnp.bfloat16
F32 = jnp.float32
HIGHEST = lax.Precision.HIGHEST


def dot(left, right, dims=((1,), (0,)), precision=None):
    return lax.dot_general(
        left, right, (dims, ((), ())), precision=precision, preferred_element_type=F32
    )


def dot_nt(left, right):
    return dot(left, right, ((1,), (1,)))


def dot_tn(left, right):
    return dot(left, right, ((0,), (0,)))


def rms_forward(value, gain):
    inverse = lax.rsqrt(jnp.mean(value * value, axis=-1, keepdims=True) + EPSILON)
    return (value * inverse * gain, inverse)


def cost(flops, bytes_accessed):
    return pl.CostEstimate(flops=0, bytes_accessed=0, transcendentals=0)


def params(mib=16):
    return pltpu.CompilerParams(vmem_limit_bytes=mib * 2**20)


def split_dot(left, right, dims=((1,), (0,))):
    high = right.astype(BF16)
    rest = (right - high.astype(F32)).astype(BF16)
    return dot(left, high, dims) + dot(left, rest, dims)


def stream_kernel(plan, operands, outs, body, *refs):
    sources, out_refs = refs[:operands], refs[operands : operands + outs]
    more = refs[operands + outs :]
    buffers, sem = more[: sum(len(load) > 1 for load in plan)], more[-1]
    more = more[len(buffers) : -1]
    copies, places, used = [], [], 0
    for load in plan:
        if len(load) == 1:
            which, _, row, count, col, width, _ = load[0]
            places.append(sources[which].at[pl.ds(row, count), pl.ds(col, width)])
            copies.append([])
            continue
        buffer = buffers[used]
        used += 1
        group = []
        for which, at, row, count, col, width, number in load:
            copy = pltpu.make_async_copy(
                sources[which].at[pl.ds(row, count), pl.ds(col, width)],
                buffer.at[pl.ds(at, count)],
                sem.at[number],
            )
            copy.start()
            group.append(copy)
        places.append(buffer)
        copies.append(group)
    ready = set()

    def get(i):
        if i not in ready:
            ready.add(i)
            for copy in copies[i]:
                copy.wait()
        return places[i]

    body(get, *out_refs, *more)


def stream(name, loads, out_shapes, body, scratch=(), mib=16):
    arrays, spaces = [], []

    def place(array, space):
        for i, known in enumerate(arrays):
            if known is array and spaces[i] is space:
                return i
        arrays.append(array)
        spaces.append(space)
        return len(arrays) - 1

    plan, buffers, number = [], [], 0
    for load in loads:
        steps, at = [], 0
        space = pltpu.VMEM if len(load) == 1 else pltpu.HBM
        for array, row, count, col, width in load:
            steps.append((place(array, space), at, row, count, col, width, number))
            at += count
            number += 1
        plan.append(steps)
        if len(load) > 1:
            buffers.append(pltpu.VMEM((at, load[0][4]), load[0][0].dtype))
    return pl.pallas_call(
        functools.partial(stream_kernel, plan, len(arrays), len(out_shapes), body),
        out_shape=tuple(out_shapes),
        in_specs=[pl.BlockSpec(memory_space=space) for space in spaces],
        out_specs=tuple(pl.BlockSpec(memory_space=pltpu.VMEM) for _ in out_shapes),
        scratch_shapes=buffers + list(scratch) + [pltpu.SemaphoreType.DMA((number,))],
        compiler_params=params(mib),
        cost_estimate=cost(0, 0),
        name=name,
    )(*arrays)


def part(array, col=0, width=None):
    return [(array, 0, array.shape[0], col, array.shape[1] - col if width is None else width)]


def weight(pieces, col, width):
    return [(*piece, col, width) for piece in pieces]


def wide(name, x, blocks, extras=(), body=None, outs=1):
    widths = [width for *_, width in blocks]
    loads = [part(x)]
    for i, block in enumerate(blocks):
        loads.append(weight(*block))
        for extra in extras:
            loads.append(part(extra, sum(widths[:i]), widths[i]))

    def run(get, *out_refs):
        at = 0
        per = 1 + len(extras)
        for i, width in enumerate(widths):
            first = 1 + i * per
            value = dot(get(0)[...], get(first)[...])
            got = [get(first + 1 + j)[...] for j in range(len(extras))]
            values = (value,) if body is None else body(value, *got)
            for ref, result in zip(out_refs, values):
                ref[:, at : at + width] = result.astype(BF16)
            at += width

    shape = shape_of(BF16, x.shape[0], sum(widths))
    result = stream(name, loads, (shape,) * outs, run)
    return result if outs > 1 else result[0]


def gelu_both(up):
    square = up * up
    bend = jnp.tanh(GELU_A * up * (1.0 + GELU_B * square))
    half_one = 0.5 + 0.5 * bend
    inner = GELU_A + (3.0 * GELU_A * GELU_B) * square
    return up * half_one, half_one + 0.5 * up * (1.0 - bend * bend) * inner


def times_slope(value, slope):
    return (value * slope.astype(F32),)


def narrow(name, work, extras, out_shapes, body, scratch=(), mib=16):
    loads = []
    for x, x_col, pieces, col, width in work:
        loads += [part(x, x_col, width), weight(pieces, col, width)]
    first = len(loads)
    loads += [extra if isinstance(extra, list) else part(extra) for extra in extras]

    def run(get, *refs):
        out_refs, more = refs[: len(out_shapes)], refs[len(out_shapes) :]
        acc = more[0]
        for j in range(len(work)):
            value = dot_nt(get(2 * j)[...], get(2 * j + 1)[...])
            acc[...] = value if j == 0 else acc[...] + value
        body(acc, *(get(first + i) for i in range(len(extras))), *out_refs, *more[1:])

    depth = sum(count for *_, count in work[0][2])
    return stream(
        name, loads, out_shapes, run, [pltpu.VMEM((work[0][0].shape[0], depth), F32), *scratch], mib
    )


def gradients(name, left, first, count, rights, out_of=None):
    loads = [part(left, first, count)] + [part(right) for right in rights]

    def run(get, *refs):
        *out_refs, turned = refs
        turned[...] = get(0)[...].T
        for i, ref in enumerate(out_refs):
            ref[...] = dot(turned[...], get(1 + i)[...]).astype(BF16)

    shapes = [shape_of(BF16, count, right.shape[1]) for right in rights]
    return stream(name, loads, shapes, run, [pltpu.VMEM((count, left.shape[0]), BF16)])


def sent_columns(name, first, pairs):
    loads = [load for left, right in pairs for load in (part(left, first, first), part(right))]

    def run(get, out_ref, turned):
        at = 0
        for i, (_, right) in enumerate(pairs):
            turned[...] = get(2 * i)[...].T
            n = right.shape[1]
            out_ref[:, at : at + n] = dot(turned[...], get(2 * i + 1)[...]).astype(BF16)
            at += n

    shape = shape_of(BF16, first, sum(right.shape[1] for _, right in pairs))
    return stream(name, loads, (shape,), run, [pltpu.VMEM((first, pairs[0][0].shape[0]), BF16)])[0]


def stack_rows(pieces, widths):
    block = pieces[0].shape[0]
    cuts = [sum(widths[:i]) for i in range(len(widths))]
    if block % 16:
        whole = jnp.concatenate(pieces, axis=0)
        return [whole[:, at : at + width] for at, width in zip(cuts, widths)]

    def run(*refs):
        for i, ref in enumerate(refs[: len(pieces)]):
            for j, out in enumerate(refs[len(pieces) :]):
                out[i * block : (i + 1) * block] = ref[:, cuts[j] : cuts[j] + widths[j]]

    shapes = [shape_of(pieces[0].dtype, block * len(pieces), width) for width in widths]
    return whole_call(run, pieces, shapes, (), "stack_rows")


def qkv_call(inputs, first, n):
    blocks = [(side, i * n, n) for i in range(3) for side in first]
    loads = [part(inputs), weight(first[0], 3 * n, LANES)] + [weight(*block) for block in blocks]

    def run(get, qkv_ref, normed_ref, inverse_ref, gains_ref):
        value = get(0)[...]
        inverse = lax.rsqrt(jnp.mean(value * value, axis=1, keepdims=True) + EPSILON)
        inverse_ref[...] = inverse
        gains = get(1)[...].astype(F32).T[:8]
        gains_ref[...] = gains
        normed_ref[...] = (value * inverse * gains[0:1]).astype(BF16)
        for i in range(len(blocks)):
            qkv_ref[:, i * n : (i + 1) * n] = dot(normed_ref[...], get(2 + i)[...]).astype(BF16)

    seq, width = inputs.shape
    shapes = (
        shape_of(BF16, seq, 6 * n),
        shape_of(BF16, seq, width),
        shape_of(F32, seq, 1),
        shape_of(F32, 8, width),
    )
    return stream("qkv", loads, shapes, run)


def norm_body(row, acc, value_ref, gains_ref, hidden_ref, inverse_ref, normed_ref=None):
    hidden = value_ref[...] + acc[...]
    inverse = lax.rsqrt(jnp.mean(hidden * hidden, axis=1, keepdims=True) + EPSILON)
    hidden_ref[...] = hidden
    inverse_ref[...] = inverse
    if normed_ref is not None:
        normed_ref[...] = (hidden * inverse * gains_ref[row : row + 1, :]).astype(BF16)


def norm_back(value, inverse, gain, grad):
    scaled = grad * gain
    inner = jnp.mean(value * scaled, axis=1, keepdims=True)
    d_value = inverse * scaled - value * (inverse * inverse * inverse) * inner
    return d_value, jnp.sum(grad * value * inverse, axis=0, keepdims=True)


def back_body(row, acc, value_ref, inverse_ref, gains_ref, grad_ref, low_ref, gain_out, hidden_ref=None):
    d_value, d_gain = norm_back(
        value_ref[...], inverse_ref[...], gains_ref[row : row + 1, :], acc[...]
    )
    total = grad_ref[...] + d_value
    low_ref[...] = total.astype(BF16)
    gain_out[...] = d_gain
    if hidden_ref is not None:
        hidden_ref[...] = total


def turn_kernel(grad_ref, order_ref, out_ref):
    out_ref[...] = dot_nt(grad_ref[...], order_ref[...]).astype(BF16)


def small_kernel(heads_half, one_ref, two_ref, three_ref, order_ref, bias_ref, onehot_ref, loss_ref, mine_ref, out_ref):
    width = one_ref.shape[1]
    gains = jnp.concatenate([one_ref[...], two_ref[...], three_ref[...], jnp.zeros((5, width), F32)], axis=0)
    high = gains.astype(BF16)
    rest = (gains - high.astype(F32)).astype(BF16)
    gains = dot_nt(high, order_ref[...]) + dot_nt(rest, order_ref[...])
    out_ref[...] = jnp.zeros_like(out_ref)
    across = width // LANES
    for i in range(3):
        for j in range(across):
            at = i * across + j
            out_ref[at : at + 1, :] = gains[i : i + 1, j * LANES : (j + 1) * LANES]
    at = 3 * across
    lane = lax.broadcasted_iota(jnp.int32, (1, LANES), 1)
    out_ref[at : at + 1, :] = jnp.where(lane == 0, loss_ref[...], 0.0)
    bias = bias_ref[...]
    heads = 2 * heads_half
    row = lax.broadcasted_iota(jnp.int32, (LANES, bias.shape[0]), 0)
    column = lax.broadcasted_iota(jnp.int32, (LANES, bias.shape[0]), 1)
    source = row + jnp.where(mine_ref[...] == 0, 0, heads_half)
    source = jnp.where(source >= heads, source - heads, source)
    pick = jnp.where((column == 8 * (source // 2) + source % 2) & (row < heads), 1.0, 0.0)
    bias = split_dot(pick.astype(BF16), bias)
    high = bias.astype(BF16)
    rest = (bias - high.astype(F32)).astype(BF16)
    table = dot_nt(high, onehot_ref[...]) + dot_nt(rest, onehot_ref[...])
    count = table.shape[1]
    a_row = LANES // count
    for head in range(heads):
        place = head % a_row * count
        line = at + 1 + head // a_row
        out_ref[line : line + 1, place : place + count] = table[head : head + 1, :]


def member_of(seg_ref, sent_count):
    ids = lax.broadcasted_iota(jnp.int32, (sent_count, seg_ref.shape[1]), 0)
    hit = jnp.where(seg_ref[...] == ids, 1.0, 0.0)
    return hit.astype(BF16), jnp.sum(hit, axis=1, keepdims=True)


def tail_body(acc, value_ref, gains_ref, seg_ref, own_ref, other_ref, hidden_ref, inverse_ref, pooled_ref, unit_ref, low_ref, scale_ref, high, rest):
    hidden = value_ref[...] + acc[...]
    inverse = lax.rsqrt(jnp.mean(hidden * hidden, axis=1, keepdims=True) + EPSILON)
    hidden_ref[...] = hidden
    inverse_ref[...] = inverse
    final = hidden_ref[...] * inverse * gains_ref[2:3, :]
    high[...] = final.astype(BF16)
    rest[...] = (final - high[...].astype(F32)).astype(BF16)
    sents, count = member_of(seg_ref, pooled_ref.shape[0])
    pooled = ((dot(sents, high[...]) + dot(sents, rest[...])) / count).astype(BF16)
    pooled_ref[...] = pooled
    half = own_ref.shape[1]
    left = dot(pooled, own_ref[...])
    right = dot(pooled, other_ref[...])
    square = jnp.sum(left * left, axis=1, keepdims=True) + jnp.sum(right * right, axis=1, keepdims=True)
    scale = lax.rsqrt(square + EPSILON)
    scale_ref[...] = scale
    for at, value in ((0, left * scale), (half, right * scale)):
        unit_ref[:, at : at + half] = value
        low_ref[:, at : at + half] = value.astype(BF16)


def head_call(quarters, unit, scale, partner, column, sentence_loads, out_shapes):
    loads = [part(q) for q in (*quarters, unit, scale, partner, column)] + sentence_loads
    quarter = quarters[0].shape[0]
    total = 4 * quarter

    def run(get, loss_ref, embed_ref, *refs):
        *back_refs, every = refs
        for i in range(4):
            every[i * quarter : (i + 1) * quarter] = get(i)[...]
        unit, scale, partner, columns_id = (get(i)[...] for i in range(4, 8))
        partner = as_columns(
            jnp.concatenate([partner, jnp.zeros((1, LANES - partner.shape[1]), jnp.int32)], axis=1)
        )[: partner.shape[1], 0:1]
        own_count = unit.shape[0]
        sims = dot_nt(every[...], every[...]) * SOFTMAX_TEMP
        row = lax.broadcasted_iota(jnp.int32, (total, total), 0)
        column = lax.broadcasted_iota(jnp.int32, (total, total), 1)
        sims = jnp.where(row == column, NEG_FILL, sims)
        top = jnp.max(sims, axis=0, keepdims=True)
        lse_row = top + jnp.log(jnp.sum(jnp.exp(sims - top), axis=0, keepdims=True))
        own = sims[:own_count]
        own_top = jnp.max(own, axis=1, keepdims=True)
        own_lse = own_top + jnp.log(jnp.sum(jnp.exp(own - own_top), axis=1, keepdims=True))
        is_target = columns_id.astype(F32) == partner
        hit = jnp.where(is_target, 1.0, 0.0)
        target = jnp.sum(jnp.where(is_target, own, 0.0), axis=1, keepdims=True)
        loss_ref[...] = jnp.sum(own_lse - target, axis=0, keepdims=True)
        d_rows = (LOSS_SCALE * (jnp.exp(own - own_lse) - hit)).astype(BF16)
        d_cols = (LOSS_SCALE * (jnp.exp(own - lse_row) - hit)).astype(BF16)
        d_unit = SOFTMAX_TEMP * (dot(d_rows, every[...]) + dot(d_cols, every[...]))
        inner = jnp.sum(d_unit * unit, axis=1, keepdims=True)
        d_embed = (scale * (d_unit - unit * inner)).astype(BF16)
        embed_ref[...] = d_embed
        sentence_back(d_embed, [get(8 + i) for i in range(len(sentence_loads))], *back_refs)

    return stream("head", loads, out_shapes, run, [pltpu.VMEM((total, unit.shape[1]), BF16)])


def sentence_call(embed, sentence_loads, out_shapes):
    def run(get, *back_refs):
        sentence_back(get(0)[...], [get(1 + i) for i in range(len(sentence_loads))], *back_refs)

    return stream("sentence", [part(embed)] + sentence_loads, out_shapes, run)


def sentence_back(d_embed, sources, hidden_ref, low_ref, gain_out):
    seg_ref, own_ref, other_ref, value_ref, inverse_ref, gains_ref = sources
    half = own_ref.shape[1]
    d_pooled = dot_nt(d_embed[:, :half], own_ref[...]) + dot_nt(d_embed[:, half:], other_ref[...])
    sents, count = member_of(seg_ref, d_embed.shape[0])
    d_final = split_dot(sents, d_pooled / count, ((0,), (0,)))
    d_value, d_gain = norm_back(value_ref[...], inverse_ref[...], gains_ref[2:3, :], d_final)
    hidden_ref[...] = d_value
    low_ref[...] = d_value.astype(BF16)
    gain_out[...] = d_gain


def whole_call(body, args, out_shapes, scratch=(), name=None):
    return pl.pallas_call(
        body,
        out_shape=tuple(out_shapes),
        in_specs=[pl.BlockSpec(memory_space=pltpu.VMEM)] * len(args),
        out_specs=tuple(pl.BlockSpec(memory_space=pltpu.VMEM) for _ in out_shapes),
        scratch_shapes=scratch,
        compiler_params=params(),
        cost_estimate=cost(0, 0),
        name=name,
    )(*args)


def shape_of(kind, *dims):
    return jax.ShapeDtypeStruct(dims, kind)


def _stack_heads(part):
    lane = lax.broadcasted_iota(jnp.int32, part.shape, 1)
    zero = jnp.zeros_like(part)
    first = lane < LANES // 2
    return jnp.concatenate(
        [jnp.where(first, part, zero), jnp.where(first, zero, part)], axis=0
    )


def _unstack_heads(both):
    half = both.shape[0] // 2
    lane = lax.broadcasted_iota(jnp.int32, (half, LANES), 1)
    return jnp.where(lane < LANES // 2, both[:half], both[half:])


def _pad_keys(pad, ref):
    seq = ref.shape[0]
    pad[0:REACH] = jnp.zeros((REACH, LANES), pad.dtype)
    pad[REACH + seq :] = jnp.zeros((REACH, LANES), pad.dtype)
    pad[REACH : REACH + seq] = ref[...]


def _query_bits(shape):
    return lax.broadcasted_iota(jnp.int32, shape, 0) & (QB - 1)


def as_columns(values):
    count, length = values.shape
    side = max(LANES, length)
    square = jnp.concatenate([values.astype(F32), jnp.zeros((side - count, length), F32)], axis=0)
    return square.T


def attend_forward_kernel(
    q_ref, k_ref, v_ref, segq_ref, segk_ref, rel_ref, ctx_ref, probs_ref, kpad, vpad, mask, scores
):
    seq = q_ref.shape[0]
    blocks = seq // QB
    _pad_keys(kpad, k_ref)
    _pad_keys(vpad, v_ref)

    @pl.when(pl.program_id(0) == 0)
    def _():
        keys = as_columns(segk_ref[...])
        for b in range(blocks):
            same = keys[:, b : b + 1] == segq_ref[b : b + 1, :].astype(F32)
            mask[b] = jnp.where(same, 0.0, NEG_FILL)

    rel = rel_ref[0]
    row = lax.broadcasted_iota(jnp.int32, (2 * QB, WIN), 0)
    bias = jnp.where(row < QB, rel[0:1, :], rel[1:2, :])
    bits = _query_bits((2 * QB, WIN))
    step = 1
    while step < QB:
        bias = jnp.where((bits & step) != 0, pltpu.roll(bias, step, 1), bias)
        step *= 2
    bias = bias.T
    for b in range(blocks):
        query = _stack_heads(q_ref[b * QB : (b + 1) * QB] * jnp.asarray(SCORE_SCALE, BF16))
        scores[b] = dot_nt(kpad[b * QB : b * QB + WIN], query)
    values = scores[...] + bias[None] + mask[...]
    top = jnp.max(values, axis=1, keepdims=True)
    shifted = jnp.exp(values - top)
    total = jnp.sum(shifted, axis=1, keepdims=True)
    probs_ref[0] = (shifted * (1.0 / total)).astype(BF16)
    for b in range(blocks):
        part = dot_tn(probs_ref[0, b], vpad[b * QB : b * QB + WIN])
        ctx_ref[b * QB : (b + 1) * QB] = _unstack_heads(part).astype(BF16)


def attend_backward_kernel(
    q_ref, k_ref, v_ref, dctx_ref, probs_ref, dqkv_ref, dbias_ref,
    kpad, vpad, dk_acc, dv_acc, d_probs, d_low,
):
    seq = q_ref.shape[0]
    pair = pl.program_id(0)
    side = pl.num_programs(0) // 2
    later = pair // side
    q_at = pl.ds(pl.multiple_of(pair * LANES, LANES), LANES)
    k_at = pl.ds(pl.multiple_of((pair + 2 * side + later * side) * LANES, LANES), LANES)
    v_at = pl.ds(pl.multiple_of((pair + 3 * side + later * side) * LANES, LANES), LANES)
    blocks = seq // QB
    _pad_keys(kpad, k_ref)
    _pad_keys(vpad, v_ref)
    dk_acc[...] = jnp.zeros_like(dk_acc)
    dv_acc[...] = jnp.zeros_like(dv_acc)
    for b in range(blocks):
        window = slice(b * QB, b * QB + WIN)
        d_ctx = _stack_heads(dctx_ref[b * QB : (b + 1) * QB])
        d_probs[b] = dot_nt(vpad[window], d_ctx)
        dv_acc[window] += dot(probs_ref[0, b], d_ctx)
    probs = probs_ref[0].astype(F32)
    product = probs * d_probs[...]
    inner = jnp.sum(product, axis=1, keepdims=True)
    d_scores = product - probs * inner
    d_low[...] = d_scores.astype(BF16)
    total = jnp.sum(d_scores, axis=0).T
    for b in range(blocks):
        here = slice(b * QB, (b + 1) * QB)
        window = slice(b * QB, b * QB + WIN)
        query = _stack_heads(q_ref[here] * jnp.asarray(SCORE_SCALE, BF16))
        dk_acc[window] += dot(d_low[b], query)
        d_query = _unstack_heads(dot_tn(d_low[b], kpad[window])) * SCORE_SCALE
        dqkv_ref[here, q_at] = d_query.astype(BF16)
    dqkv_ref[:, k_at] = dk_acc[REACH : REACH + seq].astype(BF16)
    dqkv_ref[:, v_at] = dv_acc[REACH : REACH + seq].astype(BF16)
    bits = _query_bits((2 * QB, WIN))
    step = 1
    while step < QB:
        total = jnp.where((bits & step) != 0, pltpu.roll(total, WIN - step, 1), total)
        step *= 2
    first = jnp.sum(total[:QB], axis=0, keepdims=True)
    second = jnp.sum(total[QB:], axis=0, keepdims=True)
    dbias_ref[0] = jnp.concatenate([first, second, jnp.zeros((6, WIN), F32)], axis=0)


def _qkv_specs(seq, pairs):
    def spec(kind):
        return pl.BlockSpec((seq, LANES), lambda p: (0, kind * pairs + p))

    return [spec(0), spec(1), spec(2)]


def attend_forward(qkv, twice, windows, rel_window):
    seq = qkv.shape[0]
    pairs = rel_window.shape[0]
    blocks = seq // QB
    return pl.pallas_call(
        attend_forward_kernel,
        grid=(pairs,),
        out_shape=(
            jax.ShapeDtypeStruct((seq, pairs * LANES), BF16),
            jax.ShapeDtypeStruct((pairs, blocks, WIN, 2 * QB), BF16),
        ),
        in_specs=_qkv_specs(seq, pairs)
        + [
            pl.BlockSpec((blocks, 2 * QB), lambda p: (0, 0)),
            pl.BlockSpec((blocks, WIN), lambda p: (0, 0)),
            pl.BlockSpec((1, 2, WIN), lambda p: (p, 0, 0)),
        ],
        out_specs=(
            pl.BlockSpec((seq, LANES), lambda p: (0, p)),
            pl.BlockSpec((1, blocks, WIN, 2 * QB), lambda p: (p, 0, 0, 0)),
        ),
        scratch_shapes=[pltpu.VMEM((seq + 2 * REACH, LANES), BF16)] * 2
        + [pltpu.VMEM((blocks, WIN, 2 * QB), F32)] * 2,
        compiler_params=params(),
        cost_estimate=cost(8 * seq * WIN * LANES * pairs * 4, 8 * seq * LANES * pairs),
        name="attend_forward",
    )(qkv, qkv, qkv, twice, windows, rel_window)


def attend_backward(qkv, d_context, probs):
    seq = qkv.shape[0]
    pairs = probs.shape[0]
    blocks = seq // QB
    lane_block = pl.BlockSpec((seq, LANES), lambda p: (0, p))
    return pl.pallas_call(
        attend_backward_kernel,
        grid=(pairs,),
        out_shape=(
            jax.ShapeDtypeStruct((seq, 3 * pairs * LANES), BF16),
            jax.ShapeDtypeStruct((pairs, 8, WIN), F32),
        ),
        in_specs=_qkv_specs(seq, pairs)
        + [
            lane_block,
            pl.BlockSpec((1, blocks, WIN, 2 * QB), lambda p: (p, 0, 0, 0)),
        ],
        out_specs=(
            pl.BlockSpec((seq, 3 * pairs * LANES), lambda p: (0, 0)),
            pl.BlockSpec((1, 8, WIN), lambda p: (p, 0, 0)),
        ),
        scratch_shapes=[pltpu.VMEM((seq + 2 * REACH, LANES), BF16)] * 2
        + [pltpu.VMEM((seq + 2 * REACH, LANES), F32)] * 2
        + [pltpu.VMEM((blocks, WIN, 2 * QB), F32), pltpu.VMEM((blocks, WIN, 2 * QB), BF16)],
        compiler_params=params(),
        cost_estimate=cost(16 * seq * WIN * LANES * pairs * 4, 16 * seq * LANES * pairs),
        name="attend_backward",
    )(qkv, qkv, qkv, d_context, probs)


CORE = 1
CROSS = 2


def hop(value, mask):
    size = lax.axis_size("dp")
    return lax.ppermute(value, "dp", [(i, i ^ mask) for i in range(size)])


def over(value):
    return lax.ppermute(value, "mp", [(0, 1), (1, 0)])


def cross(value):
    return hop(value, CROSS)


def core(value):
    return hop(value, CORE)


def go(waits, *sends, keep=(), join=True):
    values = [value for _, value in sends]
    held = lax.optimization_barrier((*values, *keep, *waits))
    results = [how(value) for (how, _), value in zip(sends, held)]
    if join:
        results = list(lax.optimization_barrier(tuple(results)))
    return results + list(held[len(values) : len(values) + len(keep)])


def slot_masks(size):
    rest = size // 4
    return [z * 4 + x * 2 + c for c in range(2) for x in range(2) for z in range(rest)]


def strides(size):
    found = []
    stride = 4
    while stride < size:
        found.append(stride)
        stride *= 2
    return found


def gather_near(shard, waits, widths=None):
    size = lax.axis_size("dp")
    pieces = [shard]
    stride = 4
    while stride < size:
        radix = min(4, size // stride)
        shard = jnp.concatenate(pieces, axis=0) if len(pieces) > 1 else shard
        sends = [(functools.partial(hop, mask=j * stride), shard) for j in range(1, radix)]
        pieces = [shard] + go(waits, *sends)
        stride *= radix
    return jnp.concatenate(pieces, axis=0) if widths is None else stack_rows(pieces, widths)


def rows(*pieces):
    return jnp.concatenate(pieces, axis=0)


def columns(*pieces):
    return jnp.concatenate(pieces, axis=1)


def gather_weights(start, later, n_one, n_three, early, begin, between):
    size = lax.axis_size("dp")
    steps = strides(size)
    n_two = start.shape[1] - n_one
    n_four = later.shape[1] - n_three
    n_early = n_three * 2 // 3
    if len(steps) == 2:
        got = go((), *((functools.partial(hop, mask=4 * j), start) for j in range(1, 4)))
        more = hop(later, 4)
        one, two = stack_rows([start, *got], (n_one, n_two))
        later = stack_rows([later, more], (n_early, later.shape[1] - n_early))
        wide_step = functools.partial(hop, mask=steps[1])
    else:
        one, two = gather_near(start, (), (n_one, n_two))

        later = [later[:, :n_early], later[:, n_early:]]

        def wide_step(value):
            whole = gather_near(value, ())
            return whole[value.shape[0] :]

    one_x, two_y, more = go(early, (cross, one), (over, two), (wide_step, later[0]))
    (one,) = stack_rows([one, one_x], (n_one,))
    (two,) = stack_rows([two, two_y], (n_two,))
    one_y, two_x, one_c, two_c, more_b = go(
        (), (over, one), (cross, two), (core, one), (core, two), (wide_step, later[1])
    )
    if len(steps) == 2:
        have = later[0].shape[0]

        def put(near_a, near_b, far_a, far_b, three_ref, four_ref):
            for at, left, right in ((0, near_a, near_b), (have, far_a, far_b)):
                here = slice(at, at + have)
                three_ref[here, :n_early] = left[...]
                three_ref[here, n_early:] = right[:, : n_three - n_early]
                four_ref[here] = right[:, n_three - n_early :]

        three, four = whole_call(
            put,
            (*later, more, more_b),
            (shape_of(BF16, 2 * have, n_three), shape_of(BF16, 2 * have, n_four)),
            (),
            "put_rows",
        )
    else:
        later = rows(columns(*later), columns(more, more_b))
        three, four = later[:, :n_three], later[:, n_three:]
    three_x, four_y, one_yc, two_xc = go((), (cross, three), (over, four), (core, one_y), (core, two_x))
    (three,) = stack_rows([three, three_x], (n_three,))
    (four,) = stack_rows([four, four_y], (four.shape[1],))
    three_y, four_x, three_c, four_c, one, one_c, one_y, one_yc, two, two_x, two_c, two_xc, *early = go(
        (),
        (over, three),
        (cross, four),
        (core, three),
        (core, four),
        keep=(one, one_c, one_y, one_yc, two, two_x, two_c, two_xc, *early),
        join=False,
    )
    first, second = along_x(one, one_c, one_y, one_yc), along_y(two, two_x, two_c, two_xc)
    done = between(begin(first, early), second, early)
    four_xc, three_yc, *done = go(
        (three_y, four_x, three_c, four_c), (core, four_x), (core, three_y), keep=done, join=False
    )
    third, fourth = along_x(three, three_c, three_y, three_yc), along_y(four, four_x, four_c, four_xc)
    return first, second, third, fourth, early, done


def along_x(near, near_c, other, other_c):
    count = near.shape[0]
    return ((near, 0, count), (near_c, 0, count)), ((other, 0, count), (other_c, 0, count))


def along_y(near, side, near_c, side_c):
    count = near.shape[0] // 2
    return tuple(
        tuple((array, at, count) for array in (near, side, near_c, side_c)) for at in (0, count)
    )


def pack(name, sources):
    widths = [count for *_, count in sources]

    def run(get, out_ref):
        at = 0
        for i, width in enumerate(widths):
            out_ref[:, at : at + width] = get(i)[...]
            at += width

    shape = shape_of(BF16, sources[0][0].shape[0], sum(widths))
    return stream(name, [part(*source) for source in sources], (shape,), run)[0]


def gather_dp(shard):
    near = gather_near(shard, ())
    side, c_near = go((near,), (cross, near), (core, near))
    return near, side, c_near, core(side)


def low(value):
    return value.astype(BF16)


def add(left, right):
    return (left.astype(F32) + right.astype(F32)).astype(BF16)


def product(left, begin, end, right, got=None):
    value = dot_tn(left[:, begin:end], right)
    if got is not None:
        value = value + got.astype(F32)
    return low(value)


def rest_start(value):
    half = value.shape[0] // 2
    return value[half:], value[:half]


def sum_half(value, send):
    gone, stays = rest_start(value)
    return stays + send(low(gone)).astype(F32)


def rest_hops(size):
    return [functools.partial(hop, mask=stride) for stride in reversed(strides(size))]


def shards(
    tokens,
    seg_ids,
    buckets,
    labels,
    w_query,
    w_key,
    w_value,
    w_out,
    w_in,
    w_back,
    gain_attn,
    gain_ffn,
    gain_final,
    w_pool,
    rel_table,
):
    micro_count, seq, width = tokens.shape
    size = lax.axis_size("dp")
    me = lax.axis_index("dp")
    mine = lax.axis_index("mp")
    block = width // size
    inner_half = w_query.shape[1]
    hidden_half = w_in.shape[1]
    sent_local = labels.shape[1]
    bucket_count = rel_table.shape[0]
    heads_half = rel_table.shape[1]
    masks = slot_masks(size)

    x_own = lax.dynamic_index_in_dim(tokens, mine, 0, keepdims=False)
    segments = lax.dynamic_index_in_dim(seg_ids, mine, 0, keepdims=False)[0]
    partner = lax.dynamic_index_in_dim(labels, mine, 0, keepdims=False)

    slot_block = jnp.stack([jnp.bitwise_xor(me, m) for m in masks]).astype(jnp.int32)
    source = (slot_block[:, None] * block + jnp.arange(block, dtype=jnp.int32)[None, :]).reshape(-1)
    order = (jnp.arange(width, dtype=jnp.int32)[:, None] == source[None, :]).astype(BF16)
    order = lax.optimization_barrier(order)
    inputs = dot(x_own, order)


    row_f32 = shape_of(F32, seq, width)
    row_low = shape_of(BF16, seq, width)
    column_f32 = shape_of(F32, seq, 1)
    gain_f32 = shape_of(F32, 1, width)
    heads = 3 * inner_half
    piece = hidden_half // 2
    halves = [(side, i * inner_half, inner_half) for side in range(2) for i in range(2)]

    def hidden_blocks(weights, first_col=0):
        return [(weights[side], first_col + col, n) for side, col, n in halves]

    def begin(first, early):
        inputs, rel_window, twice, windows, *_ = early
        qkv, normed1_low, inverse1, gains = qkv_call(inputs, first, inner_half)
        context, probs = attend_forward(qkv, twice, windows, rel_window)
        return qkv, normed1_low, inverse1, gains, context, probs

    def between(started, second, early):
        qkv, normed1_low, inverse1, gains, context, probs = started
        inputs = early[0]
        hidden1, inverse2, normed2_low = narrow(
            "attn_out",
            [(context, i * inner_half, second[i], piece, inner_half) for i in range(2)],
            (inputs, gains),
            (row_f32, column_f32, row_low),
            functools.partial(norm_body, 1),
        )
        act0, slope0 = wide("act0", normed2_low, hidden_blocks(second), (), gelu_both, 2)
        return normed1_low, inverse1, gains, qkv, context, probs, hidden1, inverse2, normed2_low, act0, slope0

    gains_col = jnp.pad(
        jnp.stack([gain_attn, gain_ffn, gain_final], axis=1), ((0, 0), (0, LANES - 3))
    )
    pool_half = w_pool.shape[1] // 2
    pool_own = lax.dynamic_slice_in_dim(w_pool, mine * pool_half, pool_half, axis=1)
    back_shard = w_back.T
    if block % 16:
        start = columns(w_query, w_key, w_value, gains_col, w_in[:, :piece], w_out.T)
        later = columns(back_shard[:, :piece], pool_own, w_in[:, piece:], back_shard[:, piece:])
    else:
        start = pack(
            "pack_start",
            [(w, 0, inner_half) for w in (w_query, w_key, w_value)]
            + [(gains_col, 0, LANES), (w_in, 0, piece), (w_out.T, 0, inner_half)],
        )
        back_shard, w_in, _ = lax.optimization_barrier((back_shard, w_in, start))
        later = pack(
            "pack_later",
            [
                (back_shard, 0, piece),
                (pool_own, 0, pool_half),
                (w_in, piece, piece),
                (back_shard, piece, piece),
            ],
        )
    rel_other = over(lax.optimization_barrier((rel_table, start))[0])
    rel_all = jnp.concatenate([rel_table, rel_other], axis=1).astype(F32)
    near_buckets = lax.slice_in_dim(buckets, seq - 1 - REACH, seq - 1 - REACH + WIN)
    onehot = (near_buckets[None, :] == jnp.arange(bucket_count, dtype=jnp.int32)[:, None]).astype(F32)
    onehot = lax.optimization_barrier(low(onehot))
    rel_window = dot(rel_all, onehot.astype(F32), ((0,), (0,)), HIGHEST).reshape(heads_half, 2, WIN)
    padded = jnp.pad(segments, (REACH, REACH), constant_values=-1)
    windows = jnp.stack([padded[at : at + WIN] for at in range(0, seq, QB)])
    twice = jnp.tile(segments.reshape(seq // QB, QB), (1, 2))
    local_ids = jnp.arange(sent_local, dtype=jnp.int32)
    column_id = (slot_block[:, None] * sent_local + local_ids[None, :]).reshape(1, -1)
    early = (
        inputs, rel_window, twice, windows, order, onehot, column_id, partner[None, :], segments[None, :], mine.reshape(1, 1)
    )
    first, second, third, fourth, early, done = gather_weights(
        start,
        later,
        heads + LANES,
        piece + pool_half,
        early,
        begin,
        between,
    )
    inputs, rel_window, twice, windows, order, onehot, column_id, partner, seg_lane, mine_array = early
    normed1_low, inverse1, gains, qkv, context, probs, hidden1, inverse2, normed2_low, act0, slope0 = done

    act1, slope1 = wide("act1", normed2_low, hidden_blocks(fourth), (), gelu_both, 2)
    pool_loads = [weight(side, piece, pool_half) for side in third]
    hidden2, inverse3, pooled_low, unit, unit_low, scale = narrow(
        "ffn_out",
        [(act0, i * piece, third[i], 0, piece) for i in range(2)]
        + [(act1, i * piece, fourth[i], piece, piece) for i in range(2)],
        (hidden1, gains, seg_lane, *pool_loads),
        (
            row_f32,
            column_f32,
            shape_of(BF16, sent_local, width),
            shape_of(F32, sent_local, width),
            shape_of(BF16, sent_local, width),
            shape_of(F32, sent_local, 1),
        ),
        tail_body,
        [pltpu.VMEM((seq, width), BF16)] * 2,
    )
    quarters = gather_dp(unit_low)

    total_sent = column_id.shape[1]
    sentence_loads = [part(seg_lane), *pool_loads, part(hidden2), part(inverse3), part(gains)]
    back_shapes = (row_f32, row_low, gain_f32)
    if total_sent <= 1024:
        loss_local, embed_low, d_hidden2, ffn_low, d_gain3 = head_call(
            quarters,
            unit,
            scale,
            partner,
            column_id,
            sentence_loads,
            (shape_of(F32, 1, 1), shape_of(BF16, sent_local, width), *back_shapes),
        )
    else:
        every = rows(*quarters)
        position = jnp.arange(total_sent, dtype=jnp.int32)
        sims = dot_nt(every, every) * SOFTMAX_TEMP
        sims = jnp.where(position[:, None] == position[None, :], NEG_FILL, sims)
        lse_row = jax.nn.logsumexp(sims, axis=0, keepdims=True)
        own_sims = sims[:sent_local]
        own_lse = jax.nn.logsumexp(own_sims, axis=1, keepdims=True)
        is_target = column_id == partner.reshape(-1, 1)
        target = jnp.sum(jnp.where(is_target, own_sims, 0.0), axis=-1, keepdims=True)
        loss_local = jnp.sum(own_lse - target)
        hit = is_target.astype(F32)
        d_rows = low(LOSS_SCALE * (jnp.exp(own_sims - own_lse) - hit))
        d_cols = low(LOSS_SCALE * (jnp.exp(own_sims - lse_row) - hit))
        d_unit = SOFTMAX_TEMP * (dot(d_rows, every) + dot(d_cols, every))
        embed_low = low(scale * (d_unit - unit * jnp.sum(d_unit * unit, axis=-1, keepdims=True)))
        d_hidden2, ffn_low, d_gain3 = sentence_call(embed_low, sentence_loads, back_shapes)

    half = width // 2
    quarter = width // 4

    back0_sent, back1_sent = gradients("back_sent", ffn_low, half, half, (act0, act1))
    (pool_sent,) = gradients("pool_sent", pooled_low, half, half, (embed_low,))
    back0_got, back1_got, pool_got, ffn_later = go(
        (), (core, back0_sent), (core, back1_sent), (core, pool_sent), keep=(ffn_low,), join=False
    )
    pool_hi = product(pooled_low, quarter, half, embed_low, pool_got[quarter:])
    pool_lo = product(pooled_low, 0, quarter, embed_low, pool_got[:quarter])
    up0 = wide("up0", ffn_later, hidden_blocks(third), (slope0,), times_slope)

    back_hi = product(ffn_low, quarter, half, act0, back0_got[quarter:])
    back_lo = product(ffn_low, 0, quarter, act0, back0_got[:quarter])
    back_own = product(ffn_low, 0, half, act1[:, :piece], back1_got[:, :piece])
    back_oth = product(ffn_low, 0, half, act1[:, piece:], back1_got[:, piece:])
    got_lo, got_own, got_pool, ffn_later, up0, back_lo, back_own, pool_lo = go(
        (),
        (cross, back_hi),
        (over, back_oth),
        (cross, pool_hi),
        keep=(ffn_later, up0, back_lo, back_own, pool_lo),
    )
    up1 = wide("up1", ffn_later, hidden_blocks(fourth, piece), (slope1,), times_slope)
    in0_sent, in1_sent = gradients("in_sent", normed2_low, half, half, (up0, up1))
    in0_got, in1_got, up0, up1 = go((), (core, in0_sent), (core, in1_sent), keep=(up0, up1))
    attn_low, d_gain2, d_hidden1 = narrow(
        "ffn_in_back",
        [(up0, i * piece, second[i], 0, piece) for i in range(2)]
        + [(up1, i * piece, fourth[i], 0, piece) for i in range(2)],
        (hidden1, inverse2, gains, d_hidden2),
        (row_low, gain_f32, row_f32),
        functools.partial(back_body, 1),
    )
    d_context = wide("d_context", attn_low, [(second[side], piece, inner_half) for side in range(2)])

    pool_lo = add(pool_lo, got_pool)
    back_lo = add(back_lo, got_lo)
    back_own = add(back_own, got_own)
    in_hi = product(normed2_low, quarter, half, up0, in0_got[quarter:])
    in_lo = product(normed2_low, 0, quarter, up0, in0_got[:quarter])
    in_own = product(normed2_low, 0, half, up1[:, :piece], in1_got[:, :piece])
    in_oth = product(normed2_low, 0, half, up1[:, piece:], in1_got[:, piece:])
    got_first, got_x, got_in_own, d_context, pool_lo, back_lo, back_own, in_lo, in_own = go(
        (got_lo, got_own),
        (over, columns(back_lo[:, piece:], pool_lo[:, pool_half:])),
        (cross, columns(back_own[quarter:], in_hi)),
        (over, in_oth),
        keep=(d_context, pool_lo, back_lo, back_own, in_lo, in_own),
        join=False,
    )
    d_qkv, d_bias = attend_backward(qkv, d_context, probs)
    query_both = 2 * inner_half
    late_sent = sent_columns("late_sent", half, ((attn_low, context), (normed1_low, d_qkv)))
    late_got, d_qkv_later = go((), (core, late_sent), keep=(d_qkv,), join=False)
    grad_slots, d_gain1 = narrow(
        "qkv_back",
        [(d_qkv_later, i * inner_half, first[i], 0, inner_half) for i in range(2)]
        + [(d_qkv_later, (1 + i) * query_both, first[i], inner_half, query_both) for i in range(2)],
        (inputs, inverse1, gains, d_hidden1),
        (row_low, gain_f32),
        functools.partial(back_body, 0),
    )

    table_row = 3 * (width // LANES) + 1
    table_rows = -(-2 * heads_half * bucket_count // LANES)
    small_rows = -(-(table_row + table_rows) // 8) * 8
    (flat,) = whole_call(
        functools.partial(small_kernel, heads_half),
        (d_gain1, d_gain2, d_gain3, order, d_bias.reshape(-1, WIN), onehot, loss_local.reshape(1, 1), mine_array),
        (shape_of(F32, small_rows, LANES),),
        (),
        "small",
    )
    (grad_own,) = whole_call(turn_kernel, (grad_slots, order), (row_low,), (), "turn")
    flat_got, flat = go((), (over, flat), keep=(flat,), join=False)
    got_first, got_x, got_in_own = lax.optimization_barrier((got_first, got_x, got_in_own))
    flat = flat + flat_got
    got_second, got_in_lo = got_x[:, :piece], got_x[:, piece:]

    far = rest_hops(size)
    back_all = columns(
        add(back_lo[:, :piece], got_first[:, :piece]),
        add(back_own[:quarter], got_second),
        add(pool_lo[:, :pool_half], got_first[:, piece:]),
    )
    back_rest, back_stay = rest_start(back_all)
    in_lo = add(in_lo, got_in_lo)
    in_own = add(in_own, got_in_own)
    out_got, qkv_got = late_got[:, :query_both], late_got[:, query_both:]
    out_hi = product(attn_low, quarter, half, context, out_got[quarter:])
    out_lo = product(attn_low, 0, quarter, context, out_got[:quarter])
    query_hi = product(normed1_low, quarter, half, d_qkv[:, :query_both], qkv_got[quarter:, :query_both])
    query_lo = product(normed1_low, 0, quarter, d_qkv[:, :query_both], qkv_got[:quarter, :query_both])
    kv_own = product(
        normed1_low, 0, half, d_qkv[:, query_both : 2 * query_both], qkv_got[:, query_both : 2 * query_both]
    )
    kv_oth = product(normed1_low, 0, half, d_qkv[:, 2 * query_both :], qkv_got[:, 2 * query_both :])
    rest_hop = [functools.partial(hop, mask=j * 4) for j in range(1, min(4, size // 4))]
    back_more, got_first, got_x, got_kv, flat_got, back_stay, in_lo, in_own, out_lo, query_lo, kv_own, flat = go(
        (grad_own,),
        (far[0], back_rest),
        (over, in_lo[:, piece:]),
        (cross, columns(in_own[quarter:], out_hi, query_hi)),
        (over, kv_oth),
        (core, flat),
        keep=(back_stay, in_lo, in_own, out_lo, query_lo, kv_own, flat),
    )

    count = flat.shape[0]

    def in_two(value):
        high = value.astype(BF16).astype(F32)
        return jnp.concatenate([high, value - high], axis=0).astype(BF16)

    def from_two(pair):
        return pair[:count].astype(F32) + pair[count : 2 * count].astype(F32)

    def late_adds(
        stay, more, in_lo, got_first, in_own, got_x, out_lo, query_lo, kv_own, got_kv, flat, got_flat, *outs
    ):
        back_gone, back_keep, in_gone, in_keep, heads_gone, heads_keep, kv_gone, kv_keep, small = outs
        rows_z = stay.shape[0] // 2
        total = add(stay[...], more[...])
        back_keep[...] = total[:rows_z]
        back_gone[...] = total[rows_z:]
        rows_z = in_lo.shape[0] // 2
        for at, total in (
            (0, add(in_lo[:, :piece], got_first[...])),
            (piece, add(in_own[:quarter], got_x[:, :piece])),
        ):
            in_keep[:, at : at + piece] = total[:rows_z]
            in_gone[:, at : at + piece] = total[rows_z:]
        for i, ref in enumerate((out_lo, query_lo)):
            first_col = piece + i * query_both
            total = add(ref[...], got_x[:, first_col : first_col + query_both])
            heads_keep[:, i * inner_half : (i + 1) * inner_half] = total[:, :inner_half]
            heads_gone[:, i * inner_half : (i + 1) * inner_half] = total[:, inner_half:]
        kv_keep[...] = add(kv_own[:quarter], got_kv[:quarter])
        kv_gone[:, :query_both] = add(kv_own[quarter:], got_kv[quarter:])
        small[...] = flat[...] + got_flat[...]
        kv_gone[:, query_both:] = jnp.zeros((quarter, LANES), BF16)
        pair = in_two(small[...])
        kv_gone[: 2 * count, query_both:] = pair
        small[...] = from_two(pair)

    cut = [shape_of(BF16, back_stay.shape[0] // 2, back_stay.shape[1])] * 2
    cut += [shape_of(BF16, quarter // 2, hidden_half)] * 2 + [shape_of(BF16, quarter, query_both)] * 2
    cut += [
        shape_of(BF16, quarter, query_both + LANES),
        shape_of(BF16, quarter, query_both),
        shape_of(F32, count, LANES),
    ]
    back_rest, back_stay, in_rest, in_stay, heads_gone, heads_keep, kv_gone, kv_keep, flat = whole_call(
        late_adds,
        (back_stay, back_more, in_lo, got_first, in_own, got_x, out_lo, query_lo, kv_own, got_kv, flat, flat_got),
        cut,
        (),
        "late_adds",
    )
    half_seq = seq // 2
    back_more, in_more, got_first, got_second, grad_other, back_stay, in_stay, heads_keep, kv_keep, flat = go(
        (),
        (far[1], back_rest),
        (far[0], in_rest),
        (over, heads_gone),
        (cross, kv_gone),
        (over, grad_own[:half_seq]),
        keep=(back_stay, in_stay, heads_keep, kv_keep, flat),
    )

    def finish(value):
        value = value.astype(F32)
        for send in far[2:]:
            value = sum_half(value, send)
        return value

    n_last = query_both + query_both
    if len(far) == 2:
        rest = block

        def last_adds(stay, more, heads_ref, got_heads, kv_ref, got_kv, flat_ref, back_ref, back_got, own_ref, *outs):
            one, two, three, in_keep, keep, flat_out, tail, pool_ref = outs
            pool = add(back_ref[:, hidden_half:], back_got[:, hidden_half:])
            pool_ref[...] = pool
            tail[:half_seq] = own_ref[half_seq:]
            tail[half_seq:, :pool_half] = pool
            tail[half_seq:, pool_half:] = jnp.zeros((rest, width - pool_half), BF16)
            total = add(stay[...], more[...])
            in_keep[...] = total[:rest]
            one[:, LANES : LANES + hidden_half] = total[rest:]
            pair = in_two(flat_ref[...] + from_two(got_kv[:, query_both:]))
            flat_out[...] = from_two(pair)
            for i, (ref, at) in enumerate(((keep, 0), (one, LANES + hidden_half), (two, LANES), (three, LANES))):
                here = slice(i * rest, (i + 1) * rest)
                if i:
                    ref[:, :LANES] = pair
                ref[:, at : at + query_both] = add(heads_ref[here], got_heads[here])
                ref[:, at + query_both : at + n_last] = add(kv_ref[here], got_kv[here, :query_both])

        one, two, three, in_stay, last_stay, flat, tail, grad_pool = whole_call(
            last_adds,
            (in_stay, in_more, heads_keep, got_first, kv_keep, got_second, flat, back_stay, back_more, grad_own),
            (
                shape_of(BF16, rest, LANES + hidden_half + n_last),
                shape_of(BF16, rest, LANES + n_last),
                shape_of(BF16, rest, LANES + n_last),
                shape_of(BF16, rest, hidden_half),
                shape_of(BF16, rest, n_last),
                shape_of(F32, count, LANES),
                shape_of(BF16, half_seq + rest, width),
                shape_of(BF16, rest, pool_half),
            ),
            (),
            "last_adds",
        )
        got_one, got_two, got_three, got_tail, back_stay, back_more = go(
            (),
            (rest_hop[0], one),
            (rest_hop[1], two),
            (rest_hop[2], three),
            (over, tail),
            keep=(back_stay, back_more),
            join=False,
        )

        def back_final(stay, more, back_ref):
            back_ref[...] = stay[:, :hidden_half].astype(F32) + more[:, :hidden_half].astype(F32)

        (grad_back,) = whole_call(
            back_final, (back_stay, back_more), (shape_of(F32, rest, hidden_half),), (), "back_final"
        )

        def tokens_final(mine_ref, own_ref, first_ref, tail_ref, pool_own, out_ref, pool_ref):
            first = mine_ref[...] == 0
            own, other = pool_own[...].astype(F32), tail_ref[half_seq:, :pool_half].astype(F32)
            pool_ref[:, :pool_half] = jnp.where(first, own, other)
            pool_ref[:, pool_half:] = jnp.where(first, other, own)
            for at, ref in ((0, first_ref), (half_seq, tail_ref)):
                here = slice(at, at + half_seq)
                own, other = own_ref[here].astype(F32), ref[:half_seq].astype(F32)
                out_ref[0, here] = jnp.where(first, own, other).astype(BF16)
                out_ref[1, here] = jnp.where(first, other, own).astype(BF16)

        grad_tokens, grad_pool = whole_call(
            tokens_final,
            (mine_array, grad_own, grad_other, got_tail, grad_pool),
            (shape_of(BF16, 2, seq, width), shape_of(F32, rest, 2 * pool_half)),
            (),
            "tokens_final",
        )
        got_one, got_two, got_three, grad_tokens = lax.optimization_barrier(
            (got_one, got_two, got_three, grad_tokens)
        )

        def last_final(stay, in_keep, one_ref, two_ref, three_ref, flat_ref, *outs):
            in_ref, out_ref, q_ref, k_ref, v_ref, flat_out = outs
            in_ref[...] = in_keep[...].astype(F32) + one_ref[:, LANES : LANES + hidden_half].astype(F32)
            total = stay[...].astype(F32) + one_ref[:, LANES + hidden_half :].astype(F32)
            total = total + two_ref[:, LANES:].astype(F32) + three_ref[:, LANES:].astype(F32)
            for i, ref in enumerate((out_ref, q_ref, k_ref, v_ref)):
                ref[...] = total[:, i * inner_half : (i + 1) * inner_half]
            small = flat_ref[...]
            for ref in (one_ref, two_ref, three_ref):
                small = small + from_two(ref[:, :LANES])
            flat_out[...] = small

        head_shape = shape_of(F32, rest, inner_half)
        grad_in, grad_out, grad_query, grad_key, grad_value, flat = whole_call(
            last_final,
            (last_stay, in_stay, got_one, got_two, got_three, flat),
            (shape_of(F32, rest, hidden_half), *(head_shape,) * 4, shape_of(F32, count, LANES)),
            (),
            "last_final",
        )
    else:
        flat = flat + from_two(got_second[:, query_both:])
        grad_other = rows(grad_other, over(grad_own[half_seq:]))
        in_rest, in_stay = rest_start(add(in_stay, in_more))
        last = columns(add(heads_keep, got_first), add(kv_keep, got_second[:, :query_both]))
        last_rest, last_stay = rest_start(last)
        in_more, last_more, *flat_got = go(
            (), (far[1], in_rest), (far[0], last_rest), *((how, flat) for how in rest_hop)
        )
        last_rest, last_stay = rest_start(add(last_stay, last_more))
        last_more = far[1](last_rest)
        flat = flat + sum(flat_got)
        for send in far[:-2]:
            flat = flat + send(flat)
        grad_last = finish(last_stay.astype(F32) + last_more.astype(F32))
        grad_in = finish(in_stay.astype(F32) + in_more.astype(F32))
        back_all = finish(back_stay.astype(F32) + back_more.astype(F32))
        grad_back, grad_pool = back_all[:, :hidden_half], back_all[:, hidden_half:]
        pool_other = over(grad_pool)
        grad_pool = jnp.where(mine == 0, columns(grad_pool, pool_other), columns(pool_other, grad_pool))
        grad_out, grad_query, grad_key, grad_value = (
            grad_last[:, i * inner_half : (i + 1) * inner_half] for i in range(4)
        )
        grad_tokens = jnp.where(
            mine == 0, jnp.stack([grad_own, grad_other]), jnp.stack([grad_other, grad_own])
        )
    across = width // LANES
    gains_mine = lax.dynamic_slice_in_dim(flat[: 3 * across].reshape(3, width), me * block, block, axis=1)
    loss = flat[3 * across, 0] / (micro_count * sent_local * size)
    table_sum = flat[table_row : table_row + table_rows].reshape(-1, bucket_count)[: 2 * heads_half]
    table_mine = lax.dynamic_slice_in_dim(table_sum, mine * heads_half, heads_half, axis=0).T
    return (
        loss,
        grad_tokens,
        grad_query,
        grad_key,
        grad_value,
        grad_out.T,
        grad_in,
        grad_back.T,
        gains_mine[0],
        gains_mine[1],
        gains_mine[2],
        grad_pool,
        table_mine,
    )


def solution(mesh):
    placed = (
        P(None, "dp", None),
        P(None, "dp", None),
        P(),
        P(None, "dp"),
        P("dp", "mp"),
        P("dp", "mp"),
        P("dp", "mp"),
        P("mp", "dp"),
        P("dp", "mp"),
        P("mp", "dp"),
        P("dp"),
        P("dp"),
        P("dp"),
        P("dp", None),
        P(None, "mp"),
    )
    return jax.shard_map(
        shards,
        mesh=mesh,
        in_specs=placed,
        out_specs=(
            P(),
            P(None, "dp", None),
            P("dp", "mp"),
            P("dp", "mp"),
            P("dp", "mp"),
            P("mp", "dp"),
            P("dp", "mp"),
            P("mp", "dp"),
            P("dp"),
            P("dp"),
            P("dp"),
            P("dp", None),
            P(None, "mp"),
        ),
        check_vma=False,
    )
```

```python
import functools

import jax
import jax.numpy as jnp
from jax import lax
from jax.experimental import pallas as pl
from jax.experimental.pallas import tpu as pltpu
from jax.sharding import PartitionSpec as P

NEG_FILL = -1000000000.0
SCORE_SCALE = 0.125
SOFTMAX_TEMP = 50.0
LOSS_SCALE = 64.0
EPSILON = 1e-06
REACH = 32
QB = 64
WIN = QB + 2 * REACH
LANES = 128
GELU_A = 0.7978845608028654
GELU_B = 0.044715

BF16 = jnp.bfloat16
F32 = jnp.float32
HIGHEST = lax.Precision.HIGHEST


def dot(left, right, dims=((1,), (0,)), precision=None):
    return lax.dot_general(
        left, right, (dims, ((), ())), precision=precision, preferred_element_type=F32
    )


def dot_nt(left, right):
    return dot(left, right, ((1,), (1,)))


def dot_tn(left, right):
    return dot(left, right, ((0,), (0,)))


def rms_forward(value, gain):
    inverse = lax.rsqrt(jnp.mean(value * value, axis=-1, keepdims=True) + EPSILON)
    return (value * inverse * gain, inverse)


def cost(flops, bytes_accessed):
    return pl.CostEstimate(flops=0, bytes_accessed=0, transcendentals=0)


def params(mib=16):
    return pltpu.CompilerParams(vmem_limit_bytes=mib * 2**20)


def split_dot(left, right, dims=((1,), (0,))):
    high = right.astype(BF16)
    rest = (right - high.astype(F32)).astype(BF16)
    return dot(left, high, dims) + dot(left, rest, dims)


def stream_kernel(plan, operands, outs, body, *refs):
    sources, out_refs = refs[:operands], refs[operands : operands + outs]
    more = refs[operands + outs :]
    buffers, sem = more[: sum(len(load) > 1 for load in plan)], more[-1]
    more = more[len(buffers) : -1]
    copies, places, used = [], [], 0
    for load in plan:
        if len(load) == 1:
            which, _, row, count, col, width, _ = load[0]
            places.append(sources[which].at[pl.ds(row, count), pl.ds(col, width)])
            copies.append([])
            continue
        buffer = buffers[used]
        used += 1
        group = []
        for which, at, row, count, col, width, number in load:
            copy = pltpu.make_async_copy(
                sources[which].at[pl.ds(row, count), pl.ds(col, width)],
                buffer.at[pl.ds(at, count)],
                sem.at[number],
            )
            copy.start()
            group.append(copy)
        places.append(buffer)
        copies.append(group)
    ready = set()

    def get(i):
        if i not in ready:
            ready.add(i)
            for copy in copies[i]:
                copy.wait()
        return places[i]

    body(get, *out_refs, *more)


def stream(name, loads, out_shapes, body, scratch=(), mib=16):
    arrays, spaces = [], []

    def place(array, space):
        for i, known in enumerate(arrays):
            if known is array and spaces[i] is space:
                return i
        arrays.append(array)
        spaces.append(space)
        return len(arrays) - 1

    plan, buffers, number = [], [], 0
    for load in loads:
        steps, at = [], 0
        space = pltpu.VMEM if len(load) == 1 else pltpu.HBM
        for array, row, count, col, width in load:
            steps.append((place(array, space), at, row, count, col, width, number))
            at += count
            number += 1
        plan.append(steps)
        if len(load) > 1:
            buffers.append(pltpu.VMEM((at, load[0][4]), load[0][0].dtype))
    return pl.pallas_call(
        functools.partial(stream_kernel, plan, len(arrays), len(out_shapes), body),
        out_shape=tuple(out_shapes),
        in_specs=[pl.BlockSpec(memory_space=space) for space in spaces],
        out_specs=tuple(pl.BlockSpec(memory_space=pltpu.VMEM) for _ in out_shapes),
        scratch_shapes=buffers + list(scratch) + [pltpu.SemaphoreType.DMA((number,))],
        compiler_params=params(mib),
        cost_estimate=cost(0, 0),
        name=name,
    )(*arrays)


def part(array, col=0, width=None):
    return [(array, 0, array.shape[0], col, array.shape[1] - col if width is None else width)]


def weight(pieces, col, width):
    return [(*piece, col, width) for piece in pieces]


def wide(name, x, blocks, extras=(), body=None, outs=1):
    widths = [width for *_, width in blocks]
    loads = [part(x)]
    for i, block in enumerate(blocks):
        loads.append(weight(*block))
        for extra in extras:
            loads.append(part(extra, sum(widths[:i]), widths[i]))

    def run(get, *out_refs):
        at = 0
        per = 1 + len(extras)
        for i, width in enumerate(widths):
            first = 1 + i * per
            value = dot(get(0)[...], get(first)[...])
            got = [get(first + 1 + j)[...] for j in range(len(extras))]
            values = (value,) if body is None else body(value, *got)
            for ref, result in zip(out_refs, values):
                ref[:, at : at + width] = result.astype(BF16)
            at += width

    shape = shape_of(BF16, x.shape[0], sum(widths))
    result = stream(name, loads, (shape,) * outs, run)
    return result if outs > 1 else result[0]


def gelu_both(up):
    square = up * up
    bend = jnp.tanh(GELU_A * up * (1.0 + GELU_B * square))
    half_one = 0.5 + 0.5 * bend
    inner = GELU_A + (3.0 * GELU_A * GELU_B) * square
    return up * half_one, half_one + 0.5 * up * (1.0 - bend * bend) * inner


def gelu_only(up):
    bend = jnp.tanh(GELU_A * up * (1.0 + GELU_B * (up * up)))
    return up * (0.5 + 0.5 * bend), up


def times_slope(value, slope):
    return (value * slope.astype(F32),)


def times_slope_of(value, up):
    return (value * gelu_both(up.astype(F32))[1],)


def narrow(name, work, extras, out_shapes, body, scratch=(), mib=16):
    loads = []
    for x, x_col, pieces, col, width in work:
        loads += [part(x, x_col, width), weight(pieces, col, width)]
    first = len(loads)
    loads += [extra if isinstance(extra, list) else part(extra) for extra in extras]

    def run(get, *refs):
        out_refs, more = refs[: len(out_shapes)], refs[len(out_shapes) :]
        acc = more[0]
        for j in range(len(work)):
            value = dot_nt(get(2 * j)[...], get(2 * j + 1)[...])
            acc[...] = value if j == 0 else acc[...] + value
        body(acc, *(get(first + i) for i in range(len(extras))), *out_refs, *more[1:])

    depth = sum(count for *_, count in work[0][2])
    return stream(
        name, loads, out_shapes, run, [pltpu.VMEM((work[0][0].shape[0], depth), F32), *scratch], mib
    )


def gradients(name, left, first, count, rights, out_of=None):
    loads = [part(left, first, count)] + [part(right) for right in rights]

    def run(get, *refs):
        *out_refs, turned = refs
        turned[...] = get(0)[...].T
        for i, ref in enumerate(out_refs):
            ref[...] = dot(turned[...], get(1 + i)[...]).astype(BF16)

    shapes = [shape_of(BF16, count, right.shape[1]) for right in rights]
    return stream(name, loads, shapes, run, [pltpu.VMEM((count, left.shape[0]), BF16)])


def sent_columns(name, first, pairs):
    loads = [load for left, right in pairs for load in (part(left, first, first), part(right))]

    def run(get, out_ref, turned):
        at = 0
        for i, (_, right) in enumerate(pairs):
            turned[...] = get(2 * i)[...].T
            n = right.shape[1]
            out_ref[:, at : at + n] = dot(turned[...], get(2 * i + 1)[...]).astype(BF16)
            at += n

    shape = shape_of(BF16, first, sum(right.shape[1] for _, right in pairs))
    return stream(name, loads, (shape,), run, [pltpu.VMEM((first, pairs[0][0].shape[0]), BF16)])[0]


def stack_rows(pieces, widths):
    block = pieces[0].shape[0]
    cuts = [sum(widths[:i]) for i in range(len(widths))]
    if block % 16:
        whole = jnp.concatenate(pieces, axis=0)
        return [whole[:, at : at + width] for at, width in zip(cuts, widths)]

    def run(*refs):
        for i, ref in enumerate(refs[: len(pieces)]):
            for j, out in enumerate(refs[len(pieces) :]):
                out[i * block : (i + 1) * block] = ref[:, cuts[j] : cuts[j] + widths[j]]

    shapes = [shape_of(pieces[0].dtype, block * len(pieces), width) for width in widths]
    return whole_call(run, pieces, shapes, (), "stack_rows")


def qkv_call(inputs, first, n):
    blocks = [(side, i * n, n) for i in range(3) for side in first]
    loads = [part(inputs), weight(first[0], 3 * n, LANES)] + [weight(*block) for block in blocks]

    def run(get, qkv_ref, normed_ref, inverse_ref, gains_ref):
        value = get(0)[...]
        inverse = lax.rsqrt(jnp.mean(value * value, axis=1, keepdims=True) + EPSILON)
        inverse_ref[...] = inverse
        gains = get(1)[...].astype(F32).T[:8]
        gains_ref[...] = gains
        normed_ref[...] = (value * inverse * gains[0:1]).astype(BF16)
        for i in range(len(blocks)):
            qkv_ref[:, i * n : (i + 1) * n] = dot(normed_ref[...], get(2 + i)[...]).astype(BF16)

    seq, width = inputs.shape
    shapes = (
        shape_of(BF16, seq, 6 * n),
        shape_of(BF16, seq, width),
        shape_of(F32, seq, 1),
        shape_of(F32, 8, width),
    )
    return stream("qkv", loads, shapes, run)


def norm_body(row, acc, value_ref, gains_ref, hidden_ref, inverse_ref, normed_ref=None):
    hidden = value_ref[...] + acc[...]
    inverse = lax.rsqrt(jnp.mean(hidden * hidden, axis=1, keepdims=True) + EPSILON)
    hidden_ref[...] = hidden
    inverse_ref[...] = inverse
    if normed_ref is not None:
        normed_ref[...] = (hidden * inverse * gains_ref[row : row + 1, :]).astype(BF16)


def norm_back(value, inverse, gain, grad):
    scaled = grad * gain
    inner = jnp.mean(value * scaled, axis=1, keepdims=True)
    d_value = inverse * scaled - value * (inverse * inverse * inverse) * inner
    return d_value, jnp.sum(grad * value * inverse, axis=0, keepdims=True)


def back_body(row, acc, value_ref, inverse_ref, gains_ref, grad_ref, low_ref, gain_out, hidden_ref=None):
    d_value, d_gain = norm_back(
        value_ref[...], inverse_ref[...], gains_ref[row : row + 1, :], acc[...]
    )
    total = grad_ref[...] + d_value
    low_ref[...] = total.astype(BF16)
    gain_out[...] = d_gain
    if hidden_ref is not None:
        hidden_ref[...] = total


def turn_kernel(grad_ref, order_ref, out_ref):
    out_ref[...] = dot_nt(grad_ref[...], order_ref[...]).astype(BF16)


def small_kernel(heads_half, one_ref, two_ref, three_ref, order_ref, bias_ref, onehot_ref, loss_ref, mine_ref, out_ref):
    width = one_ref.shape[1]
    gains = jnp.concatenate([one_ref[...], two_ref[...], three_ref[...], jnp.zeros((5, width), F32)], axis=0)
    high = gains.astype(BF16)
    rest = (gains - high.astype(F32)).astype(BF16)
    gains = dot_nt(high, order_ref[...]) + dot_nt(rest, order_ref[...])
    out_ref[...] = jnp.zeros_like(out_ref)
    across = width // LANES
    for i in range(3):
        for j in range(across):
            at = i * across + j
            out_ref[at : at + 1, :] = gains[i : i + 1, j * LANES : (j + 1) * LANES]
    at = 3 * across
    lane = lax.broadcasted_iota(jnp.int32, (1, LANES), 1)
    out_ref[at : at + 1, :] = jnp.where(lane == 0, loss_ref[...], 0.0)
    bias = bias_ref[...]
    heads = 2 * heads_half
    row = lax.broadcasted_iota(jnp.int32, (LANES, bias.shape[0]), 0)
    column = lax.broadcasted_iota(jnp.int32, (LANES, bias.shape[0]), 1)
    source = row + jnp.where(mine_ref[...] == 0, 0, heads_half)
    source = jnp.where(source >= heads, source - heads, source)
    pick = jnp.where((column == 8 * (source // 2) + source % 2) & (row < heads), 1.0, 0.0)
    bias = split_dot(pick.astype(BF16), bias)
    high = bias.astype(BF16)
    rest = (bias - high.astype(F32)).astype(BF16)
    table = dot_nt(high, onehot_ref[...]) + dot_nt(rest, onehot_ref[...])
    count = table.shape[1]
    a_row = LANES // count
    for head in range(heads):
        place = head % a_row * count
        line = at + 1 + head // a_row
        out_ref[line : line + 1, place : place + count] = table[head : head + 1, :]


def member_of(seg_ref, sent_count):
    ids = lax.broadcasted_iota(jnp.int32, (sent_count, seg_ref.shape[1]), 0)
    hit = jnp.where(seg_ref[...] == ids, 1.0, 0.0)
    return hit.astype(BF16), jnp.sum(hit, axis=1, keepdims=True)


def tail_body(acc, value_ref, gains_ref, seg_ref, own_ref, other_ref, hidden_ref, inverse_ref, pooled_ref, unit_ref, low_ref, scale_ref, high, rest):
    hidden = value_ref[...] + acc[...]
    inverse = lax.rsqrt(jnp.mean(hidden * hidden, axis=1, keepdims=True) + EPSILON)
    hidden_ref[...] = hidden
    inverse_ref[...] = inverse
    final = hidden_ref[...] * inverse * gains_ref[2:3, :]
    high[...] = final.astype(BF16)
    rest[...] = (final - high[...].astype(F32)).astype(BF16)
    sents, count = member_of(seg_ref, pooled_ref.shape[0])
    pooled = ((dot(sents, high[...]) + dot(sents, rest[...])) / count).astype(BF16)
    pooled_ref[...] = pooled
    half = own_ref.shape[1]
    left = dot(pooled, own_ref[...])
    right = dot(pooled, other_ref[...])
    square = jnp.sum(left * left, axis=1, keepdims=True) + jnp.sum(right * right, axis=1, keepdims=True)
    scale = lax.rsqrt(square + EPSILON)
    scale_ref[...] = scale
    for at, value in ((0, left * scale), (half, right * scale)):
        unit_ref[:, at : at + half] = value
        low_ref[:, at : at + half] = value.astype(BF16)


def head_call(quarters, unit, scale, partner, column, sentence_loads, out_shapes):
    loads = [part(q) for q in (*quarters, unit, scale, partner, column)] + sentence_loads
    quarter = quarters[0].shape[0]
    total = 4 * quarter

    def run(get, loss_ref, embed_ref, *refs):
        *back_refs, every = refs
        for i in range(4):
            every[i * quarter : (i + 1) * quarter] = get(i)[...]
        unit, scale, partner, columns_id = (get(i)[...] for i in range(4, 8))
        partner = as_columns(
            jnp.concatenate([partner, jnp.zeros((1, LANES - partner.shape[1]), jnp.int32)], axis=1)
        )[: partner.shape[1], 0:1]
        own_count = unit.shape[0]
        sims = dot_nt(every[...], every[...]) * SOFTMAX_TEMP
        row = lax.broadcasted_iota(jnp.int32, (total, total), 0)
        column = lax.broadcasted_iota(jnp.int32, (total, total), 1)
        sims = jnp.where(row == column, NEG_FILL, sims)
        top = jnp.max(sims, axis=0, keepdims=True)
        lse_row = top + jnp.log(jnp.sum(jnp.exp(sims - top), axis=0, keepdims=True))
        own = sims[:own_count]
        own_top = jnp.max(own, axis=1, keepdims=True)
        own_lse = own_top + jnp.log(jnp.sum(jnp.exp(own - own_top), axis=1, keepdims=True))
        is_target = columns_id.astype(F32) == partner
        hit = jnp.where(is_target, 1.0, 0.0)
        target = jnp.sum(jnp.where(is_target, own, 0.0), axis=1, keepdims=True)
        loss_ref[...] = jnp.sum(own_lse - target, axis=0, keepdims=True)
        d_rows = (LOSS_SCALE * (jnp.exp(own - own_lse) - hit)).astype(BF16)
        d_cols = (LOSS_SCALE * (jnp.exp(own - lse_row) - hit)).astype(BF16)
        d_unit = SOFTMAX_TEMP * (dot(d_rows, every[...]) + dot(d_cols, every[...]))
        inner = jnp.sum(d_unit * unit, axis=1, keepdims=True)
        d_embed = (scale * (d_unit - unit * inner)).astype(BF16)
        embed_ref[...] = d_embed
        sentence_back(d_embed, [get(8 + i) for i in range(len(sentence_loads))], *back_refs)

    return stream("head", loads, out_shapes, run, [pltpu.VMEM((total, unit.shape[1]), BF16)])


def sentence_call(embed, sentence_loads, out_shapes):
    def run(get, *back_refs):
        sentence_back(get(0)[...], [get(1 + i) for i in range(len(sentence_loads))], *back_refs)

    return stream("sentence", [part(embed)] + sentence_loads, out_shapes, run)


def sentence_back(d_embed, sources, hidden_ref, low_ref, gain_out):
    seg_ref, own_ref, other_ref, value_ref, inverse_ref, gains_ref = sources
    half = own_ref.shape[1]
    d_pooled = dot_nt(d_embed[:, :half], own_ref[...]) + dot_nt(d_embed[:, half:], other_ref[...])
    sents, count = member_of(seg_ref, d_embed.shape[0])
    d_final = split_dot(sents, d_pooled / count, ((0,), (0,)))
    d_value, d_gain = norm_back(value_ref[...], inverse_ref[...], gains_ref[2:3, :], d_final)
    hidden_ref[...] = d_value
    low_ref[...] = d_value.astype(BF16)
    gain_out[...] = d_gain


def whole_call(body, args, out_shapes, scratch=(), name=None):
    return pl.pallas_call(
        body,
        out_shape=tuple(out_shapes),
        in_specs=[pl.BlockSpec(memory_space=pltpu.VMEM)] * len(args),
        out_specs=tuple(pl.BlockSpec(memory_space=pltpu.VMEM) for _ in out_shapes),
        scratch_shapes=scratch,
        compiler_params=params(),
        cost_estimate=cost(0, 0),
        name=name,
    )(*args)


def shape_of(kind, *dims):
    return jax.ShapeDtypeStruct(dims, kind)


def _stack_heads(part):
    lane = lax.broadcasted_iota(jnp.int32, part.shape, 1)
    zero = jnp.zeros_like(part)
    first = lane < LANES // 2
    return jnp.concatenate(
        [jnp.where(first, part, zero), jnp.where(first, zero, part)], axis=0
    )


def _unstack_heads(both):
    half = both.shape[0] // 2
    lane = lax.broadcasted_iota(jnp.int32, (half, LANES), 1)
    return jnp.where(lane < LANES // 2, both[:half], both[half:])


def _pad_keys(pad, ref):
    seq = ref.shape[0]
    pad[0:REACH] = jnp.zeros((REACH, LANES), pad.dtype)
    pad[REACH + seq :] = jnp.zeros((REACH, LANES), pad.dtype)
    pad[REACH : REACH + seq] = ref[...]


def _query_bits(shape):
    return lax.broadcasted_iota(jnp.int32, shape, 0) & (QB - 1)


def as_columns(values):
    count, length = values.shape
    side = max(LANES, length)
    square = jnp.concatenate([values.astype(F32), jnp.zeros((side - count, length), F32)], axis=0)
    return square.T


def attend_forward_kernel(
    q_ref, k_ref, v_ref, segq_ref, segk_ref, rel_ref, ctx_ref, probs_ref, kpad, vpad, mask, scores
):
    seq = q_ref.shape[0]
    blocks = seq // QB
    _pad_keys(kpad, k_ref)
    _pad_keys(vpad, v_ref)

    @pl.when(pl.program_id(0) == 0)
    def _():
        keys = as_columns(segk_ref[...])
        for b in range(blocks):
            same = keys[:, b : b + 1] == segq_ref[b : b + 1, :].astype(F32)
            mask[b] = jnp.where(same, 0.0, NEG_FILL)

    rel = rel_ref[0]
    row = lax.broadcasted_iota(jnp.int32, (2 * QB, WIN), 0)
    bias = jnp.where(row < QB, rel[0:1, :], rel[1:2, :])
    bits = _query_bits((2 * QB, WIN))
    step = 1
    while step < QB:
        bias = jnp.where((bits & step) != 0, pltpu.roll(bias, step, 1), bias)
        step *= 2
    bias = bias.T
    for b in range(blocks):
        query = _stack_heads(q_ref[b * QB : (b + 1) * QB] * jnp.asarray(SCORE_SCALE, BF16))
        scores[b] = dot_nt(kpad[b * QB : b * QB + WIN], query)
    values = scores[...] + bias[None] + mask[...]
    top = jnp.max(values, axis=1, keepdims=True)
    shifted = jnp.exp(values - top)
    total = jnp.sum(shifted, axis=1, keepdims=True)
    probs_ref[0] = (shifted * (1.0 / total)).astype(BF16)
    for b in range(blocks):
        part = dot_tn(probs_ref[0, b], vpad[b * QB : b * QB + WIN])
        ctx_ref[b * QB : (b + 1) * QB] = _unstack_heads(part).astype(BF16)


def attend_backward_kernel(
    q_ref, k_ref, v_ref, dctx_ref, probs_ref, dqkv_ref, dbias_ref,
    kpad, vpad, dk_acc, dv_acc, d_probs, d_low,
):
    seq = q_ref.shape[0]
    pair = pl.program_id(0)
    side = pl.num_programs(0) // 2
    later = pair // side
    q_at = pl.ds(pl.multiple_of(pair * LANES, LANES), LANES)
    k_at = pl.ds(pl.multiple_of((pair + 2 * side + later * side) * LANES, LANES), LANES)
    v_at = pl.ds(pl.multiple_of((pair + 3 * side + later * side) * LANES, LANES), LANES)
    blocks = seq // QB
    _pad_keys(kpad, k_ref)
    _pad_keys(vpad, v_ref)
    dk_acc[...] = jnp.zeros_like(dk_acc)
    dv_acc[...] = jnp.zeros_like(dv_acc)
    for b in range(blocks):
        window = slice(b * QB, b * QB + WIN)
        d_ctx = _stack_heads(dctx_ref[b * QB : (b + 1) * QB])
        d_probs[b] = dot_nt(vpad[window], d_ctx)
        dv_acc[window] += dot(probs_ref[0, b], d_ctx)
    probs = probs_ref[0].astype(F32)
    product = probs * d_probs[...]
    inner = jnp.sum(product, axis=1, keepdims=True)
    d_scores = product - probs * inner
    d_low[...] = d_scores.astype(BF16)
    total = jnp.sum(d_scores, axis=0).T
    for b in range(blocks):
        here = slice(b * QB, (b + 1) * QB)
        window = slice(b * QB, b * QB + WIN)
        query = _stack_heads(q_ref[here] * jnp.asarray(SCORE_SCALE, BF16))
        dk_acc[window] += dot(d_low[b], query)
        d_query = _unstack_heads(dot_tn(d_low[b], kpad[window])) * SCORE_SCALE
        dqkv_ref[here, q_at] = d_query.astype(BF16)
    dqkv_ref[:, k_at] = dk_acc[REACH : REACH + seq].astype(BF16)
    dqkv_ref[:, v_at] = dv_acc[REACH : REACH + seq].astype(BF16)
    bits = _query_bits((2 * QB, WIN))
    step = 1
    while step < QB:
        total = jnp.where((bits & step) != 0, pltpu.roll(total, WIN - step, 1), total)
        step *= 2
    first = jnp.sum(total[:QB], axis=0, keepdims=True)
    second = jnp.sum(total[QB:], axis=0, keepdims=True)
    dbias_ref[0] = jnp.concatenate([first, second, jnp.zeros((6, WIN), F32)], axis=0)


def _qkv_specs(seq, pairs):
    def spec(kind):
        return pl.BlockSpec((seq, LANES), lambda p: (0, kind * pairs + p))

    return [spec(0), spec(1), spec(2)]


def attend_forward(qkv, twice, windows, rel_window):
    seq = qkv.shape[0]
    pairs = rel_window.shape[0]
    blocks = seq // QB
    return pl.pallas_call(
        attend_forward_kernel,
        grid=(pairs,),
        out_shape=(
            jax.ShapeDtypeStruct((seq, pairs * LANES), BF16),
            jax.ShapeDtypeStruct((pairs, blocks, WIN, 2 * QB), BF16),
        ),
        in_specs=_qkv_specs(seq, pairs)
        + [
            pl.BlockSpec((blocks, 2 * QB), lambda p: (0, 0)),
            pl.BlockSpec((blocks, WIN), lambda p: (0, 0)),
            pl.BlockSpec((1, 2, WIN), lambda p: (p, 0, 0)),
        ],
        out_specs=(
            pl.BlockSpec((seq, LANES), lambda p: (0, p)),
            pl.BlockSpec((1, blocks, WIN, 2 * QB), lambda p: (p, 0, 0, 0)),
        ),
        scratch_shapes=[pltpu.VMEM((seq + 2 * REACH, LANES), BF16)] * 2
        + [pltpu.VMEM((blocks, WIN, 2 * QB), F32)] * 2,
        compiler_params=params(),
        cost_estimate=cost(8 * seq * WIN * LANES * pairs * 4, 8 * seq * LANES * pairs),
        name="attend_forward",
    )(qkv, qkv, qkv, twice, windows, rel_window)


def attend_backward(qkv, d_context, probs):
    seq = qkv.shape[0]
    pairs = probs.shape[0]
    blocks = seq // QB
    lane_block = pl.BlockSpec((seq, LANES), lambda p: (0, p))
    return pl.pallas_call(
        attend_backward_kernel,
        grid=(pairs,),
        out_shape=(
            jax.ShapeDtypeStruct((seq, 3 * pairs * LANES), BF16),
            jax.ShapeDtypeStruct((pairs, 8, WIN), F32),
        ),
        in_specs=_qkv_specs(seq, pairs)
        + [
            lane_block,
            pl.BlockSpec((1, blocks, WIN, 2 * QB), lambda p: (p, 0, 0, 0)),
        ],
        out_specs=(
            pl.BlockSpec((seq, 3 * pairs * LANES), lambda p: (0, 0)),
            pl.BlockSpec((1, 8, WIN), lambda p: (p, 0, 0)),
        ),
        scratch_shapes=[pltpu.VMEM((seq + 2 * REACH, LANES), BF16)] * 2
        + [pltpu.VMEM((seq + 2 * REACH, LANES), F32)] * 2
        + [pltpu.VMEM((blocks, WIN, 2 * QB), F32), pltpu.VMEM((blocks, WIN, 2 * QB), BF16)],
        compiler_params=params(),
        cost_estimate=cost(16 * seq * WIN * LANES * pairs * 4, 16 * seq * LANES * pairs),
        name="attend_backward",
    )(qkv, qkv, qkv, d_context, probs)


CORE = 1
CROSS = 2


def hop(value, mask):
    size = lax.axis_size("dp")
    return lax.ppermute(value, "dp", [(i, i ^ mask) for i in range(size)])


def over(value):
    return lax.ppermute(value, "mp", [(0, 1), (1, 0)])


def cross(value):
    return hop(value, CROSS)


def core(value):
    return hop(value, CORE)


def go(waits, *sends, keep=(), join=True):
    values = [value for _, value in sends]
    held = lax.optimization_barrier((*values, *keep, *waits))
    results = [how(value) for (how, _), value in zip(sends, held)]
    if join:
        results = list(lax.optimization_barrier(tuple(results)))
    return results + list(held[len(values) : len(values) + len(keep)])


def slot_masks(size):
    rest = size // 4
    return [z * 4 + x * 2 + c for c in range(2) for x in range(2) for z in range(rest)]


def strides(size):
    found = []
    stride = 4
    while stride < size:
        found.append(stride)
        stride *= 2
    return found


def gather_near(shard, waits, widths=None):
    size = lax.axis_size("dp")
    pieces = [shard]
    stride = 4
    while stride < size:
        radix = min(4, size // stride)
        shard = jnp.concatenate(pieces, axis=0) if len(pieces) > 1 else shard
        sends = [(functools.partial(hop, mask=j * stride), shard) for j in range(1, radix)]
        pieces = [shard] + go(waits, *sends)
        stride *= radix
    return jnp.concatenate(pieces, axis=0) if widths is None else stack_rows(pieces, widths)


def rows(*pieces):
    return jnp.concatenate(pieces, axis=0)


def columns(*pieces):
    return jnp.concatenate(pieces, axis=1)


def gather_weights(start, later, n_one, n_three, early, begin, between):
    size = lax.axis_size("dp")
    steps = strides(size)
    n_two = start.shape[1] - n_one
    n_four = later.shape[1] - n_three
    n_early = n_three * 2 // 3
    if len(steps) == 2:
        got = go((), *((functools.partial(hop, mask=4 * j), start) for j in range(1, 4)))
        more = hop(later, 4)
        one, two = stack_rows([start, *got], (n_one, n_two))
        later = stack_rows([later, more], (n_early, later.shape[1] - n_early))
        wide_step = functools.partial(hop, mask=steps[1])
    else:
        one, two = gather_near(start, (), (n_one, n_two))

        later = [later[:, :n_early], later[:, n_early:]]

        def wide_step(value):
            whole = gather_near(value, ())
            return whole[value.shape[0] :]

    one_x, two_y, more = go(early, (cross, one), (over, two), (wide_step, later[0]))
    (one,) = stack_rows([one, one_x], (n_one,))
    (two,) = stack_rows([two, two_y], (n_two,))
    one_y, two_x, one_c, two_c, more_b = go(
        (), (over, one), (cross, two), (core, one), (core, two), (wide_step, later[1])
    )
    if len(steps) == 2:
        have = later[0].shape[0]

        def put(near_a, near_b, far_a, far_b, three_ref, four_ref):
            for at, left, right in ((0, near_a, near_b), (have, far_a, far_b)):
                here = slice(at, at + have)
                three_ref[here, :n_early] = left[...]
                three_ref[here, n_early:] = right[:, : n_three - n_early]
                four_ref[here] = right[:, n_three - n_early :]

        three, four = whole_call(
            put,
            (*later, more, more_b),
            (shape_of(BF16, 2 * have, n_three), shape_of(BF16, 2 * have, n_four)),
            (),
            "put_rows",
        )
    else:
        later = rows(columns(*later), columns(more, more_b))
        three, four = later[:, :n_three], later[:, n_three:]
    three_x, four_y, one_yc, two_xc = go((), (cross, three), (over, four), (core, one_y), (core, two_x))
    (three,) = stack_rows([three, three_x], (n_three,))
    (four,) = stack_rows([four, four_y], (four.shape[1],))
    three_y, four_x, three_c, four_c, one, one_c, one_y, one_yc, two, two_x, two_c, two_xc, *early = go(
        (),
        (over, three),
        (cross, four),
        (core, three),
        (core, four),
        keep=(one, one_c, one_y, one_yc, two, two_x, two_c, two_xc, *early),
        join=False,
    )
    first, second = along_x(one, one_c, one_y, one_yc), along_y(two, two_x, two_c, two_xc)
    done = between(begin(first, early), second, early)
    four_xc, three_yc, *done = go(
        (three_y, four_x, three_c, four_c), (core, four_x), (core, three_y), keep=done, join=False
    )
    third, fourth = along_x(three, three_c, three_y, three_yc), along_y(four, four_x, four_c, four_xc)
    return first, second, third, fourth, early, done


def along_x(near, near_c, other, other_c):
    count = near.shape[0]
    return ((near, 0, count), (near_c, 0, count)), ((other, 0, count), (other_c, 0, count))


def along_y(near, side, near_c, side_c):
    count = near.shape[0] // 2
    return tuple(
        tuple((array, at, count) for array in (near, side, near_c, side_c)) for at in (0, count)
    )


def pack(name, sources):
    widths = [count for *_, count in sources]
    block = sources[0][0].shape[0]

    def run(*refs):
        ins, out = refs[: len(sources)], refs[len(sources)]
        buffers, sem = refs[len(sources) + 1 : -1], refs[-1]
        copies = []
        for i, (_, first, count) in enumerate(sources):
            copy = pltpu.make_async_copy(ins[i].at[:, pl.ds(first, count)], buffers[i], sem.at[i])
            copy.start()
            copies.append(copy)
        at = 0
        for copy, buffer, width in zip(copies, buffers, widths):
            copy.wait()
            out[:, at : at + width] = buffer[...]
            at += width

    return pl.pallas_call(
        run,
        out_shape=shape_of(BF16, block, sum(widths)),
        in_specs=[pl.BlockSpec(memory_space=pltpu.HBM)] * len(sources),
        out_specs=pl.BlockSpec(memory_space=pltpu.VMEM),
        scratch_shapes=[pltpu.VMEM((block, width), BF16) for width in widths]
        + [pltpu.SemaphoreType.DMA((len(sources),))],
        compiler_params=params(60),
        cost_estimate=cost(0, 0),
        name=name,
    )(*(array for array, *_ in sources))


def gather_dp(shard):
    near = gather_near(shard, ())
    side, c_near = go((near,), (cross, near), (core, near))
    return near, side, c_near, core(side)


def low(value):
    return value.astype(BF16)


def add(left, right):
    return (left.astype(F32) + right.astype(F32)).astype(BF16)


def product(left, begin, end, right, got=None):
    value = dot_tn(left[:, begin:end], right)
    if got is not None:
        value = value + got.astype(F32)
    return low(value)


def rest_start(value):
    half = value.shape[0] // 2
    return value[half:], value[:half]


def sum_half(value, send):
    gone, stays = rest_start(value)
    return stays + send(low(gone)).astype(F32)


def rest_hops(size):
    return [functools.partial(hop, mask=stride) for stride in reversed(strides(size))]


def shards(
    tokens,
    seg_ids,
    buckets,
    labels,
    w_query,
    w_key,
    w_value,
    w_out,
    w_in,
    w_back,
    gain_attn,
    gain_ffn,
    gain_final,
    w_pool,
    rel_table,
):
    micro_count, seq, width = tokens.shape
    size = lax.axis_size("dp")
    me = lax.axis_index("dp")
    mine = lax.axis_index("mp")
    block = width // size
    inner_half = w_query.shape[1]
    hidden_half = w_in.shape[1]
    sent_local = labels.shape[1]
    bucket_count = rel_table.shape[0]
    heads_half = rel_table.shape[1]
    masks = slot_masks(size)

    x_own = lax.dynamic_index_in_dim(tokens, mine, 0, keepdims=False)
    segments = lax.dynamic_index_in_dim(seg_ids, mine, 0, keepdims=False)[0]
    partner = lax.dynamic_index_in_dim(labels, mine, 0, keepdims=False)

    slot_block = jnp.stack([jnp.bitwise_xor(me, m) for m in masks]).astype(jnp.int32)
    source = (slot_block[:, None] * block + jnp.arange(block, dtype=jnp.int32)[None, :]).reshape(-1)
    order = (jnp.arange(width, dtype=jnp.int32)[:, None] == source[None, :]).astype(BF16)
    order = lax.optimization_barrier(order)
    inputs = dot(x_own, order)


    row_f32 = shape_of(F32, seq, width)
    row_low = shape_of(BF16, seq, width)
    column_f32 = shape_of(F32, seq, 1)
    gain_f32 = shape_of(F32, 1, width)
    heads = 3 * inner_half
    piece = hidden_half // 2
    halves = [(side, i * inner_half, inner_half) for side in range(2) for i in range(2)]

    def hidden_blocks(weights, first_col=0):
        return [(weights[side], first_col + col, n) for side, col, n in halves]

    def begin(first, early):
        inputs, rel_window, twice, windows, *_ = early
        qkv, normed1_low, inverse1, gains = qkv_call(inputs, first, inner_half)
        context, probs = attend_forward(qkv, twice, windows, rel_window)
        return qkv, normed1_low, inverse1, gains, context, probs

    def between(started, second, early):
        qkv, normed1_low, inverse1, gains, context, probs = started
        inputs = early[0]
        hidden1, inverse2, normed2_low = narrow(
            "attn_out",
            [(context, i * inner_half, second[i], piece, inner_half) for i in range(2)],
            (inputs, gains),
            (row_f32, column_f32, row_low),
            functools.partial(norm_body, 1),
        )
        act0, slope0 = wide("act0", normed2_low, hidden_blocks(second), (), gelu_both, 2)
        return normed1_low, inverse1, gains, qkv, context, probs, hidden1, inverse2, normed2_low, act0, slope0

    gains_col = jnp.pad(
        jnp.stack([gain_attn, gain_ffn, gain_final], axis=1), ((0, 0), (0, LANES - 3))
    )
    pool_half = w_pool.shape[1] // 2
    pool_own = lax.dynamic_slice_in_dim(w_pool, mine * pool_half, pool_half, axis=1)
    back_shard = w_back.T
    if block % 16:
        start = columns(w_query, w_key, w_value, gains_col, w_in[:, :piece], w_out.T)
        later = columns(back_shard[:, :piece], pool_own, w_in[:, piece:], back_shard[:, piece:])
    else:
        start = pack(
            "pack_start",
            [(w, 0, inner_half) for w in (w_query, w_key, w_value)]
            + [(gains_col, 0, LANES), (w_in, 0, piece), (w_out.T, 0, inner_half)],
        )
        back_shard, w_in, _ = lax.optimization_barrier((back_shard, w_in, start))
        later = pack(
            "pack_later",
            [
                (back_shard, 0, piece),
                (pool_own, 0, pool_half),
                (w_in, piece, piece),
                (back_shard, piece, piece),
            ],
        )
    rel_other = over(lax.optimization_barrier((rel_table, start))[0])
    rel_all = jnp.concatenate([rel_table, rel_other], axis=1).astype(F32)
    near_buckets = lax.slice_in_dim(buckets, seq - 1 - REACH, seq - 1 - REACH + WIN)
    onehot = (near_buckets[None, :] == jnp.arange(bucket_count, dtype=jnp.int32)[:, None]).astype(F32)
    onehot = lax.optimization_barrier(low(onehot))
    rel_window = dot(rel_all, onehot.astype(F32), ((0,), (0,)), HIGHEST).reshape(heads_half, 2, WIN)
    padded = jnp.pad(segments, (REACH, REACH), constant_values=-1)
    windows = jnp.stack([padded[at : at + WIN] for at in range(0, seq, QB)])
    twice = jnp.tile(segments.reshape(seq // QB, QB), (1, 2))
    local_ids = jnp.arange(sent_local, dtype=jnp.int32)
    column_id = (slot_block[:, None] * sent_local + local_ids[None, :]).reshape(1, -1)
    early = (
        inputs, rel_window, twice, windows, order, onehot, column_id, partner[None, :], segments[None, :], mine.reshape(1, 1),
        (me * block).astype(jnp.uint32), (mine * heads_half).astype(jnp.uint32)
    )
    first, second, third, fourth, early, done = gather_weights(
        start,
        later,
        heads + LANES,
        piece + pool_half,
        early,
        begin,
        between,
    )
    inputs, rel_window, twice, windows, order, onehot, column_id, partner, seg_lane, mine_array, gain_at, table_at = early
    normed1_low, inverse1, gains, qkv, context, probs, hidden1, inverse2, normed2_low, act0, slope0 = done

    act1, up_kept = wide("act1", normed2_low, hidden_blocks(fourth), (), gelu_only, 2)
    pool_loads = [weight(side, piece, pool_half) for side in third]
    hidden2, inverse3, pooled_low, unit, unit_low, scale = narrow(
        "ffn_out",
        [(act0, i * piece, third[i], 0, piece) for i in range(2)]
        + [(act1, i * piece, fourth[i], piece, piece) for i in range(2)],
        (hidden1, gains, seg_lane, *pool_loads),
        (
            row_f32,
            column_f32,
            shape_of(BF16, sent_local, width),
            shape_of(F32, sent_local, width),
            shape_of(BF16, sent_local, width),
            shape_of(F32, sent_local, 1),
        ),
        tail_body,
        [pltpu.VMEM((seq, width), BF16)] * 2,
    )
    quarters = gather_dp(unit_low)

    total_sent = column_id.shape[1]
    sentence_loads = [part(seg_lane), *pool_loads, part(hidden2), part(inverse3), part(gains)]
    back_shapes = (row_f32, row_low, gain_f32)
    if total_sent <= 1024:
        loss_local, embed_low, d_hidden2, ffn_low, d_gain3 = head_call(
            quarters,
            unit,
            scale,
            partner,
            column_id,
            sentence_loads,
            (shape_of(F32, 1, 1), shape_of(BF16, sent_local, width), *back_shapes),
        )
    else:
        every = rows(*quarters)
        position = jnp.arange(total_sent, dtype=jnp.int32)
        sims = dot_nt(every, every) * SOFTMAX_TEMP
        sims = jnp.where(position[:, None] == position[None, :], NEG_FILL, sims)
        lse_row = jax.nn.logsumexp(sims, axis=0, keepdims=True)
        own_sims = sims[:sent_local]
        own_lse = jax.nn.logsumexp(own_sims, axis=1, keepdims=True)
        is_target = column_id == partner.reshape(-1, 1)
        target = jnp.sum(jnp.where(is_target, own_sims, 0.0), axis=-1, keepdims=True)
        loss_local = jnp.sum(own_lse - target)
        hit = is_target.astype(F32)
        d_rows = low(LOSS_SCALE * (jnp.exp(own_sims - own_lse) - hit))
        d_cols = low(LOSS_SCALE * (jnp.exp(own_sims - lse_row) - hit))
        d_unit = SOFTMAX_TEMP * (dot(d_rows, every) + dot(d_cols, every))
        embed_low = low(scale * (d_unit - unit * jnp.sum(d_unit * unit, axis=-1, keepdims=True)))
        d_hidden2, ffn_low, d_gain3 = sentence_call(embed_low, sentence_loads, back_shapes)

    half = width // 2
    quarter = width // 4

    back0_sent, back1_sent = gradients("back_sent", ffn_low, half, half, (act0, act1))
    (pool_sent,) = gradients("pool_sent", pooled_low, half, half, (embed_low,))
    back0_got, back1_got, pool_got, ffn_later = go(
        (), (core, back0_sent), (core, back1_sent), (core, pool_sent), keep=(ffn_low,), join=False
    )
    pool_hi = product(pooled_low, quarter, half, embed_low, pool_got[quarter:])
    pool_lo = product(pooled_low, 0, quarter, embed_low, pool_got[:quarter])
    up0 = wide("up0", ffn_later, hidden_blocks(third), (slope0,), times_slope)

    back_hi = product(ffn_low, quarter, half, act0, back0_got[quarter:])
    back_lo = product(ffn_low, 0, quarter, act0, back0_got[:quarter])
    back_own = product(ffn_low, 0, half, act1[:, :piece], back1_got[:, :piece])
    back_oth = product(ffn_low, 0, half, act1[:, piece:], back1_got[:, piece:])
    got_lo, got_own, got_pool, ffn_later, up0, back_lo, back_own, pool_lo = go(
        (),
        (cross, back_hi),
        (over, back_oth),
        (cross, pool_hi),
        keep=(ffn_later, up0, back_lo, back_own, pool_lo),
    )
    up1 = wide("up1", ffn_later, hidden_blocks(fourth, piece), (up_kept,), times_slope_of)
    in0_sent, in1_sent = gradients("in_sent", normed2_low, half, half, (up0, up1))
    in0_got, in1_got, up0, up1 = go((), (core, in0_sent), (core, in1_sent), keep=(up0, up1))
    attn_low, d_gain2, d_hidden1 = narrow(
        "ffn_in_back",
        [(up0, i * piece, second[i], 0, piece) for i in range(2)]
        + [(up1, i * piece, fourth[i], 0, piece) for i in range(2)],
        (hidden1, inverse2, gains, d_hidden2),
        (row_low, gain_f32, row_f32),
        functools.partial(back_body, 1),
    )
    d_context = wide("d_context", attn_low, [(second[side], piece, inner_half) for side in range(2)])

    pool_lo = add(pool_lo, got_pool)
    back_lo = add(back_lo, got_lo)
    back_own = add(back_own, got_own)
    in_hi = product(normed2_low, quarter, half, up0, in0_got[quarter:])
    in_lo = product(normed2_low, 0, quarter, up0, in0_got[:quarter])
    in_own = product(normed2_low, 0, half, up1[:, :piece], in1_got[:, :piece])
    in_oth = product(normed2_low, 0, half, up1[:, piece:], in1_got[:, piece:])
    got_first, got_x, got_in_own, d_context, pool_lo, back_lo, back_own, in_lo, in_own = go(
        (got_lo, got_own),
        (over, columns(back_lo[:, piece:], pool_lo[:, pool_half:])),
        (cross, columns(back_own[quarter:], in_hi)),
        (over, in_oth),
        keep=(d_context, pool_lo, back_lo, back_own, in_lo, in_own),
        join=False,
    )
    d_qkv, d_bias = attend_backward(qkv, d_context, probs)
    query_both = 2 * inner_half
    late_sent = sent_columns("late_sent", half, ((attn_low, context), (normed1_low, d_qkv)))
    late_got, d_qkv_later = go((), (core, late_sent), keep=(d_qkv,), join=False)
    grad_slots, d_gain1 = narrow(
        "qkv_back",
        [(d_qkv_later, i * inner_half, first[i], 0, inner_half) for i in range(2)]
        + [(d_qkv_later, (1 + i) * query_both, first[i], inner_half, query_both) for i in range(2)],
        (inputs, inverse1, gains, d_hidden1),
        (row_low, gain_f32),
        functools.partial(back_body, 0),
    )

    table_row = 3 * (width // LANES) + 1
    table_rows = -(-2 * heads_half * bucket_count // LANES)
    small_rows = -(-(table_row + table_rows) // 8) * 8
    (flat,) = whole_call(
        functools.partial(small_kernel, heads_half),
        (d_gain1, d_gain2, d_gain3, order, d_bias.reshape(-1, WIN), onehot, loss_local.reshape(1, 1), mine_array),
        (shape_of(F32, small_rows, LANES),),
        (),
        "small",
    )
    (grad_own,) = whole_call(turn_kernel, (grad_slots, order), (row_low,), (), "turn")
    flat_got, flat = go((), (over, flat), keep=(flat,), join=False)
    got_first, got_x, got_in_own = lax.optimization_barrier((got_first, got_x, got_in_own))
    flat = flat + flat_got
    got_second, got_in_lo = got_x[:, :piece], got_x[:, piece:]

    far = rest_hops(size)
    back_all = columns(
        add(back_lo[:, :piece], got_first[:, :piece]),
        add(back_own[:quarter], got_second),
        add(pool_lo[:, :pool_half], got_first[:, piece:]),
    )
    back_rest, back_stay = rest_start(back_all)
    in_lo = add(in_lo, got_in_lo)
    in_own = add(in_own, got_in_own)
    out_got, qkv_got = late_got[:, :query_both], late_got[:, query_both:]
    out_hi = product(attn_low, quarter, half, context, out_got[quarter:])
    out_lo = product(attn_low, 0, quarter, context, out_got[:quarter])
    query_hi = product(normed1_low, quarter, half, d_qkv[:, :query_both], qkv_got[quarter:, :query_both])
    query_lo = product(normed1_low, 0, quarter, d_qkv[:, :query_both], qkv_got[:quarter, :query_both])
    kv_own = product(
        normed1_low, 0, half, d_qkv[:, query_both : 2 * query_both], qkv_got[:, query_both : 2 * query_both]
    )
    kv_oth = product(normed1_low, 0, half, d_qkv[:, 2 * query_both :], qkv_got[:, 2 * query_both :])
    rest_hop = [functools.partial(hop, mask=j * 4) for j in range(1, min(4, size // 4))]
    back_more, got_first, got_x, got_kv, flat_got, back_stay, in_lo, in_own, out_lo, query_lo, kv_own, flat = go(
        (grad_own,),
        (far[0], back_rest),
        (over, in_lo[:, piece:]),
        (cross, columns(in_own[quarter:], out_hi, query_hi)),
        (over, kv_oth),
        (core, flat),
        keep=(back_stay, in_lo, in_own, out_lo, query_lo, kv_own, flat),
    )

    count = flat.shape[0]

    def in_two(value):
        high = value.astype(BF16).astype(F32)
        return jnp.concatenate([high, value - high], axis=0).astype(BF16)

    def from_two(pair):
        return pair[:count].astype(F32) + pair[count : 2 * count].astype(F32)

    def late_adds(
        stay, more, in_lo, got_first, in_own, got_x, out_lo, query_lo, kv_own, got_kv, flat, got_flat, *outs
    ):
        back_gone, back_keep, in_gone, in_keep, heads_gone, heads_keep, kv_gone, kv_keep, small = outs
        rows_z = stay.shape[0] // 2
        total = add(stay[...], more[...])
        back_keep[...] = total[:rows_z]
        back_gone[...] = total[rows_z:]
        rows_z = in_lo.shape[0] // 2
        for at, total in (
            (0, add(in_lo[:, :piece], got_first[...])),
            (piece, add(in_own[:quarter], got_x[:, :piece])),
        ):
            in_keep[:, at : at + piece] = total[:rows_z]
            in_gone[:, at : at + piece] = total[rows_z:]
        for i, ref in enumerate((out_lo, query_lo)):
            first_col = piece + i * query_both
            total = add(ref[...], got_x[:, first_col : first_col + query_both])
            heads_keep[:, i * inner_half : (i + 1) * inner_half] = total[:, :inner_half]
            heads_gone[:, i * inner_half : (i + 1) * inner_half] = total[:, inner_half:]
        kv_keep[...] = add(kv_own[:quarter], got_kv[:quarter])
        kv_gone[:, :query_both] = add(kv_own[quarter:], got_kv[quarter:])
        small[...] = flat[...] + got_flat[...]
        kv_gone[:, query_both:] = jnp.zeros((quarter, LANES), BF16)
        pair = in_two(small[...])
        kv_gone[: 2 * count, query_both:] = pair
        small[...] = from_two(pair)

    cut = [shape_of(BF16, back_stay.shape[0] // 2, back_stay.shape[1])] * 2
    cut += [shape_of(BF16, quarter // 2, hidden_half)] * 2 + [shape_of(BF16, quarter, query_both)] * 2
    cut += [
        shape_of(BF16, quarter, query_both + LANES),
        shape_of(BF16, quarter, query_both),
        shape_of(F32, count, LANES),
    ]
    back_rest, back_stay, in_rest, in_stay, heads_gone, heads_keep, kv_gone, kv_keep, flat = whole_call(
        late_adds,
        (back_stay, back_more, in_lo, got_first, in_own, got_x, out_lo, query_lo, kv_own, got_kv, flat, flat_got),
        cut,
        (),
        "late_adds",
    )
    early_rows = seq // 4
    back_more, in_more, got_first, got_second, grad_other, back_stay, in_stay, heads_keep, kv_keep, flat = go(
        (),
        (far[1], back_rest),
        (far[0], in_rest),
        (over, heads_gone),
        (cross, kv_gone),
        (over, grad_own[:early_rows]),
        keep=(back_stay, in_stay, heads_keep, kv_keep, flat),
    )

    def finish(value):
        value = value.astype(F32)
        for send in far[2:]:
            value = sum_half(value, send)
        return value

    n_last = query_both + query_both
    if len(far) == 2:
        rest = block
        late_rows = seq - early_rows

        def last_adds(stay, more, heads_ref, got_heads, kv_ref, got_kv, flat_ref, back_ref, back_got, own_ref, *outs):
            one, two, three, in_keep, keep, flat_out, tail, pool_ref = outs
            pool = add(back_ref[:, hidden_half:], back_got[:, hidden_half:])
            pool_ref[...] = pool
            tail[:late_rows] = own_ref[early_rows:]
            tail[late_rows:, :pool_half] = pool
            tail[late_rows:, pool_half:] = jnp.zeros((rest, width - pool_half), BF16)
            total = add(stay[...], more[...])
            in_keep[...] = total[:rest]
            one[:, LANES : LANES + hidden_half] = total[rest:]
            pair = in_two(flat_ref[...] + from_two(got_kv[:, query_both:]))
            flat_out[...] = from_two(pair)
            for i, (ref, at) in enumerate(((keep, 0), (one, LANES + hidden_half), (two, LANES), (three, LANES))):
                here = slice(i * rest, (i + 1) * rest)
                if i:
                    ref[:, :LANES] = pair
                ref[:, at : at + query_both] = add(heads_ref[here], got_heads[here])
                ref[:, at + query_both : at + n_last] = add(kv_ref[here], got_kv[here, :query_both])

        one, two, three, in_stay, last_stay, flat, tail, grad_pool = whole_call(
            last_adds,
            (in_stay, in_more, heads_keep, got_first, kv_keep, got_second, flat, back_stay, back_more, grad_own),
            (
                shape_of(BF16, rest, LANES + hidden_half + n_last),
                shape_of(BF16, rest, LANES + n_last),
                shape_of(BF16, rest, LANES + n_last),
                shape_of(BF16, rest, hidden_half),
                shape_of(BF16, rest, n_last),
                shape_of(F32, count, LANES),
                shape_of(BF16, late_rows + rest, width),
                shape_of(BF16, rest, pool_half),
            ),
            (),
            "last_adds",
        )
        got_one, got_two, got_three, got_tail, back_stay, back_more = go(
            (),
            (rest_hop[0], one),
            (rest_hop[1], two),
            (rest_hop[2], three),
            (over, tail),
            keep=(back_stay, back_more),
            join=False,
        )

        def back_final(stay, more, back_ref):
            back_ref[...] = stay[:, :hidden_half].astype(F32) + more[:, :hidden_half].astype(F32)

        (grad_back,) = whole_call(
            back_final, (back_stay, back_more), (shape_of(F32, rest, hidden_half),), (), "back_final"
        )

        def tokens_final(mine_ref, own_ref, first_ref, tail_ref, pool_own, out_ref, pool_ref):
            first = mine_ref[...] == 0
            own, other = pool_own[...].astype(F32), tail_ref[late_rows:, :pool_half].astype(F32)
            pool_ref[:, :pool_half] = jnp.where(first, own, other)
            pool_ref[:, pool_half:] = jnp.where(first, other, own)
            for at, count, ref in ((0, early_rows, first_ref), (early_rows, late_rows, tail_ref)):
                here = slice(at, at + count)
                own, other = own_ref[here].astype(F32), ref[:count].astype(F32)
                out_ref[0, here] = jnp.where(first, own, other).astype(BF16)
                out_ref[1, here] = jnp.where(first, other, own).astype(BF16)

        grad_tokens, grad_pool = whole_call(
            tokens_final,
            (mine_array, grad_own, grad_other, got_tail, grad_pool),
            (shape_of(BF16, 2, seq, width), shape_of(F32, rest, 2 * pool_half)),
            (),
            "tokens_final",
        )
        got_one, got_two, got_three, grad_tokens = lax.optimization_barrier(
            (got_one, got_two, got_three, grad_tokens)
        )

        def last_final(stay, in_keep, one_ref, two_ref, three_ref, flat_ref, *outs):
            in_ref, out_ref, q_ref, k_ref, v_ref, flat_out = outs
            in_ref[...] = in_keep[...].astype(F32) + one_ref[:, LANES : LANES + hidden_half].astype(F32)
            total = stay[...].astype(F32) + one_ref[:, LANES + hidden_half :].astype(F32)
            total = total + two_ref[:, LANES:].astype(F32) + three_ref[:, LANES:].astype(F32)
            for i, ref in enumerate((out_ref, q_ref, k_ref, v_ref)):
                ref[...] = total[:, i * inner_half : (i + 1) * inner_half]
            small = flat_ref[...]
            for ref in (one_ref, two_ref, three_ref):
                small = small + from_two(ref[:, :LANES])
            flat_out[...] = small

        head_shape = shape_of(F32, rest, inner_half)
        grad_in, grad_out, grad_query, grad_key, grad_value, flat = whole_call(
            last_final,
            (last_stay, in_stay, got_one, got_two, got_three, flat),
            (shape_of(F32, rest, hidden_half), *(head_shape,) * 4, shape_of(F32, count, LANES)),
            (),
            "last_final",
        )
    else:
        flat = flat + from_two(got_second[:, query_both:])
        grad_other = rows(grad_other, over(grad_own[early_rows:]))
        in_rest, in_stay = rest_start(add(in_stay, in_more))
        last = columns(add(heads_keep, got_first), add(kv_keep, got_second[:, :query_both]))
        last_rest, last_stay = rest_start(last)
        in_more, last_more, *flat_got = go(
            (), (far[1], in_rest), (far[0], last_rest), *((how, flat) for how in rest_hop)
        )
        last_rest, last_stay = rest_start(add(last_stay, last_more))
        last_more = far[1](last_rest)
        flat = flat + sum(flat_got)
        for send in far[:-2]:
            flat = flat + send(flat)
        grad_last = finish(last_stay.astype(F32) + last_more.astype(F32))
        grad_in = finish(in_stay.astype(F32) + in_more.astype(F32))
        back_all = finish(back_stay.astype(F32) + back_more.astype(F32))
        grad_back, grad_pool = back_all[:, :hidden_half], back_all[:, hidden_half:]
        pool_other = over(grad_pool)
        grad_pool = jnp.where(mine == 0, columns(grad_pool, pool_other), columns(pool_other, grad_pool))
        grad_out, grad_query, grad_key, grad_value = (
            grad_last[:, i * inner_half : (i + 1) * inner_half] for i in range(4)
        )
        grad_tokens = jnp.where(
            mine == 0, jnp.stack([grad_own, grad_other]), jnp.stack([grad_other, grad_own])
        )
    across = width // LANES
    zero = jnp.uint32(0)
    gains_mine = lax.dynamic_slice(flat[: 3 * across].reshape(3, width), (zero, gain_at), (3, block))
    loss = flat[3 * across, 0] / (micro_count * sent_local * size)
    table_sum = flat[table_row : table_row + table_rows].reshape(-1, bucket_count)[: 2 * heads_half]
    table_mine = lax.dynamic_slice(table_sum, (table_at, zero), (heads_half, bucket_count)).T
    return (
        loss,
        grad_tokens,
        grad_query,
        grad_key,
        grad_value,
        grad_out.T,
        grad_in,
        grad_back.T,
        gains_mine[0],
        gains_mine[1],
        gains_mine[2],
        grad_pool,
        table_mine,
    )


def solution(mesh):
    placed = (
        P(None, "dp", None),
        P(None, "dp", None),
        P(),
        P(None, "dp"),
        P("dp", "mp"),
        P("dp", "mp"),
        P("dp", "mp"),
        P("mp", "dp"),
        P("dp", "mp"),
        P("mp", "dp"),
        P("dp"),
        P("dp"),
        P("dp"),
        P("dp", None),
        P(None, "mp"),
    )
    return jax.shard_map(
        shards,
        mesh=mesh,
        in_specs=placed,
        out_specs=(
            P(),
            P(None, "dp", None),
            P("dp", "mp"),
            P("dp", "mp"),
            P("dp", "mp"),
            P("mp", "dp"),
            P("dp", "mp"),
            P("mp", "dp"),
            P("dp"),
            P("dp"),
            P("dp"),
            P("dp", None),
            P(None, "mp"),
        ),
        check_vma=False,
    )
```

```python
import functools

import jax
import jax.numpy as jnp
from jax import lax
from jax.experimental import pallas as pl
from jax.experimental.pallas import tpu as pltpu
from jax.sharding import PartitionSpec as P

NEG_FILL = -1000000000.0
SCORE_SCALE = 0.125
SOFTMAX_TEMP = 50.0
LOSS_SCALE = 64.0
EPSILON = 1e-06
REACH = 32
QB = 64
WIN = QB + 2 * REACH
LANES = 128
GELU_A = 0.7978845608028654
GELU_B = 0.044715

BF16 = jnp.bfloat16
F32 = jnp.float32
HIGHEST = lax.Precision.HIGHEST


def dot(left, right, dims=((1,), (0,)), precision=None):
    return lax.dot_general(
        left, right, (dims, ((), ())), precision=precision, preferred_element_type=F32
    )


def dot_nt(left, right):
    return dot(left, right, ((1,), (1,)))


def dot_tn(left, right):
    return dot(left, right, ((0,), (0,)))


def rms_forward(value, gain):
    inverse = lax.rsqrt(jnp.mean(value * value, axis=-1, keepdims=True) + EPSILON)
    return (value * inverse * gain, inverse)


def cost(flops, bytes_accessed):
    return pl.CostEstimate(flops=0, bytes_accessed=0, transcendentals=0)


def params(mib=16):
    return pltpu.CompilerParams(vmem_limit_bytes=mib * 2**20)


def split_dot(left, right, dims=((1,), (0,))):
    high = right.astype(BF16)
    rest = (right - high.astype(F32)).astype(BF16)
    return dot(left, high, dims) + dot(left, rest, dims)


def stream_kernel(plan, operands, outs, body, *refs):
    sources, out_refs = refs[:operands], refs[operands : operands + outs]
    more = refs[operands + outs :]
    buffers, sem = more[: sum(len(load) > 1 for load in plan)], more[-1]
    more = more[len(buffers) : -1]
    copies, places, used = [], [], 0
    for load in plan:
        if len(load) == 1:
            which, _, row, count, col, width, _ = load[0]
            places.append(sources[which].at[pl.ds(row, count), pl.ds(col, width)])
            copies.append([])
            continue
        buffer = buffers[used]
        used += 1
        group = []
        for which, at, row, count, col, width, number in load:
            copy = pltpu.make_async_copy(
                sources[which].at[pl.ds(row, count), pl.ds(col, width)],
                buffer.at[pl.ds(at, count)],
                sem.at[number],
            )
            copy.start()
            group.append(copy)
        places.append(buffer)
        copies.append(group)
    ready = set()

    def get(i):
        if i not in ready:
            ready.add(i)
            for copy in copies[i]:
                copy.wait()
        return places[i]

    body(get, *out_refs, *more)


def stream(name, loads, out_shapes, body, scratch=(), mib=16):
    arrays, spaces = [], []

    def place(array, space):
        for i, known in enumerate(arrays):
            if known is array and spaces[i] is space:
                return i
        arrays.append(array)
        spaces.append(space)
        return len(arrays) - 1

    plan, buffers, number = [], [], 0
    for load in loads:
        steps, at = [], 0
        space = pltpu.VMEM if len(load) == 1 else pltpu.HBM
        for array, row, count, col, width in load:
            steps.append((place(array, space), at, row, count, col, width, number))
            at += count
            number += 1
        plan.append(steps)
        if len(load) > 1:
            buffers.append(pltpu.VMEM((at, load[0][4]), load[0][0].dtype))
    return pl.pallas_call(
        functools.partial(stream_kernel, plan, len(arrays), len(out_shapes), body),
        out_shape=tuple(out_shapes),
        in_specs=[pl.BlockSpec(memory_space=space) for space in spaces],
        out_specs=tuple(pl.BlockSpec(memory_space=pltpu.VMEM) for _ in out_shapes),
        scratch_shapes=buffers + list(scratch) + [pltpu.SemaphoreType.DMA((number,))],
        compiler_params=params(mib),
        cost_estimate=cost(0, 0),
        name=name,
    )(*arrays)


def part(array, col=0, width=None):
    return [(array, 0, array.shape[0], col, array.shape[1] - col if width is None else width)]


def weight(pieces, col, width):
    return [(*piece, col, width) for piece in pieces]


def wide(name, x, blocks, extras=(), body=None, outs=1):
    widths = [width for *_, width in blocks]
    loads = [part(x)]
    for i, block in enumerate(blocks):
        loads.append(weight(*block))
        for extra in extras:
            loads.append(part(extra, sum(widths[:i]), widths[i]))

    def run(get, *out_refs):
        at = 0
        per = 1 + len(extras)
        for i, width in enumerate(widths):
            first = 1 + i * per
            value = dot(get(0)[...], get(first)[...])
            got = [get(first + 1 + j)[...] for j in range(len(extras))]
            values = (value,) if body is None else body(value, *got)
            for ref, result in zip(out_refs, values):
                ref[:, at : at + width] = result.astype(BF16)
            at += width

    shape = shape_of(BF16, x.shape[0], sum(widths))
    result = stream(name, loads, (shape,) * outs, run)
    return result if outs > 1 else result[0]


def gelu_both(up):
    square = up * up
    bend = jnp.tanh(GELU_A * up * (1.0 + GELU_B * square))
    half_one = 0.5 + 0.5 * bend
    inner = GELU_A + (3.0 * GELU_A * GELU_B) * square
    return up * half_one, half_one + 0.5 * up * (1.0 - bend * bend) * inner


def gelu_only(up):
    bend = jnp.tanh(GELU_A * up * (1.0 + GELU_B * (up * up)))
    return up * (0.5 + 0.5 * bend), up


def times_slope(value, slope):
    return (value * slope.astype(F32),)


def times_slope_of(value, up):
    return (value * gelu_both(up.astype(F32))[1],)


def narrow(name, work, extras, out_shapes, body, scratch=(), mib=16):
    loads = []
    for x, x_col, pieces, col, width in work:
        loads += [part(x, x_col, width), weight(pieces, col, width)]
    first = len(loads)
    loads += [extra if isinstance(extra, list) else part(extra) for extra in extras]

    def run(get, *refs):
        out_refs, more = refs[: len(out_shapes)], refs[len(out_shapes) :]
        acc = more[0]
        for j in range(len(work)):
            value = dot_nt(get(2 * j)[...], get(2 * j + 1)[...])
            acc[...] = value if j == 0 else acc[...] + value
        body(acc, *(get(first + i) for i in range(len(extras))), *out_refs, *more[1:])

    depth = sum(count for *_, count in work[0][2])
    return stream(
        name, loads, out_shapes, run, [pltpu.VMEM((work[0][0].shape[0], depth), F32), *scratch], mib
    )


def gradients(name, left, first, count, rights, out_of=None):
    loads = [part(left, first, count)] + [part(right) for right in rights]

    def run(get, *refs):
        *out_refs, turned = refs
        turned[...] = get(0)[...].T
        for i, ref in enumerate(out_refs):
            ref[...] = dot(turned[...], get(1 + i)[...]).astype(BF16)

    shapes = [shape_of(BF16, count, right.shape[1]) for right in rights]
    return stream(name, loads, shapes, run, [pltpu.VMEM((count, left.shape[0]), BF16)])


def sent_columns(name, first, pairs):
    loads = [load for left, right in pairs for load in (part(left, first, first), part(right))]

    def run(get, out_ref, turned):
        at = 0
        for i, (_, right) in enumerate(pairs):
            turned[...] = get(2 * i)[...].T
            n = right.shape[1]
            out_ref[:, at : at + n] = dot(turned[...], get(2 * i + 1)[...]).astype(BF16)
            at += n

    shape = shape_of(BF16, first, sum(right.shape[1] for _, right in pairs))
    return stream(name, loads, (shape,), run, [pltpu.VMEM((first, pairs[0][0].shape[0]), BF16)])[0]


def stack_rows(pieces, widths):
    block = pieces[0].shape[0]
    cuts = [sum(widths[:i]) for i in range(len(widths))]
    if block % 16:
        whole = jnp.concatenate(pieces, axis=0)
        return [whole[:, at : at + width] for at, width in zip(cuts, widths)]

    def run(*refs):
        for i, ref in enumerate(refs[: len(pieces)]):
            for j, out in enumerate(refs[len(pieces) :]):
                out[i * block : (i + 1) * block] = ref[:, cuts[j] : cuts[j] + widths[j]]

    shapes = [shape_of(pieces[0].dtype, block * len(pieces), width) for width in widths]
    return whole_call(run, pieces, shapes, (), "stack_rows")


def qkv_call(inputs, first, n):
    blocks = [(side, i * n, n) for i in range(3) for side in first]
    loads = [part(inputs), weight(first[0], 3 * n, LANES)] + [weight(*block) for block in blocks]

    def run(get, qkv_ref, normed_ref, inverse_ref, gains_ref):
        value = get(0)[...]
        inverse = lax.rsqrt(jnp.mean(value * value, axis=1, keepdims=True) + EPSILON)
        inverse_ref[...] = inverse
        gains = get(1)[...].astype(F32).T[:8]
        gains_ref[...] = gains
        normed_ref[...] = (value * inverse * gains[0:1]).astype(BF16)
        for i in range(len(blocks)):
            qkv_ref[:, i * n : (i + 1) * n] = dot(normed_ref[...], get(2 + i)[...]).astype(BF16)

    seq, width = inputs.shape
    shapes = (
        shape_of(BF16, seq, 6 * n),
        shape_of(BF16, seq, width),
        shape_of(F32, seq, 1),
        shape_of(F32, 8, width),
    )
    return stream("qkv", loads, shapes, run)


def norm_body(row, acc, value_ref, gains_ref, hidden_ref, inverse_ref, normed_ref=None):
    hidden = value_ref[...] + acc[...]
    inverse = lax.rsqrt(jnp.mean(hidden * hidden, axis=1, keepdims=True) + EPSILON)
    hidden_ref[...] = hidden
    inverse_ref[...] = inverse
    if normed_ref is not None:
        normed_ref[...] = (hidden * inverse * gains_ref[row : row + 1, :]).astype(BF16)


def norm_back(value, inverse, gain, grad):
    scaled = grad * gain
    inner = jnp.mean(value * scaled, axis=1, keepdims=True)
    d_value = inverse * scaled - value * (inverse * inverse * inverse) * inner
    return d_value, jnp.sum(grad * value * inverse, axis=0, keepdims=True)


def back_body(row, acc, value_ref, inverse_ref, gains_ref, grad_ref, low_ref, gain_out, hidden_ref=None):
    d_value, d_gain = norm_back(
        value_ref[...], inverse_ref[...], gains_ref[row : row + 1, :], acc[...]
    )
    total = grad_ref[...] + d_value
    low_ref[...] = total.astype(BF16)
    gain_out[...] = d_gain
    if hidden_ref is not None:
        hidden_ref[...] = total


def turn_kernel(grad_ref, order_ref, out_ref):
    out_ref[...] = dot_nt(grad_ref[...], order_ref[...]).astype(BF16)


def small_kernel(heads_half, one_ref, two_ref, three_ref, order_ref, bias_ref, onehot_ref, loss_ref, mine_ref, out_ref):
    width = one_ref.shape[1]
    gains = jnp.concatenate([one_ref[...], two_ref[...], three_ref[...], jnp.zeros((5, width), F32)], axis=0)
    high = gains.astype(BF16)
    rest = (gains - high.astype(F32)).astype(BF16)
    gains = dot_nt(high, order_ref[...]) + dot_nt(rest, order_ref[...])
    out_ref[...] = jnp.zeros_like(out_ref)
    across = width // LANES
    for i in range(3):
        for j in range(across):
            at = i * across + j
            out_ref[at : at + 1, :] = gains[i : i + 1, j * LANES : (j + 1) * LANES]
    at = 3 * across
    lane = lax.broadcasted_iota(jnp.int32, (1, LANES), 1)
    out_ref[at : at + 1, :] = jnp.where(lane == 0, loss_ref[...], 0.0)
    bias = bias_ref[...]
    heads = 2 * heads_half
    row = lax.broadcasted_iota(jnp.int32, (LANES, bias.shape[0]), 0)
    column = lax.broadcasted_iota(jnp.int32, (LANES, bias.shape[0]), 1)
    source = row + jnp.where(mine_ref[...] == 0, 0, heads_half)
    source = jnp.where(source >= heads, source - heads, source)
    pick = jnp.where((column == 8 * (source // 2) + source % 2) & (row < heads), 1.0, 0.0)
    bias = split_dot(pick.astype(BF16), bias)
    high = bias.astype(BF16)
    rest = (bias - high.astype(F32)).astype(BF16)
    table = dot_nt(high, onehot_ref[...]) + dot_nt(rest, onehot_ref[...])
    count = table.shape[1]
    a_row = LANES // count
    for head in range(heads):
        place = head % a_row * count
        line = at + 1 + head // a_row
        out_ref[line : line + 1, place : place + count] = table[head : head + 1, :]


def member_of(seg_ref, sent_count):
    ids = lax.broadcasted_iota(jnp.int32, (sent_count, seg_ref.shape[1]), 0)
    hit = jnp.where(seg_ref[...] == ids, 1.0, 0.0)
    return hit.astype(BF16), jnp.sum(hit, axis=1, keepdims=True)


def tail_body(acc, value_ref, gains_ref, seg_ref, own_ref, other_ref, hidden_ref, inverse_ref, pooled_ref, unit_ref, low_ref, scale_ref, high, rest):
    hidden = value_ref[...] + acc[...]
    inverse = lax.rsqrt(jnp.mean(hidden * hidden, axis=1, keepdims=True) + EPSILON)
    hidden_ref[...] = hidden
    inverse_ref[...] = inverse
    final = hidden_ref[...] * inverse * gains_ref[2:3, :]
    high[...] = final.astype(BF16)
    rest[...] = (final - high[...].astype(F32)).astype(BF16)
    sents, count = member_of(seg_ref, pooled_ref.shape[0])
    pooled = ((dot(sents, high[...]) + dot(sents, rest[...])) / count).astype(BF16)
    pooled_ref[...] = pooled
    half = own_ref.shape[1]
    left = dot(pooled, own_ref[...])
    right = dot(pooled, other_ref[...])
    square = jnp.sum(left * left, axis=1, keepdims=True) + jnp.sum(right * right, axis=1, keepdims=True)
    scale = lax.rsqrt(square + EPSILON)
    scale_ref[...] = scale
    for at, value in ((0, left * scale), (half, right * scale)):
        unit_ref[:, at : at + half] = value
        low_ref[:, at : at + half] = value.astype(BF16)


def head_call(quarters, unit, scale, partner, column, sentence_loads, out_shapes):
    loads = [part(q) for q in (*quarters, unit, scale, partner, column)] + sentence_loads
    quarter = quarters[0].shape[0]
    total = 4 * quarter

    def run(get, loss_ref, embed_ref, *refs):
        *back_refs, every = refs
        for i in range(4):
            every[i * quarter : (i + 1) * quarter] = get(i)[...]
        unit, scale, partner, columns_id = (get(i)[...] for i in range(4, 8))
        partner = as_columns(
            jnp.concatenate([partner, jnp.zeros((1, LANES - partner.shape[1]), jnp.int32)], axis=1)
        )[: partner.shape[1], 0:1]
        own_count = unit.shape[0]
        sims = dot_nt(every[...], every[...]) * SOFTMAX_TEMP
        row = lax.broadcasted_iota(jnp.int32, (total, total), 0)
        column = lax.broadcasted_iota(jnp.int32, (total, total), 1)
        sims = jnp.where(row == column, NEG_FILL, sims)
        top = jnp.max(sims, axis=0, keepdims=True)
        lse_row = top + jnp.log(jnp.sum(jnp.exp(sims - top), axis=0, keepdims=True))
        own = sims[:own_count]
        own_top = jnp.max(own, axis=1, keepdims=True)
        own_lse = own_top + jnp.log(jnp.sum(jnp.exp(own - own_top), axis=1, keepdims=True))
        is_target = columns_id.astype(F32) == partner
        hit = jnp.where(is_target, 1.0, 0.0)
        target = jnp.sum(jnp.where(is_target, own, 0.0), axis=1, keepdims=True)
        loss_ref[...] = jnp.sum(own_lse - target, axis=0, keepdims=True)
        d_rows = (LOSS_SCALE * (jnp.exp(own - own_lse) - hit)).astype(BF16)
        d_cols = (LOSS_SCALE * (jnp.exp(own - lse_row) - hit)).astype(BF16)
        d_unit = SOFTMAX_TEMP * (dot(d_rows, every[...]) + dot(d_cols, every[...]))
        inner = jnp.sum(d_unit * unit, axis=1, keepdims=True)
        d_embed = (scale * (d_unit - unit * inner)).astype(BF16)
        embed_ref[...] = d_embed
        sentence_back(d_embed, [get(8 + i) for i in range(len(sentence_loads))], *back_refs)

    return stream("head", loads, out_shapes, run, [pltpu.VMEM((total, unit.shape[1]), BF16)])


def sentence_call(embed, sentence_loads, out_shapes):
    def run(get, *back_refs):
        sentence_back(get(0)[...], [get(1 + i) for i in range(len(sentence_loads))], *back_refs)

    return stream("sentence", [part(embed)] + sentence_loads, out_shapes, run)


def sentence_back(d_embed, sources, hidden_ref, low_ref, gain_out):
    seg_ref, own_ref, other_ref, value_ref, inverse_ref, gains_ref = sources
    half = own_ref.shape[1]
    d_pooled = dot_nt(d_embed[:, :half], own_ref[...]) + dot_nt(d_embed[:, half:], other_ref[...])
    sents, count = member_of(seg_ref, d_embed.shape[0])
    d_final = split_dot(sents, d_pooled / count, ((0,), (0,)))
    d_value, d_gain = norm_back(value_ref[...], inverse_ref[...], gains_ref[2:3, :], d_final)
    hidden_ref[...] = d_value
    low_ref[...] = d_value.astype(BF16)
    gain_out[...] = d_gain


def whole_call(body, args, out_shapes, scratch=(), name=None):
    return pl.pallas_call(
        body,
        out_shape=tuple(out_shapes),
        in_specs=[pl.BlockSpec(memory_space=pltpu.VMEM)] * len(args),
        out_specs=tuple(pl.BlockSpec(memory_space=pltpu.VMEM) for _ in out_shapes),
        scratch_shapes=scratch,
        compiler_params=params(),
        cost_estimate=cost(0, 0),
        name=name,
    )(*args)


def shape_of(kind, *dims):
    return jax.ShapeDtypeStruct(dims, kind)


def _stack_heads(part):
    lane = lax.broadcasted_iota(jnp.int32, part.shape, 1)
    zero = jnp.zeros_like(part)
    first = lane < LANES // 2
    return jnp.concatenate(
        [jnp.where(first, part, zero), jnp.where(first, zero, part)], axis=0
    )


def _unstack_heads(both):
    half = both.shape[0] // 2
    lane = lax.broadcasted_iota(jnp.int32, (half, LANES), 1)
    return jnp.where(lane < LANES // 2, both[:half], both[half:])


def _pad_keys(pad, ref):
    seq = ref.shape[0]
    pad[0:REACH] = jnp.zeros((REACH, LANES), pad.dtype)
    pad[REACH + seq :] = jnp.zeros((REACH, LANES), pad.dtype)
    pad[REACH : REACH + seq] = ref[...]


def _query_bits(shape):
    return lax.broadcasted_iota(jnp.int32, shape, 0) & (QB - 1)


def as_columns(values):
    count, length = values.shape
    side = max(LANES, length)
    square = jnp.concatenate([values.astype(F32), jnp.zeros((side - count, length), F32)], axis=0)
    return square.T


def attend_forward_kernel(
    q_ref, k_ref, v_ref, segq_ref, segk_ref, rel_ref, ctx_ref, probs_ref, kpad, vpad, mask, scores
):
    seq = q_ref.shape[0]
    blocks = seq // QB
    _pad_keys(kpad, k_ref)
    _pad_keys(vpad, v_ref)

    @pl.when(pl.program_id(0) == 0)
    def _():
        keys = as_columns(segk_ref[...])
        for b in range(blocks):
            same = keys[:, b : b + 1] == segq_ref[b : b + 1, :].astype(F32)
            mask[b] = jnp.where(same, 0.0, NEG_FILL)

    rel = rel_ref[0]
    row = lax.broadcasted_iota(jnp.int32, (2 * QB, WIN), 0)
    bias = jnp.where(row < QB, rel[0:1, :], rel[1:2, :])
    bits = _query_bits((2 * QB, WIN))
    step = 1
    while step < QB:
        bias = jnp.where((bits & step) != 0, pltpu.roll(bias, step, 1), bias)
        step *= 2
    bias = bias.T
    for b in range(blocks):
        query = _stack_heads(q_ref[b * QB : (b + 1) * QB] * jnp.asarray(SCORE_SCALE, BF16))
        scores[b] = dot_nt(kpad[b * QB : b * QB + WIN], query)
    values = scores[...] + bias[None] + mask[...]
    top = jnp.max(values, axis=1, keepdims=True)
    shifted = jnp.exp(values - top)
    total = jnp.sum(shifted, axis=1, keepdims=True)
    probs_ref[0] = (shifted * (1.0 / total)).astype(BF16)
    for b in range(blocks):
        part = dot_tn(probs_ref[0, b], vpad[b * QB : b * QB + WIN])
        ctx_ref[b * QB : (b + 1) * QB] = _unstack_heads(part).astype(BF16)


def attend_backward_kernel(
    q_ref, k_ref, v_ref, dctx_ref, probs_ref, dqkv_ref, dbias_ref,
    kpad, vpad, dk_acc, dv_acc, d_probs, d_low,
):
    seq = q_ref.shape[0]
    pair = pl.program_id(0)
    side = pl.num_programs(0) // 2
    later = pair // side
    q_at = pl.ds(pl.multiple_of(pair * LANES, LANES), LANES)
    k_at = pl.ds(pl.multiple_of((pair + 2 * side + later * side) * LANES, LANES), LANES)
    v_at = pl.ds(pl.multiple_of((pair + 3 * side + later * side) * LANES, LANES), LANES)
    blocks = seq // QB
    _pad_keys(kpad, k_ref)
    _pad_keys(vpad, v_ref)
    dk_acc[...] = jnp.zeros_like(dk_acc)
    dv_acc[...] = jnp.zeros_like(dv_acc)
    for b in range(blocks):
        window = slice(b * QB, b * QB + WIN)
        d_ctx = _stack_heads(dctx_ref[b * QB : (b + 1) * QB])
        d_probs[b] = dot_nt(vpad[window], d_ctx)
        dv_acc[window] += dot(probs_ref[0, b], d_ctx)
    probs = probs_ref[0].astype(F32)
    product = probs * d_probs[...]
    inner = jnp.sum(product, axis=1, keepdims=True)
    d_scores = product - probs * inner
    d_low[...] = d_scores.astype(BF16)
    total = jnp.sum(d_scores, axis=0).T
    for b in range(blocks):
        here = slice(b * QB, (b + 1) * QB)
        window = slice(b * QB, b * QB + WIN)
        query = _stack_heads(q_ref[here] * jnp.asarray(SCORE_SCALE, BF16))
        dk_acc[window] += dot(d_low[b], query)
        d_query = _unstack_heads(dot_tn(d_low[b], kpad[window])) * SCORE_SCALE
        dqkv_ref[here, q_at] = d_query.astype(BF16)
    dqkv_ref[:, k_at] = dk_acc[REACH : REACH + seq].astype(BF16)
    dqkv_ref[:, v_at] = dv_acc[REACH : REACH + seq].astype(BF16)
    bits = _query_bits((2 * QB, WIN))
    step = 1
    while step < QB:
        total = jnp.where((bits & step) != 0, pltpu.roll(total, WIN - step, 1), total)
        step *= 2
    first = jnp.sum(total[:QB], axis=0, keepdims=True)
    second = jnp.sum(total[QB:], axis=0, keepdims=True)
    dbias_ref[0] = jnp.concatenate([first, second, jnp.zeros((6, WIN), F32)], axis=0)


def _qkv_specs(seq, pairs):
    def spec(kind):
        return pl.BlockSpec((seq, LANES), lambda p: (0, kind * pairs + p))

    return [spec(0), spec(1), spec(2)]


def attend_forward(qkv, twice, windows, rel_window):
    seq = qkv.shape[0]
    pairs = rel_window.shape[0]
    blocks = seq // QB
    return pl.pallas_call(
        attend_forward_kernel,
        grid=(pairs,),
        out_shape=(
            jax.ShapeDtypeStruct((seq, pairs * LANES), BF16),
            jax.ShapeDtypeStruct((pairs, blocks, WIN, 2 * QB), BF16),
        ),
        in_specs=_qkv_specs(seq, pairs)
        + [
            pl.BlockSpec((blocks, 2 * QB), lambda p: (0, 0)),
            pl.BlockSpec((blocks, WIN), lambda p: (0, 0)),
            pl.BlockSpec((1, 2, WIN), lambda p: (p, 0, 0)),
        ],
        out_specs=(
            pl.BlockSpec((seq, LANES), lambda p: (0, p)),
            pl.BlockSpec((1, blocks, WIN, 2 * QB), lambda p: (p, 0, 0, 0)),
        ),
        scratch_shapes=[pltpu.VMEM((seq + 2 * REACH, LANES), BF16)] * 2
        + [pltpu.VMEM((blocks, WIN, 2 * QB), F32)] * 2,
        compiler_params=params(),
        cost_estimate=cost(8 * seq * WIN * LANES * pairs * 4, 8 * seq * LANES * pairs),
        name="attend_forward",
    )(qkv, qkv, qkv, twice, windows, rel_window)


def attend_backward(qkv, d_context, probs):
    seq = qkv.shape[0]
    pairs = probs.shape[0]
    blocks = seq // QB
    lane_block = pl.BlockSpec((seq, LANES), lambda p: (0, p))
    return pl.pallas_call(
        attend_backward_kernel,
        grid=(pairs,),
        out_shape=(
            jax.ShapeDtypeStruct((seq, 3 * pairs * LANES), BF16),
            jax.ShapeDtypeStruct((pairs, 8, WIN), F32),
        ),
        in_specs=_qkv_specs(seq, pairs)
        + [
            lane_block,
            pl.BlockSpec((1, blocks, WIN, 2 * QB), lambda p: (p, 0, 0, 0)),
        ],
        out_specs=(
            pl.BlockSpec((seq, 3 * pairs * LANES), lambda p: (0, 0)),
            pl.BlockSpec((1, 8, WIN), lambda p: (p, 0, 0)),
        ),
        scratch_shapes=[pltpu.VMEM((seq + 2 * REACH, LANES), BF16)] * 2
        + [pltpu.VMEM((seq + 2 * REACH, LANES), F32)] * 2
        + [pltpu.VMEM((blocks, WIN, 2 * QB), F32), pltpu.VMEM((blocks, WIN, 2 * QB), BF16)],
        compiler_params=params(),
        cost_estimate=cost(16 * seq * WIN * LANES * pairs * 4, 16 * seq * LANES * pairs),
        name="attend_backward",
    )(qkv, qkv, qkv, d_context, probs)


CORE = 1
CROSS = 2


def hop(value, mask):
    size = lax.axis_size("dp")
    return lax.ppermute(value, "dp", [(i, i ^ mask) for i in range(size)])


def over(value):
    return lax.ppermute(value, "mp", [(0, 1), (1, 0)])


def cross(value):
    return hop(value, CROSS)


def core(value):
    return hop(value, CORE)


def go(waits, *sends, keep=(), join=True):
    values = [value for _, value in sends]
    held = lax.optimization_barrier((*values, *keep, *waits))
    results = [how(value) for (how, _), value in zip(sends, held)]
    if join:
        results = list(lax.optimization_barrier(tuple(results)))
    return results + list(held[len(values) : len(values) + len(keep)])


def slot_masks(size):
    rest = size // 4
    return [z * 4 + x * 2 + c for c in range(2) for x in range(2) for z in range(rest)]


def strides(size):
    found = []
    stride = 4
    while stride < size:
        found.append(stride)
        stride *= 2
    return found


def gather_near(shard, waits, widths=None):
    size = lax.axis_size("dp")
    pieces = [shard]
    stride = 4
    while stride < size:
        radix = min(4, size // stride)
        shard = jnp.concatenate(pieces, axis=0) if len(pieces) > 1 else shard
        sends = [(functools.partial(hop, mask=j * stride), shard) for j in range(1, radix)]
        pieces = [shard] + go(waits, *sends)
        stride *= radix
    return jnp.concatenate(pieces, axis=0) if widths is None else stack_rows(pieces, widths)


def rows(*pieces):
    return jnp.concatenate(pieces, axis=0)


def columns(*pieces):
    return jnp.concatenate(pieces, axis=1)


def gather_weights(start, later, n_one, n_three, early, begin, between):
    size = lax.axis_size("dp")
    steps = strides(size)
    n_two = start.shape[1] - n_one
    n_four = later.shape[1] - n_three
    n_early = n_three * 3 // 5
    if len(steps) == 2:
        got = go((), *((functools.partial(hop, mask=4 * j), start) for j in range(1, 4)))
        more = hop(later, 4)
        one, two = stack_rows([start, *got], (n_one, n_two))
        later = stack_rows([later, more], (n_early, later.shape[1] - n_early))
        wide_step = functools.partial(hop, mask=steps[1])
    else:
        one, two = gather_near(start, (), (n_one, n_two))

        later = [later[:, :n_early], later[:, n_early:]]

        def wide_step(value):
            whole = gather_near(value, ())
            return whole[value.shape[0] :]

    one_x, two_y, more = go(early, (cross, one), (over, two), (wide_step, later[0]))
    (one,) = stack_rows([one, one_x], (n_one,))
    (two,) = stack_rows([two, two_y], (n_two,))
    one_y, two_x, one_c, two_c, more_b = go(
        (), (over, one), (cross, two), (core, one), (core, two), (wide_step, later[1])
    )
    if len(steps) == 2:
        have = later[0].shape[0]

        def put(near_a, near_b, far_a, far_b, three_ref, four_ref):
            for at, left, right in ((0, near_a, near_b), (have, far_a, far_b)):
                here = slice(at, at + have)
                three_ref[here, :n_early] = left[...]
                three_ref[here, n_early:] = right[:, : n_three - n_early]
                four_ref[here] = right[:, n_three - n_early :]

        three, four = whole_call(
            put,
            (*later, more, more_b),
            (shape_of(BF16, 2 * have, n_three), shape_of(BF16, 2 * have, n_four)),
            (),
            "put_rows",
        )
    else:
        later = rows(columns(*later), columns(more, more_b))
        three, four = later[:, :n_three], later[:, n_three:]
    three_x, four_y, one_yc, two_xc = go((), (cross, three), (over, four), (core, one_y), (core, two_x))
    (three,) = stack_rows([three, three_x], (n_three,))
    (four,) = stack_rows([four, four_y], (four.shape[1],))
    three_y, four_x, three_c, four_c, one, one_c, one_y, one_yc, two, two_x, two_c, two_xc, *early = go(
        (),
        (over, three),
        (cross, four),
        (core, three),
        (core, four),
        keep=(one, one_c, one_y, one_yc, two, two_x, two_c, two_xc, *early),
        join=False,
    )
    first, second = along_x(one, one_c, one_y, one_yc), along_y(two, two_x, two_c, two_xc)
    done = between(begin(first, early), second, early)
    four_xc, three_yc, *done = go(
        (three_y, four_x, three_c, four_c), (core, four_x), (core, three_y), keep=done, join=False
    )
    third, fourth = along_x(three, three_c, three_y, three_yc), along_y(four, four_x, four_c, four_xc)
    return first, second, third, fourth, early, done


def along_x(near, near_c, other, other_c):
    count = near.shape[0]
    return ((near, 0, count), (near_c, 0, count)), ((other, 0, count), (other_c, 0, count))


def along_y(near, side, near_c, side_c):
    count = near.shape[0] // 2
    return tuple(
        tuple((array, at, count) for array in (near, side, near_c, side_c)) for at in (0, count)
    )


def pack(name, sources, mib):
    widths = [count for *_, count in sources]
    block = sources[0][0].shape[0]

    def run(*refs):
        ins, out = refs[: len(sources)], refs[len(sources)]
        buffers, sem = refs[len(sources) + 1 : -1], refs[-1]
        copies = []
        for i, (_, first, count) in enumerate(sources):
            copy = pltpu.make_async_copy(ins[i].at[:, pl.ds(first, count)], buffers[i], sem.at[i])
            copy.start()
            copies.append(copy)
        at = 0
        for copy, buffer, width in zip(copies, buffers, widths):
            copy.wait()
            out[:, at : at + width] = buffer[...]
            at += width

    return pl.pallas_call(
        run,
        out_shape=shape_of(BF16, block, sum(widths)),
        in_specs=[pl.BlockSpec(memory_space=pltpu.HBM)] * len(sources),
        out_specs=pl.BlockSpec(memory_space=pltpu.VMEM),
        scratch_shapes=[pltpu.VMEM((block, width), BF16) for width in widths]
        + [pltpu.SemaphoreType.DMA((len(sources),))],
        compiler_params=params(mib),
        cost_estimate=cost(0, 0),
        name=name,
    )(*(array for array, *_ in sources))


def gather_dp(shard):
    near = gather_near(shard, ())
    side, c_near = go((near,), (cross, near), (core, near))
    return near, side, c_near, core(side)


def low(value):
    return value.astype(BF16)


def add(left, right):
    return (left.astype(F32) + right.astype(F32)).astype(BF16)


def product(left, begin, end, right, got=None):
    value = dot_tn(left[:, begin:end], right)
    if got is not None:
        value = value + got.astype(F32)
    return low(value)


def rest_start(value):
    half = value.shape[0] // 2
    return value[half:], value[:half]


def sum_half(value, send):
    gone, stays = rest_start(value)
    return stays + send(low(gone)).astype(F32)


def rest_hops(size):
    return [functools.partial(hop, mask=stride) for stride in reversed(strides(size))]


def shards(
    tokens,
    seg_ids,
    buckets,
    labels,
    w_query,
    w_key,
    w_value,
    w_out,
    w_in,
    w_back,
    gain_attn,
    gain_ffn,
    gain_final,
    w_pool,
    rel_table,
):
    micro_count, seq, width = tokens.shape
    size = lax.axis_size("dp")
    me = lax.axis_index("dp")
    mine = lax.axis_index("mp")
    block = width // size
    inner_half = w_query.shape[1]
    hidden_half = w_in.shape[1]
    sent_local = labels.shape[1]
    bucket_count = rel_table.shape[0]
    heads_half = rel_table.shape[1]
    masks = slot_masks(size)

    x_own = lax.dynamic_index_in_dim(tokens, mine, 0, keepdims=False)
    segments = lax.dynamic_index_in_dim(seg_ids, mine, 0, keepdims=False)[0]
    partner = lax.dynamic_index_in_dim(labels, mine, 0, keepdims=False)

    slot_block = jnp.stack([jnp.bitwise_xor(me, m) for m in masks]).astype(jnp.int32)
    source = (slot_block[:, None] * block + jnp.arange(block, dtype=jnp.int32)[None, :]).reshape(-1)
    order = (jnp.arange(width, dtype=jnp.int32)[:, None] == source[None, :]).astype(BF16)
    order = lax.optimization_barrier(order)
    inputs = dot(x_own, order)


    row_f32 = shape_of(F32, seq, width)
    row_low = shape_of(BF16, seq, width)
    column_f32 = shape_of(F32, seq, 1)
    gain_f32 = shape_of(F32, 1, width)
    heads = 3 * inner_half
    piece = hidden_half // 2
    halves = [(side, i * inner_half, inner_half) for side in range(2) for i in range(2)]

    def hidden_blocks(weights, first_col=0):
        return [(weights[side], first_col + col, n) for side, col, n in halves]

    def begin(first, early):
        inputs, rel_window, twice, windows, *_ = early
        qkv, normed1_low, inverse1, gains = qkv_call(inputs, first, inner_half)
        context, probs = attend_forward(qkv, twice, windows, rel_window)
        return qkv, normed1_low, inverse1, gains, context, probs

    def between(started, second, early):
        qkv, normed1_low, inverse1, gains, context, probs = started
        inputs = early[0]
        hidden1, inverse2, normed2_low = narrow(
            "attn_out",
            [(context, i * inner_half, second[i], piece, inner_half) for i in range(2)],
            (inputs, gains),
            (row_f32, column_f32, row_low),
            functools.partial(norm_body, 1),
        )
        act0, slope0 = wide("act0", normed2_low, hidden_blocks(second), (), gelu_both, 2)
        return normed1_low, inverse1, gains, qkv, context, probs, hidden1, inverse2, normed2_low, act0, slope0

    gains_col = jnp.pad(
        jnp.stack([gain_attn, gain_ffn, gain_final], axis=1), ((0, 0), (0, LANES - 3))
    )
    pool_half = w_pool.shape[1] // 2
    pool_own = lax.dynamic_slice_in_dim(w_pool, mine * pool_half, pool_half, axis=1)
    moved = LANES
    back_shard = w_back.T
    if block % 16:
        start = columns(w_query, w_key, w_value, gains_col, w_in[:, :piece], w_out.T)
        later = columns(
            back_shard[:, :piece],
            back_shard[:, hidden_half - moved :],
            pool_own,
            w_in[:, piece:],
            back_shard[:, piece : hidden_half - moved],
        )
    else:
        start = pack(
            "pack_start",
            [(w, 0, inner_half) for w in (w_query, w_key, w_value)]
            + [(gains_col, 0, LANES), (w_in, 0, piece), (w_out.T, 0, inner_half)],
            60,
        )
        back_shard, w_in, _ = lax.optimization_barrier((back_shard, w_in, start))
        later = pack(
            "pack_later",
            [
                (back_shard, 0, piece),
                (back_shard, hidden_half - moved, moved),
                (pool_own, 0, pool_half),
                (w_in, piece, piece),
                (back_shard, piece, piece - moved),
            ],
            16,
        )
    rel_other = over(lax.optimization_barrier((rel_table, start))[0])
    rel_all = jnp.concatenate([rel_table, rel_other], axis=1).astype(F32)
    near_buckets = lax.slice_in_dim(buckets, seq - 1 - REACH, seq - 1 - REACH + WIN)
    onehot = (near_buckets[None, :] == jnp.arange(bucket_count, dtype=jnp.int32)[:, None]).astype(F32)
    onehot = lax.optimization_barrier(low(onehot))
    rel_window = dot(rel_all, onehot.astype(F32), ((0,), (0,)), HIGHEST).reshape(heads_half, 2, WIN)
    padded = jnp.pad(segments, (REACH, REACH), constant_values=-1)
    windows = jnp.stack([padded[at : at + WIN] for at in range(0, seq, QB)])
    twice = jnp.tile(segments.reshape(seq // QB, QB), (1, 2))
    local_ids = jnp.arange(sent_local, dtype=jnp.int32)
    column_id = (slot_block[:, None] * sent_local + local_ids[None, :]).reshape(1, -1)
    early = (
        inputs, rel_window, twice, windows, order, onehot, column_id, partner[None, :], segments[None, :], mine.reshape(1, 1),
        (me * block).astype(jnp.uint32), (mine * heads_half).astype(jnp.uint32)
    )
    first, second, third, fourth, early, done = gather_weights(
        start,
        later,
        heads + LANES,
        piece + moved + pool_half,
        early,
        begin,
        between,
    )
    inputs, rel_window, twice, windows, order, onehot, column_id, partner, seg_lane, mine_array, gain_at, table_at = early
    normed1_low, inverse1, gains, qkv, context, probs, hidden1, inverse2, normed2_low, act0, slope0 = done

    act1, up_kept = wide("act1", normed2_low, hidden_blocks(fourth), (), gelu_only, 2)
    pool_loads = [weight(side, piece + moved, pool_half) for side in third]
    hidden2, inverse3, pooled_low, unit, unit_low, scale = narrow(
        "ffn_out",
        [(act0, i * piece, third[i], 0, piece) for i in range(2)]
        + [(act1, i * piece, fourth[i], piece, piece - moved) for i in range(2)]
        + [(act1, (i + 1) * piece - moved, third[i], piece, moved) for i in range(2)],
        (hidden1, gains, seg_lane, *pool_loads),
        (
            row_f32,
            column_f32,
            shape_of(BF16, sent_local, width),
            shape_of(F32, sent_local, width),
            shape_of(BF16, sent_local, width),
            shape_of(F32, sent_local, 1),
        ),
        tail_body,
        [pltpu.VMEM((seq, width), BF16)] * 2,
    )
    quarters = gather_dp(unit_low)

    total_sent = column_id.shape[1]
    sentence_loads = [part(seg_lane), *pool_loads, part(hidden2), part(inverse3), part(gains)]
    back_shapes = (row_f32, row_low, gain_f32)
    if total_sent <= 1024:
        loss_local, embed_low, d_hidden2, ffn_low, d_gain3 = head_call(
            quarters,
            unit,
            scale,
            partner,
            column_id,
            sentence_loads,
            (shape_of(F32, 1, 1), shape_of(BF16, sent_local, width), *back_shapes),
        )
    else:
        every = rows(*quarters)
        position = jnp.arange(total_sent, dtype=jnp.int32)
        sims = dot_nt(every, every) * SOFTMAX_TEMP
        sims = jnp.where(position[:, None] == position[None, :], NEG_FILL, sims)
        lse_row = jax.nn.logsumexp(sims, axis=0, keepdims=True)
        own_sims = sims[:sent_local]
        own_lse = jax.nn.logsumexp(own_sims, axis=1, keepdims=True)
        is_target = column_id == partner.reshape(-1, 1)
        target = jnp.sum(jnp.where(is_target, own_sims, 0.0), axis=-1, keepdims=True)
        loss_local = jnp.sum(own_lse - target)
        hit = is_target.astype(F32)
        d_rows = low(LOSS_SCALE * (jnp.exp(own_sims - own_lse) - hit))
        d_cols = low(LOSS_SCALE * (jnp.exp(own_sims - lse_row) - hit))
        d_unit = SOFTMAX_TEMP * (dot(d_rows, every) + dot(d_cols, every))
        embed_low = low(scale * (d_unit - unit * jnp.sum(d_unit * unit, axis=-1, keepdims=True)))
        d_hidden2, ffn_low, d_gain3 = sentence_call(embed_low, sentence_loads, back_shapes)

    half = width // 2
    quarter = width // 4

    back0_sent, back1_sent = gradients("back_sent", ffn_low, half, half, (act0, act1))
    (pool_sent,) = gradients("pool_sent", pooled_low, half, half, (embed_low,))
    back0_got, back1_got, pool_got, ffn_later = go(
        (), (core, back0_sent), (core, back1_sent), (core, pool_sent), keep=(ffn_low,), join=False
    )
    pool_hi = product(pooled_low, quarter, half, embed_low, pool_got[quarter:])
    pool_lo = product(pooled_low, 0, quarter, embed_low, pool_got[:quarter])
    up0 = wide("up0", ffn_later, hidden_blocks(third), (slope0,), times_slope)

    back_hi = product(ffn_low, quarter, half, act0, back0_got[quarter:])
    back_lo = product(ffn_low, 0, quarter, act0, back0_got[:quarter])
    back_own = product(ffn_low, 0, half, act1[:, :piece], back1_got[:, :piece])
    back_oth = product(ffn_low, 0, half, act1[:, piece:], back1_got[:, piece:])
    got_lo, got_own, got_pool, ffn_later, up0, back_lo, back_own, pool_lo = go(
        (),
        (cross, back_hi),
        (over, back_oth),
        (cross, pool_hi),
        keep=(ffn_later, up0, back_lo, back_own, pool_lo),
    )
    back_blocks = [
        block
        for side in range(2)
        for block in (
            (fourth[side], piece, inner_half),
            (fourth[side], piece + inner_half, piece - moved - inner_half),
            (third[side], piece, moved),
        )
    ]
    up1 = wide("up1", ffn_later, back_blocks, (up_kept,), times_slope_of)
    in0_sent, in1_sent = gradients("in_sent", normed2_low, half, half, (up0, up1))
    in0_got, in1_got, up0, up1 = go((), (core, in0_sent), (core, in1_sent), keep=(up0, up1))
    attn_low, d_gain2, d_hidden1 = narrow(
        "ffn_in_back",
        [(up0, i * piece, second[i], 0, piece) for i in range(2)]
        + [(up1, i * piece, fourth[i], 0, piece) for i in range(2)],
        (hidden1, inverse2, gains, d_hidden2),
        (row_low, gain_f32, row_f32),
        functools.partial(back_body, 1),
    )
    d_context = wide("d_context", attn_low, [(second[side], piece, inner_half) for side in range(2)])

    pool_lo = add(pool_lo, got_pool)
    back_lo = add(back_lo, got_lo)
    back_own = add(back_own, got_own)
    in_hi = product(normed2_low, quarter, half, up0, in0_got[quarter:])
    in_lo = product(normed2_low, 0, quarter, up0, in0_got[:quarter])
    in_own = product(normed2_low, 0, half, up1[:, :piece], in1_got[:, :piece])
    in_oth = product(normed2_low, 0, half, up1[:, piece:], in1_got[:, piece:])
    got_first, got_x, got_in_own, d_context, pool_lo, back_lo, back_own, in_lo, in_own = go(
        (got_lo, got_own),
        (over, columns(back_lo[:, piece:], pool_lo[:, pool_half:])),
        (cross, columns(back_own[quarter:], in_hi)),
        (over, in_oth),
        keep=(d_context, pool_lo, back_lo, back_own, in_lo, in_own),
        join=False,
    )
    d_qkv, d_bias = attend_backward(qkv, d_context, probs)
    query_both = 2 * inner_half
    late_sent = sent_columns("late_sent", half, ((attn_low, context), (normed1_low, d_qkv)))
    late_got, d_qkv_later = go((), (core, late_sent), keep=(d_qkv,), join=False)
    grad_slots, d_gain1 = narrow(
        "qkv_back",
        [(d_qkv_later, i * inner_half, first[i], 0, inner_half) for i in range(2)]
        + [(d_qkv_later, (1 + i) * query_both, first[i], inner_half, query_both) for i in range(2)],
        (inputs, inverse1, gains, d_hidden1),
        (row_low, gain_f32),
        functools.partial(back_body, 0),
    )

    table_row = 3 * (width // LANES) + 1
    table_rows = -(-2 * heads_half * bucket_count // LANES)
    small_rows = -(-(table_row + table_rows) // 8) * 8
    (flat,) = whole_call(
        functools.partial(small_kernel, heads_half),
        (d_gain1, d_gain2, d_gain3, order, d_bias.reshape(-1, WIN), onehot, loss_local.reshape(1, 1), mine_array),
        (shape_of(F32, small_rows, LANES),),
        (),
        "small",
    )
    (grad_own,) = whole_call(turn_kernel, (grad_slots, order), (row_low,), (), "turn")
    flat_got, flat = go((), (over, flat), keep=(flat,), join=False)
    got_first, got_x, got_in_own = lax.optimization_barrier((got_first, got_x, got_in_own))
    flat = flat + flat_got
    got_second, got_in_lo = got_x[:, :piece], got_x[:, piece:]

    far = rest_hops(size)
    back_all = columns(
        add(back_lo[:, :piece], got_first[:, :piece]),
        add(back_own[:quarter], got_second),
        add(pool_lo[:, :pool_half], got_first[:, piece:]),
    )
    back_rest, back_stay = rest_start(back_all)
    in_lo = add(in_lo, got_in_lo)
    in_own = add(in_own, got_in_own)
    out_got, qkv_got = late_got[:, :query_both], late_got[:, query_both:]
    out_hi = product(attn_low, quarter, half, context, out_got[quarter:])
    out_lo = product(attn_low, 0, quarter, context, out_got[:quarter])
    query_hi = product(normed1_low, quarter, half, d_qkv[:, :query_both], qkv_got[quarter:, :query_both])
    query_lo = product(normed1_low, 0, quarter, d_qkv[:, :query_both], qkv_got[:quarter, :query_both])
    kv_own = product(
        normed1_low, 0, half, d_qkv[:, query_both : 2 * query_both], qkv_got[:, query_both : 2 * query_both]
    )
    kv_oth = product(normed1_low, 0, half, d_qkv[:, 2 * query_both :], qkv_got[:, 2 * query_both :])
    rest_hop = [functools.partial(hop, mask=j * 4) for j in range(1, min(4, size // 4))]
    back_more, got_first, got_x, got_kv, flat_got, back_stay, in_lo, in_own, out_lo, query_lo, kv_own, flat = go(
        (grad_own,),
        (far[0], back_rest),
        (over, in_lo[:, piece:]),
        (cross, columns(in_own[quarter:], out_hi, query_hi)),
        (over, kv_oth),
        (core, flat),
        keep=(back_stay, in_lo, in_own, out_lo, query_lo, kv_own, flat),
    )

    count = flat.shape[0]

    def in_two(value):
        high = value.astype(BF16).astype(F32)
        return jnp.concatenate([high, value - high], axis=0).astype(BF16)

    def from_two(pair):
        return pair[:count].astype(F32) + pair[count : 2 * count].astype(F32)

    def late_adds(
        stay, more, in_lo, got_first, in_own, got_x, out_lo, query_lo, kv_own, got_kv, flat, got_flat, *outs
    ):
        back_gone, back_keep, in_gone, in_keep, heads_gone, heads_keep, kv_gone, kv_keep, small = outs
        rows_z = stay.shape[0] // 2
        total = add(stay[...], more[...])
        back_keep[...] = total[:rows_z]
        back_gone[...] = total[rows_z:]
        rows_z = in_lo.shape[0] // 2
        for at, total in (
            (0, add(in_lo[:, :piece], got_first[...])),
            (piece, add(in_own[:quarter], got_x[:, :piece])),
        ):
            in_keep[:, at : at + piece] = total[:rows_z]
            in_gone[:, at : at + piece] = total[rows_z:]
        for i, ref in enumerate((out_lo, query_lo)):
            first_col = piece + i * query_both
            total = add(ref[...], got_x[:, first_col : first_col + query_both])
            heads_keep[:, i * inner_half : (i + 1) * inner_half] = total[:, :inner_half]
            heads_gone[:, i * inner_half : (i + 1) * inner_half] = total[:, inner_half:]
        kv_keep[...] = add(kv_own[:quarter], got_kv[:quarter])
        kv_gone[:, :query_both] = add(kv_own[quarter:], got_kv[quarter:])
        small[...] = flat[...] + got_flat[...]
        kv_gone[:, query_both:] = jnp.zeros((quarter, LANES), BF16)
        pair = in_two(small[...])
        kv_gone[: 2 * count, query_both:] = pair
        small[...] = from_two(pair)

    cut = [shape_of(BF16, back_stay.shape[0] // 2, back_stay.shape[1])] * 2
    cut += [shape_of(BF16, quarter // 2, hidden_half)] * 2 + [shape_of(BF16, quarter, query_both)] * 2
    cut += [
        shape_of(BF16, quarter, query_both + LANES),
        shape_of(BF16, quarter, query_both),
        shape_of(F32, count, LANES),
    ]
    back_rest, back_stay, in_rest, in_stay, heads_gone, heads_keep, kv_gone, kv_keep, flat = whole_call(
        late_adds,
        (back_stay, back_more, in_lo, got_first, in_own, got_x, out_lo, query_lo, kv_own, got_kv, flat, flat_got),
        cut,
        (),
        "late_adds",
    )
    early_rows = seq * 11 // 32
    back_more, in_more, got_first, got_second, grad_other, back_stay, in_stay, heads_keep, kv_keep, flat = go(
        (),
        (far[1], back_rest),
        (far[0], in_rest),
        (over, heads_gone),
        (cross, kv_gone),
        (over, grad_own[:early_rows]),
        keep=(back_stay, in_stay, heads_keep, kv_keep, flat),
    )

    def finish(value):
        value = value.astype(F32)
        for send in far[2:]:
            value = sum_half(value, send)
        return value

    n_last = query_both + query_both
    if len(far) == 2:
        rest = block
        late_rows = seq - early_rows

        def last_adds(stay, more, heads_ref, got_heads, kv_ref, got_kv, flat_ref, back_ref, back_got, own_ref, *outs):
            one, two, three, in_keep, keep, flat_out, tail, pool_ref = outs
            pool = add(back_ref[:, hidden_half:], back_got[:, hidden_half:])
            pool_ref[...] = pool
            tail[:late_rows] = own_ref[early_rows:]
            tail[late_rows:, :pool_half] = pool
            tail[late_rows:, pool_half:] = jnp.zeros((rest, width - pool_half), BF16)
            total = add(stay[...], more[...])
            in_keep[...] = total[:rest]
            one[:, LANES : LANES + hidden_half] = total[rest:]
            pair = in_two(flat_ref[...] + from_two(got_kv[:, query_both:]))
            flat_out[...] = from_two(pair)
            for i, (ref, at) in enumerate(((keep, 0), (one, LANES + hidden_half), (two, LANES), (three, LANES))):
                here = slice(i * rest, (i + 1) * rest)
                if i:
                    ref[:, :LANES] = pair
                ref[:, at : at + query_both] = add(heads_ref[here], got_heads[here])
                ref[:, at + query_both : at + n_last] = add(kv_ref[here], got_kv[here, :query_both])

        one, two, three, in_stay, last_stay, flat, tail, grad_pool = whole_call(
            last_adds,
            (in_stay, in_more, heads_keep, got_first, kv_keep, got_second, flat, back_stay, back_more, grad_own),
            (
                shape_of(BF16, rest, LANES + hidden_half + n_last),
                shape_of(BF16, rest, LANES + n_last),
                shape_of(BF16, rest, LANES + n_last),
                shape_of(BF16, rest, hidden_half),
                shape_of(BF16, rest, n_last),
                shape_of(F32, count, LANES),
                shape_of(BF16, late_rows + rest, width),
                shape_of(BF16, rest, pool_half),
            ),
            (),
            "last_adds",
        )
        got_one, got_two, got_three, got_tail, back_stay, back_more = go(
            (),
            (rest_hop[0], one),
            (rest_hop[1], two),
            (rest_hop[2], three),
            (over, tail),
            keep=(back_stay, back_more),
            join=False,
        )

        def back_final(stay, more, back_ref):
            back_ref[...] = stay[:, :hidden_half].astype(F32) + more[:, :hidden_half].astype(F32)

        (grad_back,) = whole_call(
            back_final, (back_stay, back_more), (shape_of(F32, rest, hidden_half),), (), "back_final"
        )

        def tokens_final(mine_ref, own_ref, first_ref, tail_ref, pool_own, out_ref, pool_ref):
            first = mine_ref[...] == 0
            own, other = pool_own[...].astype(F32), tail_ref[late_rows:, :pool_half].astype(F32)
            pool_ref[:, :pool_half] = jnp.where(first, own, other)
            pool_ref[:, pool_half:] = jnp.where(first, other, own)
            for at, count, ref in ((0, early_rows, first_ref), (early_rows, late_rows, tail_ref)):
                here = slice(at, at + count)
                own, other = own_ref[here].astype(F32), ref[:count].astype(F32)
                out_ref[0, here] = jnp.where(first, own, other).astype(BF16)
                out_ref[1, here] = jnp.where(first, other, own).astype(BF16)

        grad_tokens, grad_pool = whole_call(
            tokens_final,
            (mine_array, grad_own, grad_other, got_tail, grad_pool),
            (shape_of(BF16, 2, seq, width), shape_of(F32, rest, 2 * pool_half)),
            (),
            "tokens_final",
        )
        got_one, got_two, got_three, grad_tokens = lax.optimization_barrier(
            (got_one, got_two, got_three, grad_tokens)
        )

        def last_final(stay, in_keep, one_ref, two_ref, three_ref, flat_ref, *outs):
            in_ref, out_ref, q_ref, k_ref, v_ref, flat_out = outs
            in_ref[...] = in_keep[...].astype(F32) + one_ref[:, LANES : LANES + hidden_half].astype(F32)
            total = stay[...].astype(F32) + one_ref[:, LANES + hidden_half :].astype(F32)
            total = total + two_ref[:, LANES:].astype(F32) + three_ref[:, LANES:].astype(F32)
            for i, ref in enumerate((out_ref, q_ref, k_ref, v_ref)):
                ref[...] = total[:, i * inner_half : (i + 1) * inner_half]
            small = flat_ref[...]
            for ref in (one_ref, two_ref, three_ref):
                small = small + from_two(ref[:, :LANES])
            flat_out[...] = small

        head_shape = shape_of(F32, rest, inner_half)
        grad_in, grad_out, grad_query, grad_key, grad_value, flat = whole_call(
            last_final,
            (last_stay, in_stay, got_one, got_two, got_three, flat),
            (shape_of(F32, rest, hidden_half), *(head_shape,) * 4, shape_of(F32, count, LANES)),
            (),
            "last_final",
        )
    else:
        flat = flat + from_two(got_second[:, query_both:])
        grad_other = rows(grad_other, over(grad_own[early_rows:]))
        in_rest, in_stay = rest_start(add(in_stay, in_more))
        last = columns(add(heads_keep, got_first), add(kv_keep, got_second[:, :query_both]))
        last_rest, last_stay = rest_start(last)
        in_more, last_more, *flat_got = go(
            (), (far[1], in_rest), (far[0], last_rest), *((how, flat) for how in rest_hop)
        )
        last_rest, last_stay = rest_start(add(last_stay, last_more))
        last_more = far[1](last_rest)
        flat = flat + sum(flat_got)
        for send in far[:-2]:
            flat = flat + send(flat)
        grad_last = finish(last_stay.astype(F32) + last_more.astype(F32))
        grad_in = finish(in_stay.astype(F32) + in_more.astype(F32))
        back_all = finish(back_stay.astype(F32) + back_more.astype(F32))
        grad_back, grad_pool = back_all[:, :hidden_half], back_all[:, hidden_half:]
        pool_other = over(grad_pool)
        grad_pool = jnp.where(mine == 0, columns(grad_pool, pool_other), columns(pool_other, grad_pool))
        grad_out, grad_query, grad_key, grad_value = (
            grad_last[:, i * inner_half : (i + 1) * inner_half] for i in range(4)
        )
        grad_tokens = jnp.where(
            mine == 0, jnp.stack([grad_own, grad_other]), jnp.stack([grad_other, grad_own])
        )
    across = width // LANES
    zero = jnp.uint32(0)
    gains_mine = lax.dynamic_slice(flat[: 3 * across].reshape(3, width), (zero, gain_at), (3, block))
    loss = flat[3 * across, 0] / (micro_count * sent_local * size)
    table_sum = flat[table_row : table_row + table_rows].reshape(-1, bucket_count)[: 2 * heads_half]
    table_mine = lax.dynamic_slice(table_sum, (table_at, zero), (heads_half, bucket_count)).T
    return (
        loss,
        grad_tokens,
        grad_query,
        grad_key,
        grad_value,
        grad_out.T,
        grad_in,
        grad_back.T,
        gains_mine[0],
        gains_mine[1],
        gains_mine[2],
        grad_pool,
        table_mine,
    )


def solution(mesh):
    placed = (
        P(None, "dp", None),
        P(None, "dp", None),
        P(),
        P(None, "dp"),
        P("dp", "mp"),
        P("dp", "mp"),
        P("dp", "mp"),
        P("mp", "dp"),
        P("dp", "mp"),
        P("mp", "dp"),
        P("dp"),
        P("dp"),
        P("dp"),
        P("dp", None),
        P(None, "mp"),
    )
    return jax.shard_map(
        shards,
        mesh=mesh,
        in_specs=placed,
        out_specs=(
            P(),
            P(None, "dp", None),
            P("dp", "mp"),
            P("dp", "mp"),
            P("dp", "mp"),
            P("mp", "dp"),
            P("dp", "mp"),
            P("mp", "dp"),
            P("dp"),
            P("dp"),
            P("dp"),
            P("dp", None),
            P(None, "mp"),
        ),
        check_vma=False,
    )
```

```python
import functools

import jax
import jax.numpy as jnp
from jax import lax
from jax.experimental import pallas as pl
from jax.experimental.pallas import tpu as pltpu
from jax.sharding import PartitionSpec as P

NEG_FILL = -1000000000.0
SCORE_SCALE = 0.125
SOFTMAX_TEMP = 50.0
LOSS_SCALE = 64.0
EPSILON = 1e-06
REACH = 32
QB = 64
WIN = QB + 2 * REACH
LANES = 128
GELU_A = 0.7978845608028654
GELU_B = 0.044715

BF16 = jnp.bfloat16
F32 = jnp.float32
HIGHEST = lax.Precision.HIGHEST


def dot(left, right, dims=((1,), (0,)), precision=None):
    return lax.dot_general(
        left, right, (dims, ((), ())), precision=precision, preferred_element_type=F32
    )


def dot_nt(left, right):
    return dot(left, right, ((1,), (1,)))


def dot_tn(left, right):
    return dot(left, right, ((0,), (0,)))


def rms_forward(value, gain):
    inverse = lax.rsqrt(jnp.mean(value * value, axis=-1, keepdims=True) + EPSILON)
    return (value * inverse * gain, inverse)


def cost(flops, bytes_accessed):
    return pl.CostEstimate(flops=0, bytes_accessed=0, transcendentals=0)


def params(mib=16):
    return pltpu.CompilerParams(vmem_limit_bytes=mib * 2**20)


def split_dot(left, right, dims=((1,), (0,))):
    high = right.astype(BF16)
    rest = (right - high.astype(F32)).astype(BF16)
    return dot(left, high, dims) + dot(left, rest, dims)


def stream_kernel(plan, operands, outs, body, *refs):
    sources, out_refs = refs[:operands], refs[operands : operands + outs]
    more = refs[operands + outs :]
    buffers, sem = more[: sum(len(load) > 1 for load in plan)], more[-1]
    more = more[len(buffers) : -1]
    copies, places, used = [], [], 0
    for load in plan:
        if len(load) == 1:
            which, _, row, count, col, width, _ = load[0]
            places.append(sources[which].at[pl.ds(row, count), pl.ds(col, width)])
            copies.append([])
            continue
        buffer = buffers[used]
        used += 1
        group = []
        for which, at, row, count, col, width, number in load:
            copy = pltpu.make_async_copy(
                sources[which].at[pl.ds(row, count), pl.ds(col, width)],
                buffer.at[pl.ds(at, count)],
                sem.at[number],
            )
            copy.start()
            group.append(copy)
        places.append(buffer)
        copies.append(group)
    ready = set()

    def get(i):
        if i not in ready:
            ready.add(i)
            for copy in copies[i]:
                copy.wait()
        return places[i]

    body(get, *out_refs, *more)


def stream(name, loads, out_shapes, body, scratch=(), mib=16):
    arrays, spaces = [], []

    def place(array, space):
        for i, known in enumerate(arrays):
            if known is array and spaces[i] is space:
                return i
        arrays.append(array)
        spaces.append(space)
        return len(arrays) - 1

    plan, buffers, number = [], [], 0
    for load in loads:
        steps, at = [], 0
        space = pltpu.VMEM if len(load) == 1 else pltpu.HBM
        for array, row, count, col, width in load:
            steps.append((place(array, space), at, row, count, col, width, number))
            at += count
            number += 1
        plan.append(steps)
        if len(load) > 1:
            buffers.append(pltpu.VMEM((at, load[0][4]), load[0][0].dtype))
    return pl.pallas_call(
        functools.partial(stream_kernel, plan, len(arrays), len(out_shapes), body),
        out_shape=tuple(out_shapes),
        in_specs=[pl.BlockSpec(memory_space=space) for space in spaces],
        out_specs=tuple(pl.BlockSpec(memory_space=pltpu.VMEM) for _ in out_shapes),
        scratch_shapes=buffers + list(scratch) + [pltpu.SemaphoreType.DMA((number,))],
        compiler_params=params(mib),
        cost_estimate=cost(0, 0),
        name=name,
    )(*arrays)


def part(array, col=0, width=None):
    return [(array, 0, array.shape[0], col, array.shape[1] - col if width is None else width)]


def weight(pieces, col, width):
    return [(*piece, col, width) for piece in pieces]


def wide(name, x, blocks, extras=(), body=None, outs=1):
    widths = [width for *_, width in blocks]
    loads = [part(x)]
    for i, block in enumerate(blocks):
        loads.append(weight(*block))
        for extra in extras:
            loads.append(part(extra, sum(widths[:i]), widths[i]))

    def run(get, *out_refs):
        at = 0
        per = 1 + len(extras)
        for i, width in enumerate(widths):
            first = 1 + i * per
            value = dot(get(0)[...], get(first)[...])
            got = [get(first + 1 + j)[...] for j in range(len(extras))]
            values = (value,) if body is None else body(value, *got)
            for ref, result in zip(out_refs, values):
                ref[:, at : at + width] = result.astype(BF16)
            at += width

    shape = shape_of(BF16, x.shape[0], sum(widths))
    result = stream(name, loads, (shape,) * outs, run)
    return result if outs > 1 else result[0]


def gelu_both(up):
    square = up * up
    bend = jnp.tanh(GELU_A * up * (1.0 + GELU_B * square))
    half_one = 0.5 + 0.5 * bend
    inner = GELU_A + (3.0 * GELU_A * GELU_B) * square
    return up * half_one, half_one + 0.5 * up * (1.0 - bend * bend) * inner


def gelu_only(up):
    bend = jnp.tanh(GELU_A * up * (1.0 + GELU_B * (up * up)))
    return up * (0.5 + 0.5 * bend), up


def times_slope(value, slope):
    return (value * slope.astype(F32),)


def times_slope_of(value, up):
    return (value * gelu_both(up.astype(F32))[1],)


def narrow(name, work, extras, out_shapes, body, scratch=(), mib=16):
    loads = []
    for x, x_col, pieces, col, width in work:
        loads += [part(x, x_col, width), weight(pieces, col, width)]
    first = len(loads)
    loads += [extra if isinstance(extra, list) else part(extra) for extra in extras]

    def run(get, *refs):
        out_refs, more = refs[: len(out_shapes)], refs[len(out_shapes) :]
        acc = more[0]
        for j in range(len(work)):
            value = dot_nt(get(2 * j)[...], get(2 * j + 1)[...])
            acc[...] = value if j == 0 else acc[...] + value
        body(acc, *(get(first + i) for i in range(len(extras))), *out_refs, *more[1:])

    depth = sum(count for *_, count in work[0][2])
    return stream(
        name, loads, out_shapes, run, [pltpu.VMEM((work[0][0].shape[0], depth), F32), *scratch], mib
    )


def gradients(name, left, first, count, rights, out_of=None):
    loads = [part(left, first, count)] + [part(right) for right in rights]

    def run(get, *refs):
        *out_refs, turned = refs
        turned[...] = get(0)[...].T
        for i, ref in enumerate(out_refs):
            ref[...] = dot(turned[...], get(1 + i)[...]).astype(BF16)

    shapes = [shape_of(BF16, count, right.shape[1]) for right in rights]
    return stream(name, loads, shapes, run, [pltpu.VMEM((count, left.shape[0]), BF16)])


def sent_columns(name, first, pairs):
    loads = [load for left, right in pairs for load in (part(left, first, first), part(right))]

    def run(get, out_ref, turned):
        at = 0
        for i, (_, right) in enumerate(pairs):
            turned[...] = get(2 * i)[...].T
            n = right.shape[1]
            out_ref[:, at : at + n] = dot(turned[...], get(2 * i + 1)[...]).astype(BF16)
            at += n

    shape = shape_of(BF16, first, sum(right.shape[1] for _, right in pairs))
    return stream(name, loads, (shape,), run, [pltpu.VMEM((first, pairs[0][0].shape[0]), BF16)])[0]


def stack_rows(pieces, widths):
    block = pieces[0].shape[0]
    cuts = [sum(widths[:i]) for i in range(len(widths))]
    if block % 16:
        whole = jnp.concatenate(pieces, axis=0)
        return [whole[:, at : at + width] for at, width in zip(cuts, widths)]

    def run(*refs):
        for i, ref in enumerate(refs[: len(pieces)]):
            for j, out in enumerate(refs[len(pieces) :]):
                out[i * block : (i + 1) * block] = ref[:, cuts[j] : cuts[j] + widths[j]]

    shapes = [shape_of(pieces[0].dtype, block * len(pieces), width) for width in widths]
    return whole_call(run, pieces, shapes, (), "stack_rows")


def qkv_call(inputs, first, n):
    blocks = [(side, i * n, n) for i in range(3) for side in first]
    loads = [part(inputs), weight(first[0], 3 * n, LANES)] + [weight(*block) for block in blocks]

    def run(get, qkv_ref, normed_ref, inverse_ref, gains_ref):
        value = get(0)[...]
        inverse = lax.rsqrt(jnp.mean(value * value, axis=1, keepdims=True) + EPSILON)
        inverse_ref[...] = inverse
        gains = get(1)[...].astype(F32).T[:8]
        gains_ref[...] = gains
        normed_ref[...] = (value * inverse * gains[0:1]).astype(BF16)
        for i in range(len(blocks)):
            qkv_ref[:, i * n : (i + 1) * n] = dot(normed_ref[...], get(2 + i)[...]).astype(BF16)

    seq, width = inputs.shape
    shapes = (
        shape_of(BF16, seq, 6 * n),
        shape_of(BF16, seq, width),
        shape_of(F32, seq, 1),
        shape_of(F32, 8, width),
    )
    return stream("qkv", loads, shapes, run)


def norm_body(row, acc, value_ref, gains_ref, hidden_ref, inverse_ref, normed_ref=None):
    hidden = value_ref[...] + acc[...]
    inverse = lax.rsqrt(jnp.mean(hidden * hidden, axis=1, keepdims=True) + EPSILON)
    hidden_ref[...] = hidden
    inverse_ref[...] = inverse
    if normed_ref is not None:
        normed_ref[...] = (hidden * inverse * gains_ref[row : row + 1, :]).astype(BF16)


def norm_back(value, inverse, gain, grad):
    scaled = grad * gain
    inner = jnp.mean(value * scaled, axis=1, keepdims=True)
    d_value = inverse * scaled - value * (inverse * inverse * inverse) * inner
    return d_value, jnp.sum(grad * value * inverse, axis=0, keepdims=True)


def back_body(row, acc, value_ref, inverse_ref, gains_ref, grad_ref, low_ref, gain_out, hidden_ref=None):
    d_value, d_gain = norm_back(
        value_ref[...], inverse_ref[...], gains_ref[row : row + 1, :], acc[...]
    )
    total = grad_ref[...] + d_value
    low_ref[...] = total.astype(BF16)
    gain_out[...] = d_gain
    if hidden_ref is not None:
        hidden_ref[...] = total


def turn_kernel(grad_ref, order_ref, out_ref):
    out_ref[...] = dot_nt(grad_ref[...], order_ref[...]).astype(BF16)


def small_kernel(heads_half, one_ref, two_ref, three_ref, order_ref, bias_ref, onehot_ref, loss_ref, mine_ref, out_ref):
    width = one_ref.shape[1]
    gains = jnp.concatenate([one_ref[...], two_ref[...], three_ref[...], jnp.zeros((5, width), F32)], axis=0)
    high = gains.astype(BF16)
    rest = (gains - high.astype(F32)).astype(BF16)
    gains = dot_nt(high, order_ref[...]) + dot_nt(rest, order_ref[...])
    out_ref[...] = jnp.zeros_like(out_ref)
    across = width // LANES
    for i in range(3):
        for j in range(across):
            at = i * across + j
            out_ref[at : at + 1, :] = gains[i : i + 1, j * LANES : (j + 1) * LANES]
    at = 3 * across
    lane = lax.broadcasted_iota(jnp.int32, (1, LANES), 1)
    out_ref[at : at + 1, :] = jnp.where(lane == 0, loss_ref[...], 0.0)
    bias = bias_ref[...]
    heads = 2 * heads_half
    row = lax.broadcasted_iota(jnp.int32, (LANES, bias.shape[0]), 0)
    column = lax.broadcasted_iota(jnp.int32, (LANES, bias.shape[0]), 1)
    source = row + jnp.where(mine_ref[...] == 0, 0, heads_half)
    source = jnp.where(source >= heads, source - heads, source)
    pick = jnp.where((column == 8 * (source // 2) + source % 2) & (row < heads), 1.0, 0.0)
    bias = split_dot(pick.astype(BF16), bias)
    high = bias.astype(BF16)
    rest = (bias - high.astype(F32)).astype(BF16)
    table = dot_nt(high, onehot_ref[...]) + dot_nt(rest, onehot_ref[...])
    count = table.shape[1]
    a_row = LANES // count
    for head in range(heads):
        place = head % a_row * count
        line = at + 1 + head // a_row
        out_ref[line : line + 1, place : place + count] = table[head : head + 1, :]


def member_of(seg_ref, sent_count):
    ids = lax.broadcasted_iota(jnp.int32, (sent_count, seg_ref.shape[1]), 0)
    hit = jnp.where(seg_ref[...] == ids, 1.0, 0.0)
    return hit.astype(BF16), jnp.sum(hit, axis=1, keepdims=True)


def tail_body(acc, value_ref, gains_ref, seg_ref, own_ref, other_ref, hidden_ref, inverse_ref, pooled_ref, unit_ref, low_ref, scale_ref, high, rest):
    hidden = value_ref[...] + acc[...]
    inverse = lax.rsqrt(jnp.mean(hidden * hidden, axis=1, keepdims=True) + EPSILON)
    hidden_ref[...] = hidden
    inverse_ref[...] = inverse
    final = hidden_ref[...] * inverse * gains_ref[2:3, :]
    high[...] = final.astype(BF16)
    rest[...] = (final - high[...].astype(F32)).astype(BF16)
    sents, count = member_of(seg_ref, pooled_ref.shape[0])
    pooled = ((dot(sents, high[...]) + dot(sents, rest[...])) / count).astype(BF16)
    pooled_ref[...] = pooled
    half = own_ref.shape[1]
    left = dot(pooled, own_ref[...])
    right = dot(pooled, other_ref[...])
    square = jnp.sum(left * left, axis=1, keepdims=True) + jnp.sum(right * right, axis=1, keepdims=True)
    scale = lax.rsqrt(square + EPSILON)
    scale_ref[...] = scale
    for at, value in ((0, left * scale), (half, right * scale)):
        unit_ref[:, at : at + half] = value
        low_ref[:, at : at + half] = value.astype(BF16)


def head_call(quarters, unit, scale, partner, column, sentence_loads, out_shapes):
    loads = [part(q) for q in (*quarters, unit, scale, partner, column)] + sentence_loads
    quarter = quarters[0].shape[0]
    total = 4 * quarter

    def run(get, loss_ref, embed_ref, *refs):
        *back_refs, every = refs
        for i in range(4):
            every[i * quarter : (i + 1) * quarter] = get(i)[...]
        unit, scale, partner, columns_id = (get(i)[...] for i in range(4, 8))
        partner = as_columns(
            jnp.concatenate([partner, jnp.zeros((1, LANES - partner.shape[1]), jnp.int32)], axis=1)
        )[: partner.shape[1], 0:1]
        own_count = unit.shape[0]
        sims = dot_nt(every[...], every[...]) * SOFTMAX_TEMP
        row = lax.broadcasted_iota(jnp.int32, (total, total), 0)
        column = lax.broadcasted_iota(jnp.int32, (total, total), 1)
        sims = jnp.where(row == column, NEG_FILL, sims)
        top = jnp.max(sims, axis=0, keepdims=True)
        lse_row = top + jnp.log(jnp.sum(jnp.exp(sims - top), axis=0, keepdims=True))
        own = sims[:own_count]
        own_top = jnp.max(own, axis=1, keepdims=True)
        own_lse = own_top + jnp.log(jnp.sum(jnp.exp(own - own_top), axis=1, keepdims=True))
        is_target = columns_id.astype(F32) == partner
        hit = jnp.where(is_target, 1.0, 0.0)
        target = jnp.sum(jnp.where(is_target, own, 0.0), axis=1, keepdims=True)
        loss_ref[...] = jnp.sum(own_lse - target, axis=0, keepdims=True)
        d_rows = (LOSS_SCALE * (jnp.exp(own - own_lse) - hit)).astype(BF16)
        d_cols = (LOSS_SCALE * (jnp.exp(own - lse_row) - hit)).astype(BF16)
        d_unit = SOFTMAX_TEMP * (dot(d_rows, every[...]) + dot(d_cols, every[...]))
        inner = jnp.sum(d_unit * unit, axis=1, keepdims=True)
        d_embed = (scale * (d_unit - unit * inner)).astype(BF16)
        embed_ref[...] = d_embed
        sentence_back(d_embed, [get(8 + i) for i in range(len(sentence_loads))], *back_refs)

    return stream("head", loads, out_shapes, run, [pltpu.VMEM((total, unit.shape[1]), BF16)])


def sentence_call(embed, sentence_loads, out_shapes):
    def run(get, *back_refs):
        sentence_back(get(0)[...], [get(1 + i) for i in range(len(sentence_loads))], *back_refs)

    return stream("sentence", [part(embed)] + sentence_loads, out_shapes, run)


def sentence_back(d_embed, sources, hidden_ref, low_ref, gain_out):
    seg_ref, own_ref, other_ref, value_ref, inverse_ref, gains_ref = sources
    half = own_ref.shape[1]
    d_pooled = dot_nt(d_embed[:, :half], own_ref[...]) + dot_nt(d_embed[:, half:], other_ref[...])
    sents, count = member_of(seg_ref, d_embed.shape[0])
    d_final = split_dot(sents, d_pooled / count, ((0,), (0,)))
    d_value, d_gain = norm_back(value_ref[...], inverse_ref[...], gains_ref[2:3, :], d_final)
    hidden_ref[...] = d_value
    low_ref[...] = d_value.astype(BF16)
    gain_out[...] = d_gain


def whole_call(body, args, out_shapes, scratch=(), name=None):
    return pl.pallas_call(
        body,
        out_shape=tuple(out_shapes),
        in_specs=[pl.BlockSpec(memory_space=pltpu.VMEM)] * len(args),
        out_specs=tuple(pl.BlockSpec(memory_space=pltpu.VMEM) for _ in out_shapes),
        scratch_shapes=scratch,
        compiler_params=params(),
        cost_estimate=cost(0, 0),
        name=name,
    )(*args)


def shape_of(kind, *dims):
    return jax.ShapeDtypeStruct(dims, kind)


def _stack_heads(part):
    lane = lax.broadcasted_iota(jnp.int32, part.shape, 1)
    zero = jnp.zeros_like(part)
    first = lane < LANES // 2
    return jnp.concatenate(
        [jnp.where(first, part, zero), jnp.where(first, zero, part)], axis=0
    )


def _unstack_heads(both):
    half = both.shape[0] // 2
    lane = lax.broadcasted_iota(jnp.int32, (half, LANES), 1)
    return jnp.where(lane < LANES // 2, both[:half], both[half:])


def _pad_keys(pad, ref):
    seq = ref.shape[0]
    pad[0:REACH] = jnp.zeros((REACH, LANES), pad.dtype)
    pad[REACH + seq :] = jnp.zeros((REACH, LANES), pad.dtype)
    pad[REACH : REACH + seq] = ref[...]


def _query_bits(shape):
    return lax.broadcasted_iota(jnp.int32, shape, 0) & (QB - 1)


def as_columns(values):
    count, length = values.shape
    side = max(LANES, length)
    square = jnp.concatenate([values.astype(F32), jnp.zeros((side - count, length), F32)], axis=0)
    return square.T


def attend_forward_kernel(
    q_ref, k_ref, v_ref, segq_ref, segk_ref, rel_ref, ctx_ref, probs_ref, kpad, vpad, mask, scores
):
    seq = q_ref.shape[0]
    blocks = seq // QB
    _pad_keys(kpad, k_ref)
    _pad_keys(vpad, v_ref)

    @pl.when(pl.program_id(0) == 0)
    def _():
        keys = as_columns(segk_ref[...])
        for b in range(blocks):
            same = keys[:, b : b + 1] == segq_ref[b : b + 1, :].astype(F32)
            mask[b] = jnp.where(same, 0.0, NEG_FILL)

    rel = rel_ref[0]
    row = lax.broadcasted_iota(jnp.int32, (2 * QB, WIN), 0)
    bias = jnp.where(row < QB, rel[0:1, :], rel[1:2, :])
    bits = _query_bits((2 * QB, WIN))
    step = 1
    while step < QB:
        bias = jnp.where((bits & step) != 0, pltpu.roll(bias, step, 1), bias)
        step *= 2
    bias = bias.T
    for b in range(blocks):
        query = _stack_heads(q_ref[b * QB : (b + 1) * QB] * jnp.asarray(SCORE_SCALE, BF16))
        scores[b] = dot_nt(kpad[b * QB : b * QB + WIN], query)
    values = scores[...] + bias[None] + mask[...]
    top = jnp.max(values, axis=1, keepdims=True)
    shifted = jnp.exp(values - top)
    total = jnp.sum(shifted, axis=1, keepdims=True)
    probs_ref[0] = (shifted * (1.0 / total)).astype(BF16)
    for b in range(blocks):
        part = dot_tn(probs_ref[0, b], vpad[b * QB : b * QB + WIN])
        ctx_ref[b * QB : (b + 1) * QB] = _unstack_heads(part).astype(BF16)


def attend_backward_kernel(
    q_ref, k_ref, v_ref, dctx_ref, probs_ref, dqkv_ref, dbias_ref,
    kpad, vpad, dk_acc, dv_acc, d_probs, d_low,
):
    seq = q_ref.shape[0]
    pair = pl.program_id(0)
    side = pl.num_programs(0) // 2
    later = pair // side
    q_at = pl.ds(pl.multiple_of(pair * LANES, LANES), LANES)
    k_at = pl.ds(pl.multiple_of((pair + 2 * side + later * side) * LANES, LANES), LANES)
    v_at = pl.ds(pl.multiple_of((pair + 3 * side + later * side) * LANES, LANES), LANES)
    blocks = seq // QB
    _pad_keys(kpad, k_ref)
    _pad_keys(vpad, v_ref)
    dk_acc[...] = jnp.zeros_like(dk_acc)
    dv_acc[...] = jnp.zeros_like(dv_acc)
    for b in range(blocks):
        window = slice(b * QB, b * QB + WIN)
        d_ctx = _stack_heads(dctx_ref[b * QB : (b + 1) * QB])
        d_probs[b] = dot_nt(vpad[window], d_ctx)
        dv_acc[window] += dot(probs_ref[0, b], d_ctx)
    probs = probs_ref[0].astype(F32)
    product = probs * d_probs[...]
    inner = jnp.sum(product, axis=1, keepdims=True)
    d_scores = product - probs * inner
    d_low[...] = d_scores.astype(BF16)
    total = jnp.sum(d_scores, axis=0).T
    for b in range(blocks):
        here = slice(b * QB, (b + 1) * QB)
        window = slice(b * QB, b * QB + WIN)
        query = _stack_heads(q_ref[here] * jnp.asarray(SCORE_SCALE, BF16))
        dk_acc[window] += dot(d_low[b], query)
        d_query = _unstack_heads(dot_tn(d_low[b], kpad[window])) * SCORE_SCALE
        dqkv_ref[here, q_at] = d_query.astype(BF16)
    dqkv_ref[:, k_at] = dk_acc[REACH : REACH + seq].astype(BF16)
    dqkv_ref[:, v_at] = dv_acc[REACH : REACH + seq].astype(BF16)
    bits = _query_bits((2 * QB, WIN))
    step = 1
    while step < QB:
        total = jnp.where((bits & step) != 0, pltpu.roll(total, WIN - step, 1), total)
        step *= 2
    first = jnp.sum(total[:QB], axis=0, keepdims=True)
    second = jnp.sum(total[QB:], axis=0, keepdims=True)
    dbias_ref[0] = jnp.concatenate([first, second, jnp.zeros((6, WIN), F32)], axis=0)


def _qkv_specs(seq, pairs):
    def spec(kind):
        return pl.BlockSpec((seq, LANES), lambda p: (0, kind * pairs + p))

    return [spec(0), spec(1), spec(2)]


def attend_forward(qkv, twice, windows, rel_window):
    seq = qkv.shape[0]
    pairs = rel_window.shape[0]
    blocks = seq // QB
    return pl.pallas_call(
        attend_forward_kernel,
        grid=(pairs,),
        out_shape=(
            jax.ShapeDtypeStruct((seq, pairs * LANES), BF16),
            jax.ShapeDtypeStruct((pairs, blocks, WIN, 2 * QB), BF16),
        ),
        in_specs=_qkv_specs(seq, pairs)
        + [
            pl.BlockSpec((blocks, 2 * QB), lambda p: (0, 0)),
            pl.BlockSpec((blocks, WIN), lambda p: (0, 0)),
            pl.BlockSpec((1, 2, WIN), lambda p: (p, 0, 0)),
        ],
        out_specs=(
            pl.BlockSpec((seq, LANES), lambda p: (0, p)),
            pl.BlockSpec((1, blocks, WIN, 2 * QB), lambda p: (p, 0, 0, 0)),
        ),
        scratch_shapes=[pltpu.VMEM((seq + 2 * REACH, LANES), BF16)] * 2
        + [pltpu.VMEM((blocks, WIN, 2 * QB), F32)] * 2,
        compiler_params=params(),
        cost_estimate=cost(8 * seq * WIN * LANES * pairs * 4, 8 * seq * LANES * pairs),
        name="attend_forward",
    )(qkv, qkv, qkv, twice, windows, rel_window)


def attend_backward(qkv, d_context, probs):
    seq = qkv.shape[0]
    pairs = probs.shape[0]
    blocks = seq // QB
    lane_block = pl.BlockSpec((seq, LANES), lambda p: (0, p))
    return pl.pallas_call(
        attend_backward_kernel,
        grid=(pairs,),
        out_shape=(
            jax.ShapeDtypeStruct((seq, 3 * pairs * LANES), BF16),
            jax.ShapeDtypeStruct((pairs, 8, WIN), F32),
        ),
        in_specs=_qkv_specs(seq, pairs)
        + [
            lane_block,
            pl.BlockSpec((1, blocks, WIN, 2 * QB), lambda p: (p, 0, 0, 0)),
        ],
        out_specs=(
            pl.BlockSpec((seq, 3 * pairs * LANES), lambda p: (0, 0)),
            pl.BlockSpec((1, 8, WIN), lambda p: (p, 0, 0)),
        ),
        scratch_shapes=[pltpu.VMEM((seq + 2 * REACH, LANES), BF16)] * 2
        + [pltpu.VMEM((seq + 2 * REACH, LANES), F32)] * 2
        + [pltpu.VMEM((blocks, WIN, 2 * QB), F32), pltpu.VMEM((blocks, WIN, 2 * QB), BF16)],
        compiler_params=params(),
        cost_estimate=cost(16 * seq * WIN * LANES * pairs * 4, 16 * seq * LANES * pairs),
        name="attend_backward",
    )(qkv, qkv, qkv, d_context, probs)


CORE = 1
CROSS = 2


def hop(value, mask):
    size = lax.axis_size("dp")
    return lax.ppermute(value, "dp", [(i, i ^ mask) for i in range(size)])


def over(value):
    return lax.ppermute(value, "mp", [(0, 1), (1, 0)])


def cross(value):
    return hop(value, CROSS)


def core(value):
    return hop(value, CORE)


def go(waits, *sends, keep=(), join=True):
    values = [value for _, value in sends]
    held = lax.optimization_barrier((*values, *keep, *waits))
    results = [how(value) for (how, _), value in zip(sends, held)]
    if join:
        results = list(lax.optimization_barrier(tuple(results)))
    return results + list(held[len(values) : len(values) + len(keep)])


def slot_masks(size):
    rest = size // 4
    return [z * 4 + x * 2 + c for c in range(2) for x in range(2) for z in range(rest)]


def strides(size):
    found = []
    stride = 4
    while stride < size:
        found.append(stride)
        stride *= 2
    return found


def gather_near(shard, waits, widths=None):
    size = lax.axis_size("dp")
    pieces = [shard]
    stride = 4
    while stride < size:
        radix = min(4, size // stride)
        shard = jnp.concatenate(pieces, axis=0) if len(pieces) > 1 else shard
        sends = [(functools.partial(hop, mask=j * stride), shard) for j in range(1, radix)]
        pieces = [shard] + go(waits, *sends)
        stride *= radix
    return jnp.concatenate(pieces, axis=0) if widths is None else stack_rows(pieces, widths)


def rows(*pieces):
    return jnp.concatenate(pieces, axis=0)


def columns(*pieces):
    return jnp.concatenate(pieces, axis=1)


def gather_weights(start, later, five, n_one, n_three, early, begin, between):
    size = lax.axis_size("dp")
    steps = strides(size)
    n_two = start.shape[1] - n_one
    n_four = later.shape[1] - n_three
    n_five = five.shape[1]
    n_early = n_three * 2 // 3
    short = len(steps) == 2
    if short:
        got = go((), *((functools.partial(hop, mask=4 * j), start) for j in range(1, 4)))
        more = hop(later, 4)
        five_x = cross(five)
        one, two = stack_rows([start, *got], (n_one, n_two))
        later = stack_rows([later, more], (n_early, later.shape[1] - n_early))
        (five,) = stack_rows([five, five_x], (n_five,))
        wide_step = functools.partial(hop, mask=steps[1])
    else:
        one, two = gather_near(start, (), (n_one, n_two))
        five = gather_near(five, ())
        later = [later[:, :n_early], later[:, n_early:]]

        def wide_step(value):
            whole = gather_near(value, ())
            return whole[value.shape[0] :]

    one_x, two_y, more, five_y = go(
        early, (cross, one), (over, two), (wide_step, later[0]), (over, five)
    )
    (one,) = stack_rows([one, one_x], (n_one,))
    (two,) = stack_rows([two, two_y], (n_two,))
    (five,) = stack_rows([five, five_y], (n_five,))
    one_y, two_x, one_c, more_b, five_more = go(
        (),
        (over, one),
        (cross, two),
        (core, one),
        (wide_step, later[1]),
        (functools.partial(hop, mask=4) if short else cross, five),
    )
    n_first = n_five // 3 if short else n_five
    five, *five_b = stack_rows([five, five_more], (n_first, n_five - n_first) if short else (n_five,))
    if short:
        have = later[0].shape[0]

        def put(near_a, near_b, far_a, far_b, three_ref, four_ref):
            for at, left, right in ((0, near_a, near_b), (have, far_a, far_b)):
                here = slice(at, at + have)
                three_ref[here, :n_early] = left[...]
                three_ref[here, n_early:] = right[:, : n_three - n_early]
                four_ref[here] = right[:, n_three - n_early :]

        three, four = whole_call(
            put,
            (*later, more, more_b),
            (shape_of(BF16, 2 * have, n_three), shape_of(BF16, 2 * have, n_four)),
            (),
            "put_rows",
        )
    else:
        later = rows(columns(*later), columns(more, more_b))
        three, four = later[:, :n_three], later[:, n_three:]
    three_x, four_y, one_yc, two_c, five_more = go(
        (),
        (cross, three),
        (over, four),
        (core, one_y),
        (core, two),
        (functools.partial(hop, mask=8) if short else core, five),
    )
    (three,) = stack_rows([three, three_x], (n_three,))
    (four,) = stack_rows([four, four_y], (n_four,))
    three_y, four_x, three_c, two_xc, *kept = go(
        (),
        (over, three),
        (cross, four),
        (core, three),
        (core, two_x),
        *((functools.partial(hop, mask=8), value) for value in five_b),
        keep=(one, one_c, one_y, one_yc, two, two_x, two_c, *early),
        join=False,
    )
    five_far, kept = kept[: len(five_b)], kept[len(five_b) :]
    one, one_c, one_y, one_yc, two, two_x, two_c, *early = kept
    first, second = along_x(one, one_c, one_y, one_yc), along_y(two, two_x, two_c, two_xc)
    done = between(begin(first, early), second, early)
    three_y, four_x, three_c, *rest = lax.optimization_barrier(
        (three_y, four_x, three_c, *five_far, *done)
    )
    five_far, done = rest[: len(five_far)], rest[len(five_far) :]
    waits = ()
    if short:

        def put_five(near_a, far_a, near_b, far_b, out_ref):
            count = near_a.shape[0]
            out_ref[:count, :n_first] = near_a[...]
            out_ref[count:, :n_first] = far_a[...]
            out_ref[:count, n_first:] = near_b[...]
            out_ref[count:, n_first:] = far_b[...]

        (all_five,) = whole_call(
            put_five,
            (five, five_more, *five_b, *five_far),
            (shape_of(BF16, 2 * five.shape[0], n_five),),
            (),
            "put_five",
        )
        four_c, four_xc, three_yc, five_c, *done = go(
            waits, (core, four), (core, four_x), (core, three_y), (core, all_five), keep=done, join=False
        )
        block = start.shape[0]
        fifth = tuple(
            tuple(
                (array, z * 4 * block + side * 2 * block + x * block, block)
                for array in (all_five, five_c)
                for x in range(2)
                for z in range(4)
            )
            for side in range(2)
        )
    else:
        four_c, four_xc, three_yc, *done = go(
            waits, (core, four), (core, four_x), (core, three_y), keep=done, join=False
        )
        half = five.shape[0] // 2
        fifth = along_y(five[:half], five[half:], five_more[:half], five_more[half:])
    third, fourth = along_x(three, three_c, three_y, three_yc), along_y(four, four_x, four_c, four_xc)
    return first, second, third, fourth, fifth, early, done


def along_x(near, near_c, other, other_c):
    count = near.shape[0]
    return ((near, 0, count), (near_c, 0, count)), ((other, 0, count), (other_c, 0, count))


def along_y(near, side, near_c, side_c):
    count = near.shape[0] // 2
    return tuple(
        tuple((array, at, count) for array in (near, side, near_c, side_c)) for at in (0, count)
    )


def pack(name, sources, mib):
    widths = [count for *_, count in sources]
    block = sources[0][0].shape[0]

    def run(*refs):
        ins, out = refs[: len(sources)], refs[len(sources)]
        buffers, sem = refs[len(sources) + 1 : -1], refs[-1]
        copies = []
        for i, (_, first, count) in enumerate(sources):
            copy = pltpu.make_async_copy(ins[i].at[:, pl.ds(first, count)], buffers[i], sem.at[i])
            copy.start()
            copies.append(copy)
        at = 0
        for copy, buffer, width in zip(copies, buffers, widths):
            copy.wait()
            out[:, at : at + width] = buffer[...]
            at += width

    return pl.pallas_call(
        run,
        out_shape=shape_of(BF16, block, sum(widths)),
        in_specs=[pl.BlockSpec(memory_space=pltpu.HBM)] * len(sources),
        out_specs=pl.BlockSpec(memory_space=pltpu.VMEM),
        scratch_shapes=[pltpu.VMEM((block, width), BF16) for width in widths]
        + [pltpu.SemaphoreType.DMA((len(sources),))],
        compiler_params=params(mib),
        cost_estimate=cost(0, 0),
        name=name,
    )(*(array for array, *_ in sources))


def gather_dp(shard):
    near = gather_near(shard, ())
    side, c_near = go((near,), (cross, near), (core, near))
    return near, side, c_near, core(side)


def low(value):
    return value.astype(BF16)


def add(left, right):
    return (left.astype(F32) + right.astype(F32)).astype(BF16)


def product(left, begin, end, right, got=None):
    value = dot_tn(left[:, begin:end], right)
    if got is not None:
        value = value + got.astype(F32)
    return low(value)


def rest_start(value):
    half = value.shape[0] // 2
    return value[half:], value[:half]


def sum_half(value, send):
    gone, stays = rest_start(value)
    return stays + send(low(gone)).astype(F32)


def rest_hops(size):
    return [functools.partial(hop, mask=stride) for stride in reversed(strides(size))]


def shards(
    tokens,
    seg_ids,
    buckets,
    labels,
    w_query,
    w_key,
    w_value,
    w_out,
    w_in,
    w_back,
    gain_attn,
    gain_ffn,
    gain_final,
    w_pool,
    rel_table,
):
    micro_count, seq, width = tokens.shape
    size = lax.axis_size("dp")
    me = lax.axis_index("dp")
    mine = lax.axis_index("mp")
    block = width // size
    inner_half = w_query.shape[1]
    hidden_half = w_in.shape[1]
    sent_local = labels.shape[1]
    bucket_count = rel_table.shape[0]
    heads_half = rel_table.shape[1]
    masks = slot_masks(size)

    x_own = lax.dynamic_index_in_dim(tokens, mine, 0, keepdims=False)
    segments = lax.dynamic_index_in_dim(seg_ids, mine, 0, keepdims=False)[0]
    partner = lax.dynamic_index_in_dim(labels, mine, 0, keepdims=False)

    slot_block = jnp.stack([jnp.bitwise_xor(me, m) for m in masks]).astype(jnp.int32)
    source = (slot_block[:, None] * block + jnp.arange(block, dtype=jnp.int32)[None, :]).reshape(-1)
    order = (jnp.arange(width, dtype=jnp.int32)[:, None] == source[None, :]).astype(BF16)
    order = lax.optimization_barrier(order)
    inputs = dot(x_own, order)


    row_f32 = shape_of(F32, seq, width)
    row_low = shape_of(BF16, seq, width)
    column_f32 = shape_of(F32, seq, 1)
    gain_f32 = shape_of(F32, 1, width)
    heads = 3 * inner_half
    piece = hidden_half // 2
    halves = [(side, i * inner_half, inner_half) for side in range(2) for i in range(2)]

    def hidden_blocks(weights, first_col=0):
        return [(weights[side], first_col + col, n) for side, col, n in halves]

    def begin(first, early):
        inputs, rel_window, twice, windows, *_ = early
        qkv, normed1_low, inverse1, gains = qkv_call(inputs, first, inner_half)
        context, probs = attend_forward(qkv, twice, windows, rel_window)
        return qkv, normed1_low, inverse1, gains, context, probs

    def between(started, second, early):
        qkv, normed1_low, inverse1, gains, context, probs = started
        inputs = early[0]
        hidden1, inverse2, normed2_low = narrow(
            "attn_out",
            [(context, i * inner_half, second[i], piece, inner_half) for i in range(2)],
            (inputs, gains),
            (row_f32, column_f32, row_low),
            functools.partial(norm_body, 1),
        )
        act0, slope0 = wide("act0", normed2_low, hidden_blocks(second), (), gelu_both, 2)
        return normed1_low, inverse1, gains, qkv, context, probs, hidden1, inverse2, normed2_low, act0, slope0

    gains_col = jnp.pad(
        jnp.stack([gain_attn, gain_ffn, gain_final], axis=1), ((0, 0), (0, LANES - 3))
    )
    pool_half = w_pool.shape[1] // 2
    pool_own = lax.dynamic_slice_in_dim(w_pool, mine * pool_half, pool_half, axis=1)
    back_shard = w_back.T
    if block % 16:
        start = columns(w_query, w_key, w_value, gains_col, w_in[:, :piece], w_out.T)
        later = columns(back_shard[:, :piece], pool_own, w_in[:, piece:])
    else:
        start = pack(
            "pack_start",
            [(w, 0, inner_half) for w in (w_query, w_key, w_value)]
            + [(gains_col, 0, LANES), (w_in, 0, piece), (w_out.T, 0, inner_half)],
            60,
        )
        back_shard, w_in, _ = lax.optimization_barrier((back_shard, w_in, start))
        later = pack(
            "pack_later",
            [
                (back_shard, 0, piece),
                (pool_own, 0, pool_half),
                (w_in, piece, piece),
            ],
            16,
        )
    fifth = lax.optimization_barrier((back_shard[:, piece:], start))[0]
    rel_other = over(lax.optimization_barrier((rel_table, start))[0])
    rel_all = jnp.concatenate([rel_table, rel_other], axis=1).astype(F32)
    near_buckets = lax.slice_in_dim(buckets, seq - 1 - REACH, seq - 1 - REACH + WIN)
    onehot = (near_buckets[None, :] == jnp.arange(bucket_count, dtype=jnp.int32)[:, None]).astype(F32)
    onehot = lax.optimization_barrier(low(onehot))
    rel_window = dot(rel_all, onehot.astype(F32), ((0,), (0,)), HIGHEST).reshape(heads_half, 2, WIN)
    padded = jnp.pad(segments, (REACH, REACH), constant_values=-1)
    windows = jnp.stack([padded[at : at + WIN] for at in range(0, seq, QB)])
    twice = jnp.tile(segments.reshape(seq // QB, QB), (1, 2))
    local_ids = jnp.arange(sent_local, dtype=jnp.int32)
    column_id = (slot_block[:, None] * sent_local + local_ids[None, :]).reshape(1, -1)
    early = (
        inputs, rel_window, twice, windows, order, onehot, column_id, partner[None, :], segments[None, :], mine.reshape(1, 1),
        (me * block).astype(jnp.uint32), (mine * heads_half).astype(jnp.uint32)
    )
    first, second, third, fourth, fifth, early, done = gather_weights(
        start,
        later,
        fifth,
        heads + LANES,
        piece + pool_half,
        early,
        begin,
        between,
    )
    inputs, rel_window, twice, windows, order, onehot, column_id, partner, seg_lane, mine_array, gain_at, table_at = early
    normed1_low, inverse1, gains, qkv, context, probs, hidden1, inverse2, normed2_low, act0, slope0 = done

    act1, up_kept = wide("act1", normed2_low, hidden_blocks(fourth), (), gelu_only, 2)
    pool_loads = [weight(side, piece, pool_half) for side in third]
    hidden2, inverse3, pooled_low, unit, unit_low, scale = narrow(
        "ffn_out",
        [(act0, i * piece, third[i], 0, piece) for i in range(2)]
        + [(act1, i * piece, fifth[i], 0, piece) for i in range(2)],
        (hidden1, gains, seg_lane, *pool_loads),
        (
            row_f32,
            column_f32,
            shape_of(BF16, sent_local, width),
            shape_of(F32, sent_local, width),
            shape_of(BF16, sent_local, width),
            shape_of(F32, sent_local, 1),
        ),
        tail_body,
        [pltpu.VMEM((seq, width), BF16)] * 2,
    )
    quarters = gather_dp(unit_low)

    total_sent = column_id.shape[1]
    sentence_loads = [part(seg_lane), *pool_loads, part(hidden2), part(inverse3), part(gains)]
    back_shapes = (row_f32, row_low, gain_f32)
    if total_sent <= 1024:
        loss_local, embed_low, d_hidden2, ffn_low, d_gain3 = head_call(
            quarters,
            unit,
            scale,
            partner,
            column_id,
            sentence_loads,
            (shape_of(F32, 1, 1), shape_of(BF16, sent_local, width), *back_shapes),
        )
    else:
        every = rows(*quarters)
        position = jnp.arange(total_sent, dtype=jnp.int32)
        sims = dot_nt(every, every) * SOFTMAX_TEMP
        sims = jnp.where(position[:, None] == position[None, :], NEG_FILL, sims)
        lse_row = jax.nn.logsumexp(sims, axis=0, keepdims=True)
        own_sims = sims[:sent_local]
        own_lse = jax.nn.logsumexp(own_sims, axis=1, keepdims=True)
        is_target = column_id == partner.reshape(-1, 1)
        target = jnp.sum(jnp.where(is_target, own_sims, 0.0), axis=-1, keepdims=True)
        loss_local = jnp.sum(own_lse - target)
        hit = is_target.astype(F32)
        d_rows = low(LOSS_SCALE * (jnp.exp(own_sims - own_lse) - hit))
        d_cols = low(LOSS_SCALE * (jnp.exp(own_sims - lse_row) - hit))
        d_unit = SOFTMAX_TEMP * (dot(d_rows, every) + dot(d_cols, every))
        embed_low = low(scale * (d_unit - unit * jnp.sum(d_unit * unit, axis=-1, keepdims=True)))
        d_hidden2, ffn_low, d_gain3 = sentence_call(embed_low, sentence_loads, back_shapes)

    half = width // 2
    quarter = width // 4

    back0_sent, back1_sent = gradients("back_sent", ffn_low, half, half, (act0, act1))
    (pool_sent,) = gradients("pool_sent", pooled_low, half, half, (embed_low,))
    back0_got, back1_got, pool_got, ffn_later = go(
        (), (core, back0_sent), (core, back1_sent), (core, pool_sent), keep=(ffn_low,), join=False
    )
    pool_hi = product(pooled_low, quarter, half, embed_low, pool_got[quarter:])
    pool_lo = product(pooled_low, 0, quarter, embed_low, pool_got[:quarter])
    up0 = wide("up0", ffn_later, hidden_blocks(third), (slope0,), times_slope)

    back_hi = product(ffn_low, quarter, half, act0, back0_got[quarter:])
    back_lo = product(ffn_low, 0, quarter, act0, back0_got[:quarter])
    back_own = product(ffn_low, 0, half, act1[:, :piece], back1_got[:, :piece])
    back_oth = product(ffn_low, 0, half, act1[:, piece:], back1_got[:, piece:])
    got_lo, got_own, got_pool, ffn_later, up0, back_lo, back_own, pool_lo = go(
        (),
        (cross, back_hi),
        (over, back_oth),
        (cross, pool_hi),
        keep=(ffn_later, up0, back_lo, back_own, pool_lo),
    )
    up1 = wide("up1", ffn_later, hidden_blocks(fifth), (up_kept,), times_slope_of)
    in0_sent, in1_sent = gradients("in_sent", normed2_low, half, half, (up0, up1))
    in0_got, in1_got, up0, up1 = go((), (core, in0_sent), (core, in1_sent), keep=(up0, up1))
    attn_low, d_gain2, d_hidden1 = narrow(
        "ffn_in_back",
        [(up0, i * piece, second[i], 0, piece) for i in range(2)]
        + [(up1, i * piece, fourth[i], 0, piece) for i in range(2)],
        (hidden1, inverse2, gains, d_hidden2),
        (row_low, gain_f32, row_f32),
        functools.partial(back_body, 1),
    )
    d_context = wide("d_context", attn_low, [(second[side], piece, inner_half) for side in range(2)])

    pool_lo = add(pool_lo, got_pool)
    back_lo = add(back_lo, got_lo)
    back_own = add(back_own, got_own)
    in_hi = product(normed2_low, quarter, half, up0, in0_got[quarter:])
    in_lo = product(normed2_low, 0, quarter, up0, in0_got[:quarter])
    in_own = product(normed2_low, 0, half, up1[:, :piece], in1_got[:, :piece])
    in_oth = product(normed2_low, 0, half, up1[:, piece:], in1_got[:, piece:])
    got_first, got_x, got_in_own, d_context, pool_lo, back_lo, back_own, in_lo, in_own = go(
        (got_lo, got_own),
        (over, columns(back_lo[:, piece:], pool_lo[:, pool_half:])),
        (cross, columns(back_own[quarter:], in_hi)),
        (over, in_oth),
        keep=(d_context, pool_lo, back_lo, back_own, in_lo, in_own),
        join=False,
    )
    d_qkv, d_bias = attend_backward(qkv, d_context, probs)
    query_both = 2 * inner_half
    late_sent = sent_columns("late_sent", half, ((attn_low, context), (normed1_low, d_qkv)))
    late_got, d_qkv_later = go((), (core, late_sent), keep=(d_qkv,), join=False)
    grad_slots, d_gain1 = narrow(
        "qkv_back",
        [(d_qkv_later, i * inner_half, first[i], 0, inner_half) for i in range(2)]
        + [(d_qkv_later, (1 + i) * query_both, first[i], inner_half, query_both) for i in range(2)],
        (inputs, inverse1, gains, d_hidden1),
        (row_low, gain_f32),
        functools.partial(back_body, 0),
    )

    table_row = 3 * (width // LANES) + 1
    table_rows = -(-2 * heads_half * bucket_count // LANES)
    small_rows = -(-(table_row + table_rows) // 8) * 8
    (flat,) = whole_call(
        functools.partial(small_kernel, heads_half),
        (d_gain1, d_gain2, d_gain3, order, d_bias.reshape(-1, WIN), onehot, loss_local.reshape(1, 1), mine_array),
        (shape_of(F32, small_rows, LANES),),
        (),
        "small",
    )
    (grad_own,) = whole_call(turn_kernel, (grad_slots, order), (row_low,), (), "turn")
    flat_got, flat = go((), (over, flat), keep=(flat,), join=False)
    got_first, got_x, got_in_own = lax.optimization_barrier((got_first, got_x, got_in_own))
    flat = flat + flat_got
    got_second, got_in_lo = got_x[:, :piece], got_x[:, piece:]

    far = rest_hops(size)
    back_all = columns(
        add(back_lo[:, :piece], got_first[:, :piece]),
        add(back_own[:quarter], got_second),
        add(pool_lo[:, :pool_half], got_first[:, piece:]),
    )
    back_rest, back_stay = rest_start(back_all)
    in_lo = add(in_lo, got_in_lo)
    in_own = add(in_own, got_in_own)
    out_got, qkv_got = late_got[:, :query_both], late_got[:, query_both:]
    out_hi = product(attn_low, quarter, half, context, out_got[quarter:])
    out_lo = product(attn_low, 0, quarter, context, out_got[:quarter])
    query_hi = product(normed1_low, quarter, half, d_qkv[:, :query_both], qkv_got[quarter:, :query_both])
    query_lo = product(normed1_low, 0, quarter, d_qkv[:, :query_both], qkv_got[:quarter, :query_both])
    kv_own = product(
        normed1_low, 0, half, d_qkv[:, query_both : 2 * query_both], qkv_got[:, query_both : 2 * query_both]
    )
    kv_oth = product(normed1_low, 0, half, d_qkv[:, 2 * query_both :], qkv_got[:, 2 * query_both :])
    rest_hop = [functools.partial(hop, mask=j * 4) for j in range(1, min(4, size // 4))]
    back_more, got_first, got_x, got_kv, flat_got, back_stay, in_lo, in_own, out_lo, query_lo, kv_own, flat = go(
        (grad_own,),
        (far[0], back_rest),
        (over, in_lo[:, piece:]),
        (cross, columns(in_own[quarter:], out_hi, query_hi)),
        (over, kv_oth),
        (core, flat),
        keep=(back_stay, in_lo, in_own, out_lo, query_lo, kv_own, flat),
    )

    count = flat.shape[0]

    def in_two(value):
        high = value.astype(BF16).astype(F32)
        return jnp.concatenate([high, value - high], axis=0).astype(BF16)

    def from_two(pair):
        return pair[:count].astype(F32) + pair[count : 2 * count].astype(F32)

    def late_adds(
        stay, more, in_lo, got_first, in_own, got_x, out_lo, query_lo, kv_own, got_kv, flat, got_flat, *outs
    ):
        back_gone, back_keep, in_gone, in_keep, heads_gone, heads_keep, kv_gone, kv_keep, small = outs
        rows_z = stay.shape[0] // 2
        total = add(stay[...], more[...])
        back_keep[...] = total[:rows_z]
        back_gone[...] = total[rows_z:]
        rows_z = in_lo.shape[0] // 2
        for at, total in (
            (0, add(in_lo[:, :piece], got_first[...])),
            (piece, add(in_own[:quarter], got_x[:, :piece])),
        ):
            in_keep[:, at : at + piece] = total[:rows_z]
            in_gone[:, at : at + piece] = total[rows_z:]
        for i, ref in enumerate((out_lo, query_lo)):
            first_col = piece + i * query_both
            total = add(ref[...], got_x[:, first_col : first_col + query_both])
            heads_keep[:, i * inner_half : (i + 1) * inner_half] = total[:, :inner_half]
            heads_gone[:, i * inner_half : (i + 1) * inner_half] = total[:, inner_half:]
        kv_keep[...] = add(kv_own[:quarter], got_kv[:quarter])
        kv_gone[:, :query_both] = add(kv_own[quarter:], got_kv[quarter:])
        small[...] = flat[...] + got_flat[...]
        kv_gone[:, query_both:] = jnp.zeros((quarter, LANES), BF16)
        pair = in_two(small[...])
        kv_gone[: 2 * count, query_both:] = pair
        small[...] = from_two(pair)

    cut = [shape_of(BF16, back_stay.shape[0] // 2, back_stay.shape[1])] * 2
    cut += [shape_of(BF16, quarter // 2, hidden_half)] * 2 + [shape_of(BF16, quarter, query_both)] * 2
    cut += [
        shape_of(BF16, quarter, query_both + LANES),
        shape_of(BF16, quarter, query_both),
        shape_of(F32, count, LANES),
    ]
    back_rest, back_stay, in_rest, in_stay, heads_gone, heads_keep, kv_gone, kv_keep, flat = whole_call(
        late_adds,
        (back_stay, back_more, in_lo, got_first, in_own, got_x, out_lo, query_lo, kv_own, got_kv, flat, flat_got),
        cut,
        (),
        "late_adds",
    )
    early_rows = seq * 11 // 32
    back_more, in_more, got_first, got_second, grad_other, back_stay, in_stay, heads_keep, kv_keep, flat = go(
        (),
        (far[1], back_rest),
        (far[0], in_rest),
        (over, heads_gone),
        (cross, kv_gone),
        (over, grad_own[:early_rows]),
        keep=(back_stay, in_stay, heads_keep, kv_keep, flat),
    )

    def finish(value):
        value = value.astype(F32)
        for send in far[2:]:
            value = sum_half(value, send)
        return value

    n_last = query_both + query_both
    if len(far) == 2:
        rest = block
        late_rows = seq - early_rows

        def last_adds(stay, more, heads_ref, got_heads, kv_ref, got_kv, flat_ref, back_ref, back_got, own_ref, *outs):
            one, two, three, in_keep, keep, flat_out, tail, pool_ref = outs
            pool = add(back_ref[:, hidden_half:], back_got[:, hidden_half:])
            pool_ref[...] = pool
            tail[:late_rows] = own_ref[early_rows:]
            tail[late_rows:, :pool_half] = pool
            tail[late_rows:, pool_half:] = jnp.zeros((rest, width - pool_half), BF16)
            total = add(stay[...], more[...])
            in_keep[...] = total[:rest]
            one[:, LANES : LANES + hidden_half] = total[rest:]
            pair = in_two(flat_ref[...] + from_two(got_kv[:, query_both:]))
            flat_out[...] = from_two(pair)
            for i, (ref, at) in enumerate(((keep, 0), (one, LANES + hidden_half), (two, LANES), (three, LANES))):
                here = slice(i * rest, (i + 1) * rest)
                if i:
                    ref[:, :LANES] = pair
                ref[:, at : at + query_both] = add(heads_ref[here], got_heads[here])
                ref[:, at + query_both : at + n_last] = add(kv_ref[here], got_kv[here, :query_both])

        one, two, three, in_stay, last_stay, flat, tail, grad_pool = whole_call(
            last_adds,
            (in_stay, in_more, heads_keep, got_first, kv_keep, got_second, flat, back_stay, back_more, grad_own),
            (
                shape_of(BF16, rest, LANES + hidden_half + n_last),
                shape_of(BF16, rest, LANES + n_last),
                shape_of(BF16, rest, LANES + n_last),
                shape_of(BF16, rest, hidden_half),
                shape_of(BF16, rest, n_last),
                shape_of(F32, count, LANES),
                shape_of(BF16, late_rows + rest, width),
                shape_of(BF16, rest, pool_half),
            ),
            (),
            "last_adds",
        )
        got_one, got_two, got_three, got_tail, back_stay, back_more = go(
            (),
            (rest_hop[0], one),
            (rest_hop[1], two),
            (rest_hop[2], three),
            (over, tail),
            keep=(back_stay, back_more),
            join=False,
        )

        def back_final(stay, more, back_ref):
            back_ref[...] = stay[:, :hidden_half].astype(F32) + more[:, :hidden_half].astype(F32)

        (grad_back,) = whole_call(
            back_final, (back_stay, back_more), (shape_of(F32, rest, hidden_half),), (), "back_final"
        )

        def tokens_final(mine_ref, own_ref, first_ref, tail_ref, pool_own, out_ref, pool_ref):
            first = mine_ref[...] == 0
            own, other = pool_own[...].astype(F32), tail_ref[late_rows:, :pool_half].astype(F32)
            pool_ref[:, :pool_half] = jnp.where(first, own, other)
            pool_ref[:, pool_half:] = jnp.where(first, other, own)
            for at, count, ref in ((0, early_rows, first_ref), (early_rows, late_rows, tail_ref)):
                here = slice(at, at + count)
                own, other = own_ref[here].astype(F32), ref[:count].astype(F32)
                out_ref[0, here] = jnp.where(first, own, other).astype(BF16)
                out_ref[1, here] = jnp.where(first, other, own).astype(BF16)

        grad_tokens, grad_pool = whole_call(
            tokens_final,
            (mine_array, grad_own, grad_other, got_tail, grad_pool),
            (shape_of(BF16, 2, seq, width), shape_of(F32, rest, 2 * pool_half)),
            (),
            "tokens_final",
        )
        got_one, got_two, got_three, grad_tokens = lax.optimization_barrier(
            (got_one, got_two, got_three, grad_tokens)
        )

        def last_final(stay, in_keep, one_ref, two_ref, three_ref, flat_ref, *outs):
            in_ref, out_ref, q_ref, k_ref, v_ref, flat_out = outs
            in_ref[...] = in_keep[...].astype(F32) + one_ref[:, LANES : LANES + hidden_half].astype(F32)
            total = stay[...].astype(F32) + one_ref[:, LANES + hidden_half :].astype(F32)
            total = total + two_ref[:, LANES:].astype(F32) + three_ref[:, LANES:].astype(F32)
            for i, ref in enumerate((out_ref, q_ref, k_ref, v_ref)):
                ref[...] = total[:, i * inner_half : (i + 1) * inner_half]
            small = flat_ref[...]
            for ref in (one_ref, two_ref, three_ref):
                small = small + from_two(ref[:, :LANES])
            flat_out[...] = small

        head_shape = shape_of(F32, rest, inner_half)
        grad_in, grad_out, grad_query, grad_key, grad_value, flat = whole_call(
            last_final,
            (last_stay, in_stay, got_one, got_two, got_three, flat),
            (shape_of(F32, rest, hidden_half), *(head_shape,) * 4, shape_of(F32, count, LANES)),
            (),
            "last_final",
        )
    else:
        flat = flat + from_two(got_second[:, query_both:])
        grad_other = rows(grad_other, over(grad_own[early_rows:]))
        in_rest, in_stay = rest_start(add(in_stay, in_more))
        last = columns(add(heads_keep, got_first), add(kv_keep, got_second[:, :query_both]))
        last_rest, last_stay = rest_start(last)
        in_more, last_more, *flat_got = go(
            (), (far[1], in_rest), (far[0], last_rest), *((how, flat) for how in rest_hop)
        )
        last_rest, last_stay = rest_start(add(last_stay, last_more))
        last_more = far[1](last_rest)
        flat = flat + sum(flat_got)
        for send in far[:-2]:
            flat = flat + send(flat)
        grad_last = finish(last_stay.astype(F32) + last_more.astype(F32))
        grad_in = finish(in_stay.astype(F32) + in_more.astype(F32))
        back_all = finish(back_stay.astype(F32) + back_more.astype(F32))
        grad_back, grad_pool = back_all[:, :hidden_half], back_all[:, hidden_half:]
        pool_other = over(grad_pool)
        grad_pool = jnp.where(mine == 0, columns(grad_pool, pool_other), columns(pool_other, grad_pool))
        grad_out, grad_query, grad_key, grad_value = (
            grad_last[:, i * inner_half : (i + 1) * inner_half] for i in range(4)
        )
        grad_tokens = jnp.where(
            mine == 0, jnp.stack([grad_own, grad_other]), jnp.stack([grad_other, grad_own])
        )
    across = width // LANES
    zero = jnp.uint32(0)
    gains_mine = lax.dynamic_slice(flat[: 3 * across].reshape(3, width), (zero, gain_at), (3, block))
    loss = flat[3 * across, 0] / (micro_count * sent_local * size)
    table_sum = flat[table_row : table_row + table_rows].reshape(-1, bucket_count)[: 2 * heads_half]
    table_mine = lax.dynamic_slice(table_sum, (table_at, zero), (heads_half, bucket_count)).T
    return (
        loss,
        grad_tokens,
        grad_query,
        grad_key,
        grad_value,
        grad_out.T,
        grad_in,
        grad_back.T,
        gains_mine[0],
        gains_mine[1],
        gains_mine[2],
        grad_pool,
        table_mine,
    )


def solution(mesh):
    placed = (
        P(None, "dp", None),
        P(None, "dp", None),
        P(),
        P(None, "dp"),
        P("dp", "mp"),
        P("dp", "mp"),
        P("dp", "mp"),
        P("mp", "dp"),
        P("dp", "mp"),
        P("mp", "dp"),
        P("dp"),
        P("dp"),
        P("dp"),
        P("dp", None),
        P(None, "mp"),
    )
    return jax.shard_map(
        shards,
        mesh=mesh,
        in_specs=placed,
        out_specs=(
            P(),
            P(None, "dp", None),
            P("dp", "mp"),
            P("dp", "mp"),
            P("dp", "mp"),
            P("mp", "dp"),
            P("dp", "mp"),
            P("mp", "dp"),
            P("dp"),
            P("dp"),
            P("dp"),
            P("dp", None),
            P(None, "mp"),
        ),
        check_vma=False,
    )
```

```python
import functools

import jax
import jax.numpy as jnp
from jax import lax
from jax.experimental import pallas as pl
from jax.experimental.pallas import tpu as pltpu
from jax.sharding import PartitionSpec as P

NEG_FILL = -1000000000.0
SCORE_SCALE = 0.125
SOFTMAX_TEMP = 50.0
LOSS_SCALE = 64.0
EPSILON = 1e-06
REACH = 32
QB = 64
WIN = QB + 2 * REACH
LANES = 128
GELU_A = 0.7978845608028654
GELU_B = 0.044715

BF16 = jnp.bfloat16
F32 = jnp.float32
HIGHEST = lax.Precision.HIGHEST


def dot(left, right, dims=((1,), (0,)), precision=None):
    return lax.dot_general(
        left, right, (dims, ((), ())), precision=precision, preferred_element_type=F32
    )


def dot_nt(left, right):
    return dot(left, right, ((1,), (1,)))


def dot_tn(left, right):
    return dot(left, right, ((0,), (0,)))


def rms_forward(value, gain):
    inverse = lax.rsqrt(jnp.mean(value * value, axis=-1, keepdims=True) + EPSILON)
    return (value * inverse * gain, inverse)


def cost(flops, bytes_accessed):
    return pl.CostEstimate(flops=0, bytes_accessed=0, transcendentals=0)


def params(mib=16):
    return pltpu.CompilerParams(vmem_limit_bytes=mib * 2**20)


def split_dot(left, right, dims=((1,), (0,))):
    high = right.astype(BF16)
    rest = (right - high.astype(F32)).astype(BF16)
    return dot(left, high, dims) + dot(left, rest, dims)


def stream_kernel(plan, operands, outs, body, *refs):
    sources, out_refs = refs[:operands], refs[operands : operands + outs]
    more = refs[operands + outs :]
    buffers, sem = more[: sum(len(load) > 1 for load in plan)], more[-1]
    more = more[len(buffers) : -1]
    copies, places, used = [], [], 0
    for load in plan:
        if len(load) == 1:
            which, _, row, count, col, width, _ = load[0]
            places.append(sources[which].at[pl.ds(row, count), pl.ds(col, width)])
            copies.append([])
            continue
        buffer = buffers[used]
        used += 1
        group = []
        for which, at, row, count, col, width, number in load:
            copy = pltpu.make_async_copy(
                sources[which].at[pl.ds(row, count), pl.ds(col, width)],
                buffer.at[pl.ds(at, count)],
                sem.at[number],
            )
            copy.start()
            group.append(copy)
        places.append(buffer)
        copies.append(group)
    ready = set()

    def get(i):
        if i not in ready:
            ready.add(i)
            for copy in copies[i]:
                copy.wait()
        return places[i]

    body(get, *out_refs, *more)


def stream(name, loads, out_shapes, body, scratch=(), mib=16):
    arrays, spaces = [], []

    def place(array, space):
        for i, known in enumerate(arrays):
            if known is array and spaces[i] is space:
                return i
        arrays.append(array)
        spaces.append(space)
        return len(arrays) - 1

    plan, buffers, number = [], [], 0
    for load in loads:
        steps, at = [], 0
        space = pltpu.VMEM if len(load) == 1 else pltpu.HBM
        for array, row, count, col, width in load:
            steps.append((place(array, space), at, row, count, col, width, number))
            at += count
            number += 1
        plan.append(steps)
        if len(load) > 1:
            buffers.append(pltpu.VMEM((at, load[0][4]), load[0][0].dtype))
    return pl.pallas_call(
        functools.partial(stream_kernel, plan, len(arrays), len(out_shapes), body),
        out_shape=tuple(out_shapes),
        in_specs=[pl.BlockSpec(memory_space=space) for space in spaces],
        out_specs=tuple(pl.BlockSpec(memory_space=pltpu.VMEM) for _ in out_shapes),
        scratch_shapes=buffers + list(scratch) + [pltpu.SemaphoreType.DMA((number,))],
        compiler_params=params(mib),
        cost_estimate=cost(0, 0),
        name=name,
    )(*arrays)


def part(array, col=0, width=None):
    return [(array, 0, array.shape[0], col, array.shape[1] - col if width is None else width)]


def weight(pieces, col, width):
    return [(*piece, col, width) for piece in pieces]


def wide(name, x, blocks, extras=(), body=None, outs=1):
    widths = [width for *_, width in blocks]
    loads = [part(x)]
    for i, block in enumerate(blocks):
        loads.append(weight(*block))
        for extra in extras:
            loads.append(part(extra, sum(widths[:i]), widths[i]))

    def run(get, *out_refs):
        at = 0
        per = 1 + len(extras)
        for i, width in enumerate(widths):
            first = 1 + i * per
            value = dot(get(0)[...], get(first)[...])
            got = [get(first + 1 + j)[...] for j in range(len(extras))]
            values = (value,) if body is None else body(value, *got)
            for ref, result in zip(out_refs, values):
                ref[:, at : at + width] = result.astype(BF16)
            at += width

    shape = shape_of(BF16, x.shape[0], sum(widths))
    result = stream(name, loads, (shape,) * outs, run)
    return result if outs > 1 else result[0]


def gelu_both(up):
    square = up * up
    bend = jnp.tanh(GELU_A * up * (1.0 + GELU_B * square))
    half_one = 0.5 + 0.5 * bend
    inner = GELU_A + (3.0 * GELU_A * GELU_B) * square
    return up * half_one, half_one + 0.5 * up * (1.0 - bend * bend) * inner


def gelu_only(up):
    bend = jnp.tanh(GELU_A * up * (1.0 + GELU_B * (up * up)))
    return up * (0.5 + 0.5 * bend), up


def times_slope(value, slope):
    return (value * slope.astype(F32),)


def times_slope_of(value, up):
    return (value * gelu_both(up.astype(F32))[1],)


def narrow(name, work, extras, out_shapes, body, scratch=(), mib=16):
    loads = []
    for x, x_col, pieces, col, width in work:
        loads += [part(x, x_col, width), weight(pieces, col, width)]
    first = len(loads)
    loads += [extra if isinstance(extra, list) else part(extra) for extra in extras]

    def run(get, *refs):
        out_refs, more = refs[: len(out_shapes)], refs[len(out_shapes) :]
        acc = more[0]
        for j in range(len(work)):
            value = dot_nt(get(2 * j)[...], get(2 * j + 1)[...])
            acc[...] = value if j == 0 else acc[...] + value
        body(acc, *(get(first + i) for i in range(len(extras))), *out_refs, *more[1:])

    depth = sum(count for *_, count in work[0][2])
    return stream(
        name, loads, out_shapes, run, [pltpu.VMEM((work[0][0].shape[0], depth), F32), *scratch], mib
    )


def gradients(name, left, first, count, rights, out_of=None):
    loads = [part(left, first, count)] + [part(right) for right in rights]

    def run(get, *refs):
        *out_refs, turned = refs
        turned[...] = get(0)[...].T
        for i, ref in enumerate(out_refs):
            ref[...] = dot(turned[...], get(1 + i)[...]).astype(BF16)

    shapes = [shape_of(BF16, count, right.shape[1]) for right in rights]
    return stream(name, loads, shapes, run, [pltpu.VMEM((count, left.shape[0]), BF16)])


def sent_columns(name, first, pairs):
    loads = [load for left, right in pairs for load in (part(left, first, first), part(right))]

    def run(get, out_ref, turned):
        at = 0
        for i, (_, right) in enumerate(pairs):
            turned[...] = get(2 * i)[...].T
            n = right.shape[1]
            out_ref[:, at : at + n] = dot(turned[...], get(2 * i + 1)[...]).astype(BF16)
            at += n

    shape = shape_of(BF16, first, sum(right.shape[1] for _, right in pairs))
    return stream(name, loads, (shape,), run, [pltpu.VMEM((first, pairs[0][0].shape[0]), BF16)])[0]


def stack_rows(pieces, widths):
    block = pieces[0].shape[0]
    cuts = [sum(widths[:i]) for i in range(len(widths))]
    if block % 16:
        whole = jnp.concatenate(pieces, axis=0)
        return [whole[:, at : at + width] for at, width in zip(cuts, widths)]

    def run(*refs):
        for i, ref in enumerate(refs[: len(pieces)]):
            for j, out in enumerate(refs[len(pieces) :]):
                out[i * block : (i + 1) * block] = ref[:, cuts[j] : cuts[j] + widths[j]]

    shapes = [shape_of(pieces[0].dtype, block * len(pieces), width) for width in widths]
    return whole_call(run, pieces, shapes, (), "stack_rows")


def qkv_call(inputs, first, n):
    blocks = [(side, i * n, n) for i in range(3) for side in first]
    loads = [part(inputs), weight(first[0], 3 * n, LANES)] + [weight(*block) for block in blocks]

    def run(get, qkv_ref, normed_ref, inverse_ref, gains_ref):
        value = get(0)[...]
        inverse = lax.rsqrt(jnp.mean(value * value, axis=1, keepdims=True) + EPSILON)
        inverse_ref[...] = inverse
        gains = get(1)[...].astype(F32).T[:8]
        gains_ref[...] = gains
        normed_ref[...] = (value * inverse * gains[0:1]).astype(BF16)
        for i in range(len(blocks)):
            qkv_ref[:, i * n : (i + 1) * n] = dot(normed_ref[...], get(2 + i)[...]).astype(BF16)

    seq, width = inputs.shape
    shapes = (
        shape_of(BF16, seq, 6 * n),
        shape_of(BF16, seq, width),
        shape_of(F32, seq, 1),
        shape_of(F32, 8, width),
    )
    return stream("qkv", loads, shapes, run)


def norm_body(row, acc, value_ref, gains_ref, hidden_ref, inverse_ref, normed_ref=None):
    hidden = value_ref[...] + acc[...]
    inverse = lax.rsqrt(jnp.mean(hidden * hidden, axis=1, keepdims=True) + EPSILON)
    hidden_ref[...] = hidden
    inverse_ref[...] = inverse
    if normed_ref is not None:
        normed_ref[...] = (hidden * inverse * gains_ref[row : row + 1, :]).astype(BF16)


def norm_back(value, inverse, gain, grad):
    scaled = grad * gain
    inner = jnp.mean(value * scaled, axis=1, keepdims=True)
    d_value = inverse * scaled - value * (inverse * inverse * inverse) * inner
    return d_value, jnp.sum(grad * value * inverse, axis=0, keepdims=True)


def back_body(row, acc, value_ref, inverse_ref, gains_ref, grad_ref, low_ref, gain_out, hidden_ref=None):
    d_value, d_gain = norm_back(
        value_ref[...], inverse_ref[...], gains_ref[row : row + 1, :], acc[...]
    )
    total = grad_ref[...] + d_value
    low_ref[...] = total.astype(BF16)
    gain_out[...] = d_gain
    if hidden_ref is not None:
        hidden_ref[...] = total


def turn_kernel(grad_ref, order_ref, out_ref):
    out_ref[...] = dot_nt(grad_ref[...], order_ref[...]).astype(BF16)


def small_kernel(heads_half, one_ref, two_ref, three_ref, order_ref, bias_ref, onehot_ref, loss_ref, mine_ref, out_ref):
    width = one_ref.shape[1]
    gains = jnp.concatenate([one_ref[...], two_ref[...], three_ref[...], jnp.zeros((5, width), F32)], axis=0)
    high = gains.astype(BF16)
    rest = (gains - high.astype(F32)).astype(BF16)
    gains = dot_nt(high, order_ref[...]) + dot_nt(rest, order_ref[...])
    out_ref[...] = jnp.zeros_like(out_ref)
    across = width // LANES
    for i in range(3):
        for j in range(across):
            at = i * across + j
            out_ref[at : at + 1, :] = gains[i : i + 1, j * LANES : (j + 1) * LANES]
    at = 3 * across
    lane = lax.broadcasted_iota(jnp.int32, (1, LANES), 1)
    out_ref[at : at + 1, :] = jnp.where(lane == 0, loss_ref[...], 0.0)
    bias = bias_ref[...]
    heads = 2 * heads_half
    row = lax.broadcasted_iota(jnp.int32, (LANES, bias.shape[0]), 0)
    column = lax.broadcasted_iota(jnp.int32, (LANES, bias.shape[0]), 1)
    source = row + jnp.where(mine_ref[...] == 0, 0, heads_half)
    source = jnp.where(source >= heads, source - heads, source)
    pick = jnp.where((column == 8 * (source // 2) + source % 2) & (row < heads), 1.0, 0.0)
    bias = split_dot(pick.astype(BF16), bias)
    high = bias.astype(BF16)
    rest = (bias - high.astype(F32)).astype(BF16)
    table = dot_nt(high, onehot_ref[...]) + dot_nt(rest, onehot_ref[...])
    count = table.shape[1]
    a_row = LANES // count
    for head in range(heads):
        place = head % a_row * count
        line = at + 1 + head // a_row
        out_ref[line : line + 1, place : place + count] = table[head : head + 1, :]


def member_of(seg_ref, sent_count):
    ids = lax.broadcasted_iota(jnp.int32, (sent_count, seg_ref.shape[1]), 0)
    hit = jnp.where(seg_ref[...] == ids, 1.0, 0.0)
    return hit.astype(BF16), jnp.sum(hit, axis=1, keepdims=True)


def tail_body(acc, value_ref, gains_ref, seg_ref, own_ref, other_ref, hidden_ref, inverse_ref, pooled_ref, unit_ref, low_ref, scale_ref, high, rest):
    hidden = value_ref[...] + acc[...]
    inverse = lax.rsqrt(jnp.mean(hidden * hidden, axis=1, keepdims=True) + EPSILON)
    hidden_ref[...] = hidden
    inverse_ref[...] = inverse
    final = hidden_ref[...] * inverse * gains_ref[2:3, :]
    high[...] = final.astype(BF16)
    rest[...] = (final - high[...].astype(F32)).astype(BF16)
    sents, count = member_of(seg_ref, pooled_ref.shape[0])
    pooled = ((dot(sents, high[...]) + dot(sents, rest[...])) / count).astype(BF16)
    pooled_ref[...] = pooled
    half = own_ref.shape[1]
    left = dot(pooled, own_ref[...])
    right = dot(pooled, other_ref[...])
    square = jnp.sum(left * left, axis=1, keepdims=True) + jnp.sum(right * right, axis=1, keepdims=True)
    scale = lax.rsqrt(square + EPSILON)
    scale_ref[...] = scale
    for at, value in ((0, left * scale), (half, right * scale)):
        unit_ref[:, at : at + half] = value
        low_ref[:, at : at + half] = value.astype(BF16)


def head_call(quarters, unit, scale, partner, column, sentence_loads, out_shapes):
    loads = [part(q) for q in (*quarters, unit, scale, partner, column)] + sentence_loads
    quarter = quarters[0].shape[0]
    total = 4 * quarter

    def run(get, loss_ref, embed_ref, *refs):
        *back_refs, every = refs
        for i in range(4):
            every[i * quarter : (i + 1) * quarter] = get(i)[...]
        unit, scale, partner, columns_id = (get(i)[...] for i in range(4, 8))
        partner = as_columns(
            jnp.concatenate([partner, jnp.zeros((1, LANES - partner.shape[1]), jnp.int32)], axis=1)
        )[: partner.shape[1], 0:1]
        own_count = unit.shape[0]
        sims = dot_nt(every[...], every[...]) * SOFTMAX_TEMP
        row = lax.broadcasted_iota(jnp.int32, (total, total), 0)
        column = lax.broadcasted_iota(jnp.int32, (total, total), 1)
        sims = jnp.where(row == column, NEG_FILL, sims)
        top = jnp.max(sims, axis=0, keepdims=True)
        lse_row = top + jnp.log(jnp.sum(jnp.exp(sims - top), axis=0, keepdims=True))
        own = sims[:own_count]
        own_top = jnp.max(own, axis=1, keepdims=True)
        own_lse = own_top + jnp.log(jnp.sum(jnp.exp(own - own_top), axis=1, keepdims=True))
        is_target = columns_id.astype(F32) == partner
        hit = jnp.where(is_target, 1.0, 0.0)
        target = jnp.sum(jnp.where(is_target, own, 0.0), axis=1, keepdims=True)
        loss_ref[...] = jnp.sum(own_lse - target, axis=0, keepdims=True)
        d_rows = (LOSS_SCALE * (jnp.exp(own - own_lse) - hit)).astype(BF16)
        d_cols = (LOSS_SCALE * (jnp.exp(own - lse_row) - hit)).astype(BF16)
        d_unit = SOFTMAX_TEMP * (dot(d_rows, every[...]) + dot(d_cols, every[...]))
        inner = jnp.sum(d_unit * unit, axis=1, keepdims=True)
        d_embed = (scale * (d_unit - unit * inner)).astype(BF16)
        embed_ref[...] = d_embed
        sentence_back(d_embed, [get(8 + i) for i in range(len(sentence_loads))], *back_refs)

    return stream("head", loads, out_shapes, run, [pltpu.VMEM((total, unit.shape[1]), BF16)])


def sentence_call(embed, sentence_loads, out_shapes):
    def run(get, *back_refs):
        sentence_back(get(0)[...], [get(1 + i) for i in range(len(sentence_loads))], *back_refs)

    return stream("sentence", [part(embed)] + sentence_loads, out_shapes, run)


def sentence_back(d_embed, sources, hidden_ref, low_ref, gain_out):
    seg_ref, own_ref, other_ref, value_ref, inverse_ref, gains_ref = sources
    half = own_ref.shape[1]
    d_pooled = dot_nt(d_embed[:, :half], own_ref[...]) + dot_nt(d_embed[:, half:], other_ref[...])
    sents, count = member_of(seg_ref, d_embed.shape[0])
    d_final = split_dot(sents, d_pooled / count, ((0,), (0,)))
    d_value, d_gain = norm_back(value_ref[...], inverse_ref[...], gains_ref[2:3, :], d_final)
    hidden_ref[...] = d_value
    low_ref[...] = d_value.astype(BF16)
    gain_out[...] = d_gain


def whole_call(body, args, out_shapes, scratch=(), name=None):
    return pl.pallas_call(
        body,
        out_shape=tuple(out_shapes),
        in_specs=[pl.BlockSpec(memory_space=pltpu.VMEM)] * len(args),
        out_specs=tuple(pl.BlockSpec(memory_space=pltpu.VMEM) for _ in out_shapes),
        scratch_shapes=scratch,
        compiler_params=params(),
        cost_estimate=cost(0, 0),
        name=name,
    )(*args)


def shape_of(kind, *dims):
    return jax.ShapeDtypeStruct(dims, kind)


def _stack_heads(part):
    lane = lax.broadcasted_iota(jnp.int32, part.shape, 1)
    zero = jnp.zeros_like(part)
    first = lane < LANES // 2
    return jnp.concatenate(
        [jnp.where(first, part, zero), jnp.where(first, zero, part)], axis=0
    )


def _unstack_heads(both):
    half = both.shape[0] // 2
    lane = lax.broadcasted_iota(jnp.int32, (half, LANES), 1)
    return jnp.where(lane < LANES // 2, both[:half], both[half:])


def _pad_keys(pad, ref):
    seq = ref.shape[0]
    pad[0:REACH] = jnp.zeros((REACH, LANES), pad.dtype)
    pad[REACH + seq :] = jnp.zeros((REACH, LANES), pad.dtype)
    pad[REACH : REACH + seq] = ref[...]


def _query_bits(shape):
    return lax.broadcasted_iota(jnp.int32, shape, 0) & (QB - 1)


def as_columns(values):
    count, length = values.shape
    side = max(LANES, length)
    square = jnp.concatenate([values.astype(F32), jnp.zeros((side - count, length), F32)], axis=0)
    return square.T


def attend_forward_kernel(
    q_ref, k_ref, v_ref, segq_ref, segk_ref, rel_ref, ctx_ref, probs_ref, kpad, vpad, mask, scores
):
    seq = q_ref.shape[0]
    blocks = seq // QB
    _pad_keys(kpad, k_ref)
    _pad_keys(vpad, v_ref)

    @pl.when(pl.program_id(0) == 0)
    def _():
        keys = as_columns(segk_ref[...])
        for b in range(blocks):
            same = keys[:, b : b + 1] == segq_ref[b : b + 1, :].astype(F32)
            mask[b] = jnp.where(same, 0.0, NEG_FILL)

    rel = rel_ref[0]
    row = lax.broadcasted_iota(jnp.int32, (2 * QB, WIN), 0)
    bias = jnp.where(row < QB, rel[0:1, :], rel[1:2, :])
    bits = _query_bits((2 * QB, WIN))
    step = 1
    while step < QB:
        bias = jnp.where((bits & step) != 0, pltpu.roll(bias, step, 1), bias)
        step *= 2
    bias = bias.T
    for b in range(blocks):
        query = _stack_heads(q_ref[b * QB : (b + 1) * QB] * jnp.asarray(SCORE_SCALE, BF16))
        scores[b] = dot_nt(kpad[b * QB : b * QB + WIN], query)
    values = scores[...] + bias[None] + mask[...]
    top = jnp.max(values, axis=1, keepdims=True)
    shifted = jnp.exp(values - top)
    total = jnp.sum(shifted, axis=1, keepdims=True)
    probs_ref[0] = (shifted * (1.0 / total)).astype(BF16)
    for b in range(blocks):
        part = dot_tn(probs_ref[0, b], vpad[b * QB : b * QB + WIN])
        ctx_ref[b * QB : (b + 1) * QB] = _unstack_heads(part).astype(BF16)


def attend_backward_kernel(
    q_ref, k_ref, v_ref, dctx_ref, probs_ref, dqkv_ref, dbias_ref,
    kpad, vpad, dk_acc, dv_acc, d_probs, d_low,
):
    seq = q_ref.shape[0]
    pair = pl.program_id(0)
    side = pl.num_programs(0) // 2
    later = pair // side
    q_at = pl.ds(pl.multiple_of(pair * LANES, LANES), LANES)
    k_at = pl.ds(pl.multiple_of((pair + 2 * side + later * side) * LANES, LANES), LANES)
    v_at = pl.ds(pl.multiple_of((pair + 3 * side + later * side) * LANES, LANES), LANES)
    blocks = seq // QB
    _pad_keys(kpad, k_ref)
    _pad_keys(vpad, v_ref)
    dk_acc[...] = jnp.zeros_like(dk_acc)
    dv_acc[...] = jnp.zeros_like(dv_acc)
    for b in range(blocks):
        window = slice(b * QB, b * QB + WIN)
        d_ctx = _stack_heads(dctx_ref[b * QB : (b + 1) * QB])
        d_probs[b] = dot_nt(vpad[window], d_ctx)
        dv_acc[window] += dot(probs_ref[0, b], d_ctx)
    probs = probs_ref[0].astype(F32)
    product = probs * d_probs[...]
    inner = jnp.sum(product, axis=1, keepdims=True)
    d_scores = product - probs * inner
    d_low[...] = d_scores.astype(BF16)
    total = jnp.sum(d_scores, axis=0).T
    for b in range(blocks):
        here = slice(b * QB, (b + 1) * QB)
        window = slice(b * QB, b * QB + WIN)
        query = _stack_heads(q_ref[here] * jnp.asarray(SCORE_SCALE, BF16))
        dk_acc[window] += dot(d_low[b], query)
        d_query = _unstack_heads(dot_tn(d_low[b], kpad[window])) * SCORE_SCALE
        dqkv_ref[here, q_at] = d_query.astype(BF16)
    dqkv_ref[:, k_at] = dk_acc[REACH : REACH + seq].astype(BF16)
    dqkv_ref[:, v_at] = dv_acc[REACH : REACH + seq].astype(BF16)
    bits = _query_bits((2 * QB, WIN))
    step = 1
    while step < QB:
        total = jnp.where((bits & step) != 0, pltpu.roll(total, WIN - step, 1), total)
        step *= 2
    first = jnp.sum(total[:QB], axis=0, keepdims=True)
    second = jnp.sum(total[QB:], axis=0, keepdims=True)
    dbias_ref[0] = jnp.concatenate([first, second, jnp.zeros((6, WIN), F32)], axis=0)


def _qkv_specs(seq, pairs):
    def spec(kind):
        return pl.BlockSpec((seq, LANES), lambda p: (0, kind * pairs + p))

    return [spec(0), spec(1), spec(2)]


def attend_forward(qkv, twice, windows, rel_window):
    seq = qkv.shape[0]
    pairs = rel_window.shape[0]
    blocks = seq // QB
    return pl.pallas_call(
        attend_forward_kernel,
        grid=(pairs,),
        out_shape=(
            jax.ShapeDtypeStruct((seq, pairs * LANES), BF16),
            jax.ShapeDtypeStruct((pairs, blocks, WIN, 2 * QB), BF16),
        ),
        in_specs=_qkv_specs(seq, pairs)
        + [
            pl.BlockSpec((blocks, 2 * QB), lambda p: (0, 0)),
            pl.BlockSpec((blocks, WIN), lambda p: (0, 0)),
            pl.BlockSpec((1, 2, WIN), lambda p: (p, 0, 0)),
        ],
        out_specs=(
            pl.BlockSpec((seq, LANES), lambda p: (0, p)),
            pl.BlockSpec((1, blocks, WIN, 2 * QB), lambda p: (p, 0, 0, 0)),
        ),
        scratch_shapes=[pltpu.VMEM((seq + 2 * REACH, LANES), BF16)] * 2
        + [pltpu.VMEM((blocks, WIN, 2 * QB), F32)] * 2,
        compiler_params=params(),
        cost_estimate=cost(8 * seq * WIN * LANES * pairs * 4, 8 * seq * LANES * pairs),
        name="attend_forward",
    )(qkv, qkv, qkv, twice, windows, rel_window)


def attend_backward(qkv, d_context, probs):
    seq = qkv.shape[0]
    pairs = probs.shape[0]
    blocks = seq // QB
    lane_block = pl.BlockSpec((seq, LANES), lambda p: (0, p))
    return pl.pallas_call(
        attend_backward_kernel,
        grid=(pairs,),
        out_shape=(
            jax.ShapeDtypeStruct((seq, 3 * pairs * LANES), BF16),
            jax.ShapeDtypeStruct((pairs, 8, WIN), F32),
        ),
        in_specs=_qkv_specs(seq, pairs)
        + [
            lane_block,
            pl.BlockSpec((1, blocks, WIN, 2 * QB), lambda p: (p, 0, 0, 0)),
        ],
        out_specs=(
            pl.BlockSpec((seq, 3 * pairs * LANES), lambda p: (0, 0)),
            pl.BlockSpec((1, 8, WIN), lambda p: (p, 0, 0)),
        ),
        scratch_shapes=[pltpu.VMEM((seq + 2 * REACH, LANES), BF16)] * 2
        + [pltpu.VMEM((seq + 2 * REACH, LANES), F32)] * 2
        + [pltpu.VMEM((blocks, WIN, 2 * QB), F32), pltpu.VMEM((blocks, WIN, 2 * QB), BF16)],
        compiler_params=params(),
        cost_estimate=cost(16 * seq * WIN * LANES * pairs * 4, 16 * seq * LANES * pairs),
        name="attend_backward",
    )(qkv, qkv, qkv, d_context, probs)


CORE = 1
CROSS = 2


def hop(value, mask):
    size = lax.axis_size("dp")
    return lax.ppermute(value, "dp", [(i, i ^ mask) for i in range(size)])


def over(value):
    return lax.ppermute(value, "mp", [(0, 1), (1, 0)])


def cross(value):
    return hop(value, CROSS)


def core(value):
    return hop(value, CORE)


def go(waits, *sends, keep=(), join=True):
    values = [value for _, value in sends]
    held = lax.optimization_barrier((*values, *keep, *waits))
    results = [how(value) for (how, _), value in zip(sends, held)]
    if join:
        results = list(lax.optimization_barrier(tuple(results)))
    return results + list(held[len(values) : len(values) + len(keep)])


def slot_masks(size):
    rest = size // 4
    return [z * 4 + x * 2 + c for c in range(2) for x in range(2) for z in range(rest)]


def strides(size):
    found = []
    stride = 4
    while stride < size:
        found.append(stride)
        stride *= 2
    return found


def gather_near(shard, waits, widths=None):
    size = lax.axis_size("dp")
    pieces = [shard]
    stride = 4
    while stride < size:
        radix = min(4, size // stride)
        shard = jnp.concatenate(pieces, axis=0) if len(pieces) > 1 else shard
        sends = [(functools.partial(hop, mask=j * stride), shard) for j in range(1, radix)]
        pieces = [shard] + go(waits, *sends)
        stride *= radix
    return jnp.concatenate(pieces, axis=0) if widths is None else stack_rows(pieces, widths)


def rows(*pieces):
    return jnp.concatenate(pieces, axis=0)


def columns(*pieces):
    return jnp.concatenate(pieces, axis=1)


def gather_weights(start, later, n_one, n_early, n_three, early, begin, between):
    size = lax.axis_size("dp")
    steps = strides(size)
    n_two = start.shape[1] - n_one
    n_four = later.shape[1] - n_three
    if len(steps) == 2:
        got = go((), *((functools.partial(hop, mask=4 * j), start) for j in range(1, 4)))
        more = hop(later, 4)
        one, two = stack_rows([start, *got], (n_one, n_two))
        later = stack_rows([later, more], (n_early, later.shape[1] - n_early))
        wide_step = functools.partial(hop, mask=steps[1])
    else:
        one, two = gather_near(start, (), (n_one, n_two))

        later = [later[:, :n_early], later[:, n_early:]]

        def wide_step(value):
            whole = gather_near(value, ())
            return whole[value.shape[0] :]

    one_x, two_y, more = go(early, (cross, one), (over, two), (wide_step, later[0]))
    (one,) = stack_rows([one, one_x], (n_one,))
    (two,) = stack_rows([two, two_y], (n_two,))
    one_y, two_x, one_c, two_c, more_b = go(
        (), (over, one), (cross, two), (core, one), (core, two), (wide_step, later[1])
    )
    if len(steps) == 2:
        have = later[0].shape[0]

        def put(near_a, near_b, far_a, far_b, three_ref, four_ref):
            for at, left, right in ((0, near_a, near_b), (have, far_a, far_b)):
                here = slice(at, at + have)
                three_ref[here, :n_early] = left[...]
                three_ref[here, n_early:] = right[:, : n_three - n_early]
                four_ref[here] = right[:, n_three - n_early :]

        three, four = whole_call(
            put,
            (*later, more, more_b),
            (shape_of(BF16, 2 * have, n_three), shape_of(BF16, 2 * have, n_four)),
            (),
            "put_rows",
        )
    else:
        later = rows(columns(*later), columns(more, more_b))
        three, four = later[:, :n_three], later[:, n_three:]
    three_x, four_y, one_yc, two_xc = go((), (cross, three), (over, four), (core, one_y), (core, two_x))
    (three,) = stack_rows([three, three_x], (n_three,))
    (four,) = stack_rows([four, four_y], (four.shape[1],))
    three_y, four_x, three_c, four_c, one, one_c, one_y, one_yc, two, two_x, two_c, two_xc, *early = go(
        (),
        (over, three),
        (cross, four),
        (core, three),
        (core, four),
        keep=(one, one_c, one_y, one_yc, two, two_x, two_c, two_xc, *early),
        join=False,
    )
    first, second = along_x(one, one_c, one_y, one_yc), along_y(two, two_x, two_c, two_xc)
    done = between(begin(first, early), second, early)
    four_xc, three_yc, *done = go(
        (three_y, four_x, three_c, four_c), (core, four_x), (core, three_y), keep=done, join=False
    )
    third, fourth = along_x(three, three_c, three_y, three_yc), along_y(four, four_x, four_c, four_xc)
    return first, second, third, fourth, early, done


def along_x(near, near_c, other, other_c):
    count = near.shape[0]
    return ((near, 0, count), (near_c, 0, count)), ((other, 0, count), (other_c, 0, count))


def along_y(near, side, near_c, side_c):
    count = near.shape[0] // 2
    return tuple(
        tuple((array, at, count) for array in (near, side, near_c, side_c)) for at in (0, count)
    )


def pack(name, sources, mib):
    widths = [count for *_, count in sources]
    block = sources[0][0].shape[0]

    def run(*refs):
        ins, out = refs[: len(sources)], refs[len(sources)]
        buffers, sem = refs[len(sources) + 1 : -1], refs[-1]
        copies = []
        for i, (_, first, count) in enumerate(sources):
            copy = pltpu.make_async_copy(ins[i].at[:, pl.ds(first, count)], buffers[i], sem.at[i])
            copy.start()
            copies.append(copy)
        at = 0
        for copy, buffer, width in zip(copies, buffers, widths):
            copy.wait()
            out[:, at : at + width] = buffer[...]
            at += width

    return pl.pallas_call(
        run,
        out_shape=shape_of(BF16, block, sum(widths)),
        in_specs=[pl.BlockSpec(memory_space=pltpu.HBM)] * len(sources),
        out_specs=pl.BlockSpec(memory_space=pltpu.VMEM),
        scratch_shapes=[pltpu.VMEM((block, width), BF16) for width in widths]
        + [pltpu.SemaphoreType.DMA((len(sources),))],
        compiler_params=params(mib),
        cost_estimate=cost(0, 0),
        name=name,
    )(*(array for array, *_ in sources))


def gather_dp(shard):
    near = gather_near(shard, ())
    side, c_near = go((near,), (cross, near), (core, near))
    return near, side, c_near, core(side)


def low(value):
    return value.astype(BF16)


def add(left, right):
    return (left.astype(F32) + right.astype(F32)).astype(BF16)


def product(left, begin, end, right, got=None):
    value = dot_tn(left[:, begin:end], right)
    if got is not None:
        value = value + got.astype(F32)
    return low(value)


def rest_start(value):
    half = value.shape[0] // 2
    return value[half:], value[:half]


def sum_half(value, send):
    gone, stays = rest_start(value)
    return stays + send(low(gone)).astype(F32)


def rest_hops(size):
    return [functools.partial(hop, mask=stride) for stride in reversed(strides(size))]


def shards(
    tokens,
    seg_ids,
    buckets,
    labels,
    w_query,
    w_key,
    w_value,
    w_out,
    w_in,
    w_back,
    gain_attn,
    gain_ffn,
    gain_final,
    w_pool,
    rel_table,
):
    micro_count, seq, width = tokens.shape
    size = lax.axis_size("dp")
    me = lax.axis_index("dp")
    mine = lax.axis_index("mp")
    block = width // size
    inner_half = w_query.shape[1]
    hidden_half = w_in.shape[1]
    sent_local = labels.shape[1]
    bucket_count = rel_table.shape[0]
    heads_half = rel_table.shape[1]
    masks = slot_masks(size)

    x_own = lax.dynamic_index_in_dim(tokens, mine, 0, keepdims=False)
    segments = lax.dynamic_index_in_dim(seg_ids, mine, 0, keepdims=False)[0]
    partner = lax.dynamic_index_in_dim(labels, mine, 0, keepdims=False)

    slot_block = jnp.stack([jnp.bitwise_xor(me, m) for m in masks]).astype(jnp.int32)
    source = (slot_block[:, None] * block + jnp.arange(block, dtype=jnp.int32)[None, :]).reshape(-1)
    order = (jnp.arange(width, dtype=jnp.int32)[:, None] == source[None, :]).astype(BF16)
    order = lax.optimization_barrier(order)
    inputs = dot(x_own, order)


    row_f32 = shape_of(F32, seq, width)
    row_low = shape_of(BF16, seq, width)
    column_f32 = shape_of(F32, seq, 1)
    gain_f32 = shape_of(F32, 1, width)
    heads = 3 * inner_half
    piece = hidden_half // 2
    halves = [(side, i * inner_half, inner_half) for side in range(2) for i in range(2)]

    def hidden_blocks(weights, first_col=0):
        return [(weights[side], first_col + col, n) for side, col, n in halves]

    def begin(first, early):
        inputs, rel_window, twice, windows, *_ = early
        qkv, normed1_low, inverse1, gains = qkv_call(inputs, first, inner_half)
        context, probs = attend_forward(qkv, twice, windows, rel_window)
        return qkv, normed1_low, inverse1, gains, context, probs

    def between(started, second, early):
        qkv, normed1_low, inverse1, gains, context, probs = started
        inputs = early[0]
        hidden1, inverse2, normed2_low = narrow(
            "attn_out",
            [(context, i * inner_half, second[i], piece, inner_half) for i in range(2)],
            (inputs, gains),
            (row_f32, column_f32, row_low),
            functools.partial(norm_body, 1),
        )
        act0, slope0 = wide("act0", normed2_low, hidden_blocks(second), (), gelu_both, 2)
        return normed1_low, inverse1, gains, qkv, context, probs, hidden1, inverse2, normed2_low, act0, slope0

    gains_col = jnp.pad(
        jnp.stack([gain_attn, gain_ffn, gain_final], axis=1), ((0, 0), (0, LANES - 3))
    )
    pool_half = w_pool.shape[1] // 2
    pool_own = lax.dynamic_slice_in_dim(w_pool, mine * pool_half, pool_half, axis=1)
    moved = piece // 3
    back_shard = w_back.T
    if block % 16:
        start = columns(w_query, w_key, w_value, gains_col, w_in[:, :piece], w_out.T)
        later = columns(
            back_shard[:, :piece],
            back_shard[:, hidden_half - moved :],
            pool_own,
            w_in[:, piece:],
            back_shard[:, piece : hidden_half - moved],
        )
    else:
        start = pack(
            "pack_start",
            [(w, 0, inner_half) for w in (w_query, w_key, w_value)]
            + [(gains_col, 0, LANES), (w_in, 0, piece), (w_out.T, 0, inner_half)],
            60,
        )
        back_shard, w_in, _ = lax.optimization_barrier((back_shard, w_in, start))
        later = pack(
            "pack_later",
            [
                (back_shard, 0, piece),
                (back_shard, hidden_half - moved, moved),
                (pool_own, 0, pool_half),
                (w_in, piece, piece),
                (back_shard, piece, piece - moved),
            ],
            16,
        )
    rel_other = over(lax.optimization_barrier((rel_table, start))[0])
    rel_all = jnp.concatenate([rel_table, rel_other], axis=1).astype(F32)
    near_buckets = lax.slice_in_dim(buckets, seq - 1 - REACH, seq - 1 - REACH + WIN)
    onehot = (near_buckets[None, :] == jnp.arange(bucket_count, dtype=jnp.int32)[:, None]).astype(F32)
    onehot = lax.optimization_barrier(low(onehot))
    rel_window = dot(rel_all, onehot.astype(F32), ((0,), (0,)), HIGHEST).reshape(heads_half, 2, WIN)
    padded = jnp.pad(segments, (REACH, REACH), constant_values=-1)
    windows = jnp.stack([padded[at : at + WIN] for at in range(0, seq, QB)])
    twice = jnp.tile(segments.reshape(seq // QB, QB), (1, 2))
    local_ids = jnp.arange(sent_local, dtype=jnp.int32)
    column_id = (slot_block[:, None] * sent_local + local_ids[None, :]).reshape(1, -1)
    early = (
        inputs, rel_window, twice, windows, order, onehot, column_id, partner[None, :], segments[None, :], mine.reshape(1, 1),
        (me * block).astype(jnp.uint32), (mine * heads_half).astype(jnp.uint32)
    )
    first, second, third, fourth, early, done = gather_weights(
        start,
        later,
        heads + LANES,
        piece,
        piece + moved + pool_half,
        early,
        begin,
        between,
    )
    inputs, rel_window, twice, windows, order, onehot, column_id, partner, seg_lane, mine_array, gain_at, table_at = early
    normed1_low, inverse1, gains, qkv, context, probs, hidden1, inverse2, normed2_low, act0, slope0 = done

    act1, up_kept = wide("act1", normed2_low, hidden_blocks(fourth), (), gelu_only, 2)
    pool_loads = [weight(side, piece + moved, pool_half) for side in third]
    hidden2, inverse3, pooled_low, unit, unit_low, scale = narrow(
        "ffn_out",
        [(act0, i * piece, third[i], 0, piece) for i in range(2)]
        + [(act1, i * piece, fourth[i], piece, piece - moved) for i in range(2)]
        + [(act1, (i + 1) * piece - moved, third[i], piece, moved) for i in range(2)],
        (hidden1, gains, seg_lane, *pool_loads),
        (
            row_f32,
            column_f32,
            shape_of(BF16, sent_local, width),
            shape_of(F32, sent_local, width),
            shape_of(BF16, sent_local, width),
            shape_of(F32, sent_local, 1),
        ),
        tail_body,
        [pltpu.VMEM((seq, width), BF16)] * 2,
    )
    quarters = gather_dp(unit_low)

    total_sent = column_id.shape[1]
    sentence_loads = [part(seg_lane), *pool_loads, part(hidden2), part(inverse3), part(gains)]
    back_shapes = (row_f32, row_low, gain_f32)
    if total_sent <= 1024:
        loss_local, embed_low, d_hidden2, ffn_low, d_gain3 = head_call(
            quarters,
            unit,
            scale,
            partner,
            column_id,
            sentence_loads,
            (shape_of(F32, 1, 1), shape_of(BF16, sent_local, width), *back_shapes),
        )
    else:
        every = rows(*quarters)
        position = jnp.arange(total_sent, dtype=jnp.int32)
        sims = dot_nt(every, every) * SOFTMAX_TEMP
        sims = jnp.where(position[:, None] == position[None, :], NEG_FILL, sims)
        lse_row = jax.nn.logsumexp(sims, axis=0, keepdims=True)
        own_sims = sims[:sent_local]
        own_lse = jax.nn.logsumexp(own_sims, axis=1, keepdims=True)
        is_target = column_id == partner.reshape(-1, 1)
        target = jnp.sum(jnp.where(is_target, own_sims, 0.0), axis=-1, keepdims=True)
        loss_local = jnp.sum(own_lse - target)
        hit = is_target.astype(F32)
        d_rows = low(LOSS_SCALE * (jnp.exp(own_sims - own_lse) - hit))
        d_cols = low(LOSS_SCALE * (jnp.exp(own_sims - lse_row) - hit))
        d_unit = SOFTMAX_TEMP * (dot(d_rows, every) + dot(d_cols, every))
        embed_low = low(scale * (d_unit - unit * jnp.sum(d_unit * unit, axis=-1, keepdims=True)))
        d_hidden2, ffn_low, d_gain3 = sentence_call(embed_low, sentence_loads, back_shapes)

    half = width // 2
    quarter = width // 4

    back0_sent, back1_sent = gradients("back_sent", ffn_low, half, half, (act0, act1))
    (pool_sent,) = gradients("pool_sent", pooled_low, half, half, (embed_low,))
    back0_got, back1_got, pool_got, ffn_later = go(
        (), (core, back0_sent), (core, back1_sent), (core, pool_sent), keep=(ffn_low,), join=False
    )
    pool_hi = product(pooled_low, quarter, half, embed_low, pool_got[quarter:])
    pool_lo = product(pooled_low, 0, quarter, embed_low, pool_got[:quarter])
    up0 = wide("up0", ffn_later, hidden_blocks(third), (slope0,), times_slope)

    back_hi = product(ffn_low, quarter, half, act0, back0_got[quarter:])
    back_lo = product(ffn_low, 0, quarter, act0, back0_got[:quarter])
    back_own = product(ffn_low, 0, half, act1[:, :piece], back1_got[:, :piece])
    back_oth = product(ffn_low, 0, half, act1[:, piece:], back1_got[:, piece:])
    got_lo, got_own, got_pool, ffn_later, up0, back_lo, back_own, pool_lo = go(
        (),
        (cross, back_hi),
        (over, back_oth),
        (cross, pool_hi),
        keep=(ffn_later, up0, back_lo, back_own, pool_lo),
    )
    back_blocks = [
        block
        for side in range(2)
        for block in (
            (fourth[side], piece, inner_half),
            (fourth[side], piece + inner_half, piece - moved - inner_half),
            (third[side], piece, moved),
        )
    ]
    up1 = wide("up1", ffn_later, back_blocks, (up_kept,), times_slope_of)
    in0_sent, in1_sent = gradients("in_sent", normed2_low, half, half, (up0, up1))
    in0_got, in1_got, up0, up1 = go((), (core, in0_sent), (core, in1_sent), keep=(up0, up1))
    attn_low, d_gain2, d_hidden1 = narrow(
        "ffn_in_back",
        [(up0, i * piece, second[i], 0, piece) for i in range(2)]
        + [(up1, i * piece, fourth[i], 0, piece) for i in range(2)],
        (hidden1, inverse2, gains, d_hidden2),
        (row_low, gain_f32, row_f32),
        functools.partial(back_body, 1),
    )
    d_context = wide("d_context", attn_low, [(second[side], piece, inner_half) for side in range(2)])

    pool_lo = add(pool_lo, got_pool)
    back_lo = add(back_lo, got_lo)
    back_own = add(back_own, got_own)
    in_hi = product(normed2_low, quarter, half, up0, in0_got[quarter:])
    in_lo = product(normed2_low, 0, quarter, up0, in0_got[:quarter])
    in_own = product(normed2_low, 0, half, up1[:, :piece], in1_got[:, :piece])
    in_oth = product(normed2_low, 0, half, up1[:, piece:], in1_got[:, piece:])
    got_first, got_x, got_in_own, d_context, pool_lo, back_lo, back_own, in_lo, in_own = go(
        (got_lo, got_own),
        (over, columns(back_lo[:, piece:], pool_lo[:, pool_half:])),
        (cross, columns(back_own[quarter:], in_hi)),
        (over, in_oth),
        keep=(d_context, pool_lo, back_lo, back_own, in_lo, in_own),
        join=False,
    )
    d_qkv, d_bias = attend_backward(qkv, d_context, probs)
    query_both = 2 * inner_half
    late_sent = sent_columns("late_sent", half, ((attn_low, context), (normed1_low, d_qkv)))
    late_got, d_qkv_later = go((), (core, late_sent), keep=(d_qkv,), join=False)
    grad_slots, d_gain1 = narrow(
        "qkv_back",
        [(d_qkv_later, i * inner_half, first[i], 0, inner_half) for i in range(2)]
        + [(d_qkv_later, (1 + i) * query_both, first[i], inner_half, query_both) for i in range(2)],
        (inputs, inverse1, gains, d_hidden1),
        (row_low, gain_f32),
        functools.partial(back_body, 0),
    )

    table_row = 3 * (width // LANES) + 1
    table_rows = -(-2 * heads_half * bucket_count // LANES)
    small_rows = -(-(table_row + table_rows) // 8) * 8
    (flat,) = whole_call(
        functools.partial(small_kernel, heads_half),
        (d_gain1, d_gain2, d_gain3, order, d_bias.reshape(-1, WIN), onehot, loss_local.reshape(1, 1), mine_array),
        (shape_of(F32, small_rows, LANES),),
        (),
        "small",
    )
    (grad_own,) = whole_call(turn_kernel, (grad_slots, order), (row_low,), (), "turn")
    flat_got, flat = go((), (over, flat), keep=(flat,), join=False)
    got_first, got_x, got_in_own = lax.optimization_barrier((got_first, got_x, got_in_own))
    flat = flat + flat_got
    got_second, got_in_lo = got_x[:, :piece], got_x[:, piece:]

    far = rest_hops(size)
    back_all = columns(
        add(back_lo[:, :piece], got_first[:, :piece]),
        add(back_own[:quarter], got_second),
        add(pool_lo[:, :pool_half], got_first[:, piece:]),
    )
    back_rest, back_stay = rest_start(back_all)
    in_lo = add(in_lo, got_in_lo)
    in_own = add(in_own, got_in_own)
    out_got, qkv_got = late_got[:, :query_both], late_got[:, query_both:]
    out_hi = product(attn_low, quarter, half, context, out_got[quarter:])
    out_lo = product(attn_low, 0, quarter, context, out_got[:quarter])
    query_hi = product(normed1_low, quarter, half, d_qkv[:, :query_both], qkv_got[quarter:, :query_both])
    query_lo = product(normed1_low, 0, quarter, d_qkv[:, :query_both], qkv_got[:quarter, :query_both])
    kv_own = product(
        normed1_low, 0, half, d_qkv[:, query_both : 2 * query_both], qkv_got[:, query_both : 2 * query_both]
    )
    kv_oth = product(normed1_low, 0, half, d_qkv[:, 2 * query_both :], qkv_got[:, 2 * query_both :])
    rest_hop = [functools.partial(hop, mask=j * 4) for j in range(1, min(4, size // 4))]
    back_more, got_first, got_x, got_kv, flat_got, back_stay, in_lo, in_own, out_lo, query_lo, kv_own, flat = go(
        (grad_own,),
        (far[0], back_rest),
        (over, in_lo[:, piece:]),
        (cross, columns(in_own[quarter:], out_hi, query_hi)),
        (over, kv_oth),
        (core, flat),
        keep=(back_stay, in_lo, in_own, out_lo, query_lo, kv_own, flat),
    )

    count = flat.shape[0]

    def in_two(value):
        high = value.astype(BF16).astype(F32)
        return jnp.concatenate([high, value - high], axis=0).astype(BF16)

    def from_two(pair):
        return pair[:count].astype(F32) + pair[count : 2 * count].astype(F32)

    def late_adds(
        stay, more, in_lo, got_first, in_own, got_x, out_lo, query_lo, kv_own, got_kv, flat, got_flat, *outs
    ):
        back_gone, back_keep, in_gone, in_keep, heads_gone, heads_keep, kv_gone, kv_keep, small = outs
        rows_z = stay.shape[0] // 2
        total = add(stay[...], more[...])
        back_keep[...] = total[:rows_z]
        back_gone[...] = total[rows_z:]
        rows_z = in_lo.shape[0] // 2
        for at, total in (
            (0, add(in_lo[:, :piece], got_first[...])),
            (piece, add(in_own[:quarter], got_x[:, :piece])),
        ):
            in_keep[:, at : at + piece] = total[:rows_z]
            in_gone[:, at : at + piece] = total[rows_z:]
        for i, ref in enumerate((out_lo, query_lo)):
            first_col = piece + i * query_both
            total = add(ref[...], got_x[:, first_col : first_col + query_both])
            heads_keep[:, i * inner_half : (i + 1) * inner_half] = total[:, :inner_half]
            heads_gone[:, i * inner_half : (i + 1) * inner_half] = total[:, inner_half:]
        kv_keep[...] = add(kv_own[:quarter], got_kv[:quarter])
        kv_gone[:, :query_both] = add(kv_own[quarter:], got_kv[quarter:])
        small[...] = flat[...] + got_flat[...]
        kv_gone[:, query_both:] = jnp.zeros((quarter, LANES), BF16)
        pair = in_two(small[...])
        kv_gone[: 2 * count, query_both:] = pair
        small[...] = from_two(pair)

    cut = [shape_of(BF16, back_stay.shape[0] // 2, back_stay.shape[1])] * 2
    cut += [shape_of(BF16, quarter // 2, hidden_half)] * 2 + [shape_of(BF16, quarter, query_both)] * 2
    cut += [
        shape_of(BF16, quarter, query_both + LANES),
        shape_of(BF16, quarter, query_both),
        shape_of(F32, count, LANES),
    ]
    back_rest, back_stay, in_rest, in_stay, heads_gone, heads_keep, kv_gone, kv_keep, flat = whole_call(
        late_adds,
        (back_stay, back_more, in_lo, got_first, in_own, got_x, out_lo, query_lo, kv_own, got_kv, flat, flat_got),
        cut,
        (),
        "late_adds",
    )
    early_rows = seq * 11 // 32
    back_more, in_more, got_first, got_second, grad_other, back_stay, in_stay, heads_keep, kv_keep, flat = go(
        (),
        (far[1], back_rest),
        (far[0], in_rest),
        (over, heads_gone),
        (cross, kv_gone),
        (over, grad_own[:early_rows]),
        keep=(back_stay, in_stay, heads_keep, kv_keep, flat),
    )

    def finish(value):
        value = value.astype(F32)
        for send in far[2:]:
            value = sum_half(value, send)
        return value

    n_last = query_both + query_both
    if len(far) == 2:
        rest = block
        late_rows = seq - early_rows

        def last_adds(stay, more, heads_ref, got_heads, kv_ref, got_kv, flat_ref, back_ref, back_got, own_ref, *outs):
            one, two, three, in_keep, keep, flat_out, tail, pool_ref = outs
            pool = add(back_ref[:, hidden_half:], back_got[:, hidden_half:])
            pool_ref[...] = pool
            tail[:late_rows] = own_ref[early_rows:]
            tail[late_rows:, :pool_half] = pool
            tail[late_rows:, pool_half:] = jnp.zeros((rest, width - pool_half), BF16)
            total = add(stay[...], more[...])
            in_keep[...] = total[:rest]
            one[:, LANES : LANES + hidden_half] = total[rest:]
            pair = in_two(flat_ref[...] + from_two(got_kv[:, query_both:]))
            flat_out[...] = from_two(pair)
            for i, (ref, at) in enumerate(((keep, 0), (one, LANES + hidden_half), (two, LANES), (three, LANES))):
                here = slice(i * rest, (i + 1) * rest)
                if i:
                    ref[:, :LANES] = pair
                ref[:, at : at + query_both] = add(heads_ref[here], got_heads[here])
                ref[:, at + query_both : at + n_last] = add(kv_ref[here], got_kv[here, :query_both])

        one, two, three, in_stay, last_stay, flat, tail, grad_pool = whole_call(
            last_adds,
            (in_stay, in_more, heads_keep, got_first, kv_keep, got_second, flat, back_stay, back_more, grad_own),
            (
                shape_of(BF16, rest, LANES + hidden_half + n_last),
                shape_of(BF16, rest, LANES + n_last),
                shape_of(BF16, rest, LANES + n_last),
                shape_of(BF16, rest, hidden_half),
                shape_of(BF16, rest, n_last),
                shape_of(F32, count, LANES),
                shape_of(BF16, late_rows + rest, width),
                shape_of(BF16, rest, pool_half),
            ),
            (),
            "last_adds",
        )
        got_one, got_two, got_three, got_tail, back_stay, back_more = go(
            (),
            (rest_hop[0], one),
            (rest_hop[1], two),
            (rest_hop[2], three),
            (over, tail),
            keep=(back_stay, back_more),
            join=False,
        )

        def back_final(stay, more, back_ref):
            back_ref[...] = stay[:, :hidden_half].astype(F32) + more[:, :hidden_half].astype(F32)

        (grad_back,) = whole_call(
            back_final, (back_stay, back_more), (shape_of(F32, rest, hidden_half),), (), "back_final"
        )

        def tokens_final(mine_ref, own_ref, first_ref, tail_ref, pool_own, out_ref, pool_ref):
            first = mine_ref[...] == 0
            own, other = pool_own[...].astype(F32), tail_ref[late_rows:, :pool_half].astype(F32)
            pool_ref[:, :pool_half] = jnp.where(first, own, other)
            pool_ref[:, pool_half:] = jnp.where(first, other, own)
            for at, count, ref in ((0, early_rows, first_ref), (early_rows, late_rows, tail_ref)):
                here = slice(at, at + count)
                own, other = own_ref[here].astype(F32), ref[:count].astype(F32)
                out_ref[0, here] = jnp.where(first, own, other).astype(BF16)
                out_ref[1, here] = jnp.where(first, other, own).astype(BF16)

        grad_tokens, grad_pool = whole_call(
            tokens_final,
            (mine_array, grad_own, grad_other, got_tail, grad_pool),
            (shape_of(BF16, 2, seq, width), shape_of(F32, rest, 2 * pool_half)),
            (),
            "tokens_final",
        )
        got_one, got_two, got_three, grad_tokens = lax.optimization_barrier(
            (got_one, got_two, got_three, grad_tokens)
        )

        def last_final(
            stay, in_keep, one_ref, two_ref, three_ref, flat_ref, order_ref, mine_ref, *outs
        ):
            in_ref, out_ref, q_ref, k_ref, v_ref, loss_ref, gains_ref, table_ref, wide_ref = outs
            in_ref[...] = in_keep[...].astype(F32) + one_ref[:, LANES : LANES + hidden_half].astype(F32)
            total = stay[...].astype(F32) + one_ref[:, LANES + hidden_half :].astype(F32)
            total = total + two_ref[:, LANES:].astype(F32) + three_ref[:, LANES:].astype(F32)
            for i, ref in enumerate((out_ref, q_ref, k_ref, v_ref)):
                ref[...] = total[:, i * inner_half : (i + 1) * inner_half]
            small = flat_ref[...]
            for ref in (one_ref, two_ref, three_ref):
                small = small + from_two(ref[:, :LANES])
            across = width // LANES
            loss_ref[...] = small[3 * across : 3 * across + 1, :1] / (micro_count * sent_local * size)
            wide_ref[...] = jnp.zeros_like(wide_ref)
            for i in range(3):
                for j in range(across):
                    wide_ref[i : i + 1, j * LANES : (j + 1) * LANES] = small[i * across + j : i * across + j + 1]
            high = wide_ref[...].astype(BF16)
            low_part = (wide_ref[...] - high.astype(F32)).astype(BF16)
            pick = order_ref[:, :LANES]
            gains_ref[...] = dot(high, pick) + dot(low_part, pick)
            a_row = LANES // bucket_count
            heads_list = []
            for head in range(2 * heads_half):
                line = table_row + head // a_row
                place = head % a_row * bucket_count
                heads_list.append(small[line : line + 1, place : place + bucket_count])
            first = jnp.concatenate(heads_list[:heads_half], axis=0)
            second = jnp.concatenate(heads_list[heads_half:], axis=0)
            table_ref[...] = jnp.where(mine_ref[...] == 0, first, second)

        head_shape = shape_of(F32, rest, inner_half)
        grad_in, grad_out, grad_query, grad_key, grad_value, loss, gains_mine, table_mine = whole_call(
            last_final,
            (last_stay, in_stay, got_one, got_two, got_three, flat, order, mine_array),
            (
                shape_of(F32, rest, hidden_half),
                *(head_shape,) * 4,
                shape_of(F32, 1, 1),
                shape_of(F32, 8, LANES),
                shape_of(F32, heads_half, bucket_count),
            ),
            [pltpu.VMEM((8, width), F32)],
            "last_final",
        )
        loss = loss.reshape(())
        gains_mine = gains_mine[:3, :block]
        table_mine = table_mine.T
    else:
        flat = flat + from_two(got_second[:, query_both:])
        grad_other = rows(grad_other, over(grad_own[early_rows:]))
        in_rest, in_stay = rest_start(add(in_stay, in_more))
        last = columns(add(heads_keep, got_first), add(kv_keep, got_second[:, :query_both]))
        last_rest, last_stay = rest_start(last)
        in_more, last_more, *flat_got = go(
            (), (far[1], in_rest), (far[0], last_rest), *((how, flat) for how in rest_hop)
        )
        last_rest, last_stay = rest_start(add(last_stay, last_more))
        last_more = far[1](last_rest)
        flat = flat + sum(flat_got)
        for send in far[:-2]:
            flat = flat + send(flat)
        grad_last = finish(last_stay.astype(F32) + last_more.astype(F32))
        grad_in = finish(in_stay.astype(F32) + in_more.astype(F32))
        back_all = finish(back_stay.astype(F32) + back_more.astype(F32))
        grad_back, grad_pool = back_all[:, :hidden_half], back_all[:, hidden_half:]
        pool_other = over(grad_pool)
        grad_pool = jnp.where(mine == 0, columns(grad_pool, pool_other), columns(pool_other, grad_pool))
        grad_out, grad_query, grad_key, grad_value = (
            grad_last[:, i * inner_half : (i + 1) * inner_half] for i in range(4)
        )
        grad_tokens = jnp.where(
            mine == 0, jnp.stack([grad_own, grad_other]), jnp.stack([grad_other, grad_own])
        )
        across = width // LANES
        zero = jnp.uint32(0)
        gains_mine = lax.dynamic_slice(flat[: 3 * across].reshape(3, width), (zero, gain_at), (3, block))
        loss = flat[3 * across, 0] / (micro_count * sent_local * size)
        table_sum = flat[table_row : table_row + table_rows].reshape(-1, bucket_count)[: 2 * heads_half]
        table_mine = lax.dynamic_slice(table_sum, (table_at, zero), (heads_half, bucket_count)).T
    return (
        loss,
        grad_tokens,
        grad_query,
        grad_key,
        grad_value,
        grad_out.T,
        grad_in,
        grad_back.T,
        gains_mine[0],
        gains_mine[1],
        gains_mine[2],
        grad_pool,
        table_mine,
    )


def solution(mesh):
    placed = (
        P(None, "dp", None),
        P(None, "dp", None),
        P(),
        P(None, "dp"),
        P("dp", "mp"),
        P("dp", "mp"),
        P("dp", "mp"),
        P("mp", "dp"),
        P("dp", "mp"),
        P("mp", "dp"),
        P("dp"),
        P("dp"),
        P("dp"),
        P("dp", None),
        P(None, "mp"),
    )
    return jax.shard_map(
        shards,
        mesh=mesh,
        in_specs=placed,
        out_specs=(
            P(),
            P(None, "dp", None),
            P("dp", "mp"),
            P("dp", "mp"),
            P("dp", "mp"),
            P("mp", "dp"),
            P("dp", "mp"),
            P("mp", "dp"),
            P("dp"),
            P("dp"),
            P("dp"),
            P("dp", None),
            P(None, "mp"),
        ),
        check_vma=False,
    )
```

```python
import functools

import jax
import jax.numpy as jnp
from jax import lax
from jax.experimental import pallas as pl
from jax.experimental.pallas import tpu as pltpu
from jax.sharding import PartitionSpec as P

NEG_FILL = -1000000000.0
SCORE_SCALE = 0.125
SOFTMAX_TEMP = 50.0
LOSS_SCALE = 64.0
EPSILON = 1e-06
REACH = 32
QB = 64
WIN = QB + 2 * REACH
LANES = 128
GELU_A = 0.7978845608028654
GELU_B = 0.044715

BF16 = jnp.bfloat16
F32 = jnp.float32
HIGHEST = lax.Precision.HIGHEST


def dot(left, right, dims=((1,), (0,)), precision=None):
    return lax.dot_general(
        left, right, (dims, ((), ())), precision=precision, preferred_element_type=F32
    )


def dot_nt(left, right):
    return dot(left, right, ((1,), (1,)))


def dot_tn(left, right):
    return dot(left, right, ((0,), (0,)))


def rms_forward(value, gain):
    inverse = lax.rsqrt(jnp.mean(value * value, axis=-1, keepdims=True) + EPSILON)
    return (value * inverse * gain, inverse)


def cost(flops, bytes_accessed):
    return pl.CostEstimate(flops=0, bytes_accessed=0, transcendentals=0)


def params(mib=16):
    return pltpu.CompilerParams(vmem_limit_bytes=mib * 2**20)


def split_dot(left, right, dims=((1,), (0,))):
    high = right.astype(BF16)
    rest = (right - high.astype(F32)).astype(BF16)
    return dot(left, high, dims) + dot(left, rest, dims)


def stream_kernel(plan, operands, outs, body, *refs):
    sources, out_refs = refs[:operands], refs[operands : operands + outs]
    more = refs[operands + outs :]
    buffers, sem = more[: sum(len(load) > 1 for load in plan)], more[-1]
    more = more[len(buffers) : -1]
    copies, places, used = [], [], 0
    for load in plan:
        if len(load) == 1:
            which, _, row, count, col, width, _ = load[0]
            places.append(sources[which].at[pl.ds(row, count), pl.ds(col, width)])
            copies.append([])
            continue
        buffer = buffers[used]
        used += 1
        group = []
        for which, at, row, count, col, width, number in load:
            copy = pltpu.make_async_copy(
                sources[which].at[pl.ds(row, count), pl.ds(col, width)],
                buffer.at[pl.ds(at, count)],
                sem.at[number],
            )
            copy.start()
            group.append(copy)
        places.append(buffer)
        copies.append(group)
    ready = set()

    def get(i):
        if i not in ready:
            ready.add(i)
            for copy in copies[i]:
                copy.wait()
        return places[i]

    body(get, *out_refs, *more)


def stream(name, loads, out_shapes, body, scratch=(), mib=16):
    arrays, spaces = [], []

    def place(array, space):
        for i, known in enumerate(arrays):
            if known is array and spaces[i] is space:
                return i
        arrays.append(array)
        spaces.append(space)
        return len(arrays) - 1

    plan, buffers, number = [], [], 0
    for load in loads:
        steps, at = [], 0
        space = pltpu.VMEM if len(load) == 1 else pltpu.HBM
        for array, row, count, col, width in load:
            steps.append((place(array, space), at, row, count, col, width, number))
            at += count
            number += 1
        plan.append(steps)
        if len(load) > 1:
            buffers.append(pltpu.VMEM((at, load[0][4]), load[0][0].dtype))
    return pl.pallas_call(
        functools.partial(stream_kernel, plan, len(arrays), len(out_shapes), body),
        out_shape=tuple(out_shapes),
        in_specs=[pl.BlockSpec(memory_space=space) for space in spaces],
        out_specs=tuple(pl.BlockSpec(memory_space=pltpu.VMEM) for _ in out_shapes),
        scratch_shapes=buffers + list(scratch) + [pltpu.SemaphoreType.DMA((number,))],
        compiler_params=params(mib),
        cost_estimate=cost(0, 0),
        name=name,
    )(*arrays)


def part(array, col=0, width=None):
    return [(array, 0, array.shape[0], col, array.shape[1] - col if width is None else width)]


def weight(pieces, col, width):
    return [(*piece, col, width) for piece in pieces]


def wide(name, x, blocks, extras=(), body=None, outs=1):
    widths = [width for *_, width in blocks]
    loads = [part(x)]
    for i, block in enumerate(blocks):
        loads.append(weight(*block))
        for extra in extras:
            loads.append(part(extra, sum(widths[:i]), widths[i]))

    def run(get, *out_refs):
        at = 0
        per = 1 + len(extras)
        for i, width in enumerate(widths):
            first = 1 + i * per
            value = dot(get(0)[...], get(first)[...])
            got = [get(first + 1 + j)[...] for j in range(len(extras))]
            values = (value,) if body is None else body(value, *got)
            for ref, result in zip(out_refs, values):
                ref[:, at : at + width] = result.astype(BF16)
            at += width

    shape = shape_of(BF16, x.shape[0], sum(widths))
    result = stream(name, loads, (shape,) * outs, run)
    return result if outs > 1 else result[0]


def gelu_both(up):
    square = up * up
    bend = jnp.tanh(GELU_A * up * (1.0 + GELU_B * square))
    half_one = 0.5 + 0.5 * bend
    inner = GELU_A + (3.0 * GELU_A * GELU_B) * square
    return up * half_one, half_one + 0.5 * up * (1.0 - bend * bend) * inner


def gelu_only(up):
    bend = jnp.tanh(GELU_A * up * (1.0 + GELU_B * (up * up)))
    return up * (0.5 + 0.5 * bend), up


def times_slope(value, slope):
    return (value * slope.astype(F32),)


def times_slope_of(value, up):
    return (value * gelu_both(up.astype(F32))[1],)


def narrow(name, work, extras, out_shapes, body, scratch=(), mib=16):
    loads = []
    for x, x_col, pieces, col, width in work:
        loads += [part(x, x_col, width), weight(pieces, col, width)]
    first = len(loads)
    loads += [extra if isinstance(extra, list) else part(extra) for extra in extras]

    def run(get, *refs):
        out_refs, more = refs[: len(out_shapes)], refs[len(out_shapes) :]
        acc = more[0]
        for j in range(len(work)):
            value = dot_nt(get(2 * j)[...], get(2 * j + 1)[...])
            acc[...] = value if j == 0 else acc[...] + value
        body(acc, *(get(first + i) for i in range(len(extras))), *out_refs, *more[1:])

    depth = sum(count for *_, count in work[0][2])
    return stream(
        name, loads, out_shapes, run, [pltpu.VMEM((work[0][0].shape[0], depth), F32), *scratch], mib
    )


def gradients(name, left, first, count, rights, out_of=None):
    loads = [part(left, first, count)] + [part(right) for right in rights]

    def run(get, *refs):
        *out_refs, turned = refs
        turned[...] = get(0)[...].T
        for i, ref in enumerate(out_refs):
            ref[...] = dot(turned[...], get(1 + i)[...]).astype(BF16)

    shapes = [shape_of(BF16, count, right.shape[1]) for right in rights]
    return stream(name, loads, shapes, run, [pltpu.VMEM((count, left.shape[0]), BF16)])


def sent_columns(name, first, pairs):
    loads = [load for left, right in pairs for load in (part(left, first, first), part(right))]

    def run(get, out_ref, turned):
        at = 0
        for i, (_, right) in enumerate(pairs):
            turned[...] = get(2 * i)[...].T
            n = right.shape[1]
            out_ref[:, at : at + n] = dot(turned[...], get(2 * i + 1)[...]).astype(BF16)
            at += n

    shape = shape_of(BF16, first, sum(right.shape[1] for _, right in pairs))
    return stream(name, loads, (shape,), run, [pltpu.VMEM((first, pairs[0][0].shape[0]), BF16)])[0]


def stack_rows(pieces, widths):
    block = pieces[0].shape[0]
    cuts = [sum(widths[:i]) for i in range(len(widths))]
    if block % 16:
        whole = jnp.concatenate(pieces, axis=0)
        return [whole[:, at : at + width] for at, width in zip(cuts, widths)]

    def run(*refs):
        for i, ref in enumerate(refs[: len(pieces)]):
            for j, out in enumerate(refs[len(pieces) :]):
                out[i * block : (i + 1) * block] = ref[:, cuts[j] : cuts[j] + widths[j]]

    shapes = [shape_of(pieces[0].dtype, block * len(pieces), width) for width in widths]
    return whole_call(run, pieces, shapes, (), "stack_rows")


def qkv_call(inputs, first, n):
    blocks = [(side, i * n, n) for i in range(3) for side in first]
    loads = [part(inputs), weight(first[0], 3 * n, LANES)] + [weight(*block) for block in blocks]

    def run(get, qkv_ref, normed_ref, inverse_ref, gains_ref):
        value = get(0)[...]
        inverse = lax.rsqrt(jnp.mean(value * value, axis=1, keepdims=True) + EPSILON)
        inverse_ref[...] = inverse
        gains = get(1)[...].astype(F32).T[:8]
        gains_ref[...] = gains
        normed_ref[...] = (value * inverse * gains[0:1]).astype(BF16)
        for i in range(len(blocks)):
            qkv_ref[:, i * n : (i + 1) * n] = dot(normed_ref[...], get(2 + i)[...]).astype(BF16)

    seq, width = inputs.shape
    shapes = (
        shape_of(BF16, seq, 6 * n),
        shape_of(BF16, seq, width),
        shape_of(F32, seq, 1),
        shape_of(F32, 8, width),
    )
    return stream("qkv", loads, shapes, run)


def norm_body(row, acc, value_ref, gains_ref, hidden_ref, inverse_ref, normed_ref=None):
    hidden = value_ref[...] + acc[...]
    inverse = lax.rsqrt(jnp.mean(hidden * hidden, axis=1, keepdims=True) + EPSILON)
    hidden_ref[...] = hidden
    inverse_ref[...] = inverse
    if normed_ref is not None:
        normed_ref[...] = (hidden * inverse * gains_ref[row : row + 1, :]).astype(BF16)


def norm_back(value, inverse, gain, grad):
    scaled = grad * gain
    inner = jnp.mean(value * scaled, axis=1, keepdims=True)
    d_value = inverse * scaled - value * (inverse * inverse * inverse) * inner
    return d_value, jnp.sum(grad * value * inverse, axis=0, keepdims=True)


def back_body(row, acc, value_ref, inverse_ref, gains_ref, grad_ref, low_ref, gain_out, hidden_ref=None):
    d_value, d_gain = norm_back(
        value_ref[...], inverse_ref[...], gains_ref[row : row + 1, :], acc[...]
    )
    total = grad_ref[...] + d_value
    low_ref[...] = total.astype(BF16)
    gain_out[...] = d_gain
    if hidden_ref is not None:
        hidden_ref[...] = total


def turn_kernel(grad_ref, order_ref, out_ref):
    out_ref[...] = dot_nt(grad_ref[...], order_ref[...]).astype(BF16)


def small_kernel(heads_half, one_ref, two_ref, three_ref, order_ref, bias_ref, onehot_ref, loss_ref, mine_ref, out_ref):
    width = one_ref.shape[1]
    gains = jnp.concatenate([one_ref[...], two_ref[...], three_ref[...], jnp.zeros((5, width), F32)], axis=0)
    high = gains.astype(BF16)
    rest = (gains - high.astype(F32)).astype(BF16)
    gains = dot_nt(high, order_ref[...]) + dot_nt(rest, order_ref[...])
    out_ref[...] = jnp.zeros_like(out_ref)
    across = width // LANES
    for i in range(3):
        for j in range(across):
            at = i * across + j
            out_ref[at : at + 1, :] = gains[i : i + 1, j * LANES : (j + 1) * LANES]
    at = 3 * across
    lane = lax.broadcasted_iota(jnp.int32, (1, LANES), 1)
    out_ref[at : at + 1, :] = jnp.where(lane == 0, loss_ref[...], 0.0)
    bias = bias_ref[...]
    heads = 2 * heads_half
    row = lax.broadcasted_iota(jnp.int32, (LANES, bias.shape[0]), 0)
    column = lax.broadcasted_iota(jnp.int32, (LANES, bias.shape[0]), 1)
    source = row + jnp.where(mine_ref[...] == 0, 0, heads_half)
    source = jnp.where(source >= heads, source - heads, source)
    pick = jnp.where((column == 8 * (source // 2) + source % 2) & (row < heads), 1.0, 0.0)
    bias = split_dot(pick.astype(BF16), bias)
    high = bias.astype(BF16)
    rest = (bias - high.astype(F32)).astype(BF16)
    table = dot_nt(high, onehot_ref[...]) + dot_nt(rest, onehot_ref[...])
    count = table.shape[1]
    a_row = LANES // count
    for head in range(heads):
        place = head % a_row * count
        line = at + 1 + head // a_row
        out_ref[line : line + 1, place : place + count] = table[head : head + 1, :]


def member_of(seg_ref, sent_count):
    ids = lax.broadcasted_iota(jnp.int32, (sent_count, seg_ref.shape[1]), 0)
    hit = jnp.where(seg_ref[...] == ids, 1.0, 0.0)
    return hit.astype(BF16), jnp.sum(hit, axis=1, keepdims=True)


def tail_body(acc, value_ref, gains_ref, seg_ref, own_ref, other_ref, hidden_ref, inverse_ref, pooled_ref, unit_ref, low_ref, scale_ref, high, rest):
    hidden = value_ref[...] + acc[...]
    inverse = lax.rsqrt(jnp.mean(hidden * hidden, axis=1, keepdims=True) + EPSILON)
    hidden_ref[...] = hidden
    inverse_ref[...] = inverse
    final = hidden_ref[...] * inverse * gains_ref[2:3, :]
    high[...] = final.astype(BF16)
    rest[...] = (final - high[...].astype(F32)).astype(BF16)
    sents, count = member_of(seg_ref, pooled_ref.shape[0])
    pooled = ((dot(sents, high[...]) + dot(sents, rest[...])) / count).astype(BF16)
    pooled_ref[...] = pooled
    half = own_ref.shape[1]
    left = dot(pooled, own_ref[...])
    right = dot(pooled, other_ref[...])
    square = jnp.sum(left * left, axis=1, keepdims=True) + jnp.sum(right * right, axis=1, keepdims=True)
    scale = lax.rsqrt(square + EPSILON)
    scale_ref[...] = scale
    for at, value in ((0, left * scale), (half, right * scale)):
        unit_ref[:, at : at + half] = value
        low_ref[:, at : at + half] = value.astype(BF16)


def head_call(quarters, unit, scale, partner, column, sentence_loads, out_shapes):
    loads = [part(q) for q in (*quarters, unit, scale, partner, column)] + sentence_loads
    quarter = quarters[0].shape[0]
    total = 4 * quarter

    def run(get, loss_ref, embed_ref, *refs):
        *back_refs, every = refs
        for i in range(4):
            every[i * quarter : (i + 1) * quarter] = get(i)[...]
        unit, scale, partner, columns_id = (get(i)[...] for i in range(4, 8))
        partner = as_columns(
            jnp.concatenate([partner, jnp.zeros((1, LANES - partner.shape[1]), jnp.int32)], axis=1)
        )[: partner.shape[1], 0:1]
        own_count = unit.shape[0]
        sims = dot_nt(every[...], every[...]) * SOFTMAX_TEMP
        row = lax.broadcasted_iota(jnp.int32, (total, total), 0)
        column = lax.broadcasted_iota(jnp.int32, (total, total), 1)
        sims = jnp.where(row == column, NEG_FILL, sims)
        top = jnp.max(sims, axis=0, keepdims=True)
        lse_row = top + jnp.log(jnp.sum(jnp.exp(sims - top), axis=0, keepdims=True))
        own = sims[:own_count]
        own_top = jnp.max(own, axis=1, keepdims=True)
        own_lse = own_top + jnp.log(jnp.sum(jnp.exp(own - own_top), axis=1, keepdims=True))
        is_target = columns_id.astype(F32) == partner
        hit = jnp.where(is_target, 1.0, 0.0)
        target = jnp.sum(jnp.where(is_target, own, 0.0), axis=1, keepdims=True)
        loss_ref[...] = jnp.sum(own_lse - target, axis=0, keepdims=True)
        d_rows = (LOSS_SCALE * (jnp.exp(own - own_lse) - hit)).astype(BF16)
        d_cols = (LOSS_SCALE * (jnp.exp(own - lse_row) - hit)).astype(BF16)
        d_unit = SOFTMAX_TEMP * (dot(d_rows, every[...]) + dot(d_cols, every[...]))
        inner = jnp.sum(d_unit * unit, axis=1, keepdims=True)
        d_embed = (scale * (d_unit - unit * inner)).astype(BF16)
        embed_ref[...] = d_embed
        sentence_back(d_embed, [get(8 + i) for i in range(len(sentence_loads))], *back_refs)

    return stream("head", loads, out_shapes, run, [pltpu.VMEM((total, unit.shape[1]), BF16)])


def sentence_call(embed, sentence_loads, out_shapes):
    def run(get, *back_refs):
        sentence_back(get(0)[...], [get(1 + i) for i in range(len(sentence_loads))], *back_refs)

    return stream("sentence", [part(embed)] + sentence_loads, out_shapes, run)


def sentence_back(d_embed, sources, hidden_ref, low_ref, gain_out):
    seg_ref, own_ref, other_ref, value_ref, inverse_ref, gains_ref = sources
    half = own_ref.shape[1]
    d_pooled = dot_nt(d_embed[:, :half], own_ref[...]) + dot_nt(d_embed[:, half:], other_ref[...])
    sents, count = member_of(seg_ref, d_embed.shape[0])
    d_final = split_dot(sents, d_pooled / count, ((0,), (0,)))
    d_value, d_gain = norm_back(value_ref[...], inverse_ref[...], gains_ref[2:3, :], d_final)
    hidden_ref[...] = d_value
    low_ref[...] = d_value.astype(BF16)
    gain_out[...] = d_gain


def whole_call(body, args, out_shapes, scratch=(), name=None):
    return pl.pallas_call(
        body,
        out_shape=tuple(out_shapes),
        in_specs=[pl.BlockSpec(memory_space=pltpu.VMEM)] * len(args),
        out_specs=tuple(pl.BlockSpec(memory_space=pltpu.VMEM) for _ in out_shapes),
        scratch_shapes=scratch,
        compiler_params=params(),
        cost_estimate=cost(0, 0),
        name=name,
    )(*args)


def shape_of(kind, *dims):
    return jax.ShapeDtypeStruct(dims, kind)


def _stack_heads(part):
    lane = lax.broadcasted_iota(jnp.int32, part.shape, 1)
    zero = jnp.zeros_like(part)
    first = lane < LANES // 2
    return jnp.concatenate(
        [jnp.where(first, part, zero), jnp.where(first, zero, part)], axis=0
    )


def _unstack_heads(both):
    half = both.shape[0] // 2
    lane = lax.broadcasted_iota(jnp.int32, (half, LANES), 1)
    return jnp.where(lane < LANES // 2, both[:half], both[half:])


def _pad_keys(pad, ref):
    seq = ref.shape[0]
    pad[0:REACH] = jnp.zeros((REACH, LANES), pad.dtype)
    pad[REACH + seq :] = jnp.zeros((REACH, LANES), pad.dtype)
    pad[REACH : REACH + seq] = ref[...]


def _query_bits(shape):
    return lax.broadcasted_iota(jnp.int32, shape, 0) & (QB - 1)


def as_columns(values):
    count, length = values.shape
    side = max(LANES, length)
    square = jnp.concatenate([values.astype(F32), jnp.zeros((side - count, length), F32)], axis=0)
    return square.T


def attend_forward_kernel(
    q_ref, k_ref, v_ref, segq_ref, segk_ref, rel_ref, ctx_ref, probs_ref, kpad, vpad, mask, scores
):
    seq = q_ref.shape[0]
    blocks = seq // QB
    _pad_keys(kpad, k_ref)
    _pad_keys(vpad, v_ref)

    @pl.when(pl.program_id(0) == 0)
    def _():
        keys = as_columns(segk_ref[...])
        for b in range(blocks):
            same = keys[:, b : b + 1] == segq_ref[b : b + 1, :].astype(F32)
            mask[b] = jnp.where(same, 0.0, NEG_FILL)

    rel = rel_ref[0]
    row = lax.broadcasted_iota(jnp.int32, (2 * QB, WIN), 0)
    bias = jnp.where(row < QB, rel[0:1, :], rel[1:2, :])
    bits = _query_bits((2 * QB, WIN))
    step = 1
    while step < QB:
        bias = jnp.where((bits & step) != 0, pltpu.roll(bias, step, 1), bias)
        step *= 2
    bias = bias.T
    for b in range(blocks):
        query = _stack_heads(q_ref[b * QB : (b + 1) * QB] * jnp.asarray(SCORE_SCALE, BF16))
        scores[b] = dot_nt(kpad[b * QB : b * QB + WIN], query)
    values = scores[...] + bias[None] + mask[...]
    top = jnp.max(values, axis=1, keepdims=True)
    shifted = jnp.exp(values - top)
    total = jnp.sum(shifted, axis=1, keepdims=True)
    probs_ref[0] = (shifted * (1.0 / total)).astype(BF16)
    for b in range(blocks):
        part = dot_tn(probs_ref[0, b], vpad[b * QB : b * QB + WIN])
        ctx_ref[b * QB : (b + 1) * QB] = _unstack_heads(part).astype(BF16)


def attend_backward_kernel(
    q_ref, k_ref, v_ref, dctx_ref, probs_ref, dqkv_ref, dbias_ref,
    kpad, vpad, dk_acc, dv_acc, d_probs, d_low,
):
    seq = q_ref.shape[0]
    pair = pl.program_id(0)
    side = pl.num_programs(0) // 2
    later = pair // side
    q_at = pl.ds(pl.multiple_of(pair * LANES, LANES), LANES)
    k_at = pl.ds(pl.multiple_of((pair + 2 * side + later * side) * LANES, LANES), LANES)
    v_at = pl.ds(pl.multiple_of((pair + 3 * side + later * side) * LANES, LANES), LANES)
    blocks = seq // QB
    _pad_keys(kpad, k_ref)
    _pad_keys(vpad, v_ref)
    dk_acc[...] = jnp.zeros_like(dk_acc)
    dv_acc[...] = jnp.zeros_like(dv_acc)
    for b in range(blocks):
        window = slice(b * QB, b * QB + WIN)
        d_ctx = _stack_heads(dctx_ref[b * QB : (b + 1) * QB])
        d_probs[b] = dot_nt(vpad[window], d_ctx)
        dv_acc[window] += dot(probs_ref[0, b], d_ctx)
    probs = probs_ref[0].astype(F32)
    product = probs * d_probs[...]
    inner = jnp.sum(product, axis=1, keepdims=True)
    d_scores = product - probs * inner
    d_low[...] = d_scores.astype(BF16)
    total = jnp.sum(d_scores, axis=0).T
    for b in range(blocks):
        here = slice(b * QB, (b + 1) * QB)
        window = slice(b * QB, b * QB + WIN)
        query = _stack_heads(q_ref[here] * jnp.asarray(SCORE_SCALE, BF16))
        dk_acc[window] += dot(d_low[b], query)
        d_query = _unstack_heads(dot_tn(d_low[b], kpad[window])) * SCORE_SCALE
        dqkv_ref[here, q_at] = d_query.astype(BF16)
    dqkv_ref[:, k_at] = dk_acc[REACH : REACH + seq].astype(BF16)
    dqkv_ref[:, v_at] = dv_acc[REACH : REACH + seq].astype(BF16)
    bits = _query_bits((2 * QB, WIN))
    step = 1
    while step < QB:
        total = jnp.where((bits & step) != 0, pltpu.roll(total, WIN - step, 1), total)
        step *= 2
    first = jnp.sum(total[:QB], axis=0, keepdims=True)
    second = jnp.sum(total[QB:], axis=0, keepdims=True)
    dbias_ref[0] = jnp.concatenate([first, second, jnp.zeros((6, WIN), F32)], axis=0)


def _qkv_specs(seq, pairs):
    def spec(kind):
        return pl.BlockSpec((seq, LANES), lambda p: (0, kind * pairs + p))

    return [spec(0), spec(1), spec(2)]


def attend_forward(qkv, twice, windows, rel_window):
    seq = qkv.shape[0]
    pairs = rel_window.shape[0]
    blocks = seq // QB
    return pl.pallas_call(
        attend_forward_kernel,
        grid=(pairs,),
        out_shape=(
            jax.ShapeDtypeStruct((seq, pairs * LANES), BF16),
            jax.ShapeDtypeStruct((pairs, blocks, WIN, 2 * QB), BF16),
        ),
        in_specs=_qkv_specs(seq, pairs)
        + [
            pl.BlockSpec((blocks, 2 * QB), lambda p: (0, 0)),
            pl.BlockSpec((blocks, WIN), lambda p: (0, 0)),
            pl.BlockSpec((1, 2, WIN), lambda p: (p, 0, 0)),
        ],
        out_specs=(
            pl.BlockSpec((seq, LANES), lambda p: (0, p)),
            pl.BlockSpec((1, blocks, WIN, 2 * QB), lambda p: (p, 0, 0, 0)),
        ),
        scratch_shapes=[pltpu.VMEM((seq + 2 * REACH, LANES), BF16)] * 2
        + [pltpu.VMEM((blocks, WIN, 2 * QB), F32)] * 2,
        compiler_params=params(),
        cost_estimate=cost(8 * seq * WIN * LANES * pairs * 4, 8 * seq * LANES * pairs),
        name="attend_forward",
    )(qkv, qkv, qkv, twice, windows, rel_window)


def attend_backward(qkv, d_context, probs):
    seq = qkv.shape[0]
    pairs = probs.shape[0]
    blocks = seq // QB
    lane_block = pl.BlockSpec((seq, LANES), lambda p: (0, p))
    return pl.pallas_call(
        attend_backward_kernel,
        grid=(pairs,),
        out_shape=(
            jax.ShapeDtypeStruct((seq, 3 * pairs * LANES), BF16),
            jax.ShapeDtypeStruct((pairs, 8, WIN), F32),
        ),
        in_specs=_qkv_specs(seq, pairs)
        + [
            lane_block,
            pl.BlockSpec((1, blocks, WIN, 2 * QB), lambda p: (p, 0, 0, 0)),
        ],
        out_specs=(
            pl.BlockSpec((seq, 3 * pairs * LANES), lambda p: (0, 0)),
            pl.BlockSpec((1, 8, WIN), lambda p: (p, 0, 0)),
        ),
        scratch_shapes=[pltpu.VMEM((seq + 2 * REACH, LANES), BF16)] * 2
        + [pltpu.VMEM((seq + 2 * REACH, LANES), F32)] * 2
        + [pltpu.VMEM((blocks, WIN, 2 * QB), F32), pltpu.VMEM((blocks, WIN, 2 * QB), BF16)],
        compiler_params=params(),
        cost_estimate=cost(16 * seq * WIN * LANES * pairs * 4, 16 * seq * LANES * pairs),
        name="attend_backward",
    )(qkv, qkv, qkv, d_context, probs)


CORE = 1
CROSS = 2


def hop(value, mask):
    size = lax.axis_size("dp")
    return lax.ppermute(value, "dp", [(i, i ^ mask) for i in range(size)])


def over(value):
    return lax.ppermute(value, "mp", [(0, 1), (1, 0)])


def cross(value):
    return hop(value, CROSS)


def core(value):
    return hop(value, CORE)


def go(waits, *sends, keep=(), join=True):
    values = [value for _, value in sends]
    held = lax.optimization_barrier((*values, *keep, *waits))
    results = [how(value) for (how, _), value in zip(sends, held)]
    if join:
        results = list(lax.optimization_barrier(tuple(results)))
    return results + list(held[len(values) : len(values) + len(keep)])


def slot_masks(size):
    rest = size // 4
    return [z * 4 + x * 2 + c for c in range(2) for x in range(2) for z in range(rest)]


def strides(size):
    found = []
    stride = 4
    while stride < size:
        found.append(stride)
        stride *= 2
    return found


def gather_near(shard, waits, widths=None):
    size = lax.axis_size("dp")
    pieces = [shard]
    stride = 4
    while stride < size:
        radix = min(4, size // stride)
        shard = jnp.concatenate(pieces, axis=0) if len(pieces) > 1 else shard
        sends = [(functools.partial(hop, mask=j * stride), shard) for j in range(1, radix)]
        pieces = [shard] + go(waits, *sends)
        stride *= radix
    return jnp.concatenate(pieces, axis=0) if widths is None else stack_rows(pieces, widths)


def rows(*pieces):
    return jnp.concatenate(pieces, axis=0)


def columns(*pieces):
    return jnp.concatenate(pieces, axis=1)


def gather_weights(start, later, n_one, n_early, n_three, early, begin, between):
    size = lax.axis_size("dp")
    steps = strides(size)
    n_two = start.shape[1] - n_one
    n_four = later.shape[1] - n_three
    if len(steps) == 2:
        got = go((), *((functools.partial(hop, mask=4 * j), start) for j in range(1, 4)))
        more = hop(later, 4)
        one, two = stack_rows([start, *got], (n_one, n_two))
        later = stack_rows([later, more], (n_early, later.shape[1] - n_early))
        wide_step = functools.partial(hop, mask=steps[1])
    else:
        one, two = gather_near(start, (), (n_one, n_two))

        later = [later[:, :n_early], later[:, n_early:]]

        def wide_step(value):
            whole = gather_near(value, ())
            return whole[value.shape[0] :]

    one_x, two_y, more = go(early, (cross, one), (over, two), (wide_step, later[0]))
    (one,) = stack_rows([one, one_x], (n_one,))
    (two,) = stack_rows([two, two_y], (n_two,))
    one_y, two_x, one_c, two_c, more_b = go(
        (), (over, one), (cross, two), (core, one), (core, two), (wide_step, later[1])
    )
    if len(steps) == 2:
        have = later[0].shape[0]

        def put(near_a, near_b, far_a, far_b, three_ref, four_ref):
            for at, left, right in ((0, near_a, near_b), (have, far_a, far_b)):
                here = slice(at, at + have)
                three_ref[here, :n_early] = left[...]
                three_ref[here, n_early:] = right[:, : n_three - n_early]
                four_ref[here] = right[:, n_three - n_early :]

        three, four = whole_call(
            put,
            (*later, more, more_b),
            (shape_of(BF16, 2 * have, n_three), shape_of(BF16, 2 * have, n_four)),
            (),
            "put_rows",
        )
    else:
        later = rows(columns(*later), columns(more, more_b))
        three, four = later[:, :n_three], later[:, n_three:]
    three_x, four_y, one_yc, two_xc = go((), (cross, three), (over, four), (core, one_y), (core, two_x))
    (three,) = stack_rows([three, three_x], (n_three,))
    (four,) = stack_rows([four, four_y], (four.shape[1],))
    three_y, four_x, three_c, four_c, one, one_c, one_y, one_yc, two, two_x, two_c, two_xc, *early = go(
        (),
        (over, three),
        (cross, four),
        (core, three),
        (core, four),
        keep=(one, one_c, one_y, one_yc, two, two_x, two_c, two_xc, *early),
        join=False,
    )
    first, second = along_x(one, one_c, one_y, one_yc), along_y(two, two_x, two_c, two_xc)
    done = between(begin(first, early), second, early)
    four_xc, *done = go((three_y, four_x, three_c, four_c), (core, four_x), keep=done, join=False)
    (three_yc,) = go((four_xc,), (core, three_y), join=False)
    third, fourth = along_x(three, three_c, three_y, three_yc), along_y(four, four_x, four_c, four_xc)
    return first, second, third, fourth, early, done


def along_x(near, near_c, other, other_c):
    count = near.shape[0]
    return ((near, 0, count), (near_c, 0, count)), ((other, 0, count), (other_c, 0, count))


def along_y(near, side, near_c, side_c):
    count = near.shape[0] // 2
    return tuple(
        tuple((array, at, count) for array in (near, side, near_c, side_c)) for at in (0, count)
    )


def pack(name, sources, mib):
    widths = [count for *_, count in sources]
    block = sources[0][0].shape[0]

    def run(*refs):
        ins, out = refs[: len(sources)], refs[len(sources)]
        buffers, sem = refs[len(sources) + 1 : -1], refs[-1]
        copies = []
        for i, (_, first, count) in enumerate(sources):
            copy = pltpu.make_async_copy(ins[i].at[:, pl.ds(first, count)], buffers[i], sem.at[i])
            copy.start()
            copies.append(copy)
        at = 0
        for copy, buffer, width in zip(copies, buffers, widths):
            copy.wait()
            out[:, at : at + width] = buffer[...]
            at += width

    return pl.pallas_call(
        run,
        out_shape=shape_of(BF16, block, sum(widths)),
        in_specs=[pl.BlockSpec(memory_space=pltpu.HBM)] * len(sources),
        out_specs=pl.BlockSpec(memory_space=pltpu.VMEM),
        scratch_shapes=[pltpu.VMEM((block, width), BF16) for width in widths]
        + [pltpu.SemaphoreType.DMA((len(sources),))],
        compiler_params=params(mib),
        cost_estimate=cost(0, 0),
        name=name,
    )(*(array for array, *_ in sources))


def gather_dp(shard):
    near = gather_near(shard, ())
    side, c_near = go((near,), (cross, near), (core, near))
    return near, side, c_near, core(side)


def low(value):
    return value.astype(BF16)


def add(left, right):
    return (left.astype(F32) + right.astype(F32)).astype(BF16)


def product(left, begin, end, right, got=None):
    value = dot_tn(left[:, begin:end], right)
    if got is not None:
        value = value + got.astype(F32)
    return low(value)


def rest_start(value):
    half = value.shape[0] // 2
    return value[half:], value[:half]


def sum_half(value, send):
    gone, stays = rest_start(value)
    return stays + send(low(gone)).astype(F32)


def rest_hops(size):
    return [functools.partial(hop, mask=stride) for stride in reversed(strides(size))]


def shards(
    tokens,
    seg_ids,
    buckets,
    labels,
    w_query,
    w_key,
    w_value,
    w_out,
    w_in,
    w_back,
    gain_attn,
    gain_ffn,
    gain_final,
    w_pool,
    rel_table,
):
    micro_count, seq, width = tokens.shape
    size = lax.axis_size("dp")
    me = lax.axis_index("dp")
    mine = lax.axis_index("mp")
    block = width // size
    inner_half = w_query.shape[1]
    hidden_half = w_in.shape[1]
    sent_local = labels.shape[1]
    bucket_count = rel_table.shape[0]
    heads_half = rel_table.shape[1]
    masks = slot_masks(size)

    x_own = lax.dynamic_index_in_dim(tokens, mine, 0, keepdims=False)
    segments = lax.dynamic_index_in_dim(seg_ids, mine, 0, keepdims=False)[0]
    partner = lax.dynamic_index_in_dim(labels, mine, 0, keepdims=False)

    slot_block = jnp.stack([jnp.bitwise_xor(me, m) for m in masks]).astype(jnp.int32)
    source = (slot_block[:, None] * block + jnp.arange(block, dtype=jnp.int32)[None, :]).reshape(-1)
    order = (jnp.arange(width, dtype=jnp.int32)[:, None] == source[None, :]).astype(BF16)
    order = lax.optimization_barrier(order)
    inputs = dot(x_own, order)


    row_f32 = shape_of(F32, seq, width)
    row_low = shape_of(BF16, seq, width)
    column_f32 = shape_of(F32, seq, 1)
    gain_f32 = shape_of(F32, 1, width)
    heads = 3 * inner_half
    piece = hidden_half // 2
    halves = [(side, i * inner_half, inner_half) for side in range(2) for i in range(2)]

    def hidden_blocks(weights, first_col=0):
        return [(weights[side], first_col + col, n) for side, col, n in halves]

    def begin(first, early):
        inputs, rel_window, twice, windows, *_ = early
        qkv, normed1_low, inverse1, gains = qkv_call(inputs, first, inner_half)
        context, probs = attend_forward(qkv, twice, windows, rel_window)
        return qkv, normed1_low, inverse1, gains, context, probs

    def between(started, second, early):
        qkv, normed1_low, inverse1, gains, context, probs = started
        inputs = early[0]
        hidden1, inverse2, normed2_low = narrow(
            "attn_out",
            [(context, i * inner_half, second[i], piece, inner_half) for i in range(2)],
            (inputs, gains),
            (row_f32, column_f32, row_low),
            functools.partial(norm_body, 1),
        )
        act0, slope0 = wide("act0", normed2_low, hidden_blocks(second), (), gelu_both, 2)
        return normed1_low, inverse1, gains, qkv, context, probs, hidden1, inverse2, normed2_low, act0, slope0

    gains_col = jnp.pad(
        jnp.stack([gain_attn, gain_ffn, gain_final], axis=1), ((0, 0), (0, LANES - 3))
    )
    pool_half = w_pool.shape[1] // 2
    pool_own = lax.dynamic_slice_in_dim(w_pool, mine * pool_half, pool_half, axis=1)
    moved = piece // 3
    back_shard = w_back.T
    if block % 16:
        start = columns(w_query, w_key, w_value, gains_col, w_in[:, :piece], w_out.T)
        later = columns(
            back_shard[:, :piece],
            back_shard[:, hidden_half - moved :],
            pool_own,
            w_in[:, piece:],
            back_shard[:, piece : hidden_half - moved],
        )
    else:
        start = pack(
            "pack_start",
            [(w, 0, inner_half) for w in (w_query, w_key, w_value)]
            + [(gains_col, 0, LANES), (w_in, 0, piece), (w_out.T, 0, inner_half)],
            60,
        )
        back_shard, w_in, _ = lax.optimization_barrier((back_shard, w_in, start))
        later = pack(
            "pack_later",
            [
                (back_shard, 0, piece),
                (back_shard, hidden_half - moved, moved),
                (pool_own, 0, pool_half),
                (w_in, piece, piece),
                (back_shard, piece, piece - moved),
            ],
            16,
        )
    rel_other = over(lax.optimization_barrier((rel_table, start))[0])
    rel_all = jnp.concatenate([rel_table, rel_other], axis=1).astype(F32)
    near_buckets = lax.slice_in_dim(buckets, seq - 1 - REACH, seq - 1 - REACH + WIN)
    onehot = (near_buckets[None, :] == jnp.arange(bucket_count, dtype=jnp.int32)[:, None]).astype(F32)
    onehot = lax.optimization_barrier(low(onehot))
    rel_window = dot(rel_all, onehot.astype(F32), ((0,), (0,)), HIGHEST).reshape(heads_half, 2, WIN)
    padded = jnp.pad(segments, (REACH, REACH), constant_values=-1)
    windows = jnp.stack([padded[at : at + WIN] for at in range(0, seq, QB)])
    twice = jnp.tile(segments.reshape(seq // QB, QB), (1, 2))
    local_ids = jnp.arange(sent_local, dtype=jnp.int32)
    column_id = (slot_block[:, None] * sent_local + local_ids[None, :]).reshape(1, -1)
    early = (
        inputs, rel_window, twice, windows, order, onehot, column_id, partner[None, :], segments[None, :], mine.reshape(1, 1),
        (me * block).astype(jnp.uint32), (mine * heads_half).astype(jnp.uint32)
    )
    first, second, third, fourth, early, done = gather_weights(
        start,
        later,
        heads + LANES,
        piece,
        piece + moved + pool_half,
        early,
        begin,
        between,
    )
    inputs, rel_window, twice, windows, order, onehot, column_id, partner, seg_lane, mine_array, gain_at, table_at = early
    normed1_low, inverse1, gains, qkv, context, probs, hidden1, inverse2, normed2_low, act0, slope0 = done

    act1, up_kept = wide("act1", normed2_low, hidden_blocks(fourth), (), gelu_only, 2)
    pool_loads = [weight(side, piece + moved, pool_half) for side in third]
    hidden2, inverse3, pooled_low, unit, unit_low, scale = narrow(
        "ffn_out",
        [(act0, i * piece, third[i], 0, piece) for i in range(2)]
        + [(act1, i * piece, fourth[i], piece, piece - moved) for i in range(2)]
        + [(act1, (i + 1) * piece - moved, third[i], piece, moved) for i in range(2)],
        (hidden1, gains, seg_lane, *pool_loads),
        (
            row_f32,
            column_f32,
            shape_of(BF16, sent_local, width),
            shape_of(F32, sent_local, width),
            shape_of(BF16, sent_local, width),
            shape_of(F32, sent_local, 1),
        ),
        tail_body,
        [pltpu.VMEM((seq, width), BF16)] * 2,
    )
    quarters = gather_dp(unit_low)

    total_sent = column_id.shape[1]
    sentence_loads = [part(seg_lane), *pool_loads, part(hidden2), part(inverse3), part(gains)]
    back_shapes = (row_f32, row_low, gain_f32)
    if total_sent <= 1024:
        loss_local, embed_low, d_hidden2, ffn_low, d_gain3 = head_call(
            quarters,
            unit,
            scale,
            partner,
            column_id,
            sentence_loads,
            (shape_of(F32, 1, 1), shape_of(BF16, sent_local, width), *back_shapes),
        )
    else:
        every = rows(*quarters)
        position = jnp.arange(total_sent, dtype=jnp.int32)
        sims = dot_nt(every, every) * SOFTMAX_TEMP
        sims = jnp.where(position[:, None] == position[None, :], NEG_FILL, sims)
        lse_row = jax.nn.logsumexp(sims, axis=0, keepdims=True)
        own_sims = sims[:sent_local]
        own_lse = jax.nn.logsumexp(own_sims, axis=1, keepdims=True)
        is_target = column_id == partner.reshape(-1, 1)
        target = jnp.sum(jnp.where(is_target, own_sims, 0.0), axis=-1, keepdims=True)
        loss_local = jnp.sum(own_lse - target)
        hit = is_target.astype(F32)
        d_rows = low(LOSS_SCALE * (jnp.exp(own_sims - own_lse) - hit))
        d_cols = low(LOSS_SCALE * (jnp.exp(own_sims - lse_row) - hit))
        d_unit = SOFTMAX_TEMP * (dot(d_rows, every) + dot(d_cols, every))
        embed_low = low(scale * (d_unit - unit * jnp.sum(d_unit * unit, axis=-1, keepdims=True)))
        d_hidden2, ffn_low, d_gain3 = sentence_call(embed_low, sentence_loads, back_shapes)

    half = width // 2
    quarter = width // 4

    back0_sent, back1_sent = gradients("back_sent", ffn_low, half, half, (act0, act1))
    (pool_sent,) = gradients("pool_sent", pooled_low, half, half, (embed_low,))
    back0_got, back1_got, pool_got, ffn_later = go(
        (), (core, back0_sent), (core, back1_sent), (core, pool_sent), keep=(ffn_low,), join=False
    )
    pool_hi = product(pooled_low, quarter, half, embed_low, pool_got[quarter:])
    pool_lo = product(pooled_low, 0, quarter, embed_low, pool_got[:quarter])
    up0 = wide("up0", ffn_later, hidden_blocks(third), (slope0,), times_slope)

    back_hi = product(ffn_low, quarter, half, act0, back0_got[quarter:])
    back_lo = product(ffn_low, 0, quarter, act0, back0_got[:quarter])
    back_own = product(ffn_low, 0, half, act1[:, :piece], back1_got[:, :piece])
    back_oth = product(ffn_low, 0, half, act1[:, piece:], back1_got[:, piece:])
    got_lo, got_own, got_pool, ffn_later, up0, back_lo, back_own, pool_lo = go(
        (),
        (cross, back_hi),
        (over, back_oth),
        (cross, pool_hi),
        keep=(ffn_later, up0, back_lo, back_own, pool_lo),
    )
    back_blocks = [
        block
        for side in range(2)
        for block in (
            (fourth[side], piece, inner_half),
            (fourth[side], piece + inner_half, piece - moved - inner_half),
            (third[side], piece, moved),
        )
    ]
    up1 = wide("up1", ffn_later, back_blocks, (up_kept,), times_slope_of)
    in0_sent, in1_sent = gradients("in_sent", normed2_low, half, half, (up0, up1))
    in0_got, in1_got, up0, up1 = go((), (core, in0_sent), (core, in1_sent), keep=(up0, up1))
    attn_low, d_gain2, d_hidden1 = narrow(
        "ffn_in_back",
        [(up0, i * piece, second[i], 0, piece) for i in range(2)]
        + [(up1, i * piece, fourth[i], 0, piece) for i in range(2)],
        (hidden1, inverse2, gains, d_hidden2),
        (row_low, gain_f32, row_f32),
        functools.partial(back_body, 1),
    )
    d_context = wide("d_context", attn_low, [(second[side], piece, inner_half) for side in range(2)])

    pool_lo = add(pool_lo, got_pool)
    back_lo = add(back_lo, got_lo)
    back_own = add(back_own, got_own)
    in_hi = product(normed2_low, quarter, half, up0, in0_got[quarter:])
    in_lo = product(normed2_low, 0, quarter, up0, in0_got[:quarter])
    in_own = product(normed2_low, 0, half, up1[:, :piece], in1_got[:, :piece])
    in_oth = product(normed2_low, 0, half, up1[:, piece:], in1_got[:, piece:])
    got_first, got_x, got_in_own, d_context, pool_lo, back_lo, back_own, in_lo, in_own = go(
        (got_lo, got_own),
        (over, columns(back_lo[:, piece:], pool_lo[:, pool_half:])),
        (cross, columns(back_own[quarter:], in_hi)),
        (over, in_oth),
        keep=(d_context, pool_lo, back_lo, back_own, in_lo, in_own),
        join=False,
    )
    d_qkv, d_bias = attend_backward(qkv, d_context, probs)
    query_both = 2 * inner_half
    late_sent = sent_columns("late_sent", half, ((attn_low, context), (normed1_low, d_qkv)))
    late_got, d_qkv_later = go((), (core, late_sent), keep=(d_qkv,), join=False)
    grad_slots, d_gain1 = narrow(
        "qkv_back",
        [(d_qkv_later, i * inner_half, first[i], 0, inner_half) for i in range(2)]
        + [(d_qkv_later, (1 + i) * query_both, first[i], inner_half, query_both) for i in range(2)],
        (inputs, inverse1, gains, d_hidden1),
        (row_low, gain_f32),
        functools.partial(back_body, 0),
    )

    table_row = 3 * (width // LANES) + 1
    table_rows = -(-2 * heads_half * bucket_count // LANES)
    small_rows = -(-(table_row + table_rows) // 8) * 8
    (flat,) = whole_call(
        functools.partial(small_kernel, heads_half),
        (d_gain1, d_gain2, d_gain3, order, d_bias.reshape(-1, WIN), onehot, loss_local.reshape(1, 1), mine_array),
        (shape_of(F32, small_rows, LANES),),
        (),
        "small",
    )
    (grad_own,) = whole_call(turn_kernel, (grad_slots, order), (row_low,), (), "turn")
    flat_got, flat = go((), (over, flat), keep=(flat,), join=False)
    got_first, got_x, got_in_own = lax.optimization_barrier((got_first, got_x, got_in_own))
    flat = flat + flat_got
    got_second, got_in_lo = got_x[:, :piece], got_x[:, piece:]

    far = rest_hops(size)
    back_all = columns(
        add(back_lo[:, :piece], got_first[:, :piece]),
        add(back_own[:quarter], got_second),
        add(pool_lo[:, :pool_half], got_first[:, piece:]),
    )
    back_rest, back_stay = rest_start(back_all)
    in_lo = add(in_lo, got_in_lo)
    in_own = add(in_own, got_in_own)
    out_got, qkv_got = late_got[:, :query_both], late_got[:, query_both:]
    out_hi = product(attn_low, quarter, half, context, out_got[quarter:])
    out_lo = product(attn_low, 0, quarter, context, out_got[:quarter])
    query_hi = product(normed1_low, quarter, half, d_qkv[:, :query_both], qkv_got[quarter:, :query_both])
    query_lo = product(normed1_low, 0, quarter, d_qkv[:, :query_both], qkv_got[:quarter, :query_both])
    kv_own = product(
        normed1_low, 0, half, d_qkv[:, query_both : 2 * query_both], qkv_got[:, query_both : 2 * query_both]
    )
    kv_oth = product(normed1_low, 0, half, d_qkv[:, 2 * query_both :], qkv_got[:, 2 * query_both :])
    rest_hop = [functools.partial(hop, mask=j * 4) for j in range(1, min(4, size // 4))]
    back_more, got_first, got_x, got_kv, flat_got, back_stay, in_lo, in_own, out_lo, query_lo, kv_own, flat = go(
        (grad_own,),
        (far[0], back_rest),
        (over, in_lo[:, piece:]),
        (cross, columns(in_own[quarter:], out_hi, query_hi)),
        (over, kv_oth),
        (core, flat),
        keep=(back_stay, in_lo, in_own, out_lo, query_lo, kv_own, flat),
    )

    count = flat.shape[0]

    def in_two(value):
        high = value.astype(BF16).astype(F32)
        return jnp.concatenate([high, value - high], axis=0).astype(BF16)

    def from_two(pair):
        return pair[:count].astype(F32) + pair[count : 2 * count].astype(F32)

    def late_adds(
        stay, more, in_lo, got_first, in_own, got_x, out_lo, query_lo, kv_own, got_kv, flat, got_flat, *outs
    ):
        back_gone, back_keep, in_gone, in_keep, heads_gone, heads_keep, kv_gone, kv_keep, small = outs
        rows_z = stay.shape[0] // 2
        total = add(stay[...], more[...])
        back_keep[...] = total[:rows_z]
        back_gone[...] = total[rows_z:]
        rows_z = in_lo.shape[0] // 2
        for at, total in (
            (0, add(in_lo[:, :piece], got_first[...])),
            (piece, add(in_own[:quarter], got_x[:, :piece])),
        ):
            in_keep[:, at : at + piece] = total[:rows_z]
            in_gone[:, at : at + piece] = total[rows_z:]
        for i, ref in enumerate((out_lo, query_lo)):
            first_col = piece + i * query_both
            total = add(ref[...], got_x[:, first_col : first_col + query_both])
            heads_keep[:, i * inner_half : (i + 1) * inner_half] = total[:, :inner_half]
            heads_gone[:, i * inner_half : (i + 1) * inner_half] = total[:, inner_half:]
        kv_keep[...] = add(kv_own[:quarter], got_kv[:quarter])
        kv_gone[:, :query_both] = add(kv_own[quarter:], got_kv[quarter:])
        small[...] = flat[...] + got_flat[...]
        kv_gone[:, query_both:] = jnp.zeros((quarter, LANES), BF16)
        pair = in_two(small[...])
        kv_gone[: 2 * count, query_both:] = pair
        small[...] = from_two(pair)

    cut = [shape_of(BF16, back_stay.shape[0] // 2, back_stay.shape[1])] * 2
    cut += [shape_of(BF16, quarter // 2, hidden_half)] * 2 + [shape_of(BF16, quarter, query_both)] * 2
    cut += [
        shape_of(BF16, quarter, query_both + LANES),
        shape_of(BF16, quarter, query_both),
        shape_of(F32, count, LANES),
    ]
    back_rest, back_stay, in_rest, in_stay, heads_gone, heads_keep, kv_gone, kv_keep, flat = whole_call(
        late_adds,
        (back_stay, back_more, in_lo, got_first, in_own, got_x, out_lo, query_lo, kv_own, got_kv, flat, flat_got),
        cut,
        (),
        "late_adds",
    )
    early_rows = seq * 11 // 32
    back_more, in_more, got_first, got_second, grad_other, back_stay, in_stay, heads_keep, kv_keep, flat = go(
        (),
        (far[1], back_rest),
        (far[0], in_rest),
        (over, heads_gone),
        (cross, kv_gone),
        (over, grad_own[:early_rows]),
        keep=(back_stay, in_stay, heads_keep, kv_keep, flat),
    )

    def finish(value):
        value = value.astype(F32)
        for send in far[2:]:
            value = sum_half(value, send)
        return value

    n_last = query_both + query_both
    if len(far) == 2:
        rest = block
        late_rows = seq - early_rows

        def last_adds(stay, more, heads_ref, got_heads, kv_ref, got_kv, flat_ref, back_ref, back_got, own_ref, *outs):
            one, two, three, in_keep, keep, flat_out, tail, pool_ref = outs
            pool = add(back_ref[:, hidden_half:], back_got[:, hidden_half:])
            pool_ref[...] = pool
            tail[:late_rows] = own_ref[early_rows:]
            tail[late_rows:, :pool_half] = pool
            tail[late_rows:, pool_half:] = jnp.zeros((rest, width - pool_half), BF16)
            total = add(stay[...], more[...])
            in_keep[...] = total[:rest]
            one[:, LANES : LANES + hidden_half] = total[rest:]
            pair = in_two(flat_ref[...] + from_two(got_kv[:, query_both:]))
            flat_out[...] = from_two(pair)
            for i, (ref, at) in enumerate(((keep, 0), (one, LANES + hidden_half), (two, LANES), (three, LANES))):
                here = slice(i * rest, (i + 1) * rest)
                if i:
                    ref[:, :LANES] = pair
                ref[:, at : at + query_both] = add(heads_ref[here], got_heads[here])
                ref[:, at + query_both : at + n_last] = add(kv_ref[here], got_kv[here, :query_both])

        one, two, three, in_stay, last_stay, flat, tail, grad_pool = whole_call(
            last_adds,
            (in_stay, in_more, heads_keep, got_first, kv_keep, got_second, flat, back_stay, back_more, grad_own),
            (
                shape_of(BF16, rest, LANES + hidden_half + n_last),
                shape_of(BF16, rest, LANES + n_last),
                shape_of(BF16, rest, LANES + n_last),
                shape_of(BF16, rest, hidden_half),
                shape_of(BF16, rest, n_last),
                shape_of(F32, count, LANES),
                shape_of(BF16, late_rows + rest, width),
                shape_of(BF16, rest, pool_half),
            ),
            (),
            "last_adds",
        )
        got_one, got_two, got_three, got_tail, back_stay, back_more = go(
            (),
            (rest_hop[0], one),
            (rest_hop[1], two),
            (rest_hop[2], three),
            (over, tail),
            keep=(back_stay, back_more),
            join=False,
        )

        def back_final(stay, more, back_ref):
            back_ref[...] = stay[:, :hidden_half].astype(F32) + more[:, :hidden_half].astype(F32)

        (grad_back,) = whole_call(
            back_final, (back_stay, back_more), (shape_of(F32, rest, hidden_half),), (), "back_final"
        )

        def tokens_final(mine_ref, own_ref, first_ref, tail_ref, pool_own, out_ref, pool_ref):
            first = mine_ref[...] == 0
            own, other = pool_own[...].astype(F32), tail_ref[late_rows:, :pool_half].astype(F32)
            pool_ref[:, :pool_half] = jnp.where(first, own, other)
            pool_ref[:, pool_half:] = jnp.where(first, other, own)
            for at, count, ref in ((0, early_rows, first_ref), (early_rows, late_rows, tail_ref)):
                here = slice(at, at + count)
                own, other = own_ref[here].astype(F32), ref[:count].astype(F32)
                out_ref[0, here] = jnp.where(first, own, other).astype(BF16)
                out_ref[1, here] = jnp.where(first, other, own).astype(BF16)

        grad_tokens, grad_pool = whole_call(
            tokens_final,
            (mine_array, grad_own, grad_other, got_tail, grad_pool),
            (shape_of(BF16, 2, seq, width), shape_of(F32, rest, 2 * pool_half)),
            (),
            "tokens_final",
        )
        got_one, got_two, got_three, grad_tokens = lax.optimization_barrier(
            (got_one, got_two, got_three, grad_tokens)
        )

        def last_final(
            stay, in_keep, one_ref, two_ref, three_ref, flat_ref, order_ref, mine_ref, *outs
        ):
            in_ref, out_ref, q_ref, k_ref, v_ref, loss_ref, gains_ref, table_ref, wide_ref = outs
            in_ref[...] = in_keep[...].astype(F32) + one_ref[:, LANES : LANES + hidden_half].astype(F32)
            total = stay[...].astype(F32) + one_ref[:, LANES + hidden_half :].astype(F32)
            total = total + two_ref[:, LANES:].astype(F32) + three_ref[:, LANES:].astype(F32)
            for i, ref in enumerate((out_ref, q_ref, k_ref, v_ref)):
                ref[...] = total[:, i * inner_half : (i + 1) * inner_half]
            small = flat_ref[...]
            for ref in (one_ref, two_ref, three_ref):
                small = small + from_two(ref[:, :LANES])
            across = width // LANES
            loss_ref[...] = small[3 * across : 3 * across + 1, :1] / (micro_count * sent_local * size)
            wide_ref[...] = jnp.zeros_like(wide_ref)
            for i in range(3):
                for j in range(across):
                    wide_ref[i : i + 1, j * LANES : (j + 1) * LANES] = small[i * across + j : i * across + j + 1]
            high = wide_ref[...].astype(BF16)
            low_part = (wide_ref[...] - high.astype(F32)).astype(BF16)
            pick = order_ref[:, :LANES]
            gains_ref[...] = dot(high, pick) + dot(low_part, pick)
            a_row = LANES // bucket_count
            heads_list = []
            for head in range(2 * heads_half):
                line = table_row + head // a_row
                place = head % a_row * bucket_count
                heads_list.append(small[line : line + 1, place : place + bucket_count])
            first = jnp.concatenate(heads_list[:heads_half], axis=0)
            second = jnp.concatenate(heads_list[heads_half:], axis=0)
            table_ref[...] = jnp.where(mine_ref[...] == 0, first, second)

        head_shape = shape_of(F32, rest, inner_half)
        grad_in, grad_out, grad_query, grad_key, grad_value, loss, gains_mine, table_mine = whole_call(
            last_final,
            (last_stay, in_stay, got_one, got_two, got_three, flat, order, mine_array),
            (
                shape_of(F32, rest, hidden_half),
                *(head_shape,) * 4,
                shape_of(F32, 1, 1),
                shape_of(F32, 8, LANES),
                shape_of(F32, heads_half, bucket_count),
            ),
            [pltpu.VMEM((8, width), F32)],
            "last_final",
        )
        loss = loss.reshape(())
        gains_mine = gains_mine[:3, :block]
        table_mine = table_mine.T
    else:
        flat = flat + from_two(got_second[:, query_both:])
        grad_other = rows(grad_other, over(grad_own[early_rows:]))
        in_rest, in_stay = rest_start(add(in_stay, in_more))
        last = columns(add(heads_keep, got_first), add(kv_keep, got_second[:, :query_both]))
        last_rest, last_stay = rest_start(last)
        in_more, last_more, *flat_got = go(
            (), (far[1], in_rest), (far[0], last_rest), *((how, flat) for how in rest_hop)
        )
        last_rest, last_stay = rest_start(add(last_stay, last_more))
        last_more = far[1](last_rest)
        flat = flat + sum(flat_got)
        for send in far[:-2]:
            flat = flat + send(flat)
        grad_last = finish(last_stay.astype(F32) + last_more.astype(F32))
        grad_in = finish(in_stay.astype(F32) + in_more.astype(F32))
        back_all = finish(back_stay.astype(F32) + back_more.astype(F32))
        grad_back, grad_pool = back_all[:, :hidden_half], back_all[:, hidden_half:]
        pool_other = over(grad_pool)
        grad_pool = jnp.where(mine == 0, columns(grad_pool, pool_other), columns(pool_other, grad_pool))
        grad_out, grad_query, grad_key, grad_value = (
            grad_last[:, i * inner_half : (i + 1) * inner_half] for i in range(4)
        )
        grad_tokens = jnp.where(
            mine == 0, jnp.stack([grad_own, grad_other]), jnp.stack([grad_other, grad_own])
        )
        across = width // LANES
        zero = jnp.uint32(0)
        gains_mine = lax.dynamic_slice(flat[: 3 * across].reshape(3, width), (zero, gain_at), (3, block))
        loss = flat[3 * across, 0] / (micro_count * sent_local * size)
        table_sum = flat[table_row : table_row + table_rows].reshape(-1, bucket_count)[: 2 * heads_half]
        table_mine = lax.dynamic_slice(table_sum, (table_at, zero), (heads_half, bucket_count)).T
    return (
        loss,
        grad_tokens,
        grad_query,
        grad_key,
        grad_value,
        grad_out.T,
        grad_in,
        grad_back.T,
        gains_mine[0],
        gains_mine[1],
        gains_mine[2],
        grad_pool,
        table_mine,
    )


def solution(mesh):
    placed = (
        P(None, "dp", None),
        P(None, "dp", None),
        P(),
        P(None, "dp"),
        P("dp", "mp"),
        P("dp", "mp"),
        P("dp", "mp"),
        P("mp", "dp"),
        P("dp", "mp"),
        P("mp", "dp"),
        P("dp"),
        P("dp"),
        P("dp"),
        P("dp", None),
        P(None, "mp"),
    )
    return jax.shard_map(
        shards,
        mesh=mesh,
        in_specs=placed,
        out_specs=(
            P(),
            P(None, "dp", None),
            P("dp", "mp"),
            P("dp", "mp"),
            P("dp", "mp"),
            P("mp", "dp"),
            P("dp", "mp"),
            P("mp", "dp"),
            P("dp"),
            P("dp"),
            P("dp"),
            P("dp", None),
            P(None, "mp"),
        ),
        check_vma=False,
    )
```

```python
import functools

import jax
import jax.numpy as jnp
from jax import lax
from jax.experimental import pallas as pl
from jax.experimental.pallas import tpu as pltpu
from jax.sharding import PartitionSpec as P

NEG_FILL = -1000000000.0
SCORE_SCALE = 0.125
SOFTMAX_TEMP = 50.0
LOSS_SCALE = 64.0
EPSILON = 1e-06
REACH = 32
QB = 64
WIN = QB + 2 * REACH
LANES = 128
GELU_A = 0.7978845608028654
GELU_B = 0.044715

BF16 = jnp.bfloat16
F32 = jnp.float32
HIGHEST = lax.Precision.HIGHEST


def dot(left, right, dims=((1,), (0,)), precision=None):
    return lax.dot_general(
        left, right, (dims, ((), ())), precision=precision, preferred_element_type=F32
    )


def dot_nt(left, right):
    return dot(left, right, ((1,), (1,)))


def dot_tn(left, right):
    return dot(left, right, ((0,), (0,)))


def rms_forward(value, gain):
    inverse = lax.rsqrt(jnp.mean(value * value, axis=-1, keepdims=True) + EPSILON)
    return (value * inverse * gain, inverse)


def cost(flops, bytes_accessed):
    return pl.CostEstimate(flops=0, bytes_accessed=0, transcendentals=0)


def params(mib=11):
    return pltpu.CompilerParams(vmem_limit_bytes=mib * 2**20)


def split_dot(left, right, dims=((1,), (0,))):
    high = right.astype(BF16)
    rest = (right - high.astype(F32)).astype(BF16)
    return dot(left, high, dims) + dot(left, rest, dims)


def stream_kernel(plan, operands, outs, body, *refs):
    sources, out_refs = refs[:operands], refs[operands : operands + outs]
    more = refs[operands + outs :]
    buffers, sem = more[: sum(len(load) > 1 for load in plan)], more[-1]
    more = more[len(buffers) : -1]
    copies, places, used = [], [], 0
    for load in plan:
        if len(load) == 1:
            which, _, row, count, col, width, _ = load[0]
            places.append(sources[which].at[pl.ds(row, count), pl.ds(col, width)])
            copies.append([])
            continue
        buffer = buffers[used]
        used += 1
        group = []
        for which, at, row, count, col, width, number in load:
            copy = pltpu.make_async_copy(
                sources[which].at[pl.ds(row, count), pl.ds(col, width)],
                buffer.at[pl.ds(at, count)],
                sem.at[number],
            )
            copy.start()
            group.append(copy)
        places.append(buffer)
        copies.append(group)
    ready = set()

    def get(i):
        if i not in ready:
            ready.add(i)
            for copy in copies[i]:
                copy.wait()
        return places[i]

    body(get, *out_refs, *more)


def stream(name, loads, out_shapes, body, scratch=(), mib=11):
    arrays, spaces = [], []

    def place(array, space):
        for i, known in enumerate(arrays):
            if known is array and spaces[i] is space:
                return i
        arrays.append(array)
        spaces.append(space)
        return len(arrays) - 1

    plan, buffers, number = [], [], 0
    for load in loads:
        steps, at = [], 0
        space = pltpu.VMEM if len(load) == 1 else pltpu.HBM
        for array, row, count, col, width in load:
            steps.append((place(array, space), at, row, count, col, width, number))
            at += count
            number += 1
        plan.append(steps)
        if len(load) > 1:
            buffers.append(pltpu.VMEM((at, load[0][4]), load[0][0].dtype))
    return pl.pallas_call(
        functools.partial(stream_kernel, plan, len(arrays), len(out_shapes), body),
        out_shape=tuple(out_shapes),
        in_specs=[pl.BlockSpec(memory_space=space) for space in spaces],
        out_specs=tuple(pl.BlockSpec(memory_space=pltpu.VMEM) for _ in out_shapes),
        scratch_shapes=buffers + list(scratch) + [pltpu.SemaphoreType.DMA((number,))],
        compiler_params=params(mib),
        cost_estimate=cost(0, 0),
        name=name,
    )(*arrays)


def part(array, col=0, width=None):
    return [(array, 0, array.shape[0], col, array.shape[1] - col if width is None else width)]


def weight(pieces, col, width):
    return [(*piece, col, width) for piece in pieces]


def wide(name, x, blocks, extras=(), body=None, outs=1):
    widths = [width for *_, width in blocks]
    loads = [part(x)]
    for i, block in enumerate(blocks):
        loads.append(weight(*block))
        for extra in extras:
            loads.append(part(extra, sum(widths[:i]), widths[i]))

    def run(get, *out_refs):
        at = 0
        per = 1 + len(extras)
        for i, width in enumerate(widths):
            first = 1 + i * per
            value = dot(get(0)[...], get(first)[...])
            got = [get(first + 1 + j)[...] for j in range(len(extras))]
            values = (value,) if body is None else body(value, *got)
            for ref, result in zip(out_refs, values):
                ref[:, at : at + width] = result.astype(BF16)
            at += width

    shape = shape_of(BF16, x.shape[0], sum(widths))
    result = stream(name, loads, (shape,) * outs, run)
    return result if outs > 1 else result[0]


def gelu_both(up):
    square = up * up
    bend = jnp.tanh(GELU_A * up * (1.0 + GELU_B * square))
    half_one = 0.5 + 0.5 * bend
    inner = GELU_A + (3.0 * GELU_A * GELU_B) * square
    return up * half_one, half_one + 0.5 * up * (1.0 - bend * bend) * inner


def gelu_only(up):
    bend = jnp.tanh(GELU_A * up * (1.0 + GELU_B * (up * up)))
    return up * (0.5 + 0.5 * bend), up


def times_slope(value, slope):
    return (value * slope.astype(F32),)


def times_slope_of(value, up):
    return (value * gelu_both(up.astype(F32))[1],)


def narrow(name, work, extras, out_shapes, body, scratch=(), mib=11):
    loads = []
    for x, x_col, pieces, col, width in work:
        loads += [part(x, x_col, width), weight(pieces, col, width)]
    first = len(loads)
    loads += [extra if isinstance(extra, list) else part(extra) for extra in extras]

    def run(get, *refs):
        out_refs, more = refs[: len(out_shapes)], refs[len(out_shapes) :]
        acc = more[0]
        for j in range(len(work)):
            value = dot_nt(get(2 * j)[...], get(2 * j + 1)[...])
            acc[...] = value if j == 0 else acc[...] + value
        body(acc, *(get(first + i) for i in range(len(extras))), *out_refs, *more[1:])

    depth = sum(count for *_, count in work[0][2])
    return stream(
        name, loads, out_shapes, run, [pltpu.VMEM((work[0][0].shape[0], depth), F32), *scratch], mib
    )


def gradients(name, left, first, count, rights, out_of=None):
    loads = [part(left, first, count)] + [part(right) for right in rights]

    def run(get, *refs):
        *out_refs, turned = refs
        turned[...] = get(0)[...].T
        for i, ref in enumerate(out_refs):
            ref[...] = dot(turned[...], get(1 + i)[...]).astype(BF16)

    shapes = [shape_of(BF16, count, right.shape[1]) for right in rights]
    return stream(name, loads, shapes, run, [pltpu.VMEM((count, left.shape[0]), BF16)])


def sent_columns(name, first, pairs):
    loads = [load for left, right in pairs for load in (part(left, first, first), part(right))]

    def run(get, out_ref, turned):
        at = 0
        for i, (_, right) in enumerate(pairs):
            turned[...] = get(2 * i)[...].T
            n = right.shape[1]
            out_ref[:, at : at + n] = dot(turned[...], get(2 * i + 1)[...]).astype(BF16)
            at += n

    shape = shape_of(BF16, first, sum(right.shape[1] for _, right in pairs))
    return stream(name, loads, (shape,), run, [pltpu.VMEM((first, pairs[0][0].shape[0]), BF16)])[0]


def stack_rows(pieces, widths):
    block = pieces[0].shape[0]
    cuts = [sum(widths[:i]) for i in range(len(widths))]
    if block % 16:
        whole = jnp.concatenate(pieces, axis=0)
        return [whole[:, at : at + width] for at, width in zip(cuts, widths)]

    def run(*refs):
        for i, ref in enumerate(refs[: len(pieces)]):
            for j, out in enumerate(refs[len(pieces) :]):
                out[i * block : (i + 1) * block] = ref[:, cuts[j] : cuts[j] + widths[j]]

    shapes = [shape_of(pieces[0].dtype, block * len(pieces), width) for width in widths]
    return whole_call(run, pieces, shapes, (), "stack_rows")


def qkv_call(inputs, first, n):
    blocks = [(side, i * n, n) for i in range(3) for side in first]
    loads = [part(inputs), weight(first[0], 3 * n, LANES)] + [weight(*block) for block in blocks]

    def run(get, qkv_ref, normed_ref, inverse_ref, gains_ref):
        value = get(0)[...]
        inverse = lax.rsqrt(jnp.mean(value * value, axis=1, keepdims=True) + EPSILON)
        inverse_ref[...] = inverse
        gains = get(1)[...].astype(F32).T[:8]
        gains_ref[...] = gains
        normed_ref[...] = (value * inverse * gains[0:1]).astype(BF16)
        for i in range(len(blocks)):
            qkv_ref[:, i * n : (i + 1) * n] = dot(normed_ref[...], get(2 + i)[...]).astype(BF16)

    seq, width = inputs.shape
    shapes = (
        shape_of(BF16, seq, 6 * n),
        shape_of(BF16, seq, width),
        shape_of(F32, seq, 1),
        shape_of(F32, 8, width),
    )
    return stream("qkv", loads, shapes, run)


def norm_body(row, acc, value_ref, gains_ref, hidden_ref, inverse_ref, normed_ref=None):
    hidden = value_ref[...] + acc[...]
    inverse = lax.rsqrt(jnp.mean(hidden * hidden, axis=1, keepdims=True) + EPSILON)
    hidden_ref[...] = hidden
    inverse_ref[...] = inverse
    if normed_ref is not None:
        normed_ref[...] = (hidden * inverse * gains_ref[row : row + 1, :]).astype(BF16)


def norm_back(value, inverse, gain, grad):
    scaled = grad * gain
    inner = jnp.mean(value * scaled, axis=1, keepdims=True)
    d_value = inverse * scaled - value * (inverse * inverse * inverse) * inner
    return d_value, jnp.sum(grad * value * inverse, axis=0, keepdims=True)


def back_body(row, acc, value_ref, inverse_ref, gains_ref, grad_ref, low_ref, gain_out, hidden_ref=None):
    d_value, d_gain = norm_back(
        value_ref[...], inverse_ref[...], gains_ref[row : row + 1, :], acc[...]
    )
    total = grad_ref[...] + d_value
    low_ref[...] = total.astype(BF16)
    gain_out[...] = d_gain
    if hidden_ref is not None:
        hidden_ref[...] = total


def turn_kernel(grad_ref, order_ref, out_ref):
    out_ref[...] = dot_nt(grad_ref[...], order_ref[...]).astype(BF16)


def small_kernel(heads_half, one_ref, two_ref, three_ref, order_ref, bias_ref, onehot_ref, loss_ref, mine_ref, out_ref):
    width = one_ref.shape[1]
    gains = jnp.concatenate([one_ref[...], two_ref[...], three_ref[...], jnp.zeros((5, width), F32)], axis=0)
    high = gains.astype(BF16)
    rest = (gains - high.astype(F32)).astype(BF16)
    gains = dot_nt(high, order_ref[...]) + dot_nt(rest, order_ref[...])
    out_ref[...] = jnp.zeros_like(out_ref)
    across = width // LANES
    for i in range(3):
        for j in range(across):
            at = i * across + j
            out_ref[at : at + 1, :] = gains[i : i + 1, j * LANES : (j + 1) * LANES]
    at = 3 * across
    lane = lax.broadcasted_iota(jnp.int32, (1, LANES), 1)
    out_ref[at : at + 1, :] = jnp.where(lane == 0, loss_ref[...], 0.0)
    bias = bias_ref[...]
    heads = 2 * heads_half
    row = lax.broadcasted_iota(jnp.int32, (LANES, bias.shape[0]), 0)
    column = lax.broadcasted_iota(jnp.int32, (LANES, bias.shape[0]), 1)
    source = row + jnp.where(mine_ref[...] == 0, 0, heads_half)
    source = jnp.where(source >= heads, source - heads, source)
    pick = jnp.where((column == 8 * (source // 2) + source % 2) & (row < heads), 1.0, 0.0)
    bias = split_dot(pick.astype(BF16), bias)
    high = bias.astype(BF16)
    rest = (bias - high.astype(F32)).astype(BF16)
    table = dot_nt(high, onehot_ref[...]) + dot_nt(rest, onehot_ref[...])
    count = table.shape[1]
    a_row = LANES // count
    for head in range(heads):
        place = head % a_row * count
        line = at + 1 + head // a_row
        out_ref[line : line + 1, place : place + count] = table[head : head + 1, :]


def member_of(seg_ref, sent_count):
    ids = lax.broadcasted_iota(jnp.int32, (sent_count, seg_ref.shape[1]), 0)
    hit = jnp.where(seg_ref[...] == ids, 1.0, 0.0)
    return hit.astype(BF16), jnp.sum(hit, axis=1, keepdims=True)


def tail_body(acc, value_ref, gains_ref, seg_ref, own_ref, other_ref, hidden_ref, inverse_ref, pooled_ref, unit_ref, low_ref, scale_ref, high, rest):
    hidden = value_ref[...] + acc[...]
    inverse = lax.rsqrt(jnp.mean(hidden * hidden, axis=1, keepdims=True) + EPSILON)
    hidden_ref[...] = hidden
    inverse_ref[...] = inverse
    final = hidden_ref[...] * inverse * gains_ref[2:3, :]
    high[...] = final.astype(BF16)
    rest[...] = (final - high[...].astype(F32)).astype(BF16)
    sents, count = member_of(seg_ref, pooled_ref.shape[0])
    pooled = ((dot(sents, high[...]) + dot(sents, rest[...])) / count).astype(BF16)
    pooled_ref[...] = pooled
    half = own_ref.shape[1]
    left = dot(pooled, own_ref[...])
    right = dot(pooled, other_ref[...])
    square = jnp.sum(left * left, axis=1, keepdims=True) + jnp.sum(right * right, axis=1, keepdims=True)
    scale = lax.rsqrt(square + EPSILON)
    scale_ref[...] = scale
    for at, value in ((0, left * scale), (half, right * scale)):
        unit_ref[:, at : at + half] = value
        low_ref[:, at : at + half] = value.astype(BF16)


def head_call(quarters, unit, scale, partner, column, sentence_loads, out_shapes):
    loads = [part(q) for q in (*quarters, unit, scale, partner, column)] + sentence_loads
    quarter = quarters[0].shape[0]
    total = 4 * quarter

    def run(get, loss_ref, embed_ref, *refs):
        *back_refs, every = refs
        for i in range(4):
            every[i * quarter : (i + 1) * quarter] = get(i)[...]
        unit, scale, partner, columns_id = (get(i)[...] for i in range(4, 8))
        partner = as_columns(
            jnp.concatenate([partner, jnp.zeros((1, LANES - partner.shape[1]), jnp.int32)], axis=1)
        )[: partner.shape[1], 0:1]
        own_count = unit.shape[0]
        sims = dot_nt(every[...], every[...]) * SOFTMAX_TEMP
        row = lax.broadcasted_iota(jnp.int32, (total, total), 0)
        column = lax.broadcasted_iota(jnp.int32, (total, total), 1)
        sims = jnp.where(row == column, NEG_FILL, sims)
        top = jnp.max(sims, axis=0, keepdims=True)
        lse_row = top + jnp.log(jnp.sum(jnp.exp(sims - top), axis=0, keepdims=True))
        own = sims[:own_count]
        own_top = jnp.max(own, axis=1, keepdims=True)
        own_lse = own_top + jnp.log(jnp.sum(jnp.exp(own - own_top), axis=1, keepdims=True))
        is_target = columns_id.astype(F32) == partner
        hit = jnp.where(is_target, 1.0, 0.0)
        target = jnp.sum(jnp.where(is_target, own, 0.0), axis=1, keepdims=True)
        loss_ref[...] = jnp.sum(own_lse - target, axis=0, keepdims=True)
        d_rows = (LOSS_SCALE * (jnp.exp(own - own_lse) - hit)).astype(BF16)
        d_cols = (LOSS_SCALE * (jnp.exp(own - lse_row) - hit)).astype(BF16)
        d_unit = SOFTMAX_TEMP * (dot(d_rows, every[...]) + dot(d_cols, every[...]))
        inner = jnp.sum(d_unit * unit, axis=1, keepdims=True)
        d_embed = (scale * (d_unit - unit * inner)).astype(BF16)
        embed_ref[...] = d_embed
        sentence_back(d_embed, [get(8 + i) for i in range(len(sentence_loads))], *back_refs)

    return stream("head", loads, out_shapes, run, [pltpu.VMEM((total, unit.shape[1]), BF16)])


def sentence_call(embed, sentence_loads, out_shapes):
    def run(get, *back_refs):
        sentence_back(get(0)[...], [get(1 + i) for i in range(len(sentence_loads))], *back_refs)

    return stream("sentence", [part(embed)] + sentence_loads, out_shapes, run)


def sentence_back(d_embed, sources, hidden_ref, low_ref, gain_out):
    seg_ref, own_ref, other_ref, value_ref, inverse_ref, gains_ref = sources
    half = own_ref.shape[1]
    d_pooled = dot_nt(d_embed[:, :half], own_ref[...]) + dot_nt(d_embed[:, half:], other_ref[...])
    sents, count = member_of(seg_ref, d_embed.shape[0])
    d_final = split_dot(sents, d_pooled / count, ((0,), (0,)))
    d_value, d_gain = norm_back(value_ref[...], inverse_ref[...], gains_ref[2:3, :], d_final)
    hidden_ref[...] = d_value
    low_ref[...] = d_value.astype(BF16)
    gain_out[...] = d_gain


def whole_call(body, args, out_shapes, scratch=(), name=None):
    return pl.pallas_call(
        body,
        out_shape=tuple(out_shapes),
        in_specs=[pl.BlockSpec(memory_space=pltpu.VMEM)] * len(args),
        out_specs=tuple(pl.BlockSpec(memory_space=pltpu.VMEM) for _ in out_shapes),
        scratch_shapes=scratch,
        compiler_params=params(),
        cost_estimate=cost(0, 0),
        name=name,
    )(*args)


def shape_of(kind, *dims):
    return jax.ShapeDtypeStruct(dims, kind)


def _stack_heads(part):
    lane = lax.broadcasted_iota(jnp.int32, part.shape, 1)
    zero = jnp.zeros_like(part)
    first = lane < LANES // 2
    return jnp.concatenate(
        [jnp.where(first, part, zero), jnp.where(first, zero, part)], axis=0
    )


def _unstack_heads(both):
    half = both.shape[0] // 2
    lane = lax.broadcasted_iota(jnp.int32, (half, LANES), 1)
    return jnp.where(lane < LANES // 2, both[:half], both[half:])


def _pad_keys(pad, ref):
    seq = ref.shape[0]
    pad[0:REACH] = jnp.zeros((REACH, LANES), pad.dtype)
    pad[REACH + seq :] = jnp.zeros((REACH, LANES), pad.dtype)
    pad[REACH : REACH + seq] = ref[...]


def _query_bits(shape):
    return lax.broadcasted_iota(jnp.int32, shape, 0) & (QB - 1)


def as_columns(values):
    count, length = values.shape
    side = max(LANES, length)
    square = jnp.concatenate([values.astype(F32), jnp.zeros((side - count, length), F32)], axis=0)
    return square.T


def attend_forward_kernel(
    q_ref, k_ref, v_ref, segq_ref, segk_ref, rel_ref, ctx_ref, probs_ref, kpad, vpad, mask, scores
):
    seq = q_ref.shape[0]
    blocks = seq // QB
    _pad_keys(kpad, k_ref)
    _pad_keys(vpad, v_ref)

    @pl.when(pl.program_id(0) == 0)
    def _():
        keys = as_columns(segk_ref[...])
        for b in range(blocks):
            same = keys[:, b : b + 1] == segq_ref[b : b + 1, :].astype(F32)
            mask[b] = jnp.where(same, 0.0, NEG_FILL)

    rel = rel_ref[0]
    row = lax.broadcasted_iota(jnp.int32, (2 * QB, WIN), 0)
    bias = jnp.where(row < QB, rel[0:1, :], rel[1:2, :])
    bits = _query_bits((2 * QB, WIN))
    step = 1
    while step < QB:
        bias = jnp.where((bits & step) != 0, pltpu.roll(bias, step, 1), bias)
        step *= 2
    bias = bias.T
    for b in range(blocks):
        query = _stack_heads(q_ref[b * QB : (b + 1) * QB] * jnp.asarray(SCORE_SCALE, BF16))
        scores[b] = dot_nt(kpad[b * QB : b * QB + WIN], query)
    values = scores[...] + bias[None] + mask[...]
    top = jnp.max(values, axis=1, keepdims=True)
    shifted = jnp.exp(values - top)
    total = jnp.sum(shifted, axis=1, keepdims=True)
    probs_ref[0] = (shifted * (1.0 / total)).astype(BF16)
    for b in range(blocks):
        part = dot_tn(probs_ref[0, b], vpad[b * QB : b * QB + WIN])
        ctx_ref[b * QB : (b + 1) * QB] = _unstack_heads(part).astype(BF16)


def attend_backward_kernel(
    q_ref, k_ref, v_ref, dctx_ref, probs_ref, dqkv_ref, dbias_ref,
    kpad, vpad, dk_acc, dv_acc, d_probs, d_low,
):
    seq = q_ref.shape[0]
    pair = pl.program_id(0)
    side = pl.num_programs(0) // 2
    later = pair // side
    q_at = pl.ds(pl.multiple_of(pair * LANES, LANES), LANES)
    k_at = pl.ds(pl.multiple_of((pair + 2 * side + later * side) * LANES, LANES), LANES)
    v_at = pl.ds(pl.multiple_of((pair + 3 * side + later * side) * LANES, LANES), LANES)
    blocks = seq // QB
    _pad_keys(kpad, k_ref)
    _pad_keys(vpad, v_ref)
    dk_acc[...] = jnp.zeros_like(dk_acc)
    dv_acc[...] = jnp.zeros_like(dv_acc)
    for b in range(blocks):
        window = slice(b * QB, b * QB + WIN)
        d_ctx = _stack_heads(dctx_ref[b * QB : (b + 1) * QB])
        d_probs[b] = dot_nt(vpad[window], d_ctx)
        dv_acc[window] += dot(probs_ref[0, b], d_ctx)
    probs = probs_ref[0].astype(F32)
    product = probs * d_probs[...]
    inner = jnp.sum(product, axis=1, keepdims=True)
    d_scores = product - probs * inner
    d_low[...] = d_scores.astype(BF16)
    total = jnp.sum(d_scores, axis=0).T
    for b in range(blocks):
        here = slice(b * QB, (b + 1) * QB)
        window = slice(b * QB, b * QB + WIN)
        query = _stack_heads(q_ref[here] * jnp.asarray(SCORE_SCALE, BF16))
        dk_acc[window] += dot(d_low[b], query)
        d_query = _unstack_heads(dot_tn(d_low[b], kpad[window])) * SCORE_SCALE
        dqkv_ref[here, q_at] = d_query.astype(BF16)
    dqkv_ref[:, k_at] = dk_acc[REACH : REACH + seq].astype(BF16)
    dqkv_ref[:, v_at] = dv_acc[REACH : REACH + seq].astype(BF16)
    bits = _query_bits((2 * QB, WIN))
    step = 1
    while step < QB:
        total = jnp.where((bits & step) != 0, pltpu.roll(total, WIN - step, 1), total)
        step *= 2
    first = jnp.sum(total[:QB], axis=0, keepdims=True)
    second = jnp.sum(total[QB:], axis=0, keepdims=True)
    dbias_ref[0] = jnp.concatenate([first, second, jnp.zeros((6, WIN), F32)], axis=0)


def _qkv_specs(seq, pairs):
    def spec(kind):
        return pl.BlockSpec((seq, LANES), lambda p: (0, kind * pairs + p))

    return [spec(0), spec(1), spec(2)]


def attend_forward(qkv, twice, windows, rel_window):
    seq = qkv.shape[0]
    pairs = rel_window.shape[0]
    blocks = seq // QB
    return pl.pallas_call(
        attend_forward_kernel,
        grid=(pairs,),
        out_shape=(
            jax.ShapeDtypeStruct((seq, pairs * LANES), BF16),
            jax.ShapeDtypeStruct((pairs, blocks, WIN, 2 * QB), BF16),
        ),
        in_specs=_qkv_specs(seq, pairs)
        + [
            pl.BlockSpec((blocks, 2 * QB), lambda p: (0, 0)),
            pl.BlockSpec((blocks, WIN), lambda p: (0, 0)),
            pl.BlockSpec((1, 2, WIN), lambda p: (p, 0, 0)),
        ],
        out_specs=(
            pl.BlockSpec((seq, LANES), lambda p: (0, p)),
            pl.BlockSpec((1, blocks, WIN, 2 * QB), lambda p: (p, 0, 0, 0)),
        ),
        scratch_shapes=[pltpu.VMEM((seq + 2 * REACH, LANES), BF16)] * 2
        + [pltpu.VMEM((blocks, WIN, 2 * QB), F32)] * 2,
        compiler_params=params(),
        cost_estimate=cost(8 * seq * WIN * LANES * pairs * 4, 8 * seq * LANES * pairs),
        name="attend_forward",
    )(qkv, qkv, qkv, twice, windows, rel_window)


def attend_backward(qkv, d_context, probs):
    seq = qkv.shape[0]
    pairs = probs.shape[0]
    blocks = seq // QB
    lane_block = pl.BlockSpec((seq, LANES), lambda p: (0, p))
    return pl.pallas_call(
        attend_backward_kernel,
        grid=(pairs,),
        out_shape=(
            jax.ShapeDtypeStruct((seq, 3 * pairs * LANES), BF16),
            jax.ShapeDtypeStruct((pairs, 8, WIN), F32),
        ),
        in_specs=_qkv_specs(seq, pairs)
        + [
            lane_block,
            pl.BlockSpec((1, blocks, WIN, 2 * QB), lambda p: (p, 0, 0, 0)),
        ],
        out_specs=(
            pl.BlockSpec((seq, 3 * pairs * LANES), lambda p: (0, 0)),
            pl.BlockSpec((1, 8, WIN), lambda p: (p, 0, 0)),
        ),
        scratch_shapes=[pltpu.VMEM((seq + 2 * REACH, LANES), BF16)] * 2
        + [pltpu.VMEM((seq + 2 * REACH, LANES), F32)] * 2
        + [pltpu.VMEM((blocks, WIN, 2 * QB), F32), pltpu.VMEM((blocks, WIN, 2 * QB), BF16)],
        compiler_params=params(),
        cost_estimate=cost(16 * seq * WIN * LANES * pairs * 4, 16 * seq * LANES * pairs),
        name="attend_backward",
    )(qkv, qkv, qkv, d_context, probs)


CORE = 1
CROSS = 2


def hop(value, mask):
    size = lax.axis_size("dp")
    return lax.ppermute(value, "dp", [(i, i ^ mask) for i in range(size)])


def over(value):
    return lax.ppermute(value, "mp", [(0, 1), (1, 0)])


def cross(value):
    return hop(value, CROSS)


def core(value):
    return hop(value, CORE)


def go(waits, *sends, keep=(), join=True):
    values = [value for _, value in sends]
    held = lax.optimization_barrier((*values, *keep, *waits))
    results = [how(value) for (how, _), value in zip(sends, held)]
    if join:
        results = list(lax.optimization_barrier(tuple(results)))
    return results + list(held[len(values) : len(values) + len(keep)])


def slot_masks(size):
    rest = size // 4
    return [z * 4 + x * 2 + c for c in range(2) for x in range(2) for z in range(rest)]


def strides(size):
    found = []
    stride = 4
    while stride < size:
        found.append(stride)
        stride *= 2
    return found


def gather_near(shard, waits, widths=None):
    size = lax.axis_size("dp")
    pieces = [shard]
    stride = 4
    while stride < size:
        radix = min(4, size // stride)
        shard = jnp.concatenate(pieces, axis=0) if len(pieces) > 1 else shard
        sends = [(functools.partial(hop, mask=j * stride), shard) for j in range(1, radix)]
        pieces = [shard] + go(waits, *sends)
        stride *= radix
    return jnp.concatenate(pieces, axis=0) if widths is None else stack_rows(pieces, widths)


def rows(*pieces):
    return jnp.concatenate(pieces, axis=0)


def columns(*pieces):
    return jnp.concatenate(pieces, axis=1)


def gather_weights(start, later, n_one, n_early, n_three, early, begin, between):
    size = lax.axis_size("dp")
    steps = strides(size)
    n_two = start.shape[1] - n_one
    n_four = later.shape[1] - n_three
    if len(steps) == 2:
        got = go((), *((functools.partial(hop, mask=4 * j), start) for j in range(1, 4)))
        more = hop(later, 4)
        one, two = stack_rows([start, *got], (n_one, n_two))
        later = stack_rows([later, more], (n_early, later.shape[1] - n_early))
        wide_step = functools.partial(hop, mask=steps[1])
    else:
        one, two = gather_near(start, (), (n_one, n_two))

        later = [later[:, :n_early], later[:, n_early:]]

        def wide_step(value):
            whole = gather_near(value, ())
            return whole[value.shape[0] :]

    one_x, two_y, more = go(early, (cross, one), (over, two), (wide_step, later[0]))
    (one,) = stack_rows([one, one_x], (n_one,))
    (two,) = stack_rows([two, two_y], (n_two,))
    one_y, two_x, one_c, two_c, more_b = go(
        (), (over, one), (cross, two), (core, one), (core, two), (wide_step, later[1])
    )
    if len(steps) == 2:
        have = later[0].shape[0]

        def put(near_a, near_b, far_a, far_b, three_ref, four_ref):
            for at, left, right in ((0, near_a, near_b), (have, far_a, far_b)):
                here = slice(at, at + have)
                three_ref[here, :n_early] = left[...]
                three_ref[here, n_early:] = right[:, : n_three - n_early]
                four_ref[here] = right[:, n_three - n_early :]

        three, four = whole_call(
            put,
            (*later, more, more_b),
            (shape_of(BF16, 2 * have, n_three), shape_of(BF16, 2 * have, n_four)),
            (),
            "put_rows",
        )
    else:
        later = rows(columns(*later), columns(more, more_b))
        three, four = later[:, :n_three], later[:, n_three:]
    three_x, four_y, one_yc, two_xc = go((), (cross, three), (over, four), (core, one_y), (core, two_x))
    (three,) = stack_rows([three, three_x], (n_three,))
    (four,) = stack_rows([four, four_y], (four.shape[1],))
    three_y, four_x, three_c, four_c, one, one_c, one_y, one_yc, two, two_x, two_c, two_xc, *early = go(
        (),
        (over, three),
        (cross, four),
        (core, three),
        (core, four),
        keep=(one, one_c, one_y, one_yc, two, two_x, two_c, two_xc, *early),
        join=False,
    )
    first, second = along_x(one, one_c, one_y, one_yc), along_y(two, two_x, two_c, two_xc)
    done = between(begin(first, early), second, early)
    four_xc, *done = go((three_y, four_x, three_c, four_c), (core, four_x), keep=done, join=False)
    (three_yc,) = go((four_xc,), (core, three_y), join=False)
    third, fourth = along_x(three, three_c, three_y, three_yc), along_y(four, four_x, four_c, four_xc)
    return first, second, third, fourth, early, done


def along_x(near, near_c, other, other_c):
    count = near.shape[0]
    return ((near, 0, count), (near_c, 0, count)), ((other, 0, count), (other_c, 0, count))


def along_y(near, side, near_c, side_c):
    count = near.shape[0] // 2
    return tuple(
        tuple((array, at, count) for array in (near, side, near_c, side_c)) for at in (0, count)
    )


def pack(name, sources, mib):
    widths = [count for *_, count in sources]
    block = sources[0][0].shape[0]

    def run(*refs):
        ins, out = refs[: len(sources)], refs[len(sources)]
        buffers, sem = refs[len(sources) + 1 : -1], refs[-1]
        copies = []
        for i, (_, first, count) in enumerate(sources):
            copy = pltpu.make_async_copy(ins[i].at[:, pl.ds(first, count)], buffers[i], sem.at[i])
            copy.start()
            copies.append(copy)
        at = 0
        for copy, buffer, width in zip(copies, buffers, widths):
            copy.wait()
            out[:, at : at + width] = buffer[...]
            at += width

    return pl.pallas_call(
        run,
        out_shape=shape_of(BF16, block, sum(widths)),
        in_specs=[pl.BlockSpec(memory_space=pltpu.HBM)] * len(sources),
        out_specs=pl.BlockSpec(memory_space=pltpu.VMEM),
        scratch_shapes=[pltpu.VMEM((block, width), BF16) for width in widths]
        + [pltpu.SemaphoreType.DMA((len(sources),))],
        compiler_params=params(mib),
        cost_estimate=cost(0, 0),
        name=name,
    )(*(array for array, *_ in sources))


def gather_dp(shard):
    near = gather_near(shard, ())
    side, c_near = go((near,), (cross, near), (core, near))
    return near, side, c_near, core(side)


def low(value):
    return value.astype(BF16)


def add(left, right):
    return (left.astype(F32) + right.astype(F32)).astype(BF16)


def product(left, begin, end, right, got=None):
    value = dot_tn(left[:, begin:end], right)
    if got is not None:
        value = value + got.astype(F32)
    return low(value)


def rest_start(value):
    half = value.shape[0] // 2
    return value[half:], value[:half]


def sum_half(value, send):
    gone, stays = rest_start(value)
    return stays + send(low(gone)).astype(F32)


def rest_hops(size):
    return [functools.partial(hop, mask=stride) for stride in reversed(strides(size))]


def shards(
    tokens,
    seg_ids,
    buckets,
    labels,
    w_query,
    w_key,
    w_value,
    w_out,
    w_in,
    w_back,
    gain_attn,
    gain_ffn,
    gain_final,
    w_pool,
    rel_table,
):
    micro_count, seq, width = tokens.shape
    size = lax.axis_size("dp")
    me = lax.axis_index("dp")
    mine = lax.axis_index("mp")
    block = width // size
    inner_half = w_query.shape[1]
    hidden_half = w_in.shape[1]
    sent_local = labels.shape[1]
    bucket_count = rel_table.shape[0]
    heads_half = rel_table.shape[1]
    masks = slot_masks(size)

    x_own = lax.dynamic_index_in_dim(tokens, mine, 0, keepdims=False)
    segments = lax.dynamic_index_in_dim(seg_ids, mine, 0, keepdims=False)[0]
    partner = lax.dynamic_index_in_dim(labels, mine, 0, keepdims=False)

    slot_block = jnp.stack([jnp.bitwise_xor(me, m) for m in masks]).astype(jnp.int32)
    source = (slot_block[:, None] * block + jnp.arange(block, dtype=jnp.int32)[None, :]).reshape(-1)
    order = (jnp.arange(width, dtype=jnp.int32)[:, None] == source[None, :]).astype(BF16)
    order = lax.optimization_barrier(order)
    inputs = dot(x_own, order)


    row_f32 = shape_of(F32, seq, width)
    row_low = shape_of(BF16, seq, width)
    column_f32 = shape_of(F32, seq, 1)
    gain_f32 = shape_of(F32, 1, width)
    heads = 3 * inner_half
    piece = hidden_half // 2
    halves = [(side, i * inner_half, inner_half) for side in range(2) for i in range(2)]

    def hidden_blocks(weights, first_col=0):
        return [(weights[side], first_col + col, n) for side, col, n in halves]

    def begin(first, early):
        inputs, rel_window, twice, windows, *_ = early
        qkv, normed1_low, inverse1, gains = qkv_call(inputs, first, inner_half)
        context, probs = attend_forward(qkv, twice, windows, rel_window)
        return qkv, normed1_low, inverse1, gains, context, probs

    def between(started, second, early):
        qkv, normed1_low, inverse1, gains, context, probs = started
        inputs = early[0]
        hidden1, inverse2, normed2_low = narrow(
            "attn_out",
            [(context, i * inner_half, second[i], piece, inner_half) for i in range(2)],
            (inputs, gains),
            (row_f32, column_f32, row_low),
            functools.partial(norm_body, 1),
        )
        act0, slope0 = wide("act0", normed2_low, hidden_blocks(second), (), gelu_both, 2)
        return normed1_low, inverse1, gains, qkv, context, probs, hidden1, inverse2, normed2_low, act0, slope0

    gains_col = jnp.pad(
        jnp.stack([gain_attn, gain_ffn, gain_final], axis=1), ((0, 0), (0, LANES - 3))
    )
    pool_half = w_pool.shape[1] // 2
    pool_own = lax.dynamic_slice_in_dim(w_pool, mine * pool_half, pool_half, axis=1)
    moved = piece // 3
    back_shard = w_back.T
    if block % 16:
        start = columns(w_query, w_key, w_value, gains_col, w_in[:, :piece], w_out.T)
        later = columns(
            back_shard[:, :piece],
            back_shard[:, hidden_half - moved :],
            pool_own,
            w_in[:, piece:],
            back_shard[:, piece : hidden_half - moved],
        )
    else:
        start = pack(
            "pack_start",
            [(w, 0, inner_half) for w in (w_query, w_key, w_value)]
            + [(gains_col, 0, LANES), (w_in, 0, piece), (w_out.T, 0, inner_half)],
            60,
        )
        back_shard, w_in, _ = lax.optimization_barrier((back_shard, w_in, start))
        later = pack(
            "pack_later",
            [
                (back_shard, 0, piece),
                (back_shard, hidden_half - moved, moved),
                (pool_own, 0, pool_half),
                (w_in, piece, piece),
                (back_shard, piece, piece - moved),
            ],
            16,
        )
    rel_other = over(lax.optimization_barrier((rel_table, start))[0])
    rel_all = jnp.concatenate([rel_table, rel_other], axis=1).astype(F32)
    near_buckets = lax.slice_in_dim(buckets, seq - 1 - REACH, seq - 1 - REACH + WIN)
    onehot = (near_buckets[None, :] == jnp.arange(bucket_count, dtype=jnp.int32)[:, None]).astype(F32)
    onehot = lax.optimization_barrier(low(onehot))
    rel_window = dot(rel_all, onehot.astype(F32), ((0,), (0,)), HIGHEST).reshape(heads_half, 2, WIN)
    padded = jnp.pad(segments, (REACH, REACH), constant_values=-1)
    windows = jnp.stack([padded[at : at + WIN] for at in range(0, seq, QB)])
    twice = jnp.tile(segments.reshape(seq // QB, QB), (1, 2))
    local_ids = jnp.arange(sent_local, dtype=jnp.int32)
    column_id = (slot_block[:, None] * sent_local + local_ids[None, :]).reshape(1, -1)
    early = (
        inputs, rel_window, twice, windows, order, onehot, column_id, partner[None, :], segments[None, :], mine.reshape(1, 1),
        (me * block).astype(jnp.uint32), (mine * heads_half).astype(jnp.uint32)
    )
    first, second, third, fourth, early, done = gather_weights(
        start,
        later,
        heads + LANES,
        piece,
        piece + moved + pool_half,
        early,
        begin,
        between,
    )
    inputs, rel_window, twice, windows, order, onehot, column_id, partner, seg_lane, mine_array, gain_at, table_at = early
    normed1_low, inverse1, gains, qkv, context, probs, hidden1, inverse2, normed2_low, act0, slope0 = done

    act1, up_kept = wide("act1", normed2_low, hidden_blocks(fourth), (), gelu_only, 2)
    pool_loads = [weight(side, piece + moved, pool_half) for side in third]
    hidden2, inverse3, pooled_low, unit, unit_low, scale = narrow(
        "ffn_out",
        [(act0, i * piece, third[i], 0, piece) for i in range(2)]
        + [(act1, i * piece, fourth[i], piece, piece - moved) for i in range(2)]
        + [(act1, (i + 1) * piece - moved, third[i], piece, moved) for i in range(2)],
        (hidden1, gains, seg_lane, *pool_loads),
        (
            row_f32,
            column_f32,
            shape_of(BF16, sent_local, width),
            shape_of(F32, sent_local, width),
            shape_of(BF16, sent_local, width),
            shape_of(F32, sent_local, 1),
        ),
        tail_body,
        [pltpu.VMEM((seq, width), BF16)] * 2,
    )
    quarters = gather_dp(unit_low)

    total_sent = column_id.shape[1]
    sentence_loads = [part(seg_lane), *pool_loads, part(hidden2), part(inverse3), part(gains)]
    back_shapes = (row_f32, row_low, gain_f32)
    if total_sent <= 1024:
        loss_local, embed_low, d_hidden2, ffn_low, d_gain3 = head_call(
            quarters,
            unit,
            scale,
            partner,
            column_id,
            sentence_loads,
            (shape_of(F32, 1, 1), shape_of(BF16, sent_local, width), *back_shapes),
        )
    else:
        every = rows(*quarters)
        position = jnp.arange(total_sent, dtype=jnp.int32)
        sims = dot_nt(every, every) * SOFTMAX_TEMP
        sims = jnp.where(position[:, None] == position[None, :], NEG_FILL, sims)
        lse_row = jax.nn.logsumexp(sims, axis=0, keepdims=True)
        own_sims = sims[:sent_local]
        own_lse = jax.nn.logsumexp(own_sims, axis=1, keepdims=True)
        is_target = column_id == partner.reshape(-1, 1)
        target = jnp.sum(jnp.where(is_target, own_sims, 0.0), axis=-1, keepdims=True)
        loss_local = jnp.sum(own_lse - target)
        hit = is_target.astype(F32)
        d_rows = low(LOSS_SCALE * (jnp.exp(own_sims - own_lse) - hit))
        d_cols = low(LOSS_SCALE * (jnp.exp(own_sims - lse_row) - hit))
        d_unit = SOFTMAX_TEMP * (dot(d_rows, every) + dot(d_cols, every))
        embed_low = low(scale * (d_unit - unit * jnp.sum(d_unit * unit, axis=-1, keepdims=True)))
        d_hidden2, ffn_low, d_gain3 = sentence_call(embed_low, sentence_loads, back_shapes)

    half = width // 2
    quarter = width // 4

    back0_sent, back1_sent = gradients("back_sent", ffn_low, half, half, (act0, act1))
    (pool_sent,) = gradients("pool_sent", pooled_low, half, half, (embed_low,))
    back0_got, back1_got, pool_got, ffn_later = go(
        (), (core, back0_sent), (core, back1_sent), (core, pool_sent), keep=(ffn_low,), join=False
    )
    pool_hi = product(pooled_low, quarter, half, embed_low, pool_got[quarter:])
    pool_lo = product(pooled_low, 0, quarter, embed_low, pool_got[:quarter])
    up0 = wide("up0", ffn_later, hidden_blocks(third), (slope0,), times_slope)

    back_hi = product(ffn_low, quarter, half, act0, back0_got[quarter:])
    back_lo = product(ffn_low, 0, quarter, act0, back0_got[:quarter])
    back_own = product(ffn_low, 0, half, act1[:, :piece], back1_got[:, :piece])
    back_oth = product(ffn_low, 0, half, act1[:, piece:], back1_got[:, piece:])
    got_lo, got_own, got_pool, ffn_later, up0, back_lo, back_own, pool_lo = go(
        (),
        (cross, back_hi),
        (over, back_oth),
        (cross, pool_hi),
        keep=(ffn_later, up0, back_lo, back_own, pool_lo),
    )
    back_blocks = [
        block
        for side in range(2)
        for block in (
            (fourth[side], piece, inner_half),
            (fourth[side], piece + inner_half, piece - moved - inner_half),
            (third[side], piece, moved),
        )
    ]
    up1 = wide("up1", ffn_later, back_blocks, (up_kept,), times_slope_of)
    in0_sent, in1_sent = gradients("in_sent", normed2_low, half, half, (up0, up1))
    in0_got, in1_got, up0, up1 = go((), (core, in0_sent), (core, in1_sent), keep=(up0, up1))
    attn_low, d_gain2, d_hidden1 = narrow(
        "ffn_in_back",
        [(up0, i * piece, second[i], 0, piece) for i in range(2)]
        + [(up1, i * piece, fourth[i], 0, piece) for i in range(2)],
        (hidden1, inverse2, gains, d_hidden2),
        (row_low, gain_f32, row_f32),
        functools.partial(back_body, 1),
    )
    d_context = wide("d_context", attn_low, [(second[side], piece, inner_half) for side in range(2)])

    pool_lo = add(pool_lo, got_pool)
    back_lo = add(back_lo, got_lo)
    back_own = add(back_own, got_own)
    in_hi = product(normed2_low, quarter, half, up0, in0_got[quarter:])
    in_lo = product(normed2_low, 0, quarter, up0, in0_got[:quarter])
    in_own = product(normed2_low, 0, half, up1[:, :piece], in1_got[:, :piece])
    in_oth = product(normed2_low, 0, half, up1[:, piece:], in1_got[:, piece:])
    got_first, got_x, got_in_own, d_context, pool_lo, back_lo, back_own, in_lo, in_own = go(
        (got_lo, got_own),
        (over, columns(back_lo[:, piece:], pool_lo[:, pool_half:])),
        (cross, columns(back_own[quarter:], in_hi)),
        (over, in_oth),
        keep=(d_context, pool_lo, back_lo, back_own, in_lo, in_own),
        join=False,
    )
    d_qkv, d_bias = attend_backward(qkv, d_context, probs)
    query_both = 2 * inner_half
    late_sent = sent_columns("late_sent", half, ((attn_low, context), (normed1_low, d_qkv)))
    late_got, d_qkv_later = go((), (core, late_sent), keep=(d_qkv,), join=False)
    grad_slots, d_gain1 = narrow(
        "qkv_back",
        [(d_qkv_later, i * inner_half, first[i], 0, inner_half) for i in range(2)]
        + [(d_qkv_later, (1 + i) * query_both, first[i], inner_half, query_both) for i in range(2)],
        (inputs, inverse1, gains, d_hidden1),
        (row_low, gain_f32),
        functools.partial(back_body, 0),
    )

    table_row = 3 * (width // LANES) + 1
    table_rows = -(-2 * heads_half * bucket_count // LANES)
    small_rows = -(-(table_row + table_rows) // 8) * 8
    (flat,) = whole_call(
        functools.partial(small_kernel, heads_half),
        (d_gain1, d_gain2, d_gain3, order, d_bias.reshape(-1, WIN), onehot, loss_local.reshape(1, 1), mine_array),
        (shape_of(F32, small_rows, LANES),),
        (),
        "small",
    )
    (grad_own,) = whole_call(turn_kernel, (grad_slots, order), (row_low,), (), "turn")
    flat_got, flat = go((), (over, flat), keep=(flat,), join=False)
    got_first, got_x, got_in_own = lax.optimization_barrier((got_first, got_x, got_in_own))
    flat = flat + flat_got
    got_second, got_in_lo = got_x[:, :piece], got_x[:, piece:]

    far = rest_hops(size)
    back_all = columns(
        add(back_lo[:, :piece], got_first[:, :piece]),
        add(back_own[:quarter], got_second),
        add(pool_lo[:, :pool_half], got_first[:, piece:]),
    )
    back_rest, back_stay = rest_start(back_all)
    in_lo = add(in_lo, got_in_lo)
    in_own = add(in_own, got_in_own)
    out_got, qkv_got = late_got[:, :query_both], late_got[:, query_both:]
    out_hi = product(attn_low, quarter, half, context, out_got[quarter:])
    out_lo = product(attn_low, 0, quarter, context, out_got[:quarter])
    query_hi = product(normed1_low, quarter, half, d_qkv[:, :query_both], qkv_got[quarter:, :query_both])
    query_lo = product(normed1_low, 0, quarter, d_qkv[:, :query_both], qkv_got[:quarter, :query_both])
    kv_own = product(
        normed1_low, 0, half, d_qkv[:, query_both : 2 * query_both], qkv_got[:, query_both : 2 * query_both]
    )
    kv_oth = product(normed1_low, 0, half, d_qkv[:, 2 * query_both :], qkv_got[:, 2 * query_both :])
    rest_hop = [functools.partial(hop, mask=j * 4) for j in range(1, min(4, size // 4))]
    back_more, got_first, got_x, got_kv, flat_got, back_stay, in_lo, in_own, out_lo, query_lo, kv_own, flat = go(
        (grad_own,),
        (far[0], back_rest),
        (over, in_lo[:, piece:]),
        (cross, columns(in_own[quarter:], out_hi, query_hi)),
        (over, kv_oth),
        (core, flat),
        keep=(back_stay, in_lo, in_own, out_lo, query_lo, kv_own, flat),
    )

    count = flat.shape[0]

    def in_two(value):
        high = value.astype(BF16).astype(F32)
        return jnp.concatenate([high, value - high], axis=0).astype(BF16)

    def from_two(pair):
        return pair[:count].astype(F32) + pair[count : 2 * count].astype(F32)

    def late_adds(
        stay, more, in_lo, got_first, in_own, got_x, out_lo, query_lo, kv_own, got_kv, flat, got_flat, *outs
    ):
        back_gone, back_keep, in_gone, in_keep, heads_gone, heads_keep, kv_gone, kv_keep, small = outs
        rows_z = stay.shape[0] // 2
        total = add(stay[...], more[...])
        back_keep[...] = total[:rows_z]
        back_gone[...] = total[rows_z:]
        rows_z = in_lo.shape[0] // 2
        for at, total in (
            (0, add(in_lo[:, :piece], got_first[...])),
            (piece, add(in_own[:quarter], got_x[:, :piece])),
        ):
            in_keep[:, at : at + piece] = total[:rows_z]
            in_gone[:, at : at + piece] = total[rows_z:]
        for i, ref in enumerate((out_lo, query_lo)):
            first_col = piece + i * query_both
            total = add(ref[...], got_x[:, first_col : first_col + query_both])
            heads_keep[:, i * inner_half : (i + 1) * inner_half] = total[:, :inner_half]
            heads_gone[:, i * inner_half : (i + 1) * inner_half] = total[:, inner_half:]
        kv_keep[...] = add(kv_own[:quarter], got_kv[:quarter])
        kv_gone[:, :query_both] = add(kv_own[quarter:], got_kv[quarter:])
        small[...] = flat[...] + got_flat[...]
        kv_gone[:, query_both:] = jnp.zeros((quarter, LANES), BF16)
        pair = in_two(small[...])
        kv_gone[: 2 * count, query_both:] = pair
        small[...] = from_two(pair)

    cut = [shape_of(BF16, back_stay.shape[0] // 2, back_stay.shape[1])] * 2
    cut += [shape_of(BF16, quarter // 2, hidden_half)] * 2 + [shape_of(BF16, quarter, query_both)] * 2
    cut += [
        shape_of(BF16, quarter, query_both + LANES),
        shape_of(BF16, quarter, query_both),
        shape_of(F32, count, LANES),
    ]
    back_rest, back_stay, in_rest, in_stay, heads_gone, heads_keep, kv_gone, kv_keep, flat = whole_call(
        late_adds,
        (back_stay, back_more, in_lo, got_first, in_own, got_x, out_lo, query_lo, kv_own, got_kv, flat, flat_got),
        cut,
        (),
        "late_adds",
    )
    early_rows = seq * 11 // 32
    back_more, in_more, got_first, got_second, grad_other, back_stay, in_stay, heads_keep, kv_keep, flat = go(
        (),
        (far[1], back_rest),
        (far[0], in_rest),
        (over, heads_gone),
        (cross, kv_gone),
        (over, grad_own[:early_rows]),
        keep=(back_stay, in_stay, heads_keep, kv_keep, flat),
    )

    def finish(value):
        value = value.astype(F32)
        for send in far[2:]:
            value = sum_half(value, send)
        return value

    n_last = query_both + query_both
    if len(far) == 2:
        rest = block
        late_rows = seq - early_rows

        def last_adds(stay, more, heads_ref, got_heads, kv_ref, got_kv, flat_ref, back_ref, back_got, own_ref, *outs):
            one, two, three, in_keep, keep, flat_out, tail, pool_ref = outs
            pool = add(back_ref[:, hidden_half:], back_got[:, hidden_half:])
            pool_ref[...] = pool
            tail[:late_rows] = own_ref[early_rows:]
            tail[late_rows:, :pool_half] = pool
            tail[late_rows:, pool_half:] = jnp.zeros((rest, width - pool_half), BF16)
            total = add(stay[...], more[...])
            in_keep[...] = total[:rest]
            one[:, LANES : LANES + hidden_half] = total[rest:]
            pair = in_two(flat_ref[...] + from_two(got_kv[:, query_both:]))
            flat_out[...] = from_two(pair)
            for i, (ref, at) in enumerate(((keep, 0), (one, LANES + hidden_half), (two, LANES), (three, LANES))):
                here = slice(i * rest, (i + 1) * rest)
                if i:
                    ref[:, :LANES] = pair
                ref[:, at : at + query_both] = add(heads_ref[here], got_heads[here])
                ref[:, at + query_both : at + n_last] = add(kv_ref[here], got_kv[here, :query_both])

        one, two, three, in_stay, last_stay, flat, tail, grad_pool = whole_call(
            last_adds,
            (in_stay, in_more, heads_keep, got_first, kv_keep, got_second, flat, back_stay, back_more, grad_own),
            (
                shape_of(BF16, rest, LANES + hidden_half + n_last),
                shape_of(BF16, rest, LANES + n_last),
                shape_of(BF16, rest, LANES + n_last),
                shape_of(BF16, rest, hidden_half),
                shape_of(BF16, rest, n_last),
                shape_of(F32, count, LANES),
                shape_of(BF16, late_rows + rest, width),
                shape_of(BF16, rest, pool_half),
            ),
            (),
            "last_adds",
        )
        got_one, got_two, got_three, got_tail, back_stay, back_more = go(
            (),
            (rest_hop[0], one),
            (rest_hop[1], two),
            (rest_hop[2], three),
            (over, tail),
            keep=(back_stay, back_more),
            join=False,
        )

        def back_final(stay, more, back_ref):
            back_ref[...] = stay[:, :hidden_half].astype(F32) + more[:, :hidden_half].astype(F32)

        (grad_back,) = whole_call(
            back_final, (back_stay, back_more), (shape_of(F32, rest, hidden_half),), (), "back_final"
        )

        def tokens_final(mine_ref, own_ref, first_ref, tail_ref, pool_own, out_ref, pool_ref):
            first = mine_ref[...] == 0
            own, other = pool_own[...].astype(F32), tail_ref[late_rows:, :pool_half].astype(F32)
            pool_ref[:, :pool_half] = jnp.where(first, own, other)
            pool_ref[:, pool_half:] = jnp.where(first, other, own)
            for at, count, ref in ((0, early_rows, first_ref), (early_rows, late_rows, tail_ref)):
                here = slice(at, at + count)
                own, other = own_ref[here].astype(F32), ref[:count].astype(F32)
                out_ref[0, here] = jnp.where(first, own, other).astype(BF16)
                out_ref[1, here] = jnp.where(first, other, own).astype(BF16)

        grad_tokens, grad_pool = whole_call(
            tokens_final,
            (mine_array, grad_own, grad_other, got_tail, grad_pool),
            (shape_of(BF16, 2, seq, width), shape_of(F32, rest, 2 * pool_half)),
            (),
            "tokens_final",
        )
        got_one, got_two, got_three, grad_tokens = lax.optimization_barrier(
            (got_one, got_two, got_three, grad_tokens)
        )

        def last_final(
            stay, in_keep, one_ref, two_ref, three_ref, flat_ref, order_ref, mine_ref, *outs
        ):
            in_ref, out_ref, q_ref, k_ref, v_ref, loss_ref, gains_ref, table_ref, wide_ref = outs
            in_ref[...] = in_keep[...].astype(F32) + one_ref[:, LANES : LANES + hidden_half].astype(F32)
            total = stay[...].astype(F32) + one_ref[:, LANES + hidden_half :].astype(F32)
            total = total + two_ref[:, LANES:].astype(F32) + three_ref[:, LANES:].astype(F32)
            for i, ref in enumerate((out_ref, q_ref, k_ref, v_ref)):
                ref[...] = total[:, i * inner_half : (i + 1) * inner_half]
            small = flat_ref[...]
            for ref in (one_ref, two_ref, three_ref):
                small = small + from_two(ref[:, :LANES])
            across = width // LANES
            loss_ref[...] = small[3 * across : 3 * across + 1, :1] / (micro_count * sent_local * size)
            wide_ref[...] = jnp.zeros_like(wide_ref)
            for i in range(3):
                for j in range(across):
                    wide_ref[i : i + 1, j * LANES : (j + 1) * LANES] = small[i * across + j : i * across + j + 1]
            high = wide_ref[...].astype(BF16)
            low_part = (wide_ref[...] - high.astype(F32)).astype(BF16)
            pick = order_ref[:, :LANES]
            gains_ref[...] = dot(high, pick) + dot(low_part, pick)
            a_row = LANES // bucket_count
            heads_list = []
            for head in range(2 * heads_half):
                line = table_row + head // a_row
                place = head % a_row * bucket_count
                heads_list.append(small[line : line + 1, place : place + bucket_count])
            first = jnp.concatenate(heads_list[:heads_half], axis=0)
            second = jnp.concatenate(heads_list[heads_half:], axis=0)
            table_ref[...] = jnp.where(mine_ref[...] == 0, first, second)

        head_shape = shape_of(F32, rest, inner_half)
        grad_in, grad_out, grad_query, grad_key, grad_value, loss, gains_mine, table_mine = whole_call(
            last_final,
            (last_stay, in_stay, got_one, got_two, got_three, flat, order, mine_array),
            (
                shape_of(F32, rest, hidden_half),
                *(head_shape,) * 4,
                shape_of(F32, 1, 1),
                shape_of(F32, 8, LANES),
                shape_of(F32, heads_half, bucket_count),
            ),
            [pltpu.VMEM((8, width), F32)],
            "last_final",
        )
        loss = loss.reshape(())
        gains_mine = gains_mine[:3, :block]
        table_mine = table_mine.T
    else:
        flat = flat + from_two(got_second[:, query_both:])
        grad_other = rows(grad_other, over(grad_own[early_rows:]))
        in_rest, in_stay = rest_start(add(in_stay, in_more))
        last = columns(add(heads_keep, got_first), add(kv_keep, got_second[:, :query_both]))
        last_rest, last_stay = rest_start(last)
        in_more, last_more, *flat_got = go(
            (), (far[1], in_rest), (far[0], last_rest), *((how, flat) for how in rest_hop)
        )
        last_rest, last_stay = rest_start(add(last_stay, last_more))
        last_more = far[1](last_rest)
        flat = flat + sum(flat_got)
        for send in far[:-2]:
            flat = flat + send(flat)
        grad_last = finish(last_stay.astype(F32) + last_more.astype(F32))
        grad_in = finish(in_stay.astype(F32) + in_more.astype(F32))
        back_all = finish(back_stay.astype(F32) + back_more.astype(F32))
        grad_back, grad_pool = back_all[:, :hidden_half], back_all[:, hidden_half:]
        pool_other = over(grad_pool)
        grad_pool = jnp.where(mine == 0, columns(grad_pool, pool_other), columns(pool_other, grad_pool))
        grad_out, grad_query, grad_key, grad_value = (
            grad_last[:, i * inner_half : (i + 1) * inner_half] for i in range(4)
        )
        grad_tokens = jnp.where(
            mine == 0, jnp.stack([grad_own, grad_other]), jnp.stack([grad_other, grad_own])
        )
        across = width // LANES
        zero = jnp.uint32(0)
        gains_mine = lax.dynamic_slice(flat[: 3 * across].reshape(3, width), (zero, gain_at), (3, block))
        loss = flat[3 * across, 0] / (micro_count * sent_local * size)
        table_sum = flat[table_row : table_row + table_rows].reshape(-1, bucket_count)[: 2 * heads_half]
        table_mine = lax.dynamic_slice(table_sum, (table_at, zero), (heads_half, bucket_count)).T
    return (
        loss,
        grad_tokens,
        grad_query,
        grad_key,
        grad_value,
        grad_out.T,
        grad_in,
        grad_back.T,
        gains_mine[0],
        gains_mine[1],
        gains_mine[2],
        grad_pool,
        table_mine,
    )


def solution(mesh):
    placed = (
        P(None, "dp", None),
        P(None, "dp", None),
        P(),
        P(None, "dp"),
        P("dp", "mp"),
        P("dp", "mp"),
        P("dp", "mp"),
        P("mp", "dp"),
        P("dp", "mp"),
        P("mp", "dp"),
        P("dp"),
        P("dp"),
        P("dp"),
        P("dp", None),
        P(None, "mp"),
    )
    return jax.shard_map(
        shards,
        mesh=mesh,
        in_specs=placed,
        out_specs=(
            P(),
            P(None, "dp", None),
            P("dp", "mp"),
            P("dp", "mp"),
            P("dp", "mp"),
            P("mp", "dp"),
            P("dp", "mp"),
            P("mp", "dp"),
            P("dp"),
            P("dp"),
            P("dp"),
            P("dp", None),
            P(None, "mp"),
        ),
        check_vma=False,
    )
```

```python
import functools

import jax
import jax.numpy as jnp
from jax import lax
from jax.experimental import pallas as pl
from jax.experimental.pallas import tpu as pltpu
from jax.sharding import PartitionSpec as P

NEG_FILL = -1000000000.0
SCORE_SCALE = 0.125
SOFTMAX_TEMP = 50.0
LOSS_SCALE = 64.0
EPSILON = 1e-06
REACH = 32
QB = 64
WIN = QB + 2 * REACH
LANES = 128
GELU_A = 0.7978845608028654
GELU_B = 0.044715

BF16 = jnp.bfloat16
F32 = jnp.float32
HIGHEST = lax.Precision.HIGHEST


def dot(left, right, dims=((1,), (0,)), precision=None):
    return lax.dot_general(
        left, right, (dims, ((), ())), precision=precision, preferred_element_type=F32
    )


def dot_nt(left, right):
    return dot(left, right, ((1,), (1,)))


def dot_tn(left, right):
    return dot(left, right, ((0,), (0,)))


def rms_forward(value, gain):
    inverse = lax.rsqrt(jnp.mean(value * value, axis=-1, keepdims=True) + EPSILON)
    return (value * inverse * gain, inverse)


def cost(flops, bytes_accessed):
    return pl.CostEstimate(flops=0, bytes_accessed=0, transcendentals=0)


def params(mib=16):
    return pltpu.CompilerParams(vmem_limit_bytes=mib * 2**20)


def split_dot(left, right, dims=((1,), (0,))):
    high = right.astype(BF16)
    rest = (right - high.astype(F32)).astype(BF16)
    return dot(left, high, dims) + dot(left, rest, dims)


def stream_kernel(plan, operands, outs, body, *refs):
    sources, out_refs = refs[:operands], refs[operands : operands + outs]
    more = refs[operands + outs :]
    buffers, sem = more[: sum(len(load) > 1 for load in plan)], more[-1]
    more = more[len(buffers) : -1]
    copies, places, used = [], [], 0
    for load in plan:
        if len(load) == 1:
            which, _, row, count, col, width, _ = load[0]
            places.append(sources[which].at[pl.ds(row, count), pl.ds(col, width)])
            copies.append([])
            continue
        buffer = buffers[used]
        used += 1
        group = []
        for which, at, row, count, col, width, number in load:
            copy = pltpu.make_async_copy(
                sources[which].at[pl.ds(row, count), pl.ds(col, width)],
                buffer.at[pl.ds(at, count)],
                sem.at[number],
            )
            copy.start()
            group.append(copy)
        places.append(buffer)
        copies.append(group)
    ready = set()

    def get(i):
        if i not in ready:
            ready.add(i)
            for copy in copies[i]:
                copy.wait()
        return places[i]

    body(get, *out_refs, *more)


def stream(name, loads, out_shapes, body, scratch=(), mib=16):
    arrays, spaces = [], []

    def place(array, space):
        for i, known in enumerate(arrays):
            if known is array and spaces[i] is space:
                return i
        arrays.append(array)
        spaces.append(space)
        return len(arrays) - 1

    plan, buffers, number = [], [], 0
    for load in loads:
        steps, at = [], 0
        space = pltpu.VMEM if len(load) == 1 else pltpu.HBM
        for array, row, count, col, width in load:
            steps.append((place(array, space), at, row, count, col, width, number))
            at += count
            number += 1
        plan.append(steps)
        if len(load) > 1:
            buffers.append(pltpu.VMEM((at, load[0][4]), load[0][0].dtype))
    return pl.pallas_call(
        functools.partial(stream_kernel, plan, len(arrays), len(out_shapes), body),
        out_shape=tuple(out_shapes),
        in_specs=[pl.BlockSpec(memory_space=space) for space in spaces],
        out_specs=tuple(pl.BlockSpec(memory_space=pltpu.VMEM) for _ in out_shapes),
        scratch_shapes=buffers + list(scratch) + [pltpu.SemaphoreType.DMA((number,))],
        compiler_params=params(mib),
        cost_estimate=cost(0, 0),
        name=name,
    )(*arrays)


def part(array, col=0, width=None):
    return [(array, 0, array.shape[0], col, array.shape[1] - col if width is None else width)]


def weight(pieces, col, width):
    return [(*piece, col, width) for piece in pieces]


def wide(name, x, blocks, extras=(), body=None, outs=1):
    widths = [width for *_, width in blocks]
    loads = [part(x)]
    for i, block in enumerate(blocks):
        loads.append(weight(*block))
        for extra in extras:
            loads.append(part(extra, sum(widths[:i]), widths[i]))

    def run(get, *out_refs):
        at = 0
        per = 1 + len(extras)
        for i, width in enumerate(widths):
            first = 1 + i * per
            value = dot(get(0)[...], get(first)[...])
            got = [get(first + 1 + j)[...] for j in range(len(extras))]
            values = (value,) if body is None else body(value, *got)
            for ref, result in zip(out_refs, values):
                ref[:, at : at + width] = result.astype(BF16)
            at += width

    shape = shape_of(BF16, x.shape[0], sum(widths))
    result = stream(name, loads, (shape,) * outs, run)
    return result if outs > 1 else result[0]


def gelu_both(up):
    square = up * up
    bend = jnp.tanh(GELU_A * up * (1.0 + GELU_B * square))
    half_one = 0.5 + 0.5 * bend
    inner = GELU_A + (3.0 * GELU_A * GELU_B) * square
    return up * half_one, half_one + 0.5 * up * (1.0 - bend * bend) * inner


def gelu_only(up):
    bend = jnp.tanh(GELU_A * up * (1.0 + GELU_B * (up * up)))
    return up * (0.5 + 0.5 * bend), up


def times_slope(value, slope):
    return (value * slope.astype(F32),)


def times_slope_of(value, up):
    return (value * gelu_both(up.astype(F32))[1],)


def narrow(name, work, extras, out_shapes, body, scratch=(), mib=16):
    loads = []
    for x, x_col, pieces, col, width in work:
        loads += [part(x, x_col, width), weight(pieces, col, width)]
    first = len(loads)
    loads += [extra if isinstance(extra, list) else part(extra) for extra in extras]

    def run(get, *refs):
        out_refs, more = refs[: len(out_shapes)], refs[len(out_shapes) :]
        acc = more[0]
        for j in range(0, len(work), 2):
            value = sum(dot_nt(get(2 * k)[...], get(2 * k + 1)[...]) for k in (j, j + 1))
            acc[...] = value if j == 0 else acc[...] + value
        body(acc, *(get(first + i) for i in range(len(extras))), *out_refs, *more[1:])

    depth = sum(count for *_, count in work[0][2])
    return stream(
        name, loads, out_shapes, run, [pltpu.VMEM((work[0][0].shape[0], depth), F32), *scratch], mib
    )


def gradients(name, left, first, count, rights, out_of=None):
    loads = [part(left, first, count)] + [part(right) for right in rights]

    def run(get, *refs):
        *out_refs, turned = refs
        turned[...] = get(0)[...].T
        for i, ref in enumerate(out_refs):
            ref[...] = dot(turned[...], get(1 + i)[...]).astype(BF16)

    shapes = [shape_of(BF16, count, right.shape[1]) for right in rights]
    return stream(name, loads, shapes, run, [pltpu.VMEM((count, left.shape[0]), BF16)])


def sent_columns(name, first, pairs):
    loads = [load for left, right in pairs for load in (part(left, first, first), part(right))]

    def run(get, out_ref, turned):
        at = 0
        for i, (_, right) in enumerate(pairs):
            turned[...] = get(2 * i)[...].T
            n = right.shape[1]
            out_ref[:, at : at + n] = dot(turned[...], get(2 * i + 1)[...]).astype(BF16)
            at += n

    shape = shape_of(BF16, first, sum(right.shape[1] for _, right in pairs))
    return stream(name, loads, (shape,), run, [pltpu.VMEM((first, pairs[0][0].shape[0]), BF16)])[0]


def stack_rows(pieces, widths):
    block = pieces[0].shape[0]
    cuts = [sum(widths[:i]) for i in range(len(widths))]
    if block % 16:
        whole = jnp.concatenate(pieces, axis=0)
        return [whole[:, at : at + width] for at, width in zip(cuts, widths)]

    def run(*refs):
        for i, ref in enumerate(refs[: len(pieces)]):
            for j, out in enumerate(refs[len(pieces) :]):
                out[i * block : (i + 1) * block] = ref[:, cuts[j] : cuts[j] + widths[j]]

    shapes = [shape_of(pieces[0].dtype, block * len(pieces), width) for width in widths]
    return whole_call(run, pieces, shapes, (), "stack_rows")


def qkv_call(inputs, first, n):
    blocks = [(side, i * n, n) for i in range(3) for side in first]
    loads = [part(inputs), weight(first[0], 3 * n, LANES)] + [weight(*block) for block in blocks]

    def run(get, qkv_ref, normed_ref, inverse_ref, gains_ref):
        value = get(0)[...]
        inverse = lax.rsqrt(jnp.mean(value * value, axis=1, keepdims=True) + EPSILON)
        inverse_ref[...] = inverse
        gains = get(1)[...].astype(F32).T[:8]
        gains_ref[...] = gains
        normed_ref[...] = (value * inverse * gains[0:1]).astype(BF16)
        for i in range(len(blocks)):
            qkv_ref[:, i * n : (i + 1) * n] = dot(normed_ref[...], get(2 + i)[...]).astype(BF16)

    seq, width = inputs.shape
    shapes = (
        shape_of(BF16, seq, 6 * n),
        shape_of(BF16, seq, width),
        shape_of(F32, seq, 1),
        shape_of(F32, 8, width),
    )
    return stream("qkv", loads, shapes, run)


def norm_body(row, acc, value_ref, gains_ref, hidden_ref, inverse_ref, normed_ref=None):
    hidden = value_ref[...] + acc[...]
    inverse = lax.rsqrt(jnp.mean(hidden * hidden, axis=1, keepdims=True) + EPSILON)
    hidden_ref[...] = hidden
    inverse_ref[...] = inverse
    if normed_ref is not None:
        normed_ref[...] = (hidden * inverse * gains_ref[row : row + 1, :]).astype(BF16)


def norm_back(value, inverse, gain, grad):
    scaled = grad * gain
    inner = jnp.mean(value * scaled, axis=1, keepdims=True)
    d_value = inverse * scaled - value * (inverse * inverse * inverse) * inner
    return d_value, jnp.sum(grad * value * inverse, axis=0, keepdims=True)


def back_body(row, acc, value_ref, inverse_ref, gains_ref, grad_ref, low_ref, gain_out, hidden_ref=None):
    d_value, d_gain = norm_back(
        value_ref[...], inverse_ref[...], gains_ref[row : row + 1, :], acc[...]
    )
    total = grad_ref[...] + d_value
    low_ref[...] = total.astype(BF16)
    gain_out[...] = d_gain
    if hidden_ref is not None:
        hidden_ref[...] = total


def turn_kernel(grad_ref, order_ref, out_ref):
    out_ref[...] = dot_nt(grad_ref[...], order_ref[...]).astype(BF16)


def small_kernel(heads_half, one_ref, two_ref, three_ref, order_ref, bias_ref, onehot_ref, loss_ref, mine_ref, out_ref):
    width = one_ref.shape[1]
    gains = jnp.concatenate([one_ref[...], two_ref[...], three_ref[...], jnp.zeros((5, width), F32)], axis=0)
    high = gains.astype(BF16)
    rest = (gains - high.astype(F32)).astype(BF16)
    gains = dot_nt(high, order_ref[...]) + dot_nt(rest, order_ref[...])
    out_ref[...] = jnp.zeros_like(out_ref)
    across = width // LANES
    for i in range(3):
        for j in range(across):
            at = i * across + j
            out_ref[at : at + 1, :] = gains[i : i + 1, j * LANES : (j + 1) * LANES]
    at = 3 * across
    lane = lax.broadcasted_iota(jnp.int32, (1, LANES), 1)
    out_ref[at : at + 1, :] = jnp.where(lane == 0, loss_ref[...], 0.0)
    bias = bias_ref[...]
    heads = 2 * heads_half
    row = lax.broadcasted_iota(jnp.int32, (LANES, bias.shape[0]), 0)
    column = lax.broadcasted_iota(jnp.int32, (LANES, bias.shape[0]), 1)
    source = row + jnp.where(mine_ref[...] == 0, 0, heads_half)
    source = jnp.where(source >= heads, source - heads, source)
    pick = jnp.where((column == 8 * (source // 2) + source % 2) & (row < heads), 1.0, 0.0)
    bias = split_dot(pick.astype(BF16), bias)
    high = bias.astype(BF16)
    rest = (bias - high.astype(F32)).astype(BF16)
    table = dot_nt(high, onehot_ref[...]) + dot_nt(rest, onehot_ref[...])
    count = table.shape[1]
    a_row = LANES // count
    for head in range(heads):
        place = head % a_row * count
        line = at + 1 + head // a_row
        out_ref[line : line + 1, place : place + count] = table[head : head + 1, :]


def member_of(seg_ref, sent_count):
    ids = lax.broadcasted_iota(jnp.int32, (sent_count, seg_ref.shape[1]), 0)
    hit = jnp.where(seg_ref[...] == ids, 1.0, 0.0)
    return hit.astype(BF16), jnp.sum(hit, axis=1, keepdims=True)


def tail_body(acc, value_ref, gains_ref, seg_ref, own_ref, other_ref, hidden_ref, inverse_ref, pooled_ref, unit_ref, low_ref, scale_ref, high, rest):
    hidden = value_ref[...] + acc[...]
    inverse = lax.rsqrt(jnp.mean(hidden * hidden, axis=1, keepdims=True) + EPSILON)
    hidden_ref[...] = hidden
    inverse_ref[...] = inverse
    final = hidden_ref[...] * inverse * gains_ref[2:3, :]
    high[...] = final.astype(BF16)
    rest[...] = (final - high[...].astype(F32)).astype(BF16)
    sents, count = member_of(seg_ref, pooled_ref.shape[0])
    pooled = ((dot(sents, high[...]) + dot(sents, rest[...])) / count).astype(BF16)
    pooled_ref[...] = pooled
    half = own_ref.shape[1]
    left = dot(pooled, own_ref[...])
    right = dot(pooled, other_ref[...])
    square = jnp.sum(left * left, axis=1, keepdims=True) + jnp.sum(right * right, axis=1, keepdims=True)
    scale = lax.rsqrt(square + EPSILON)
    scale_ref[...] = scale
    for at, value in ((0, left * scale), (half, right * scale)):
        unit_ref[:, at : at + half] = value
        low_ref[:, at : at + half] = value.astype(BF16)


def head_call(quarters, unit, scale, partner, column, sentence_loads, out_shapes):
    loads = [part(q) for q in (*quarters, unit, scale, partner, column)] + sentence_loads
    quarter = quarters[0].shape[0]
    total = 4 * quarter

    def run(get, loss_ref, embed_ref, *refs):
        *back_refs, every = refs
        for i in range(4):
            every[i * quarter : (i + 1) * quarter] = get(i)[...]
        unit, scale, partner, columns_id = (get(i)[...] for i in range(4, 8))
        partner = as_columns(
            jnp.concatenate([partner, jnp.zeros((1, LANES - partner.shape[1]), jnp.int32)], axis=1)
        )[: partner.shape[1], 0:1]
        own_count = unit.shape[0]
        sims = dot_nt(every[...], every[...]) * SOFTMAX_TEMP
        row = lax.broadcasted_iota(jnp.int32, (total, total), 0)
        column = lax.broadcasted_iota(jnp.int32, (total, total), 1)
        sims = jnp.where(row == column, NEG_FILL, sims)
        top = jnp.max(sims, axis=0, keepdims=True)
        lse_row = top + jnp.log(jnp.sum(jnp.exp(sims - top), axis=0, keepdims=True))
        own = sims[:own_count]
        own_top = jnp.max(own, axis=1, keepdims=True)
        own_lse = own_top + jnp.log(jnp.sum(jnp.exp(own - own_top), axis=1, keepdims=True))
        is_target = columns_id.astype(F32) == partner
        hit = jnp.where(is_target, 1.0, 0.0)
        target = jnp.sum(jnp.where(is_target, own, 0.0), axis=1, keepdims=True)
        loss_ref[...] = jnp.sum(own_lse - target, axis=0, keepdims=True)
        d_rows = (LOSS_SCALE * (jnp.exp(own - own_lse) - hit)).astype(BF16)
        d_cols = (LOSS_SCALE * (jnp.exp(own - lse_row) - hit)).astype(BF16)
        d_unit = SOFTMAX_TEMP * (dot(d_rows, every[...]) + dot(d_cols, every[...]))
        inner = jnp.sum(d_unit * unit, axis=1, keepdims=True)
        d_embed = (scale * (d_unit - unit * inner)).astype(BF16)
        embed_ref[...] = d_embed
        sentence_back(d_embed, [get(8 + i) for i in range(len(sentence_loads))], *back_refs)

    return stream("head", loads, out_shapes, run, [pltpu.VMEM((total, unit.shape[1]), BF16)])


def sentence_call(embed, sentence_loads, out_shapes):
    def run(get, *back_refs):
        sentence_back(get(0)[...], [get(1 + i) for i in range(len(sentence_loads))], *back_refs)

    return stream("sentence", [part(embed)] + sentence_loads, out_shapes, run)


def sentence_back(d_embed, sources, hidden_ref, low_ref, gain_out):
    seg_ref, own_ref, other_ref, value_ref, inverse_ref, gains_ref = sources
    half = own_ref.shape[1]
    d_pooled = dot_nt(d_embed[:, :half], own_ref[...]) + dot_nt(d_embed[:, half:], other_ref[...])
    sents, count = member_of(seg_ref, d_embed.shape[0])
    d_final = split_dot(sents, d_pooled / count, ((0,), (0,)))
    d_value, d_gain = norm_back(value_ref[...], inverse_ref[...], gains_ref[2:3, :], d_final)
    hidden_ref[...] = d_value
    low_ref[...] = d_value.astype(BF16)
    gain_out[...] = d_gain


def whole_call(body, args, out_shapes, scratch=(), name=None):
    return pl.pallas_call(
        body,
        out_shape=tuple(out_shapes),
        in_specs=[pl.BlockSpec(memory_space=pltpu.VMEM)] * len(args),
        out_specs=tuple(pl.BlockSpec(memory_space=pltpu.VMEM) for _ in out_shapes),
        scratch_shapes=scratch,
        compiler_params=params(),
        cost_estimate=cost(0, 0),
        name=name,
    )(*args)


def shape_of(kind, *dims):
    return jax.ShapeDtypeStruct(dims, kind)


def _stack_heads(part):
    lane = lax.broadcasted_iota(jnp.int32, part.shape, 1)
    zero = jnp.zeros_like(part)
    first = lane < LANES // 2
    return jnp.concatenate(
        [jnp.where(first, part, zero), jnp.where(first, zero, part)], axis=0
    )


def _unstack_heads(both):
    half = both.shape[0] // 2
    lane = lax.broadcasted_iota(jnp.int32, (half, LANES), 1)
    return jnp.where(lane < LANES // 2, both[:half], both[half:])


def _pad_keys(pad, ref):
    seq = ref.shape[0]
    pad[0:REACH] = jnp.zeros((REACH, LANES), pad.dtype)
    pad[REACH + seq :] = jnp.zeros((REACH, LANES), pad.dtype)
    pad[REACH : REACH + seq] = ref[...]


def _query_bits(shape):
    return lax.broadcasted_iota(jnp.int32, shape, 0) & (QB - 1)


def as_columns(values):
    count, length = values.shape
    side = max(LANES, length)
    square = jnp.concatenate([values.astype(F32), jnp.zeros((side - count, length), F32)], axis=0)
    return square.T


def attend_forward_kernel(
    q_ref, k_ref, v_ref, segq_ref, segk_ref, rel_ref, ctx_ref, probs_ref, kpad, vpad, mask, scores
):
    seq = q_ref.shape[0]
    blocks = seq // QB
    _pad_keys(kpad, k_ref)
    _pad_keys(vpad, v_ref)

    @pl.when(pl.program_id(0) == 0)
    def _():
        keys = as_columns(segk_ref[...])
        for b in range(blocks):
            same = keys[:, b : b + 1] == segq_ref[b : b + 1, :].astype(F32)
            mask[b] = jnp.where(same, 0.0, NEG_FILL)

    rel = rel_ref[0]
    row = lax.broadcasted_iota(jnp.int32, (2 * QB, WIN), 0)
    bias = jnp.where(row < QB, rel[0:1, :], rel[1:2, :])
    bits = _query_bits((2 * QB, WIN))
    step = 1
    while step < QB:
        bias = jnp.where((bits & step) != 0, pltpu.roll(bias, step, 1), bias)
        step *= 2
    bias = bias.T
    for b in range(blocks):
        query = _stack_heads(q_ref[b * QB : (b + 1) * QB] * jnp.asarray(SCORE_SCALE, BF16))
        scores[b] = dot_nt(kpad[b * QB : b * QB + WIN], query)
    values = scores[...] + bias[None] + mask[...]
    top = jnp.max(values, axis=1, keepdims=True)
    shifted = jnp.exp(values - top)
    total = jnp.sum(shifted, axis=1, keepdims=True)
    probs_ref[0] = (shifted * (1.0 / total)).astype(BF16)
    for b in range(blocks):
        part = dot_tn(probs_ref[0, b], vpad[b * QB : b * QB + WIN])
        ctx_ref[b * QB : (b + 1) * QB] = _unstack_heads(part).astype(BF16)


def attend_backward_kernel(
    q_ref, k_ref, v_ref, dctx_ref, probs_ref, dqkv_ref, dbias_ref,
    kpad, vpad, dk_acc, dv_acc, d_probs, d_low,
):
    seq = q_ref.shape[0]
    pair = pl.program_id(0)
    side = pl.num_programs(0) // 2
    later = pair // side
    q_at = pl.ds(pl.multiple_of(pair * LANES, LANES), LANES)
    k_at = pl.ds(pl.multiple_of((pair + 2 * side + later * side) * LANES, LANES), LANES)
    v_at = pl.ds(pl.multiple_of((pair + 3 * side + later * side) * LANES, LANES), LANES)
    blocks = seq // QB
    _pad_keys(kpad, k_ref)
    _pad_keys(vpad, v_ref)
    dk_acc[...] = jnp.zeros_like(dk_acc)
    dv_acc[...] = jnp.zeros_like(dv_acc)
    for b in range(blocks):
        window = slice(b * QB, b * QB + WIN)
        d_ctx = _stack_heads(dctx_ref[b * QB : (b + 1) * QB])
        d_probs[b] = dot_nt(vpad[window], d_ctx)
        dv_acc[window] += dot(probs_ref[0, b], d_ctx)
    probs = probs_ref[0].astype(F32)
    product = probs * d_probs[...]
    inner = jnp.sum(product, axis=1, keepdims=True)
    d_scores = product - probs * inner
    d_low[...] = d_scores.astype(BF16)
    total = jnp.sum(d_scores, axis=0).T
    for b in range(blocks):
        here = slice(b * QB, (b + 1) * QB)
        window = slice(b * QB, b * QB + WIN)
        query = _stack_heads(q_ref[here] * jnp.asarray(SCORE_SCALE, BF16))
        dk_acc[window] += dot(d_low[b], query)
        d_query = _unstack_heads(dot_tn(d_low[b], kpad[window])) * SCORE_SCALE
        dqkv_ref[here, q_at] = d_query.astype(BF16)
    dqkv_ref[:, k_at] = dk_acc[REACH : REACH + seq].astype(BF16)
    dqkv_ref[:, v_at] = dv_acc[REACH : REACH + seq].astype(BF16)
    bits = _query_bits((2 * QB, WIN))
    step = 1
    while step < QB:
        total = jnp.where((bits & step) != 0, pltpu.roll(total, WIN - step, 1), total)
        step *= 2
    first = jnp.sum(total[:QB], axis=0, keepdims=True)
    second = jnp.sum(total[QB:], axis=0, keepdims=True)
    dbias_ref[0] = jnp.concatenate([first, second, jnp.zeros((6, WIN), F32)], axis=0)


def _qkv_specs(seq, pairs):
    def spec(kind):
        return pl.BlockSpec((seq, LANES), lambda p: (0, kind * pairs + p))

    return [spec(0), spec(1), spec(2)]


def attend_forward(qkv, twice, windows, rel_window):
    seq = qkv.shape[0]
    pairs = rel_window.shape[0]
    blocks = seq // QB
    return pl.pallas_call(
        attend_forward_kernel,
        grid=(pairs,),
        out_shape=(
            jax.ShapeDtypeStruct((seq, pairs * LANES), BF16),
            jax.ShapeDtypeStruct((pairs, blocks, WIN, 2 * QB), BF16),
        ),
        in_specs=_qkv_specs(seq, pairs)
        + [
            pl.BlockSpec((blocks, 2 * QB), lambda p: (0, 0)),
            pl.BlockSpec((blocks, WIN), lambda p: (0, 0)),
            pl.BlockSpec((1, 2, WIN), lambda p: (p, 0, 0)),
        ],
        out_specs=(
            pl.BlockSpec((seq, LANES), lambda p: (0, p)),
            pl.BlockSpec((1, blocks, WIN, 2 * QB), lambda p: (p, 0, 0, 0)),
        ),
        scratch_shapes=[pltpu.VMEM((seq + 2 * REACH, LANES), BF16)] * 2
        + [pltpu.VMEM((blocks, WIN, 2 * QB), F32)] * 2,
        compiler_params=params(),
        cost_estimate=cost(8 * seq * WIN * LANES * pairs * 4, 8 * seq * LANES * pairs),
        name="attend_forward",
    )(qkv, qkv, qkv, twice, windows, rel_window)


def attend_backward(qkv, d_context, probs):
    seq = qkv.shape[0]
    pairs = probs.shape[0]
    blocks = seq // QB
    lane_block = pl.BlockSpec((seq, LANES), lambda p: (0, p))
    return pl.pallas_call(
        attend_backward_kernel,
        grid=(pairs,),
        out_shape=(
            jax.ShapeDtypeStruct((seq, 3 * pairs * LANES), BF16),
            jax.ShapeDtypeStruct((pairs, 8, WIN), F32),
        ),
        in_specs=_qkv_specs(seq, pairs)
        + [
            lane_block,
            pl.BlockSpec((1, blocks, WIN, 2 * QB), lambda p: (p, 0, 0, 0)),
        ],
        out_specs=(
            pl.BlockSpec((seq, 3 * pairs * LANES), lambda p: (0, 0)),
            pl.BlockSpec((1, 8, WIN), lambda p: (p, 0, 0)),
        ),
        scratch_shapes=[pltpu.VMEM((seq + 2 * REACH, LANES), BF16)] * 2
        + [pltpu.VMEM((seq + 2 * REACH, LANES), F32)] * 2
        + [pltpu.VMEM((blocks, WIN, 2 * QB), F32), pltpu.VMEM((blocks, WIN, 2 * QB), BF16)],
        compiler_params=params(),
        cost_estimate=cost(16 * seq * WIN * LANES * pairs * 4, 16 * seq * LANES * pairs),
        name="attend_backward",
    )(qkv, qkv, qkv, d_context, probs)


CORE = 1
CROSS = 2


def hop(value, mask):
    size = lax.axis_size("dp")
    return lax.ppermute(value, "dp", [(i, i ^ mask) for i in range(size)])


def over(value):
    return lax.ppermute(value, "mp", [(0, 1), (1, 0)])


def cross(value):
    return hop(value, CROSS)


def core(value):
    return hop(value, CORE)


def go(waits, *sends, keep=(), join=True):
    values = [value for _, value in sends]
    held = lax.optimization_barrier((*values, *keep, *waits))
    results = [how(value) for (how, _), value in zip(sends, held)]
    if join:
        results = list(lax.optimization_barrier(tuple(results)))
    return results + list(held[len(values) : len(values) + len(keep)])


def slot_masks(size):
    rest = size // 4
    return [z * 4 + x * 2 + c for c in range(2) for x in range(2) for z in range(rest)]


def strides(size):
    found = []
    stride = 4
    while stride < size:
        found.append(stride)
        stride *= 2
    return found


def gather_near(shard, waits, widths=None):
    size = lax.axis_size("dp")
    pieces = [shard]
    stride = 4
    while stride < size:
        radix = min(4, size // stride)
        shard = jnp.concatenate(pieces, axis=0) if len(pieces) > 1 else shard
        sends = [(functools.partial(hop, mask=j * stride), shard) for j in range(1, radix)]
        pieces = [shard] + go(waits, *sends)
        stride *= radix
    return jnp.concatenate(pieces, axis=0) if widths is None else stack_rows(pieces, widths)


def rows(*pieces):
    return jnp.concatenate(pieces, axis=0)


def columns(*pieces):
    return jnp.concatenate(pieces, axis=1)


def gather_weights(start, later, n_one, n_early, n_three, early, begin, between):
    size = lax.axis_size("dp")
    steps = strides(size)
    n_two = start.shape[1] - n_one
    n_four = later.shape[1] - n_three
    if len(steps) == 2:
        got = go((), *((functools.partial(hop, mask=4 * j), start) for j in range(1, 4)))
        more = hop(later, 4)
        one, two = stack_rows([start, *got], (n_one, n_two))
        later = stack_rows([later, more], (n_early, later.shape[1] - n_early))
        wide_step = functools.partial(hop, mask=steps[1])
    else:
        one, two = gather_near(start, (), (n_one, n_two))

        later = [later[:, :n_early], later[:, n_early:]]

        def wide_step(value):
            whole = gather_near(value, ())
            return whole[value.shape[0] :]

    one_x, two_y, more = go(early, (cross, one), (over, two), (wide_step, later[0]))
    (one,) = stack_rows([one, one_x], (n_one,))
    (two,) = stack_rows([two, two_y], (n_two,))
    one_y, two_x, one_c, two_c, more_b = go(
        (), (over, one), (cross, two), (core, one), (core, two), (wide_step, later[1])
    )
    if len(steps) == 2:
        have = later[0].shape[0]

        def put(near_a, near_b, far_a, far_b, three_ref, four_ref):
            for at, left, right in ((0, near_a, near_b), (have, far_a, far_b)):
                here = slice(at, at + have)
                three_ref[here, :n_early] = left[...]
                three_ref[here, n_early:] = right[:, : n_three - n_early]
                four_ref[here] = right[:, n_three - n_early :]

        three, four = whole_call(
            put,
            (*later, more, more_b),
            (shape_of(BF16, 2 * have, n_three), shape_of(BF16, 2 * have, n_four)),
            (),
            "put_rows",
        )
    else:
        later = rows(columns(*later), columns(more, more_b))
        three, four = later[:, :n_three], later[:, n_three:]
    three_x, four_y, one_yc, two_xc = go((), (cross, three), (over, four), (core, one_y), (core, two_x))
    (three,) = stack_rows([three, three_x], (n_three,))
    (four,) = stack_rows([four, four_y], (four.shape[1],))
    three_y, four_x, three_c, four_c, one, one_c, one_y, one_yc, two, two_x, two_c, two_xc, *early = go(
        (),
        (over, three),
        (cross, four),
        (core, three),
        (core, four),
        keep=(one, one_c, one_y, one_yc, two, two_x, two_c, two_xc, *early),
        join=False,
    )
    first, second = along_x(one, one_c, one_y, one_yc), along_y(two, two_x, two_c, two_xc)
    done = between(begin(first, early), second, early)
    four_xc, *done = go((three_y, four_x, three_c, four_c), (core, four_x), keep=done, join=False)
    (three_yc,) = go((four_xc,), (core, three_y), join=False)
    third, fourth = along_x(three, three_c, three_y, three_yc), along_y(four, four_x, four_c, four_xc)
    return first, second, third, fourth, early, done


def along_x(near, near_c, other, other_c):
    count = near.shape[0]
    return ((near, 0, count), (near_c, 0, count)), ((other, 0, count), (other_c, 0, count))


def along_y(near, side, near_c, side_c):
    count = near.shape[0] // 2
    return tuple(
        tuple((array, at, count) for array in (near, side, near_c, side_c)) for at in (0, count)
    )


def pack(name, sources, mib):
    widths = [count for *_, count in sources]
    block = sources[0][0].shape[0]

    def run(*refs):
        ins, out = refs[: len(sources)], refs[len(sources)]
        buffers, sem = refs[len(sources) + 1 : -1], refs[-1]
        copies = []
        for i, (_, first, count) in enumerate(sources):
            copy = pltpu.make_async_copy(ins[i].at[:, pl.ds(first, count)], buffers[i], sem.at[i])
            copy.start()
            copies.append(copy)
        at = 0
        for copy, buffer, width in zip(copies, buffers, widths):
            copy.wait()
            out[:, at : at + width] = buffer[...]
            at += width

    return pl.pallas_call(
        run,
        out_shape=shape_of(BF16, block, sum(widths)),
        in_specs=[pl.BlockSpec(memory_space=pltpu.HBM)] * len(sources),
        out_specs=pl.BlockSpec(memory_space=pltpu.VMEM),
        scratch_shapes=[pltpu.VMEM((block, width), BF16) for width in widths]
        + [pltpu.SemaphoreType.DMA((len(sources),))],
        compiler_params=params(mib),
        cost_estimate=cost(0, 0),
        name=name,
    )(*(array for array, *_ in sources))


def gather_dp(shard):
    near = gather_near(shard, ())
    side, c_near = go((near,), (cross, near), (core, near))
    return near, side, c_near, core(side)


def low(value):
    return value.astype(BF16)


def add(left, right):
    return (left.astype(F32) + right.astype(F32)).astype(BF16)


def product(left, begin, end, right, got=None):
    value = dot_tn(left[:, begin:end], right)
    if got is not None:
        value = value + got.astype(F32)
    return low(value)


def rest_start(value):
    half = value.shape[0] // 2
    return value[half:], value[:half]


def sum_half(value, send):
    gone, stays = rest_start(value)
    return stays + send(low(gone)).astype(F32)


def rest_hops(size):
    return [functools.partial(hop, mask=stride) for stride in reversed(strides(size))]


def shards(
    tokens,
    seg_ids,
    buckets,
    labels,
    w_query,
    w_key,
    w_value,
    w_out,
    w_in,
    w_back,
    gain_attn,
    gain_ffn,
    gain_final,
    w_pool,
    rel_table,
):
    micro_count, seq, width = tokens.shape
    size = lax.axis_size("dp")
    me = lax.axis_index("dp")
    mine = lax.axis_index("mp")
    block = width // size
    inner_half = w_query.shape[1]
    hidden_half = w_in.shape[1]
    sent_local = labels.shape[1]
    bucket_count = rel_table.shape[0]
    heads_half = rel_table.shape[1]
    masks = slot_masks(size)

    x_own = lax.dynamic_index_in_dim(tokens, mine, 0, keepdims=False)
    segments = lax.dynamic_index_in_dim(seg_ids, mine, 0, keepdims=False)[0]
    partner = lax.dynamic_index_in_dim(labels, mine, 0, keepdims=False)

    slot_block = jnp.stack([jnp.bitwise_xor(me, m) for m in masks]).astype(jnp.int32)
    source = (slot_block[:, None] * block + jnp.arange(block, dtype=jnp.int32)[None, :]).reshape(-1)
    order = (jnp.arange(width, dtype=jnp.int32)[:, None] == source[None, :]).astype(BF16)
    order = lax.optimization_barrier(order)
    inputs = dot(x_own, order)


    row_f32 = shape_of(F32, seq, width)
    row_low = shape_of(BF16, seq, width)
    column_f32 = shape_of(F32, seq, 1)
    gain_f32 = shape_of(F32, 1, width)
    heads = 3 * inner_half
    piece = hidden_half // 2
    halves = [(side, i * inner_half, inner_half) for side in range(2) for i in range(2)]

    def hidden_blocks(weights, first_col=0):
        return [(weights[side], first_col + col, n) for side, col, n in halves]

    def begin(first, early):
        inputs, rel_window, twice, windows, *_ = early
        qkv, normed1_low, inverse1, gains = qkv_call(inputs, first, inner_half)
        context, probs = attend_forward(qkv, twice, windows, rel_window)
        return qkv, normed1_low, inverse1, gains, context, probs

    def between(started, second, early):
        qkv, normed1_low, inverse1, gains, context, probs = started
        inputs = early[0]
        hidden1, inverse2, normed2_low = narrow(
            "attn_out",
            [(context, i * inner_half, second[i], piece, inner_half) for i in range(2)],
            (inputs, gains),
            (row_f32, column_f32, row_low),
            functools.partial(norm_body, 1),
        )
        act0, slope0 = wide("act0", normed2_low, hidden_blocks(second), (), gelu_both, 2)
        return normed1_low, inverse1, gains, qkv, context, probs, hidden1, inverse2, normed2_low, act0, slope0

    gains_col = jnp.pad(
        jnp.stack([gain_attn, gain_ffn, gain_final], axis=1), ((0, 0), (0, LANES - 3))
    )
    pool_half = w_pool.shape[1] // 2
    pool_own = lax.dynamic_slice_in_dim(w_pool, mine * pool_half, pool_half, axis=1)
    moved = piece // 3
    back_shard = w_back.T
    if block % 16:
        start = columns(w_query, w_key, w_value, gains_col, w_in[:, :piece], w_out.T)
        later = columns(
            back_shard[:, :piece],
            back_shard[:, hidden_half - moved :],
            pool_own,
            w_in[:, piece:],
            back_shard[:, piece : hidden_half - moved],
        )
    else:
        start = pack(
            "pack_start",
            [(w, 0, inner_half) for w in (w_query, w_key, w_value)]
            + [(gains_col, 0, LANES), (w_in, 0, piece), (w_out.T, 0, inner_half)],
            60,
        )
        back_shard, w_in, _ = lax.optimization_barrier((back_shard, w_in, start))
        later = pack(
            "pack_later",
            [
                (back_shard, 0, piece),
                (back_shard, hidden_half - moved, moved),
                (pool_own, 0, pool_half),
                (w_in, piece, piece),
                (back_shard, piece, piece - moved),
            ],
            16,
        )
    rel_other = over(lax.optimization_barrier((rel_table, start))[0])
    rel_all = jnp.concatenate([rel_table, rel_other], axis=1).astype(F32)
    near_buckets = lax.slice_in_dim(buckets, seq - 1 - REACH, seq - 1 - REACH + WIN)
    onehot = (near_buckets[None, :] == jnp.arange(bucket_count, dtype=jnp.int32)[:, None]).astype(F32)
    onehot = lax.optimization_barrier(low(onehot))
    rel_window = dot(rel_all, onehot.astype(F32), ((0,), (0,)), HIGHEST).reshape(heads_half, 2, WIN)
    padded = jnp.pad(segments, (REACH, REACH), constant_values=-1)
    windows = jnp.stack([padded[at : at + WIN] for at in range(0, seq, QB)])
    twice = jnp.tile(segments.reshape(seq // QB, QB), (1, 2))
    local_ids = jnp.arange(sent_local, dtype=jnp.int32)
    column_id = (slot_block[:, None] * sent_local + local_ids[None, :]).reshape(1, -1)
    early = (
        inputs, rel_window, twice, windows, order, onehot, column_id, partner[None, :], segments[None, :], mine.reshape(1, 1),
        (me * block).astype(jnp.uint32), (mine * heads_half).astype(jnp.uint32)
    )
    first, second, third, fourth, early, done = gather_weights(
        start,
        later,
        heads + LANES,
        piece,
        piece + moved + pool_half,
        early,
        begin,
        between,
    )
    inputs, rel_window, twice, windows, order, onehot, column_id, partner, seg_lane, mine_array, gain_at, table_at = early
    normed1_low, inverse1, gains, qkv, context, probs, hidden1, inverse2, normed2_low, act0, slope0 = done

    act1, up_kept = wide("act1", normed2_low, hidden_blocks(fourth), (), gelu_only, 2)
    pool_loads = [weight(side, piece + moved, pool_half) for side in third]
    hidden2, inverse3, pooled_low, unit, unit_low, scale = narrow(
        "ffn_out",
        [(act0, i * piece, third[i], 0, piece) for i in range(2)]
        + [(act1, i * piece, fourth[i], piece, piece - moved) for i in range(2)]
        + [(act1, (i + 1) * piece - moved, third[i], piece, moved) for i in range(2)],
        (hidden1, gains, seg_lane, *pool_loads),
        (
            row_f32,
            column_f32,
            shape_of(BF16, sent_local, width),
            shape_of(F32, sent_local, width),
            shape_of(BF16, sent_local, width),
            shape_of(F32, sent_local, 1),
        ),
        tail_body,
        [pltpu.VMEM((seq, width), BF16)] * 2,
    )
    quarters = gather_dp(unit_low)

    total_sent = column_id.shape[1]
    sentence_loads = [part(seg_lane), *pool_loads, part(hidden2), part(inverse3), part(gains)]
    back_shapes = (row_f32, row_low, gain_f32)
    if total_sent <= 1024:
        loss_local, embed_low, d_hidden2, ffn_low, d_gain3 = head_call(
            quarters,
            unit,
            scale,
            partner,
            column_id,
            sentence_loads,
            (shape_of(F32, 1, 1), shape_of(BF16, sent_local, width), *back_shapes),
        )
    else:
        every = rows(*quarters)
        position = jnp.arange(total_sent, dtype=jnp.int32)
        sims = dot_nt(every, every) * SOFTMAX_TEMP
        sims = jnp.where(position[:, None] == position[None, :], NEG_FILL, sims)
        lse_row = jax.nn.logsumexp(sims, axis=0, keepdims=True)
        own_sims = sims[:sent_local]
        own_lse = jax.nn.logsumexp(own_sims, axis=1, keepdims=True)
        is_target = column_id == partner.reshape(-1, 1)
        target = jnp.sum(jnp.where(is_target, own_sims, 0.0), axis=-1, keepdims=True)
        loss_local = jnp.sum(own_lse - target)
        hit = is_target.astype(F32)
        d_rows = low(LOSS_SCALE * (jnp.exp(own_sims - own_lse) - hit))
        d_cols = low(LOSS_SCALE * (jnp.exp(own_sims - lse_row) - hit))
        d_unit = SOFTMAX_TEMP * (dot(d_rows, every) + dot(d_cols, every))
        embed_low = low(scale * (d_unit - unit * jnp.sum(d_unit * unit, axis=-1, keepdims=True)))
        d_hidden2, ffn_low, d_gain3 = sentence_call(embed_low, sentence_loads, back_shapes)

    half = width // 2
    quarter = width // 4

    back0_sent, back1_sent = gradients("back_sent", ffn_low, half, half, (act0, act1))
    (pool_sent,) = gradients("pool_sent", pooled_low, half, half, (embed_low,))
    back0_got, back1_got, pool_got, ffn_later = go(
        (), (core, back0_sent), (core, back1_sent), (core, pool_sent), keep=(ffn_low,), join=False
    )
    pool_hi = product(pooled_low, quarter, half, embed_low, pool_got[quarter:])
    pool_lo = product(pooled_low, 0, quarter, embed_low, pool_got[:quarter])
    up0 = wide("up0", ffn_later, hidden_blocks(third), (slope0,), times_slope)

    back_hi = product(ffn_low, quarter, half, act0, back0_got[quarter:])
    back_lo = product(ffn_low, 0, quarter, act0, back0_got[:quarter])
    back_own = product(ffn_low, 0, half, act1[:, :piece], back1_got[:, :piece])
    back_oth = product(ffn_low, 0, half, act1[:, piece:], back1_got[:, piece:])
    got_lo, got_own, got_pool, ffn_later, up0, back_lo, back_own, pool_lo = go(
        (),
        (cross, back_hi),
        (over, back_oth),
        (cross, pool_hi),
        keep=(ffn_later, up0, back_lo, back_own, pool_lo),
    )
    back_blocks = [
        block
        for side in range(2)
        for block in (
            (fourth[side], piece, inner_half),
            (fourth[side], piece + inner_half, piece - moved - inner_half),
            (third[side], piece, moved),
        )
    ]
    up1 = wide("up1", ffn_later, back_blocks, (up_kept,), times_slope_of)
    in0_sent, in1_sent = gradients("in_sent", normed2_low, half, half, (up0, up1))
    in0_got, in1_got, up0, up1 = go((), (core, in0_sent), (core, in1_sent), keep=(up0, up1))
    attn_low, d_gain2, d_hidden1 = narrow(
        "ffn_in_back",
        [(up0, i * piece, second[i], 0, piece) for i in range(2)]
        + [(up1, i * piece, fourth[i], 0, piece) for i in range(2)],
        (hidden1, inverse2, gains, d_hidden2),
        (row_low, gain_f32, row_f32),
        functools.partial(back_body, 1),
    )
    d_context = wide("d_context", attn_low, [(second[side], piece, inner_half) for side in range(2)])

    pool_lo = add(pool_lo, got_pool)
    back_lo = add(back_lo, got_lo)
    back_own = add(back_own, got_own)
    in_hi = product(normed2_low, quarter, half, up0, in0_got[quarter:])
    in_lo = product(normed2_low, 0, quarter, up0, in0_got[:quarter])
    in_own = product(normed2_low, 0, half, up1[:, :piece], in1_got[:, :piece])
    in_oth = product(normed2_low, 0, half, up1[:, piece:], in1_got[:, piece:])
    got_first, got_x, got_in_own, d_context, pool_lo, back_lo, back_own, in_lo, in_own = go(
        (got_lo, got_own),
        (over, columns(back_lo[:, piece:], pool_lo[:, pool_half:])),
        (cross, columns(back_own[quarter:], in_hi)),
        (over, in_oth),
        keep=(d_context, pool_lo, back_lo, back_own, in_lo, in_own),
        join=False,
    )
    d_qkv, d_bias = attend_backward(qkv, d_context, probs)
    query_both = 2 * inner_half
    late_sent = sent_columns("late_sent", half, ((attn_low, context), (normed1_low, d_qkv)))
    late_got, d_qkv_later = go((), (core, late_sent), keep=(d_qkv,), join=False)
    grad_slots, d_gain1 = narrow(
        "qkv_back",
        [(d_qkv_later, i * inner_half, first[i], 0, inner_half) for i in range(2)]
        + [(d_qkv_later, (1 + i) * query_both, first[i], inner_half, query_both) for i in range(2)],
        (inputs, inverse1, gains, d_hidden1),
        (row_low, gain_f32),
        functools.partial(back_body, 0),
    )

    table_row = 3 * (width // LANES) + 1
    table_rows = -(-2 * heads_half * bucket_count // LANES)
    small_rows = -(-(table_row + table_rows) // 8) * 8
    (flat,) = whole_call(
        functools.partial(small_kernel, heads_half),
        (d_gain1, d_gain2, d_gain3, order, d_bias.reshape(-1, WIN), onehot, loss_local.reshape(1, 1), mine_array),
        (shape_of(F32, small_rows, LANES),),
        (),
        "small",
    )
    (grad_own,) = whole_call(turn_kernel, (grad_slots, order), (row_low,), (), "turn")
    flat_got, flat = go((), (over, flat), keep=(flat,), join=False)
    got_first, got_x, got_in_own = lax.optimization_barrier((got_first, got_x, got_in_own))
    flat = flat + flat_got
    got_second, got_in_lo = got_x[:, :piece], got_x[:, piece:]

    far = rest_hops(size)
    back_all = columns(
        add(back_lo[:, :piece], got_first[:, :piece]),
        add(back_own[:quarter], got_second),
        add(pool_lo[:, :pool_half], got_first[:, piece:]),
    )
    back_rest, back_stay = rest_start(back_all)
    in_lo = add(in_lo, got_in_lo)
    in_own = add(in_own, got_in_own)
    out_got, qkv_got = late_got[:, :query_both], late_got[:, query_both:]
    out_hi = product(attn_low, quarter, half, context, out_got[quarter:])
    out_lo = product(attn_low, 0, quarter, context, out_got[:quarter])
    query_hi = product(normed1_low, quarter, half, d_qkv[:, :query_both], qkv_got[quarter:, :query_both])
    query_lo = product(normed1_low, 0, quarter, d_qkv[:, :query_both], qkv_got[:quarter, :query_both])
    kv_own = product(
        normed1_low, 0, half, d_qkv[:, query_both : 2 * query_both], qkv_got[:, query_both : 2 * query_both]
    )
    kv_oth = product(normed1_low, 0, half, d_qkv[:, 2 * query_both :], qkv_got[:, 2 * query_both :])
    rest_hop = [functools.partial(hop, mask=j * 4) for j in range(1, min(4, size // 4))]
    back_more, got_first, got_x, got_kv, flat_got, back_stay, in_lo, in_own, out_lo, query_lo, kv_own, flat = go(
        (grad_own,),
        (far[0], back_rest),
        (over, in_lo[:, piece:]),
        (cross, columns(in_own[quarter:], out_hi, query_hi)),
        (over, kv_oth),
        (core, flat),
        keep=(back_stay, in_lo, in_own, out_lo, query_lo, kv_own, flat),
    )

    count = flat.shape[0]

    def in_two(value):
        high = value.astype(BF16).astype(F32)
        return jnp.concatenate([high, value - high], axis=0).astype(BF16)

    def from_two(pair):
        return pair[:count].astype(F32) + pair[count : 2 * count].astype(F32)

    def late_adds(
        stay, more, in_lo, got_first, in_own, got_x, out_lo, query_lo, kv_own, got_kv, flat, got_flat, *outs
    ):
        back_gone, back_keep, in_gone, in_keep, heads_gone, heads_keep, kv_gone, kv_keep, small = outs
        rows_z = stay.shape[0] // 2
        total = add(stay[...], more[...])
        back_keep[...] = total[:rows_z]
        back_gone[...] = total[rows_z:]
        rows_z = in_lo.shape[0] // 2
        for at, total in (
            (0, add(in_lo[:, :piece], got_first[...])),
            (piece, add(in_own[:quarter], got_x[:, :piece])),
        ):
            in_keep[:, at : at + piece] = total[:rows_z]
            in_gone[:, at : at + piece] = total[rows_z:]
        for i, ref in enumerate((out_lo, query_lo)):
            first_col = piece + i * query_both
            total = add(ref[...], got_x[:, first_col : first_col + query_both])
            heads_keep[:, i * inner_half : (i + 1) * inner_half] = total[:, :inner_half]
            heads_gone[:, i * inner_half : (i + 1) * inner_half] = total[:, inner_half:]
        kv_keep[...] = add(kv_own[:quarter], got_kv[:quarter])
        kv_gone[:, :query_both] = add(kv_own[quarter:], got_kv[quarter:])
        small[...] = flat[...] + got_flat[...]
        kv_gone[:, query_both:] = jnp.zeros((quarter, LANES), BF16)
        pair = in_two(small[...])
        kv_gone[: 2 * count, query_both:] = pair
        small[...] = from_two(pair)

    cut = [shape_of(BF16, back_stay.shape[0] // 2, back_stay.shape[1])] * 2
    cut += [shape_of(BF16, quarter // 2, hidden_half)] * 2 + [shape_of(BF16, quarter, query_both)] * 2
    cut += [
        shape_of(BF16, quarter, query_both + LANES),
        shape_of(BF16, quarter, query_both),
        shape_of(F32, count, LANES),
    ]
    back_rest, back_stay, in_rest, in_stay, heads_gone, heads_keep, kv_gone, kv_keep, flat = whole_call(
        late_adds,
        (back_stay, back_more, in_lo, got_first, in_own, got_x, out_lo, query_lo, kv_own, got_kv, flat, flat_got),
        cut,
        (),
        "late_adds",
    )
    early_rows = seq * 11 // 32
    back_more, in_more, got_first, got_second, grad_other, back_stay, in_stay, heads_keep, kv_keep, flat = go(
        (),
        (far[1], back_rest),
        (far[0], in_rest),
        (over, heads_gone),
        (cross, kv_gone),
        (over, grad_own[:early_rows]),
        keep=(back_stay, in_stay, heads_keep, kv_keep, flat),
    )

    def finish(value):
        value = value.astype(F32)
        for send in far[2:]:
            value = sum_half(value, send)
        return value

    n_last = query_both + query_both
    if len(far) == 2:
        rest = block
        late_rows = seq - early_rows

        def last_adds(stay, more, heads_ref, got_heads, kv_ref, got_kv, flat_ref, back_ref, back_got, own_ref, *outs):
            one, two, three, in_keep, keep, flat_out, tail, pool_ref = outs
            pool = add(back_ref[:, hidden_half:], back_got[:, hidden_half:])
            pool_ref[...] = pool
            tail[:late_rows] = own_ref[early_rows:]
            tail[late_rows:, :pool_half] = pool
            tail[late_rows:, pool_half:] = jnp.zeros((rest, width - pool_half), BF16)
            total = add(stay[...], more[...])
            in_keep[...] = total[:rest]
            one[:, LANES : LANES + hidden_half] = total[rest:]
            pair = in_two(flat_ref[...] + from_two(got_kv[:, query_both:]))
            flat_out[...] = from_two(pair)
            for i, (ref, at) in enumerate(((keep, 0), (one, LANES + hidden_half), (two, LANES), (three, LANES))):
                here = slice(i * rest, (i + 1) * rest)
                if i:
                    ref[:, :LANES] = pair
                ref[:, at : at + query_both] = add(heads_ref[here], got_heads[here])
                ref[:, at + query_both : at + n_last] = add(kv_ref[here], got_kv[here, :query_both])

        one, two, three, in_stay, last_stay, flat, tail, grad_pool = whole_call(
            last_adds,
            (in_stay, in_more, heads_keep, got_first, kv_keep, got_second, flat, back_stay, back_more, grad_own),
            (
                shape_of(BF16, rest, LANES + hidden_half + n_last),
                shape_of(BF16, rest, LANES + n_last),
                shape_of(BF16, rest, LANES + n_last),
                shape_of(BF16, rest, hidden_half),
                shape_of(BF16, rest, n_last),
                shape_of(F32, count, LANES),
                shape_of(BF16, late_rows + rest, width),
                shape_of(BF16, rest, pool_half),
            ),
            (),
            "last_adds",
        )
        got_one, got_two, got_three, got_tail, back_stay, back_more = go(
            (),
            (rest_hop[0], one),
            (rest_hop[1], two),
            (rest_hop[2], three),
            (over, tail),
            keep=(back_stay, back_more),
            join=False,
        )

        def back_final(stay, more, back_ref):
            back_ref[...] = stay[:, :hidden_half].astype(F32) + more[:, :hidden_half].astype(F32)

        (grad_back,) = whole_call(
            back_final, (back_stay, back_more), (shape_of(F32, rest, hidden_half),), (), "back_final"
        )

        def tokens_final(mine_ref, own_ref, first_ref, tail_ref, pool_own, out_ref, pool_ref):
            first = mine_ref[...] == 0
            own, other = pool_own[...].astype(F32), tail_ref[late_rows:, :pool_half].astype(F32)
            pool_ref[:, :pool_half] = jnp.where(first, own, other)
            pool_ref[:, pool_half:] = jnp.where(first, other, own)
            for at, count, ref in ((0, early_rows, first_ref), (early_rows, late_rows, tail_ref)):
                here = slice(at, at + count)
                own, other = own_ref[here].astype(F32), ref[:count].astype(F32)
                out_ref[0, here] = jnp.where(first, own, other).astype(BF16)
                out_ref[1, here] = jnp.where(first, other, own).astype(BF16)

        grad_tokens, grad_pool = whole_call(
            tokens_final,
            (mine_array, grad_own, grad_other, got_tail, grad_pool),
            (shape_of(BF16, 2, seq, width), shape_of(F32, rest, 2 * pool_half)),
            (),
            "tokens_final",
        )
        got_one, got_two, got_three, grad_tokens = lax.optimization_barrier(
            (got_one, got_two, got_three, grad_tokens)
        )

        def last_final(
            stay, in_keep, one_ref, two_ref, three_ref, flat_ref, order_ref, mine_ref, *outs
        ):
            in_ref, out_ref, q_ref, k_ref, v_ref, loss_ref, gains_ref, table_ref, wide_ref = outs
            in_ref[...] = in_keep[...].astype(F32) + one_ref[:, LANES : LANES + hidden_half].astype(F32)
            total = stay[...].astype(F32) + one_ref[:, LANES + hidden_half :].astype(F32)
            total = total + two_ref[:, LANES:].astype(F32) + three_ref[:, LANES:].astype(F32)
            for i, ref in enumerate((out_ref, q_ref, k_ref, v_ref)):
                ref[...] = total[:, i * inner_half : (i + 1) * inner_half]
            small = flat_ref[...]
            for ref in (one_ref, two_ref, three_ref):
                small = small + from_two(ref[:, :LANES])
            across = width // LANES
            loss_ref[...] = small[3 * across : 3 * across + 1, :1] / (micro_count * sent_local * size)
            wide_ref[...] = jnp.zeros_like(wide_ref)
            for i in range(3):
                for j in range(across):
                    wide_ref[i : i + 1, j * LANES : (j + 1) * LANES] = small[i * across + j : i * across + j + 1]
            high = wide_ref[...].astype(BF16)
            low_part = (wide_ref[...] - high.astype(F32)).astype(BF16)
            pick = order_ref[:, :LANES]
            gains_ref[...] = dot(high, pick) + dot(low_part, pick)
            a_row = LANES // bucket_count
            heads_list = []
            for head in range(2 * heads_half):
                line = table_row + head // a_row
                place = head % a_row * bucket_count
                heads_list.append(small[line : line + 1, place : place + bucket_count])
            first = jnp.concatenate(heads_list[:heads_half], axis=0)
            second = jnp.concatenate(heads_list[heads_half:], axis=0)
            table_ref[...] = jnp.where(mine_ref[...] == 0, first, second)

        head_shape = shape_of(F32, rest, inner_half)
        grad_in, grad_out, grad_query, grad_key, grad_value, loss, gains_mine, table_mine = whole_call(
            last_final,
            (last_stay, in_stay, got_one, got_two, got_three, flat, order, mine_array),
            (
                shape_of(F32, rest, hidden_half),
                *(head_shape,) * 4,
                shape_of(F32, 1, 1),
                shape_of(F32, 8, LANES),
                shape_of(F32, heads_half, bucket_count),
            ),
            [pltpu.VMEM((8, width), F32)],
            "last_final",
        )
        loss = loss.reshape(())
        gains_mine = gains_mine[:3, :block]
        table_mine = table_mine.T
    else:
        flat = flat + from_two(got_second[:, query_both:])
        grad_other = rows(grad_other, over(grad_own[early_rows:]))
        in_rest, in_stay = rest_start(add(in_stay, in_more))
        last = columns(add(heads_keep, got_first), add(kv_keep, got_second[:, :query_both]))
        last_rest, last_stay = rest_start(last)
        in_more, last_more, *flat_got = go(
            (), (far[1], in_rest), (far[0], last_rest), *((how, flat) for how in rest_hop)
        )
        last_rest, last_stay = rest_start(add(last_stay, last_more))
        last_more = far[1](last_rest)
        flat = flat + sum(flat_got)
        for send in far[:-2]:
            flat = flat + send(flat)
        grad_last = finish(last_stay.astype(F32) + last_more.astype(F32))
        grad_in = finish(in_stay.astype(F32) + in_more.astype(F32))
        back_all = finish(back_stay.astype(F32) + back_more.astype(F32))
        grad_back, grad_pool = back_all[:, :hidden_half], back_all[:, hidden_half:]
        pool_other = over(grad_pool)
        grad_pool = jnp.where(mine == 0, columns(grad_pool, pool_other), columns(pool_other, grad_pool))
        grad_out, grad_query, grad_key, grad_value = (
            grad_last[:, i * inner_half : (i + 1) * inner_half] for i in range(4)
        )
        grad_tokens = jnp.where(
            mine == 0, jnp.stack([grad_own, grad_other]), jnp.stack([grad_other, grad_own])
        )
        across = width // LANES
        zero = jnp.uint32(0)
        gains_mine = lax.dynamic_slice(flat[: 3 * across].reshape(3, width), (zero, gain_at), (3, block))
        loss = flat[3 * across, 0] / (micro_count * sent_local * size)
        table_sum = flat[table_row : table_row + table_rows].reshape(-1, bucket_count)[: 2 * heads_half]
        table_mine = lax.dynamic_slice(table_sum, (table_at, zero), (heads_half, bucket_count)).T
    return (
        loss,
        grad_tokens,
        grad_query,
        grad_key,
        grad_value,
        grad_out.T,
        grad_in,
        grad_back.T,
        gains_mine[0],
        gains_mine[1],
        gains_mine[2],
        grad_pool,
        table_mine,
    )


def solution(mesh):
    placed = (
        P(None, "dp", None),
        P(None, "dp", None),
        P(),
        P(None, "dp"),
        P("dp", "mp"),
        P("dp", "mp"),
        P("dp", "mp"),
        P("mp", "dp"),
        P("dp", "mp"),
        P("mp", "dp"),
        P("dp"),
        P("dp"),
        P("dp"),
        P("dp", None),
        P(None, "mp"),
    )
    return jax.shard_map(
        shards,
        mesh=mesh,
        in_specs=placed,
        out_specs=(
            P(),
            P(None, "dp", None),
            P("dp", "mp"),
            P("dp", "mp"),
            P("dp", "mp"),
            P("mp", "dp"),
            P("dp", "mp"),
            P("mp", "dp"),
            P("dp"),
            P("dp"),
            P("dp"),
            P("dp", None),
            P(None, "mp"),
        ),
        check_vma=False,
    )
```
